32 devices in a mesh: dp: 8 (over z, core), row: 2 (over x), col: 2 (over y).
Axes of the slice: x: 2, y: 2, z: 4, core: 2. Of those that a mesh axis runs over, the one named last changes fastest.
Arguments:
- inputs: bfloat16 [8192, 1280], P(('dp', 'row'), 'col'), may hold values from -6 to 6
- gain_attn: float32 [1280], P('col'), may hold values from 0.1 to 1.9
- w_qkv: bfloat16 [1280, 3, 1280], P('col', None, 'row'), may hold values from -0.25 to 0.25
- query_scale: float32 [80], replicated, may hold values from -1 to 1
- w_out: bfloat16 [1280, 1280], P('row', 'col'), may hold values from -0.625 to 0.625
- gain_mlp: float32 [1280], P('col'), may hold values from 0.1 to 1.9
- w_up: bfloat16 [1280, 1280], P('col', 'row'), may hold values from -0.15625 to 0.15625
- b_up: bfloat16 [1280], P('row'), may hold values from -3 to 3
- w_down: bfloat16 [1280, 1280], P('row', 'col'), may hold values from -0.15625 to 0.15625
- b_down: bfloat16 [1280], P('col'), may hold values from -2 to 2
- series_ids: int32 [8192], P('dp'), may hold values from 0 to 15, never falling along the last dimension, each value on 1 to 1024 neighbouring positions
- pad_mask: int32 [8192], P('dp'), may hold values 0 or 1
- cotangent: bfloat16 [8192, 1280], P(('dp', 'row'), 'col'), may hold values from -6 to 6
Outputs:
- layer_out: bfloat16 [8192, 1280], P(('dp', 'row'), 'col')
- grad_inputs: float32 [8192, 1280], P(('dp', 'row'), 'col')
- grad_gain_attn: float32 [1280], P('col')
- grad_w_qkv: float32 [1280, 3, 1280], P('col', None, 'row')
- grad_query_scale: float32 [80], replicated
- grad_w_out: float32 [1280, 1280], P('row', 'col')
- grad_gain_mlp: float32 [1280], P('col')
- grad_w_up: float32 [1280, 1280], P('col', 'row')
- grad_b_up: float32 [1280], P('row')
- grad_w_down: float32 [1280, 1280], P('row', 'col')
- grad_b_down: float32 [1280], P('col')
The draws below stay inside these ranges and needn't reach their ends.
Inputs may be any that keep to these rules, and one draw needn't show every extreme that they name: series_ids never falls along the tokens; a series has 1 to 1024 tokens.
All inputs are finite; a program needn't handle non-finite values. No bound on the sum of `pad_mask` on one device may be relied on, other than what follows from the above.
Results may differ from the reference program's by a relative error of at most 0.015.
The reference program's roundings to bfloat16 on the way count: a program that leaves them out, or rounds other values in their place, can miss the bound.
Values may be sent and summed in bfloat16 or wider, within the bound.
No kernel may reach another device: no remote copies, remote signals or barrier semaphores. Data moves between devices by JAX's collectives and lax.ppermute only.
A program may use at most 128 MiB of HBM per device.

```python
import math
import jax
import jax.numpy as jnp
import numpy as np
from jax import lax

D = 1280
HEADS = 16
HEAD_DIM = 80
HIDDEN_SIZE = 1280
PACK = 1024
TOKENS = 8192
SERIES = 1024
SEGMENTS = 16
QBLOCK = 512
N_DP = 8


def set_ends(array, rng, smallest, largest):
    longest = array.shape.index(max(array.shape))
    spots = []
    for shift in (0, 1):
        where = [jax.random.randint(jax.random.fold_in(rng, axis), (), 0, length) for axis, length in enumerate(array.shape)]
        where[longest] = (where[longest] + shift) % array.shape[longest]
        spots.append(tuple(where))
    return array.at[spots[0]].set(smallest).at[spots[1]].set(largest)


def block_scale(rng, extent, cuts, low, high):
    level = 1.0
    for position, shards_of in cuts:
        draws = jax.random.uniform(jax.random.fold_in(jax.random.fold_in(rng, 6), position), (shards_of,), jnp.float32, low / len(cuts), high / len(cuts))
        level = level * jnp.repeat(jnp.exp(draws), extent[position] // shards_of).reshape((-1,) + (1,) * (len(extent) - 1 - position))
    return level


def profile(amount, total, most, lean):
    portions = [(1 << 20) // math.isqrt(grade ** lean) + 1 for grade in range(2, amount + 1)]
    surplus, given = total - most - (amount - 1), [1] * (amount - 1)
    while surplus > 0:
        movable = [i for i in range(amount - 1) if given[i] < most]
        pool, budget = sum([portions[i] for i in movable]), surplus
        for i in movable:
            more = min(most - given[i], max(1, budget * portions[i] // pool), surplus)
            given[i] = given[i] + more
            surplus = surplus - more
    return np.array([most] + given)


def uneven(own_key, number_of, total, most, slope):
    if number_of == 2:
        one = jax.random.randint(own_key, (), max(1, total - most), min(most, total - 1) + 1)
        return jnp.stack([one, total - one])
    lengths = jnp.asarray(profile(number_of, total, most, slope), jnp.int32)
    twos = (number_of - 1) // 2
    source_of, receiver = lengths[1:1 + 2 * twos:2], lengths[2:2 + 2 * twos:2]
    margin = jnp.minimum(source_of - 1, most - receiver)
    moved = jax.random.randint(jax.random.fold_in(own_key, 1), (twos,), 0, 1 << 20) % (margin + 1)
    lengths = lengths.at[1:1 + 2 * twos:2].set(source_of - moved).at[2:2 + 2 * twos:2].set(receiver + moved)
    return lengths[jax.random.permutation(jax.random.fold_in(own_key, 2), number_of)]


def bell_draw(own_key, shape, scale, limit, shards=(), kind=jnp.bfloat16):
    loudness = block_scale(own_key, shape, shards, -0.22, 0.18) if shards else 1.0
    values = jax.random.normal(own_key, shape, jnp.float32) * scale * loudness
    return jnp.minimum(jnp.maximum(values, -limit), limit).astype(kind)


def setup_inputs(seed: int = 0) -> dict:
    seeds = jax.random.split(jax.random.key(seed), 14)
    return {
        "inputs": bell_draw(seeds[0], (TOKENS, D), 1.0, 6.0, ((0, 16), (1, 2))),
        "gain_attn": jnp.clip(1.0 + 0.18 * jax.random.normal(seeds[1], (D,), jnp.float32), 0.1, 1.9),
        "w_qkv": bell_draw(seeds[2], (D, 3, HEADS * HEAD_DIM), (D // 2) ** -0.5, 0.25, ((0, 2), (2, 2))),
        "query_scale": jnp.clip(jax.random.uniform(seeds[3], (HEAD_DIM,), jnp.float32, -1.0, 1.0), -1.0, 1.0),
        "w_out": bell_draw(seeds[4], (HEADS * HEAD_DIM, D), (HEADS * HEAD_DIM // 16) ** -0.5, 0.625, ((0, 2), (1, 2))),
        "gain_mlp": jnp.clip(1.0 + 0.18 * jax.random.normal(seeds[5], (D,), jnp.float32), 0.1, 1.9),
        "w_up": bell_draw(seeds[6], (D, HIDDEN_SIZE), D ** -0.5, 0.15625, ((0, 2), (1, 2))),
        "b_up": bell_draw(seeds[7], (HIDDEN_SIZE,), 0.5, 3.0, ((0, 2),)),
        "w_down": bell_draw(seeds[8], (HIDDEN_SIZE, D), HIDDEN_SIZE ** -0.5, 0.15625, ((0, 2), (1, 2))),
        "b_down": bell_draw(seeds[9], (D,), 0.3, 2.0, ((0, 2),)),
        "series_ids": jnp.searchsorted(jnp.cumsum(uneven(seeds[10], SEGMENTS, TOKENS, SERIES, 0)), jnp.arange(TOKENS), side="right").astype(jnp.int32),
        "pad_mask": set_ends((jax.random.randint(seeds[11], (TOKENS,), 0, 8) < 1).astype(jnp.int32), jax.random.fold_in(seeds[11], 1), 0, 1),
        "cotangent": bell_draw(seeds[12], (TOKENS, D), 1.0, 6.0, ((0, 16), (1, 2))),
    }


EPS = 1e-06
QUERY_CONST = 1.442695041
MASKED = -1e+30
HIGHEST_PREC = lax.Precision.HIGHEST

@jax.custom_vjp
def low(v):
    return lax.optimization_barrier(v.astype(jnp.bfloat16)).astype(jnp.float32)

@jax.custom_vjp
def low_back(v):
    return v

def low_keep(v):
    return (low(v), None)

def low_pass(kept, grad):
    return (grad,)

def back_keep(v):
    return (v, None)

def back_low(kept, grad):
    return (low(grad),)
low.defvjp(low_keep, low_pass)
low_back.defvjp(back_keep, back_low)

def rms_norm(tensor, gain_vec):
    scaled = lax.rsqrt(lax.optimization_barrier(jnp.mean(tensor * tensor, axis=-1, keepdims=True)) + EPS)
    return tensor * scaled * gain_vec

def attend_block(queries, begin_at, keys_in, values_in, series, padding):
    width = queries.shape[0]
    row_ids = begin_at + jnp.arange(width, dtype=jnp.int32)
    col_ids = jnp.arange(keys_in.shape[0], dtype=jnp.int32)
    series_rows = lax.dynamic_slice_in_dim(series, begin_at, width)
    allowed = (series_rows[:, None] == series[None, :]) & (col_ids[None, :] <= row_ids[:, None])
    allowed = allowed & ((padding[None, :] == 0) | (col_ids[None, :] == row_ids[:, None]))
    scores = low_back(jnp.einsum('qhd,khd->hqk', queries, keys_in, precision=HIGHEST_PREC))
    scores = jnp.where(allowed[None], scores, MASKED)
    row_top = lax.optimization_barrier(jnp.max(scores, axis=-1, keepdims=True))
    weights_exp = jnp.exp(scores - row_top)
    chances = weights_exp / lax.optimization_barrier(jnp.sum(weights_exp, axis=-1, keepdims=True))
    return jnp.einsum('hqk,khd->qhd', low(chances), values_in, precision=HIGHEST_PREC)

def attend_pack(queries, keys_in, values_in, series, padding):
    blocks = PACK // QBLOCK
    begins = jnp.arange(blocks, dtype=jnp.int32) * QBLOCK
    pieces = queries.reshape(blocks, QBLOCK, HEADS, HEAD_DIM)

    def per_block(entry):
        return attend_block(entry[0], entry[1], keys_in, values_in, series, padding)
    return lax.map(jax.checkpoint(per_block), (pieces, begins)).reshape(PACK, HEADS, HEAD_DIM)

def attend_all(queries, keys_in, values_in, series, padding):
    shape_four = (N_DP, PACK, HEADS, HEAD_DIM)

    def per_pack(entry):
        return attend_pack(entry[0], entry[1], entry[2], entry[3], entry[4])
    outcome = lax.map(jax.checkpoint(per_pack), (queries.reshape(shape_four), keys_in.reshape(shape_four), values_in.reshape(shape_four), series.reshape(N_DP, PACK), padding.reshape(N_DP, PACK)))
    return outcome.reshape(TOKENS, HEADS * HEAD_DIM)

def layer(inputs, gain_attn, w_qkv, query_scale, w_out, gain_mlp, w_up, b_up, w_down, b_down, series, padding):
    normed_one = low(rms_norm(inputs, gain_attn))
    projected = low_back(jnp.einsum('td,dsh->tsh', normed_one, w_qkv, precision=HIGHEST_PREC))
    factor = QUERY_CONST / math.sqrt(HEAD_DIM) * jax.nn.softplus(query_scale)
    queries = low(projected[:, 0].reshape(TOKENS, HEADS, HEAD_DIM) * factor)
    keys_in = low(projected[:, 1].reshape(TOKENS, HEADS, HEAD_DIM))
    values_in = low(projected[:, 2].reshape(TOKENS, HEADS, HEAD_DIM))
    attended = low(low_back(attend_all(queries, keys_in, values_in, series, padding)))
    middle = inputs + low_back(jnp.dot(attended, w_out, precision=HIGHEST_PREC))
    normed_two = low(rms_norm(middle, gain_mlp))
    pre_act = low_back(jnp.dot(normed_two, w_up, precision=HIGHEST_PREC) + b_up)
    hidden = low(jax.nn.silu(pre_act))
    return middle + jnp.dot(hidden, w_down, precision=HIGHEST_PREC) + b_down

def reference(inputs, gain_attn, w_qkv, query_scale, w_out, gain_mlp, w_up, b_up, w_down, b_down, series_ids, pad_mask, cotangent):
    floats = [arr.astype(jnp.float32) for arr in (inputs, gain_attn, w_qkv, query_scale, w_out, gain_mlp, w_up, b_up, w_down, b_down)]

    def forward(*params):
        return layer(*params, series_ids, pad_mask)
    result, pullback = jax.vjp(forward, *floats)
    grads = pullback(cotangent.astype(jnp.float32))
    return (result.astype(jnp.bfloat16), grads[0], grads[1], grads[2], grads[3], grads[4], grads[5], grads[6], grads[7], grads[8], grads[9])
```

```python
import functools
import math

import jax
import jax.numpy as jnp
from jax import lax
from jax.experimental import pallas as pl
from jax.experimental.pallas import tpu as pltpu
from jax.sharding import Mesh
from jax.sharding import PartitionSpec as P

D = 1280
HEAD_DIM = 80
EPS = 1e-06
QUERY_CONST = 1.442695041
MASKED = -1e30
BF = jnp.bfloat16
F32 = jnp.float32
VMEM_LIMIT = 50 * 1024 * 1024


def size(axis):
    return lax.axis_size(axis)


def swap(x, axis):
    return lax.ppermute(x, axis, [(0, 1), (1, 0)])


def flip(blocks, axis):
    if size(axis) != 2:
        return list(blocks)
    first = lax.axis_index(axis) == 0
    a, b = blocks
    return [jnp.where(first, a, b), jnp.where(first, b, a)]


def flip_dim(x, axis, dim):
    if size(axis) != 2:
        return x
    return jnp.concatenate(flip(jnp.split(x, 2, axis=dim), axis), axis=dim)


def gather(x, axis):
    if size(axis) == 2:
        return [x, swap(x, axis)]
    whole = lax.all_gather(x, axis, axis=0, tiled=False)
    return [whole[i] for i in range(size(axis))]


def gather_grid(x):
    if size("row") != 2:
        return [gather(b, "col") for b in gather(x, "row")]
    along_row, along_col = swap(x, "row"), swap(x, "col")
    half = x.shape[0] // 2
    across = jnp.concatenate(
        [swap(along_row[:half], "col"), swap(along_col[half:], "row")], axis=0
    )
    return [[x, along_col], [along_row, across]]


def scatter_sum(x, axis, dim):
    if size(axis) != 2:
        return lax.psum_scatter(x, axis, scatter_dimension=dim, tiled=True)
    mine, theirs = jnp.split(x, 2, axis=dim)
    return (mine.astype(F32) + swap(theirs, axis).astype(F32)).astype(x.dtype)


def exchange(x, axis, split, join):
    if size(axis) != 2:
        return lax.all_to_all(x, axis, split, join, tiled=True)
    mine, theirs = jnp.split(x, 2, axis=split)
    return jnp.concatenate([mine, swap(theirs, axis)], axis=join)


def core_half(x, dim):
    return lax.dynamic_slice_in_dim(
        x, lax.axis_index("core") * (x.shape[dim] // 2), x.shape[dim] // 2, dim
    )


def weight_gather(w, row_dim):
    part = core_half(w, 0)
    blocks = gather_grid(part)
    if row_dim == 1:
        blocks = [list(b) for b in zip(*blocks)]
    mine = jnp.stack([jnp.concatenate(b, axis=1) for b in blocks])
    other = swap(mine, "core")
    first = lax.axis_index("core") == 0
    both = jnp.stack([jnp.where(first, mine, other), jnp.where(first, other, mine)], axis=1)
    return both.reshape(-1, both.shape[-1])


def weight_sum(g, row_dim):
    dim_axis = ("row", "col") if row_dim == 0 else ("col", "row")
    n0 = size(dim_axis[0])
    g = g.reshape(n0, 2, g.shape[0] // n0 // 2, g.shape[1])
    core = lax.axis_index("core")
    keep = lax.dynamic_index_in_dim(g, core, 1, keepdims=False)
    give = lax.dynamic_index_in_dim(g, 1 - core, 1, keepdims=False).astype(BF)
    part = (keep + swap(give, "core").astype(F32)).astype(BF)
    part = scatter_sum(part, dim_axis[0], 0)
    part = scatter_sum(part[0], dim_axis[1], 1)
    return z_sum(part)


def z_sum(part):
    total = lax.psum(part, "z")
    other = swap(total, "core")
    return flip_core(total, other)


def flip_core(total, other):
    first = lax.axis_index("core") == 0
    return jnp.concatenate(
        [jnp.where(first, total, other), jnp.where(first, other, total)], axis=-2
    ).astype(F32)


def dot(a, b, contract):
    return lax.dot_general(a, b, ((contract[0:1], contract[1:2]), ((), ())), preferred_element_type=F32)


def bias_block(series_row, series_col, key_pos, q0, k0, qb, kb, diagonal):
    q_pos = q0 + lax.broadcasted_iota(jnp.int32, (1, qb), 1)
    allowed = (series_col == series_row) & (key_pos <= q_pos)
    if diagonal:
        k_pos = k0 + lax.broadcasted_iota(jnp.int32, (kb, 1), 0)
        allowed = allowed | (k_pos == q_pos)
    return jnp.where(allowed, 0.0, MASKED)


def forward_kernel(block, qkv_ref, srow_ref, scol_ref, kpos_ref, out_ref, lse_ref, bias_ref, krow_ref, s_ref):
    t = qkv_ref.shape[3]
    n = t // block
    krow_ref[...] = qkv_ref[1, 0].astype(F32).T.astype(BF)

    def bias_slot(j, i):
        return j * (j + 1) // 2 + i

    @pl.when(pl.program_id(0) == 0)
    def _():
        for j in range(n):
            for i in range(j + 1):
                keys = pl.ds(i * block, block)
                bias_ref[bias_slot(j, i)] = bias_block(
                    srow_ref[:, j * block : (j + 1) * block],
                    scol_ref[keys, :],
                    kpos_ref[keys, :],
                    j * block,
                    i * block,
                    block,
                    block,
                    i == j,
                )

    for j in range(n):
        cols = slice(j * block, (j + 1) * block)
        q = qkv_ref[0, 0, :, cols]
        top = None
        for i in range(j + 1):
            s = dot(krow_ref[i * block : (i + 1) * block, :], q, (1, 0)) + bias_ref[bias_slot(j, i)]
            s_ref[i * block : (i + 1) * block, :] = s
            here = jnp.max(s, axis=0, keepdims=True)
            top = here if top is None else jnp.maximum(top, here)
        total = jnp.zeros((1, block), F32)
        acc = jnp.zeros((HEAD_DIM, block), F32)
        for i in range(j + 1):
            p = jnp.exp(s_ref[i * block : (i + 1) * block, :] - top)
            total += jnp.sum(p, axis=0, keepdims=True)
            acc += dot(qkv_ref[2, 0, :, i * block : (i + 1) * block], p.astype(BF), (1, 0))
        out_ref[0, :, cols] = (acc / total).astype(BF)
        lse_ref[0, :, cols] = top + jnp.log(total)


def backward_kernel(
    block, qkv_ref, raw_ref, factor_ref, out_ref, gout_ref, lse_ref, srow_ref, scol_ref, kpos_ref,
    grad_ref, gscale_ref, bias_ref, krow_ref, vrow_ref, gk_ref, gv_ref,
):
    t = qkv_ref.shape[3]
    n = t // block
    krow_ref[...] = qkv_ref[1, 0].astype(F32).T.astype(BF)
    vrow_ref[...] = qkv_ref[2, 0].astype(F32).T.astype(BF)

    def bias_slot(j, i):
        return j * (j + 1) // 2 + i

    @pl.when(pl.program_id(0) == 0)
    def _():
        for j in range(n):
            for i in range(j + 1):
                keys = pl.ds(i * block, block)
                bias_ref[bias_slot(j, i)] = bias_block(
                    srow_ref[:, j * block : (j + 1) * block],
                    scol_ref[keys, :],
                    kpos_ref[keys, :],
                    j * block,
                    i * block,
                    block,
                    block,
                    i == j,
                )

    gscale = jnp.zeros((HEAD_DIM, 1), F32)
    for j in range(n):
        cols = slice(j * block, (j + 1) * block)
        q = qkv_ref[0, 0, :, cols]
        go = gout_ref[0, :, cols]
        lse = lse_ref[0, :, cols]
        delta = jnp.sum(go.astype(F32) * out_ref[0, :, cols].astype(F32), axis=0, keepdims=True)
        gq = jnp.zeros((HEAD_DIM, block), F32)
        for i in range(j + 1):
            keys = slice(i * block, (i + 1) * block)
            s = dot(krow_ref[keys, :], q, (1, 0)) + bias_ref[bias_slot(j, i)]
            p = jnp.exp(s - lse)
            gp = dot(vrow_ref[keys, :], go, (1, 0))
            gs = (p * (gp - delta)).astype(BF)
            gq += dot(qkv_ref[1, 0, :, keys], gs, (1, 0))
            gk = dot(q, gs, (1, 1))
            gv = dot(go, p.astype(BF), (1, 1))
            if i == j:
                gk_ref[:, keys] = gk
                gv_ref[:, keys] = gv
            else:
                gk_ref[:, keys] += gk
                gv_ref[:, keys] += gv
        gscale += jnp.sum(gq * raw_ref[0, :, cols], axis=1, keepdims=True)
        grad_ref[0, 0, :, cols] = (gq * factor_ref[...]).astype(BF)
    grad_ref[1, 0] = gk_ref[...].astype(BF)
    grad_ref[2, 0] = gv_ref[...].astype(BF)
    gscale_ref[0] = gscale


def mask_args(series, padding):
    t = series.shape[0]
    pos = jnp.arange(t, dtype=jnp.int32)
    return series.reshape(1, t), series.reshape(t, 1), jnp.where(padding == 0, pos, t).reshape(t, 1)


def attention_forward(qkv, masks):
    _, heads, hd, t = qkv.shape
    block = min(256, t) if t <= 2048 else 512
    n = t // block
    whole = lambda shape: pl.BlockSpec(shape, lambda h: (0,) * len(shape))
    return pl.pallas_call(
        functools.partial(forward_kernel, block),
        grid=(heads,),
        in_specs=[
            pl.BlockSpec((3, 1, hd, t), lambda h: (0, h, 0, 0)),
            whole((1, t)),
            whole((t, 1)),
            whole((t, 1)),
        ],
        out_specs=[
            pl.BlockSpec((1, hd, t), lambda h: (h, 0, 0)),
            pl.BlockSpec((1, 1, t), lambda h: (h, 0, 0)),
        ],
        out_shape=[
            jax.ShapeDtypeStruct((heads, hd, t), BF),
            jax.ShapeDtypeStruct((heads, 1, t), F32),
        ],
        scratch_shapes=[
            pltpu.VMEM((n * (n + 1) // 2, block, block), F32),
            pltpu.VMEM((t, hd), BF),
            pltpu.VMEM((t, block), F32),
        ],
        compiler_params=pltpu.CompilerParams(vmem_limit_bytes=VMEM_LIMIT),
        cost_estimate=pl.CostEstimate(
            flops=heads * 4 * t * t * 128, bytes_accessed=heads * hd * t * 8, transcendentals=heads * t * t // 2
        ),
        name="attention_forward",
    )(qkv, *masks)


def attention_backward(qkv, raw, factor, out, gout, lse, masks):
    _, heads, hd, t = qkv.shape
    block = min(256, t) if t <= 2048 else 512
    n = t // block
    whole = lambda shape: pl.BlockSpec(shape, lambda h: (0,) * len(shape))
    head = lambda: pl.BlockSpec((1, hd, t), lambda h: (h, 0, 0))
    return pl.pallas_call(
        functools.partial(backward_kernel, block),
        grid=(heads,),
        in_specs=[
            pl.BlockSpec((3, 1, hd, t), lambda h: (0, h, 0, 0)),
            head(),
            whole((hd, 1)),
            head(),
            head(),
            pl.BlockSpec((1, 1, t), lambda h: (h, 0, 0)),
            whole((1, t)),
            whole((t, 1)),
            whole((t, 1)),
        ],
        out_specs=[
            pl.BlockSpec((3, 1, hd, t), lambda h: (0, h, 0, 0)),
            pl.BlockSpec((1, hd, 1), lambda h: (h, 0, 0)),
        ],
        out_shape=[
            jax.ShapeDtypeStruct((3, heads, hd, t), BF),
            jax.ShapeDtypeStruct((heads, hd, 1), F32),
        ],
        scratch_shapes=[
            pltpu.VMEM((n * (n + 1) // 2, block, block), F32),
            pltpu.VMEM((t, hd), BF),
            pltpu.VMEM((t, hd), BF),
            pltpu.VMEM((hd, t), F32),
            pltpu.VMEM((hd, t), F32),
        ],
        compiler_params=pltpu.CompilerParams(vmem_limit_bytes=VMEM_LIMIT),
        cost_estimate=pl.CostEstimate(
            flops=heads * 10 * t * t * 128, bytes_accessed=heads * hd * t * 20, transcendentals=heads * t * t // 2
        ),
        name="attention_backward",
    )(qkv, raw, factor, out, gout, lse, *masks)


def norm_scale(x):
    return lax.rsqrt(jnp.mean(x * x, axis=1, keepdims=True) + EPS)


def body(
    inputs, gain_attn, w_qkv, query_scale, w_out, gain_mlp, w_up, b_up, w_down, b_down, series_ids, pad_mask, cotangent
):
    rows, cols = size("row"), size("col")
    tok = inputs.shape[0]
    feat = inputs.shape[1]
    share = tok // cols
    t = series_ids.shape[0]
    head_rows = w_qkv.shape[2] // cols
    heads = head_rows // HEAD_DIM
    r, c = lax.axis_index("row"), lax.axis_index("col")

    blocks = gather_grid(inputs)
    strips = [jnp.concatenate(b, axis=1) for b in blocks]
    x_own = strips[0] if rows == 2 else lax.dynamic_index_in_dim(jnp.stack(strips), r, 0, keepdims=False)
    x_all = jnp.concatenate(flip(strips, "row"), axis=0)
    gain_one = jnp.concatenate(gather(gain_attn, "col"))
    gain_two = jnp.concatenate(gather(gain_mlp, "col"))
    bias_up = jnp.concatenate(gather(b_up, "row")).astype(F32)
    bias_down = jnp.concatenate(gather(b_down, "col")).astype(F32)

    w3 = jnp.transpose(w_qkv, (1, 0, 2)).reshape(3, feat, cols, head_rows)
    w_mine = lax.dynamic_index_in_dim(w3, c, 2, keepdims=False)
    w_give = lax.dynamic_index_in_dim(w3, 1 - c, 2, keepdims=False)
    w_half = swap(core_half(w_give, 1), "col")
    w_other = swap(w_half, "core")
    first = lax.axis_index("core") == 0
    w_full = jnp.concatenate(
        [w_mine, jnp.where(first, w_half, w_other), jnp.where(first, w_other, w_half)], axis=1
    )

    xf = x_all.astype(F32)
    scale_one = norm_scale(xf)
    normed_one = (xf * scale_one * gain_one).astype(BF)
    projected = jnp.einsum("td,sdh->sht", normed_one, w_full, preferred_element_type=F32)
    projected = projected.reshape(3, heads, HEAD_DIM, t)
    factor = QUERY_CONST / math.sqrt(HEAD_DIM) * jax.nn.softplus(query_scale)
    raw_q = projected[0]
    qkv = jnp.stack([raw_q * factor[None, :, None], projected[1], projected[2]]).astype(BF)
    masks = mask_args(series_ids, pad_mask)
    attended, lse = attention_forward(qkv, masks)

    def to_tokens(y):
        y = flip_dim(y.reshape(head_rows, rows, cols, share), "row", 1)
        y = flip_dim(y, "col", 2)
        y = exchange(y.reshape(1, head_rows, rows, cols, share), "row", 2, 0)
        y = exchange(y.reshape(rows, 1, head_rows, cols, share), "col", 3, 1)
        y = flip_dim(y.reshape(rows, cols, head_rows, share), "col", 1)
        return y.reshape(rows * cols * head_rows, share)

    def to_heads(y):
        y = flip_dim(y.reshape(rows, cols, head_rows, share), "col", 1)
        y = exchange(y.reshape(rows, cols, head_rows, 1, share), "col", 1, 3)
        y = exchange(y.reshape(rows, head_rows, 1, cols, share), "row", 0, 2)
        y = flip_dim(y.reshape(head_rows, rows, cols, share), "col", 2)
        return flip_dim(y, "row", 1).reshape(head_rows, t)

    w_out_all = weight_gather(w_out, 0)
    w_up_all = weight_gather(w_up, 1)
    w_down_all = weight_gather(w_down, 0)

    def my_share(y):
        return lax.dynamic_slice_in_dim(y, c * share, share, 0)

    att = to_tokens(attended.reshape(head_rows, t))
    x_mine = my_share(x_own).astype(F32)
    middle = x_mine + dot(att, w_out_all, (0, 0))
    scale_two = norm_scale(middle)
    normed_two = (middle * scale_two * gain_two).astype(BF)
    pre_act = dot(normed_two, w_up_all, (1, 0)) + bias_up
    sig = jax.nn.sigmoid(pre_act)
    hidden = (pre_act * sig).astype(BF)
    result = (middle + dot(hidden, w_down_all, (1, 0)) + bias_down).astype(BF)

    def to_block(y):
        mine, theirs = jnp.split(y, 2, axis=1)
        return jnp.concatenate(flip([mine, swap(theirs, "col")], "col"), axis=0)

    layer_out = to_block(result)

    g_give = lax.dynamic_slice_in_dim(cotangent, (1 - c) * share, share, 0)
    g = jnp.concatenate([my_share(cotangent), swap(g_give, "col")], axis=1)
    grad_w_down = dot(hidden, g, (0, 0))
    grad_hidden = dot(g, w_down_all, (1, 1))
    grad_pre_f = grad_hidden * sig * (1.0 + pre_act * (1.0 - sig))
    grad_pre = grad_pre_f.astype(BF)
    grad_b_up = jnp.sum(grad_pre.astype(F32), axis=0)
    grad_w_up = dot(normed_two, grad_pre, (0, 0))
    grad_normed_two = dot(grad_pre, w_up_all, (1, 1))
    weighted = grad_normed_two * gain_two
    inner = jnp.sum(weighted * middle, axis=1, keepdims=True)
    grad_middle = g.astype(F32) + scale_two * weighted - middle * (scale_two**3 * inner / D)
    grad_gain_mlp = jnp.sum(grad_normed_two * middle * scale_two, axis=0)
    grad_branch = grad_middle.astype(BF)
    grad_w_out = dot(att, grad_branch, (1, 0))
    grad_att = dot(w_out_all, grad_branch, (1, 1)).astype(BF)
    grad_attended = to_heads(grad_att).reshape(heads, HEAD_DIM, t)
    grad_middle_block = to_block(grad_middle)

    sum_down = weight_sum(grad_w_down, 0)
    sum_up = weight_sum(grad_w_up, 1)
    sum_out = weight_sum(grad_w_out, 0)

    grad_proj, gscale = attention_backward(
        qkv, raw_q, factor.reshape(HEAD_DIM, 1), attended, grad_attended, lse, masks
    )
    slope = QUERY_CONST / math.sqrt(HEAD_DIM) * jax.nn.sigmoid(query_scale)
    grad_query_scale = jnp.sum(gscale, axis=(0, 2)) * slope
    grad_proj = grad_proj.reshape(3, head_rows, t)
    grad_normed_one = jnp.einsum("sht,sdh->td", grad_proj, w_full, preferred_element_type=F32)
    weighted_one = grad_normed_one * gain_one
    inner_one = jnp.sum(weighted_one * xf, axis=1)
    grad_gain_attn = jnp.sum(grad_normed_one * xf * scale_one, axis=0)
    inner_one = lax.psum(inner_one, ("row", "col"))
    grad_w = jnp.einsum("td,sht->sdh", normed_one, grad_proj, preferred_element_type=F32)
    grad_w = grad_w.reshape(3, cols, 2, feat // 2, head_rows)
    core = lax.axis_index("core")
    keep = lax.dynamic_index_in_dim(grad_w, core, 2, keepdims=False)
    give = lax.dynamic_index_in_dim(grad_w, 1 - core, 2, keepdims=False).astype(BF)
    part = (keep + swap(give, "core").astype(F32)).astype(BF)
    part = jnp.concatenate(flip([part[:, 0], swap(part[:, 1], "col")], "col"), axis=2)
    sum_qkv = jnp.transpose(z_sum(part), (1, 0, 2))

    e = jnp.concatenate(flip(jnp.split(grad_normed_one.astype(BF), 2, axis=0), "row"), axis=0) if rows == 2 else (
        grad_normed_one.astype(BF)
    )
    e = scatter_sum(e, "row", 0)
    e = scatter_sum(e, "col", 1).astype(F32)
    my_rows = lambda y: lax.dynamic_slice_in_dim(y, r * tok, tok, 0)
    scale_mine = my_rows(scale_one)
    inner_mine = my_rows(inner_one.reshape(t, 1))
    grad_inputs = grad_middle_block + scale_mine * (e * gain_attn) - inputs.astype(F32) * (
        scale_mine**3 * inner_mine / D
    )

    grad_b_down = jnp.sum(g.astype(F32), axis=0)
    vectors = jnp.concatenate(
        [
            flip_dim(grad_gain_attn, "col", 0),
            flip_dim(grad_gain_mlp, "col", 0),
            flip_dim(grad_b_down, "col", 0),
            flip_dim(grad_b_up, "row", 0),
            grad_query_scale,
        ]
    )
    vectors = lax.psum(vectors, ("z", "core", "row", "col"))
    mine_col = lambda at: lax.dynamic_slice_in_dim(vectors, at * D + c * feat, feat, 0)
    units = b_up.shape[0]
    return (
        layer_out,
        grad_inputs,
        mine_col(0),
        sum_qkv,
        vectors[4 * D :],
        sum_out,
        mine_col(1),
        sum_up,
        lax.dynamic_slice_in_dim(vectors, 3 * D + r * units, units, 0),
        sum_down,
        mine_col(2),
    )


def solution(mesh):
    dp, rows, cols = mesh.shape["dp"], mesh.shape["row"], mesh.shape["col"]
    split = Mesh(mesh.devices.reshape(dp // 2, 2, rows, cols), ("z", "core", "row", "col"))
    tokens = P(("z", "core", "row"), "col")
    in_specs = (
        tokens,
        P("col"),
        P("col", None, "row"),
        P(),
        P("row", "col"),
        P("col"),
        P("col", "row"),
        P("row"),
        P("row", "col"),
        P("col"),
        P(("z", "core")),
        P(("z", "core")),
        tokens,
    )
    out_specs = (
        tokens,
        tokens,
        P("col"),
        P("col", None, "row"),
        P(),
        P("row", "col"),
        P("col"),
        P("col", "row"),
        P("row"),
        P("row", "col"),
        P("col"),
    )
    return jax.shard_map(body, mesh=split, in_specs=in_specs, out_specs=out_specs, check_vma=False)
```

```python
import functools
import math

import jax
import jax.numpy as jnp
from jax import lax
from jax.experimental import pallas as pl
from jax.experimental.pallas import tpu as pltpu
from jax.sharding import Mesh
from jax.sharding import PartitionSpec as P

D = 1280
HEAD_DIM = 80
EPS = 1e-06
QUERY_CONST = 1.442695041
MASKED = -1e30
BF = jnp.bfloat16
F32 = jnp.float32
VMEM_LIMIT = 50 * 1024 * 1024


def size(axis):
    return lax.axis_size(axis)


def swap(x, axis):
    return lax.ppermute(x, axis, [(0, 1), (1, 0)])


def flip(blocks, axis):
    if size(axis) != 2:
        return list(blocks)
    first = lax.axis_index(axis) == 0
    a, b = blocks
    return [jnp.where(first, a, b), jnp.where(first, b, a)]


def flip_dim(x, axis, dim):
    if size(axis) != 2:
        return x
    return jnp.concatenate(flip(jnp.split(x, 2, axis=dim), axis), axis=dim)


def gather(x, axis):
    if size(axis) == 2:
        return [x, swap(x, axis)]
    whole = lax.all_gather(x, axis, axis=0, tiled=False)
    return [whole[i] for i in range(size(axis))]


def gather_grid(x):
    if size("row") != 2:
        return [gather(b, "col") for b in gather(x, "row")]
    along_row, along_col = swap(x, "row"), swap(x, "col")
    half = x.shape[0] // 2
    across = jnp.concatenate(
        [swap(along_row[:half], "col"), swap(along_col[half:], "row")], axis=0
    )
    return [[x, along_col], [along_row, across]]


def scatter_sum(x, axis, dim):
    if size(axis) != 2:
        return lax.psum_scatter(x, axis, scatter_dimension=dim, tiled=True)
    mine, theirs = jnp.split(x, 2, axis=dim)
    return (mine.astype(F32) + swap(theirs, axis).astype(F32)).astype(x.dtype)


def exchange(x, axis, split, join):
    if size(axis) != 2:
        return lax.all_to_all(x, axis, split, join, tiled=True)
    mine, theirs = jnp.split(x, 2, axis=split)
    return jnp.concatenate([mine, swap(theirs, axis)], axis=join)


def core_half(x, dim):
    return lax.dynamic_slice_in_dim(
        x, lax.axis_index("core") * (x.shape[dim] // 2), x.shape[dim] // 2, dim
    )


def weight_gather(w, row_dim):
    part = core_half(w, 0)
    blocks = gather_grid(part)
    if row_dim == 1:
        blocks = [list(b) for b in zip(*blocks)]
    mine = jnp.stack([jnp.concatenate(b, axis=1) for b in blocks])
    other = swap(mine, "core")
    first = lax.axis_index("core") == 0
    both = jnp.stack([jnp.where(first, mine, other), jnp.where(first, other, mine)], axis=1)
    return both.reshape(-1, both.shape[-1])


def weight_sum(g, row_dim):
    dim_axis = ("row", "col") if row_dim == 0 else ("col", "row")
    n0 = size(dim_axis[0])
    g = g.reshape(n0, 2, g.shape[0] // n0 // 2, g.shape[1])
    core = lax.axis_index("core")
    keep = lax.dynamic_index_in_dim(g, core, 1, keepdims=False)
    give = lax.dynamic_index_in_dim(g, 1 - core, 1, keepdims=False).astype(BF)
    part = (keep + swap(give, "core").astype(F32)).astype(BF)
    part = scatter_sum(part, dim_axis[0], 0)
    part = scatter_sum(part[0], dim_axis[1], 1)
    return z_sum(part)


def z_sum(part):
    total = lax.psum(part, "z")
    other = swap(total, "core")
    return flip_core(total, other)


def flip_core(total, other):
    first = lax.axis_index("core") == 0
    return jnp.concatenate(
        [jnp.where(first, total, other), jnp.where(first, other, total)], axis=-2
    ).astype(F32)


def dot(a, b, contract):
    return lax.dot_general(a, b, ((contract[0:1], contract[1:2]), ((), ())), preferred_element_type=F32)


def bias_block(series_row, series_col, key_pos, q0, k0, qb, kb, diagonal):
    q_pos = q0 + lax.broadcasted_iota(jnp.int32, (1, qb), 1)
    allowed = (series_col == series_row) & (key_pos <= q_pos)
    if diagonal:
        k_pos = k0 + lax.broadcasted_iota(jnp.int32, (kb, 1), 0)
        allowed = allowed | (k_pos == q_pos)
    return jnp.where(allowed, 0.0, MASKED)


def forward_kernel(block, qkv_ref, srow_ref, scol_ref, kpos_ref, out_ref, lse_ref, bias_ref, krow_ref, s_ref):
    t = qkv_ref.shape[3]
    n = t // block
    krow_ref[...] = qkv_ref[1, 0].astype(F32).T.astype(BF)

    def bias_slot(j, i):
        return j * (j + 1) // 2 + i

    @pl.when(pl.program_id(0) == 0)
    def _():
        for j in range(n):
            for i in range(j + 1):
                keys = pl.ds(i * block, block)
                bias_ref[bias_slot(j, i)] = bias_block(
                    srow_ref[:, j * block : (j + 1) * block],
                    scol_ref[keys, :],
                    kpos_ref[keys, :],
                    j * block,
                    i * block,
                    block,
                    block,
                    i == j,
                )

    for j in range(n):
        cols = slice(j * block, (j + 1) * block)
        q = qkv_ref[0, 0, :, cols]
        top = None
        for i in range(j + 1):
            s = dot(krow_ref[i * block : (i + 1) * block, :], q, (1, 0)) + bias_ref[bias_slot(j, i)]
            s_ref[i * block : (i + 1) * block, :] = s
            here = jnp.max(s, axis=0, keepdims=True)
            top = here if top is None else jnp.maximum(top, here)
        total = jnp.zeros((1, block), F32)
        acc = jnp.zeros((HEAD_DIM, block), F32)
        for i in range(j + 1):
            p = jnp.exp(s_ref[i * block : (i + 1) * block, :] - top)
            total += jnp.sum(p, axis=0, keepdims=True)
            acc += dot(qkv_ref[2, 0, :, i * block : (i + 1) * block], p.astype(BF), (1, 0))
        out_ref[0, :, cols] = (acc / total).astype(BF)
        lse_ref[0, :, cols] = top + jnp.log(total)


def backward_kernel(
    block, qkv_ref, raw_ref, factor_ref, out_ref, gout_ref, lse_ref, srow_ref, scol_ref, kpos_ref,
    grad_ref, gscale_ref, bias_ref, krow_ref, vrow_ref, gk_ref, gv_ref,
):
    t = qkv_ref.shape[3]
    n = t // block
    krow_ref[...] = qkv_ref[1, 0].astype(F32).T.astype(BF)
    vrow_ref[...] = qkv_ref[2, 0].astype(F32).T.astype(BF)

    def bias_slot(j, i):
        return j * (j + 1) // 2 + i

    @pl.when(pl.program_id(0) == 0)
    def _():
        for j in range(n):
            for i in range(j + 1):
                keys = pl.ds(i * block, block)
                bias_ref[bias_slot(j, i)] = bias_block(
                    srow_ref[:, j * block : (j + 1) * block],
                    scol_ref[keys, :],
                    kpos_ref[keys, :],
                    j * block,
                    i * block,
                    block,
                    block,
                    i == j,
                )

    gscale = jnp.zeros((HEAD_DIM, 1), F32)
    for j in range(n):
        cols = slice(j * block, (j + 1) * block)
        q = qkv_ref[0, 0, :, cols]
        go = gout_ref[0, :, cols]
        lse = lse_ref[0, :, cols]
        delta = jnp.sum(go.astype(F32) * out_ref[0, :, cols].astype(F32), axis=0, keepdims=True)
        gq = jnp.zeros((HEAD_DIM, block), F32)
        for i in range(j + 1):
            keys = slice(i * block, (i + 1) * block)
            s = dot(krow_ref[keys, :], q, (1, 0)) + bias_ref[bias_slot(j, i)]
            p = jnp.exp(s - lse)
            gp = dot(vrow_ref[keys, :], go, (1, 0))
            gs = (p * (gp - delta)).astype(BF)
            gq += dot(qkv_ref[1, 0, :, keys], gs, (1, 0))
            gk = dot(q, gs, (1, 1))
            gv = dot(go, p.astype(BF), (1, 1))
            if i == j:
                gk_ref[:, keys] = gk
                gv_ref[:, keys] = gv
            else:
                gk_ref[:, keys] += gk
                gv_ref[:, keys] += gv
        gscale += jnp.sum(gq * raw_ref[0, :, cols], axis=1, keepdims=True)
        grad_ref[0, 0, :, cols] = (gq * factor_ref[...]).astype(BF)
    grad_ref[1, 0] = gk_ref[...].astype(BF)
    grad_ref[2, 0] = gv_ref[...].astype(BF)
    gscale_ref[0] = gscale


def mask_args(series, padding):
    t = series.shape[0]
    pos = jnp.arange(t, dtype=jnp.int32)
    return series.reshape(1, t), series.reshape(t, 1), jnp.where(padding == 0, pos, t).reshape(t, 1)


def attention_forward(qkv, masks):
    _, heads, hd, t = qkv.shape
    block = min(256, t) if t <= 2048 else 512
    n = t // block
    whole = lambda shape: pl.BlockSpec(shape, lambda h: (0,) * len(shape))
    return pl.pallas_call(
        functools.partial(forward_kernel, block),
        grid=(heads,),
        in_specs=[
            pl.BlockSpec((3, 1, hd, t), lambda h: (0, h, 0, 0)),
            whole((1, t)),
            whole((t, 1)),
            whole((t, 1)),
        ],
        out_specs=[
            pl.BlockSpec((1, hd, t), lambda h: (h, 0, 0)),
            pl.BlockSpec((1, 1, t), lambda h: (h, 0, 0)),
        ],
        out_shape=[
            jax.ShapeDtypeStruct((heads, hd, t), BF),
            jax.ShapeDtypeStruct((heads, 1, t), F32),
        ],
        scratch_shapes=[
            pltpu.VMEM((n * (n + 1) // 2, block, block), F32),
            pltpu.VMEM((t, hd), BF),
            pltpu.VMEM((t, block), F32),
        ],
        compiler_params=pltpu.CompilerParams(vmem_limit_bytes=VMEM_LIMIT),
        cost_estimate=pl.CostEstimate(
            flops=heads * 4 * t * t * 128, bytes_accessed=heads * hd * t * 8, transcendentals=heads * t * t // 2
        ),
        name="attention_forward",
    )(qkv, *masks)


def attention_backward(qkv, raw, factor, out, gout, lse, masks):
    _, heads, hd, t = qkv.shape
    block = min(256, t) if t <= 2048 else 512
    n = t // block
    whole = lambda shape: pl.BlockSpec(shape, lambda h: (0,) * len(shape))
    head = lambda: pl.BlockSpec((1, hd, t), lambda h: (h, 0, 0))
    return pl.pallas_call(
        functools.partial(backward_kernel, block),
        grid=(heads,),
        in_specs=[
            pl.BlockSpec((3, 1, hd, t), lambda h: (0, h, 0, 0)),
            head(),
            whole((hd, 1)),
            head(),
            head(),
            pl.BlockSpec((1, 1, t), lambda h: (h, 0, 0)),
            whole((1, t)),
            whole((t, 1)),
            whole((t, 1)),
        ],
        out_specs=[
            pl.BlockSpec((3, 1, hd, t), lambda h: (0, h, 0, 0)),
            pl.BlockSpec((1, hd, 1), lambda h: (h, 0, 0)),
        ],
        out_shape=[
            jax.ShapeDtypeStruct((3, heads, hd, t), BF),
            jax.ShapeDtypeStruct((heads, hd, 1), F32),
        ],
        scratch_shapes=[
            pltpu.VMEM((n * (n + 1) // 2, block, block), F32),
            pltpu.VMEM((t, hd), BF),
            pltpu.VMEM((t, hd), BF),
            pltpu.VMEM((hd, t), F32),
            pltpu.VMEM((hd, t), F32),
        ],
        compiler_params=pltpu.CompilerParams(vmem_limit_bytes=VMEM_LIMIT),
        cost_estimate=pl.CostEstimate(
            flops=heads * 10 * t * t * 128, bytes_accessed=heads * hd * t * 20, transcendentals=heads * t * t // 2
        ),
        name="attention_backward",
    )(qkv, raw, factor, out, gout, lse, *masks)


def norm_scale(x):
    return lax.rsqrt(jnp.mean(x * x, axis=1, keepdims=True) + EPS)


def body_any(
    inputs, gain_attn, w_qkv, query_scale, w_out, gain_mlp, w_up, b_up, w_down, b_down, series_ids, pad_mask, cotangent
):
    rows, cols = size("row"), size("col")
    tok = inputs.shape[0]
    feat = inputs.shape[1]
    share = tok // cols
    t = series_ids.shape[0]
    head_rows = w_qkv.shape[2] // cols
    heads = head_rows // HEAD_DIM
    r, c = lax.axis_index("row"), lax.axis_index("col")

    blocks = gather_grid(inputs)
    strips = [jnp.concatenate(b, axis=1) for b in blocks]
    x_own = strips[0] if rows == 2 else lax.dynamic_index_in_dim(jnp.stack(strips), r, 0, keepdims=False)
    x_all = jnp.concatenate(flip(strips, "row"), axis=0)
    gain_one = jnp.concatenate(gather(gain_attn, "col"))
    gain_two = jnp.concatenate(gather(gain_mlp, "col"))
    bias_up = jnp.concatenate(gather(b_up, "row")).astype(F32)
    bias_down = jnp.concatenate(gather(b_down, "col")).astype(F32)

    w3 = jnp.transpose(w_qkv, (1, 0, 2)).reshape(3, feat, cols, head_rows)
    w_mine = lax.dynamic_index_in_dim(w3, c, 2, keepdims=False)
    w_give = lax.dynamic_index_in_dim(w3, 1 - c, 2, keepdims=False)
    w_half = swap(core_half(w_give, 1), "col")
    w_other = swap(w_half, "core")
    first = lax.axis_index("core") == 0
    w_full = jnp.concatenate(
        [w_mine, jnp.where(first, w_half, w_other), jnp.where(first, w_other, w_half)], axis=1
    )

    xf = x_all.astype(F32)
    scale_one = norm_scale(xf)
    normed_one = (xf * scale_one * gain_one).astype(BF)
    projected = jnp.einsum("td,sdh->sht", normed_one, w_full, preferred_element_type=F32)
    projected = projected.reshape(3, heads, HEAD_DIM, t)
    factor = QUERY_CONST / math.sqrt(HEAD_DIM) * jax.nn.softplus(query_scale)
    raw_q = projected[0]
    qkv = jnp.stack([raw_q * factor[None, :, None], projected[1], projected[2]]).astype(BF)
    masks = mask_args(series_ids, pad_mask)
    attended, lse = attention_forward(qkv, masks)

    def to_tokens(y):
        y = flip_dim(y.reshape(head_rows, rows, cols, share), "row", 1)
        y = flip_dim(y, "col", 2)
        y = exchange(y.reshape(1, head_rows, rows, cols, share), "row", 2, 0)
        y = exchange(y.reshape(rows, 1, head_rows, cols, share), "col", 3, 1)
        y = flip_dim(y.reshape(rows, cols, head_rows, share), "col", 1)
        return y.reshape(rows * cols * head_rows, share)

    def to_heads(y):
        y = flip_dim(y.reshape(rows, cols, head_rows, share), "col", 1)
        y = exchange(y.reshape(rows, cols, head_rows, 1, share), "col", 1, 3)
        y = exchange(y.reshape(rows, head_rows, 1, cols, share), "row", 0, 2)
        y = flip_dim(y.reshape(head_rows, rows, cols, share), "col", 2)
        return flip_dim(y, "row", 1).reshape(head_rows, t)

    w_out_all = weight_gather(w_out, 0)
    w_up_all = weight_gather(w_up, 1)
    w_down_all = weight_gather(w_down, 0)

    def my_share(y):
        return lax.dynamic_slice_in_dim(y, c * share, share, 0)

    att = to_tokens(attended.reshape(head_rows, t))
    x_mine = my_share(x_own).astype(F32)
    middle = x_mine + dot(att, w_out_all, (0, 0))
    scale_two = norm_scale(middle)
    normed_two = (middle * scale_two * gain_two).astype(BF)
    pre_act = dot(normed_two, w_up_all, (1, 0)) + bias_up
    sig = jax.nn.sigmoid(pre_act)
    hidden = (pre_act * sig).astype(BF)
    result = (middle + dot(hidden, w_down_all, (1, 0)) + bias_down).astype(BF)

    def to_block(y):
        mine, theirs = jnp.split(y, 2, axis=1)
        return jnp.concatenate(flip([mine, swap(theirs, "col")], "col"), axis=0)

    layer_out = to_block(result)

    g_give = lax.dynamic_slice_in_dim(cotangent, (1 - c) * share, share, 0)
    g = jnp.concatenate([my_share(cotangent), swap(g_give, "col")], axis=1)
    grad_w_down = dot(hidden, g, (0, 0))
    grad_hidden = dot(g, w_down_all, (1, 1))
    grad_pre_f = grad_hidden * sig * (1.0 + pre_act * (1.0 - sig))
    grad_pre = grad_pre_f.astype(BF)
    grad_b_up = jnp.sum(grad_pre.astype(F32), axis=0)
    grad_w_up = dot(normed_two, grad_pre, (0, 0))
    grad_normed_two = dot(grad_pre, w_up_all, (1, 1))
    weighted = grad_normed_two * gain_two
    inner = jnp.sum(weighted * middle, axis=1, keepdims=True)
    grad_middle = g.astype(F32) + scale_two * weighted - middle * (scale_two**3 * inner / D)
    grad_gain_mlp = jnp.sum(grad_normed_two * middle * scale_two, axis=0)
    grad_branch = grad_middle.astype(BF)
    grad_w_out = dot(att, grad_branch, (1, 0))
    grad_att = dot(w_out_all, grad_branch, (1, 1)).astype(BF)
    grad_attended = to_heads(grad_att).reshape(heads, HEAD_DIM, t)
    grad_middle_block = to_block(grad_middle)

    sum_down = weight_sum(grad_w_down, 0)
    sum_up = weight_sum(grad_w_up, 1)
    sum_out = weight_sum(grad_w_out, 0)

    grad_proj, gscale = attention_backward(
        qkv, raw_q, factor.reshape(HEAD_DIM, 1), attended, grad_attended, lse, masks
    )
    slope = QUERY_CONST / math.sqrt(HEAD_DIM) * jax.nn.sigmoid(query_scale)
    grad_query_scale = jnp.sum(gscale, axis=(0, 2)) * slope
    grad_proj = grad_proj.reshape(3, head_rows, t)
    grad_normed_one = jnp.einsum("sht,sdh->td", grad_proj, w_full, preferred_element_type=F32)
    weighted_one = grad_normed_one * gain_one
    inner_one = jnp.sum(weighted_one * xf, axis=1)
    grad_gain_attn = jnp.sum(grad_normed_one * xf * scale_one, axis=0)
    inner_one = lax.psum(inner_one, ("row", "col"))
    grad_w = jnp.einsum("td,sht->sdh", normed_one, grad_proj, preferred_element_type=F32)
    grad_w = grad_w.reshape(3, cols, 2, feat // 2, head_rows)
    core = lax.axis_index("core")
    keep = lax.dynamic_index_in_dim(grad_w, core, 2, keepdims=False)
    give = lax.dynamic_index_in_dim(grad_w, 1 - core, 2, keepdims=False).astype(BF)
    part = (keep + swap(give, "core").astype(F32)).astype(BF)
    part = jnp.concatenate(flip([part[:, 0], swap(part[:, 1], "col")], "col"), axis=2)
    sum_qkv = jnp.transpose(z_sum(part), (1, 0, 2))

    e = jnp.concatenate(flip(jnp.split(grad_normed_one.astype(BF), 2, axis=0), "row"), axis=0) if rows == 2 else (
        grad_normed_one.astype(BF)
    )
    e = scatter_sum(e, "row", 0)
    e = scatter_sum(e, "col", 1).astype(F32)
    my_rows = lambda y: lax.dynamic_slice_in_dim(y, r * tok, tok, 0)
    scale_mine = my_rows(scale_one)
    inner_mine = my_rows(inner_one.reshape(t, 1))
    grad_inputs = grad_middle_block + scale_mine * (e * gain_attn) - inputs.astype(F32) * (
        scale_mine**3 * inner_mine / D
    )

    grad_b_down = jnp.sum(g.astype(F32), axis=0)
    vectors = jnp.concatenate(
        [
            flip_dim(grad_gain_attn, "col", 0),
            flip_dim(grad_gain_mlp, "col", 0),
            flip_dim(grad_b_down, "col", 0),
            flip_dim(grad_b_up, "row", 0),
            grad_query_scale,
        ]
    )
    vectors = lax.psum(vectors, ("z", "core", "row", "col"))
    mine_col = lambda at: lax.dynamic_slice_in_dim(vectors, at * D + c * feat, feat, 0)
    units = b_up.shape[0]
    return (
        layer_out,
        grad_inputs,
        mine_col(0),
        sum_qkv,
        vectors[4 * D :],
        sum_out,
        mine_col(1),
        sum_up,
        lax.dynamic_slice_in_dim(vectors, 3 * D + r * units, units, 0),
        sum_down,
        mine_col(2),
    )


SMEM = pl.BlockSpec(memory_space=pltpu.SMEM)
ANY = pl.BlockSpec(memory_space=pl.ANY)


def call(kernel, name, args, specs, outs, scratch=(), flops=0, **more):
    return pl.pallas_call(
        kernel,
        in_specs=specs,
        out_shape=outs,
        scratch_shapes=list(scratch),
        compiler_params=pltpu.CompilerParams(vmem_limit_bytes=VMEM_LIMIT),
        cost_estimate=pl.CostEstimate(flops=flops, bytes_accessed=8 << 20, transcendentals=0),
        name=name,
        **more,
    )(*args)


VM = pl.BlockSpec(memory_space=pltpu.VMEM)


def shape(dims, kind):
    return jax.ShapeDtypeStruct(dims, kind)


def project_kernel(
    at, x00, x01, x10, x11, gain, factor, w_mine, w_a, w_b, qkv, raw, normed, scale_own, w_full
):
    r, k = at[0], at[2]
    tok, feat = x00.shape
    hr = w_mine.shape[1]
    half = hr // 2
    for s in range(3):
        w_full[pl.ds(s * hr, hr), 0:feat] = w_mine[s]
        w_full[pl.ds(pl.multiple_of(s * hr + k * half, 16), half), feat:] = w_a[s]
        w_full[pl.ds(pl.multiple_of(s * hr + (1 - k) * half, 16), half), feat:] = w_b[s]
    for i, (a_ref, b_ref) in enumerate(((x00, x01), (x10, x11))):
        a, b = a_ref[...].astype(F32), b_ref[...].astype(F32)
        total = jnp.sum(a * a, axis=1, keepdims=True) + jnp.sum(b * b, axis=1, keepdims=True)
        scale = lax.rsqrt(total / (2 * feat) + EPS)
        if i == 0:
            scale_own[...] = scale
        rows = pl.ds(pl.multiple_of((r ^ i) * tok, tok), tok)
        normed[rows, 0:feat] = (a * scale * gain[:, 0:feat]).astype(BF)
        normed[rows, feat:] = (b * scale * gain[:, feat:]).astype(BF)
        y = normed[rows, :]
        q = dot(w_full[0:hr, :], y, (1, 1))
        raw[:, rows] = q
        qkv[0, :, rows] = (q * factor[...]).astype(BF)
        qkv[1, :, rows] = dot(w_full[hr : 2 * hr, :], y, (1, 1)).astype(BF)
        qkv[2, :, rows] = dot(w_full[2 * hr : 3 * hr, :], y, (1, 1)).astype(BF)


def feed_kernel(
    at, a0, a1, a2, a3, x_own, x_col, g_own, g_col, gain, bias_up, bias_down,
    w_out, w_up, w_down, hx, hy, d0, d1, hx2, hy2, d02, d12,
    out_own, out_give, gm_own, gm_give, keep, give, t0, t1, t2, t3, vectors,
    w, att, turned, sems,
):
    r, c, k = at[0], at[1], at[2]
    hr, share = a0.shape
    feat = x_own.shape[1]
    half = feat // 2
    quarter = half // 2
    copies = []
    for n, shard in enumerate((w_out, w_up, w_down)):
        rx, cx, ry, cy = (0, feat, feat, 0) if n == 1 else (feat, 0, 0, feat)
        mine = []
        mine.append((shard, w.at[n, 0:feat, 0:feat]))
        for core, (px, py, p0, p1) in ((k, (hx, hy, d0, d1)), (1 - k, (hx2, hy2, d02, d12))):
            down = core * half
            at_x = pl.ds(pl.multiple_of(rx + down, 16), half)
            at_y = pl.ds(pl.multiple_of(ry + down, 16), half)
            at_0 = pl.ds(pl.multiple_of(feat + down, 16), quarter)
            at_1 = pl.ds(pl.multiple_of(feat + down + quarter, 16), quarter)
            mine.append((px.at[n], w.at[n, at_x, cx : cx + feat]))
            mine.append((py.at[n], w.at[n, at_y, cy : cy + feat]))
            mine.append((p0.at[n], w.at[n, at_0, feat : 2 * feat]))
            mine.append((p1.at[n], w.at[n, at_1, feat : 2 * feat]))
        started = []
        for m, (src, dst) in enumerate(mine):
            copy = pltpu.make_async_copy(src, dst, sems.at[n, m])
            copy.start()
            started.append(copy)
        copies.append(started)

    rows = pl.ds(pl.multiple_of(c * share, share), share)
    for s, a in enumerate((a0, a1, a2, a3)):
        to = (s // 2) * 2 * hr + (c ^ (s % 2)) * hr
        att[pl.ds(pl.multiple_of(to, 16), hr), :] = a[...]
    x = jnp.concatenate([x_own[rows, :], x_col[rows, :]], axis=1).astype(F32)
    g = jnp.concatenate([g_own[rows, :], g_col[...]], axis=1)
    for copy in copies[0]:
        copy.wait()
    middle = x + dot(att[...], w[0], (0, 0))
    scale = lax.rsqrt(jnp.sum(middle * middle, axis=1, keepdims=True) / D + EPS)
    normed = (middle * scale * gain[...]).astype(BF)
    for copy in copies[1]:
        copy.wait()
    pre = dot(normed, w[1], (1, 0)) + bias_up[...]
    sig = jax.nn.sigmoid(pre)
    hidden = (pre * sig).astype(BF)
    for copy in copies[2]:
        copy.wait()
    result = (middle + dot(hidden, w[2], (1, 0)) + bias_down[...]).astype(BF)
    out_own[...] = result[:, :feat]
    out_give[...] = result[:, feat:]

    def weight_grad(n, left_ref, right):
        for b in range(2):
            for ref, core in ((keep, k), (give, 1 - k)):
                part = pl.ds(pl.multiple_of(b * feat + core * half, 16), half)
                ref[n, b] = dot(left_ref[part, :], right, (1, 0)).astype(BF)

    turned[...] = hidden.astype(F32).T.astype(BF)
    grad_pre_f = dot(g, w[2], (1, 1)) * sig * (1.0 + pre * (1.0 - sig))
    grad_pre = grad_pre_f.astype(BF)
    weight_grad(2, turned, g)
    grad_normed = dot(grad_pre, w[1], (1, 1))
    weighted = grad_normed * gain[...]
    inner = jnp.sum(weighted * middle, axis=1, keepdims=True)
    gf = g.astype(F32)
    grad_middle = gf + scale * weighted - middle * (scale * scale * scale * inner / D)
    gm_own[...] = grad_middle[:, :feat]
    gm_give[...] = grad_middle[:, feat:].astype(BF)
    branch = grad_middle.astype(BF)
    for s, t in enumerate((t0, t1, t2, t3)):
        come = (s // 2) * 2 * hr + (c ^ (s % 2)) * hr
        t[...] = dot(w[0, pl.ds(pl.multiple_of(come, 16), hr), :], branch, (1, 1)).astype(BF)
    turned[...] = normed.astype(F32).T.astype(BF)
    weight_grad(1, turned, grad_pre)
    weight_grad(0, att, branch)
    vectors[...] = jnp.concatenate(
        [
            jnp.sum(grad_normed * (middle * scale), axis=0, keepdims=True),
            jnp.sum(gf, axis=0, keepdims=True),
            jnp.sum(grad_pre.astype(F32), axis=0, keepdims=True),
        ],
        axis=0,
    )


def project_back_kernel(
    at, grad, w_full, normed, x00, x01, x10, x11, gain, keep, give, e0, e1, e2, e3, inner_own, gain_sum
):
    r, k = at[0], at[2]
    tok, feat = x00.shape
    hr = grad.shape[0] // 3
    half = hr // 2
    for ref, core in ((give, 1 - k), (keep, k)):
        for s in range(3):
            part = pl.ds(pl.multiple_of(s * hr + core * half, 16), half)
            ref[s] = dot(grad[part, :], normed[...], (1, 0)).astype(BF)
    sums = [jnp.zeros((1, feat), F32), jnp.zeros((1, feat), F32)]
    for i, (xs, es) in enumerate((((x00, x01), (e0, e1)), ((x10, x11), (e2, e3)))):
        rows = pl.ds(pl.multiple_of((r ^ i) * tok, tok), tok)
        left = grad[:, rows]
        es_f, squares, inner = [], 0.0, 0.0
        for j in range(2):
            cut = slice(j * feat, (j + 1) * feat)
            e = dot(left, w_full[:, cut], (0, 0))
            x = xs[j][...].astype(F32)
            inner = inner + jnp.sum(e * gain[:, cut] * x, axis=1, keepdims=True)
            squares = squares + jnp.sum(x * x, axis=1, keepdims=True)
            es[j][0:tok, :] = e.astype(es[j].dtype)
            es_f.append(e * x)
        scale = lax.rsqrt(squares / (2 * feat) + EPS)
        for j in range(2):
            sums[j] += jnp.sum(es_f[j] * scale, axis=0, keepdims=True)
        line = jnp.broadcast_to(inner, (tok, 128)).T[0:1, :]
        high = line.astype(BF).astype(F32)
        extra = jnp.concatenate([high, line - high, jnp.zeros((14, tok), F32)], axis=0)
        extra = jnp.concatenate([extra, jnp.zeros((16, feat - tok), F32)], axis=1).astype(BF)
        if i == 0:
            inner_own[...] = inner
            es[1][tok:, :] = extra
        else:
            es[0][tok:, :] = extra
            es[1][tok:, :] = extra
    gain_sum[:, 0:feat] = sums[0]
    gain_sum[:, feat:] = sums[1]


def after(x, *earlier):
    return lax.optimization_barrier((x, *earlier))[0]


def diagonal(x):
    return lax.ppermute(x, ("row", "col"), [(0, 3), (1, 2), (2, 1), (3, 0)])


def z_swap(x, step):
    n = size("z")
    return lax.ppermute(x, "z", [(i, i ^ step) for i in range(n)])


def body_four(
    inputs, gain_attn, w_qkv, query_scale, w_out, gain_mlp, w_up, b_up, w_down, b_down, series_ids, pad_mask, cotangent
):
    tok, feat = inputs.shape
    share = tok // 2
    t = series_ids.shape[0]
    hr = w_qkv.shape[2] // 2
    heads = hr // HEAD_DIM
    half = feat // 2
    r, c, k = lax.axis_index("row"), lax.axis_index("col"), lax.axis_index("core")
    at = jnp.stack([r, c, k, 2 * r + c]).astype(jnp.int32)
    mine_rows = lambda y, part: lax.dynamic_slice_in_dim(y, part * share, share, 0)

    x01 = swap(inputs, "col")
    x10 = swap(inputs, "row")
    small = swap(jnp.concatenate([gain_attn, gain_mlp, b_down.astype(F32)]), "col")
    up_other = swap(b_up.astype(F32), "row")
    x11 = swap(x01, "row")
    w_turned = jnp.transpose(w_qkv, (1, 2, 0)).reshape(3, 2, hr, feat)
    w_mine = lax.dynamic_index_in_dim(w_turned, c, 1, keepdims=False)
    w_give = lax.dynamic_index_in_dim(w_turned, 1 - c, 1, keepdims=False)
    w_a = swap(core_half(w_give, 1), "col")
    w_b = swap(w_a, "core")
    gain_one = jnp.concatenate([gain_attn, small[:feat]]).reshape(1, D)
    gain_two = jnp.concatenate([gain_mlp, small[feat : 2 * feat]]).reshape(1, D)
    bias_down = jnp.concatenate([b_down.astype(F32), small[2 * feat :]]).reshape(1, D)
    bias_up = jnp.concatenate([b_up.astype(F32), up_other]).reshape(1, D)
    factor = QUERY_CONST / math.sqrt(HEAD_DIM) * jax.nn.softplus(query_scale)
    factor_col = factor.reshape(HEAD_DIM, 1)

    part = jnp.stack([core_half(w_out, 0), core_half(w_up, 0), core_half(w_down, 0)])
    part = after(part, x11, w_a)
    hx, hy = swap(part, "row"), swap(part, "col")
    hx2, hy2 = swap(hx, "core"), swap(hy, "core")
    d0 = swap(hx[:, : half // 2], "col")
    d1 = swap(hy[:, half // 2 :], "row")
    d02, d12 = swap(d0, "core"), swap(d1, "core")
    g_col = swap(after(mine_rows(cotangent, 1 - c), x11, w_a), "col")

    qkv, raw, normed_one, scale_own, w_full = call(
        project_kernel,
        "project",
        (at, inputs, x01, x10, x11, gain_one, jnp.tile(factor_col, (heads, 1)), w_mine, w_a, w_b),
        [SMEM] + [VM] * 9,
        [
            shape((3, hr, t), BF),
            shape((hr, t), F32),
            shape((t, D), BF),
            shape((tok, 1), F32),
            shape((3 * hr, D), BF),
        ],
        flops=6 * t * D * hr,
    )
    qkv = qkv.reshape(3, heads, HEAD_DIM, t)
    masks = mask_args(series_ids, pad_mask)
    attended, lse = attention_forward(qkv, masks)
    own = attended.reshape(hr, t)
    cut = lambda y, slot: lax.dynamic_slice_in_dim(y, (at[3] ^ slot) * share, share, 1)
    a1, a2, a3 = swap(cut(own, 1), "col"), swap(cut(own, 2), "row"), diagonal(cut(own, 3))
    out_own, out_give, gm_own, gm_give, keep, give, t0, t1, t2, t3, vectors = call(
        feed_kernel,
        "feed_forward",
        (at, cut(own, 0), a1, a2, a3, inputs, x01, cotangent, g_col, gain_two, bias_up, bias_down)
        + (w_out, w_up, w_down, hx, hy, d0, d1, hx2, hy2, d02, d12),
        [SMEM] + [VM] * 11 + [ANY] * 11,
        [
            shape((share, feat), BF),
            shape((share, feat), BF),
            shape((share, feat), F32),
            shape((share, feat), BF),
            shape((3, 2, half, D), BF),
            shape((3, 2, half, D), BF),
        ]
        + [shape((hr, share), BF)] * 4
        + [shape((3, D), F32)],
        scratch=[
            pltpu.VMEM((3, D, D), BF),
            pltpu.VMEM((D, share), BF),
            pltpu.VMEM((D, share), BF),
            pltpu.SemaphoreType.DMA((3, 9)),
        ],
        flops=18 * share * D * D,
    )
    t1, t2, t3 = swap(t1, "col"), swap(t2, "row"), diagonal(t3)
    got = swap(give, "core")
    pair = (keep.astype(F32) + got.astype(F32)).astype(BF)
    s_row = swap(pair[0::2, 1], "row")
    s_col = swap(pair[1, 1], "col")
    one = (pair[0::2, 0].astype(F32) + s_row.astype(F32)).astype(BF)
    two = (pair[1, 0].astype(F32) + s_col.astype(F32)).astype(BF)
    one = (one[:, :, :feat].astype(F32) + swap(one[:, :, feat:], "col").astype(F32)).astype(BF)
    two = (two[:, :feat].astype(F32) + swap(two[:, feat:], "row").astype(F32)).astype(BF)
    feed_sum = lax.psum(jnp.concatenate([one, two[None]]), "z")
    feed_sum = flip_core(feed_sum, swap(feed_sum, "core"))
    flat = [t0, t1, t2, t3]
    grad_attended = jnp.stack(flat).reshape(4, heads, HEAD_DIM, share)
    order = jnp.arange(4) ^ at[3]
    grad_attended = jnp.transpose(jnp.take(grad_attended, order, axis=0), (1, 2, 0, 3)).reshape(heads, HEAD_DIM, t)

    grad_proj, gscale = attention_backward(
        qkv, raw.reshape(heads, HEAD_DIM, t), factor_col, attended, grad_attended, lse, masks
    )
    slope = QUERY_CONST / math.sqrt(HEAD_DIM) * jax.nn.sigmoid(query_scale)
    grad_query_scale = jnp.sum(gscale, axis=(0, 2)) * slope
    w_keep, w_send, e0, e1, e2, e3, inner, gain_sum = call(
        project_back_kernel,
        "project_back",
        (at, grad_proj.reshape(3 * hr, t), w_full, normed_one, inputs, x01, x10, x11, gain_one),
        [SMEM] + [VM] * 8,
        [
            shape((3, hr // 2, D), BF),
            shape((3, hr // 2, D), BF),
            shape((tok, feat), F32),
            shape((tok + 16, feat), BF),
            shape((tok + 16, feat), BF),
            shape((tok + 16, feat), BF),
            shape((tok, 1), F32),
            shape((1, D), F32),
        ],
        flops=12 * t * D * hr,
    )
    w_pair = (w_keep.astype(F32) + swap(w_send, "core").astype(F32)).astype(BF)
    w_pair = flip([w_pair[:, :, :feat], swap(w_pair[:, :, feat:], "col")], "col")
    w_pair = jnp.stack(w_pair, axis=1)
    w_sum = lax.psum(w_pair, "z")
    w_other = swap(w_sum, "core")
    first = k == 0
    w_sum = jnp.stack([jnp.where(first, w_sum, w_other), jnp.where(first, w_other, w_sum)], axis=2)
    sum_qkv = jnp.transpose(w_sum.reshape(3, 2 * hr, feat), (2, 0, 1)).astype(F32)

    e1, e2, e3 = [after(e, w_pair) for e in (e1, e2, e3)]
    e1, e2, e3 = swap(e1, "col"), swap(e2, "row"), diagonal(e3)
    e = e0
    for more in (e1, e2, e3):
        e = e + more[:tok].astype(F32)
        inner = inner + jnp.sum(more[tok : tok + 2, :tok].astype(F32), axis=0).reshape(tok, 1)
    gm_col = swap(gm_give, "col").astype(F32)
    grad_middle = jnp.concatenate(flip([gm_own, gm_col], "col"), axis=0)
    grad_inputs = grad_middle + scale_own * (e * gain_attn) - inputs.astype(F32) * (scale_own**3 * inner / D)
    layer_out = jnp.concatenate(flip([out_own, swap(out_give, "col")], "col"), axis=0)

    total = jnp.concatenate(
        [
            flip_dim(gain_sum[0], "col", 0),
            flip_dim(vectors[0], "col", 0),
            flip_dim(vectors[1], "col", 0),
            flip_dim(vectors[2], "row", 0),
            grad_query_scale,
        ]
    )
    for axis in ("core", "row", "col"):
        total = total + swap(total, axis)
    step = 1
    while step < size("z"):
        total = total + z_swap(total, step)
        step *= 2
    mine_col = lambda n: lax.dynamic_slice_in_dim(total, n * D + c * feat, feat, 0)
    units = b_up.shape[0]
    return (
        layer_out,
        grad_inputs,
        mine_col(0),
        sum_qkv,
        total[4 * D :],
        feed_sum[0],
        mine_col(1),
        feed_sum[2],
        lax.dynamic_slice_in_dim(total, 3 * D + r * units, units, 0),
        feed_sum[1],
        mine_col(2),
    )


def solution(mesh):
    dp, rows, cols = mesh.shape["dp"], mesh.shape["row"], mesh.shape["col"]
    split = Mesh(mesh.devices.reshape(dp // 2, 2, rows, cols), ("z", "core", "row", "col"))
    tokens = P(("z", "core", "row"), "col")
    in_specs = (
        tokens,
        P("col"),
        P("col", None, "row"),
        P(),
        P("row", "col"),
        P("col"),
        P("col", "row"),
        P("row"),
        P("row", "col"),
        P("col"),
        P(("z", "core")),
        P(("z", "core")),
        tokens,
    )
    out_specs = (
        tokens,
        tokens,
        P("col"),
        P("col", None, "row"),
        P(),
        P("row", "col"),
        P("col"),
        P("col", "row"),
        P("row"),
        P("row", "col"),
        P("col"),
    )
    body = body_four if rows == 2 and cols == 2 else body_any
    return jax.shard_map(body, mesh=split, in_specs=in_specs, out_specs=out_specs, check_vma=False)
```

```python
import functools
import math

import jax
import jax.numpy as jnp
from jax import lax
from jax.experimental import pallas as pl
from jax.experimental.pallas import tpu as pltpu
from jax.sharding import Mesh
from jax.sharding import PartitionSpec as P

D = 1280
HEAD_DIM = 80
EPS = 1e-06
QUERY_CONST = 1.442695041
MASKED = -1e30
BF = jnp.bfloat16
F32 = jnp.float32
VMEM_LIMIT = 50 * 1024 * 1024
CHEAP = pl.CostEstimate(flops=1, bytes_accessed=1, transcendentals=0)


def size(axis):
    return lax.axis_size(axis)


def swap(x, axis):
    return lax.ppermute(x, axis, [(0, 1), (1, 0)])


def flip(blocks, axis):
    if size(axis) != 2:
        return list(blocks)
    first = lax.axis_index(axis) == 0
    a, b = blocks
    return [jnp.where(first, a, b), jnp.where(first, b, a)]


def flip_dim(x, axis, dim):
    if size(axis) != 2:
        return x
    return jnp.concatenate(flip(jnp.split(x, 2, axis=dim), axis), axis=dim)


def gather(x, axis):
    if size(axis) == 2:
        return [x, swap(x, axis)]
    whole = lax.all_gather(x, axis, axis=0, tiled=False)
    return [whole[i] for i in range(size(axis))]


def gather_grid(x):
    if size("row") != 2:
        return [gather(b, "col") for b in gather(x, "row")]
    along_row, along_col = swap(x, "row"), swap(x, "col")
    half = x.shape[0] // 2
    across = jnp.concatenate(
        [swap(along_row[:half], "col"), swap(along_col[half:], "row")], axis=0
    )
    return [[x, along_col], [along_row, across]]


def scatter_sum(x, axis, dim):
    if size(axis) != 2:
        return lax.psum_scatter(x, axis, scatter_dimension=dim, tiled=True)
    mine, theirs = jnp.split(x, 2, axis=dim)
    return (mine.astype(F32) + swap(theirs, axis).astype(F32)).astype(x.dtype)


def exchange(x, axis, split, join):
    if size(axis) != 2:
        return lax.all_to_all(x, axis, split, join, tiled=True)
    mine, theirs = jnp.split(x, 2, axis=split)
    return jnp.concatenate([mine, swap(theirs, axis)], axis=join)


def core_half(x, dim):
    return lax.dynamic_slice_in_dim(
        x, lax.axis_index("core") * (x.shape[dim] // 2), x.shape[dim] // 2, dim
    )


def weight_gather(w, row_dim):
    part = core_half(w, 0)
    blocks = gather_grid(part)
    if row_dim == 1:
        blocks = [list(b) for b in zip(*blocks)]
    mine = jnp.stack([jnp.concatenate(b, axis=1) for b in blocks])
    other = swap(mine, "core")
    first = lax.axis_index("core") == 0
    both = jnp.stack([jnp.where(first, mine, other), jnp.where(first, other, mine)], axis=1)
    return both.reshape(-1, both.shape[-1])


def weight_sum(g, row_dim):
    dim_axis = ("row", "col") if row_dim == 0 else ("col", "row")
    n0 = size(dim_axis[0])
    g = g.reshape(n0, 2, g.shape[0] // n0 // 2, g.shape[1])
    core = lax.axis_index("core")
    keep = lax.dynamic_index_in_dim(g, core, 1, keepdims=False)
    give = lax.dynamic_index_in_dim(g, 1 - core, 1, keepdims=False).astype(BF)
    part = (keep + swap(give, "core").astype(F32)).astype(BF)
    part = scatter_sum(part, dim_axis[0], 0)
    part = scatter_sum(part[0], dim_axis[1], 1)
    return z_sum(part)


def z_sum(part):
    total = lax.psum(part, "z")
    other = swap(total, "core")
    return flip_core(total, other)


def flip_core(total, other):
    first = lax.axis_index("core") == 0
    return jnp.concatenate(
        [jnp.where(first, total, other), jnp.where(first, other, total)], axis=-2
    ).astype(F32)


def dot(a, b, contract):
    return lax.dot_general(a, b, ((contract[0:1], contract[1:2]), ((), ())), preferred_element_type=F32)


def bias_block(series_row, series_col, key_pos, q0, k0, qb, kb, diagonal):
    q_pos = q0 + lax.broadcasted_iota(jnp.int32, (1, qb), 1)
    allowed = (series_col == series_row) & (key_pos <= q_pos)
    if diagonal:
        k_pos = k0 + lax.broadcasted_iota(jnp.int32, (kb, 1), 0)
        allowed = allowed | (k_pos == q_pos)
    return jnp.where(allowed, 0.0, MASKED)


def forward_kernel(block, at, qkv_ref, srow_ref, scol_ref, kpos_ref, out_ref, lse_ref, *rest):
    *pieces, bias_ref, krow_ref, s_ref = rest
    t = qkv_ref.shape[3]
    n = t // block
    krow_ref[...] = qkv_ref[1, 0].astype(F32).T.astype(BF)

    def bias_slot(j, i):
        return j * (j + 1) // 2 + i

    @pl.when(pl.program_id(0) == 0)
    def _():
        for j in range(n):
            for i in range(j + 1):
                keys = pl.ds(i * block, block)
                bias_ref[bias_slot(j, i)] = bias_block(
                    srow_ref[:, j * block : (j + 1) * block],
                    scol_ref[keys, :],
                    kpos_ref[keys, :],
                    j * block,
                    i * block,
                    block,
                    block,
                    i == j,
                )

    for j in range(n):
        cols = slice(j * block, (j + 1) * block)
        q = qkv_ref[0, 0, :, cols]
        top = None
        for i in range(j + 1):
            s = dot(krow_ref[i * block : (i + 1) * block, :], q, (1, 0)) + bias_ref[bias_slot(j, i)]
            s_ref[i * block : (i + 1) * block, :] = s
            here = jnp.max(s, axis=0, keepdims=True)
            top = here if top is None else jnp.maximum(top, here)
        total = jnp.zeros((1, block), F32)
        acc = jnp.zeros((HEAD_DIM, block), F32)
        for i in range(j + 1):
            p = jnp.exp(s_ref[i * block : (i + 1) * block, :] - top)
            total += jnp.sum(p, axis=0, keepdims=True)
            acc += dot(qkv_ref[2, 0, :, i * block : (i + 1) * block], p.astype(BF), (1, 0))
        out_ref[0, :, cols] = (acc / total).astype(BF)
        lse_ref[0, :, cols] = top + jnp.log(total)
    for slot, piece in enumerate(pieces):
        wide = piece.shape[2]
        piece[0] = out_ref[0, :, pl.ds(pl.multiple_of((slot ^ at[3]) * wide, 128), wide)]


def backward_kernel(
    block, at, qkv_ref, raw_ref, factor_ref, out_ref, lse_ref, srow_ref, scol_ref, kpos_ref, *rest
):
    *pieces, grad_ref, gscale_ref, bias_ref, krow_ref, vrow_ref, gk_ref, gv_ref, gout_ref = rest
    if len(pieces) == 1:
        gout_ref[...] = pieces[0][0]
    else:
        for slot, piece in enumerate(pieces):
            wide = piece.shape[2]
            gout_ref[:, pl.ds(pl.multiple_of((slot ^ at[3]) * wide, 128), wide)] = piece[0]
    t = qkv_ref.shape[3]
    n = t // block
    krow_ref[...] = qkv_ref[1, 0].astype(F32).T.astype(BF)
    vrow_ref[...] = qkv_ref[2, 0].astype(F32).T.astype(BF)

    def bias_slot(j, i):
        return j * (j + 1) // 2 + i

    @pl.when(pl.program_id(0) == 0)
    def _():
        for j in range(n):
            for i in range(j + 1):
                keys = pl.ds(i * block, block)
                bias_ref[bias_slot(j, i)] = bias_block(
                    srow_ref[:, j * block : (j + 1) * block],
                    scol_ref[keys, :],
                    kpos_ref[keys, :],
                    j * block,
                    i * block,
                    block,
                    block,
                    i == j,
                )

    gscale = jnp.zeros((HEAD_DIM, 1), F32)
    for j in range(n):
        cols = slice(j * block, (j + 1) * block)
        q = qkv_ref[0, 0, :, cols]
        go = gout_ref[:, cols]
        lse = lse_ref[0, :, cols]
        delta = jnp.sum(go.astype(F32) * out_ref[0, :, cols].astype(F32), axis=0, keepdims=True)
        gq = jnp.zeros((HEAD_DIM, block), F32)
        for i in range(j + 1):
            keys = slice(i * block, (i + 1) * block)
            s = dot(krow_ref[keys, :], q, (1, 0)) + bias_ref[bias_slot(j, i)]
            p = jnp.exp(s - lse)
            gp = dot(vrow_ref[keys, :], go, (1, 0))
            gs = (p * (gp - delta)).astype(BF)
            gq += dot(qkv_ref[1, 0, :, keys], gs, (1, 0))
            gk = dot(q, gs, (1, 1))
            gv = dot(go, p.astype(BF), (1, 1))
            if i == j:
                gk_ref[:, keys] = gk
                gv_ref[:, keys] = gv
            else:
                gk_ref[:, keys] += gk
                gv_ref[:, keys] += gv
        gscale += jnp.sum(gq * raw_ref[0, :, cols], axis=1, keepdims=True)
        grad_ref[0, 0, :, cols] = (gq * factor_ref[...]).astype(BF)
    grad_ref[1, 0] = gk_ref[...].astype(BF)
    grad_ref[2, 0] = gv_ref[...].astype(BF)
    gscale_ref[0] = gscale


def mask_args(series, padding):
    t = series.shape[0]
    pos = jnp.arange(t, dtype=jnp.int32)
    return series.reshape(1, t), series.reshape(t, 1), jnp.where(padding == 0, pos, t).reshape(t, 1)


def attention_forward(at, qkv, masks, pieces=0):
    _, heads, hd, t = qkv.shape
    block = min(256, t) if t <= 2048 else 512
    n = t // block
    whole = lambda shape: pl.BlockSpec(shape, lambda h: (0,) * len(shape))
    wide = t // max(pieces, 1)
    return pl.pallas_call(
        functools.partial(forward_kernel, block),
        grid=(heads,),
        in_specs=[
            pl.BlockSpec(memory_space=pltpu.SMEM),
            pl.BlockSpec((3, 1, hd, t), lambda h: (0, h, 0, 0)),
            whole((1, t)),
            whole((t, 1)),
            whole((t, 1)),
        ],
        out_specs=[
            pl.BlockSpec((1, hd, t), lambda h: (h, 0, 0)),
            pl.BlockSpec((1, 1, t), lambda h: (h, 0, 0)),
        ]
        + [pl.BlockSpec((1, hd, wide), lambda h: (h, 0, 0))] * pieces,
        out_shape=[
            jax.ShapeDtypeStruct((heads, hd, t), BF),
            jax.ShapeDtypeStruct((heads, 1, t), F32),
        ]
        + [jax.ShapeDtypeStruct((heads, hd, wide), BF)] * pieces,
        scratch_shapes=[
            pltpu.VMEM((n * (n + 1) // 2, block, block), F32),
            pltpu.VMEM((t, hd), BF),
            pltpu.VMEM((t, block), F32),
        ],
        compiler_params=pltpu.CompilerParams(vmem_limit_bytes=VMEM_LIMIT),
        cost_estimate=CHEAP,
        name="attention_forward",
    )(at, qkv, *masks)


def attention_backward(at, qkv, raw, factor, out, pieces, lse, masks):
    _, heads, hd, t = qkv.shape
    block = min(256, t) if t <= 2048 else 512
    n = t // block
    whole = lambda shape: pl.BlockSpec(shape, lambda h: (0,) * len(shape))
    head = lambda wide=t: pl.BlockSpec((1, hd, wide), lambda h: (h, 0, 0))
    return pl.pallas_call(
        functools.partial(backward_kernel, block),
        grid=(heads,),
        in_specs=[
            pl.BlockSpec(memory_space=pltpu.SMEM),
            pl.BlockSpec((3, 1, hd, t), lambda h: (0, h, 0, 0)),
            head(),
            whole((hd, 1)),
            head(),
            pl.BlockSpec((1, 1, t), lambda h: (h, 0, 0)),
            whole((1, t)),
            whole((t, 1)),
            whole((t, 1)),
        ]
        + [head(p.shape[2]) for p in pieces],
        out_specs=[
            pl.BlockSpec((3, 1, hd, t), lambda h: (0, h, 0, 0)),
            pl.BlockSpec((1, hd, 1), lambda h: (h, 0, 0)),
        ],
        out_shape=[
            jax.ShapeDtypeStruct((3, heads, hd, t), BF),
            jax.ShapeDtypeStruct((heads, hd, 1), F32),
        ],
        scratch_shapes=[
            pltpu.VMEM((n * (n + 1) // 2, block, block), F32),
            pltpu.VMEM((t, hd), BF),
            pltpu.VMEM((t, hd), BF),
            pltpu.VMEM((hd, t), F32),
            pltpu.VMEM((hd, t), F32),
            pltpu.VMEM((hd, t), BF),
        ],
        compiler_params=pltpu.CompilerParams(vmem_limit_bytes=VMEM_LIMIT),
        cost_estimate=CHEAP,
        name="attention_backward",
    )(at, qkv, raw, factor, out, lse, *masks, *pieces)


def norm_scale(x):
    return lax.rsqrt(jnp.mean(x * x, axis=1, keepdims=True) + EPS)


def body_any(
    inputs, gain_attn, w_qkv, query_scale, w_out, gain_mlp, w_up, b_up, w_down, b_down, series_ids, pad_mask, cotangent
):
    rows, cols = size("row"), size("col")
    tok = inputs.shape[0]
    feat = inputs.shape[1]
    share = tok // cols
    t = series_ids.shape[0]
    head_rows = w_qkv.shape[2] // cols
    heads = head_rows // HEAD_DIM
    r, c = lax.axis_index("row"), lax.axis_index("col")

    blocks = gather_grid(inputs)
    strips = [jnp.concatenate(b, axis=1) for b in blocks]
    x_own = strips[0] if rows == 2 else lax.dynamic_index_in_dim(jnp.stack(strips), r, 0, keepdims=False)
    x_all = jnp.concatenate(flip(strips, "row"), axis=0)
    gain_one = jnp.concatenate(gather(gain_attn, "col"))
    gain_two = jnp.concatenate(gather(gain_mlp, "col"))
    bias_up = jnp.concatenate(gather(b_up, "row")).astype(F32)
    bias_down = jnp.concatenate(gather(b_down, "col")).astype(F32)

    w3 = jnp.transpose(w_qkv, (1, 0, 2)).reshape(3, feat, cols, head_rows)
    w_mine = lax.dynamic_index_in_dim(w3, c, 2, keepdims=False)
    w_give = lax.dynamic_index_in_dim(w3, 1 - c, 2, keepdims=False)
    w_half = swap(core_half(w_give, 1), "col")
    w_other = swap(w_half, "core")
    first = lax.axis_index("core") == 0
    w_full = jnp.concatenate(
        [w_mine, jnp.where(first, w_half, w_other), jnp.where(first, w_other, w_half)], axis=1
    )

    xf = x_all.astype(F32)
    scale_one = norm_scale(xf)
    normed_one = (xf * scale_one * gain_one).astype(BF)
    projected = jnp.einsum("td,sdh->sht", normed_one, w_full, preferred_element_type=F32)
    projected = projected.reshape(3, heads, HEAD_DIM, t)
    factor = QUERY_CONST / math.sqrt(HEAD_DIM) * jax.nn.softplus(query_scale)
    raw_q = projected[0]
    qkv = jnp.stack([raw_q * factor[None, :, None], projected[1], projected[2]]).astype(BF)
    masks = mask_args(series_ids, pad_mask)
    at = jnp.zeros((4,), jnp.int32)
    attended, lse = attention_forward(at, qkv, masks)

    def to_tokens(y):
        y = flip_dim(y.reshape(head_rows, rows, cols, share), "row", 1)
        y = flip_dim(y, "col", 2)
        y = exchange(y.reshape(1, head_rows, rows, cols, share), "row", 2, 0)
        y = exchange(y.reshape(rows, 1, head_rows, cols, share), "col", 3, 1)
        y = flip_dim(y.reshape(rows, cols, head_rows, share), "col", 1)
        return y.reshape(rows * cols * head_rows, share)

    def to_heads(y):
        y = flip_dim(y.reshape(rows, cols, head_rows, share), "col", 1)
        y = exchange(y.reshape(rows, cols, head_rows, 1, share), "col", 1, 3)
        y = exchange(y.reshape(rows, head_rows, 1, cols, share), "row", 0, 2)
        y = flip_dim(y.reshape(head_rows, rows, cols, share), "col", 2)
        return flip_dim(y, "row", 1).reshape(head_rows, t)

    w_out_all = weight_gather(w_out, 0)
    w_up_all = weight_gather(w_up, 1)
    w_down_all = weight_gather(w_down, 0)

    def my_share(y):
        return lax.dynamic_slice_in_dim(y, c * share, share, 0)

    att = to_tokens(attended.reshape(head_rows, t))
    x_mine = my_share(x_own).astype(F32)
    middle = x_mine + dot(att, w_out_all, (0, 0))
    scale_two = norm_scale(middle)
    normed_two = (middle * scale_two * gain_two).astype(BF)
    pre_act = dot(normed_two, w_up_all, (1, 0)) + bias_up
    sig = jax.nn.sigmoid(pre_act)
    hidden = (pre_act * sig).astype(BF)
    result = (middle + dot(hidden, w_down_all, (1, 0)) + bias_down).astype(BF)

    def to_block(y):
        mine, theirs = jnp.split(y, 2, axis=1)
        return jnp.concatenate(flip([mine, swap(theirs, "col")], "col"), axis=0)

    layer_out = to_block(result)

    g_give = lax.dynamic_slice_in_dim(cotangent, (1 - c) * share, share, 0)
    g = jnp.concatenate([my_share(cotangent), swap(g_give, "col")], axis=1)
    grad_w_down = dot(hidden, g, (0, 0))
    grad_hidden = dot(g, w_down_all, (1, 1))
    grad_pre_f = grad_hidden * sig * (1.0 + pre_act * (1.0 - sig))
    grad_pre = grad_pre_f.astype(BF)
    grad_b_up = jnp.sum(grad_pre.astype(F32), axis=0)
    grad_w_up = dot(normed_two, grad_pre, (0, 0))
    grad_normed_two = dot(grad_pre, w_up_all, (1, 1))
    weighted = grad_normed_two * gain_two
    inner = jnp.sum(weighted * middle, axis=1, keepdims=True)
    grad_middle = g.astype(F32) + scale_two * weighted - middle * (scale_two**3 * inner / D)
    grad_gain_mlp = jnp.sum(grad_normed_two * middle * scale_two, axis=0)
    grad_branch = grad_middle.astype(BF)
    grad_w_out = dot(att, grad_branch, (1, 0))
    grad_att = dot(w_out_all, grad_branch, (1, 1)).astype(BF)
    grad_attended = to_heads(grad_att).reshape(heads, HEAD_DIM, t)
    grad_middle_block = to_block(grad_middle)

    sum_down = weight_sum(grad_w_down, 0)
    sum_up = weight_sum(grad_w_up, 1)
    sum_out = weight_sum(grad_w_out, 0)

    grad_proj, gscale = attention_backward(
        at, qkv, raw_q, factor.reshape(HEAD_DIM, 1), attended, [grad_attended], lse, masks
    )
    slope = QUERY_CONST / math.sqrt(HEAD_DIM) * jax.nn.sigmoid(query_scale)
    grad_query_scale = jnp.sum(gscale, axis=(0, 2)) * slope
    grad_proj = grad_proj.reshape(3, head_rows, t)
    grad_normed_one = jnp.einsum("sht,sdh->td", grad_proj, w_full, preferred_element_type=F32)
    weighted_one = grad_normed_one * gain_one
    inner_one = jnp.sum(weighted_one * xf, axis=1)
    grad_gain_attn = jnp.sum(grad_normed_one * xf * scale_one, axis=0)
    inner_one = lax.psum(inner_one, ("row", "col"))
    grad_w = jnp.einsum("td,sht->sdh", normed_one, grad_proj, preferred_element_type=F32)
    grad_w = grad_w.reshape(3, cols, 2, feat // 2, head_rows)
    core = lax.axis_index("core")
    keep = lax.dynamic_index_in_dim(grad_w, core, 2, keepdims=False)
    give = lax.dynamic_index_in_dim(grad_w, 1 - core, 2, keepdims=False).astype(BF)
    part = (keep + swap(give, "core").astype(F32)).astype(BF)
    part = jnp.concatenate(flip([part[:, 0], swap(part[:, 1], "col")], "col"), axis=2)
    sum_qkv = jnp.transpose(z_sum(part), (1, 0, 2))

    e = jnp.concatenate(flip(jnp.split(grad_normed_one.astype(BF), 2, axis=0), "row"), axis=0) if rows == 2 else (
        grad_normed_one.astype(BF)
    )
    e = scatter_sum(e, "row", 0)
    e = scatter_sum(e, "col", 1).astype(F32)
    my_rows = lambda y: lax.dynamic_slice_in_dim(y, r * tok, tok, 0)
    scale_mine = my_rows(scale_one)
    inner_mine = my_rows(inner_one.reshape(t, 1))
    grad_inputs = grad_middle_block + scale_mine * (e * gain_attn) - inputs.astype(F32) * (
        scale_mine**3 * inner_mine / D
    )

    grad_b_down = jnp.sum(g.astype(F32), axis=0)
    vectors = jnp.concatenate(
        [
            flip_dim(grad_gain_attn, "col", 0),
            flip_dim(grad_gain_mlp, "col", 0),
            flip_dim(grad_b_down, "col", 0),
            flip_dim(grad_b_up, "row", 0),
            grad_query_scale,
        ]
    )
    vectors = lax.psum(vectors, ("z", "core", "row", "col"))
    mine_col = lambda at: lax.dynamic_slice_in_dim(vectors, at * D + c * feat, feat, 0)
    units = b_up.shape[0]
    return (
        layer_out,
        grad_inputs,
        mine_col(0),
        sum_qkv,
        vectors[4 * D :],
        sum_out,
        mine_col(1),
        sum_up,
        lax.dynamic_slice_in_dim(vectors, 3 * D + r * units, units, 0),
        sum_down,
        mine_col(2),
    )


SMEM = pl.BlockSpec(memory_space=pltpu.SMEM)
ANY = pl.BlockSpec(memory_space=pl.ANY)


def call(kernel, name, args, specs, outs, scratch=(), **more):
    return pl.pallas_call(
        kernel,
        in_specs=specs,
        out_shape=outs,
        scratch_shapes=list(scratch),
        compiler_params=pltpu.CompilerParams(vmem_limit_bytes=VMEM_LIMIT),
        cost_estimate=CHEAP,
        name=name,
        **more,
    )(*args)


VM = pl.BlockSpec(memory_space=pltpu.VMEM)


def shape(dims, kind):
    return jax.ShapeDtypeStruct(dims, kind)


def project_kernel(
    at, x00, x01, x10, x11, gain, factor, w_mine, w_a, w_b, qkv, raw, normed, scale_own, w_full
):
    r, k = at[0], at[2]
    tok, feat = x00.shape
    hr = w_mine.shape[1]
    half = hr // 2
    for s in range(3):
        w_full[pl.ds(s * hr, hr), 0:feat] = w_mine[s]
        w_full[pl.ds(pl.multiple_of(s * hr + k * half, 16), half), feat:] = w_a[s]
        w_full[pl.ds(pl.multiple_of(s * hr + (1 - k) * half, 16), half), feat:] = w_b[s]
    for i, (a_ref, b_ref) in enumerate(((x00, x01), (x10, x11))):
        a, b = a_ref[...].astype(F32), b_ref[...].astype(F32)
        total = jnp.sum(a * a, axis=1, keepdims=True) + jnp.sum(b * b, axis=1, keepdims=True)
        scale = lax.rsqrt(total / (2 * feat) + EPS)
        if i == 0:
            scale_own[...] = scale
        rows = pl.ds(pl.multiple_of((r ^ i) * tok, tok), tok)
        normed[rows, 0:feat] = (a * scale * gain[:, 0:feat]).astype(BF)
        normed[rows, feat:] = (b * scale * gain[:, feat:]).astype(BF)
        y = normed[rows, :]
        q = dot(w_full[0:hr, :], y, (1, 1))
        raw[:, rows] = q
        qkv[0, :, rows] = (q * factor[...]).astype(BF)
        qkv[1, :, rows] = dot(w_full[hr : 2 * hr, :], y, (1, 1)).astype(BF)
        qkv[2, :, rows] = dot(w_full[2 * hr : 3 * hr, :], y, (1, 1)).astype(BF)


def feed_kernel(
    at, a0, a1, a2, a3, x_own, x_col, g_own, g_col, gain, bias_up, bias_down,
    w_out, w_up, w_down, hx, hy, d0, d1, hx2, hy2, d02, d12,
    out_own, out_give, gm_own, gm_give, t0, t1, t2, t3, vectors,
    sx, sy, kx, ky, sx2, sy2, kx2, ky2,
    w, att, turned, sems,
):
    r, c, k = at[0], at[1], at[2]
    hr, share = a0.shape
    feat = x_own.shape[1]
    half = feat // 2
    quarter = half // 2
    copies = []
    for n, shard in enumerate((w_out, w_up, w_down)):
        rx, cx, ry, cy = (0, feat, feat, 0) if n == 1 else (feat, 0, 0, feat)
        mine = []
        mine.append((shard, w.at[n, 0:feat, 0:feat]))
        for core, (px, py, p0, p1) in ((k, (hx, hy, d0, d1)), (1 - k, (hx2, hy2, d02, d12))):
            down = core * half
            at_x = pl.ds(pl.multiple_of(rx + down, 16), half)
            at_y = pl.ds(pl.multiple_of(ry + down, 16), half)
            at_0 = pl.ds(pl.multiple_of(feat + down, 16), quarter)
            at_1 = pl.ds(pl.multiple_of(feat + down + quarter, 16), quarter)
            mine.append((px.at[n], w.at[n, at_x, cx : cx + feat]))
            mine.append((py.at[n], w.at[n, at_y, cy : cy + feat]))
            mine.append((p0.at[n], w.at[n, at_0, feat : 2 * feat]))
            mine.append((p1.at[n], w.at[n, at_1, feat : 2 * feat]))
        started = []
        for m, (src, dst) in enumerate(mine):
            copy = pltpu.make_async_copy(src, dst, sems.at[n, m])
            copy.start()
            started.append(copy)
        copies.append(started)

    rows = pl.ds(pl.multiple_of(c * share, share), share)
    for s, a in enumerate((a0, a1, a2, a3)):
        to = (s // 2) * 2 * hr + (c ^ (s % 2)) * hr
        att[pl.ds(pl.multiple_of(to, 16), hr), :] = a[...]
    x = jnp.concatenate([x_own[rows, :], x_col[rows, :]], axis=1).astype(F32)
    g = jnp.concatenate([g_own[rows, :], g_col[...]], axis=1)
    for copy in copies[0]:
        copy.wait()
    middle = x + dot(att[...], w[0], (0, 0))
    scale = lax.rsqrt(jnp.sum(middle * middle, axis=1, keepdims=True) / D + EPS)
    normed = (middle * scale * gain[...]).astype(BF)
    for copy in copies[1]:
        copy.wait()
    pre = dot(normed, w[1], (1, 0)) + bias_up[...]
    sig = jax.nn.sigmoid(pre)
    hidden = (pre * sig).astype(BF)
    for copy in copies[2]:
        copy.wait()
    result = (middle + dot(hidden, w[2], (1, 0)) + bias_down[...]).astype(BF)
    out_own[...] = result[:, :feat]
    out_give[...] = result[:, feat:]

    def weight_grad(n, left_ref, right):
        for core, by_row, by_col in ((k, (sx, kx), (sy, ky)), (1 - k, (sx2, kx2), (sy2, ky2))):
            up, low = (by_col, by_row) if n == 1 else (by_row, by_col)
            for b in range(2):
                part = pl.ds(pl.multiple_of(b * feat + core * half, 16), half)
                y = dot(left_ref[part, :], right, (1, 0)).astype(BF)
                for j in range(2):
                    cut = slice(j * feat, (j + 1) * feat)
                    up[1 - b][n, j] = y[:quarter, cut]
                    low[1 - j][n, b] = y[quarter:, cut]

    turned[...] = hidden.astype(F32).T.astype(BF)
    grad_pre_f = dot(g, w[2], (1, 1)) * sig * (1.0 + pre * (1.0 - sig))
    grad_pre = grad_pre_f.astype(BF)
    weight_grad(2, turned, g)
    grad_normed = dot(grad_pre, w[1], (1, 1))
    weighted = grad_normed * gain[...]
    inner = jnp.sum(weighted * middle, axis=1, keepdims=True)
    gf = g.astype(F32)
    grad_middle = gf + scale * weighted - middle * (scale * scale * scale * inner / D)
    gm_own[...] = grad_middle[:, :feat]
    gm_give[...] = grad_middle[:, feat:].astype(BF)
    branch = grad_middle.astype(BF)
    for s, t in enumerate((t0, t1, t2, t3)):
        come = (s // 2) * 2 * hr + (c ^ (s % 2)) * hr
        t[...] = dot(w[0, pl.ds(pl.multiple_of(come, 16), hr), :], branch, (1, 1)).astype(BF)
    turned[...] = normed.astype(F32).T.astype(BF)
    weight_grad(1, turned, grad_pre)
    weight_grad(0, att, branch)
    vectors[...] = jnp.concatenate(
        [
            jnp.sum(grad_normed * (middle * scale), axis=0, keepdims=True),
            jnp.sum(gf, axis=0, keepdims=True),
            jnp.sum(grad_pre.astype(F32), axis=0, keepdims=True),
        ],
        axis=0,
    )


def project_back_kernel(
    at, grad, w_full, normed, x00, x01, x10, x11, gain, keep, give, e0, e1, e2, e3, inner_own, gain_sum
):
    r, k = at[0], at[2]
    tok, feat = x00.shape
    hr = grad.shape[0] // 3
    half = hr // 2
    for ref, core in ((give, 1 - k), (keep, k)):
        for s in range(3):
            part = pl.ds(pl.multiple_of(s * hr + core * half, 16), half)
            y = dot(grad[part, :], normed[...], (1, 0)).astype(BF)
            ref[0, s] = y[:, :feat]
            ref[1, s] = y[:, feat:]
    sums = [jnp.zeros((1, feat), F32), jnp.zeros((1, feat), F32)]
    for i, (xs, es) in enumerate((((x00, x01), (e0, e1)), ((x10, x11), (e2, e3)))):
        rows = pl.ds(pl.multiple_of((r ^ i) * tok, tok), tok)
        left = grad[:, rows]
        es_f, squares, inner = [], 0.0, 0.0
        for j in range(2):
            cut = slice(j * feat, (j + 1) * feat)
            e = dot(left, w_full[:, cut], (0, 0))
            x = xs[j][...].astype(F32)
            inner = inner + jnp.sum(e * gain[:, cut] * x, axis=1, keepdims=True)
            squares = squares + jnp.sum(x * x, axis=1, keepdims=True)
            es[j][0:tok, :] = e.astype(es[j].dtype)
            es_f.append(e * x)
        scale = lax.rsqrt(squares / (2 * feat) + EPS)
        for j in range(2):
            sums[j] += jnp.sum(es_f[j] * scale, axis=0, keepdims=True)
        line = jnp.broadcast_to(inner, (tok, 128)).T[0:1, :]
        high = line.astype(BF).astype(F32)
        extra = jnp.concatenate([high, line - high, jnp.zeros((14, tok), F32)], axis=0)
        extra = jnp.concatenate([extra, jnp.zeros((16, feat - tok), F32)], axis=1).astype(BF)
        if i == 0:
            inner_own[...] = inner
            es[1][tok:, :] = extra
        else:
            es[0][tok:, :] = extra
            es[1][tok:, :] = extra
    gain_sum[:, 0:feat] = sums[0]
    gain_sum[:, feat:] = sums[1]


def finish_qkv_kernel(at, mine, theirs, mine2, theirs2, out, rows):
    c, k = at[1], at[2]
    half = mine.shape[1]
    for s in range(3):
        for ref, col, core in ((mine, c, k), (theirs, 1 - c, k), (mine2, c, 1 - k), (theirs2, 1 - c, 1 - k)):
            rows[pl.ds(pl.multiple_of((2 * col + core) * half, 16), half), :] = ref[s].astype(F32)
        out[s] = rows[...].T


def finish_feed_kernel(at, a, b, a2, b2, *outs):
    k = at[2]
    quarter = a.shape[1]
    for n, out in enumerate(outs):
        upper, lower = ((b, b2), (a, a2)) if n == 1 else ((a, a2), (b, b2))
        for i, core in ((0, k), (1, 1 - k)):
            for j, refs in enumerate((upper, lower)):
                to = pl.multiple_of((2 * core + j) * quarter, 16)
                out[pl.ds(to, quarter), :] = refs[i][n].astype(F32)


def after(x, *earlier):
    return lax.optimization_barrier((x, *earlier))[0]


def add(*parts):
    total = parts[0].astype(F32)
    for part in parts[1:]:
        total = total + part.astype(F32)
    return total.astype(BF)


def diagonal(x):
    return lax.ppermute(x, ("row", "col"), [(0, 3), (1, 2), (2, 1), (3, 0)])


def z_swap(x, step):
    n = size("z")
    return lax.ppermute(x, "z", [(i, i ^ step) for i in range(n)])


def z_total(a, b):
    if size("z") != 4:
        return lax.psum((a, b), "z")
    z = lax.axis_index("z")
    first = (z == 0) | (z == 3)
    mine = add(jnp.where(first, a, b), z_swap(jnp.where(first, b, a), 1))
    mine = add(mine, z_swap(mine, 3))
    other = z_swap(mine, 1)
    return jnp.where(first, mine, other), jnp.where(first, other, mine)


def body_four(
    inputs, gain_attn, w_qkv, query_scale, w_out, gain_mlp, w_up, b_up, w_down, b_down, series_ids, pad_mask, cotangent
):
    tok, feat = inputs.shape
    share = tok // 2
    t = series_ids.shape[0]
    hr = w_qkv.shape[2] // 2
    heads = hr // HEAD_DIM
    half = feat // 2
    r, c, k = lax.axis_index("row"), lax.axis_index("col"), lax.axis_index("core")
    at = jnp.stack([r, c, k, 2 * r + c]).astype(jnp.int32)
    mine_rows = lambda y, part: lax.dynamic_slice_in_dim(y, part * share, share, 0)

    x01 = swap(inputs, "col")
    x10 = swap(inputs, "row")
    small = swap(jnp.concatenate([gain_attn, gain_mlp, b_down.astype(F32)]), "col")
    up_other = swap(b_up.astype(F32), "row")
    w_turned = jnp.transpose(w_qkv, (1, 2, 0)).reshape(3, 2, hr, feat)
    w_mine = lax.dynamic_index_in_dim(w_turned, c, 1, keepdims=False)
    w_give = lax.dynamic_index_in_dim(w_turned, 1 - c, 1, keepdims=False)
    w_a = swap(core_half(w_give, 1), "col")
    x01, x10, small, up_other = lax.optimization_barrier((x01, x10, small, up_other))
    x11 = swap(x01, "row")
    w_b = swap(w_a, "core")
    gain_one = jnp.concatenate([gain_attn, small[:feat]]).reshape(1, D)
    gain_two = jnp.concatenate([gain_mlp, small[feat : 2 * feat]]).reshape(1, D)
    bias_down = jnp.concatenate([b_down.astype(F32), small[2 * feat :]]).reshape(1, D)
    bias_up = jnp.concatenate([b_up.astype(F32), up_other]).reshape(1, D)
    factor = QUERY_CONST / math.sqrt(HEAD_DIM) * jax.nn.softplus(query_scale)
    factor_col = factor.reshape(HEAD_DIM, 1)

    part = jnp.stack([core_half(w_out, 0), core_half(w_up, 0), core_half(w_down, 0)])
    part = after(part, x11, w_a)
    hx, hy = swap(part, "row"), swap(part, "col")
    hx2, hy2 = swap(hx, "core"), swap(hy, "core")
    d0 = swap(hx[:, : half // 2], "col")
    d1 = swap(hy[:, half // 2 :], "row")
    d02, d12 = swap(d0, "core"), swap(d1, "core")
    g_col = swap(after(mine_rows(cotangent, 1 - c), x11, w_a), "col")

    qkv, raw, normed_one, scale_own, w_full = call(
        project_kernel,
        "project",
        (at, inputs, x01, x10, x11, gain_one, jnp.tile(factor_col, (heads, 1)), w_mine, w_a, w_b),
        [SMEM] + [VM] * 9,
        [
            shape((3, hr, t), BF),
            shape((hr, t), F32),
            shape((t, D), BF),
            shape((tok, 1), F32),
            shape((3 * hr, D), BF),
        ],
    )
    qkv = qkv.reshape(3, heads, HEAD_DIM, t)
    masks = mask_args(series_ids, pad_mask)
    attended, lse, *a = attention_forward(at, qkv, masks, pieces=4)
    a0, a1, a2, a3 = [p.reshape(hr, share) for p in a]
    a1, a2, a3 = swap(a1, "col"), swap(a2, "row"), diagonal(a3)
    out_own, out_give, gm_own, gm_give, t0, t1, t2, t3, vectors, *grads = call(
        feed_kernel,
        "feed_forward",
        (at, a0, a1, a2, a3, inputs, x01, cotangent, g_col, gain_two, bias_up, bias_down)
        + (w_out, w_up, w_down, hx, hy, d0, d1, hx2, hy2, d02, d12),
        [SMEM] + [VM] * 11 + [ANY] * 11,
        [
            shape((share, feat), BF),
            shape((share, feat), BF),
            shape((share, feat), F32),
            shape((share, feat), BF),
        ]
        + [shape((hr, share), BF)] * 4
        + [shape((3, D), F32)]
        + [shape((3, 2, half // 2, feat), BF)] * 8,
        scratch=[
            pltpu.VMEM((3, D, D), BF),
            pltpu.VMEM((D, share), BF),
            pltpu.VMEM((D, share), BF),
            pltpu.SemaphoreType.DMA((3, 9)),
        ],
    )
    t1, t2, t3 = swap(t1, "col"), swap(t2, "row"), diagonal(t3)
    sx, sy, kx, ky, *other_core = grads
    sx2, sy2, kx2, ky2 = [swap(y, "core") for y in other_core]
    sx, sy = add(sx, sx2), add(sy, sy2)
    pieces = lax.optimization_barrier((t0, t1, t2, t3, sx, sy))[:4]
    rx, ry = swap(sx, "row"), swap(sy, "col")
    grad_proj, gscale = attention_backward(
        at,
        qkv,
        raw.reshape(heads, HEAD_DIM, t),
        factor_col,
        attended,
        [p.reshape(heads, HEAD_DIM, share) for p in pieces],
        lse,
        masks,
    )
    slope = QUERY_CONST / math.sqrt(HEAD_DIM) * jax.nn.sigmoid(query_scale)
    grad_query_scale = jnp.sum(gscale, axis=(0, 2)) * slope
    w_keep, w_send, e0, e1, e2, e3, inner, gain_sum = call(
        project_back_kernel,
        "project_back",
        (at, grad_proj.reshape(3 * hr, t), w_full, normed_one, inputs, x01, x10, x11, gain_one),
        [SMEM] + [VM] * 8,
        [
            shape((2, 3, hr // 2, feat), BF),
            shape((2, 3, hr // 2, feat), BF),
            shape((tok, feat), F32),
            shape((tok + 16, feat), BF),
            shape((tok + 16, feat), BF),
            shape((tok + 16, feat), BF),
            shape((tok, 1), F32),
            shape((1, D), F32),
        ],
    )
    w_pair = add(w_keep, swap(w_send, "core"))
    w_own, w_theirs = z_total(w_pair[0], w_pair[1])
    w_theirs = swap(w_theirs, "col")
    w_args = (at, w_own, w_theirs, swap(w_own, "core"), swap(w_theirs, "core"))
    sum_qkv = call(
        finish_qkv_kernel,
        "finish_qkv",
        w_args,
        [SMEM] + [VM] * 4,
        shape((3, feat, 2 * hr), F32),
        scratch=[pltpu.VMEM((2 * hr, feat), F32)],
    )
    sum_qkv = jnp.transpose(sum_qkv, (1, 0, 2))

    px, py = add(kx, kx2, rx), add(ky, ky2, ry)
    qx, qy = swap(px[:, 1], "col"), swap(py[:, 1], "row")
    fx, fy = add(px[:, 0], qx), add(py[:, 0], qy)
    e1, e2, e3, out_give, gm_give, fx, fy = lax.optimization_barrier((e1, e2, e3, out_give, gm_give, fx, fy))
    fx, fy = z_total(fx, fy)
    sum_out, sum_up, sum_down = call(
        finish_feed_kernel,
        "finish_feed",
        (at, fx, fy, swap(fx, "core"), swap(fy, "core")),
        [SMEM] + [VM] * 4,
        [shape((feat, feat), F32)] * 3,
    )

    e1, e2, e3 = swap(e1, "col"), swap(e2, "row"), diagonal(e3)
    e = e0
    for more in (e1, e2, e3):
        e = e + more[:tok].astype(F32)
        inner = inner + jnp.sum(more[tok : tok + 2, :tok].astype(F32), axis=0).reshape(tok, 1)
    gm_col = swap(gm_give, "col").astype(F32)
    grad_middle = jnp.concatenate(flip([gm_own, gm_col], "col"), axis=0)
    grad_inputs = grad_middle + scale_own * (e * gain_attn) - inputs.astype(F32) * (scale_own**3 * inner / D)
    layer_out = jnp.concatenate(flip([out_own, swap(out_give, "col")], "col"), axis=0)

    total = jnp.concatenate(
        [
            flip_dim(gain_sum[0], "col", 0),
            flip_dim(vectors[0], "col", 0),
            flip_dim(vectors[1], "col", 0),
            flip_dim(vectors[2], "row", 0),
            grad_query_scale,
        ]
    )
    for axis in ("core", "row", "col"):
        total = total + swap(total, axis)
    step = 1
    while step < size("z"):
        total = total + z_swap(total, step)
        step *= 2
    mine_col = lambda n: lax.dynamic_slice_in_dim(total, n * D + c * feat, feat, 0)
    units = b_up.shape[0]
    return (
        layer_out,
        grad_inputs,
        mine_col(0),
        sum_qkv,
        total[4 * D :],
        sum_out,
        mine_col(1),
        sum_up,
        lax.dynamic_slice_in_dim(total, 3 * D + r * units, units, 0),
        sum_down,
        mine_col(2),
    )


def solution(mesh):
    dp, rows, cols = mesh.shape["dp"], mesh.shape["row"], mesh.shape["col"]
    split = Mesh(mesh.devices.reshape(dp // 2, 2, rows, cols), ("z", "core", "row", "col"))
    tokens = P(("z", "core", "row"), "col")
    in_specs = (
        tokens,
        P("col"),
        P("col", None, "row"),
        P(),
        P("row", "col"),
        P("col"),
        P("col", "row"),
        P("row"),
        P("row", "col"),
        P("col"),
        P(("z", "core")),
        P(("z", "core")),
        tokens,
    )
    out_specs = (
        tokens,
        tokens,
        P("col"),
        P("col", None, "row"),
        P(),
        P("row", "col"),
        P("col"),
        P("col", "row"),
        P("row"),
        P("row", "col"),
        P("col"),
    )
    body = body_four if rows == 2 and cols == 2 else body_any
    return jax.shard_map(body, mesh=split, in_specs=in_specs, out_specs=out_specs, check_vma=False)
```

```python
import functools
import math

import jax
import jax.numpy as jnp
from jax import lax
from jax.experimental import pallas as pl
from jax.experimental.pallas import tpu as pltpu
from jax.sharding import Mesh
from jax.sharding import PartitionSpec as P

D = 1280
HEAD_DIM = 80
EPS = 1e-06
QUERY_CONST = 1.442695041
MASKED = -1e30
BF = jnp.bfloat16
F32 = jnp.float32
VMEM_LIMIT = 50 * 1024 * 1024
CHEAP = pl.CostEstimate(flops=1, bytes_accessed=1, transcendentals=0)


def size(axis):
    return lax.axis_size(axis)


def swap(x, axis):
    return lax.ppermute(x, axis, [(0, 1), (1, 0)])


def flip(blocks, axis):
    if size(axis) != 2:
        return list(blocks)
    first = lax.axis_index(axis) == 0
    a, b = blocks
    return [jnp.where(first, a, b), jnp.where(first, b, a)]


def flip_dim(x, axis, dim):
    if size(axis) != 2:
        return x
    return jnp.concatenate(flip(jnp.split(x, 2, axis=dim), axis), axis=dim)


def gather(x, axis):
    if size(axis) == 2:
        return [x, swap(x, axis)]
    whole = lax.all_gather(x, axis, axis=0, tiled=False)
    return [whole[i] for i in range(size(axis))]


def gather_grid(x):
    if size("row") != 2:
        return [gather(b, "col") for b in gather(x, "row")]
    along_row, along_col = swap(x, "row"), swap(x, "col")
    half = x.shape[0] // 2
    across = jnp.concatenate(
        [swap(along_row[:half], "col"), swap(along_col[half:], "row")], axis=0
    )
    return [[x, along_col], [along_row, across]]


def scatter_sum(x, axis, dim):
    if size(axis) != 2:
        return lax.psum_scatter(x, axis, scatter_dimension=dim, tiled=True)
    mine, theirs = jnp.split(x, 2, axis=dim)
    return (mine.astype(F32) + swap(theirs, axis).astype(F32)).astype(x.dtype)


def exchange(x, axis, split, join):
    if size(axis) != 2:
        return lax.all_to_all(x, axis, split, join, tiled=True)
    mine, theirs = jnp.split(x, 2, axis=split)
    return jnp.concatenate([mine, swap(theirs, axis)], axis=join)


def core_half(x, dim):
    return lax.dynamic_slice_in_dim(
        x, lax.axis_index("core") * (x.shape[dim] // 2), x.shape[dim] // 2, dim
    )


def weight_gather(w, row_dim):
    part = core_half(w, 0)
    blocks = gather_grid(part)
    if row_dim == 1:
        blocks = [list(b) for b in zip(*blocks)]
    mine = jnp.stack([jnp.concatenate(b, axis=1) for b in blocks])
    other = swap(mine, "core")
    first = lax.axis_index("core") == 0
    both = jnp.stack([jnp.where(first, mine, other), jnp.where(first, other, mine)], axis=1)
    return both.reshape(-1, both.shape[-1])


def weight_sum(g, row_dim):
    dim_axis = ("row", "col") if row_dim == 0 else ("col", "row")
    n0 = size(dim_axis[0])
    g = g.reshape(n0, 2, g.shape[0] // n0 // 2, g.shape[1])
    core = lax.axis_index("core")
    keep = lax.dynamic_index_in_dim(g, core, 1, keepdims=False)
    give = lax.dynamic_index_in_dim(g, 1 - core, 1, keepdims=False).astype(BF)
    part = (keep + swap(give, "core").astype(F32)).astype(BF)
    part = scatter_sum(part, dim_axis[0], 0)
    part = scatter_sum(part[0], dim_axis[1], 1)
    return z_sum(part)


def z_sum(part):
    total = lax.psum(part, "z")
    other = swap(total, "core")
    return flip_core(total, other)


def flip_core(total, other):
    first = lax.axis_index("core") == 0
    return jnp.concatenate(
        [jnp.where(first, total, other), jnp.where(first, other, total)], axis=-2
    ).astype(F32)


def dot(a, b, contract):
    return lax.dot_general(a, b, ((contract[0:1], contract[1:2]), ((), ())), preferred_element_type=F32)


def bias_block(series_row, series_col, key_pos, q0, k0, qb, kb, diagonal):
    q_pos = q0 + lax.broadcasted_iota(jnp.int32, (1, qb), 1)
    allowed = (series_col == series_row) & (key_pos <= q_pos)
    if diagonal:
        k_pos = k0 + lax.broadcasted_iota(jnp.int32, (kb, 1), 0)
        allowed = allowed | (k_pos == q_pos)
    return jnp.where(allowed, 0.0, MASKED)


def forward_kernel(block, at, qkv_ref, srow_ref, scol_ref, kpos_ref, out_ref, lse_ref, *rest):
    *pieces, bias_ref, krow_ref, s_ref, slot_ref = rest
    t = qkv_ref.shape[3]
    n = t // block
    krow_ref[...] = qkv_ref[1, 0].astype(F32).T.astype(BF)

    def bias_slot(j, i):
        return j * (j + 1) // 2 + i

    @pl.when(pl.program_id(0) == 0)
    def _():
        for j in range(n):
            for i in range(j + 1):
                keys = pl.ds(i * block, block)
                bias_ref[bias_slot(j, i)] = bias_block(
                    srow_ref[:, j * block : (j + 1) * block],
                    scol_ref[keys, :],
                    kpos_ref[keys, :],
                    j * block,
                    i * block,
                    block,
                    block,
                    i == j,
                )

    for j in range(n):
        cols = slice(j * block, (j + 1) * block)
        q = qkv_ref[0, 0, :, cols]
        top = None
        for i in range(j + 1):
            s = dot(krow_ref[i * block : (i + 1) * block, :], q, (1, 0)) + bias_ref[bias_slot(j, i)]
            s_ref[i * block : (i + 1) * block, :] = s
            here = jnp.max(s, axis=0, keepdims=True)
            top = here if top is None else jnp.maximum(top, here)
        total = jnp.zeros((1, block), F32)
        acc = jnp.zeros((HEAD_DIM, block), F32)
        for i in range(j + 1):
            p = jnp.exp(s_ref[i * block : (i + 1) * block, :] - top)
            total += jnp.sum(p, axis=0, keepdims=True)
            acc += dot(qkv_ref[2, 0, :, i * block : (i + 1) * block], p.astype(BF), (1, 0))
        found = (acc / total).astype(BF)
        out_ref[0, :, cols] = found
        if pieces:
            slot_ref[j ^ at[3]] = found
        lse_ref[0, :, cols] = top + jnp.log(total)
    for slot, piece in enumerate(pieces):
        piece[0] = slot_ref[slot]


def backward_kernel(
    block, at, qkv_ref, raw_ref, factor_ref, out_ref, lse_ref, srow_ref, scol_ref, kpos_ref, *rest
):
    *pieces, grad_ref, gscale_ref, bias_ref, krow_ref, vrow_ref, gk_ref, gv_ref, gout_ref = rest
    if len(pieces) == 1:
        gout_ref[...] = pieces[0][0]
    else:
        for slot, piece in enumerate(pieces):
            wide = piece.shape[2]
            gout_ref[:, pl.ds(pl.multiple_of((slot ^ at[3]) * wide, 128), wide)] = piece[0]
    t = qkv_ref.shape[3]
    n = t // block
    krow_ref[...] = qkv_ref[1, 0].astype(F32).T.astype(BF)
    vrow_ref[...] = qkv_ref[2, 0].astype(F32).T.astype(BF)

    def bias_slot(j, i):
        return j * (j + 1) // 2 + i

    @pl.when(pl.program_id(0) == 0)
    def _():
        for j in range(n):
            for i in range(j + 1):
                keys = pl.ds(i * block, block)
                bias_ref[bias_slot(j, i)] = bias_block(
                    srow_ref[:, j * block : (j + 1) * block],
                    scol_ref[keys, :],
                    kpos_ref[keys, :],
                    j * block,
                    i * block,
                    block,
                    block,
                    i == j,
                )

    gscale = jnp.zeros((HEAD_DIM, 1), F32)
    for j in range(n):
        cols = slice(j * block, (j + 1) * block)
        q = qkv_ref[0, 0, :, cols]
        go = gout_ref[:, cols]
        lse = lse_ref[0, :, cols]
        delta = jnp.sum(go.astype(F32) * out_ref[0, :, cols].astype(F32), axis=0, keepdims=True)
        gq = jnp.zeros((HEAD_DIM, block), F32)
        for i in range(j + 1):
            keys = slice(i * block, (i + 1) * block)
            s = dot(krow_ref[keys, :], q, (1, 0)) + bias_ref[bias_slot(j, i)]
            p = jnp.exp(s - lse)
            gp = dot(vrow_ref[keys, :], go, (1, 0))
            gs = (p * (gp - delta)).astype(BF)
            gq += dot(qkv_ref[1, 0, :, keys], gs, (1, 0))
            gk = dot(q, gs, (1, 1))
            gv = dot(go, p.astype(BF), (1, 1))
            if i == j:
                gk_ref[:, keys] = gk
                gv_ref[:, keys] = gv
            else:
                gk_ref[:, keys] += gk
                gv_ref[:, keys] += gv
        gscale += jnp.sum(gq * raw_ref[0, :, cols], axis=1, keepdims=True)
        grad_ref[0, 0, :, cols] = (gq * factor_ref[...]).astype(BF)
    grad_ref[1, 0] = gk_ref[...].astype(BF)
    grad_ref[2, 0] = gv_ref[...].astype(BF)
    gscale_ref[0] = gscale


def mask_args(series, padding):
    t = series.shape[0]
    pos = jnp.arange(t, dtype=jnp.int32)
    return series.reshape(1, t), series.reshape(t, 1), jnp.where(padding == 0, pos, t).reshape(t, 1)


def attention_forward(at, qkv, masks, pieces=0):
    _, heads, hd, t = qkv.shape
    block = min(256, t) if t <= 2048 else 512
    n = t // block
    whole = lambda shape: pl.BlockSpec(shape, lambda h: (0,) * len(shape))
    assert pieces in (0, n)
    return pl.pallas_call(
        functools.partial(forward_kernel, block),
        grid=(heads,),
        in_specs=[
            pl.BlockSpec(memory_space=pltpu.SMEM),
            pl.BlockSpec((3, 1, hd, t), lambda h: (0, h, 0, 0)),
            whole((1, t)),
            whole((t, 1)),
            whole((t, 1)),
        ],
        out_specs=[
            pl.BlockSpec((1, hd, t), lambda h: (h, 0, 0)),
            pl.BlockSpec((1, 1, t), lambda h: (h, 0, 0)),
        ]
        + [pl.BlockSpec((1, hd, block), lambda h: (h, 0, 0))] * pieces,
        out_shape=[
            jax.ShapeDtypeStruct((heads, hd, t), BF),
            jax.ShapeDtypeStruct((heads, 1, t), F32),
        ]
        + [jax.ShapeDtypeStruct((heads, hd, block), BF)] * pieces,
        scratch_shapes=[
            pltpu.VMEM((n * (n + 1) // 2, block, block), F32),
            pltpu.VMEM((t, hd), BF),
            pltpu.VMEM((t, block), F32),
            pltpu.VMEM((n, hd, block), BF),
        ],
        compiler_params=pltpu.CompilerParams(vmem_limit_bytes=VMEM_LIMIT),
        cost_estimate=CHEAP,
        name="attention_forward",
    )(at, qkv, *masks)


def attention_backward(at, qkv, raw, factor, out, pieces, lse, masks, begin=0, heads=None):
    _, all_heads, hd, t = qkv.shape
    heads = heads or all_heads
    block = min(256, t) if t <= 2048 else 512
    n = t // block
    whole = lambda shape: pl.BlockSpec(shape, lambda h: (0,) * len(shape))
    head = lambda wide=t: pl.BlockSpec((1, hd, wide), lambda h: (begin + h, 0, 0))
    return pl.pallas_call(
        functools.partial(backward_kernel, block),
        grid=(heads,),
        in_specs=[
            pl.BlockSpec(memory_space=pltpu.SMEM),
            pl.BlockSpec((3, 1, hd, t), lambda h: (0, begin + h, 0, 0)),
            head(),
            whole((hd, 1)),
            head(),
            pl.BlockSpec((1, 1, t), lambda h: (begin + h, 0, 0)),
            whole((1, t)),
            whole((t, 1)),
            whole((t, 1)),
        ]
        + [head(p.shape[2]) for p in pieces],
        out_specs=[
            pl.BlockSpec((3, 1, hd, t), lambda h: (0, h, 0, 0)),
            pl.BlockSpec((1, hd, 1), lambda h: (h, 0, 0)),
        ],
        out_shape=[
            jax.ShapeDtypeStruct((3, heads, hd, t), BF),
            jax.ShapeDtypeStruct((heads, hd, 1), F32),
        ],
        scratch_shapes=[
            pltpu.VMEM((n * (n + 1) // 2, block, block), F32),
            pltpu.VMEM((t, hd), BF),
            pltpu.VMEM((t, hd), BF),
            pltpu.VMEM((hd, t), F32),
            pltpu.VMEM((hd, t), F32),
            pltpu.VMEM((hd, t), BF),
        ],
        compiler_params=pltpu.CompilerParams(vmem_limit_bytes=VMEM_LIMIT),
        cost_estimate=CHEAP,
        name="attention_backward",
    )(at, qkv, raw, factor, out, lse, *masks, *pieces)


def norm_scale(x):
    return lax.rsqrt(jnp.mean(x * x, axis=1, keepdims=True) + EPS)


def body_any(
    inputs, gain_attn, w_qkv, query_scale, w_out, gain_mlp, w_up, b_up, w_down, b_down, series_ids, pad_mask, cotangent
):
    rows, cols = size("row"), size("col")
    tok = inputs.shape[0]
    feat = inputs.shape[1]
    share = tok // cols
    t = series_ids.shape[0]
    head_rows = w_qkv.shape[2] // cols
    heads = head_rows // HEAD_DIM
    r, c = lax.axis_index("row"), lax.axis_index("col")

    blocks = gather_grid(inputs)
    strips = [jnp.concatenate(b, axis=1) for b in blocks]
    x_own = strips[0] if rows == 2 else lax.dynamic_index_in_dim(jnp.stack(strips), r, 0, keepdims=False)
    x_all = jnp.concatenate(flip(strips, "row"), axis=0)
    gain_one = jnp.concatenate(gather(gain_attn, "col"))
    gain_two = jnp.concatenate(gather(gain_mlp, "col"))
    bias_up = jnp.concatenate(gather(b_up, "row")).astype(F32)
    bias_down = jnp.concatenate(gather(b_down, "col")).astype(F32)

    w3 = jnp.transpose(w_qkv, (1, 0, 2)).reshape(3, feat, cols, head_rows)
    w_mine = lax.dynamic_index_in_dim(w3, c, 2, keepdims=False)
    w_give = lax.dynamic_index_in_dim(w3, 1 - c, 2, keepdims=False)
    w_half = swap(core_half(w_give, 1), "col")
    w_other = swap(w_half, "core")
    first = lax.axis_index("core") == 0
    w_full = jnp.concatenate(
        [w_mine, jnp.where(first, w_half, w_other), jnp.where(first, w_other, w_half)], axis=1
    )

    xf = x_all.astype(F32)
    scale_one = norm_scale(xf)
    normed_one = (xf * scale_one * gain_one).astype(BF)
    projected = jnp.einsum("td,sdh->sht", normed_one, w_full, preferred_element_type=F32)
    projected = projected.reshape(3, heads, HEAD_DIM, t)
    factor = QUERY_CONST / math.sqrt(HEAD_DIM) * jax.nn.softplus(query_scale)
    raw_q = projected[0]
    qkv = jnp.stack([raw_q * factor[None, :, None], projected[1], projected[2]]).astype(BF)
    masks = mask_args(series_ids, pad_mask)
    at = jnp.zeros((4,), jnp.int32)
    attended, lse = attention_forward(at, qkv, masks)

    def to_tokens(y):
        y = flip_dim(y.reshape(head_rows, rows, cols, share), "row", 1)
        y = flip_dim(y, "col", 2)
        y = exchange(y.reshape(1, head_rows, rows, cols, share), "row", 2, 0)
        y = exchange(y.reshape(rows, 1, head_rows, cols, share), "col", 3, 1)
        y = flip_dim(y.reshape(rows, cols, head_rows, share), "col", 1)
        return y.reshape(rows * cols * head_rows, share)

    def to_heads(y):
        y = flip_dim(y.reshape(rows, cols, head_rows, share), "col", 1)
        y = exchange(y.reshape(rows, cols, head_rows, 1, share), "col", 1, 3)
        y = exchange(y.reshape(rows, head_rows, 1, cols, share), "row", 0, 2)
        y = flip_dim(y.reshape(head_rows, rows, cols, share), "col", 2)
        return flip_dim(y, "row", 1).reshape(head_rows, t)

    w_out_all = weight_gather(w_out, 0)
    w_up_all = weight_gather(w_up, 1)
    w_down_all = weight_gather(w_down, 0)

    def my_share(y):
        return lax.dynamic_slice_in_dim(y, c * share, share, 0)

    att = to_tokens(attended.reshape(head_rows, t))
    x_mine = my_share(x_own).astype(F32)
    middle = x_mine + dot(att, w_out_all, (0, 0))
    scale_two = norm_scale(middle)
    normed_two = (middle * scale_two * gain_two).astype(BF)
    pre_act = dot(normed_two, w_up_all, (1, 0)) + bias_up
    sig = jax.nn.sigmoid(pre_act)
    hidden = (pre_act * sig).astype(BF)
    result = (middle + dot(hidden, w_down_all, (1, 0)) + bias_down).astype(BF)

    def to_block(y):
        mine, theirs = jnp.split(y, 2, axis=1)
        return jnp.concatenate(flip([mine, swap(theirs, "col")], "col"), axis=0)

    layer_out = to_block(result)

    g_give = lax.dynamic_slice_in_dim(cotangent, (1 - c) * share, share, 0)
    g = jnp.concatenate([my_share(cotangent), swap(g_give, "col")], axis=1)
    grad_w_down = dot(hidden, g, (0, 0))
    grad_hidden = dot(g, w_down_all, (1, 1))
    grad_pre_f = grad_hidden * sig * (1.0 + pre_act * (1.0 - sig))
    grad_pre = grad_pre_f.astype(BF)
    grad_b_up = jnp.sum(grad_pre.astype(F32), axis=0)
    grad_w_up = dot(normed_two, grad_pre, (0, 0))
    grad_normed_two = dot(grad_pre, w_up_all, (1, 1))
    weighted = grad_normed_two * gain_two
    inner = jnp.sum(weighted * middle, axis=1, keepdims=True)
    grad_middle = g.astype(F32) + scale_two * weighted - middle * (scale_two**3 * inner / D)
    grad_gain_mlp = jnp.sum(grad_normed_two * middle * scale_two, axis=0)
    grad_branch = grad_middle.astype(BF)
    grad_w_out = dot(att, grad_branch, (1, 0))
    grad_att = dot(w_out_all, grad_branch, (1, 1)).astype(BF)
    grad_attended = to_heads(grad_att).reshape(heads, HEAD_DIM, t)
    grad_middle_block = to_block(grad_middle)

    sum_down = weight_sum(grad_w_down, 0)
    sum_up = weight_sum(grad_w_up, 1)
    sum_out = weight_sum(grad_w_out, 0)

    grad_proj, gscale = attention_backward(
        at, qkv, raw_q, factor.reshape(HEAD_DIM, 1), attended, [grad_attended], lse, masks
    )
    slope = QUERY_CONST / math.sqrt(HEAD_DIM) * jax.nn.sigmoid(query_scale)
    grad_query_scale = jnp.sum(gscale, axis=(0, 2)) * slope
    grad_proj = grad_proj.reshape(3, head_rows, t)
    grad_normed_one = jnp.einsum("sht,sdh->td", grad_proj, w_full, preferred_element_type=F32)
    weighted_one = grad_normed_one * gain_one
    inner_one = jnp.sum(weighted_one * xf, axis=1)
    grad_gain_attn = jnp.sum(grad_normed_one * xf * scale_one, axis=0)
    inner_one = lax.psum(inner_one, ("row", "col"))
    grad_w = jnp.einsum("td,sht->sdh", normed_one, grad_proj, preferred_element_type=F32)
    grad_w = grad_w.reshape(3, cols, 2, feat // 2, head_rows)
    core = lax.axis_index("core")
    keep = lax.dynamic_index_in_dim(grad_w, core, 2, keepdims=False)
    give = lax.dynamic_index_in_dim(grad_w, 1 - core, 2, keepdims=False).astype(BF)
    part = (keep + swap(give, "core").astype(F32)).astype(BF)
    part = jnp.concatenate(flip([part[:, 0], swap(part[:, 1], "col")], "col"), axis=2)
    sum_qkv = jnp.transpose(z_sum(part), (1, 0, 2))

    e = jnp.concatenate(flip(jnp.split(grad_normed_one.astype(BF), 2, axis=0), "row"), axis=0) if rows == 2 else (
        grad_normed_one.astype(BF)
    )
    e = scatter_sum(e, "row", 0)
    e = scatter_sum(e, "col", 1).astype(F32)
    my_rows = lambda y: lax.dynamic_slice_in_dim(y, r * tok, tok, 0)
    scale_mine = my_rows(scale_one)
    inner_mine = my_rows(inner_one.reshape(t, 1))
    grad_inputs = grad_middle_block + scale_mine * (e * gain_attn) - inputs.astype(F32) * (
        scale_mine**3 * inner_mine / D
    )

    grad_b_down = jnp.sum(g.astype(F32), axis=0)
    vectors = jnp.concatenate(
        [
            flip_dim(grad_gain_attn, "col", 0),
            flip_dim(grad_gain_mlp, "col", 0),
            flip_dim(grad_b_down, "col", 0),
            flip_dim(grad_b_up, "row", 0),
            grad_query_scale,
        ]
    )
    vectors = lax.psum(vectors, ("z", "core", "row", "col"))
    mine_col = lambda at: lax.dynamic_slice_in_dim(vectors, at * D + c * feat, feat, 0)
    units = b_up.shape[0]
    return (
        layer_out,
        grad_inputs,
        mine_col(0),
        sum_qkv,
        vectors[4 * D :],
        sum_out,
        mine_col(1),
        sum_up,
        lax.dynamic_slice_in_dim(vectors, 3 * D + r * units, units, 0),
        sum_down,
        mine_col(2),
    )


SMEM = pl.BlockSpec(memory_space=pltpu.SMEM)
ANY = pl.BlockSpec(memory_space=pl.ANY)


def call(kernel, name, args, specs, outs, scratch=(), **more):
    return pl.pallas_call(
        kernel,
        in_specs=specs,
        out_shape=outs,
        scratch_shapes=list(scratch),
        compiler_params=pltpu.CompilerParams(vmem_limit_bytes=VMEM_LIMIT),
        cost_estimate=CHEAP,
        name=name,
        **more,
    )(*args)


VM = pl.BlockSpec(memory_space=pltpu.VMEM)


def shape(dims, kind):
    return jax.ShapeDtypeStruct(dims, kind)


def project_kernel(
    at, x00, x01, x10, x11, gain, factor, w_mine, w_a, w_b, qkv, raw, normed, scale_own, w_full
):
    r, k = at[0], at[2]
    tok, feat = x00.shape
    hr = w_mine.shape[1]
    half = hr // 2
    for s in range(3):
        w_full[pl.ds(s * hr, hr), 0:feat] = w_mine[s]
        w_full[pl.ds(pl.multiple_of(s * hr + k * half, 16), half), feat:] = w_a[s]
        w_full[pl.ds(pl.multiple_of(s * hr + (1 - k) * half, 16), half), feat:] = w_b[s]
    for i, (a_ref, b_ref) in enumerate(((x00, x01), (x10, x11))):
        a, b = a_ref[...].astype(F32), b_ref[...].astype(F32)
        total = jnp.sum(a * a, axis=1, keepdims=True) + jnp.sum(b * b, axis=1, keepdims=True)
        scale = lax.rsqrt(total / (2 * feat) + EPS)
        if i == 0:
            scale_own[...] = scale
        rows = pl.ds(pl.multiple_of((r ^ i) * tok, tok), tok)
        normed[rows, 0:feat] = (a * scale * gain[:, 0:feat]).astype(BF)
        normed[rows, feat:] = (b * scale * gain[:, feat:]).astype(BF)
        y = normed[rows, :]
        q = dot(w_full[0:hr, :], y, (1, 1))
        raw[:, rows] = q
        qkv[0, :, rows] = (q * factor[...]).astype(BF)
        qkv[1, :, rows] = dot(w_full[hr : 2 * hr, :], y, (1, 1)).astype(BF)
        qkv[2, :, rows] = dot(w_full[2 * hr : 3 * hr, :], y, (1, 1)).astype(BF)


def feed_kernel(
    at, a0, a1, a2, a3, x_own, x_col, g_own, g_col, gain, bias_up, bias_down,
    w_out, w_up, w_down, hx, hy, d0, d1, hx2, hy2, d02, d12,
    out_own, out_give, gm_own, gm_give, t0, t1, t2, t3, vectors,
    sx, sy, kx, ky, sx2, sy2, kx2, ky2,
    w, att, turned, sems,
):
    r, c, k = at[0], at[1], at[2]
    hr, share = a0.shape
    feat = x_own.shape[1]
    half = feat // 2
    quarter = half // 2
    copies = []
    for n, shard in enumerate((w_out, w_up, w_down)):
        rx, cx, ry, cy = (0, feat, feat, 0) if n == 1 else (feat, 0, 0, feat)
        mine = []
        mine.append((shard, w.at[n, 0:feat, 0:feat]))
        for core, (px, py, p0, p1) in ((k, (hx, hy, d0, d1)), (1 - k, (hx2, hy2, d02, d12))):
            down = core * half
            at_x = pl.ds(pl.multiple_of(rx + down, 16), half)
            at_y = pl.ds(pl.multiple_of(ry + down, 16), half)
            at_0 = pl.ds(pl.multiple_of(feat + down, 16), quarter)
            at_1 = pl.ds(pl.multiple_of(feat + down + quarter, 16), quarter)
            mine.append((px.at[n], w.at[n, at_x, cx : cx + feat]))
            mine.append((py.at[n], w.at[n, at_y, cy : cy + feat]))
            mine.append((p0.at[n], w.at[n, at_0, feat : 2 * feat]))
            mine.append((p1.at[n], w.at[n, at_1, feat : 2 * feat]))
        started = []
        for m, (src, dst) in enumerate(mine):
            copy = pltpu.make_async_copy(src, dst, sems.at[n, m])
            copy.start()
            started.append(copy)
        copies.append(started)

    rows = pl.ds(pl.multiple_of(c * share, share), share)
    for s, a in enumerate((a0, a1, a2, a3)):
        to = (s // 2) * 2 * hr + (c ^ (s % 2)) * hr
        att[pl.ds(pl.multiple_of(to, 16), hr), :] = a[...]
    x = jnp.concatenate([x_own[rows, :], x_col[rows, :]], axis=1).astype(F32)
    g = jnp.concatenate([g_own[rows, :], g_col[...]], axis=1)
    for copy in copies[0]:
        copy.wait()
    middle = x + dot(att[...], w[0], (0, 0))
    scale = lax.rsqrt(jnp.sum(middle * middle, axis=1, keepdims=True) / D + EPS)
    normed = (middle * scale * gain[...]).astype(BF)
    for copy in copies[1]:
        copy.wait()
    pre = dot(normed, w[1], (1, 0)) + bias_up[...]
    sig = jax.nn.sigmoid(pre)
    hidden = (pre * sig).astype(BF)
    for copy in copies[2]:
        copy.wait()
    result = (middle + dot(hidden, w[2], (1, 0)) + bias_down[...]).astype(BF)
    out_own[...] = result[:, :feat]
    out_give[...] = result[:, feat:]

    def weight_grad(n, left_ref, right):
        for core, by_row, by_col in ((k, (sx, kx), (sy, ky)), (1 - k, (sx2, kx2), (sy2, ky2))):
            up, low = (by_col, by_row) if n == 1 else (by_row, by_col)
            for b in range(2):
                part = pl.ds(pl.multiple_of(b * feat + core * half, 16), half)
                y = dot(left_ref[part, :], right, (1, 0)).astype(BF)
                for j in range(2):
                    cut = slice(j * feat, (j + 1) * feat)
                    up[1 - b][j, n] = y[:quarter, cut]
                    low[1 - j][b, n] = y[quarter:, cut]

    turned[...] = hidden.astype(F32).T.astype(BF)
    grad_pre_f = dot(g, w[2], (1, 1)) * sig * (1.0 + pre * (1.0 - sig))
    grad_pre = grad_pre_f.astype(BF)
    weight_grad(2, turned, g)
    grad_normed = dot(grad_pre, w[1], (1, 1))
    weighted = grad_normed * gain[...]
    inner = jnp.sum(weighted * middle, axis=1, keepdims=True)
    gf = g.astype(F32)
    grad_middle = gf + scale * weighted - middle * (scale * scale * scale * inner / D)
    gm_own[...] = grad_middle[:, :feat]
    gm_give[...] = grad_middle[:, feat:].astype(BF)
    branch = grad_middle.astype(BF)
    for s, t in enumerate((t0, t1, t2, t3)):
        come = (s // 2) * 2 * hr + (c ^ (s % 2)) * hr
        t[...] = dot(w[0, pl.ds(pl.multiple_of(come, 16), hr), :], branch, (1, 1)).astype(BF)
    turned[...] = normed.astype(F32).T.astype(BF)
    weight_grad(1, turned, grad_pre)
    weight_grad(0, att, branch)
    vectors[...] = jnp.concatenate(
        [
            jnp.sum(grad_normed * (middle * scale), axis=0, keepdims=True),
            jnp.sum(gf, axis=0, keepdims=True),
            jnp.sum(grad_pre.astype(F32), axis=0, keepdims=True),
        ],
        axis=0,
    )


def weight_back_kernel(at, grad, normed, keep, give):
    k = at[2]
    part = keep.shape[2]
    feat = keep.shape[3]
    for ref, core in ((give, 1 - k), (keep, k)):
        for s in range(3):
            rows = pl.ds(pl.multiple_of(core * part, 16), part)
            y = dot(grad[s, rows, :], normed[...], (1, 0)).astype(BF)
            ref[0, s] = y[:, :feat]
            ref[1, s] = y[:, feat:]


def project_back_kernel(
    at, grad_a, grad_b, w_full, x00, x01, x10, x11, gain, e0, e1, e2, e3, inner_own, gain_sum, grad
):
    r = at[0]
    tok, feat = x00.shape
    part = grad_a.shape[1]
    for s in range(3):
        for n, ref in enumerate((grad_a, grad_b)):
            grad[(2 * s + n) * part : (2 * s + n + 1) * part, :] = ref[s]
    sums = [jnp.zeros((1, feat), F32), jnp.zeros((1, feat), F32)]
    for i, (xs, es) in enumerate((((x00, x01), (e0, e1)), ((x10, x11), (e2, e3)))):
        rows = pl.ds(pl.multiple_of((r ^ i) * tok, tok), tok)
        left = grad[:, rows]
        products, squares, inner = [], 0.0, 0.0
        for j in range(2):
            cut = slice(j * feat, (j + 1) * feat)
            e = dot(left, w_full[:, cut], (0, 0))
            x = xs[j][...].astype(F32)
            product = e * x
            inner = inner + jnp.sum(product * gain[:, cut], axis=1, keepdims=True)
            squares = squares + jnp.sum(x * x, axis=1, keepdims=True)
            es[j][0:tok, :] = e.astype(es[j].dtype)
            products.append(product)
        scale = lax.rsqrt(squares / (2 * feat) + EPS)
        for j in range(2):
            sums[j] += jnp.sum(products[j] * scale, axis=0, keepdims=True)
        line = jnp.broadcast_to(inner, (tok, 128)).T[0:1, :]
        high = line.astype(BF).astype(F32)
        extra = jnp.concatenate([high, line - high, jnp.zeros((14, tok), F32)], axis=0)
        extra = jnp.concatenate([extra, jnp.zeros((16, feat - tok), F32)], axis=1).astype(BF)
        if i == 0:
            inner_own[...] = inner
            es[1][tok:, :] = extra
        else:
            es[0][tok:, :] = extra
            es[1][tok:, :] = extra
    gain_sum[:, 0:feat] = sums[0]
    gain_sum[:, feat:] = sums[1]


def finish_qkv_kernel(at, *refs):
    c, k = at[1], at[2]
    *parts, out, rows = refs
    half = parts[0].shape[1]
    for s in range(3):
        for pair in range(2):
            mine, theirs, mine2, theirs2 = parts[4 * pair : 4 * pair + 4]
            for ref, col, core in ((mine, c, k), (theirs, 1 - c, k), (mine2, c, 1 - k), (theirs2, 1 - c, 1 - k)):
                to = pl.multiple_of((4 * col + 2 * pair + core) * half, 16)
                rows[pl.ds(to, half), :] = ref[s].astype(F32)
        out[s] = rows[...].T


def finish_feed_kernel(at, a, b, a2, b2, *outs):
    k = at[2]
    quarter = a.shape[1]
    for n, out in enumerate(outs):
        upper, lower = ((b, b2), (a, a2)) if n == 1 else ((a, a2), (b, b2))
        for i, core in ((0, k), (1, 1 - k)):
            for j, refs in enumerate((upper, lower)):
                to = pl.multiple_of((2 * core + j) * quarter, 16)
                out[pl.ds(to, quarter), :] = refs[i][n].astype(F32)


def after(x, *earlier):
    return lax.optimization_barrier((x, *earlier))[0]


def add(*parts):
    total = parts[0].astype(F32)
    for part in parts[1:]:
        total = total + part.astype(F32)
    return total.astype(BF)


def diagonal(x):
    return lax.ppermute(x, ("row", "col"), [(0, 3), (1, 2), (2, 1), (3, 0)])


def z_swap(x, step):
    n = size("z")
    return lax.ppermute(x, "z", [(i, i ^ step) for i in range(n)])


def z_total(a, b):
    if size("z") != 4:
        return lax.psum((a, b), "z")
    z = lax.axis_index("z")
    first = (z == 0) | (z == 3)
    mine = add(jnp.where(first, a, b), z_swap(jnp.where(first, b, a), 1))
    mine = add(mine, z_swap(mine, 3))
    other = z_swap(mine, 1)
    return jnp.where(first, mine, other), jnp.where(first, other, mine)


def body_four(
    inputs, gain_attn, w_qkv, query_scale, w_out, gain_mlp, w_up, b_up, w_down, b_down, series_ids, pad_mask, cotangent
):
    tok, feat = inputs.shape
    share = tok // 2
    t = series_ids.shape[0]
    hr = w_qkv.shape[2] // 2
    heads = hr // HEAD_DIM
    half = feat // 2
    r, c, k = lax.axis_index("row"), lax.axis_index("col"), lax.axis_index("core")
    at = jnp.stack([r, c, k, 2 * r + c]).astype(jnp.int32)
    mine_rows = lambda y, part: lax.dynamic_slice_in_dim(y, part * share, share, 0)

    x01 = swap(inputs, "col")
    x10 = swap(inputs, "row")
    small = swap(jnp.concatenate([gain_attn, gain_mlp, b_down.astype(F32)]), "col")
    up_other = swap(b_up.astype(F32), "row")
    w_turned = jnp.transpose(w_qkv, (1, 2, 0)).reshape(3, 2, hr, feat)
    w_mine = lax.dynamic_index_in_dim(w_turned, c, 1, keepdims=False)
    w_give = lax.dynamic_index_in_dim(w_turned, 1 - c, 1, keepdims=False)
    w_half = core_half(w_give, 1)
    w_a = swap(w_half, "col")
    g_col = swap(mine_rows(cotangent, 1 - c), "col")
    x01, x10, small, up_other = lax.optimization_barrier((x01, x10, small, up_other))
    x11 = swap(after(x01, w_half), "row")
    w_b = swap(w_a, "core")
    gain_one = jnp.concatenate([gain_attn, small[:feat]]).reshape(1, D)
    gain_two = jnp.concatenate([gain_mlp, small[feat : 2 * feat]]).reshape(1, D)
    bias_down = jnp.concatenate([b_down.astype(F32), small[2 * feat :]]).reshape(1, D)
    bias_up = jnp.concatenate([b_up.astype(F32), up_other]).reshape(1, D)
    factor = QUERY_CONST / math.sqrt(HEAD_DIM) * jax.nn.softplus(query_scale)
    factor_col = factor.reshape(HEAD_DIM, 1)

    part = jnp.stack([core_half(w_out, 0), core_half(w_up, 0), core_half(w_down, 0)])
    part = after(part, x11, w_a, g_col)
    hx, hy = swap(part, "row"), swap(part, "col")
    hx2, hy2 = swap(hx, "core"), swap(hy, "core")
    qkv, raw, normed_one, scale_own, w_full = call(
        project_kernel,
        "project",
        (at, inputs, x01, x10, x11, gain_one, jnp.tile(factor_col, (heads, 1)), w_mine, w_a, w_b),
        [SMEM] + [VM] * 9,
        [
            shape((3, hr, t), BF),
            shape((hr, t), F32),
            shape((t, D), BF),
            shape((tok, 1), F32),
            shape((3 * hr, D), BF),
        ],
    )
    qkv = qkv.reshape(3, heads, HEAD_DIM, t)
    masks = mask_args(series_ids, pad_mask)
    attended, lse, *a = attention_forward(at, qkv, masks, pieces=4)
    a0, a1, a2, a3 = [p.reshape(hr, share) for p in a]
    a1, a2, a3 = swap(a1, "col"), swap(a2, "row"), diagonal(a3)
    hx_on, hy_on, a1, a2, a3 = lax.optimization_barrier((hx, hy, a1, a2, a3))
    d0 = swap(hx_on[:, : half // 2], "col")
    d1 = swap(hy_on[:, half // 2 :], "row")
    d02, d12 = swap(d0, "core"), swap(d1, "core")
    out_own, out_give, gm_own, gm_give, t0, t1, t2, t3, vectors, *grads = call(
        feed_kernel,
        "feed_forward",
        (at, a0, a1, a2, a3, inputs, x01, cotangent, g_col, gain_two, bias_up, bias_down)
        + (w_out, w_up, w_down, hx, hy, d0, d1, hx2, hy2, d02, d12),
        [SMEM] + [VM] * 11 + [ANY] * 11,
        [
            shape((share, feat), BF),
            shape((share, feat), BF),
            shape((share, feat), F32),
            shape((share, feat), BF),
        ]
        + [shape((hr, share), BF)] * 4
        + [shape((3, D), F32)]
        + [shape((2, 3, half // 2, feat), BF)] * 8,
        scratch=[
            pltpu.VMEM((3, D, D), BF),
            pltpu.VMEM((D, share), BF),
            pltpu.VMEM((D, share), BF),
            pltpu.SemaphoreType.DMA((3, 9)),
        ],
    )
    t1, t2, t3 = swap(t1, "col"), swap(t2, "row"), diagonal(t3)
    sx, sy, kx, ky, *other_core = grads
    sx2, sy2, kx2, ky2 = [swap(y, "core") for y in other_core]
    sx, sy = add(sx, sx2), add(sy, sy2)
    pieces = lax.optimization_barrier((t0, t1, t2, t3, sx, sy))[:4]
    rx, ry = swap(sx, "row"), swap(sy, "col")
    pieces = [p.reshape(heads, HEAD_DIM, share) for p in pieces]
    raw = raw.reshape(heads, HEAD_DIM, t)
    few = heads // 2

    def weight_back(grad):
        kept, sent = call(
            weight_back_kernel,
            "weight_back",
            (at, grad, normed_one),
            [SMEM] + [VM] * 2,
            [shape((2, 3, hr // 4, feat), BF)] * 2,
        )
        return add(kept, swap(sent, "core"))

    grad_a, scale_a = attention_backward(at, qkv, raw, factor_col, attended, pieces, lse, masks, 0, few)
    grad_a = grad_a.reshape(3, hr // 2, t)
    w_pair_a = weight_back(grad_a)
    lse_on = after(lse, w_pair_a)
    grad_b, scale_b = attention_backward(at, qkv, raw, factor_col, attended, pieces, lse_on, masks, few, few)
    grad_b = grad_b.reshape(3, hr // 2, t)
    w_pair_b = weight_back(grad_b)
    slope = QUERY_CONST / math.sqrt(HEAD_DIM) * jax.nn.sigmoid(query_scale)
    grad_query_scale = (jnp.sum(scale_a, axis=(0, 2)) + jnp.sum(scale_b, axis=(0, 2))) * slope
    e0, e1, e2, e3, inner, gain_sum = call(
        project_back_kernel,
        "project_back",
        (at, grad_a, after(grad_b, w_pair_b), w_full, inputs, x01, x10, x11, gain_one),
        [SMEM] + [VM] * 8,
        [
            shape((tok, feat), F32),
            shape((tok + 16, feat), BF),
            shape((tok + 16, feat), BF),
            shape((tok + 16, feat), BF),
            shape((tok, 1), F32),
            shape((1, D), F32),
        ],
        scratch=[pltpu.VMEM((3 * hr, t), BF)],
    )
    w_args = [at]
    for w_pair in (w_pair_a, w_pair_b):
        w_own, w_theirs = z_total(w_pair[0], w_pair[1])
        w_theirs = swap(w_theirs, "col")
        w_args += [w_own, w_theirs, swap(w_own, "core"), swap(w_theirs, "core")]
    sum_qkv = call(
        finish_qkv_kernel,
        "finish_qkv",
        w_args,
        [SMEM] + [VM] * 8,
        shape((3, feat, 2 * hr), F32),
        scratch=[pltpu.VMEM((2 * hr, feat), F32)],
    )
    sum_qkv = jnp.transpose(sum_qkv, (1, 0, 2))

    px, py = add(kx, kx2, rx), add(ky, ky2, ry)
    qx, qy = swap(px[1], "col"), swap(py[1], "row")
    fx, fy = add(px[0], qx), add(py[0], qy)
    e1, e2, e3, out_give, gm_give, fx, fy = lax.optimization_barrier((e1, e2, e3, out_give, gm_give, fx, fy))
    fx, fy = z_total(fx, fy)
    sum_out, sum_up, sum_down = call(
        finish_feed_kernel,
        "finish_feed",
        (at, fx, fy, swap(fx, "core"), swap(fy, "core")),
        [SMEM] + [VM] * 4,
        [shape((feat, feat), F32)] * 3,
    )

    e1, e2, e3 = swap(e1, "col"), swap(e2, "row"), diagonal(e3)
    e = e0
    for more in (e1, e2, e3):
        e = e + more[:tok].astype(F32)
        inner = inner + jnp.sum(more[tok : tok + 2, :tok].astype(F32), axis=0).reshape(tok, 1)
    gm_col = swap(gm_give, "col").astype(F32)
    grad_middle = jnp.concatenate(flip([gm_own, gm_col], "col"), axis=0)
    grad_inputs = grad_middle + scale_own * (e * gain_attn) - inputs.astype(F32) * (scale_own**3 * inner / D)
    layer_out = jnp.concatenate(flip([out_own, swap(out_give, "col")], "col"), axis=0)

    total = jnp.concatenate(
        [
            flip_dim(gain_sum[0], "col", 0),
            flip_dim(vectors[0], "col", 0),
            flip_dim(vectors[1], "col", 0),
            flip_dim(vectors[2], "row", 0),
            grad_query_scale,
        ]
    )
    total = after(total, fx)
    total = total + swap(total, "core")
    total = (total + swap(total, "row")) + (swap(total, "col") + diagonal(total))
    total = after(total, w_own)
    if size("z") == 4:
        total = (total + z_swap(total, 1)) + (z_swap(total, 2) + z_swap(total, 3))
    else:
        total = lax.psum(total, "z")
    mine_col = lambda n: lax.dynamic_slice_in_dim(total, n * D + c * feat, feat, 0)
    units = b_up.shape[0]
    return (
        layer_out,
        grad_inputs,
        mine_col(0),
        sum_qkv,
        total[4 * D :],
        sum_out,
        mine_col(1),
        sum_up,
        lax.dynamic_slice_in_dim(total, 3 * D + r * units, units, 0),
        sum_down,
        mine_col(2),
    )


def solution(mesh):
    dp, rows, cols = mesh.shape["dp"], mesh.shape["row"], mesh.shape["col"]
    split = Mesh(mesh.devices.reshape(dp // 2, 2, rows, cols), ("z", "core", "row", "col"))
    tokens = P(("z", "core", "row"), "col")
    in_specs = (
        tokens,
        P("col"),
        P("col", None, "row"),
        P(),
        P("row", "col"),
        P("col"),
        P("col", "row"),
        P("row"),
        P("row", "col"),
        P("col"),
        P(("z", "core")),
        P(("z", "core")),
        tokens,
    )
    out_specs = (
        tokens,
        tokens,
        P("col"),
        P("col", None, "row"),
        P(),
        P("row", "col"),
        P("col"),
        P("col", "row"),
        P("row"),
        P("row", "col"),
        P("col"),
    )
    body = body_four if rows == 2 and cols == 2 else body_any
    return jax.shard_map(body, mesh=split, in_specs=in_specs, out_specs=out_specs, check_vma=False)
```

```python
import functools
import math

import jax
import jax.numpy as jnp
from jax import lax
from jax.experimental import pallas as pl
from jax.experimental.pallas import tpu as pltpu
from jax.sharding import Mesh
from jax.sharding import PartitionSpec as P

D = 1280
HEAD_DIM = 80
EPS = 1e-06
QUERY_CONST = 1.442695041
MASKED = -1e30
BF = jnp.bfloat16
F32 = jnp.float32
VMEM_LIMIT = 50 * 1024 * 1024
CHEAP = pl.CostEstimate(flops=1, bytes_accessed=1, transcendentals=0)


def size(axis):
    return lax.axis_size(axis)


def swap(x, axis):
    return lax.ppermute(x, axis, [(0, 1), (1, 0)])


def flip(blocks, axis):
    if size(axis) != 2:
        return list(blocks)
    first = lax.axis_index(axis) == 0
    a, b = blocks
    return [jnp.where(first, a, b), jnp.where(first, b, a)]


def flip_dim(x, axis, dim):
    if size(axis) != 2:
        return x
    return jnp.concatenate(flip(jnp.split(x, 2, axis=dim), axis), axis=dim)


def gather(x, axis):
    if size(axis) == 2:
        return [x, swap(x, axis)]
    whole = lax.all_gather(x, axis, axis=0, tiled=False)
    return [whole[i] for i in range(size(axis))]


def gather_grid(x):
    if size("row") != 2:
        return [gather(b, "col") for b in gather(x, "row")]
    along_row, along_col = swap(x, "row"), swap(x, "col")
    half = x.shape[0] // 2
    across = jnp.concatenate(
        [swap(along_row[:half], "col"), swap(along_col[half:], "row")], axis=0
    )
    return [[x, along_col], [along_row, across]]


def scatter_sum(x, axis, dim):
    if size(axis) != 2:
        return lax.psum_scatter(x, axis, scatter_dimension=dim, tiled=True)
    mine, theirs = jnp.split(x, 2, axis=dim)
    return (mine.astype(F32) + swap(theirs, axis).astype(F32)).astype(x.dtype)


def exchange(x, axis, split, join):
    if size(axis) != 2:
        return lax.all_to_all(x, axis, split, join, tiled=True)
    mine, theirs = jnp.split(x, 2, axis=split)
    return jnp.concatenate([mine, swap(theirs, axis)], axis=join)


def core_half(x, dim):
    return lax.dynamic_slice_in_dim(
        x, lax.axis_index("core") * (x.shape[dim] // 2), x.shape[dim] // 2, dim
    )


def weight_gather(w, row_dim):
    part = core_half(w, 0)
    blocks = gather_grid(part)
    if row_dim == 1:
        blocks = [list(b) for b in zip(*blocks)]
    mine = jnp.stack([jnp.concatenate(b, axis=1) for b in blocks])
    other = swap(mine, "core")
    first = lax.axis_index("core") == 0
    both = jnp.stack([jnp.where(first, mine, other), jnp.where(first, other, mine)], axis=1)
    return both.reshape(-1, both.shape[-1])


def weight_sum(g, row_dim):
    dim_axis = ("row", "col") if row_dim == 0 else ("col", "row")
    n0 = size(dim_axis[0])
    g = g.reshape(n0, 2, g.shape[0] // n0 // 2, g.shape[1])
    core = lax.axis_index("core")
    keep = lax.dynamic_index_in_dim(g, core, 1, keepdims=False)
    give = lax.dynamic_index_in_dim(g, 1 - core, 1, keepdims=False).astype(BF)
    part = (keep + swap(give, "core").astype(F32)).astype(BF)
    part = scatter_sum(part, dim_axis[0], 0)
    part = scatter_sum(part[0], dim_axis[1], 1)
    return z_sum(part)


def z_sum(part):
    total = lax.psum(part, "z")
    other = swap(total, "core")
    return flip_core(total, other)


def flip_core(total, other):
    first = lax.axis_index("core") == 0
    return jnp.concatenate(
        [jnp.where(first, total, other), jnp.where(first, other, total)], axis=-2
    ).astype(F32)


def dot(a, b, contract):
    return lax.dot_general(a, b, ((contract[0:1], contract[1:2]), ((), ())), preferred_element_type=F32)


def bias_block(series_row, series_col, key_pos, q0, k0, qb, kb, diagonal):
    q_pos = q0 + lax.broadcasted_iota(jnp.int32, (1, qb), 1)
    allowed = (series_col == series_row) & (key_pos <= q_pos)
    if diagonal:
        k_pos = k0 + lax.broadcasted_iota(jnp.int32, (kb, 1), 0)
        allowed = allowed | (k_pos == q_pos)
    return jnp.where(allowed, 0.0, MASKED)


def forward_kernel(block, at, qkv_ref, srow_ref, scol_ref, kpos_ref, out_ref, lse_ref, *rest):
    *pieces, bias_ref, krow_ref, s_ref, slot_ref = rest
    t = qkv_ref.shape[3]
    n = t // block
    krow_ref[...] = qkv_ref[1, 0].astype(F32).T.astype(BF)

    def bias_slot(j, i):
        return j * (j + 1) // 2 + i

    @pl.when(pl.program_id(0) == 0)
    def _():
        for j in range(n):
            for i in range(j + 1):
                keys = pl.ds(i * block, block)
                bias_ref[bias_slot(j, i)] = bias_block(
                    srow_ref[:, j * block : (j + 1) * block],
                    scol_ref[keys, :],
                    kpos_ref[keys, :],
                    j * block,
                    i * block,
                    block,
                    block,
                    i == j,
                )

    for j in range(n):
        cols = slice(j * block, (j + 1) * block)
        q = qkv_ref[0, 0, :, cols]
        top = None
        for i in range(j + 1):
            s = dot(krow_ref[i * block : (i + 1) * block, :], q, (1, 0)) + bias_ref[bias_slot(j, i)]
            s_ref[i * block : (i + 1) * block, :] = s
            here = jnp.max(s, axis=0, keepdims=True)
            top = here if top is None else jnp.maximum(top, here)
        total = jnp.zeros((1, block), F32)
        acc = jnp.zeros((HEAD_DIM, block), F32)
        for i in range(j + 1):
            p = jnp.exp(s_ref[i * block : (i + 1) * block, :] - top)
            total += jnp.sum(p, axis=0, keepdims=True)
            acc += dot(qkv_ref[2, 0, :, i * block : (i + 1) * block], p.astype(BF), (1, 0))
        found = (acc / total).astype(BF)
        out_ref[0, :, cols] = found
        if pieces:
            slot_ref[j ^ at[3]] = found
        lse_ref[0, :, cols] = top + jnp.log(total)
    for slot, piece in enumerate(pieces):
        piece[0] = slot_ref[slot]


def backward_kernel(
    block, at, qkv_ref, raw_ref, factor_ref, out_ref, lse_ref, srow_ref, scol_ref, kpos_ref, *rest
):
    *pieces, grad_ref, gscale_ref, bias_ref, krow_ref, vrow_ref, gk_ref, gv_ref, gout_ref = rest
    if len(pieces) == 1:
        gout_ref[...] = pieces[0][0]
    else:
        for slot, piece in enumerate(pieces):
            wide = piece.shape[2]
            gout_ref[:, pl.ds(pl.multiple_of((slot ^ at[3]) * wide, 128), wide)] = piece[0]
    t = qkv_ref.shape[3]
    n = t // block
    krow_ref[...] = qkv_ref[1, 0].astype(F32).T.astype(BF)
    vrow_ref[...] = qkv_ref[2, 0].astype(F32).T.astype(BF)

    def bias_slot(j, i):
        return j * (j + 1) // 2 + i

    @pl.when(pl.program_id(0) == 0)
    def _():
        for j in range(n):
            for i in range(j + 1):
                keys = pl.ds(i * block, block)
                bias_ref[bias_slot(j, i)] = bias_block(
                    srow_ref[:, j * block : (j + 1) * block],
                    scol_ref[keys, :],
                    kpos_ref[keys, :],
                    j * block,
                    i * block,
                    block,
                    block,
                    i == j,
                )

    gscale = jnp.zeros((HEAD_DIM, 1), F32)
    for j in range(n):
        cols = slice(j * block, (j + 1) * block)
        q = qkv_ref[0, 0, :, cols]
        go = gout_ref[:, cols]
        lse = lse_ref[0, :, cols]
        delta = jnp.sum(go.astype(F32) * out_ref[0, :, cols].astype(F32), axis=0, keepdims=True)
        gq = jnp.zeros((HEAD_DIM, block), F32)
        for i in range(j + 1):
            keys = slice(i * block, (i + 1) * block)
            s = dot(krow_ref[keys, :], q, (1, 0)) + bias_ref[bias_slot(j, i)]
            p = jnp.exp(s - lse)
            gp = dot(vrow_ref[keys, :], go, (1, 0))
            gs = (p * (gp - delta)).astype(BF)
            gq += dot(qkv_ref[1, 0, :, keys], gs, (1, 0))
            gk = dot(q, gs, (1, 1))
            gv = dot(go, p.astype(BF), (1, 1))
            if i == j:
                gk_ref[:, keys] = gk
                gv_ref[:, keys] = gv
            else:
                gk_ref[:, keys] += gk
                gv_ref[:, keys] += gv
        gscale += jnp.sum(gq * raw_ref[0, :, cols], axis=1, keepdims=True)
        grad_ref[0, 0, :, cols] = (gq * factor_ref[...]).astype(BF)
    grad_ref[1, 0] = gk_ref[...].astype(BF)
    grad_ref[2, 0] = gv_ref[...].astype(BF)
    gscale_ref[0] = gscale


def mask_args(series, padding):
    t = series.shape[0]
    pos = jnp.arange(t, dtype=jnp.int32)
    return series.reshape(1, t), series.reshape(t, 1), jnp.where(padding == 0, pos, t).reshape(t, 1)


def attention_forward(at, qkv, masks, pieces=0):
    _, heads, hd, t = qkv.shape
    block = min(256, t) if t <= 2048 else 512
    n = t // block
    whole = lambda shape: pl.BlockSpec(shape, lambda h: (0,) * len(shape))
    assert pieces in (0, n)
    return pl.pallas_call(
        functools.partial(forward_kernel, block),
        grid=(heads,),
        in_specs=[
            pl.BlockSpec(memory_space=pltpu.SMEM),
            pl.BlockSpec((3, 1, hd, t), lambda h: (0, h, 0, 0)),
            whole((1, t)),
            whole((t, 1)),
            whole((t, 1)),
        ],
        out_specs=[
            pl.BlockSpec((1, hd, t), lambda h: (h, 0, 0)),
            pl.BlockSpec((1, 1, t), lambda h: (h, 0, 0)),
        ]
        + [pl.BlockSpec((1, hd, block), lambda h: (h, 0, 0))] * pieces,
        out_shape=[
            jax.ShapeDtypeStruct((heads, hd, t), BF),
            jax.ShapeDtypeStruct((heads, 1, t), F32),
        ]
        + [jax.ShapeDtypeStruct((heads, hd, block), BF)] * pieces,
        scratch_shapes=[
            pltpu.VMEM((n * (n + 1) // 2, block, block), F32),
            pltpu.VMEM((t, hd), BF),
            pltpu.VMEM((t, block), F32),
            pltpu.VMEM((n, hd, block), BF),
        ],
        compiler_params=pltpu.CompilerParams(vmem_limit_bytes=VMEM_LIMIT),
        cost_estimate=CHEAP,
        name="attention_forward",
    )(at, qkv, *masks)


def attention_backward(at, qkv, raw, factor, out, pieces, lse, masks, begin=0, heads=None):
    _, all_heads, hd, t = qkv.shape
    heads = heads or all_heads
    block = min(256, t) if t <= 2048 else 512
    n = t // block
    whole = lambda shape: pl.BlockSpec(shape, lambda h: (0,) * len(shape))
    head = lambda wide=t: pl.BlockSpec((1, hd, wide), lambda h: (begin + h, 0, 0))
    return pl.pallas_call(
        functools.partial(backward_kernel, block),
        grid=(heads,),
        in_specs=[
            pl.BlockSpec(memory_space=pltpu.SMEM),
            pl.BlockSpec((3, 1, hd, t), lambda h: (0, begin + h, 0, 0)),
            head(),
            whole((hd, 1)),
            head(),
            pl.BlockSpec((1, 1, t), lambda h: (begin + h, 0, 0)),
            whole((1, t)),
            whole((t, 1)),
            whole((t, 1)),
        ]
        + [head(p.shape[2]) for p in pieces],
        out_specs=[
            pl.BlockSpec((3, 1, hd, t), lambda h: (0, h, 0, 0)),
            pl.BlockSpec((1, hd, 1), lambda h: (h, 0, 0)),
        ],
        out_shape=[
            jax.ShapeDtypeStruct((3, heads, hd, t), BF),
            jax.ShapeDtypeStruct((heads, hd, 1), F32),
        ],
        scratch_shapes=[
            pltpu.VMEM((n * (n + 1) // 2, block, block), F32),
            pltpu.VMEM((t, hd), BF),
            pltpu.VMEM((t, hd), BF),
            pltpu.VMEM((hd, t), F32),
            pltpu.VMEM((hd, t), F32),
            pltpu.VMEM((hd, t), BF),
        ],
        compiler_params=pltpu.CompilerParams(vmem_limit_bytes=VMEM_LIMIT),
        cost_estimate=CHEAP,
        name="attention_backward",
    )(at, qkv, raw, factor, out, lse, *masks, *pieces)


def norm_scale(x):
    return lax.rsqrt(jnp.mean(x * x, axis=1, keepdims=True) + EPS)


def body_any(
    inputs, gain_attn, w_qkv, query_scale, w_out, gain_mlp, w_up, b_up, w_down, b_down, series_ids, pad_mask, cotangent
):
    rows, cols = size("row"), size("col")
    tok = inputs.shape[0]
    feat = inputs.shape[1]
    share = tok // cols
    t = series_ids.shape[0]
    head_rows = w_qkv.shape[2] // cols
    heads = head_rows // HEAD_DIM
    r, c = lax.axis_index("row"), lax.axis_index("col")

    blocks = gather_grid(inputs)
    strips = [jnp.concatenate(b, axis=1) for b in blocks]
    x_own = strips[0] if rows == 2 else lax.dynamic_index_in_dim(jnp.stack(strips), r, 0, keepdims=False)
    x_all = jnp.concatenate(flip(strips, "row"), axis=0)
    gain_one = jnp.concatenate(gather(gain_attn, "col"))
    gain_two = jnp.concatenate(gather(gain_mlp, "col"))
    bias_up = jnp.concatenate(gather(b_up, "row")).astype(F32)
    bias_down = jnp.concatenate(gather(b_down, "col")).astype(F32)

    w3 = jnp.transpose(w_qkv, (1, 0, 2)).reshape(3, feat, cols, head_rows)
    w_mine = lax.dynamic_index_in_dim(w3, c, 2, keepdims=False)
    w_give = lax.dynamic_index_in_dim(w3, 1 - c, 2, keepdims=False)
    w_half = swap(core_half(w_give, 1), "col")
    w_other = swap(w_half, "core")
    first = lax.axis_index("core") == 0
    w_full = jnp.concatenate(
        [w_mine, jnp.where(first, w_half, w_other), jnp.where(first, w_other, w_half)], axis=1
    )

    xf = x_all.astype(F32)
    scale_one = norm_scale(xf)
    normed_one = (xf * scale_one * gain_one).astype(BF)
    projected = jnp.einsum("td,sdh->sht", normed_one, w_full, preferred_element_type=F32)
    projected = projected.reshape(3, heads, HEAD_DIM, t)
    factor = QUERY_CONST / math.sqrt(HEAD_DIM) * jax.nn.softplus(query_scale)
    raw_q = projected[0]
    qkv = jnp.stack([raw_q * factor[None, :, None], projected[1], projected[2]]).astype(BF)
    masks = mask_args(series_ids, pad_mask)
    at = jnp.zeros((4,), jnp.int32)
    attended, lse = attention_forward(at, qkv, masks)

    def to_tokens(y):
        y = flip_dim(y.reshape(head_rows, rows, cols, share), "row", 1)
        y = flip_dim(y, "col", 2)
        y = exchange(y.reshape(1, head_rows, rows, cols, share), "row", 2, 0)
        y = exchange(y.reshape(rows, 1, head_rows, cols, share), "col", 3, 1)
        y = flip_dim(y.reshape(rows, cols, head_rows, share), "col", 1)
        return y.reshape(rows * cols * head_rows, share)

    def to_heads(y):
        y = flip_dim(y.reshape(rows, cols, head_rows, share), "col", 1)
        y = exchange(y.reshape(rows, cols, head_rows, 1, share), "col", 1, 3)
        y = exchange(y.reshape(rows, head_rows, 1, cols, share), "row", 0, 2)
        y = flip_dim(y.reshape(head_rows, rows, cols, share), "col", 2)
        return flip_dim(y, "row", 1).reshape(head_rows, t)

    w_out_all = weight_gather(w_out, 0)
    w_up_all = weight_gather(w_up, 1)
    w_down_all = weight_gather(w_down, 0)

    def my_share(y):
        return lax.dynamic_slice_in_dim(y, c * share, share, 0)

    att = to_tokens(attended.reshape(head_rows, t))
    x_mine = my_share(x_own).astype(F32)
    middle = x_mine + dot(att, w_out_all, (0, 0))
    scale_two = norm_scale(middle)
    normed_two = (middle * scale_two * gain_two).astype(BF)
    pre_act = dot(normed_two, w_up_all, (1, 0)) + bias_up
    sig = jax.nn.sigmoid(pre_act)
    hidden = (pre_act * sig).astype(BF)
    result = (middle + dot(hidden, w_down_all, (1, 0)) + bias_down).astype(BF)

    def to_block(y):
        mine, theirs = jnp.split(y, 2, axis=1)
        return jnp.concatenate(flip([mine, swap(theirs, "col")], "col"), axis=0)

    layer_out = to_block(result)

    g_give = lax.dynamic_slice_in_dim(cotangent, (1 - c) * share, share, 0)
    g = jnp.concatenate([my_share(cotangent), swap(g_give, "col")], axis=1)
    grad_w_down = dot(hidden, g, (0, 0))
    grad_hidden = dot(g, w_down_all, (1, 1))
    grad_pre_f = grad_hidden * sig * (1.0 + pre_act * (1.0 - sig))
    grad_pre = grad_pre_f.astype(BF)
    grad_b_up = jnp.sum(grad_pre.astype(F32), axis=0)
    grad_w_up = dot(normed_two, grad_pre, (0, 0))
    grad_normed_two = dot(grad_pre, w_up_all, (1, 1))
    weighted = grad_normed_two * gain_two
    inner = jnp.sum(weighted * middle, axis=1, keepdims=True)
    grad_middle = g.astype(F32) + scale_two * weighted - middle * (scale_two**3 * inner / D)
    grad_gain_mlp = jnp.sum(grad_normed_two * middle * scale_two, axis=0)
    grad_branch = grad_middle.astype(BF)
    grad_w_out = dot(att, grad_branch, (1, 0))
    grad_att = dot(w_out_all, grad_branch, (1, 1)).astype(BF)
    grad_attended = to_heads(grad_att).reshape(heads, HEAD_DIM, t)
    grad_middle_block = to_block(grad_middle)

    sum_down = weight_sum(grad_w_down, 0)
    sum_up = weight_sum(grad_w_up, 1)
    sum_out = weight_sum(grad_w_out, 0)

    grad_proj, gscale = attention_backward(
        at, qkv, raw_q, factor.reshape(HEAD_DIM, 1), attended, [grad_attended], lse, masks
    )
    slope = QUERY_CONST / math.sqrt(HEAD_DIM) * jax.nn.sigmoid(query_scale)
    grad_query_scale = jnp.sum(gscale, axis=(0, 2)) * slope
    grad_proj = grad_proj.reshape(3, head_rows, t)
    grad_normed_one = jnp.einsum("sht,sdh->td", grad_proj, w_full, preferred_element_type=F32)
    weighted_one = grad_normed_one * gain_one
    inner_one = jnp.sum(weighted_one * xf, axis=1)
    grad_gain_attn = jnp.sum(grad_normed_one * xf * scale_one, axis=0)
    inner_one = lax.psum(inner_one, ("row", "col"))
    grad_w = jnp.einsum("td,sht->sdh", normed_one, grad_proj, preferred_element_type=F32)
    grad_w = grad_w.reshape(3, cols, 2, feat // 2, head_rows)
    core = lax.axis_index("core")
    keep = lax.dynamic_index_in_dim(grad_w, core, 2, keepdims=False)
    give = lax.dynamic_index_in_dim(grad_w, 1 - core, 2, keepdims=False).astype(BF)
    part = (keep + swap(give, "core").astype(F32)).astype(BF)
    part = jnp.concatenate(flip([part[:, 0], swap(part[:, 1], "col")], "col"), axis=2)
    sum_qkv = jnp.transpose(z_sum(part), (1, 0, 2))

    e = jnp.concatenate(flip(jnp.split(grad_normed_one.astype(BF), 2, axis=0), "row"), axis=0) if rows == 2 else (
        grad_normed_one.astype(BF)
    )
    e = scatter_sum(e, "row", 0)
    e = scatter_sum(e, "col", 1).astype(F32)
    my_rows = lambda y: lax.dynamic_slice_in_dim(y, r * tok, tok, 0)
    scale_mine = my_rows(scale_one)
    inner_mine = my_rows(inner_one.reshape(t, 1))
    grad_inputs = grad_middle_block + scale_mine * (e * gain_attn) - inputs.astype(F32) * (
        scale_mine**3 * inner_mine / D
    )

    grad_b_down = jnp.sum(g.astype(F32), axis=0)
    vectors = jnp.concatenate(
        [
            flip_dim(grad_gain_attn, "col", 0),
            flip_dim(grad_gain_mlp, "col", 0),
            flip_dim(grad_b_down, "col", 0),
            flip_dim(grad_b_up, "row", 0),
            grad_query_scale,
        ]
    )
    vectors = lax.psum(vectors, ("z", "core", "row", "col"))
    mine_col = lambda at: lax.dynamic_slice_in_dim(vectors, at * D + c * feat, feat, 0)
    units = b_up.shape[0]
    return (
        layer_out,
        grad_inputs,
        mine_col(0),
        sum_qkv,
        vectors[4 * D :],
        sum_out,
        mine_col(1),
        sum_up,
        lax.dynamic_slice_in_dim(vectors, 3 * D + r * units, units, 0),
        sum_down,
        mine_col(2),
    )


SMEM = pl.BlockSpec(memory_space=pltpu.SMEM)
ANY = pl.BlockSpec(memory_space=pl.ANY)


def call(kernel, name, args, specs, outs, scratch=(), **more):
    return pl.pallas_call(
        kernel,
        in_specs=specs,
        out_shape=outs,
        scratch_shapes=list(scratch),
        compiler_params=pltpu.CompilerParams(vmem_limit_bytes=VMEM_LIMIT),
        cost_estimate=CHEAP,
        name=name,
        **more,
    )(*args)


VM = pl.BlockSpec(memory_space=pltpu.VMEM)


def shape(dims, kind):
    return jax.ShapeDtypeStruct(dims, kind)


def project_kernel(
    at, x00, x01, x10, x11, gain, factor, w_mine, w_a, w_b, w_c, w_d, qkv, raw, normed, scale_own, w_full
):
    r, k, even = at[0], at[2], at[4]
    tok, feat = x00.shape
    hr = w_mine.shape[1]
    part = hr // 4
    for s in range(3):
        w_full[pl.ds(s * hr, hr), 0:feat] = w_mine[s]
        for ref, core, turn in ((w_a, k, even), (w_b, k, 1 - even), (w_c, 1 - k, even), (w_d, 1 - k, 1 - even)):
            w_full[pl.ds(pl.multiple_of(s * hr + (2 * core + turn) * part, 16), part), feat:] = ref[s]
    for i, (a_ref, b_ref) in enumerate(((x00, x01), (x10, x11))):
        a, b = a_ref[...].astype(F32), b_ref[...].astype(F32)
        total = jnp.sum(a * a, axis=1, keepdims=True) + jnp.sum(b * b, axis=1, keepdims=True)
        scale = lax.rsqrt(total / (2 * feat) + EPS)
        if i == 0:
            scale_own[...] = scale
        rows = pl.ds(pl.multiple_of((r ^ i) * tok, tok), tok)
        normed[rows, 0:feat] = (a * scale * gain[:, 0:feat]).astype(BF)
        normed[rows, feat:] = (b * scale * gain[:, feat:]).astype(BF)
        y = normed[rows, :]
        q = dot(w_full[0:hr, :], y, (1, 1))
        raw[:, rows] = q
        qkv[0, :, rows] = (q * factor[...]).astype(BF)
        qkv[1, :, rows] = dot(w_full[hr : 2 * hr, :], y, (1, 1)).astype(BF)
        qkv[2, :, rows] = dot(w_full[2 * hr : 3 * hr, :], y, (1, 1)).astype(BF)


def feed_kernel(
    at, a0, a1, a2, a3, x_own, x_col, g_own, g_col, gain, bias_up, bias_down,
    w_out, w_up, w_down, *rest
):
    blocks, rest = rest[:24], rest[24:]
    feed_body(
        at, a0, a1, a2, a3, x_own, x_col, g_own, g_col, gain, bias_up, bias_down, w_out, w_up, w_down, blocks, *rest
    )


def feed_body(
    at, a0, a1, a2, a3, x_own, x_col, g_own, g_col, gain, bias_up, bias_down, w_out, w_up, w_down, blocks,
    out_own, out_give, gm_own, gm_give, t0, t1, t2, t3, vectors,
    sx, sy, kx, ky, sx2, sy2, kx2, ky2,
    w, att, turned, sems,
):
    r, c, k = at[0], at[1], at[2]
    hr, share = a0.shape
    feat = x_own.shape[1]
    half = feat // 2
    quarter = half // 2
    even = at[4]
    copies = []
    for n in range(3):
        turn = (0, 1 + even, 2 - even)[n]
        rx, cx = (feat, 0) if n == 0 else (feat * (turn - 1), feat * (2 - turn))
        mine = [((w_out, w_up, w_down)[n], w.at[n, 0:feat, 0:feat])]
        for core, (px, py, p0, p1) in ((k, blocks[8 * n : 8 * n + 4]), (1 - k, blocks[8 * n + 4 : 8 * n + 8])):
            down = core * half
            at_x = pl.ds(pl.multiple_of(rx + down, 16), half)
            at_y = pl.ds(pl.multiple_of(feat - rx + down, 16), half)
            at_0 = pl.ds(pl.multiple_of(feat + down, 16), quarter)
            at_1 = pl.ds(pl.multiple_of(feat + down + quarter, 16), quarter)
            mine.append((px, w.at[turn, at_x, pl.ds(pl.multiple_of(cx, 128), feat)]))
            mine.append((py, w.at[turn, at_y, pl.ds(pl.multiple_of(feat - cx, 128), feat)]))
            mine.append((p0, w.at[turn, at_0, feat : 2 * feat]))
            mine.append((p1, w.at[turn, at_1, feat : 2 * feat]))
        started = []
        for m, (src, dst) in enumerate(mine):
            copy = pltpu.make_async_copy(src, dst, sems.at[n, m])
            copy.start()
            started.append(copy)
        copies.append(started)

    rows = pl.ds(pl.multiple_of(c * share, share), share)
    for s, a in enumerate((a0, a1, a2, a3)):
        to = (s // 2) * 2 * hr + (c ^ (s % 2)) * hr
        att[pl.ds(pl.multiple_of(to, 16), hr), :] = a[...]
    x = jnp.concatenate([x_own[rows, :], x_col[rows, :]], axis=1).astype(F32)
    g = jnp.concatenate([g_own[rows, :], g_col[...]], axis=1)
    for copy in copies[0]:
        copy.wait()
    middle = x + dot(att[...], w[0], (0, 0))
    scale = lax.rsqrt(jnp.sum(middle * middle, axis=1, keepdims=True) / D + EPS)
    normed = (middle * scale * gain[...]).astype(BF)
    for copy in copies[1] + copies[2]:
        copy.wait()
    pre = dot(normed, w[1], (1, 0)) + bias_up[...]
    sig = jax.nn.sigmoid(pre)
    hidden = (pre * sig).astype(BF)
    result = (middle + dot(hidden, w[2], (1, 0)) + bias_down[...]).astype(BF)
    out_own[...] = result[:, :feat]
    out_give[...] = result[:, feat:]

    def weight_grad(n, left_ref, right):
        for core, by_row, by_col in ((k, (sx, kx), (sy, ky)), (1 - k, (sx2, kx2), (sy2, ky2))):
            up, low = (by_col, by_row) if n == 1 else (by_row, by_col)
            for b in range(2):
                part = pl.ds(pl.multiple_of(b * feat + core * half, 16), half)
                y = dot(left_ref[part, :], right, (1, 0)).astype(BF)
                for j in range(2):
                    cut = slice(j * feat, (j + 1) * feat)
                    up[1 - b][j, n] = y[:quarter, cut]
                    low[1 - j][b, n] = y[quarter:, cut]

    turned[...] = hidden.astype(F32).T.astype(BF)
    grad_pre_f = dot(g, w[2], (1, 1)) * sig * (1.0 + pre * (1.0 - sig))
    grad_pre = grad_pre_f.astype(BF)
    weight_grad(2, turned, g)
    grad_normed = dot(grad_pre, w[1], (1, 1))
    weighted = grad_normed * gain[...]
    inner = jnp.sum(weighted * middle, axis=1, keepdims=True)
    gf = g.astype(F32)
    grad_middle = gf + scale * weighted - middle * (scale * scale * scale * inner / D)
    gm_own[...] = grad_middle[:, :feat]
    gm_give[...] = grad_middle[:, feat:].astype(BF)
    branch = grad_middle.astype(BF)
    for s, t in enumerate((t0, t1, t2, t3)):
        come = (s // 2) * 2 * hr + (c ^ (s % 2)) * hr
        t[...] = dot(w[0, pl.ds(pl.multiple_of(come, 16), hr), :], branch, (1, 1)).astype(BF)
    turned[...] = normed.astype(F32).T.astype(BF)
    weight_grad(1, turned, grad_pre)
    weight_grad(0, att, branch)
    vectors[...] = jnp.concatenate(
        [
            jnp.sum(grad_normed * (middle * scale), axis=0, keepdims=True),
            jnp.sum(gf, axis=0, keepdims=True),
            jnp.sum(grad_pre.astype(F32), axis=0, keepdims=True),
        ],
        axis=0,
    )


def weight_back_kernel(at, grad, normed, keep, give):
    k = at[2]
    part = keep.shape[2]
    feat = keep.shape[3]
    for ref, core in ((give, 1 - k), (keep, k)):
        for s in range(3):
            rows = pl.ds(pl.multiple_of(core * part, 16), part)
            y = dot(grad[s, rows, :], normed[...], (1, 0)).astype(BF)
            ref[0, s] = y[:, :feat]
            ref[1, s] = y[:, feat:]


def project_back_kernel(
    at, grad_a, grad_b, w_full, x00, x01, x10, x11, gain, e0, e1, e2, e3, inner_own, gain_sum, grad
):
    r = at[0]
    tok, feat = x00.shape
    part = grad_a.shape[1]
    for s in range(3):
        for n, ref in enumerate((grad_a, grad_b)):
            grad[(2 * s + n) * part : (2 * s + n + 1) * part, :] = ref[s]
    sums = [jnp.zeros((1, feat), F32), jnp.zeros((1, feat), F32)]
    for i, (xs, es) in enumerate((((x00, x01), (e0, e1)), ((x10, x11), (e2, e3)))):
        rows = pl.ds(pl.multiple_of((r ^ i) * tok, tok), tok)
        left = grad[:, rows]
        products, squares, inner = [], 0.0, 0.0
        for j in range(2):
            cut = slice(j * feat, (j + 1) * feat)
            e = dot(left, w_full[:, cut], (0, 0))
            x = xs[j][...].astype(F32)
            product = e * x
            inner = inner + jnp.sum(product * gain[:, cut], axis=1, keepdims=True)
            squares = squares + jnp.sum(x * x, axis=1, keepdims=True)
            es[j][0:tok, :] = e.astype(es[j].dtype)
            products.append(product)
        scale = lax.rsqrt(squares / (2 * feat) + EPS)
        for j in range(2):
            sums[j] += jnp.sum(products[j] * scale, axis=0, keepdims=True)
        line = jnp.broadcast_to(inner, (tok, 128)).T[0:1, :]
        high = line.astype(BF).astype(F32)
        extra = jnp.concatenate([high, line - high, jnp.zeros((14, tok), F32)], axis=0)
        extra = jnp.concatenate([extra, jnp.zeros((16, feat - tok), F32)], axis=1).astype(BF)
        if i == 0:
            inner_own[...] = inner
            es[1][tok:, :] = extra
        else:
            es[0][tok:, :] = extra
            es[1][tok:, :] = extra
    gain_sum[:, 0:feat] = sums[0]
    gain_sum[:, feat:] = sums[1]


def finish_qkv_kernel(at, *refs):
    c, k = at[1], at[2]
    *parts, out, rows = refs
    half = parts[0].shape[1]
    for s in range(3):
        for pair in range(2):
            mine, theirs, mine2, theirs2 = parts[4 * pair : 4 * pair + 4]
            for ref, col, core in ((mine, c, k), (theirs, 1 - c, k), (mine2, c, 1 - k), (theirs2, 1 - c, 1 - k)):
                to = pl.multiple_of((4 * col + 2 * pair + core) * half, 16)
                rows[pl.ds(to, half), :] = ref[s].astype(F32)
        out[s] = rows[...].T


def finish_feed_kernel(at, a, b, a2, b2, *outs):
    k = at[2]
    quarter = a.shape[1]
    for n, out in enumerate(outs):
        upper, lower = ((b, b2), (a, a2)) if n == 1 else ((a, a2), (b, b2))
        for i, core in ((0, k), (1, 1 - k)):
            for j, refs in enumerate((upper, lower)):
                to = pl.multiple_of((2 * core + j) * quarter, 16)
                out[pl.ds(to, quarter), :] = refs[i][n].astype(F32)


def after(x, *earlier):
    return lax.optimization_barrier((x, *earlier))[0]


def add(*parts):
    total = parts[0].astype(F32)
    for part in parts[1:]:
        total = total + part.astype(F32)
    return total.astype(BF)


def diagonal(x):
    return lax.ppermute(x, ("row", "col"), [(0, 3), (1, 2), (2, 1), (3, 0)])


def z_swap(x, step):
    n = size("z")
    return lax.ppermute(x, "z", [(i, i ^ step) for i in range(n)])


def z_first(z):
    return (z == 0) | (z == 3)


def z_pair(a, b):
    if size("z") != 4:
        return lax.psum((a, b), "z")
    first = z_first(lax.axis_index("z"))
    return add(jnp.where(first, a, b), z_swap(jnp.where(first, b, a), 1))


def z_meet(mine):
    return add(mine, z_swap(mine, 3)) if size("z") == 4 else mine


def z_back(mine):
    if size("z") != 4:
        return mine
    first = z_first(lax.axis_index("z"))
    other = z_swap(mine, 1)
    return jnp.where(first, mine, other), jnp.where(first, other, mine)


def body_four(
    inputs, gain_attn, w_qkv, query_scale, w_out, gain_mlp, w_up, b_up, w_down, b_down, series_ids, pad_mask, cotangent
):
    tok, feat = inputs.shape
    share = tok // 2
    t = series_ids.shape[0]
    hr = w_qkv.shape[2] // 2
    heads = hr // HEAD_DIM
    half = feat // 2
    r, c, k = lax.axis_index("row"), lax.axis_index("col"), lax.axis_index("core")
    even = lax.axis_index("z") % 2
    at = jnp.stack([r, c, k, 2 * r + c, even]).astype(jnp.int32)
    mine_rows = lambda y, part: lax.dynamic_slice_in_dim(y, part * share, share, 0)

    x01 = swap(inputs, "col")
    x10 = swap(inputs, "row")
    small = swap(jnp.concatenate([gain_attn, gain_mlp, b_down.astype(F32)]), "col")
    up_other = swap(b_up.astype(F32), "row")
    w_turned = jnp.transpose(w_qkv, (1, 2, 0)).reshape(3, 2, hr, feat)
    w_mine = lax.dynamic_index_in_dim(w_turned, c, 1, keepdims=False)
    w_give = lax.dynamic_index_in_dim(w_turned, 1 - c, 1, keepdims=False)
    w_half = core_half(w_give, 1)
    w_half = lax.dynamic_slice_in_dim(w_half, even * (hr // 4), hr // 4, 1)
    w_a = swap(w_half, "col")
    g_col = swap(mine_rows(cotangent, 1 - c), "col")
    x01, x10, small, up_other = lax.optimization_barrier((x01, x10, small, up_other))
    x11 = swap(after(x01, w_half), "row")
    w_b = z_swap(w_a, 1)
    w_c, w_d = swap(w_a, "core"), swap(w_b, "core")
    gain_one = jnp.concatenate([gain_attn, small[:feat]]).reshape(1, D)
    gain_two = jnp.concatenate([gain_mlp, small[feat : 2 * feat]]).reshape(1, D)
    bias_down = jnp.concatenate([b_down.astype(F32), small[2 * feat :]]).reshape(1, D)
    bias_up = jnp.concatenate([b_up.astype(F32), up_other]).reshape(1, D)
    factor = QUERY_CONST / math.sqrt(HEAD_DIM) * jax.nn.softplus(query_scale)
    factor_col = factor.reshape(HEAD_DIM, 1)

    part_z = jnp.where(even == 0, core_half(w_up, 0), core_half(w_down, 0))
    part_o = core_half(w_out, 0)
    part_z, part_o = lax.optimization_barrier((part_z, part_o, x11, w_a))[:2]
    hx, hy = swap(part_z, "row"), swap(part_z, "col")

    qkv, raw, normed_one, scale_own, w_full = call(
        project_kernel,
        "project",
        (at, inputs, x01, x10, x11, gain_one, jnp.tile(factor_col, (heads, 1)), w_mine, w_a, w_b, w_c, w_d),
        [SMEM] + [VM] * 11,
        [
            shape((3, hr, t), BF),
            shape((hr, t), F32),
            shape((t, D), BF),
            shape((tok, 1), F32),
            shape((3 * hr, D), BF),
        ],
    )
    qkv = qkv.reshape(3, heads, HEAD_DIM, t)
    masks = mask_args(series_ids, pad_mask)
    quarter = half // 2
    hx, hy, part_o, qkv = lax.optimization_barrier((hx, hy, part_o, qkv))
    d0, d1 = swap(hx[:quarter], "col"), swap(hy[quarter:], "row")
    hx_o, hy_o = swap(part_o, "row"), swap(part_o, "col")
    hx_z, hy_z = z_swap(hx, 1), z_swap(hy, 1)
    attended, lse, *a = attention_forward(at, qkv, masks, pieces=4)
    a0, a1, a2, a3 = [p.reshape(hr, share) for p in a]
    a1, a2, a3 = swap(a1, "col"), swap(a2, "row"), diagonal(a3)
    d0, d1, hx_o, hy_o, lse = lax.optimization_barrier((d0, d1, hx_o, hy_o, lse))
    d0_z, d1_z = z_swap(d0, 1), z_swap(d1, 1)
    d0_o, d1_o = swap(hx_o[:quarter], "col"), swap(hy_o[quarter:], "row")
    blocks = []
    for found in ((hx_o, hy_o, d0_o, d1_o), (hx, hy, d0, d1), (hx_z, hy_z, d0_z, d1_z)):
        blocks += found
        blocks += [swap(y, "core") for y in found]
    out_own, out_give, gm_own, gm_give, t0, t1, t2, t3, vectors, *grads = call(
        feed_kernel,
        "feed_forward",
        (at, a0, a1, a2, a3, inputs, x01, cotangent, g_col, gain_two, bias_up, bias_down)
        + (w_out, w_up, w_down, *blocks),
        [SMEM] + [VM] * 11 + [ANY] * 27,
        [
            shape((share, feat), BF),
            shape((share, feat), BF),
            shape((share, feat), F32),
            shape((share, feat), BF),
        ]
        + [shape((hr, share), BF)] * 4
        + [shape((3, D), F32)]
        + [shape((2, 3, half // 2, feat), BF)] * 8,
        scratch=[
            pltpu.VMEM((3, D, D), BF),
            pltpu.VMEM((D, share), BF),
            pltpu.VMEM((D, share), BF),
            pltpu.SemaphoreType.DMA((3, 9)),
        ],
    )
    t1, t2, t3 = swap(t1, "col"), swap(t2, "row"), diagonal(t3)
    sx, sy, kx, ky, *other_core = grads
    sx2, sy2, kx2, ky2 = [swap(y, "core") for y in other_core]
    sx, sy = add(sx, sx2), add(sy, sy2)
    pieces = lax.optimization_barrier((t0, t1, t2, t3, sx, sy))[:4]
    rx, ry = swap(sx, "row"), swap(sy, "col")
    pieces = [p.reshape(heads, HEAD_DIM, share) for p in pieces]
    raw = raw.reshape(heads, HEAD_DIM, t)
    few = heads // 2

    def weight_back(grad):
        kept, sent = call(
            weight_back_kernel,
            "weight_back",
            (at, grad, normed_one),
            [SMEM] + [VM] * 2,
            [shape((2, 3, hr // 4, feat), BF)] * 2,
        )
        return add(kept, swap(sent, "core"))

    grad_a, scale_a = attention_backward(at, qkv, raw, factor_col, attended, pieces, lse, masks, 0, few)
    grad_a = grad_a.reshape(3, hr // 2, t)
    w_pair_a = weight_back(grad_a)
    px, py = add(kx, kx2, rx), add(ky, ky2, ry)
    lse_on = after(lse, w_pair_a, px, py)
    grad_b, scale_b = attention_backward(at, qkv, raw, factor_col, attended, pieces, lse_on, masks, few, few)
    grad_b = grad_b.reshape(3, hr // 2, t)
    mine_a = z_pair(w_pair_a[0], w_pair_a[1])
    w_pair_b = weight_back(after(grad_b, mine_a))
    mine_b = z_pair(w_pair_b[0], w_pair_b[1])
    mine_a = z_meet(mine_a)
    slope = QUERY_CONST / math.sqrt(HEAD_DIM) * jax.nn.sigmoid(query_scale)
    grad_query_scale = (jnp.sum(scale_a, axis=(0, 2)) + jnp.sum(scale_b, axis=(0, 2))) * slope
    e0, e1, e2, e3, inner, gain_sum = call(
        project_back_kernel,
        "project_back",
        (at, grad_a, after(grad_b, mine_a, mine_b), w_full, inputs, x01, x10, x11, gain_one),
        [SMEM] + [VM] * 8,
        [
            shape((tok, feat), F32),
            shape((tok + 16, feat), BF),
            shape((tok + 16, feat), BF),
            shape((tok + 16, feat), BF),
            shape((tok, 1), F32),
            shape((1, D), F32),
        ],
        scratch=[pltpu.VMEM((3 * hr, t), BF)],
    )
    w_args = [at]
    mine_b = z_meet(mine_b)
    for mine in (mine_a, mine_b):
        w_own, w_theirs = z_back(mine)
        w_theirs = swap(w_theirs, "col")
        w_args += [w_own, w_theirs, swap(w_own, "core"), swap(w_theirs, "core")]
    sum_qkv = call(
        finish_qkv_kernel,
        "finish_qkv",
        w_args,
        [SMEM] + [VM] * 8,
        shape((3, feat, 2 * hr), F32),
        scratch=[pltpu.VMEM((2 * hr, feat), F32)],
    )
    sum_qkv = jnp.transpose(sum_qkv, (1, 0, 2))

    qx, qy = swap(px[1], "col"), swap(py[1], "row")
    fx, fy = add(px[0], qx), add(py[0], qy)
    e1, e2, e3, out_give, gm_give = lax.optimization_barrier((e1, e2, e3, out_give, gm_give))
    fx, fy = lax.psum((fx, fy), "z")
    sum_out, sum_up, sum_down = call(
        finish_feed_kernel,
        "finish_feed",
        (at, fx, fy, swap(fx, "core"), swap(fy, "core")),
        [SMEM] + [VM] * 4,
        [shape((feat, feat), F32)] * 3,
    )

    e1, e2, e3 = swap(e1, "col"), swap(e2, "row"), diagonal(e3)
    e = e0
    for more in (e1, e2, e3):
        e = e + more[:tok].astype(F32)
        inner = inner + jnp.sum(more[tok : tok + 2, :tok].astype(F32), axis=0).reshape(tok, 1)
    gm_col = swap(gm_give, "col").astype(F32)
    grad_middle = jnp.concatenate(flip([gm_own, gm_col], "col"), axis=0)
    grad_inputs = grad_middle + scale_own * (e * gain_attn) - inputs.astype(F32) * (scale_own**3 * inner / D)
    layer_out = jnp.concatenate(flip([out_own, swap(out_give, "col")], "col"), axis=0)

    total = jnp.concatenate(
        [
            flip_dim(gain_sum[0], "col", 0),
            flip_dim(vectors[0], "col", 0),
            flip_dim(vectors[1], "col", 0),
            flip_dim(vectors[2], "row", 0),
            grad_query_scale,
        ]
    )
    total = total + swap(total, "core")
    total = (total + swap(total, "row")) + (swap(total, "col") + diagonal(total))
    total = after(total, w_own)
    if size("z") == 4:
        total = (total + z_swap(total, 1)) + (z_swap(total, 2) + z_swap(total, 3))
    else:
        total = lax.psum(total, "z")
    mine_col = lambda n: lax.dynamic_slice_in_dim(total, n * D + c * feat, feat, 0)
    units = b_up.shape[0]
    return (
        layer_out,
        grad_inputs,
        mine_col(0),
        sum_qkv,
        total[4 * D :],
        sum_out,
        mine_col(1),
        sum_up,
        lax.dynamic_slice_in_dim(total, 3 * D + r * units, units, 0),
        sum_down,
        mine_col(2),
    )


def solution(mesh):
    dp, rows, cols = mesh.shape["dp"], mesh.shape["row"], mesh.shape["col"]
    split = Mesh(mesh.devices.reshape(dp // 2, 2, rows, cols), ("z", "core", "row", "col"))
    tokens = P(("z", "core", "row"), "col")
    in_specs = (
        tokens,
        P("col"),
        P("col", None, "row"),
        P(),
        P("row", "col"),
        P("col"),
        P("col", "row"),
        P("row"),
        P("row", "col"),
        P("col"),
        P(("z", "core")),
        P(("z", "core")),
        tokens,
    )
    out_specs = (
        tokens,
        tokens,
        P("col"),
        P("col", None, "row"),
        P(),
        P("row", "col"),
        P("col"),
        P("col", "row"),
        P("row"),
        P("row", "col"),
        P("col"),
    )
    body = body_four if rows == 2 and cols == 2 and dp % 4 == 0 else body_any
    return jax.shard_map(body, mesh=split, in_specs=in_specs, out_specs=out_specs, check_vma=False)
```

```python
import functools
import math

import jax
import jax.numpy as jnp
from jax import lax
from jax.experimental import pallas as pl
from jax.experimental.pallas import tpu as pltpu
from jax.sharding import Mesh
from jax.sharding import PartitionSpec as P

D = 1280
HEAD_DIM = 80
EPS = 1e-06
QUERY_CONST = 1.442695041
MASKED = -1e30
BF = jnp.bfloat16
F32 = jnp.float32
VMEM_LIMIT = 50 * 1024 * 1024
CHEAP = pl.CostEstimate(flops=1, bytes_accessed=1, transcendentals=0)


def size(axis):
    return lax.axis_size(axis)


def swap(x, axis):
    return lax.ppermute(x, axis, [(0, 1), (1, 0)])


def flip(blocks, axis):
    if size(axis) != 2:
        return list(blocks)
    first = lax.axis_index(axis) == 0
    a, b = blocks
    return [jnp.where(first, a, b), jnp.where(first, b, a)]


def flip_dim(x, axis, dim):
    if size(axis) != 2:
        return x
    return jnp.concatenate(flip(jnp.split(x, 2, axis=dim), axis), axis=dim)


def gather(x, axis):
    if size(axis) == 2:
        return [x, swap(x, axis)]
    whole = lax.all_gather(x, axis, axis=0, tiled=False)
    return [whole[i] for i in range(size(axis))]


def gather_grid(x):
    if size("row") != 2:
        return [gather(b, "col") for b in gather(x, "row")]
    along_row, along_col = swap(x, "row"), swap(x, "col")
    half = x.shape[0] // 2
    across = jnp.concatenate(
        [swap(along_row[:half], "col"), swap(along_col[half:], "row")], axis=0
    )
    return [[x, along_col], [along_row, across]]


def scatter_sum(x, axis, dim):
    if size(axis) != 2:
        return lax.psum_scatter(x, axis, scatter_dimension=dim, tiled=True)
    mine, theirs = jnp.split(x, 2, axis=dim)
    return (mine.astype(F32) + swap(theirs, axis).astype(F32)).astype(x.dtype)


def exchange(x, axis, split, join):
    if size(axis) != 2:
        return lax.all_to_all(x, axis, split, join, tiled=True)
    mine, theirs = jnp.split(x, 2, axis=split)
    return jnp.concatenate([mine, swap(theirs, axis)], axis=join)


def core_half(x, dim):
    return lax.dynamic_slice_in_dim(
        x, lax.axis_index("core") * (x.shape[dim] // 2), x.shape[dim] // 2, dim
    )


def weight_gather(w, row_dim):
    part = core_half(w, 0)
    blocks = gather_grid(part)
    if row_dim == 1:
        blocks = [list(b) for b in zip(*blocks)]
    mine = jnp.stack([jnp.concatenate(b, axis=1) for b in blocks])
    other = swap(mine, "core")
    first = lax.axis_index("core") == 0
    both = jnp.stack([jnp.where(first, mine, other), jnp.where(first, other, mine)], axis=1)
    return both.reshape(-1, both.shape[-1])


def weight_sum(g, row_dim):
    dim_axis = ("row", "col") if row_dim == 0 else ("col", "row")
    n0 = size(dim_axis[0])
    g = g.reshape(n0, 2, g.shape[0] // n0 // 2, g.shape[1])
    core = lax.axis_index("core")
    keep = lax.dynamic_index_in_dim(g, core, 1, keepdims=False)
    give = lax.dynamic_index_in_dim(g, 1 - core, 1, keepdims=False).astype(BF)
    part = (keep + swap(give, "core").astype(F32)).astype(BF)
    part = scatter_sum(part, dim_axis[0], 0)
    part = scatter_sum(part[0], dim_axis[1], 1)
    return z_sum(part)


def z_sum(part):
    total = lax.psum(part, "z")
    other = swap(total, "core")
    return flip_core(total, other)


def flip_core(total, other):
    first = lax.axis_index("core") == 0
    return jnp.concatenate(
        [jnp.where(first, total, other), jnp.where(first, other, total)], axis=-2
    ).astype(F32)


def dot(a, b, contract):
    return lax.dot_general(a, b, ((contract[0:1], contract[1:2]), ((), ())), preferred_element_type=F32)


def bias_block(series_row, series_col, key_pos, q0, k0, qb, kb, diagonal):
    q_pos = q0 + lax.broadcasted_iota(jnp.int32, (1, qb), 1)
    allowed = (series_col == series_row) & (key_pos <= q_pos)
    if diagonal:
        k_pos = k0 + lax.broadcasted_iota(jnp.int32, (kb, 1), 0)
        allowed = allowed | (k_pos == q_pos)
    return jnp.where(allowed, 0.0, MASKED)


def forward_kernel(block, at, qkv_ref, srow_ref, scol_ref, kpos_ref, out_ref, lse_ref, *rest):
    *pieces, bias_ref, krow_ref, s_ref, slot_ref = rest
    t = qkv_ref.shape[3]
    n = t // block
    krow_ref[...] = qkv_ref[1, 0].astype(F32).T.astype(BF)

    def bias_slot(j, i):
        return j * (j + 1) // 2 + i

    @pl.when(pl.program_id(0) == 0)
    def _():
        for j in range(n):
            for i in range(j + 1):
                keys = pl.ds(i * block, block)
                bias_ref[bias_slot(j, i)] = bias_block(
                    srow_ref[:, j * block : (j + 1) * block],
                    scol_ref[keys, :],
                    kpos_ref[keys, :],
                    j * block,
                    i * block,
                    block,
                    block,
                    i == j,
                )

    for j in range(n):
        cols = slice(j * block, (j + 1) * block)
        q = qkv_ref[0, 0, :, cols]
        top = None
        for i in range(j + 1):
            s = dot(krow_ref[i * block : (i + 1) * block, :], q, (1, 0)) + bias_ref[bias_slot(j, i)]
            s_ref[i * block : (i + 1) * block, :] = s
            here = jnp.max(s, axis=0, keepdims=True)
            top = here if top is None else jnp.maximum(top, here)
        total = jnp.zeros((1, block), F32)
        acc = jnp.zeros((HEAD_DIM, block), F32)
        for i in range(j + 1):
            p = jnp.exp(s_ref[i * block : (i + 1) * block, :] - top)
            total += jnp.sum(p, axis=0, keepdims=True)
            acc += dot(qkv_ref[2, 0, :, i * block : (i + 1) * block], p.astype(BF), (1, 0))
        found = (acc / total).astype(BF)
        out_ref[0, :, cols] = found
        if pieces:
            slot_ref[j ^ at[3]] = found
        lse_ref[0, :, cols] = top + jnp.log(total)
    for slot, piece in enumerate(pieces):
        piece[0] = slot_ref[slot]


def backward_kernel(
    block, at, qkv_ref, raw_ref, factor_ref, out_ref, lse_ref, srow_ref, scol_ref, kpos_ref, *rest
):
    *pieces, grad_ref, gscale_ref, bias_ref, krow_ref, vrow_ref, gk_ref, gv_ref, gout_ref = rest
    if len(pieces) == 1:
        gout_ref[...] = pieces[0][0]
    else:
        for slot, piece in enumerate(pieces):
            wide = piece.shape[2]
            gout_ref[:, pl.ds(pl.multiple_of((slot ^ at[3]) * wide, 128), wide)] = piece[0]
    t = qkv_ref.shape[3]
    n = t // block
    krow_ref[...] = qkv_ref[1, 0].astype(F32).T.astype(BF)
    vrow_ref[...] = qkv_ref[2, 0].astype(F32).T.astype(BF)

    def bias_slot(j, i):
        return j * (j + 1) // 2 + i

    @pl.when(pl.program_id(0) == 0)
    def _():
        for j in range(n):
            for i in range(j + 1):
                keys = pl.ds(i * block, block)
                bias_ref[bias_slot(j, i)] = bias_block(
                    srow_ref[:, j * block : (j + 1) * block],
                    scol_ref[keys, :],
                    kpos_ref[keys, :],
                    j * block,
                    i * block,
                    block,
                    block,
                    i == j,
                )

    gscale = jnp.zeros((HEAD_DIM, 1), F32)
    for j in range(n):
        cols = slice(j * block, (j + 1) * block)
        q = qkv_ref[0, 0, :, cols]
        go = gout_ref[:, cols]
        lse = lse_ref[0, :, cols]
        delta = jnp.sum(go.astype(F32) * out_ref[0, :, cols].astype(F32), axis=0, keepdims=True)
        gq = jnp.zeros((HEAD_DIM, block), F32)
        for i in range(j + 1):
            keys = slice(i * block, (i + 1) * block)
            s = dot(krow_ref[keys, :], q, (1, 0)) + bias_ref[bias_slot(j, i)]
            p = jnp.exp(s - lse)
            gp = dot(vrow_ref[keys, :], go, (1, 0))
            gs = (p * (gp - delta)).astype(BF)
            gq += dot(qkv_ref[1, 0, :, keys], gs, (1, 0))
            gk = dot(q, gs, (1, 1))
            gv = dot(go, p.astype(BF), (1, 1))
            if i == j:
                gk_ref[:, keys] = gk
                gv_ref[:, keys] = gv
            else:
                gk_ref[:, keys] += gk
                gv_ref[:, keys] += gv
        gscale += jnp.sum(gq * raw_ref[0, :, cols], axis=1, keepdims=True)
        grad_ref[0, 0, :, cols] = (gq * factor_ref[...]).astype(BF)
    grad_ref[1, 0] = gk_ref[...].astype(BF)
    grad_ref[2, 0] = gv_ref[...].astype(BF)
    gscale_ref[0] = gscale


def mask_args(series, padding):
    t = series.shape[0]
    pos = jnp.arange(t, dtype=jnp.int32)
    return series.reshape(1, t), series.reshape(t, 1), jnp.where(padding == 0, pos, t).reshape(t, 1)


def attention_forward(at, qkv, masks, pieces=0):
    _, heads, hd, t = qkv.shape
    block = min(256, t) if t <= 2048 else 512
    n = t // block
    whole = lambda shape: pl.BlockSpec(shape, lambda h: (0,) * len(shape))
    assert pieces in (0, n)
    return pl.pallas_call(
        functools.partial(forward_kernel, block),
        grid=(heads,),
        in_specs=[
            pl.BlockSpec(memory_space=pltpu.SMEM),
            pl.BlockSpec((3, 1, hd, t), lambda h: (0, h, 0, 0)),
            whole((1, t)),
            whole((t, 1)),
            whole((t, 1)),
        ],
        out_specs=[
            pl.BlockSpec((1, hd, t), lambda h: (h, 0, 0)),
            pl.BlockSpec((1, 1, t), lambda h: (h, 0, 0)),
        ]
        + [pl.BlockSpec((1, hd, block), lambda h: (h, 0, 0))] * pieces,
        out_shape=[
            jax.ShapeDtypeStruct((heads, hd, t), BF),
            jax.ShapeDtypeStruct((heads, 1, t), F32),
        ]
        + [jax.ShapeDtypeStruct((heads, hd, block), BF)] * pieces,
        scratch_shapes=[
            pltpu.VMEM((n * (n + 1) // 2, block, block), F32),
            pltpu.VMEM((t, hd), BF),
            pltpu.VMEM((t, block), F32),
            pltpu.VMEM((n, hd, block), BF),
        ],
        compiler_params=pltpu.CompilerParams(vmem_limit_bytes=VMEM_LIMIT),
        cost_estimate=CHEAP,
        name="attention_forward",
    )(at, qkv, *masks)


def attention_backward(at, qkv, raw, factor, out, pieces, lse, masks, begin=0, heads=None):
    _, all_heads, hd, t = qkv.shape
    heads = heads or all_heads
    block = min(256, t) if t <= 2048 else 512
    n = t // block
    whole = lambda shape: pl.BlockSpec(shape, lambda h: (0,) * len(shape))
    head = lambda wide=t: pl.BlockSpec((1, hd, wide), lambda h: (begin + h, 0, 0))
    return pl.pallas_call(
        functools.partial(backward_kernel, block),
        grid=(heads,),
        in_specs=[
            pl.BlockSpec(memory_space=pltpu.SMEM),
            pl.BlockSpec((3, 1, hd, t), lambda h: (0, begin + h, 0, 0)),
            head(),
            whole((hd, 1)),
            head(),
            pl.BlockSpec((1, 1, t), lambda h: (begin + h, 0, 0)),
            whole((1, t)),
            whole((t, 1)),
            whole((t, 1)),
        ]
        + [head(p.shape[2]) for p in pieces],
        out_specs=[
            pl.BlockSpec((3, 1, hd, t), lambda h: (0, h, 0, 0)),
            pl.BlockSpec((1, hd, 1), lambda h: (h, 0, 0)),
        ],
        out_shape=[
            jax.ShapeDtypeStruct((3, heads, hd, t), BF),
            jax.ShapeDtypeStruct((heads, hd, 1), F32),
        ],
        scratch_shapes=[
            pltpu.VMEM((n * (n + 1) // 2, block, block), F32),
            pltpu.VMEM((t, hd), BF),
            pltpu.VMEM((t, hd), BF),
            pltpu.VMEM((hd, t), F32),
            pltpu.VMEM((hd, t), F32),
            pltpu.VMEM((hd, t), BF),
        ],
        compiler_params=pltpu.CompilerParams(vmem_limit_bytes=VMEM_LIMIT),
        cost_estimate=CHEAP,
        name="attention_backward",
    )(at, qkv, raw, factor, out, lse, *masks, *pieces)


def norm_scale(x):
    return lax.rsqrt(jnp.mean(x * x, axis=1, keepdims=True) + EPS)


def body_any(
    inputs, gain_attn, w_qkv, query_scale, w_out, gain_mlp, w_up, b_up, w_down, b_down, series_ids, pad_mask, cotangent
):
    rows, cols = size("row"), size("col")
    tok = inputs.shape[0]
    feat = inputs.shape[1]
    share = tok // cols
    t = series_ids.shape[0]
    head_rows = w_qkv.shape[2] // cols
    heads = head_rows // HEAD_DIM
    r, c = lax.axis_index("row"), lax.axis_index("col")

    blocks = gather_grid(inputs)
    strips = [jnp.concatenate(b, axis=1) for b in blocks]
    x_own = strips[0] if rows == 2 else lax.dynamic_index_in_dim(jnp.stack(strips), r, 0, keepdims=False)
    x_all = jnp.concatenate(flip(strips, "row"), axis=0)
    gain_one = jnp.concatenate(gather(gain_attn, "col"))
    gain_two = jnp.concatenate(gather(gain_mlp, "col"))
    bias_up = jnp.concatenate(gather(b_up, "row")).astype(F32)
    bias_down = jnp.concatenate(gather(b_down, "col")).astype(F32)

    w3 = jnp.transpose(w_qkv, (1, 0, 2)).reshape(3, feat, cols, head_rows)
    w_mine = lax.dynamic_index_in_dim(w3, c, 2, keepdims=False)
    w_give = lax.dynamic_index_in_dim(w3, 1 - c, 2, keepdims=False)
    w_half = swap(core_half(w_give, 1), "col")
    w_other = swap(w_half, "core")
    first = lax.axis_index("core") == 0
    w_full = jnp.concatenate(
        [w_mine, jnp.where(first, w_half, w_other), jnp.where(first, w_other, w_half)], axis=1
    )

    xf = x_all.astype(F32)
    scale_one = norm_scale(xf)
    normed_one = (xf * scale_one * gain_one).astype(BF)
    projected = jnp.einsum("td,sdh->sht", normed_one, w_full, preferred_element_type=F32)
    projected = projected.reshape(3, heads, HEAD_DIM, t)
    factor = QUERY_CONST / math.sqrt(HEAD_DIM) * jax.nn.softplus(query_scale)
    raw_q = projected[0]
    qkv = jnp.stack([raw_q * factor[None, :, None], projected[1], projected[2]]).astype(BF)
    masks = mask_args(series_ids, pad_mask)
    at = jnp.zeros((4,), jnp.int32)
    attended, lse = attention_forward(at, qkv, masks)

    def to_tokens(y):
        y = flip_dim(y.reshape(head_rows, rows, cols, share), "row", 1)
        y = flip_dim(y, "col", 2)
        y = exchange(y.reshape(1, head_rows, rows, cols, share), "row", 2, 0)
        y = exchange(y.reshape(rows, 1, head_rows, cols, share), "col", 3, 1)
        y = flip_dim(y.reshape(rows, cols, head_rows, share), "col", 1)
        return y.reshape(rows * cols * head_rows, share)

    def to_heads(y):
        y = flip_dim(y.reshape(rows, cols, head_rows, share), "col", 1)
        y = exchange(y.reshape(rows, cols, head_rows, 1, share), "col", 1, 3)
        y = exchange(y.reshape(rows, head_rows, 1, cols, share), "row", 0, 2)
        y = flip_dim(y.reshape(head_rows, rows, cols, share), "col", 2)
        return flip_dim(y, "row", 1).reshape(head_rows, t)

    w_out_all = weight_gather(w_out, 0)
    w_up_all = weight_gather(w_up, 1)
    w_down_all = weight_gather(w_down, 0)

    def my_share(y):
        return lax.dynamic_slice_in_dim(y, c * share, share, 0)

    att = to_tokens(attended.reshape(head_rows, t))
    x_mine = my_share(x_own).astype(F32)
    middle = x_mine + dot(att, w_out_all, (0, 0))
    scale_two = norm_scale(middle)
    normed_two = (middle * scale_two * gain_two).astype(BF)
    pre_act = dot(normed_two, w_up_all, (1, 0)) + bias_up
    sig = jax.nn.sigmoid(pre_act)
    hidden = (pre_act * sig).astype(BF)
    result = (middle + dot(hidden, w_down_all, (1, 0)) + bias_down).astype(BF)

    def to_block(y):
        mine, theirs = jnp.split(y, 2, axis=1)
        return jnp.concatenate(flip([mine, swap(theirs, "col")], "col"), axis=0)

    layer_out = to_block(result)

    g_give = lax.dynamic_slice_in_dim(cotangent, (1 - c) * share, share, 0)
    g = jnp.concatenate([my_share(cotangent), swap(g_give, "col")], axis=1)
    grad_w_down = dot(hidden, g, (0, 0))
    grad_hidden = dot(g, w_down_all, (1, 1))
    grad_pre_f = grad_hidden * sig * (1.0 + pre_act * (1.0 - sig))
    grad_pre = grad_pre_f.astype(BF)
    grad_b_up = jnp.sum(grad_pre.astype(F32), axis=0)
    grad_w_up = dot(normed_two, grad_pre, (0, 0))
    grad_normed_two = dot(grad_pre, w_up_all, (1, 1))
    weighted = grad_normed_two * gain_two
    inner = jnp.sum(weighted * middle, axis=1, keepdims=True)
    grad_middle = g.astype(F32) + scale_two * weighted - middle * (scale_two**3 * inner / D)
    grad_gain_mlp = jnp.sum(grad_normed_two * middle * scale_two, axis=0)
    grad_branch = grad_middle.astype(BF)
    grad_w_out = dot(att, grad_branch, (1, 0))
    grad_att = dot(w_out_all, grad_branch, (1, 1)).astype(BF)
    grad_attended = to_heads(grad_att).reshape(heads, HEAD_DIM, t)
    grad_middle_block = to_block(grad_middle)

    sum_down = weight_sum(grad_w_down, 0)
    sum_up = weight_sum(grad_w_up, 1)
    sum_out = weight_sum(grad_w_out, 0)

    grad_proj, gscale = attention_backward(
        at, qkv, raw_q, factor.reshape(HEAD_DIM, 1), attended, [grad_attended], lse, masks
    )
    slope = QUERY_CONST / math.sqrt(HEAD_DIM) * jax.nn.sigmoid(query_scale)
    grad_query_scale = jnp.sum(gscale, axis=(0, 2)) * slope
    grad_proj = grad_proj.reshape(3, head_rows, t)
    grad_normed_one = jnp.einsum("sht,sdh->td", grad_proj, w_full, preferred_element_type=F32)
    weighted_one = grad_normed_one * gain_one
    inner_one = jnp.sum(weighted_one * xf, axis=1)
    grad_gain_attn = jnp.sum(grad_normed_one * xf * scale_one, axis=0)
    inner_one = lax.psum(inner_one, ("row", "col"))
    grad_w = jnp.einsum("td,sht->sdh", normed_one, grad_proj, preferred_element_type=F32)
    grad_w = grad_w.reshape(3, cols, 2, feat // 2, head_rows)
    core = lax.axis_index("core")
    keep = lax.dynamic_index_in_dim(grad_w, core, 2, keepdims=False)
    give = lax.dynamic_index_in_dim(grad_w, 1 - core, 2, keepdims=False).astype(BF)
    part = (keep + swap(give, "core").astype(F32)).astype(BF)
    part = jnp.concatenate(flip([part[:, 0], swap(part[:, 1], "col")], "col"), axis=2)
    sum_qkv = jnp.transpose(z_sum(part), (1, 0, 2))

    e = jnp.concatenate(flip(jnp.split(grad_normed_one.astype(BF), 2, axis=0), "row"), axis=0) if rows == 2 else (
        grad_normed_one.astype(BF)
    )
    e = scatter_sum(e, "row", 0)
    e = scatter_sum(e, "col", 1).astype(F32)
    my_rows = lambda y: lax.dynamic_slice_in_dim(y, r * tok, tok, 0)
    scale_mine = my_rows(scale_one)
    inner_mine = my_rows(inner_one.reshape(t, 1))
    grad_inputs = grad_middle_block + scale_mine * (e * gain_attn) - inputs.astype(F32) * (
        scale_mine**3 * inner_mine / D
    )

    grad_b_down = jnp.sum(g.astype(F32), axis=0)
    vectors = jnp.concatenate(
        [
            flip_dim(grad_gain_attn, "col", 0),
            flip_dim(grad_gain_mlp, "col", 0),
            flip_dim(grad_b_down, "col", 0),
            flip_dim(grad_b_up, "row", 0),
            grad_query_scale,
        ]
    )
    vectors = lax.psum(vectors, ("z", "core", "row", "col"))
    mine_col = lambda at: lax.dynamic_slice_in_dim(vectors, at * D + c * feat, feat, 0)
    units = b_up.shape[0]
    return (
        layer_out,
        grad_inputs,
        mine_col(0),
        sum_qkv,
        vectors[4 * D :],
        sum_out,
        mine_col(1),
        sum_up,
        lax.dynamic_slice_in_dim(vectors, 3 * D + r * units, units, 0),
        sum_down,
        mine_col(2),
    )


SMEM = pl.BlockSpec(memory_space=pltpu.SMEM)
ANY = pl.BlockSpec(memory_space=pl.ANY)


def call(kernel, name, args, specs, outs, scratch=(), **more):
    return pl.pallas_call(
        kernel,
        in_specs=specs,
        out_shape=outs,
        scratch_shapes=list(scratch),
        compiler_params=pltpu.CompilerParams(vmem_limit_bytes=VMEM_LIMIT),
        cost_estimate=CHEAP,
        name=name,
        **more,
    )(*args)


VM = pl.BlockSpec(memory_space=pltpu.VMEM)


def shape(dims, kind):
    return jax.ShapeDtypeStruct(dims, kind)


def project_kernel(
    at, x00, x01, x10, x11, gain, factor, w_mine, w_a, w_b, qkv, raw, normed, scale_own, w_full
):
    r, k = at[0], at[2]
    tok, feat = x00.shape
    hr = w_mine.shape[1]
    half = hr // 2
    for s in range(3):
        w_full[pl.ds(s * hr, hr), 0:feat] = w_mine[s]
        for ref, core in ((w_a, k), (w_b, 1 - k)):
            w_full[pl.ds(pl.multiple_of(s * hr + core * half, 16), half), feat:] = ref[s]
    for i, (a_ref, b_ref) in enumerate(((x00, x01), (x10, x11))):
        a, b = a_ref[...].astype(F32), b_ref[...].astype(F32)
        total = jnp.sum(a * a, axis=1, keepdims=True) + jnp.sum(b * b, axis=1, keepdims=True)
        scale = lax.rsqrt(total / (2 * feat) + EPS)
        if i == 0:
            scale_own[...] = scale
        rows = pl.ds(pl.multiple_of((r ^ i) * tok, tok), tok)
        normed[rows, 0:feat] = (a * scale * gain[:, 0:feat]).astype(BF)
        normed[rows, feat:] = (b * scale * gain[:, feat:]).astype(BF)
        y = normed[rows, :]
        q = dot(w_full[0:hr, :], y, (1, 1))
        raw[:, rows] = q
        qkv[0, :, rows] = (q * factor[...]).astype(BF)
        qkv[1, :, rows] = dot(w_full[hr : 2 * hr, :], y, (1, 1)).astype(BF)
        qkv[2, :, rows] = dot(w_full[2 * hr : 3 * hr, :], y, (1, 1)).astype(BF)


def feed_kernel(
    at, a0, a1, a2, a3, x_own, x_col, g_own, g_col, gain, bias_up, bias_down,
    w_out, w_up, w_down, *rest
):
    blocks, rest = rest[:24], rest[24:]
    feed_body(
        at, a0, a1, a2, a3, x_own, x_col, g_own, g_col, gain, bias_up, bias_down, w_out, w_up, w_down, blocks, *rest
    )


def feed_body(
    at, a0, a1, a2, a3, x_own, x_col, g_own, g_col, gain, bias_up, bias_down, w_out, w_up, w_down, blocks,
    out_own, out_give, gm_own, gm_give, t0, t1, t2, t3, vectors,
    sx, sy, kx, ky, sx2, sy2, kx2, ky2,
    w, att, turned, sems,
):
    r, c, k = at[0], at[1], at[2]
    hr, share = a0.shape
    feat = x_own.shape[1]
    half = feat // 2
    quarter = half // 2
    even = at[4]
    copies = []
    for n in range(3):
        turn = (0, 1 + even, 2 - even)[n]
        rx, cx = (feat, 0) if n == 0 else (feat * (turn - 1), feat * (2 - turn))
        mine = [((w_out, w_up, w_down)[n], w.at[n, 0:feat, 0:feat])]
        for core, (px, py, p0, p1) in ((k, blocks[8 * n : 8 * n + 4]), (1 - k, blocks[8 * n + 4 : 8 * n + 8])):
            down = core * half
            at_x = pl.ds(pl.multiple_of(rx + down, 16), half)
            at_y = pl.ds(pl.multiple_of(feat - rx + down, 16), half)
            at_0 = pl.ds(pl.multiple_of(feat + down, 16), quarter)
            at_1 = pl.ds(pl.multiple_of(feat + down + quarter, 16), quarter)
            mine.append((px, w.at[turn, at_x, pl.ds(pl.multiple_of(cx, 128), feat)]))
            mine.append((py, w.at[turn, at_y, pl.ds(pl.multiple_of(feat - cx, 128), feat)]))
            mine.append((p0, w.at[turn, at_0, feat : 2 * feat]))
            mine.append((p1, w.at[turn, at_1, feat : 2 * feat]))
        started = []
        for m, (src, dst) in enumerate(mine):
            copy = pltpu.make_async_copy(src, dst, sems.at[n, m])
            copy.start()
            started.append(copy)
        copies.append(started)

    rows = pl.ds(pl.multiple_of(c * share, share), share)
    for s, a in enumerate((a0, a1, a2, a3)):
        to = (s // 2) * 2 * hr + (c ^ (s % 2)) * hr
        att[pl.ds(pl.multiple_of(to, 16), hr), :] = a[...]
    x = jnp.concatenate([x_own[rows, :], x_col[rows, :]], axis=1).astype(F32)
    g = jnp.concatenate([g_own[rows, :], g_col[...]], axis=1)
    for copy in copies[0]:
        copy.wait()
    middle = x + dot(att[...], w[0], (0, 0))
    scale = lax.rsqrt(jnp.sum(middle * middle, axis=1, keepdims=True) / D + EPS)
    normed = (middle * scale * gain[...]).astype(BF)
    for copy in copies[1] + copies[2]:
        copy.wait()
    pre = dot(normed, w[1], (1, 0)) + bias_up[...]
    sig = jax.nn.sigmoid(pre)
    hidden = (pre * sig).astype(BF)
    result = (middle + dot(hidden, w[2], (1, 0)) + bias_down[...]).astype(BF)
    out_own[...] = result[:, :feat]
    out_give[...] = result[:, feat:]

    def weight_grad(n, left_ref, right):
        for core, by_row, by_col in ((k, (sx, kx), (sy, ky)), (1 - k, (sx2, kx2), (sy2, ky2))):
            up, low = (by_col, by_row) if n == 1 else (by_row, by_col)
            for b in range(2):
                part = pl.ds(pl.multiple_of(b * feat + core * half, 16), half)
                y = dot(left_ref[part, :], right, (1, 0)).astype(BF)
                for j in range(2):
                    cut = slice(j * feat, (j + 1) * feat)
                    up[1 - b][j, n] = y[:quarter, cut]
                    low[1 - j][b, n] = y[quarter:, cut]

    turned[...] = hidden.astype(F32).T.astype(BF)
    grad_pre_f = dot(g, w[2], (1, 1)) * sig * (1.0 + pre * (1.0 - sig))
    grad_pre = grad_pre_f.astype(BF)
    weight_grad(2, turned, g)
    grad_normed = dot(grad_pre, w[1], (1, 1))
    weighted = grad_normed * gain[...]
    inner = jnp.sum(weighted * middle, axis=1, keepdims=True)
    gf = g.astype(F32)
    grad_middle = gf + scale * weighted - middle * (scale * scale * scale * inner / D)
    gm_own[...] = grad_middle[:, :feat]
    gm_give[...] = grad_middle[:, feat:].astype(BF)
    branch = grad_middle.astype(BF)
    for s, t in enumerate((t0, t1, t2, t3)):
        come = (s // 2) * 2 * hr + (c ^ (s % 2)) * hr
        t[...] = dot(w[0, pl.ds(pl.multiple_of(come, 16), hr), :], branch, (1, 1)).astype(BF)
    turned[...] = normed.astype(F32).T.astype(BF)
    weight_grad(1, turned, grad_pre)
    weight_grad(0, att, branch)
    vectors[...] = jnp.concatenate(
        [
            jnp.sum(grad_normed * (middle * scale), axis=0, keepdims=True),
            jnp.sum(gf, axis=0, keepdims=True),
            jnp.sum(grad_pre.astype(F32), axis=0, keepdims=True),
        ],
        axis=0,
    )


def weight_back_kernel(at, grad, normed, keep, give):
    k = at[2]
    part = keep.shape[2]
    feat = keep.shape[3]
    for ref, core in ((give, 1 - k), (keep, k)):
        for s in range(3):
            rows = pl.ds(pl.multiple_of(core * part, 16), part)
            y = dot(grad[s, rows, :], normed[...], (1, 0)).astype(BF)
            ref[0, s] = y[:, :feat]
            ref[1, s] = y[:, feat:]


def project_back_kernel(
    at, grad_a, grad_b, w_full, x00, x01, x10, x11, gain, e0, e1, e2, e3, inner_own, gain_sum, grad
):
    r = at[0]
    tok, feat = x00.shape
    part = grad_a.shape[1]
    for s in range(3):
        for n, ref in enumerate((grad_a, grad_b)):
            grad[(2 * s + n) * part : (2 * s + n + 1) * part, :] = ref[s]
    sums = [jnp.zeros((1, feat), F32), jnp.zeros((1, feat), F32)]
    for i, (xs, es) in enumerate((((x00, x01), (e0, e1)), ((x10, x11), (e2, e3)))):
        rows = pl.ds(pl.multiple_of((r ^ i) * tok, tok), tok)
        left = grad[:, rows]
        products, squares, inner = [], 0.0, 0.0
        for j in range(2):
            cut = slice(j * feat, (j + 1) * feat)
            e = dot(left, w_full[:, cut], (0, 0))
            x = xs[j][...].astype(F32)
            product = e * x
            inner = inner + jnp.sum(product * gain[:, cut], axis=1, keepdims=True)
            squares = squares + jnp.sum(x * x, axis=1, keepdims=True)
            es[j][0:tok, :] = e.astype(es[j].dtype)
            products.append(product)
        scale = lax.rsqrt(squares / (2 * feat) + EPS)
        for j in range(2):
            sums[j] += jnp.sum(products[j] * scale, axis=0, keepdims=True)
        line = jnp.broadcast_to(inner, (tok, 128)).T[0:1, :]
        high = line.astype(BF).astype(F32)
        extra = jnp.concatenate([high, line - high, jnp.zeros((14, tok), F32)], axis=0)
        extra = jnp.concatenate([extra, jnp.zeros((16, feat - tok), F32)], axis=1).astype(BF)
        if i == 0:
            inner_own[...] = inner
            es[1][tok:, :] = extra
        else:
            es[0][tok:, :] = extra
            es[1][tok:, :] = extra
    gain_sum[:, 0:feat] = sums[0]
    gain_sum[:, feat:] = sums[1]


def merge_send_kernel(a, a2, b, b2, *outs):
    for n in range(3):
        outs[n][...] = add(a[:, n], a2[:, n])
        outs[3 + n][...] = add(b[:, n], b2[:, n])


def merge_keep_kernel(a, a2, b, b2, *refs):
    *got, p0, p1, q0, q1 = refs
    for n in range(3):
        p0[n], p1[n] = add(a[0, n], a2[0, n], got[n][0]), add(a[1, n], a2[1, n], got[n][1])
        q0[n], q1[n] = add(b[0, n], b2[0, n], got[3 + n][0]), add(b[1, n], b2[1, n], got[3 + n][1])


def finish_qkv_kernel(at, *refs):
    c, k = at[1], at[2]
    *parts, out, rows = refs
    half = parts[0].shape[1]
    for s in range(3):
        for pair in range(2):
            mine, theirs, mine2, theirs2 = parts[4 * pair : 4 * pair + 4]
            for ref, col, core in ((mine, c, k), (theirs, 1 - c, k), (mine2, c, 1 - k), (theirs2, 1 - c, 1 - k)):
                to = pl.multiple_of((4 * col + 2 * pair + core) * half, 16)
                rows[pl.ds(to, half), :] = ref[s].astype(F32)
        out[s] = rows[...].T


def finish_feed_kernel(at, a, b, a2, b2, *outs):
    k = at[2]
    quarter = a.shape[1]
    for n, out in enumerate(outs):
        upper, lower = ((b, b2), (a, a2)) if n == 1 else ((a, a2), (b, b2))
        for i, core in ((0, k), (1, 1 - k)):
            for j, refs in enumerate((upper, lower)):
                to = pl.multiple_of((2 * core + j) * quarter, 16)
                out[pl.ds(to, quarter), :] = refs[i][n].astype(F32)


def after(x, *earlier):
    return lax.optimization_barrier((x, *earlier))[0]


def add(*parts):
    total = parts[0].astype(F32)
    for part in parts[1:]:
        total = total + part.astype(F32)
    return total.astype(BF)


def diagonal(x):
    return lax.ppermute(x, ("row", "col"), [(0, 3), (1, 2), (2, 1), (3, 0)])


def z_swap(x, step):
    n = size("z")
    return lax.ppermute(x, "z", [(i, i ^ step) for i in range(n)])


def z_first():
    z = lax.axis_index("z")
    return (z == 0) | (z == 3)


def z_pair(a, b):
    first = z_first()
    return add(jnp.where(first, a, b), z_swap(jnp.where(first, b, a), 1))


def z_meet(mine):
    return add(mine, z_swap(mine, 3))


def z_back(mine):
    first = z_first()
    other = z_swap(mine, 1)
    return jnp.where(first, mine, other), jnp.where(first, other, mine)


together = lax.optimization_barrier


def body_four(
    inputs, gain_attn, w_qkv, query_scale, w_out, gain_mlp, w_up, b_up, w_down, b_down, series_ids, pad_mask, cotangent
):
    tok, feat = inputs.shape
    share = tok // 2
    t = series_ids.shape[0]
    hr = w_qkv.shape[2] // 2
    heads = hr // HEAD_DIM
    few = heads // 2
    half = feat // 2
    quarter = half // 2
    r, c, k = lax.axis_index("row"), lax.axis_index("col"), lax.axis_index("core")
    even = lax.axis_index("z") % 2
    at = jnp.stack([r, c, k, 2 * r + c, even]).astype(jnp.int32)
    mine_rows = lambda y, part: lax.dynamic_slice_in_dim(y, part * share, share, 0)
    core_swap = lambda ys: [swap(y, "core") for y in ys]
    small_f32 = lambda y: y.astype(F32)

    x01, x10 = swap(inputs, "col"), swap(inputs, "row")
    small = swap(jnp.concatenate([gain_attn, gain_mlp, small_f32(b_down)]), "col")
    up_other = swap(small_f32(b_up), "row")
    w_turned = jnp.transpose(w_qkv, (1, 2, 0)).reshape(3, 2, hr, feat)
    w_mine = lax.dynamic_index_in_dim(w_turned, c, 1, keepdims=False)
    w_half = core_half(lax.dynamic_index_in_dim(w_turned, 1 - c, 1, keepdims=False), 1)
    part_z = jnp.where(even == 0, core_half(w_up, 0), core_half(w_down, 0))
    part_o = core_half(w_out, 0)
    g_give = mine_rows(cotangent, 1 - c)
    factor = QUERY_CONST / math.sqrt(HEAD_DIM) * jax.nn.softplus(query_scale)
    factor_col = factor.reshape(HEAD_DIM, 1)
    factor_all = jnp.tile(factor_col, (heads, 1))
    x01, x10, small, up_other, w_mine, w_half, part_z, part_o, g_give, factor_all = together(
        (x01, x10, small, up_other, w_mine, w_half, part_z, part_o, g_give, factor_all)
    )

    x11 = swap(x01, "row")
    w_a = swap(w_half, "col")
    gain_one = jnp.concatenate([gain_attn, small[:feat]]).reshape(1, D)
    gain_two = jnp.concatenate([gain_mlp, small[feat : 2 * feat]]).reshape(1, D)
    bias_down = jnp.concatenate([small_f32(b_down), small[2 * feat :]]).reshape(1, D)
    bias_up = jnp.concatenate([small_f32(b_up), up_other]).reshape(1, D)
    masks = mask_args(series_ids, pad_mask)
    x11, w_a, part_z, part_o, gain_one, gain_two, bias_up, bias_down, masks = together(
        (x11, w_a, part_z, part_o, gain_one, gain_two, bias_up, bias_down, masks)
    )

    hx, hy = swap(part_z, "row"), swap(part_z, "col")
    w_b = swap(w_a, "core")
    qkv, raw, normed_one, scale_own, w_full = call(
        project_kernel,
        "project",
        (at, inputs, x01, x10, x11, gain_one, factor_all, w_mine, w_a, w_b),
        [SMEM] + [VM] * 9,
        [
            shape((3, hr, t), BF),
            shape((hr, t), F32),
            shape((t, D), BF),
            shape((tok, 1), F32),
            shape((3 * hr, D), BF),
        ],
    )
    qkv, hx, hy, part_o = together((qkv, hx, hy, part_o))

    qkv = qkv.reshape(3, heads, HEAD_DIM, t)
    raw = raw.reshape(heads, HEAD_DIM, t)
    d0, d1 = swap(hx[:quarter], "col"), swap(hy[quarter:], "row")
    hx_o, hy_o = swap(part_o, "row"), swap(part_o, "col")
    hx_z = z_swap(hx, 1)
    hx2, hy2 = core_swap((hx, hy))
    attended, lse, *a = attention_forward(at, qkv, masks, pieces=4)
    a, d0, d1, hx_o, hy_o, hx_z, hx2, hy2, g_give, hy = together(
        (a, d0, d1, hx_o, hy_o, hx_z, hx2, hy2, g_give, hy)
    )

    a0, a1, a2, a3 = [p.reshape(hr, share) for p in a]
    a1, a2, a3 = swap(a1, "col"), swap(a2, "row"), diagonal(a3)
    hy_z, d0_z, d1_z = z_swap(hy, 1), z_swap(d0, 1), z_swap(d1, 1)
    d0_o, d1_o = swap(hx_o[:quarter], "col"), swap(hy_o[quarter:], "row")
    g_col = swap(g_give, "col")
    d02, d12, hx_o2, hy_o2, hx_z2 = core_swap((d0, d1, hx_o, hy_o, hx_z))
    a1, a2, a3, hy_z, d0_z, d1_z, d0_o, d1_o, g_col, d02, d12, hx_o2, hy_o2, hx_z2 = together(
        (a1, a2, a3, hy_z, d0_z, d1_z, d0_o, d1_o, g_col, d02, d12, hx_o2, hy_o2, hx_z2)
    )
    hy_z2, d0_z2, d1_z2, d0_o2, d1_o2 = core_swap((hy_z, d0_z, d1_z, d0_o, d1_o))
    blocks = (hx_o, hy_o, d0_o, d1_o, hx_o2, hy_o2, d0_o2, d1_o2)
    blocks += (hx, hy, d0, d1, hx2, hy2, d02, d12)
    blocks += (hx_z, hy_z, d0_z, d1_z, hx_z2, hy_z2, d0_z2, d1_z2)
    out_own, out_give, gm_own, gm_give, t0, t1, t2, t3, vectors, *grads = call(
        feed_kernel,
        "feed_forward",
        (at, a0, a1, a2, a3, inputs, x01, cotangent, g_col, gain_two, bias_up, bias_down)
        + (w_out, w_up, w_down, *blocks),
        [SMEM] + [VM] * 11 + [ANY] * 27,
        [
            shape((share, feat), BF),
            shape((share, feat), BF),
            shape((share, feat), F32),
            shape((share, feat), BF),
        ]
        + [shape((hr, share), BF)] * 4
        + [shape((3, D), F32)]
        + [shape((2, 3, quarter, feat), BF)] * 8,
        scratch=[
            pltpu.VMEM((3, D, D), BF),
            pltpu.VMEM((D, share), BF),
            pltpu.VMEM((D, share), BF),
            pltpu.SemaphoreType.DMA((3, 9)),
        ],
    )

    t1, t2, t3 = swap(t1, "col"), swap(t2, "row"), diagonal(t3)
    sx, sy, kx, ky, *other_core = grads
    sx2, sy2, kx2, ky2 = core_swap(other_core)
    sends = call(
        merge_send_kernel,
        "merge_send",
        (sx, sx2, sy, sy2),
        [VM] * 4,
        [shape((2, quarter, feat), BF)] * 6,
    )
    t0, t1, t2, t3, sends, kx2, ky2 = together((t0, t1, t2, t3, sends, kx2, ky2))

    pieces = [p.reshape(heads, HEAD_DIM, share) for p in (t0, t1, t2, t3)]
    got_x, got_y = [None] * 3, [None] * 3
    got_x[0], got_y[0] = swap(sends[0], "row"), swap(sends[3], "col")
    grad_a, scale_a = attention_backward(at, qkv, raw, factor_col, attended, pieces, lse, masks, 0, few)
    grad_a, got_x[0], got_y[0], sends = together((grad_a, got_x[0], got_y[0], sends))

    def weight_back(grad):
        kept, sent = call(
            weight_back_kernel,
            "weight_back",
            (at, grad, normed_one),
            [SMEM] + [VM] * 2,
            [shape((2, 3, hr // 4, feat), BF)] * 2,
        )
        return add(kept, swap(sent, "core"))

    grad_a = grad_a.reshape(3, hr // 2, t)
    got_x[1], got_y[1] = swap(sends[1], "row"), swap(sends[4], "col")
    w_pair_a = weight_back(grad_a)
    w_pair_a, got_x[1], got_y[1], sends, lse = together((w_pair_a, got_x[1], got_y[1], sends, lse))

    got_x[2], got_y[2] = swap(sends[2], "row"), swap(sends[5], "col")
    mine_a = z_pair(w_pair_a[0], w_pair_a[1])
    grad_b, scale_b = attention_backward(at, qkv, raw, factor_col, attended, pieces, lse, masks, few, few)
    grad_b, mine_a, got_x[2], got_y[2] = together((grad_b, mine_a, got_x[2], got_y[2]))

    grad_b = grad_b.reshape(3, hr // 2, t)
    mine_a = z_meet(mine_a)
    px, px_send, py, py_send = call(
        merge_keep_kernel,
        "merge_keep",
        (kx, kx2, ky, ky2, *got_x, *got_y),
        [VM] * 10,
        [shape((3, quarter, feat), BF)] * 4,
    )
    qx, qy = swap(px_send, "col"), swap(py_send, "row")
    w_pair_b = weight_back(after(grad_b, px_send))
    mine_a, w_pair_b, qx, qy, px, py, grad_a, grad_b = together((mine_a, w_pair_b, qx, qy, px, py, grad_a, grad_b))

    back_a, theirs_a = z_back(mine_a)
    mine_b = z_pair(w_pair_b[0], w_pair_b[1])
    fx, fy = add(px, qx), add(py, qy)
    e0, e1, e2, e3, inner, gain_sum = call(
        project_back_kernel,
        "project_back",
        (at, grad_a, grad_b, w_full, inputs, x01, x10, x11, gain_one),
        [SMEM] + [VM] * 8,
        [
            shape((tok, feat), F32),
            shape((tok + 16, feat), BF),
            shape((tok + 16, feat), BF),
            shape((tok + 16, feat), BF),
            shape((tok, 1), F32),
            shape((1, D), F32),
        ],
        scratch=[pltpu.VMEM((3 * hr, t), BF)],
    )
    back_a, theirs_a, mine_b, fx, fy, e1, e2, e3, gain_sum, vectors = together(
        (back_a, theirs_a, mine_b, fx, fy, e1, e2, e3, gain_sum, vectors)
    )

    theirs_a = swap(theirs_a, "col")
    e1, e2, e3 = swap(e1, "col"), swap(e2, "row"), diagonal(e3)
    mine_b = z_meet(mine_b)
    mine_c = z_pair(fx, fy)
    slope = QUERY_CONST / math.sqrt(HEAD_DIM) * jax.nn.sigmoid(query_scale)
    grad_query_scale = (jnp.sum(scale_a, axis=(0, 2)) + jnp.sum(scale_b, axis=(0, 2))) * slope
    total = jnp.concatenate([gain_sum, vectors]).reshape(4, 2, feat)
    turn = jnp.stack([c, c, c, r]).reshape(4, 1, 1) == 1
    total = jnp.where(turn, total[:, ::-1], total).reshape(8, feat)
    total = jnp.concatenate([total, jnp.pad(grad_query_scale, (0, feat - HEAD_DIM)).reshape(1, feat)])
    total = total + swap(total, "core")
    mine_b, mine_c, theirs_a, total, out_give, gm_give = together(
        (mine_b, mine_c, theirs_a, total, out_give, gm_give)
    )

    mine_c = z_meet(mine_c)
    back_b, theirs_b = z_back(mine_b)
    theirs_b = swap(theirs_b, "col")
    out_col, gm_col = swap(out_give, "col"), swap(gm_give, "col")
    total = (total + swap(total, "row")) + (swap(total, "col") + diagonal(total))
    mine_c, back_b, theirs_b, out_col, gm_col, e1, e2, e3, total = together(
        (mine_c, back_b, theirs_b, out_col, gm_col, e1, e2, e3, total)
    )

    fx, fy = z_back(mine_c)
    w_args = (back_a, theirs_a, *core_swap((back_a, theirs_a)), back_b, theirs_b, *core_swap((back_b, theirs_b)))
    sum_qkv = call(
        finish_qkv_kernel,
        "finish_qkv",
        (at, *w_args),
        [SMEM] + [VM] * 8,
        shape((3, feat, 2 * hr), F32),
        scratch=[pltpu.VMEM((2 * hr, feat), F32)],
    )
    sum_qkv = jnp.transpose(sum_qkv, (1, 0, 2))
    e = e0
    for more in (e1, e2, e3):
        e = e + more[:tok].astype(F32)
        inner = inner + jnp.sum(more[tok : tok + 2, :tok].astype(F32), axis=0).reshape(tok, 1)
    grad_middle = jnp.concatenate(flip([gm_own, gm_col.astype(F32)], "col"), axis=0)
    grad_inputs = grad_middle + scale_own * (e * gain_attn) - inputs.astype(F32) * (scale_own**3 * inner / D)
    layer_out = jnp.concatenate(flip([out_own, out_col], "col"), axis=0)
    total = (total + z_swap(total, 1)) + (z_swap(total, 2) + z_swap(total, 3))
    sum_out, sum_up, sum_down = call(
        finish_feed_kernel,
        "finish_feed",
        (at, fx, fy, *core_swap((fx, fy))),
        [SMEM] + [VM] * 4,
        [shape((feat, feat), F32)] * 3,
    )
    pick = lambda n, place: lax.dynamic_index_in_dim(total, 2 * n + place, 0, keepdims=False)
    return (
        layer_out,
        grad_inputs,
        pick(0, c),
        sum_qkv,
        total[8, :HEAD_DIM],
        sum_out,
        pick(1, c),
        sum_up,
        pick(3, r),
        sum_down,
        pick(2, c),
    )


def solution(mesh):
    dp, rows, cols = mesh.shape["dp"], mesh.shape["row"], mesh.shape["col"]
    split = Mesh(mesh.devices.reshape(dp // 2, 2, rows, cols), ("z", "core", "row", "col"))
    tokens = P(("z", "core", "row"), "col")
    in_specs = (
        tokens,
        P("col"),
        P("col", None, "row"),
        P(),
        P("row", "col"),
        P("col"),
        P("col", "row"),
        P("row"),
        P("row", "col"),
        P("col"),
        P(("z", "core")),
        P(("z", "core")),
        tokens,
    )
    out_specs = (
        tokens,
        tokens,
        P("col"),
        P("col", None, "row"),
        P(),
        P("row", "col"),
        P("col"),
        P("col", "row"),
        P("row"),
        P("row", "col"),
        P("col"),
    )
    body = body_four if (dp, rows, cols) == (8, 2, 2) else body_any
    return jax.shard_map(body, mesh=split, in_specs=in_specs, out_specs=out_specs, check_vma=False)
```

```python
import functools
import math

import jax
import jax.numpy as jnp
from jax import lax
from jax.experimental import pallas as pl
from jax.experimental.pallas import tpu as pltpu
from jax.sharding import Mesh
from jax.sharding import PartitionSpec as P

D = 1280
HEAD_DIM = 80
EPS = 1e-06
QUERY_CONST = 1.442695041
MASKED = -1e30
BF = jnp.bfloat16
F32 = jnp.float32
VMEM_LIMIT = 50 * 1024 * 1024
CHEAP = pl.CostEstimate(flops=1, bytes_accessed=1, transcendentals=0)


def size(axis):
    return lax.axis_size(axis)


def swap(x, axis):
    return lax.ppermute(x, axis, [(0, 1), (1, 0)])


def flip(blocks, axis):
    if size(axis) != 2:
        return list(blocks)
    first = lax.axis_index(axis) == 0
    a, b = blocks
    return [jnp.where(first, a, b), jnp.where(first, b, a)]


def flip_dim(x, axis, dim):
    if size(axis) != 2:
        return x
    return jnp.concatenate(flip(jnp.split(x, 2, axis=dim), axis), axis=dim)


def gather(x, axis):
    if size(axis) == 2:
        return [x, swap(x, axis)]
    whole = lax.all_gather(x, axis, axis=0, tiled=False)
    return [whole[i] for i in range(size(axis))]


def gather_grid(x):
    if size("row") != 2:
        return [gather(b, "col") for b in gather(x, "row")]
    along_row, along_col = swap(x, "row"), swap(x, "col")
    half = x.shape[0] // 2
    across = jnp.concatenate(
        [swap(along_row[:half], "col"), swap(along_col[half:], "row")], axis=0
    )
    return [[x, along_col], [along_row, across]]


def scatter_sum(x, axis, dim):
    if size(axis) != 2:
        return lax.psum_scatter(x, axis, scatter_dimension=dim, tiled=True)
    mine, theirs = jnp.split(x, 2, axis=dim)
    return (mine.astype(F32) + swap(theirs, axis).astype(F32)).astype(x.dtype)


def exchange(x, axis, split, join):
    if size(axis) != 2:
        return lax.all_to_all(x, axis, split, join, tiled=True)
    mine, theirs = jnp.split(x, 2, axis=split)
    return jnp.concatenate([mine, swap(theirs, axis)], axis=join)


def core_half(x, dim):
    return lax.dynamic_slice_in_dim(
        x, lax.axis_index("core") * (x.shape[dim] // 2), x.shape[dim] // 2, dim
    )


def weight_gather(w, row_dim):
    part = core_half(w, 0)
    blocks = gather_grid(part)
    if row_dim == 1:
        blocks = [list(b) for b in zip(*blocks)]
    mine = jnp.stack([jnp.concatenate(b, axis=1) for b in blocks])
    other = swap(mine, "core")
    first = lax.axis_index("core") == 0
    both = jnp.stack([jnp.where(first, mine, other), jnp.where(first, other, mine)], axis=1)
    return both.reshape(-1, both.shape[-1])


def weight_sum(g, row_dim):
    dim_axis = ("row", "col") if row_dim == 0 else ("col", "row")
    n0 = size(dim_axis[0])
    g = g.reshape(n0, 2, g.shape[0] // n0 // 2, g.shape[1])
    core = lax.axis_index("core")
    keep = lax.dynamic_index_in_dim(g, core, 1, keepdims=False)
    give = lax.dynamic_index_in_dim(g, 1 - core, 1, keepdims=False).astype(BF)
    part = (keep + swap(give, "core").astype(F32)).astype(BF)
    part = scatter_sum(part, dim_axis[0], 0)
    part = scatter_sum(part[0], dim_axis[1], 1)
    return z_sum(part)


def z_sum(part):
    total = lax.psum(part, "z")
    other = swap(total, "core")
    return flip_core(total, other)


def flip_core(total, other):
    first = lax.axis_index("core") == 0
    return jnp.concatenate(
        [jnp.where(first, total, other), jnp.where(first, other, total)], axis=-2
    ).astype(F32)


def dot(a, b, contract):
    return lax.dot_general(a, b, ((contract[0:1], contract[1:2]), ((), ())), preferred_element_type=F32)


def bias_block(series_row, series_col, key_pos, q0, k0, qb, kb, diagonal):
    q_pos = q0 + lax.broadcasted_iota(jnp.int32, (1, qb), 1)
    allowed = (series_col == series_row) & (key_pos <= q_pos)
    if diagonal:
        k_pos = k0 + lax.broadcasted_iota(jnp.int32, (kb, 1), 0)
        allowed = allowed | (k_pos == q_pos)
    return jnp.where(allowed, 0.0, MASKED)


def forward_kernel(block, at, qkv_ref, srow_ref, scol_ref, kpos_ref, out_ref, lse_ref, *rest):
    *pieces, bias_ref, krow_ref, s_ref, slot_ref = rest
    t = qkv_ref.shape[3]
    n = t // block
    krow_ref[...] = qkv_ref[1, 0].astype(F32).T.astype(BF)

    def bias_slot(j, i):
        return j * (j + 1) // 2 + i

    @pl.when(pl.program_id(0) == 0)
    def _():
        for j in range(n):
            for i in range(j + 1):
                keys = pl.ds(i * block, block)
                bias_ref[bias_slot(j, i)] = bias_block(
                    srow_ref[:, j * block : (j + 1) * block],
                    scol_ref[keys, :],
                    kpos_ref[keys, :],
                    j * block,
                    i * block,
                    block,
                    block,
                    i == j,
                )

    for j in range(n):
        cols = slice(j * block, (j + 1) * block)
        q = qkv_ref[0, 0, :, cols]
        top = None
        for i in range(j + 1):
            s = dot(krow_ref[i * block : (i + 1) * block, :], q, (1, 0)) + bias_ref[bias_slot(j, i)]
            s_ref[i * block : (i + 1) * block, :] = s
            here = jnp.max(s, axis=0, keepdims=True)
            top = here if top is None else jnp.maximum(top, here)
        total = jnp.zeros((1, block), F32)
        acc = jnp.zeros((HEAD_DIM, block), F32)
        for i in range(j + 1):
            p = jnp.exp(s_ref[i * block : (i + 1) * block, :] - top)
            total += jnp.sum(p, axis=0, keepdims=True)
            acc += dot(qkv_ref[2, 0, :, i * block : (i + 1) * block], p.astype(BF), (1, 0))
        found = (acc / total).astype(BF)
        out_ref[0, :, cols] = found
        if pieces:
            slot_ref[j ^ at[3]] = found
        lse_ref[0, :, cols] = top + jnp.log(total)
    for slot, piece in enumerate(pieces):
        piece[0] = slot_ref[slot]


def backward_kernel(
    block, at, qkv_ref, raw_ref, factor_ref, out_ref, lse_ref, srow_ref, scol_ref, kpos_ref, *rest
):
    *pieces, grad_ref, gscale_ref, bias_ref, krow_ref, vrow_ref, gk_ref, gv_ref, gout_ref = rest
    if len(pieces) == 1:
        gout_ref[...] = pieces[0][0]
    else:
        for slot, piece in enumerate(pieces):
            wide = piece.shape[2]
            gout_ref[:, pl.ds(pl.multiple_of((slot ^ at[3]) * wide, 128), wide)] = piece[0]
    t = qkv_ref.shape[3]
    n = t // block
    krow_ref[...] = qkv_ref[1, 0].astype(F32).T.astype(BF)
    vrow_ref[...] = qkv_ref[2, 0].astype(F32).T.astype(BF)

    def bias_slot(j, i):
        return j * (j + 1) // 2 + i

    @pl.when(pl.program_id(0) == 0)
    def _():
        for j in range(n):
            for i in range(j + 1):
                keys = pl.ds(i * block, block)
                bias_ref[bias_slot(j, i)] = bias_block(
                    srow_ref[:, j * block : (j + 1) * block],
                    scol_ref[keys, :],
                    kpos_ref[keys, :],
                    j * block,
                    i * block,
                    block,
                    block,
                    i == j,
                )

    gscale = jnp.zeros((HEAD_DIM, 1), F32)
    for j in range(n):
        cols = slice(j * block, (j + 1) * block)
        q = qkv_ref[0, 0, :, cols]
        go = gout_ref[:, cols]
        lse = lse_ref[0, :, cols]
        delta = jnp.sum(go.astype(F32) * out_ref[0, :, cols].astype(F32), axis=0, keepdims=True)
        gq = jnp.zeros((HEAD_DIM, block), F32)
        for i in range(j + 1):
            keys = slice(i * block, (i + 1) * block)
            s = dot(krow_ref[keys, :], q, (1, 0)) + bias_ref[bias_slot(j, i)]
            p = jnp.exp(s - lse)
            gp = dot(vrow_ref[keys, :], go, (1, 0))
            gs = (p * (gp - delta)).astype(BF)
            gq += dot(qkv_ref[1, 0, :, keys], gs, (1, 0))
            gk = dot(q, gs, (1, 1))
            gv = dot(go, p.astype(BF), (1, 1))
            if i == j:
                gk_ref[:, keys] = gk
                gv_ref[:, keys] = gv
            else:
                gk_ref[:, keys] += gk
                gv_ref[:, keys] += gv
        gscale += jnp.sum(gq * raw_ref[0, :, cols], axis=1, keepdims=True)
        grad_ref[0, 0, :, cols] = (gq * factor_ref[...]).astype(BF)
    grad_ref[1, 0] = gk_ref[...].astype(BF)
    grad_ref[2, 0] = gv_ref[...].astype(BF)
    gscale_ref[0] = gscale


def mask_args(series, padding):
    t = series.shape[0]
    pos = jnp.arange(t, dtype=jnp.int32)
    return series.reshape(1, t), series.reshape(t, 1), jnp.where(padding == 0, pos, t).reshape(t, 1)


def attention_forward(at, qkv, masks, pieces=0):
    _, heads, hd, t = qkv.shape
    block = min(256, t) if t <= 2048 else 512
    n = t // block
    whole = lambda shape: pl.BlockSpec(shape, lambda h: (0,) * len(shape))
    assert pieces in (0, n)
    return pl.pallas_call(
        functools.partial(forward_kernel, block),
        grid=(heads,),
        in_specs=[
            pl.BlockSpec(memory_space=pltpu.SMEM),
            pl.BlockSpec((3, 1, hd, t), lambda h: (0, h, 0, 0)),
            whole((1, t)),
            whole((t, 1)),
            whole((t, 1)),
        ],
        out_specs=[
            pl.BlockSpec((1, hd, t), lambda h: (h, 0, 0)),
            pl.BlockSpec((1, 1, t), lambda h: (h, 0, 0)),
        ]
        + [pl.BlockSpec((1, hd, block), lambda h: (h, 0, 0))] * pieces,
        out_shape=[
            jax.ShapeDtypeStruct((heads, hd, t), BF),
            jax.ShapeDtypeStruct((heads, 1, t), F32),
        ]
        + [jax.ShapeDtypeStruct((heads, hd, block), BF)] * pieces,
        scratch_shapes=[
            pltpu.VMEM((n * (n + 1) // 2, block, block), F32),
            pltpu.VMEM((t, hd), BF),
            pltpu.VMEM((t, block), F32),
            pltpu.VMEM((n, hd, block), BF),
        ],
        compiler_params=pltpu.CompilerParams(vmem_limit_bytes=VMEM_LIMIT),
        cost_estimate=CHEAP,
        name="attention_forward",
    )(at, qkv, *masks)


def attention_backward(at, qkv, raw, factor, out, pieces, lse, masks, begin=0, heads=None):
    _, all_heads, hd, t = qkv.shape
    heads = heads or all_heads
    block = min(256, t) if t <= 2048 else 512
    n = t // block
    whole = lambda shape: pl.BlockSpec(shape, lambda h: (0,) * len(shape))
    head = lambda wide=t: pl.BlockSpec((1, hd, wide), lambda h: (begin + h, 0, 0))
    return pl.pallas_call(
        functools.partial(backward_kernel, block),
        grid=(heads,),
        in_specs=[
            pl.BlockSpec(memory_space=pltpu.SMEM),
            pl.BlockSpec((3, 1, hd, t), lambda h: (0, begin + h, 0, 0)),
            head(),
            whole((hd, 1)),
            head(),
            pl.BlockSpec((1, 1, t), lambda h: (begin + h, 0, 0)),
            whole((1, t)),
            whole((t, 1)),
            whole((t, 1)),
        ]
        + [head(p.shape[2]) for p in pieces],
        out_specs=[
            pl.BlockSpec((3, 1, hd, t), lambda h: (0, h, 0, 0)),
            pl.BlockSpec((1, hd, 1), lambda h: (h, 0, 0)),
        ],
        out_shape=[
            jax.ShapeDtypeStruct((3, heads, hd, t), BF),
            jax.ShapeDtypeStruct((heads, hd, 1), F32),
        ],
        scratch_shapes=[
            pltpu.VMEM((n * (n + 1) // 2, block, block), F32),
            pltpu.VMEM((t, hd), BF),
            pltpu.VMEM((t, hd), BF),
            pltpu.VMEM((hd, t), F32),
            pltpu.VMEM((hd, t), F32),
            pltpu.VMEM((hd, t), BF),
        ],
        compiler_params=pltpu.CompilerParams(vmem_limit_bytes=VMEM_LIMIT),
        cost_estimate=CHEAP,
        name="attention_backward",
    )(at, qkv, raw, factor, out, lse, *masks, *pieces)


def norm_scale(x):
    return lax.rsqrt(jnp.mean(x * x, axis=1, keepdims=True) + EPS)


def body_any(
    inputs, gain_attn, w_qkv, query_scale, w_out, gain_mlp, w_up, b_up, w_down, b_down, series_ids, pad_mask, cotangent
):
    rows, cols = size("row"), size("col")
    tok = inputs.shape[0]
    feat = inputs.shape[1]
    share = tok // cols
    t = series_ids.shape[0]
    head_rows = w_qkv.shape[2] // cols
    heads = head_rows // HEAD_DIM
    r, c = lax.axis_index("row"), lax.axis_index("col")

    blocks = gather_grid(inputs)
    strips = [jnp.concatenate(b, axis=1) for b in blocks]
    x_own = strips[0] if rows == 2 else lax.dynamic_index_in_dim(jnp.stack(strips), r, 0, keepdims=False)
    x_all = jnp.concatenate(flip(strips, "row"), axis=0)
    gain_one = jnp.concatenate(gather(gain_attn, "col"))
    gain_two = jnp.concatenate(gather(gain_mlp, "col"))
    bias_up = jnp.concatenate(gather(b_up, "row")).astype(F32)
    bias_down = jnp.concatenate(gather(b_down, "col")).astype(F32)

    w3 = jnp.transpose(w_qkv, (1, 0, 2)).reshape(3, feat, cols, head_rows)
    w_mine = lax.dynamic_index_in_dim(w3, c, 2, keepdims=False)
    w_give = lax.dynamic_index_in_dim(w3, 1 - c, 2, keepdims=False)
    w_half = swap(core_half(w_give, 1), "col")
    w_other = swap(w_half, "core")
    first = lax.axis_index("core") == 0
    w_full = jnp.concatenate(
        [w_mine, jnp.where(first, w_half, w_other), jnp.where(first, w_other, w_half)], axis=1
    )

    xf = x_all.astype(F32)
    scale_one = norm_scale(xf)
    normed_one = (xf * scale_one * gain_one).astype(BF)
    projected = jnp.einsum("td,sdh->sht", normed_one, w_full, preferred_element_type=F32)
    projected = projected.reshape(3, heads, HEAD_DIM, t)
    factor = QUERY_CONST / math.sqrt(HEAD_DIM) * jax.nn.softplus(query_scale)
    raw_q = projected[0]
    qkv = jnp.stack([raw_q * factor[None, :, None], projected[1], projected[2]]).astype(BF)
    masks = mask_args(series_ids, pad_mask)
    at = jnp.zeros((4,), jnp.int32)
    attended, lse = attention_forward(at, qkv, masks)

    def to_tokens(y):
        y = flip_dim(y.reshape(head_rows, rows, cols, share), "row", 1)
        y = flip_dim(y, "col", 2)
        y = exchange(y.reshape(1, head_rows, rows, cols, share), "row", 2, 0)
        y = exchange(y.reshape(rows, 1, head_rows, cols, share), "col", 3, 1)
        y = flip_dim(y.reshape(rows, cols, head_rows, share), "col", 1)
        return y.reshape(rows * cols * head_rows, share)

    def to_heads(y):
        y = flip_dim(y.reshape(rows, cols, head_rows, share), "col", 1)
        y = exchange(y.reshape(rows, cols, head_rows, 1, share), "col", 1, 3)
        y = exchange(y.reshape(rows, head_rows, 1, cols, share), "row", 0, 2)
        y = flip_dim(y.reshape(head_rows, rows, cols, share), "col", 2)
        return flip_dim(y, "row", 1).reshape(head_rows, t)

    w_out_all = weight_gather(w_out, 0)
    w_up_all = weight_gather(w_up, 1)
    w_down_all = weight_gather(w_down, 0)

    def my_share(y):
        return lax.dynamic_slice_in_dim(y, c * share, share, 0)

    att = to_tokens(attended.reshape(head_rows, t))
    x_mine = my_share(x_own).astype(F32)
    middle = x_mine + dot(att, w_out_all, (0, 0))
    scale_two = norm_scale(middle)
    normed_two = (middle * scale_two * gain_two).astype(BF)
    pre_act = dot(normed_two, w_up_all, (1, 0)) + bias_up
    sig = jax.nn.sigmoid(pre_act)
    hidden = (pre_act * sig).astype(BF)
    result = (middle + dot(hidden, w_down_all, (1, 0)) + bias_down).astype(BF)

    def to_block(y):
        mine, theirs = jnp.split(y, 2, axis=1)
        return jnp.concatenate(flip([mine, swap(theirs, "col")], "col"), axis=0)

    layer_out = to_block(result)

    g_give = lax.dynamic_slice_in_dim(cotangent, (1 - c) * share, share, 0)
    g = jnp.concatenate([my_share(cotangent), swap(g_give, "col")], axis=1)
    grad_w_down = dot(hidden, g, (0, 0))
    grad_hidden = dot(g, w_down_all, (1, 1))
    grad_pre_f = grad_hidden * sig * (1.0 + pre_act * (1.0 - sig))
    grad_pre = grad_pre_f.astype(BF)
    grad_b_up = jnp.sum(grad_pre.astype(F32), axis=0)
    grad_w_up = dot(normed_two, grad_pre, (0, 0))
    grad_normed_two = dot(grad_pre, w_up_all, (1, 1))
    weighted = grad_normed_two * gain_two
    inner = jnp.sum(weighted * middle, axis=1, keepdims=True)
    grad_middle = g.astype(F32) + scale_two * weighted - middle * (scale_two**3 * inner / D)
    grad_gain_mlp = jnp.sum(grad_normed_two * middle * scale_two, axis=0)
    grad_branch = grad_middle.astype(BF)
    grad_w_out = dot(att, grad_branch, (1, 0))
    grad_att = dot(w_out_all, grad_branch, (1, 1)).astype(BF)
    grad_attended = to_heads(grad_att).reshape(heads, HEAD_DIM, t)
    grad_middle_block = to_block(grad_middle)

    sum_down = weight_sum(grad_w_down, 0)
    sum_up = weight_sum(grad_w_up, 1)
    sum_out = weight_sum(grad_w_out, 0)

    grad_proj, gscale = attention_backward(
        at, qkv, raw_q, factor.reshape(HEAD_DIM, 1), attended, [grad_attended], lse, masks
    )
    slope = QUERY_CONST / math.sqrt(HEAD_DIM) * jax.nn.sigmoid(query_scale)
    grad_query_scale = jnp.sum(gscale, axis=(0, 2)) * slope
    grad_proj = grad_proj.reshape(3, head_rows, t)
    grad_normed_one = jnp.einsum("sht,sdh->td", grad_proj, w_full, preferred_element_type=F32)
    weighted_one = grad_normed_one * gain_one
    inner_one = jnp.sum(weighted_one * xf, axis=1)
    grad_gain_attn = jnp.sum(grad_normed_one * xf * scale_one, axis=0)
    inner_one = lax.psum(inner_one, ("row", "col"))
    grad_w = jnp.einsum("td,sht->sdh", normed_one, grad_proj, preferred_element_type=F32)
    grad_w = grad_w.reshape(3, cols, 2, feat // 2, head_rows)
    core = lax.axis_index("core")
    keep = lax.dynamic_index_in_dim(grad_w, core, 2, keepdims=False)
    give = lax.dynamic_index_in_dim(grad_w, 1 - core, 2, keepdims=False).astype(BF)
    part = (keep + swap(give, "core").astype(F32)).astype(BF)
    part = jnp.concatenate(flip([part[:, 0], swap(part[:, 1], "col")], "col"), axis=2)
    sum_qkv = jnp.transpose(z_sum(part), (1, 0, 2))

    e = jnp.concatenate(flip(jnp.split(grad_normed_one.astype(BF), 2, axis=0), "row"), axis=0) if rows == 2 else (
        grad_normed_one.astype(BF)
    )
    e = scatter_sum(e, "row", 0)
    e = scatter_sum(e, "col", 1).astype(F32)
    my_rows = lambda y: lax.dynamic_slice_in_dim(y, r * tok, tok, 0)
    scale_mine = my_rows(scale_one)
    inner_mine = my_rows(inner_one.reshape(t, 1))
    grad_inputs = grad_middle_block + scale_mine * (e * gain_attn) - inputs.astype(F32) * (
        scale_mine**3 * inner_mine / D
    )

    grad_b_down = jnp.sum(g.astype(F32), axis=0)
    vectors = jnp.concatenate(
        [
            flip_dim(grad_gain_attn, "col", 0),
            flip_dim(grad_gain_mlp, "col", 0),
            flip_dim(grad_b_down, "col", 0),
            flip_dim(grad_b_up, "row", 0),
            grad_query_scale,
        ]
    )
    vectors = lax.psum(vectors, ("z", "core", "row", "col"))
    mine_col = lambda at: lax.dynamic_slice_in_dim(vectors, at * D + c * feat, feat, 0)
    units = b_up.shape[0]
    return (
        layer_out,
        grad_inputs,
        mine_col(0),
        sum_qkv,
        vectors[4 * D :],
        sum_out,
        mine_col(1),
        sum_up,
        lax.dynamic_slice_in_dim(vectors, 3 * D + r * units, units, 0),
        sum_down,
        mine_col(2),
    )


SMEM = pl.BlockSpec(memory_space=pltpu.SMEM)
ANY = pl.BlockSpec(memory_space=pl.ANY)


def call(kernel, name, args, specs, outs, scratch=(), **more):
    return pl.pallas_call(
        kernel,
        in_specs=specs,
        out_shape=outs,
        scratch_shapes=list(scratch),
        compiler_params=pltpu.CompilerParams(vmem_limit_bytes=VMEM_LIMIT),
        cost_estimate=CHEAP,
        name=name,
        **more,
    )(*args)


VM = pl.BlockSpec(memory_space=pltpu.VMEM)


def shape(dims, kind):
    return jax.ShapeDtypeStruct(dims, kind)


def project_kernel(
    at, x00, x01, x10, x11, gain, factor, w_mine, w_a, w_b, qkv, raw, normed, scale_own, w_full
):
    r, k = at[0], at[2]
    tok, feat = x00.shape
    hr = w_mine.shape[1]
    half = hr // 2
    for s in range(3):
        w_full[pl.ds(s * hr, hr), 0:feat] = w_mine[s]
        w_full[pl.ds(pl.multiple_of(s * hr + k * half, 16), half), feat:] = w_a[s]
        w_full[pl.ds(pl.multiple_of(s * hr + (1 - k) * half, 16), half), feat:] = w_b[s]
    for i, (a_ref, b_ref) in enumerate(((x00, x01), (x10, x11))):
        a, b = a_ref[...].astype(F32), b_ref[...].astype(F32)
        total = jnp.sum(a * a, axis=1, keepdims=True) + jnp.sum(b * b, axis=1, keepdims=True)
        scale = lax.rsqrt(total / (2 * feat) + EPS)
        if i == 0:
            scale_own[...] = scale
        rows = pl.ds(pl.multiple_of((r ^ i) * tok, tok), tok)
        normed[rows, 0:feat] = (a * scale * gain[:, 0:feat]).astype(BF)
        normed[rows, feat:] = (b * scale * gain[:, feat:]).astype(BF)
        y = normed[rows, :]
        q = dot(w_full[0:hr, :], y, (1, 1))
        raw[:, rows] = q
        qkv[0, :, rows] = (q * factor[...]).astype(BF)
        qkv[1, :, rows] = dot(w_full[hr : 2 * hr, :], y, (1, 1)).astype(BF)
        qkv[2, :, rows] = dot(w_full[2 * hr : 3 * hr, :], y, (1, 1)).astype(BF)


def feed_kernel(
    at, a0, a1, a2, a3, x_own, x_col, g_own, g_col, gain, bias_up, bias_down,
    w_out, w_up, w_down, hx, hy, d0, d1, hx2, hy2, d02, d12,
    out_own, gm_own, post, t0, t1, t2, t3, vectors,
    *rest,
):
    *grads, w, att, turned, sems = rest
    r, c, k = at[0], at[1], at[2]
    hr, share = a0.shape
    feat = x_own.shape[1]
    half = feat // 2
    quarter = half // 2
    copies = []
    for n, shard in enumerate((w_out, w_up, w_down)):
        rx, cx, ry, cy = (0, feat, feat, 0) if n == 1 else (feat, 0, 0, feat)
        mine = []
        mine.append((shard, w.at[n, 0:feat, 0:feat]))
        for core, (px, py, p0, p1) in ((k, (hx, hy, d0, d1)), (1 - k, (hx2, hy2, d02, d12))):
            down = core * half
            at_x = pl.ds(pl.multiple_of(rx + down, 16), half)
            at_y = pl.ds(pl.multiple_of(ry + down, 16), half)
            first = d0.shape[1]
            at_0 = pl.ds(pl.multiple_of(feat + down, 16), first)
            at_1 = pl.ds(pl.multiple_of(feat + down + first, 16), half - first)
            mine.append((px.at[n], w.at[n, at_x, cx : cx + feat]))
            mine.append((py.at[n], w.at[n, at_y, cy : cy + feat]))
            mine.append((p0.at[n], w.at[n, at_0, feat : 2 * feat]))
            mine.append((p1.at[n], w.at[n, at_1, feat : 2 * feat]))
        started = []
        for m, (src, dst) in enumerate(mine):
            copy = pltpu.make_async_copy(src, dst, sems.at[n, m])
            copy.start()
            started.append(copy)
        copies.append(started)

    rows = pl.ds(pl.multiple_of(c * share, share), share)
    for s, a in enumerate((a0, a1, a2, a3)):
        to = (s // 2) * 2 * hr + (c ^ (s % 2)) * hr
        att[pl.ds(pl.multiple_of(to, 16), hr), :] = a[...]
    x = jnp.concatenate([x_own[rows, :], x_col[rows, :]], axis=1).astype(F32)
    g = jnp.concatenate([g_own[rows, :], g_col[...]], axis=1)
    for copy in copies[0]:
        copy.wait()
    middle = x + dot(att[...], w[0], (0, 0))
    scale = lax.rsqrt(jnp.sum(middle * middle, axis=1, keepdims=True) / D + EPS)
    normed = (middle * scale * gain[...]).astype(BF)
    for copy in copies[1]:
        copy.wait()
    pre = dot(normed, w[1], (1, 0)) + bias_up[...]
    sig = jax.nn.sigmoid(pre)
    hidden = (pre * sig).astype(BF)
    for copy in copies[2]:
        copy.wait()
    result = (middle + dot(hidden, w[2], (1, 0)) + bias_down[...]).astype(BF)
    out_own[...] = result[:, :feat]
    post[0] = result[:, feat:]

    def weight_grad(n, left_ref, right):
        for core, sets in ((k, grads[:8]), (1 - k, grads[8:])):
            by_row, by_col = sets[:4], sets[4:]
            up, low = (by_col, by_row) if n == 1 else (by_row, by_col)
            for b in range(2):
                part = pl.ds(pl.multiple_of(b * feat + core * half, 16), half)
                y = dot(left_ref[part, :], right, (1, 0)).astype(BF)
                for j in range(2):
                    cut = slice(j * feat, (j + 1) * feat)
                    up[2 * j + (1 - b)][n] = y[:quarter, cut]
                    low[2 * b + (1 - j)][n] = y[quarter:, cut]

    turned[...] = hidden.astype(F32).T.astype(BF)
    grad_pre_f = dot(g, w[2], (1, 1)) * sig * (1.0 + pre * (1.0 - sig))
    grad_pre = grad_pre_f.astype(BF)
    weight_grad(2, turned, g)
    grad_normed = dot(grad_pre, w[1], (1, 1))
    weighted = grad_normed * gain[...]
    inner = jnp.sum(weighted * middle, axis=1, keepdims=True)
    gf = g.astype(F32)
    grad_middle = gf + scale * weighted - middle * (scale * scale * scale * inner / D)
    gm_own[...] = grad_middle[:, :feat]
    post[1] = grad_middle[:, feat:].astype(BF)
    branch = grad_middle.astype(BF)
    for s, t in enumerate((t0, t1, t2, t3)):
        come = (s // 2) * 2 * hr + (c ^ (s % 2)) * hr
        t[...] = dot(w[0, pl.ds(pl.multiple_of(come, 16), hr), :], branch, (1, 1)).astype(BF)
    turned[...] = normed.astype(F32).T.astype(BF)
    weight_grad(1, turned, grad_pre)
    weight_grad(0, att, branch)
    vectors[...] = jnp.concatenate(
        [
            jnp.sum(grad_normed * (middle * scale), axis=0, keepdims=True),
            jnp.sum(gf, axis=0, keepdims=True),
            jnp.sum(grad_pre.astype(F32), axis=0, keepdims=True),
        ],
        axis=0,
    )


def weight_back_kernel(at, grad, normed, keep, give):
    k = at[2]
    part = keep.shape[2]
    feat = keep.shape[3]
    for ref, core in ((give, 1 - k), (keep, k)):
        for s in range(3):
            rows = pl.ds(pl.multiple_of(core * part, 16), part)
            y = dot(grad[s, rows, :], normed[...], (1, 0)).astype(BF)
            ref[0, s] = y[:, :feat]
            ref[1, s] = y[:, feat:]


def project_back_kernel(
    at, grad_a, grad_b, w_full, x00, x01, x10, x11, gain, e0, e1, e2, e3, inner_own, gain_sum, grad
):
    r = at[0]
    tok, feat = x00.shape
    part = grad_a.shape[1]
    for s in range(3):
        for n, ref in enumerate((grad_a, grad_b)):
            grad[(2 * s + n) * part : (2 * s + n + 1) * part, :] = ref[s]
    sums = [jnp.zeros((1, feat), F32), jnp.zeros((1, feat), F32)]
    for i, (xs, es) in enumerate((((x00, x01), (e0, e1)), ((x10, x11), (e2, e3)))):
        rows = pl.ds(pl.multiple_of((r ^ i) * tok, tok), tok)
        left = grad[:, rows]
        products, squares, inner = [], 0.0, 0.0
        for j in range(2):
            cut = slice(j * feat, (j + 1) * feat)
            e = dot(left, w_full[:, cut], (0, 0))
            x = xs[j][...].astype(F32)
            product = e * x
            inner = inner + jnp.sum(product * gain[:, cut], axis=1, keepdims=True)
            squares = squares + jnp.sum(x * x, axis=1, keepdims=True)
            es[j][0:tok, :] = e.astype(es[j].dtype)
            products.append(product)
        scale = lax.rsqrt(squares / (2 * feat) + EPS)
        for j in range(2):
            sums[j] += jnp.sum(products[j] * scale, axis=0, keepdims=True)
        line = jnp.broadcast_to(inner, (tok, 128)).T[0:1, :]
        high = line.astype(BF).astype(F32)
        extra = jnp.concatenate([high, line - high, jnp.zeros((14, tok), F32)], axis=0)
        extra = jnp.concatenate([extra, jnp.zeros((16, feat - tok), F32)], axis=1).astype(BF)
        if i == 0:
            inner_own[...] = inner
            es[1][tok:, :] = extra
        else:
            es[0][tok:, :] = extra
            es[1][tok:, :] = extra
    gain_sum[:, 0:feat] = sums[0]
    gain_sum[:, feat:] = sums[1]


def finish_qkv_kernel(at, *refs):
    c, k = at[1], at[2]
    *parts, out, rows = refs
    half = parts[0].shape[1]
    for s in range(3):
        for pair in range(2):
            mine, theirs, mine2, theirs2 = parts[4 * pair : 4 * pair + 4]
            for ref, col, core in ((mine, c, k), (theirs, 1 - c, k), (mine2, c, 1 - k), (theirs2, 1 - c, 1 - k)):
                to = pl.multiple_of((4 * col + 2 * pair + core) * half, 16)
                rows[pl.ds(to, half), :] = ref[s].astype(F32)
        out[s] = rows[...].T


def finish_feed_kernel(at, a, b, a2, b2, *outs):
    k = at[2]
    quarter = a.shape[1]
    for n, out in enumerate(outs):
        upper, lower = ((b, b2), (a, a2)) if n == 1 else ((a, a2), (b, b2))
        for i, core in ((0, k), (1, 1 - k)):
            for j, refs in enumerate((upper, lower)):
                to = pl.multiple_of((2 * core + j) * quarter, 16)
                out[pl.ds(to, quarter), :] = refs[i][n].astype(F32)


def after(x, *earlier):
    return lax.optimization_barrier((x, *earlier))[0]


def add(*parts):
    total = parts[0].astype(F32)
    for part in parts[1:]:
        total = total + part.astype(F32)
    return total.astype(BF)


def diagonal(x):
    return lax.ppermute(x, ("row", "col"), [(0, 3), (1, 2), (2, 1), (3, 0)])


def z_swap(x, step):
    n = size("z")
    return lax.ppermute(x, "z", [(i, i ^ step) for i in range(n)])


def z_first():
    z = lax.axis_index("z")
    return (z == 0) | (z == 3)


def z_pair(a, b, *earlier):
    first = z_first()
    got = z_swap(jnp.where(first, b, a), 1)
    a, b = lax.optimization_barrier((a, b, *earlier))[:2]
    return add(jnp.where(first, a, b), got)


def z_meet(mine):
    return add(mine, z_swap(mine, 3))


def z_back(mine):
    first = z_first()
    other = z_swap(mine, 1)
    return jnp.where(first, mine, other), jnp.where(first, other, mine)


def body_four(
    inputs, gain_attn, w_qkv, query_scale, w_out, gain_mlp, w_up, b_up, w_down, b_down, series_ids, pad_mask, cotangent
):
    tok, feat = inputs.shape
    share = tok // 2
    t = series_ids.shape[0]
    hr = w_qkv.shape[2] // 2
    heads = hr // HEAD_DIM
    half = feat // 2
    r, c, k = lax.axis_index("row"), lax.axis_index("col"), lax.axis_index("core")
    at = jnp.stack([r, c, k, 2 * r + c]).astype(jnp.int32)
    mine_rows = lambda y, part: lax.dynamic_slice_in_dim(y, part * share, share, 0)

    few = heads // 2
    quarter = half // 2
    first_rows = (half * 7 // 20) // 16 * 16
    x01 = swap(inputs, "col")
    x10 = swap(inputs, "row")
    small = swap(jnp.concatenate([gain_attn, gain_mlp, b_down.astype(F32)]), "col")
    up_other = swap(b_up.astype(F32), "row")
    w_turned = jnp.transpose(w_qkv, (1, 2, 0)).reshape(3, 2, hr, feat)
    w_mine = lax.dynamic_index_in_dim(w_turned, c, 1, keepdims=False)
    w_give = lax.dynamic_index_in_dim(w_turned, 1 - c, 1, keepdims=False)
    w_half = core_half(w_give, 1)
    w_a = swap(w_half, "col")
    part = jnp.stack([core_half(w_out, 0), core_half(w_up, 0), core_half(w_down, 0)])
    g_give = mine_rows(cotangent, 1 - c)
    x01, x10, small, up_other, part, g_give, w_mine = lax.optimization_barrier(
        (x01, x10, small, up_other, part, g_give, w_mine)
    )
    x11 = swap(after(x01, w_half), "row")
    w_b = swap(w_a, "core")
    gain_one = jnp.concatenate([gain_attn, small[:feat]]).reshape(1, D)
    gain_two = jnp.concatenate([gain_mlp, small[feat : 2 * feat]]).reshape(1, D)
    bias_down = jnp.concatenate([b_down.astype(F32), small[2 * feat :]]).reshape(1, D)
    bias_up = jnp.concatenate([b_up.astype(F32), up_other]).reshape(1, D)
    factor = QUERY_CONST / math.sqrt(HEAD_DIM) * jax.nn.softplus(query_scale)
    factor_col = factor.reshape(HEAD_DIM, 1)

    part = after(part, x11, w_a)
    hx, hy = swap(part, "row"), swap(part, "col")
    hx2, hy2 = swap(hx, "core"), swap(hy, "core")
    qkv, raw, normed_one, scale_own, w_full = call(
        project_kernel,
        "project",
        (at, inputs, x01, x10, x11, gain_one, jnp.tile(factor_col, (heads, 1)), w_mine, w_a, w_b),
        [SMEM] + [VM] * 9,
        [
            shape((3, hr, t), BF),
            shape((hr, t), F32),
            shape((t, D), BF),
            shape((tok, 1), F32),
            shape((3 * hr, D), BF),
        ],
    )
    qkv = qkv.reshape(3, heads, HEAD_DIM, t)
    masks = mask_args(series_ids, pad_mask)
    attended, lse, *a = attention_forward(at, qkv, masks, pieces=4)
    a0, a1, a2, a3 = [p.reshape(hr, share) for p in a]
    a1, a2, a3 = swap(a1, "col"), swap(a2, "row"), diagonal(a3)
    hx_on, hy_on, g_give, a1, a2, a3 = lax.optimization_barrier((hx, hy, g_give, a1, a2, a3))
    d0 = swap(hx_on[:, :first_rows], "col")
    d1 = swap(hy_on[:, first_rows:], "row")
    g_col = swap(g_give, "col")
    d0, d1, g_col = lax.optimization_barrier((d0, d1, g_col))
    d02, d12 = swap(d0, "core"), swap(d1, "core")
    out_own, gm_own, post, t0, t1, t2, t3, vectors, *grads = call(
        feed_kernel,
        "feed_forward",
        (at, a0, a1, a2, a3, inputs, x01, cotangent, g_col, gain_two, bias_up, bias_down)
        + (w_out, w_up, w_down, hx, hy, d0, d1, hx2, hy2, d02, d12),
        [SMEM] + [VM] * 11 + [ANY] * 11,
        [
            shape((share, feat), BF),
            shape((share, feat), F32),
            shape((2, share, feat), BF),
        ]
        + [shape((hr, share), BF)] * 4
        + [shape((3, D), F32)]
        + [shape((3, quarter, feat), BF)] * 16,
        scratch=[
            pltpu.VMEM((3, D, D), BF),
            pltpu.VMEM((D, share), BF),
            pltpu.VMEM((D, share), BF),
            pltpu.SemaphoreType.DMA((3, 9)),
        ],
    )
    t1, t2, t3 = swap(t1, "col"), swap(t2, "row"), diagonal(t3)
    (sx0, kx0, sx1, kx1, sy0, ky0, sy1, ky1), others = grads[:8], grads[8:]
    over = lambda n: swap(others[n], "core")
    sx1, sy1 = add(sx1, over(2)), add(sy1, over(6))
    sx0, sy0 = add(sx0, over(0)), add(sy0, over(4))
    *pieces, sx1, sy1, sx0, sy0 = lax.optimization_barrier((t0, t1, t2, t3, sx1, sy1, sx0, sy0))
    rx1, ry1 = swap(sx1, "row"), swap(sy1, "col")
    pieces = [p.reshape(heads, HEAD_DIM, share) for p in pieces]
    raw = raw.reshape(heads, HEAD_DIM, t)

    def weight_back(grad, *earlier):
        kept, sent = call(
            weight_back_kernel,
            "weight_back",
            (at, grad, normed_one),
            [SMEM] + [VM] * 2,
            [shape((2, 3, hr // 4, feat), BF)] * 2,
        )
        return kept, sent

    grad_a, scale_a = attention_backward(at, qkv, raw, factor_col, attended, pieces, lse, masks, 0, few)
    grad_a = grad_a.reshape(3, hr // 2, t)
    kept, sent = weight_back(grad_a)
    sent, rx1, ry1, sx0, sy0 = lax.optimization_barrier((sent, rx1, ry1, sx0, sy0))
    px1, py1 = add(kx1, over(3), rx1), add(ky1, over(7), ry1)
    w_pair_a = add(kept, swap(sent, "core"))
    qx, qy = swap(px1, "col"), swap(py1, "row")
    lse_on = after(lse, w_pair_a, px1, py1)
    grad_b, scale_b = attention_backward(at, qkv, raw, factor_col, attended, pieces, lse_on, masks, few, few)
    grad_b = grad_b.reshape(3, hr // 2, t)
    mine_a = z_pair(w_pair_a[0], w_pair_a[1], grad_b)
    kept, sent = weight_back(after(grad_b, mine_a))
    sent, qx, qy, sx0, sy0 = lax.optimization_barrier((sent, qx, qy, sx0, sy0))
    rx0, ry0 = swap(sx0, "row"), swap(sy0, "col")
    w_pair_b = add(kept, swap(sent, "core"))
    met_a = z_swap(mine_a, 3)
    slope = QUERY_CONST / math.sqrt(HEAD_DIM) * jax.nn.sigmoid(query_scale)
    grad_query_scale = (jnp.sum(scale_a, axis=(0, 2)) + jnp.sum(scale_b, axis=(0, 2))) * slope
    e0, e1, e2, e3, inner, gain_sum = call(
        project_back_kernel,
        "project_back",
        (at, grad_a, after(grad_b, w_pair_b), w_full, inputs, x01, x10, x11, gain_one),
        [SMEM] + [VM] * 8,
        [
            shape((tok, feat), F32),
            shape((tok + 16, feat), BF),
            shape((tok + 16, feat), BF),
            shape((tok + 16, feat), BF),
            shape((tok, 1), F32),
            shape((1, D), F32),
        ],
        scratch=[pltpu.VMEM((3 * hr, t), BF)],
    )
    first = z_first()
    got_b = z_swap(jnp.where(first, w_pair_b[1], w_pair_b[0]), 1)
    got_b, w_pair_b, mine_a, met_a, rx0, ry0, e1, e2, e3 = lax.optimization_barrier(
        (got_b, w_pair_b, mine_a, met_a, rx0, ry0, e1, e2, e3)
    )
    mine_a = add(mine_a, met_a)
    mine_b = z_meet(add(jnp.where(first, w_pair_b[0], w_pair_b[1]), got_b))
    fx, fy = add(kx0, over(1), rx0, qx), add(ky0, over(5), ry0, qy)
    mine_c = z_pair(fx, fy)
    e1, e2 = swap(e1, "col"), swap(e2, "row")
    mine_a, mine_b, mine_c, e1, e2, e3, post, gain_sum = lax.optimization_barrier(
        (mine_a, mine_b, mine_c, e1, e2, e3, post, gain_sum)
    )
    e3, post = diagonal(e3), swap(post, "col")
    w_args = [at]
    for mine in (mine_a, mine_b):
        w_own, w_theirs = z_back(mine)
        w_theirs = swap(w_theirs, "col")
        w_args += [w_own, w_theirs, swap(w_own, "core"), swap(w_theirs, "core")]
    mine_c = z_meet(mine_c)
    mine_c, e3, post = lax.optimization_barrier((mine_c, e3, post))
    fx, fy = z_back(mine_c)
    sum_qkv = call(
        finish_qkv_kernel,
        "finish_qkv",
        w_args,
        [SMEM] + [VM] * 8,
        shape((3, feat, 2 * hr), F32),
        scratch=[pltpu.VMEM((2 * hr, feat), F32)],
    )
    sum_qkv = jnp.transpose(sum_qkv, (1, 0, 2))

    e = e0
    for more in (e1, e2, e3):
        e = e + more[:tok].astype(F32)
        inner = inner + jnp.sum(more[tok : tok + 2, :tok].astype(F32), axis=0).reshape(tok, 1)
    grad_middle = jnp.concatenate(flip([gm_own, post[1].astype(F32)], "col"), axis=0)
    grad_inputs = grad_middle + scale_own * (e * gain_attn) - inputs.astype(F32) * (scale_own**3 * inner / D)
    layer_out = jnp.concatenate(flip([out_own, post[0]], "col"), axis=0)

    total = jnp.concatenate([gain_sum, vectors]).reshape(4, 2, feat)
    turn = jnp.stack([c, c, c, r]).reshape(4, 1, 1) == 1
    total = jnp.where(turn, total[:, ::-1], total).reshape(8, feat)
    total = jnp.concatenate([total, jnp.pad(grad_query_scale, (0, feat - HEAD_DIM)).reshape(1, feat)])
    total = total + swap(total, "core")
    total = (total + swap(total, "row")) + (swap(total, "col") + diagonal(total))
    total = after(total, w_theirs)
    total = (total + z_swap(total, 1)) + (z_swap(total, 2) + z_swap(total, 3))
    pick = lambda n, place: lax.dynamic_index_in_dim(total, 2 * n + place, 0, keepdims=False)
    sum_out, sum_up, sum_down = call(
        finish_feed_kernel,
        "finish_feed",
        (after(at, sum_qkv, grad_inputs, layer_out), fx, fy, swap(fx, "core"), swap(fy, "core")),
        [SMEM] + [VM] * 4,
        [shape((feat, feat), F32)] * 3,
    )

    return (
        layer_out,
        grad_inputs,
        pick(0, c),
        sum_qkv,
        total[8, :HEAD_DIM],
        sum_out,
        pick(1, c),
        sum_up,
        pick(3, r),
        sum_down,
        pick(2, c),
    )


def solution(mesh):
    dp, rows, cols = mesh.shape["dp"], mesh.shape["row"], mesh.shape["col"]
    split = Mesh(mesh.devices.reshape(dp // 2, 2, rows, cols), ("z", "core", "row", "col"))
    tokens = P(("z", "core", "row"), "col")
    in_specs = (
        tokens,
        P("col"),
        P("col", None, "row"),
        P(),
        P("row", "col"),
        P("col"),
        P("col", "row"),
        P("row"),
        P("row", "col"),
        P("col"),
        P(("z", "core")),
        P(("z", "core")),
        tokens,
    )
    out_specs = (
        tokens,
        tokens,
        P("col"),
        P("col", None, "row"),
        P(),
        P("row", "col"),
        P("col"),
        P("col", "row"),
        P("row"),
        P("row", "col"),
        P("col"),
    )
    body = body_four if (dp, rows, cols) == (8, 2, 2) else body_any
    return jax.shard_map(body, mesh=split, in_specs=in_specs, out_specs=out_specs, check_vma=False)
```

```python
import functools
import math

import jax
import jax.numpy as jnp
from jax import lax
from jax.experimental import pallas as pl
from jax.experimental.pallas import tpu as pltpu
from jax.sharding import Mesh
from jax.sharding import PartitionSpec as P

D = 1280
HEAD_DIM = 80
EPS = 1e-06
QUERY_CONST = 1.442695041
MASKED = -1e30
BF = jnp.bfloat16
F32 = jnp.float32
VMEM_LIMIT = 24 * 1024 * 1024
CHEAP = pl.CostEstimate(flops=1, bytes_accessed=1, transcendentals=0)


def size(axis):
    return lax.axis_size(axis)


def swap(x, axis):
    return lax.ppermute(x, axis, [(0, 1), (1, 0)])


def flip(blocks, axis):
    if size(axis) != 2:
        return list(blocks)
    first = lax.axis_index(axis) == 0
    a, b = blocks
    return [jnp.where(first, a, b), jnp.where(first, b, a)]


def flip_dim(x, axis, dim):
    if size(axis) != 2:
        return x
    return jnp.concatenate(flip(jnp.split(x, 2, axis=dim), axis), axis=dim)


def gather(x, axis):
    if size(axis) == 2:
        return [x, swap(x, axis)]
    whole = lax.all_gather(x, axis, axis=0, tiled=False)
    return [whole[i] for i in range(size(axis))]


def gather_grid(x):
    if size("row") != 2:
        return [gather(b, "col") for b in gather(x, "row")]
    along_row, along_col = swap(x, "row"), swap(x, "col")
    half = x.shape[0] // 2
    across = jnp.concatenate(
        [swap(along_row[:half], "col"), swap(along_col[half:], "row")], axis=0
    )
    return [[x, along_col], [along_row, across]]


def scatter_sum(x, axis, dim):
    if size(axis) != 2:
        return lax.psum_scatter(x, axis, scatter_dimension=dim, tiled=True)
    mine, theirs = jnp.split(x, 2, axis=dim)
    return (mine.astype(F32) + swap(theirs, axis).astype(F32)).astype(x.dtype)


def exchange(x, axis, split, join):
    if size(axis) != 2:
        return lax.all_to_all(x, axis, split, join, tiled=True)
    mine, theirs = jnp.split(x, 2, axis=split)
    return jnp.concatenate([mine, swap(theirs, axis)], axis=join)


def core_half(x, dim):
    return lax.dynamic_slice_in_dim(
        x, lax.axis_index("core") * (x.shape[dim] // 2), x.shape[dim] // 2, dim
    )


def weight_gather(w, row_dim):
    part = core_half(w, 0)
    blocks = gather_grid(part)
    if row_dim == 1:
        blocks = [list(b) for b in zip(*blocks)]
    mine = jnp.stack([jnp.concatenate(b, axis=1) for b in blocks])
    other = swap(mine, "core")
    first = lax.axis_index("core") == 0
    both = jnp.stack([jnp.where(first, mine, other), jnp.where(first, other, mine)], axis=1)
    return both.reshape(-1, both.shape[-1])


def weight_sum(g, row_dim):
    dim_axis = ("row", "col") if row_dim == 0 else ("col", "row")
    n0 = size(dim_axis[0])
    g = g.reshape(n0, 2, g.shape[0] // n0 // 2, g.shape[1])
    core = lax.axis_index("core")
    keep = lax.dynamic_index_in_dim(g, core, 1, keepdims=False)
    give = lax.dynamic_index_in_dim(g, 1 - core, 1, keepdims=False).astype(BF)
    part = (keep + swap(give, "core").astype(F32)).astype(BF)
    part = scatter_sum(part, dim_axis[0], 0)
    part = scatter_sum(part[0], dim_axis[1], 1)
    return z_sum(part)


def z_sum(part):
    total = lax.psum(part, "z")
    other = swap(total, "core")
    return flip_core(total, other)


def flip_core(total, other):
    first = lax.axis_index("core") == 0
    return jnp.concatenate(
        [jnp.where(first, total, other), jnp.where(first, other, total)], axis=-2
    ).astype(F32)


def dot(a, b, contract):
    return lax.dot_general(a, b, ((contract[0:1], contract[1:2]), ((), ())), preferred_element_type=F32)


def bias_block(series_row, series_col, key_pos, q0, k0, qb, kb, diagonal):
    q_pos = q0 + lax.broadcasted_iota(jnp.int32, (1, qb), 1)
    allowed = (series_col == series_row) & (key_pos <= q_pos)
    if diagonal:
        k_pos = k0 + lax.broadcasted_iota(jnp.int32, (kb, 1), 0)
        allowed = allowed | (k_pos == q_pos)
    return jnp.where(allowed, 0.0, MASKED)


def forward_kernel(block, at, qkv_ref, srow_ref, scol_ref, kpos_ref, out_ref, lse_ref, *rest):
    *pieces, bias_ref, krow_ref, s_ref, slot_ref = rest
    t = qkv_ref.shape[3]
    n = t // block
    krow_ref[...] = qkv_ref[1, 0].astype(F32).T.astype(BF)

    def bias_slot(j, i):
        return j * (j + 1) // 2 + i

    @pl.when(pl.program_id(0) == 0)
    def _():
        for j in range(n):
            for i in range(j + 1):
                keys = pl.ds(i * block, block)
                bias_ref[bias_slot(j, i)] = bias_block(
                    srow_ref[:, j * block : (j + 1) * block],
                    scol_ref[keys, :],
                    kpos_ref[keys, :],
                    j * block,
                    i * block,
                    block,
                    block,
                    i == j,
                )

    for j in range(n):
        cols = slice(j * block, (j + 1) * block)
        q = qkv_ref[0, 0, :, cols]
        top = None
        for i in range(j + 1):
            s = dot(krow_ref[i * block : (i + 1) * block, :], q, (1, 0)) + bias_ref[bias_slot(j, i)]
            s_ref[i * block : (i + 1) * block, :] = s
            here = jnp.max(s, axis=0, keepdims=True)
            top = here if top is None else jnp.maximum(top, here)
        total = jnp.zeros((1, block), F32)
        acc = jnp.zeros((HEAD_DIM, block), F32)
        for i in range(j + 1):
            p = jnp.exp(s_ref[i * block : (i + 1) * block, :] - top)
            total += jnp.sum(p, axis=0, keepdims=True)
            acc += dot(qkv_ref[2, 0, :, i * block : (i + 1) * block], p.astype(BF), (1, 0))
        found = (acc / total).astype(BF)
        out_ref[0, :, cols] = found
        if pieces:
            slot_ref[j ^ at[3]] = found
        lse_ref[0, :, cols] = top + jnp.log(total)
    for slot, piece in enumerate(pieces):
        piece[0] = slot_ref[slot]


def backward_kernel(
    block, at, qkv_ref, raw_ref, factor_ref, out_ref, lse_ref, srow_ref, scol_ref, kpos_ref, *rest
):
    *pieces, grad_ref, gscale_ref, bias_ref, krow_ref, vrow_ref, gk_ref, gv_ref, gout_ref = rest
    if len(pieces) == 1:
        gout_ref[...] = pieces[0][0]
    else:
        for slot, piece in enumerate(pieces):
            wide = piece.shape[2]
            gout_ref[:, pl.ds(pl.multiple_of((slot ^ at[3]) * wide, 128), wide)] = piece[0]
    t = qkv_ref.shape[3]
    n = t // block
    krow_ref[...] = qkv_ref[1, 0].astype(F32).T.astype(BF)
    vrow_ref[...] = qkv_ref[2, 0].astype(F32).T.astype(BF)

    def bias_slot(j, i):
        return j * (j + 1) // 2 + i

    @pl.when(pl.program_id(0) == 0)
    def _():
        for j in range(n):
            for i in range(j + 1):
                keys = pl.ds(i * block, block)
                bias_ref[bias_slot(j, i)] = bias_block(
                    srow_ref[:, j * block : (j + 1) * block],
                    scol_ref[keys, :],
                    kpos_ref[keys, :],
                    j * block,
                    i * block,
                    block,
                    block,
                    i == j,
                )

    gscale = jnp.zeros((HEAD_DIM, 1), F32)
    for j in range(n):
        cols = slice(j * block, (j + 1) * block)
        q = qkv_ref[0, 0, :, cols]
        go = gout_ref[:, cols]
        lse = lse_ref[0, :, cols]
        delta = jnp.sum(go.astype(F32) * out_ref[0, :, cols].astype(F32), axis=0, keepdims=True)
        gq = jnp.zeros((HEAD_DIM, block), F32)
        for i in range(j + 1):
            keys = slice(i * block, (i + 1) * block)
            s = dot(krow_ref[keys, :], q, (1, 0)) + bias_ref[bias_slot(j, i)]
            p = jnp.exp(s - lse)
            gp = dot(vrow_ref[keys, :], go, (1, 0))
            gs = (p * (gp - delta)).astype(BF)
            gq += dot(qkv_ref[1, 0, :, keys], gs, (1, 0))
            gk = dot(q, gs, (1, 1))
            gv = dot(go, p.astype(BF), (1, 1))
            if i == j:
                gk_ref[:, keys] = gk
                gv_ref[:, keys] = gv
            else:
                gk_ref[:, keys] += gk
                gv_ref[:, keys] += gv
        gscale += jnp.sum(gq * raw_ref[0, :, cols], axis=1, keepdims=True)
        grad_ref[0, 0, :, cols] = (gq * factor_ref[...]).astype(BF)
    grad_ref[1, 0] = gk_ref[...].astype(BF)
    grad_ref[2, 0] = gv_ref[...].astype(BF)
    gscale_ref[0] = gscale


def mask_args(series, padding):
    t = series.shape[0]
    pos = jnp.arange(t, dtype=jnp.int32)
    return series.reshape(1, t), series.reshape(t, 1), jnp.where(padding == 0, pos, t).reshape(t, 1)


def attention_forward(at, qkv, masks, pieces=0):
    _, heads, hd, t = qkv.shape
    block = min(256, t) if t <= 2048 else 512
    n = t // block
    whole = lambda shape: pl.BlockSpec(shape, lambda h: (0,) * len(shape))
    assert pieces in (0, n)
    return pl.pallas_call(
        functools.partial(forward_kernel, block),
        grid=(heads,),
        in_specs=[
            pl.BlockSpec(memory_space=pltpu.SMEM),
            pl.BlockSpec((3, 1, hd, t), lambda h: (0, h, 0, 0)),
            whole((1, t)),
            whole((t, 1)),
            whole((t, 1)),
        ],
        out_specs=[
            pl.BlockSpec((1, hd, t), lambda h: (h, 0, 0)),
            pl.BlockSpec((1, 1, t), lambda h: (h, 0, 0)),
        ]
        + [pl.BlockSpec((1, hd, block), lambda h: (h, 0, 0))] * pieces,
        out_shape=[
            jax.ShapeDtypeStruct((heads, hd, t), BF),
            jax.ShapeDtypeStruct((heads, 1, t), F32),
        ]
        + [jax.ShapeDtypeStruct((heads, hd, block), BF)] * pieces,
        scratch_shapes=[
            pltpu.VMEM((n * (n + 1) // 2, block, block), F32),
            pltpu.VMEM((t, hd), BF),
            pltpu.VMEM((t, block), F32),
            pltpu.VMEM((n, hd, block), BF),
        ],
        compiler_params=pltpu.CompilerParams(vmem_limit_bytes=VMEM_LIMIT),
        cost_estimate=CHEAP,
        name="attention_forward",
    )(at, qkv, *masks)


def attention_backward(at, qkv, raw, factor, out, pieces, lse, masks, begin=0, heads=None):
    _, all_heads, hd, t = qkv.shape
    heads = heads or all_heads
    block = min(256, t) if t <= 2048 else 512
    n = t // block
    whole = lambda shape: pl.BlockSpec(shape, lambda h: (0,) * len(shape))
    head = lambda wide=t: pl.BlockSpec((1, hd, wide), lambda h: (begin + h, 0, 0))
    return pl.pallas_call(
        functools.partial(backward_kernel, block),
        grid=(heads,),
        in_specs=[
            pl.BlockSpec(memory_space=pltpu.SMEM),
            pl.BlockSpec((3, 1, hd, t), lambda h: (0, begin + h, 0, 0)),
            head(),
            whole((hd, 1)),
            head(),
            pl.BlockSpec((1, 1, t), lambda h: (begin + h, 0, 0)),
            whole((1, t)),
            whole((t, 1)),
            whole((t, 1)),
        ]
        + [head(p.shape[2]) for p in pieces],
        out_specs=[
            pl.BlockSpec((3, 1, hd, t), lambda h: (0, h, 0, 0)),
            pl.BlockSpec((1, hd, 1), lambda h: (h, 0, 0)),
        ],
        out_shape=[
            jax.ShapeDtypeStruct((3, heads, hd, t), BF),
            jax.ShapeDtypeStruct((heads, hd, 1), F32),
        ],
        scratch_shapes=[
            pltpu.VMEM((n * (n + 1) // 2, block, block), F32),
            pltpu.VMEM((t, hd), BF),
            pltpu.VMEM((t, hd), BF),
            pltpu.VMEM((hd, t), F32),
            pltpu.VMEM((hd, t), F32),
            pltpu.VMEM((hd, t), BF),
        ],
        compiler_params=pltpu.CompilerParams(vmem_limit_bytes=VMEM_LIMIT),
        cost_estimate=CHEAP,
        name="attention_backward",
    )(at, qkv, raw, factor, out, lse, *masks, *pieces)


def norm_scale(x):
    return lax.rsqrt(jnp.mean(x * x, axis=1, keepdims=True) + EPS)


def body_any(
    inputs, gain_attn, w_qkv, query_scale, w_out, gain_mlp, w_up, b_up, w_down, b_down, series_ids, pad_mask, cotangent
):
    rows, cols = size("row"), size("col")
    tok = inputs.shape[0]
    feat = inputs.shape[1]
    share = tok // cols
    t = series_ids.shape[0]
    head_rows = w_qkv.shape[2] // cols
    heads = head_rows // HEAD_DIM
    r, c = lax.axis_index("row"), lax.axis_index("col")

    blocks = gather_grid(inputs)
    strips = [jnp.concatenate(b, axis=1) for b in blocks]
    x_own = strips[0] if rows == 2 else lax.dynamic_index_in_dim(jnp.stack(strips), r, 0, keepdims=False)
    x_all = jnp.concatenate(flip(strips, "row"), axis=0)
    gain_one = jnp.concatenate(gather(gain_attn, "col"))
    gain_two = jnp.concatenate(gather(gain_mlp, "col"))
    bias_up = jnp.concatenate(gather(b_up, "row")).astype(F32)
    bias_down = jnp.concatenate(gather(b_down, "col")).astype(F32)

    w3 = jnp.transpose(w_qkv, (1, 0, 2)).reshape(3, feat, cols, head_rows)
    w_mine = lax.dynamic_index_in_dim(w3, c, 2, keepdims=False)
    w_give = lax.dynamic_index_in_dim(w3, 1 - c, 2, keepdims=False)
    w_half = swap(core_half(w_give, 1), "col")
    w_other = swap(w_half, "core")
    first = lax.axis_index("core") == 0
    w_full = jnp.concatenate(
        [w_mine, jnp.where(first, w_half, w_other), jnp.where(first, w_other, w_half)], axis=1
    )

    xf = x_all.astype(F32)
    scale_one = norm_scale(xf)
    normed_one = (xf * scale_one * gain_one).astype(BF)
    projected = jnp.einsum("td,sdh->sht", normed_one, w_full, preferred_element_type=F32)
    projected = projected.reshape(3, heads, HEAD_DIM, t)
    factor = QUERY_CONST / math.sqrt(HEAD_DIM) * jax.nn.softplus(query_scale)
    raw_q = projected[0]
    qkv = jnp.stack([raw_q * factor[None, :, None], projected[1], projected[2]]).astype(BF)
    masks = mask_args(series_ids, pad_mask)
    at = jnp.zeros((4,), jnp.int32)
    attended, lse = attention_forward(at, qkv, masks)

    def to_tokens(y):
        y = flip_dim(y.reshape(head_rows, rows, cols, share), "row", 1)
        y = flip_dim(y, "col", 2)
        y = exchange(y.reshape(1, head_rows, rows, cols, share), "row", 2, 0)
        y = exchange(y.reshape(rows, 1, head_rows, cols, share), "col", 3, 1)
        y = flip_dim(y.reshape(rows, cols, head_rows, share), "col", 1)
        return y.reshape(rows * cols * head_rows, share)

    def to_heads(y):
        y = flip_dim(y.reshape(rows, cols, head_rows, share), "col", 1)
        y = exchange(y.reshape(rows, cols, head_rows, 1, share), "col", 1, 3)
        y = exchange(y.reshape(rows, head_rows, 1, cols, share), "row", 0, 2)
        y = flip_dim(y.reshape(head_rows, rows, cols, share), "col", 2)
        return flip_dim(y, "row", 1).reshape(head_rows, t)

    w_out_all = weight_gather(w_out, 0)
    w_up_all = weight_gather(w_up, 1)
    w_down_all = weight_gather(w_down, 0)

    def my_share(y):
        return lax.dynamic_slice_in_dim(y, c * share, share, 0)

    att = to_tokens(attended.reshape(head_rows, t))
    x_mine = my_share(x_own).astype(F32)
    middle = x_mine + dot(att, w_out_all, (0, 0))
    scale_two = norm_scale(middle)
    normed_two = (middle * scale_two * gain_two).astype(BF)
    pre_act = dot(normed_two, w_up_all, (1, 0)) + bias_up
    sig = jax.nn.sigmoid(pre_act)
    hidden = (pre_act * sig).astype(BF)
    result = (middle + dot(hidden, w_down_all, (1, 0)) + bias_down).astype(BF)

    def to_block(y):
        mine, theirs = jnp.split(y, 2, axis=1)
        return jnp.concatenate(flip([mine, swap(theirs, "col")], "col"), axis=0)

    layer_out = to_block(result)

    g_give = lax.dynamic_slice_in_dim(cotangent, (1 - c) * share, share, 0)
    g = jnp.concatenate([my_share(cotangent), swap(g_give, "col")], axis=1)
    grad_w_down = dot(hidden, g, (0, 0))
    grad_hidden = dot(g, w_down_all, (1, 1))
    grad_pre_f = grad_hidden * sig * (1.0 + pre_act * (1.0 - sig))
    grad_pre = grad_pre_f.astype(BF)
    grad_b_up = jnp.sum(grad_pre.astype(F32), axis=0)
    grad_w_up = dot(normed_two, grad_pre, (0, 0))
    grad_normed_two = dot(grad_pre, w_up_all, (1, 1))
    weighted = grad_normed_two * gain_two
    inner = jnp.sum(weighted * middle, axis=1, keepdims=True)
    grad_middle = g.astype(F32) + scale_two * weighted - middle * (scale_two**3 * inner / D)
    grad_gain_mlp = jnp.sum(grad_normed_two * middle * scale_two, axis=0)
    grad_branch = grad_middle.astype(BF)
    grad_w_out = dot(att, grad_branch, (1, 0))
    grad_att = dot(w_out_all, grad_branch, (1, 1)).astype(BF)
    grad_attended = to_heads(grad_att).reshape(heads, HEAD_DIM, t)
    grad_middle_block = to_block(grad_middle)

    sum_down = weight_sum(grad_w_down, 0)
    sum_up = weight_sum(grad_w_up, 1)
    sum_out = weight_sum(grad_w_out, 0)

    grad_proj, gscale = attention_backward(
        at, qkv, raw_q, factor.reshape(HEAD_DIM, 1), attended, [grad_attended], lse, masks
    )
    slope = QUERY_CONST / math.sqrt(HEAD_DIM) * jax.nn.sigmoid(query_scale)
    grad_query_scale = jnp.sum(gscale, axis=(0, 2)) * slope
    grad_proj = grad_proj.reshape(3, head_rows, t)
    grad_normed_one = jnp.einsum("sht,sdh->td", grad_proj, w_full, preferred_element_type=F32)
    weighted_one = grad_normed_one * gain_one
    inner_one = jnp.sum(weighted_one * xf, axis=1)
    grad_gain_attn = jnp.sum(grad_normed_one * xf * scale_one, axis=0)
    inner_one = lax.psum(inner_one, ("row", "col"))
    grad_w = jnp.einsum("td,sht->sdh", normed_one, grad_proj, preferred_element_type=F32)
    grad_w = grad_w.reshape(3, cols, 2, feat // 2, head_rows)
    core = lax.axis_index("core")
    keep = lax.dynamic_index_in_dim(grad_w, core, 2, keepdims=False)
    give = lax.dynamic_index_in_dim(grad_w, 1 - core, 2, keepdims=False).astype(BF)
    part = (keep + swap(give, "core").astype(F32)).astype(BF)
    part = jnp.concatenate(flip([part[:, 0], swap(part[:, 1], "col")], "col"), axis=2)
    sum_qkv = jnp.transpose(z_sum(part), (1, 0, 2))

    e = jnp.concatenate(flip(jnp.split(grad_normed_one.astype(BF), 2, axis=0), "row"), axis=0) if rows == 2 else (
        grad_normed_one.astype(BF)
    )
    e = scatter_sum(e, "row", 0)
    e = scatter_sum(e, "col", 1).astype(F32)
    my_rows = lambda y: lax.dynamic_slice_in_dim(y, r * tok, tok, 0)
    scale_mine = my_rows(scale_one)
    inner_mine = my_rows(inner_one.reshape(t, 1))
    grad_inputs = grad_middle_block + scale_mine * (e * gain_attn) - inputs.astype(F32) * (
        scale_mine**3 * inner_mine / D
    )

    grad_b_down = jnp.sum(g.astype(F32), axis=0)
    vectors = jnp.concatenate(
        [
            flip_dim(grad_gain_attn, "col", 0),
            flip_dim(grad_gain_mlp, "col", 0),
            flip_dim(grad_b_down, "col", 0),
            flip_dim(grad_b_up, "row", 0),
            grad_query_scale,
        ]
    )
    vectors = lax.psum(vectors, ("z", "core", "row", "col"))
    mine_col = lambda at: lax.dynamic_slice_in_dim(vectors, at * D + c * feat, feat, 0)
    units = b_up.shape[0]
    return (
        layer_out,
        grad_inputs,
        mine_col(0),
        sum_qkv,
        vectors[4 * D :],
        sum_out,
        mine_col(1),
        sum_up,
        lax.dynamic_slice_in_dim(vectors, 3 * D + r * units, units, 0),
        sum_down,
        mine_col(2),
    )


SMEM = pl.BlockSpec(memory_space=pltpu.SMEM)
ANY = pl.BlockSpec(memory_space=pl.ANY)


def call(kernel, name, args, specs, outs, scratch=(), **more):
    return pl.pallas_call(
        kernel,
        in_specs=specs,
        out_shape=outs,
        scratch_shapes=list(scratch),
        compiler_params=pltpu.CompilerParams(vmem_limit_bytes=VMEM_LIMIT),
        cost_estimate=CHEAP,
        name=name,
        **more,
    )(*args)


VM = pl.BlockSpec(memory_space=pltpu.VMEM)


def shape(dims, kind):
    return jax.ShapeDtypeStruct(dims, kind)


def project_kernel(
    at, x00, x01, x10, x11, gain, factor, w_mine, w_a, w_b, qkv, raw, normed, scale_own, w_full
):
    r, k = at[0], at[2]
    tok, feat = x00.shape
    hr = w_mine.shape[1]
    half = hr // 2
    for s in range(3):
        w_full[pl.ds(s * hr, hr), 0:feat] = w_mine[s]
        w_full[pl.ds(pl.multiple_of(s * hr + k * half, 16), half), feat:] = w_a[s]
        w_full[pl.ds(pl.multiple_of(s * hr + (1 - k) * half, 16), half), feat:] = w_b[s]
    for i, (a_ref, b_ref) in enumerate(((x00, x01), (x10, x11))):
        a, b = a_ref[...].astype(F32), b_ref[...].astype(F32)
        total = jnp.sum(a * a, axis=1, keepdims=True) + jnp.sum(b * b, axis=1, keepdims=True)
        scale = lax.rsqrt(total / (2 * feat) + EPS)
        if i == 0:
            scale_own[...] = scale
        rows = pl.ds(pl.multiple_of((r ^ i) * tok, tok), tok)
        normed[rows, 0:feat] = (a * scale * gain[:, 0:feat]).astype(BF)
        normed[rows, feat:] = (b * scale * gain[:, feat:]).astype(BF)
        y = normed[rows, :]
        q = dot(w_full[0:hr, :], y, (1, 1))
        raw[:, rows] = q
        qkv[0, :, rows] = (q * factor[...]).astype(BF)
        qkv[1, :, rows] = dot(w_full[hr : 2 * hr, :], y, (1, 1)).astype(BF)
        qkv[2, :, rows] = dot(w_full[2 * hr : 3 * hr, :], y, (1, 1)).astype(BF)


def feed_kernel(
    at, a0, a1, a2, a3, x_own, x_col, g_own, g_col, gain, bias_up, bias_down,
    w_out, w_up, w_down, hx, hy, d0, d1, hx2, hy2, d02, d12,
    out_own, gm_own, post, t0, t1, t2, t3, vectors,
    *rest,
):
    *grads, w, att, turned, sems = rest
    r, c, k = at[0], at[1], at[2]
    hr, share = a0.shape
    feat = x_own.shape[1]
    half = feat // 2
    quarter = half // 2
    copies = []
    for n, shard in enumerate((w_out, w_up, w_down)):
        rx, cx, ry, cy = (0, feat, feat, 0) if n == 1 else (feat, 0, 0, feat)
        mine = []
        mine.append((shard, w.at[n, 0:feat, 0:feat]))
        for core, (px, py, p0, p1) in ((k, (hx, hy, d0, d1)), (1 - k, (hx2, hy2, d02, d12))):
            down = core * half
            at_x = pl.ds(pl.multiple_of(rx + down, 16), half)
            at_y = pl.ds(pl.multiple_of(ry + down, 16), half)
            first = d0.shape[1]
            at_0 = pl.ds(pl.multiple_of(feat + down, 16), first)
            at_1 = pl.ds(pl.multiple_of(feat + down + first, 16), half - first)
            mine.append((px.at[n], w.at[n, at_x, cx : cx + feat]))
            mine.append((py.at[n], w.at[n, at_y, cy : cy + feat]))
            mine.append((p0.at[n], w.at[n, at_0, feat : 2 * feat]))
            mine.append((p1.at[n], w.at[n, at_1, feat : 2 * feat]))
        started = []
        for m, (src, dst) in enumerate(mine):
            copy = pltpu.make_async_copy(src, dst, sems.at[n, m])
            copy.start()
            started.append(copy)
        copies.append(started)

    rows = pl.ds(pl.multiple_of(c * share, share), share)
    for s, a in enumerate((a0, a1, a2, a3)):
        to = (s // 2) * 2 * hr + (c ^ (s % 2)) * hr
        att[pl.ds(pl.multiple_of(to, 16), hr), :] = a[...]
    x = jnp.concatenate([x_own[rows, :], x_col[rows, :]], axis=1).astype(F32)
    g = jnp.concatenate([g_own[rows, :], g_col[...]], axis=1)
    for copy in copies[0]:
        copy.wait()
    middle = x + dot(att[...], w[0], (0, 0))
    scale = lax.rsqrt(jnp.sum(middle * middle, axis=1, keepdims=True) / D + EPS)
    normed = (middle * scale * gain[...]).astype(BF)
    for copy in copies[1]:
        copy.wait()
    pre = dot(normed, w[1], (1, 0)) + bias_up[...]
    sig = jax.nn.sigmoid(pre)
    hidden = (pre * sig).astype(BF)
    for copy in copies[2]:
        copy.wait()
    result = (middle + dot(hidden, w[2], (1, 0)) + bias_down[...]).astype(BF)
    out_own[...] = result[:, :feat]
    post[0] = result[:, feat:]

    def weight_grad(n, left_ref, right):
        for core, sets in ((k, grads[:8]), (1 - k, grads[8:])):
            by_row, by_col = sets[:4], sets[4:]
            up, low = (by_col, by_row) if n == 1 else (by_row, by_col)
            for b in range(2):
                part = pl.ds(pl.multiple_of(b * feat + core * half, 16), half)
                y = dot(left_ref[part, :], right, (1, 0)).astype(BF)
                for j in range(2):
                    cut = slice(j * feat, (j + 1) * feat)
                    up[2 * j + (1 - b)][n] = y[:quarter, cut]
                    low[2 * b + (1 - j)][n] = y[quarter:, cut]

    turned[...] = hidden.astype(F32).T.astype(BF)
    grad_pre_f = dot(g, w[2], (1, 1)) * sig * (1.0 + pre * (1.0 - sig))
    grad_pre = grad_pre_f.astype(BF)
    weight_grad(2, turned, g)
    grad_normed = dot(grad_pre, w[1], (1, 1))
    weighted = grad_normed * gain[...]
    inner = jnp.sum(weighted * middle, axis=1, keepdims=True)
    gf = g.astype(F32)
    grad_middle = gf + scale * weighted - middle * (scale * scale * scale * inner / D)
    gm_own[...] = grad_middle[:, :feat]
    post[1] = grad_middle[:, feat:].astype(BF)
    branch = grad_middle.astype(BF)
    for s, t in enumerate((t0, t1, t2, t3)):
        come = (s // 2) * 2 * hr + (c ^ (s % 2)) * hr
        t[...] = dot(w[0, pl.ds(pl.multiple_of(come, 16), hr), :], branch, (1, 1)).astype(BF)
    turned[...] = normed.astype(F32).T.astype(BF)
    weight_grad(1, turned, grad_pre)
    weight_grad(0, att, branch)
    vectors[...] = jnp.concatenate(
        [
            jnp.sum(grad_normed * (middle * scale), axis=0, keepdims=True),
            jnp.sum(gf, axis=0, keepdims=True),
            jnp.sum(grad_pre.astype(F32), axis=0, keepdims=True),
        ],
        axis=0,
    )


def weight_back_kernel(at, grad, normed, keep, give):
    k = at[2]
    part = keep.shape[2]
    feat = keep.shape[3]
    for ref, core in ((give, 1 - k), (keep, k)):
        for s in range(3):
            rows = pl.ds(pl.multiple_of(core * part, 16), part)
            y = dot(grad[s, rows, :], normed[...], (1, 0)).astype(BF)
            ref[0, s] = y[:, :feat]
            ref[1, s] = y[:, feat:]


def project_back_kernel(
    at, grad, w_full, x00, x01, x10, x11, gain, e0, e1, e2, e3, inner_own, gain_sum
):
    r = at[0]
    tok, feat = x00.shape
    sums = [jnp.zeros((1, feat), F32), jnp.zeros((1, feat), F32)]
    for i, (xs, es) in enumerate((((x00, x01), (e0, e1)), ((x10, x11), (e2, e3)))):
        rows = pl.ds(pl.multiple_of((r ^ i) * tok, tok), tok)
        left = grad[:, rows]
        products, squares, inner = [], 0.0, 0.0
        for j in range(2):
            cut = slice(j * feat, (j + 1) * feat)
            e = dot(left, w_full[:, cut], (0, 0))
            x = xs[j][...].astype(F32)
            product = e * x
            inner = inner + jnp.sum(product * gain[:, cut], axis=1, keepdims=True)
            squares = squares + jnp.sum(x * x, axis=1, keepdims=True)
            es[j][0:tok, :] = e.astype(es[j].dtype)
            products.append(product)
        scale = lax.rsqrt(squares / (2 * feat) + EPS)
        for j in range(2):
            sums[j] += jnp.sum(products[j] * scale, axis=0, keepdims=True)
        line = jnp.broadcast_to(inner, (tok, 128)).T[0:1, :]
        high = line.astype(BF).astype(F32)
        extra = jnp.concatenate([high, line - high, jnp.zeros((14, tok), F32)], axis=0)
        extra = jnp.concatenate([extra, jnp.zeros((16, feat - tok), F32)], axis=1).astype(BF)
        if i == 0:
            inner_own[...] = inner
            es[1][tok:, :] = extra
        else:
            es[0][tok:, :] = extra
            es[1][tok:, :] = extra
    gain_sum[:, 0:feat] = sums[0]
    gain_sum[:, feat:] = sums[1]


def finish_qkv_kernel(at, mine, theirs, mine2, theirs2, out, rows):
    c, k = at[1], at[2]
    half = mine.shape[1]
    for s in range(3):
        for ref, col, core in ((mine, c, k), (theirs, 1 - c, k), (mine2, c, 1 - k), (theirs2, 1 - c, 1 - k)):
            rows[pl.ds(pl.multiple_of((2 * col + core) * half, 16), half), :] = ref[s].astype(F32)
        out[s] = rows[...].T


def finish_feed_kernel(at, a, b, a2, b2, *outs):
    k = at[2]
    quarter = a.shape[1]
    for n, out in enumerate(outs):
        upper, lower = ((b, b2), (a, a2)) if n == 1 else ((a, a2), (b, b2))
        for i, core in ((0, k), (1, 1 - k)):
            for j, refs in enumerate((upper, lower)):
                to = pl.multiple_of((2 * core + j) * quarter, 16)
                out[pl.ds(to, quarter), :] = refs[i][n].astype(F32)


together = lax.optimization_barrier


def after(x, *earlier):
    return lax.optimization_barrier((x, *earlier))[0]


def add(*parts):
    total = parts[0].astype(F32)
    for part in parts[1:]:
        total = total + part.astype(F32)
    return total.astype(BF)


def diagonal(x):
    return lax.ppermute(x, ("row", "col"), [(0, 3), (1, 2), (2, 1), (3, 0)])


def z_swap(x, step):
    n = size("z")
    return lax.ppermute(x, "z", [(i, i ^ step) for i in range(n)])


def z_first():
    z = lax.axis_index("z")
    return (z == 0) | (z == 3)


def body_four(
    inputs, gain_attn, w_qkv, query_scale, w_out, gain_mlp, w_up, b_up, w_down, b_down, series_ids, pad_mask, cotangent
):
    tok, feat = inputs.shape
    share = tok // 2
    t = series_ids.shape[0]
    hr = w_qkv.shape[2] // 2
    heads = hr // HEAD_DIM
    half = feat // 2
    r, c, k = lax.axis_index("row"), lax.axis_index("col"), lax.axis_index("core")
    at = jnp.stack([r, c, k, 2 * r + c]).astype(jnp.int32)
    mine_rows = lambda y, part: lax.dynamic_slice_in_dim(y, part * share, share, 0)

    few = heads // 2
    quarter = half // 2
    first_rows = (half * 7 // 20) // 16 * 16
    x01 = swap(inputs, "col")
    x10 = swap(inputs, "row")
    small = swap(jnp.concatenate([gain_attn, gain_mlp, b_down.astype(F32)]), "col")
    up_other = swap(b_up.astype(F32), "row")
    w_turned = jnp.transpose(w_qkv, (1, 2, 0)).reshape(3, 2, hr, feat)
    w_mine = lax.dynamic_index_in_dim(w_turned, c, 1, keepdims=False)
    w_give = lax.dynamic_index_in_dim(w_turned, 1 - c, 1, keepdims=False)
    w_half = core_half(w_give, 1)
    w_a = swap(w_half, "col")
    part = jnp.stack([core_half(w_out, 0), core_half(w_up, 0), core_half(w_down, 0)])
    g_give = mine_rows(cotangent, 1 - c)
    x01, x10, small, up_other, part, g_give, w_mine = lax.optimization_barrier(
        (x01, x10, small, up_other, part, g_give, w_mine)
    )
    x11 = swap(after(x01, w_half), "row")
    w_b = swap(w_a, "core")
    gain_one = jnp.concatenate([gain_attn, small[:feat]]).reshape(1, D)
    gain_two = jnp.concatenate([gain_mlp, small[feat : 2 * feat]]).reshape(1, D)
    bias_down = jnp.concatenate([b_down.astype(F32), small[2 * feat :]]).reshape(1, D)
    bias_up = jnp.concatenate([b_up.astype(F32), up_other]).reshape(1, D)
    factor = QUERY_CONST / math.sqrt(HEAD_DIM) * jax.nn.softplus(query_scale)
    factor_col = factor.reshape(HEAD_DIM, 1)

    part = after(part, x11, w_a)
    hx, hy = swap(part, "row"), swap(part, "col")
    hx2, hy2 = swap(hx, "core"), swap(hy, "core")
    qkv, raw, normed_one, scale_own, w_full = call(
        project_kernel,
        "project",
        (at, inputs, x01, x10, x11, gain_one, jnp.tile(factor_col, (heads, 1)), w_mine, w_a, w_b),
        [SMEM] + [VM] * 9,
        [
            shape((3, hr, t), BF),
            shape((hr, t), F32),
            shape((t, D), BF),
            shape((tok, 1), F32),
            shape((3 * hr, D), BF),
        ],
    )
    qkv = qkv.reshape(3, heads, HEAD_DIM, t)
    masks = mask_args(series_ids, pad_mask)
    attended, lse, *a = attention_forward(at, qkv, masks, pieces=4)
    a0, a1, a2, a3 = [p.reshape(hr, share) for p in a]
    a1, a2, a3 = swap(a1, "col"), swap(a2, "row"), diagonal(a3)
    hx_on, hy_on, g_give, a1, a2, a3 = lax.optimization_barrier((hx, hy, g_give, a1, a2, a3))
    d0 = swap(hx_on[:, :first_rows], "col")
    d1 = swap(hy_on[:, first_rows:], "row")
    g_col = swap(g_give, "col")
    d0, d1, g_col = lax.optimization_barrier((d0, d1, g_col))
    d02, d12 = swap(d0, "core"), swap(d1, "core")
    out_own, gm_own, post, t0, t1, t2, t3, vectors, *grads = call(
        feed_kernel,
        "feed_forward",
        (at, a0, a1, a2, a3, inputs, x01, cotangent, g_col, gain_two, bias_up, bias_down)
        + (w_out, w_up, w_down, hx, hy, d0, d1, hx2, hy2, d02, d12),
        [SMEM] + [VM] * 11 + [ANY] * 11,
        [
            shape((share, feat), BF),
            shape((share, feat), F32),
            shape((2, share, feat), BF),
        ]
        + [shape((hr, share), BF)] * 4
        + [shape((3, D), F32)]
        + [shape((3, quarter, feat), BF)] * 16,
        scratch=[
            pltpu.VMEM((3, D, D), BF),
            pltpu.VMEM((D, share), BF),
            pltpu.VMEM((D, share), BF),
            pltpu.SemaphoreType.DMA((3, 9)),
        ],
    )
    t1, t2, t3 = swap(t1, "col"), swap(t2, "row"), diagonal(t3)
    (sx0, kx0, sx1, kx1, sy0, ky0, sy1, ky1), others = grads[:8], grads[8:]
    over = lambda n: swap(others[n], "core")
    sx1, sy1 = add(sx1, over(2)), add(sy1, over(6))
    sx0, sy0 = add(sx0, over(0)), add(sy0, over(4))
    ox0, ox1, oy0, oy1 = over(1), over(3), over(5), over(7)
    pieces, sx1, sy1, sx0, sy0 = together(((t0, t1, t2, t3), sx1, sy1, sx0, sy0))
    rx1, ry1 = swap(sx1, "row"), swap(sy1, "col")
    pieces = [p.reshape(heads, HEAD_DIM, share) for p in pieces]
    raw = raw.reshape(heads, HEAD_DIM, t)

    grad_proj, gscale = attention_backward(at, qkv, raw, factor_col, attended, pieces, lse, masks)
    grad_proj = grad_proj.reshape(3, hr, t)
    kept, sent = call(
        weight_back_kernel,
        "weight_back",
        (at, grad_proj, normed_one),
        [SMEM] + [VM] * 2,
        [shape((2, 3, hr // 2, feat), BF)] * 2,
    )
    sent, rx1, ry1, sx0, sy0, ox0, ox1, oy0, oy1 = together((sent, rx1, ry1, sx0, sy0, ox0, ox1, oy0, oy1))
    got = swap(sent, "core")
    px1, py1 = add(kx1, ox1, rx1), add(ky1, oy1, ry1)
    qx, qy = swap(px1, "col"), swap(py1, "row")
    rx0, ry0 = swap(sx0, "row"), swap(sy0, "col")
    w_pair = add(kept, got)
    first = z_first()
    got_w = z_swap(jnp.where(first, w_pair[1], w_pair[0]), 1)
    slope = QUERY_CONST / math.sqrt(HEAD_DIM) * jax.nn.sigmoid(query_scale)
    grad_query_scale = jnp.sum(gscale, axis=(0, 2)) * slope
    e0, e1, e2, e3, inner, gain_sum = call(
        project_back_kernel,
        "project_back",
        (at, after(grad_proj, w_pair, px1, py1).reshape(3 * hr, t), w_full, inputs, x01, x10, x11, gain_one),
        [SMEM] + [VM] * 7,
        [
            shape((tok, feat), F32),
            shape((tok + 16, feat), BF),
            shape((tok + 16, feat), BF),
            shape((tok + 16, feat), BF),
            shape((tok, 1), F32),
            shape((1, D), F32),
        ],
    )
    got_w, w_pair, qx, qy, rx0, ry0, e1, e2, e3 = together((got_w, w_pair, qx, qy, rx0, ry0, e1, e2, e3))

    mine_w = add(jnp.where(first, w_pair[0], w_pair[1]), got_w)
    met_w = z_swap(mine_w, 3)
    fx, fy = add(kx0, ox0, rx0, qx), add(ky0, oy0, ry0, qy)
    got_c = z_swap(jnp.where(first, fy, fx), 1)
    e1, e2, e3 = swap(e1, "col"), swap(e2, "row"), diagonal(e3)
    met_w, mine_w, got_c, fx, fy, e1, e2, e3, post, gain_sum = together(
        (met_w, mine_w, got_c, fx, fy, e1, e2, e3, post, gain_sum)
    )

    mine_w = add(mine_w, met_w)
    other_w = z_swap(mine_w, 1)
    w_own, w_theirs = jnp.where(first, mine_w, other_w), jnp.where(first, other_w, mine_w)
    mine_c = add(jnp.where(first, fx, fy), got_c)
    met_c = z_swap(mine_c, 3)
    post = swap(post, "col")
    w_theirs = swap(w_theirs, "col")
    met_c, mine_c, w_own, w_theirs, post = together((met_c, mine_c, w_own, w_theirs, post))
    mine_c = add(mine_c, met_c)
    other_c = z_swap(mine_c, 1)
    w_args = (at, w_own, w_theirs, swap(w_own, "core"), swap(w_theirs, "core"))
    sum_qkv = call(
        finish_qkv_kernel,
        "finish_qkv",
        w_args,
        [SMEM] + [VM] * 4,
        shape((3, feat, 2 * hr), F32),
        scratch=[pltpu.VMEM((2 * hr, feat), F32)],
    )
    sum_qkv = jnp.transpose(sum_qkv, (1, 0, 2))

    e = e0
    for more in (e1, e2, e3):
        e = e + more[:tok].astype(F32)
        inner = inner + jnp.sum(more[tok : tok + 2, :tok].astype(F32), axis=0).reshape(tok, 1)
    grad_middle = jnp.concatenate(flip([gm_own, post[1].astype(F32)], "col"), axis=0)
    grad_inputs = grad_middle + scale_own * (e * gain_attn) - inputs.astype(F32) * (scale_own**3 * inner / D)
    layer_out = jnp.concatenate(flip([out_own, post[0]], "col"), axis=0)

    total = jnp.concatenate([gain_sum, vectors]).reshape(4, 2, feat)
    turn = jnp.stack([c, c, c, r]).reshape(4, 1, 1) == 1
    total = jnp.where(turn, total[:, ::-1], total).reshape(8, feat)
    total = jnp.concatenate([total, jnp.pad(grad_query_scale, (0, feat - HEAD_DIM)).reshape(1, feat)])
    total = total + swap(total, "core")
    total = (total + swap(total, "row")) + (swap(total, "col") + diagonal(total))
    total = after(total, w_theirs)
    total = (total + z_swap(total, 1)) + (z_swap(total, 2) + z_swap(total, 3))
    pick = lambda n, place: lax.dynamic_index_in_dim(total, 2 * n + place, 0, keepdims=False)
    mine_c = after(mine_c, sum_qkv, grad_inputs, layer_out, total)
    fx, fy = jnp.where(first, mine_c, other_c), jnp.where(first, other_c, mine_c)
    sum_out, sum_up, sum_down = call(
        finish_feed_kernel,
        "finish_feed",
        (at, fx, fy, swap(fx, "core"), swap(fy, "core")),
        [SMEM] + [VM] * 4,
        [shape((feat, feat), F32)] * 3,
    )

    return (
        layer_out,
        grad_inputs,
        pick(0, c),
        sum_qkv,
        total[8, :HEAD_DIM],
        sum_out,
        pick(1, c),
        sum_up,
        pick(3, r),
        sum_down,
        pick(2, c),
    )


def solution(mesh):
    dp, rows, cols = mesh.shape["dp"], mesh.shape["row"], mesh.shape["col"]
    split = Mesh(mesh.devices.reshape(dp // 2, 2, rows, cols), ("z", "core", "row", "col"))
    tokens = P(("z", "core", "row"), "col")
    in_specs = (
        tokens,
        P("col"),
        P("col", None, "row"),
        P(),
        P("row", "col"),
        P("col"),
        P("col", "row"),
        P("row"),
        P("row", "col"),
        P("col"),
        P(("z", "core")),
        P(("z", "core")),
        tokens,
    )
    out_specs = (
        tokens,
        tokens,
        P("col"),
        P("col", None, "row"),
        P(),
        P("row", "col"),
        P("col"),
        P("col", "row"),
        P("row"),
        P("row", "col"),
        P("col"),
    )
    body = body_four if (dp, rows, cols) == (8, 2, 2) else body_any
    return jax.shard_map(body, mesh=split, in_specs=in_specs, out_specs=out_specs, check_vma=False)
```

```python
import functools
import math

import jax
import jax.numpy as jnp
from jax import lax
from jax.experimental import pallas as pl
from jax.experimental.pallas import tpu as pltpu
from jax.sharding import Mesh
from jax.sharding import PartitionSpec as P

D = 1280
HEAD_DIM = 80
EPS = 1e-06
QUERY_CONST = 1.442695041
MASKED = -1e30
BF = jnp.bfloat16
F32 = jnp.float32
VMEM_LIMIT = 24 * 1024 * 1024
VMEM_LARGE = 50 * 1024 * 1024
CHEAP = pl.CostEstimate(flops=1, bytes_accessed=1, transcendentals=0)


def size(axis):
    return lax.axis_size(axis)


def swap(x, axis):
    return lax.ppermute(x, axis, [(0, 1), (1, 0)])


def flip(blocks, axis):
    if size(axis) != 2:
        return list(blocks)
    first = lax.axis_index(axis) == 0
    a, b = blocks
    return [jnp.where(first, a, b), jnp.where(first, b, a)]


def flip_dim(x, axis, dim):
    if size(axis) != 2:
        return x
    return jnp.concatenate(flip(jnp.split(x, 2, axis=dim), axis), axis=dim)


def gather(x, axis):
    if size(axis) == 2:
        return [x, swap(x, axis)]
    whole = lax.all_gather(x, axis, axis=0, tiled=False)
    return [whole[i] for i in range(size(axis))]


def gather_grid(x):
    if size("row") != 2:
        return [gather(b, "col") for b in gather(x, "row")]
    along_row, along_col = swap(x, "row"), swap(x, "col")
    half = x.shape[0] // 2
    across = jnp.concatenate(
        [swap(along_row[:half], "col"), swap(along_col[half:], "row")], axis=0
    )
    return [[x, along_col], [along_row, across]]


def scatter_sum(x, axis, dim):
    if size(axis) != 2:
        return lax.psum_scatter(x, axis, scatter_dimension=dim, tiled=True)
    mine, theirs = jnp.split(x, 2, axis=dim)
    return (mine.astype(F32) + swap(theirs, axis).astype(F32)).astype(x.dtype)


def exchange(x, axis, split, join):
    if size(axis) != 2:
        return lax.all_to_all(x, axis, split, join, tiled=True)
    mine, theirs = jnp.split(x, 2, axis=split)
    return jnp.concatenate([mine, swap(theirs, axis)], axis=join)


def core_half(x, dim):
    return lax.dynamic_slice_in_dim(
        x, lax.axis_index("core") * (x.shape[dim] // 2), x.shape[dim] // 2, dim
    )


def weight_gather(w, row_dim):
    part = core_half(w, 0)
    blocks = gather_grid(part)
    if row_dim == 1:
        blocks = [list(b) for b in zip(*blocks)]
    mine = jnp.stack([jnp.concatenate(b, axis=1) for b in blocks])
    other = swap(mine, "core")
    first = lax.axis_index("core") == 0
    both = jnp.stack([jnp.where(first, mine, other), jnp.where(first, other, mine)], axis=1)
    return both.reshape(-1, both.shape[-1])


def weight_sum(g, row_dim):
    dim_axis = ("row", "col") if row_dim == 0 else ("col", "row")
    n0 = size(dim_axis[0])
    g = g.reshape(n0, 2, g.shape[0] // n0 // 2, g.shape[1])
    core = lax.axis_index("core")
    keep = lax.dynamic_index_in_dim(g, core, 1, keepdims=False)
    give = lax.dynamic_index_in_dim(g, 1 - core, 1, keepdims=False).astype(BF)
    part = (keep + swap(give, "core").astype(F32)).astype(BF)
    part = scatter_sum(part, dim_axis[0], 0)
    part = scatter_sum(part[0], dim_axis[1], 1)
    return z_sum(part)


def z_sum(part):
    total = lax.psum(part, "z")
    other = swap(total, "core")
    return flip_core(total, other)


def flip_core(total, other):
    first = lax.axis_index("core") == 0
    return jnp.concatenate(
        [jnp.where(first, total, other), jnp.where(first, other, total)], axis=-2
    ).astype(F32)


def dot(a, b, contract):
    return lax.dot_general(a, b, ((contract[0:1], contract[1:2]), ((), ())), preferred_element_type=F32)


def bias_block(series_row, series_col, key_pos, q0, k0, qb, kb, diagonal):
    q_pos = q0 + lax.broadcasted_iota(jnp.int32, (1, qb), 1)
    allowed = (series_col == series_row) & (key_pos <= q_pos)
    if diagonal:
        k_pos = k0 + lax.broadcasted_iota(jnp.int32, (kb, 1), 0)
        allowed = allowed | (k_pos == q_pos)
    return jnp.where(allowed, 0.0, MASKED)


def forward_kernel(block, at, qkv_ref, srow_ref, scol_ref, kpos_ref, out_ref, lse_ref, *rest):
    *pieces, bias_ref, krow_ref, s_ref, slot_ref = rest
    t = qkv_ref.shape[3]
    n = t // block
    krow_ref[...] = qkv_ref[1, 0].astype(F32).T.astype(BF)

    def bias_slot(j, i):
        return j * (j + 1) // 2 + i

    @pl.when(pl.program_id(0) == 0)
    def _():
        for j in range(n):
            for i in range(j + 1):
                keys = pl.ds(i * block, block)
                bias_ref[bias_slot(j, i)] = bias_block(
                    srow_ref[:, j * block : (j + 1) * block],
                    scol_ref[keys, :],
                    kpos_ref[keys, :],
                    j * block,
                    i * block,
                    block,
                    block,
                    i == j,
                )

    for j in range(n):
        cols = slice(j * block, (j + 1) * block)
        q = qkv_ref[0, 0, :, cols]
        top = None
        for i in range(j + 1):
            s = dot(krow_ref[i * block : (i + 1) * block, :], q, (1, 0)) + bias_ref[bias_slot(j, i)]
            s_ref[i * block : (i + 1) * block, :] = s
            here = jnp.max(s, axis=0, keepdims=True)
            top = here if top is None else jnp.maximum(top, here)
        total = jnp.zeros((1, block), F32)
        acc = jnp.zeros((HEAD_DIM, block), F32)
        for i in range(j + 1):
            p = jnp.exp(s_ref[i * block : (i + 1) * block, :] - top)
            total += jnp.sum(p, axis=0, keepdims=True)
            acc += dot(qkv_ref[2, 0, :, i * block : (i + 1) * block], p.astype(BF), (1, 0))
        found = (acc / total).astype(BF)
        out_ref[0, :, cols] = found
        if pieces:
            slot_ref[j ^ at[3]] = found
        lse_ref[0, :, cols] = top + jnp.log(total)
    for slot, piece in enumerate(pieces):
        piece[0] = slot_ref[slot]


def backward_kernel(
    block, at, qkv_ref, raw_ref, factor_ref, out_ref, lse_ref, srow_ref, scol_ref, kpos_ref, *rest
):
    *pieces, grad_ref, gscale_ref, bias_ref, krow_ref, vrow_ref, gk_ref, gv_ref, gout_ref = rest
    if len(pieces) == 1:
        gout_ref[...] = pieces[0][0]
    else:
        for slot, piece in enumerate(pieces):
            wide = piece.shape[2]
            gout_ref[:, pl.ds(pl.multiple_of((slot ^ at[3]) * wide, 128), wide)] = piece[0]
    t = qkv_ref.shape[3]
    n = t // block
    krow_ref[...] = qkv_ref[1, 0].astype(F32).T.astype(BF)
    vrow_ref[...] = qkv_ref[2, 0].astype(F32).T.astype(BF)

    def bias_slot(j, i):
        return j * (j + 1) // 2 + i

    @pl.when(pl.program_id(0) == 0)
    def _():
        for j in range(n):
            for i in range(j + 1):
                keys = pl.ds(i * block, block)
                bias_ref[bias_slot(j, i)] = bias_block(
                    srow_ref[:, j * block : (j + 1) * block],
                    scol_ref[keys, :],
                    kpos_ref[keys, :],
                    j * block,
                    i * block,
                    block,
                    block,
                    i == j,
                )

    gscale = jnp.zeros((HEAD_DIM, 1), F32)
    for j in range(n):
        cols = slice(j * block, (j + 1) * block)
        q = qkv_ref[0, 0, :, cols]
        go = gout_ref[:, cols]
        lse = lse_ref[0, :, cols]
        delta = jnp.sum(go.astype(F32) * out_ref[0, :, cols].astype(F32), axis=0, keepdims=True)
        gq = jnp.zeros((HEAD_DIM, block), F32)
        for i in range(j + 1):
            keys = slice(i * block, (i + 1) * block)
            s = dot(krow_ref[keys, :], q, (1, 0)) + bias_ref[bias_slot(j, i)]
            p = jnp.exp(s - lse)
            gp = dot(vrow_ref[keys, :], go, (1, 0))
            gs = (p * (gp - delta)).astype(BF)
            gq += dot(qkv_ref[1, 0, :, keys], gs, (1, 0))
            gk = dot(q, gs, (1, 1))
            gv = dot(go, p.astype(BF), (1, 1))
            if i == j:
                gk_ref[:, keys] = gk
                gv_ref[:, keys] = gv
            else:
                gk_ref[:, keys] += gk
                gv_ref[:, keys] += gv
        gscale += jnp.sum(gq * raw_ref[0, :, cols], axis=1, keepdims=True)
        grad_ref[0, 0, :, cols] = (gq * factor_ref[...]).astype(BF)
    grad_ref[1, 0] = gk_ref[...].astype(BF)
    grad_ref[2, 0] = gv_ref[...].astype(BF)
    gscale_ref[0] = gscale


def mask_args(series, padding):
    t = series.shape[0]
    pos = jnp.arange(t, dtype=jnp.int32)
    return series.reshape(1, t), series.reshape(t, 1), jnp.where(padding == 0, pos, t).reshape(t, 1)


def attention_forward(at, qkv, masks, pieces=0):
    _, heads, hd, t = qkv.shape
    block = min(256, t) if t <= 2048 else 512
    n = t // block
    whole = lambda shape: pl.BlockSpec(shape, lambda h: (0,) * len(shape))
    assert pieces in (0, n)
    return pl.pallas_call(
        functools.partial(forward_kernel, block),
        grid=(heads,),
        in_specs=[
            pl.BlockSpec(memory_space=pltpu.SMEM),
            pl.BlockSpec((3, 1, hd, t), lambda h: (0, h, 0, 0)),
            whole((1, t)),
            whole((t, 1)),
            whole((t, 1)),
        ],
        out_specs=[
            pl.BlockSpec((1, hd, t), lambda h: (h, 0, 0)),
            pl.BlockSpec((1, 1, t), lambda h: (h, 0, 0)),
        ]
        + [pl.BlockSpec((1, hd, block), lambda h: (h, 0, 0))] * pieces,
        out_shape=[
            jax.ShapeDtypeStruct((heads, hd, t), BF),
            jax.ShapeDtypeStruct((heads, 1, t), F32),
        ]
        + [jax.ShapeDtypeStruct((heads, hd, block), BF)] * pieces,
        scratch_shapes=[
            pltpu.VMEM((n * (n + 1) // 2, block, block), F32),
            pltpu.VMEM((t, hd), BF),
            pltpu.VMEM((t, block), F32),
            pltpu.VMEM((n, hd, block), BF),
        ],
        compiler_params=pltpu.CompilerParams(vmem_limit_bytes=VMEM_LARGE),
        cost_estimate=CHEAP,
        name="attention_forward",
    )(at, qkv, *masks)


def attention_backward(at, qkv, raw, factor, out, pieces, lse, masks, begin=0, heads=None):
    _, all_heads, hd, t = qkv.shape
    heads = heads or all_heads
    block = min(256, t) if t <= 2048 else 512
    n = t // block
    whole = lambda shape: pl.BlockSpec(shape, lambda h: (0,) * len(shape))
    head = lambda wide=t: pl.BlockSpec((1, hd, wide), lambda h: (begin + h, 0, 0))
    return pl.pallas_call(
        functools.partial(backward_kernel, block),
        grid=(heads,),
        in_specs=[
            pl.BlockSpec(memory_space=pltpu.SMEM),
            pl.BlockSpec((3, 1, hd, t), lambda h: (0, begin + h, 0, 0)),
            head(),
            whole((hd, 1)),
            head(),
            pl.BlockSpec((1, 1, t), lambda h: (begin + h, 0, 0)),
            whole((1, t)),
            whole((t, 1)),
            whole((t, 1)),
        ]
        + [head(p.shape[2]) for p in pieces],
        out_specs=[
            pl.BlockSpec((3, 1, hd, t), lambda h: (0, h, 0, 0)),
            pl.BlockSpec((1, hd, 1), lambda h: (h, 0, 0)),
        ],
        out_shape=[
            jax.ShapeDtypeStruct((3, heads, hd, t), BF),
            jax.ShapeDtypeStruct((heads, hd, 1), F32),
        ],
        scratch_shapes=[
            pltpu.VMEM((n * (n + 1) // 2, block, block), F32),
            pltpu.VMEM((t, hd), BF),
            pltpu.VMEM((t, hd), BF),
            pltpu.VMEM((hd, t), F32),
            pltpu.VMEM((hd, t), F32),
            pltpu.VMEM((hd, t), BF),
        ],
        compiler_params=pltpu.CompilerParams(vmem_limit_bytes=VMEM_LARGE),
        cost_estimate=CHEAP,
        name="attention_backward",
    )(at, qkv, raw, factor, out, lse, *masks, *pieces)


def norm_scale(x):
    return lax.rsqrt(jnp.mean(x * x, axis=1, keepdims=True) + EPS)


def body_any(
    inputs, gain_attn, w_qkv, query_scale, w_out, gain_mlp, w_up, b_up, w_down, b_down, series_ids, pad_mask, cotangent
):
    rows, cols = size("row"), size("col")
    tok = inputs.shape[0]
    feat = inputs.shape[1]
    share = tok // cols
    t = series_ids.shape[0]
    head_rows = w_qkv.shape[2] // cols
    heads = head_rows // HEAD_DIM
    r, c = lax.axis_index("row"), lax.axis_index("col")

    blocks = gather_grid(inputs)
    strips = [jnp.concatenate(b, axis=1) for b in blocks]
    x_own = strips[0] if rows == 2 else lax.dynamic_index_in_dim(jnp.stack(strips), r, 0, keepdims=False)
    x_all = jnp.concatenate(flip(strips, "row"), axis=0)
    gain_one = jnp.concatenate(gather(gain_attn, "col"))
    gain_two = jnp.concatenate(gather(gain_mlp, "col"))
    bias_up = jnp.concatenate(gather(b_up, "row")).astype(F32)
    bias_down = jnp.concatenate(gather(b_down, "col")).astype(F32)

    w3 = jnp.transpose(w_qkv, (1, 0, 2)).reshape(3, feat, cols, head_rows)
    w_mine = lax.dynamic_index_in_dim(w3, c, 2, keepdims=False)
    w_give = lax.dynamic_index_in_dim(w3, 1 - c, 2, keepdims=False)
    w_half = swap(core_half(w_give, 1), "col")
    w_other = swap(w_half, "core")
    first = lax.axis_index("core") == 0
    w_full = jnp.concatenate(
        [w_mine, jnp.where(first, w_half, w_other), jnp.where(first, w_other, w_half)], axis=1
    )

    xf = x_all.astype(F32)
    scale_one = norm_scale(xf)
    normed_one = (xf * scale_one * gain_one).astype(BF)
    projected = jnp.einsum("td,sdh->sht", normed_one, w_full, preferred_element_type=F32)
    projected = projected.reshape(3, heads, HEAD_DIM, t)
    factor = QUERY_CONST / math.sqrt(HEAD_DIM) * jax.nn.softplus(query_scale)
    raw_q = projected[0]
    qkv = jnp.stack([raw_q * factor[None, :, None], projected[1], projected[2]]).astype(BF)
    masks = mask_args(series_ids, pad_mask)
    at = jnp.zeros((4,), jnp.int32)
    attended, lse = attention_forward(at, qkv, masks)

    def to_tokens(y):
        y = flip_dim(y.reshape(head_rows, rows, cols, share), "row", 1)
        y = flip_dim(y, "col", 2)
        y = exchange(y.reshape(1, head_rows, rows, cols, share), "row", 2, 0)
        y = exchange(y.reshape(rows, 1, head_rows, cols, share), "col", 3, 1)
        y = flip_dim(y.reshape(rows, cols, head_rows, share), "col", 1)
        return y.reshape(rows * cols * head_rows, share)

    def to_heads(y):
        y = flip_dim(y.reshape(rows, cols, head_rows, share), "col", 1)
        y = exchange(y.reshape(rows, cols, head_rows, 1, share), "col", 1, 3)
        y = exchange(y.reshape(rows, head_rows, 1, cols, share), "row", 0, 2)
        y = flip_dim(y.reshape(head_rows, rows, cols, share), "col", 2)
        return flip_dim(y, "row", 1).reshape(head_rows, t)

    w_out_all = weight_gather(w_out, 0)
    w_up_all = weight_gather(w_up, 1)
    w_down_all = weight_gather(w_down, 0)

    def my_share(y):
        return lax.dynamic_slice_in_dim(y, c * share, share, 0)

    att = to_tokens(attended.reshape(head_rows, t))
    x_mine = my_share(x_own).astype(F32)
    middle = x_mine + dot(att, w_out_all, (0, 0))
    scale_two = norm_scale(middle)
    normed_two = (middle * scale_two * gain_two).astype(BF)
    pre_act = dot(normed_two, w_up_all, (1, 0)) + bias_up
    sig = jax.nn.sigmoid(pre_act)
    hidden = (pre_act * sig).astype(BF)
    result = (middle + dot(hidden, w_down_all, (1, 0)) + bias_down).astype(BF)

    def to_block(y):
        mine, theirs = jnp.split(y, 2, axis=1)
        return jnp.concatenate(flip([mine, swap(theirs, "col")], "col"), axis=0)

    layer_out = to_block(result)

    g_give = lax.dynamic_slice_in_dim(cotangent, (1 - c) * share, share, 0)
    g = jnp.concatenate([my_share(cotangent), swap(g_give, "col")], axis=1)
    grad_w_down = dot(hidden, g, (0, 0))
    grad_hidden = dot(g, w_down_all, (1, 1))
    grad_pre_f = grad_hidden * sig * (1.0 + pre_act * (1.0 - sig))
    grad_pre = grad_pre_f.astype(BF)
    grad_b_up = jnp.sum(grad_pre.astype(F32), axis=0)
    grad_w_up = dot(normed_two, grad_pre, (0, 0))
    grad_normed_two = dot(grad_pre, w_up_all, (1, 1))
    weighted = grad_normed_two * gain_two
    inner = jnp.sum(weighted * middle, axis=1, keepdims=True)
    grad_middle = g.astype(F32) + scale_two * weighted - middle * (scale_two**3 * inner / D)
    grad_gain_mlp = jnp.sum(grad_normed_two * middle * scale_two, axis=0)
    grad_branch = grad_middle.astype(BF)
    grad_w_out = dot(att, grad_branch, (1, 0))
    grad_att = dot(w_out_all, grad_branch, (1, 1)).astype(BF)
    grad_attended = to_heads(grad_att).reshape(heads, HEAD_DIM, t)
    grad_middle_block = to_block(grad_middle)

    sum_down = weight_sum(grad_w_down, 0)
    sum_up = weight_sum(grad_w_up, 1)
    sum_out = weight_sum(grad_w_out, 0)

    grad_proj, gscale = attention_backward(
        at, qkv, raw_q, factor.reshape(HEAD_DIM, 1), attended, [grad_attended], lse, masks
    )
    slope = QUERY_CONST / math.sqrt(HEAD_DIM) * jax.nn.sigmoid(query_scale)
    grad_query_scale = jnp.sum(gscale, axis=(0, 2)) * slope
    grad_proj = grad_proj.reshape(3, head_rows, t)
    grad_normed_one = jnp.einsum("sht,sdh->td", grad_proj, w_full, preferred_element_type=F32)
    weighted_one = grad_normed_one * gain_one
    inner_one = jnp.sum(weighted_one * xf, axis=1)
    grad_gain_attn = jnp.sum(grad_normed_one * xf * scale_one, axis=0)
    inner_one = lax.psum(inner_one, ("row", "col"))
    grad_w = jnp.einsum("td,sht->sdh", normed_one, grad_proj, preferred_element_type=F32)
    grad_w = grad_w.reshape(3, cols, 2, feat // 2, head_rows)
    core = lax.axis_index("core")
    keep = lax.dynamic_index_in_dim(grad_w, core, 2, keepdims=False)
    give = lax.dynamic_index_in_dim(grad_w, 1 - core, 2, keepdims=False).astype(BF)
    part = (keep + swap(give, "core").astype(F32)).astype(BF)
    part = jnp.concatenate(flip([part[:, 0], swap(part[:, 1], "col")], "col"), axis=2)
    sum_qkv = jnp.transpose(z_sum(part), (1, 0, 2))

    e = jnp.concatenate(flip(jnp.split(grad_normed_one.astype(BF), 2, axis=0), "row"), axis=0) if rows == 2 else (
        grad_normed_one.astype(BF)
    )
    e = scatter_sum(e, "row", 0)
    e = scatter_sum(e, "col", 1).astype(F32)
    my_rows = lambda y: lax.dynamic_slice_in_dim(y, r * tok, tok, 0)
    scale_mine = my_rows(scale_one)
    inner_mine = my_rows(inner_one.reshape(t, 1))
    grad_inputs = grad_middle_block + scale_mine * (e * gain_attn) - inputs.astype(F32) * (
        scale_mine**3 * inner_mine / D
    )

    grad_b_down = jnp.sum(g.astype(F32), axis=0)
    vectors = jnp.concatenate(
        [
            flip_dim(grad_gain_attn, "col", 0),
            flip_dim(grad_gain_mlp, "col", 0),
            flip_dim(grad_b_down, "col", 0),
            flip_dim(grad_b_up, "row", 0),
            grad_query_scale,
        ]
    )
    vectors = lax.psum(vectors, ("z", "core", "row", "col"))
    mine_col = lambda at: lax.dynamic_slice_in_dim(vectors, at * D + c * feat, feat, 0)
    units = b_up.shape[0]
    return (
        layer_out,
        grad_inputs,
        mine_col(0),
        sum_qkv,
        vectors[4 * D :],
        sum_out,
        mine_col(1),
        sum_up,
        lax.dynamic_slice_in_dim(vectors, 3 * D + r * units, units, 0),
        sum_down,
        mine_col(2),
    )


SMEM = pl.BlockSpec(memory_space=pltpu.SMEM)
ANY = pl.BlockSpec(memory_space=pl.ANY)


def call(kernel, name, args, specs, outs, scratch=(), limit=VMEM_LIMIT):
    return pl.pallas_call(
        kernel,
        in_specs=specs,
        out_shape=outs,
        scratch_shapes=list(scratch),
        compiler_params=pltpu.CompilerParams(vmem_limit_bytes=limit),
        cost_estimate=CHEAP,
        name=name,
    )(*args)


VM = pl.BlockSpec(memory_space=pltpu.VMEM)


def shape(dims, kind):
    return jax.ShapeDtypeStruct(dims, kind)


def project_kernel(
    at, x00, x01, x10, x11, gain, factor, w_mine, w_a, w_b, qkv, raw, normed, scale_own, w_full
):
    r, k = at[0], at[2]
    tok, feat = x00.shape
    hr = w_mine.shape[1]
    half = hr // 2
    for s in range(3):
        w_full[pl.ds(s * hr, hr), 0:feat] = w_mine[s]
        w_full[pl.ds(pl.multiple_of(s * hr + k * half, 16), half), feat:] = w_a[s]
        w_full[pl.ds(pl.multiple_of(s * hr + (1 - k) * half, 16), half), feat:] = w_b[s]
    for i, (a_ref, b_ref) in enumerate(((x00, x01), (x10, x11))):
        a, b = a_ref[...].astype(F32), b_ref[...].astype(F32)
        total = jnp.sum(a * a, axis=1, keepdims=True) + jnp.sum(b * b, axis=1, keepdims=True)
        scale = lax.rsqrt(total / (2 * feat) + EPS)
        if i == 0:
            scale_own[...] = scale
        rows = pl.ds(pl.multiple_of((r ^ i) * tok, tok), tok)
        normed[rows, 0:feat] = (a * scale * gain[:, 0:feat]).astype(BF)
        normed[rows, feat:] = (b * scale * gain[:, feat:]).astype(BF)
        y = normed[rows, :]
        q = dot(w_full[0:hr, :], y, (1, 1))
        raw[:, rows] = q
        qkv[0, :, rows] = (q * factor[...]).astype(BF)
        qkv[1, :, rows] = dot(w_full[hr : 2 * hr, :], y, (1, 1)).astype(BF)
        qkv[2, :, rows] = dot(w_full[2 * hr : 3 * hr, :], y, (1, 1)).astype(BF)


def feed_kernel(
    at, a0, a1, a2, a3, x_own, x_col, g_own, g_col, gain, bias_up, bias_down,
    w_out, w_up, w_down, hx, hy, d0, d1, hx2, hy2, d02, d12,
    out_own, gm_own, post, t0, t1, t2, t3, vectors,
    *rest,
):
    *grads, w, att, turned, sems = rest
    r, c, k = at[0], at[1], at[2]
    hr, share = a0.shape
    feat = x_own.shape[1]
    half = feat // 2
    quarter = half // 2
    copies = []
    for n, shard in enumerate((w_out, w_up, w_down)):
        rx, cx, ry, cy = (0, feat, feat, 0) if n == 1 else (feat, 0, 0, feat)
        mine = []
        mine.append((shard, w.at[n, 0:feat, 0:feat]))
        for core, (px, py, p0, p1) in ((k, (hx, hy, d0, d1)), (1 - k, (hx2, hy2, d02, d12))):
            down = core * half
            at_x = pl.ds(pl.multiple_of(rx + down, 16), half)
            at_y = pl.ds(pl.multiple_of(ry + down, 16), half)
            first = d0.shape[1]
            at_0 = pl.ds(pl.multiple_of(feat + down, 16), first)
            at_1 = pl.ds(pl.multiple_of(feat + down + first, 16), half - first)
            mine.append((px.at[n], w.at[n, at_x, cx : cx + feat]))
            mine.append((py.at[n], w.at[n, at_y, cy : cy + feat]))
            mine.append((p0.at[n], w.at[n, at_0, feat : 2 * feat]))
            mine.append((p1.at[n], w.at[n, at_1, feat : 2 * feat]))
        started = []
        for m, (src, dst) in enumerate(mine):
            copy = pltpu.make_async_copy(src, dst, sems.at[n, m])
            copy.start()
            started.append(copy)
        copies.append(started)

    rows = pl.ds(pl.multiple_of(c * share, share), share)
    for s, a in enumerate((a0, a1, a2, a3)):
        to = (s // 2) * 2 * hr + (c ^ (s % 2)) * hr
        att[pl.ds(pl.multiple_of(to, 16), hr), :] = a[...]
    x = jnp.concatenate([x_own[rows, :], x_col[rows, :]], axis=1).astype(F32)
    g = jnp.concatenate([g_own[rows, :], g_col[...]], axis=1)
    for copy in copies[0]:
        copy.wait()
    middle = x + dot(att[...], w[0], (0, 0))
    scale = lax.rsqrt(jnp.sum(middle * middle, axis=1, keepdims=True) / D + EPS)
    normed = (middle * scale * gain[...]).astype(BF)
    for copy in copies[1]:
        copy.wait()
    pre = dot(normed, w[1], (1, 0)) + bias_up[...]
    sig = jax.nn.sigmoid(pre)
    hidden = (pre * sig).astype(BF)
    for copy in copies[2]:
        copy.wait()
    result = (middle + dot(hidden, w[2], (1, 0)) + bias_down[...]).astype(BF)
    out_own[...] = result[:, :feat]
    post[0] = result[:, feat:]

    def weight_grad(n, left_ref, right):
        for core, sets in ((k, grads[:8]), (1 - k, grads[8:])):
            by_row, by_col = sets[:4], sets[4:]
            up, low = (by_col, by_row) if n == 1 else (by_row, by_col)
            for b in range(2):
                part = pl.ds(pl.multiple_of(b * feat + core * half, 16), half)
                y = dot(left_ref[part, :], right, (1, 0)).astype(BF)
                for j in range(2):
                    cut = slice(j * feat, (j + 1) * feat)
                    up[2 * j + (1 - b)][n] = y[:quarter, cut]
                    low[2 * b + (1 - j)][n] = y[quarter:, cut]

    turned[...] = hidden.astype(F32).T.astype(BF)
    grad_pre_f = dot(g, w[2], (1, 1)) * sig * (1.0 + pre * (1.0 - sig))
    grad_pre = grad_pre_f.astype(BF)
    weight_grad(2, turned, g)
    grad_normed = dot(grad_pre, w[1], (1, 1))
    weighted = grad_normed * gain[...]
    inner = jnp.sum(weighted * middle, axis=1, keepdims=True)
    gf = g.astype(F32)
    grad_middle = gf + scale * weighted - middle * (scale * scale * scale * inner / D)
    gm_own[...] = grad_middle[:, :feat]
    post[1] = grad_middle[:, feat:].astype(BF)
    branch = grad_middle.astype(BF)
    for s, t in enumerate((t0, t1, t2, t3)):
        come = (s // 2) * 2 * hr + (c ^ (s % 2)) * hr
        t[...] = dot(w[0, pl.ds(pl.multiple_of(come, 16), hr), :], branch, (1, 1)).astype(BF)
    turned[...] = normed.astype(F32).T.astype(BF)
    weight_grad(1, turned, grad_pre)
    weight_grad(0, att, branch)
    vectors[...] = jnp.concatenate(
        [
            jnp.sum(grad_normed * (middle * scale), axis=0, keepdims=True),
            jnp.sum(gf, axis=0, keepdims=True),
            jnp.sum(grad_pre.astype(F32), axis=0, keepdims=True),
        ],
        axis=0,
    )


def weight_back_kernel(at, grad, normed, keep, give):
    k = at[2]
    part = keep.shape[2]
    feat = keep.shape[3]
    for ref, core in ((give, 1 - k), (keep, k)):
        for s in range(3):
            rows = pl.ds(pl.multiple_of(core * part, 16), part)
            y = dot(grad[s, rows, :], normed[...], (1, 0)).astype(BF)
            ref[0, s] = y[:, :feat]
            ref[1, s] = y[:, feat:]


def project_back_kernel(
    at, grad, w_full, x00, x01, x10, x11, gain, e0, e1, e2, e3, inner_own, gain_sum
):
    r = at[0]
    tok, feat = x00.shape
    sums = [jnp.zeros((1, feat), F32), jnp.zeros((1, feat), F32)]
    for i, (xs, es) in enumerate((((x00, x01), (e0, e1)), ((x10, x11), (e2, e3)))):
        rows = pl.ds(pl.multiple_of((r ^ i) * tok, tok), tok)
        left = grad[:, rows]
        products, squares, inner = [], 0.0, 0.0
        for j in range(2):
            cut = slice(j * feat, (j + 1) * feat)
            e = dot(left, w_full[:, cut], (0, 0))
            x = xs[j][...].astype(F32)
            product = e * x
            inner = inner + jnp.sum(product * gain[:, cut], axis=1, keepdims=True)
            squares = squares + jnp.sum(x * x, axis=1, keepdims=True)
            es[j][0:tok, :] = e.astype(es[j].dtype)
            products.append(product)
        scale = lax.rsqrt(squares / (2 * feat) + EPS)
        for j in range(2):
            sums[j] += jnp.sum(products[j] * scale, axis=0, keepdims=True)
        line = jnp.broadcast_to(inner, (tok, 128)).T[0:1, :]
        high = line.astype(BF).astype(F32)
        extra = jnp.concatenate([high, line - high, jnp.zeros((14, tok), F32)], axis=0)
        extra = jnp.concatenate([extra, jnp.zeros((16, feat - tok), F32)], axis=1).astype(BF)
        if i == 0:
            inner_own[...] = inner
            es[1][tok:, :] = extra
        else:
            es[0][tok:, :] = extra
            es[1][tok:, :] = extra
    gain_sum[:, 0:feat] = sums[0]
    gain_sum[:, feat:] = sums[1]


def finish_qkv_kernel(at, mine, theirs, mine2, theirs2, out, rows):
    c, k = at[1], at[2]
    half = mine.shape[1]
    for s in range(3):
        for ref, col, core in ((mine, c, k), (theirs, 1 - c, k), (mine2, c, 1 - k), (theirs2, 1 - c, 1 - k)):
            rows[pl.ds(pl.multiple_of((2 * col + core) * half, 16), half), :] = ref[s].astype(F32)
        out[s] = rows[...].T


def finish_feed_kernel(at, a, b, a2, b2, *outs):
    k = at[2]
    quarter = a.shape[1]
    for n, out in enumerate(outs):
        upper, lower = ((b, b2), (a, a2)) if n == 1 else ((a, a2), (b, b2))
        for i, core in ((0, k), (1, 1 - k)):
            for j, refs in enumerate((upper, lower)):
                to = pl.multiple_of((2 * core + j) * quarter, 16)
                out[pl.ds(to, quarter), :] = refs[i][n].astype(F32)


together = lax.optimization_barrier


def after(x, *earlier):
    return lax.optimization_barrier((x, *earlier))[0]


def add(*parts):
    total = parts[0].astype(F32)
    for part in parts[1:]:
        total = total + part.astype(F32)
    return total.astype(BF)


def diagonal(x):
    return lax.ppermute(x, ("row", "col"), [(0, 3), (1, 2), (2, 1), (3, 0)])


def z_swap(x, step):
    n = size("z")
    return lax.ppermute(x, "z", [(i, i ^ step) for i in range(n)])


def z_first():
    z = lax.axis_index("z")
    return (z == 0) | (z == 3)


def body_four(
    inputs, gain_attn, w_qkv, query_scale, w_out, gain_mlp, w_up, b_up, w_down, b_down, series_ids, pad_mask, cotangent
):
    tok, feat = inputs.shape
    share = tok // 2
    t = series_ids.shape[0]
    hr = w_qkv.shape[2] // 2
    heads = hr // HEAD_DIM
    half = feat // 2
    r, c, k = lax.axis_index("row"), lax.axis_index("col"), lax.axis_index("core")
    at = jnp.stack([r, c, k, 2 * r + c]).astype(jnp.int32)
    mine_rows = lambda y, part: lax.dynamic_slice_in_dim(y, part * share, share, 0)

    few = heads // 2
    quarter = half // 2
    first_rows = (half * 7 // 20) // 16 * 16
    x01 = swap(inputs, "col")
    x10 = swap(inputs, "row")
    small = swap(jnp.concatenate([gain_attn, gain_mlp, b_down.astype(F32)]), "col")
    up_other = swap(b_up.astype(F32), "row")
    w_turned = jnp.transpose(w_qkv, (1, 2, 0)).reshape(3, 2, hr, feat)
    w_mine = lax.dynamic_index_in_dim(w_turned, c, 1, keepdims=False)
    w_give = lax.dynamic_index_in_dim(w_turned, 1 - c, 1, keepdims=False)
    w_half = core_half(w_give, 1)
    w_a = swap(w_half, "col")
    part = jnp.stack([core_half(w_out, 0), core_half(w_up, 0), core_half(w_down, 0)])
    g_give = mine_rows(cotangent, 1 - c)
    x01, x10, small, up_other, part, g_give, w_mine = lax.optimization_barrier(
        (x01, x10, small, up_other, part, g_give, w_mine)
    )
    x11 = swap(after(x01, w_half), "row")
    w_b = swap(w_a, "core")
    gain_one = jnp.concatenate([gain_attn, small[:feat]]).reshape(1, D)
    gain_two = jnp.concatenate([gain_mlp, small[feat : 2 * feat]]).reshape(1, D)
    bias_down = jnp.concatenate([b_down.astype(F32), small[2 * feat :]]).reshape(1, D)
    bias_up = jnp.concatenate([b_up.astype(F32), up_other]).reshape(1, D)
    factor = QUERY_CONST / math.sqrt(HEAD_DIM) * jax.nn.softplus(query_scale)
    factor_col = factor.reshape(HEAD_DIM, 1)

    part = after(part, x11, w_a)
    hx, hy = swap(part, "row"), swap(part, "col")
    hx2, hy2 = swap(hx, "core"), swap(hy, "core")
    qkv, raw, normed_one, scale_own, w_full = call(
        project_kernel,
        "project",
        (at, inputs, x01, x10, x11, gain_one, jnp.tile(factor_col, (heads, 1)), w_mine, w_a, w_b),
        [SMEM] + [VM] * 9,
        [
            shape((3, hr, t), BF),
            shape((hr, t), F32),
            shape((t, D), BF),
            shape((tok, 1), F32),
            shape((3 * hr, D), BF),
        ],
        limit=VMEM_LARGE,
    )
    qkv = qkv.reshape(3, heads, HEAD_DIM, t)
    masks = mask_args(series_ids, pad_mask)
    attended, lse, *a = attention_forward(at, qkv, masks, pieces=4)
    a0, a1, a2, a3 = [p.reshape(hr, share) for p in a]
    a1, a2, a3 = swap(a1, "col"), swap(a2, "row"), diagonal(a3)
    hx_on, hy_on, g_give = lax.optimization_barrier((hx, hy, g_give, lse))[:3]
    d0 = swap(hx_on[:, :first_rows], "col")
    d1 = swap(hy_on[:, first_rows:], "row")
    g_col = swap(g_give, "col")
    d0, d1, g_col, a1, a2, a3 = together((d0, d1, g_col, a1, a2, a3))
    d02, d12 = swap(d0, "core"), swap(d1, "core")
    out_own, gm_own, post, t0, t1, t2, t3, vectors, *grads = call(
        feed_kernel,
        "feed_forward",
        (at, a0, a1, a2, a3, inputs, x01, cotangent, g_col, gain_two, bias_up, bias_down)
        + (w_out, w_up, w_down, hx, hy, d0, d1, hx2, hy2, d02, d12),
        [SMEM] + [VM] * 11 + [ANY] * 11,
        [
            shape((share, feat), BF),
            shape((share, feat), F32),
            shape((2, share, feat), BF),
        ]
        + [shape((hr, share), BF)] * 4
        + [shape((3, D), F32)]
        + [shape((3, quarter, feat), BF)] * 16,
        scratch=[
            pltpu.VMEM((3, D, D), BF),
            pltpu.VMEM((D, share), BF),
            pltpu.VMEM((D, share), BF),
            pltpu.SemaphoreType.DMA((3, 9)),
        ],
    )
    t3 = diagonal(t3)
    t1, t2 = swap(t1, "col"), swap(t2, "row")
    others = grads[8:]
    over = lambda n: swap(others[n], "core")
    t1, t2, t3, grads, osx0, osx1, osy0, osy1 = together((t1, t2, t3, grads[:8], over(0), over(2), over(4), over(6)))
    sx0, kx0, sx1, kx1, sy0, ky0, sy1, ky1 = grads
    sx1, sy1 = add(sx1, osx1), add(sy1, osy1)
    ox0, ox1, oy0, oy1 = over(1), over(3), over(5), over(7)
    pieces, sx1, sy1, sx0, sy0 = together(((t0, t1, t2, t3), sx1, sy1, sx0, sy0))
    sx0, sy0 = add(sx0, osx0), add(sy0, osy0)
    rx1, ry1 = swap(sx1, "row"), swap(sy1, "col")
    rx0, ry0 = swap(sx0, "row"), swap(sy0, "col")
    pieces = [p.reshape(heads, HEAD_DIM, share) for p in pieces]
    raw = raw.reshape(heads, HEAD_DIM, t)

    grad_proj, gscale = attention_backward(at, qkv, raw, factor_col, attended, pieces, lse, masks)
    grad_proj = grad_proj.reshape(3, hr, t)
    kept, sent = call(
        weight_back_kernel,
        "weight_back",
        (at, grad_proj, normed_one),
        [SMEM] + [VM] * 2,
        [shape((2, 3, hr // 2, feat), BF)] * 2,
    )
    sent, rx1, ry1, rx0, ry0, ox0, ox1, oy0, oy1 = together((sent, rx1, ry1, rx0, ry0, ox0, ox1, oy0, oy1))
    got = swap(sent, "core")
    px1, py1 = add(kx1, ox1, rx1), add(ky1, oy1, ry1)
    qx, qy = swap(px1, "col"), swap(py1, "row")
    w_pair = add(kept, got)
    first = z_first()
    got_w = z_swap(jnp.where(first, w_pair[1], w_pair[0]), 1)
    slope = QUERY_CONST / math.sqrt(HEAD_DIM) * jax.nn.sigmoid(query_scale)
    grad_query_scale = jnp.sum(gscale, axis=(0, 2)) * slope
    e0, e1, e2, e3, inner, gain_sum = call(
        project_back_kernel,
        "project_back",
        (at, after(grad_proj, w_pair, px1, py1).reshape(3 * hr, t), w_full, inputs, x01, x10, x11, gain_one),
        [SMEM] + [VM] * 7,
        [
            shape((tok, feat), F32),
            shape((tok + 16, feat), BF),
            shape((tok + 16, feat), BF),
            shape((tok + 16, feat), BF),
            shape((tok, 1), F32),
            shape((1, D), F32),
        ],
    )
    total = jnp.concatenate([gain_sum, vectors]).reshape(4, 2, feat)
    turn = jnp.stack([c, c, c, r]).reshape(4, 1, 1) == 1
    total = jnp.where(turn, total[:, ::-1], total).reshape(8, feat)
    total = jnp.concatenate([total, jnp.pad(grad_query_scale, (0, feat - HEAD_DIM)).reshape(1, feat)])
    total = total + swap(total, "core")
    qx, qy, w_pair, e1, e2, e3 = together((qx, qy, w_pair, e1, e2, e3))

    mine_w = add(jnp.where(first, w_pair[0], w_pair[1]), got_w)
    met_w = z_swap(mine_w, 3)
    fx, fy = add(kx0, ox0, rx0, qx), add(ky0, oy0, ry0, qy)
    got_c = z_swap(jnp.where(first, fy, fx), 1)
    e1, e2 = swap(e1, "col"), swap(e2, "row")
    total = total + swap(total, "row")
    total = total + swap(total, "col")
    met_w, mine_w, got_c, fx, fy, e1, e2, e3, post, total = together(
        (met_w, mine_w, got_c, fx, fy, e1, e2, e3, post, total)
    )

    mine_w = add(mine_w, met_w)
    other_w = z_swap(mine_w, 1)
    w_own, w_theirs = jnp.where(first, mine_w, other_w), jnp.where(first, other_w, mine_w)
    mine_c = add(jnp.where(first, fx, fy), got_c)
    met_c = z_swap(mine_c, 3)
    e3, post = diagonal(e3), swap(post, "col")
    w_theirs = swap(w_theirs, "col")
    total = total + z_swap(total, 1)
    total = total + z_swap(total, 3)
    met_c, mine_c, w_own, w_theirs, post, e3, total = together((met_c, mine_c, w_own, w_theirs, post, e3, total))
    mine_c = add(mine_c, met_c)
    other_c = z_swap(mine_c, 1)
    w_args = (at, w_own, w_theirs, swap(w_own, "core"), swap(w_theirs, "core"))
    sum_qkv = call(
        finish_qkv_kernel,
        "finish_qkv",
        w_args,
        [SMEM] + [VM] * 4,
        shape((3, feat, 2 * hr), F32),
        scratch=[pltpu.VMEM((2 * hr, feat), F32)],
    )
    sum_qkv = jnp.transpose(sum_qkv, (1, 0, 2))

    e = e0
    for more in (e1, e2, e3):
        e = e + more[:tok].astype(F32)
        inner = inner + jnp.sum(more[tok : tok + 2, :tok].astype(F32), axis=0).reshape(tok, 1)
    grad_middle = jnp.concatenate(flip([gm_own, post[1].astype(F32)], "col"), axis=0)
    grad_inputs = grad_middle + scale_own * (e * gain_attn) - inputs.astype(F32) * (scale_own**3 * inner / D)
    layer_out = jnp.concatenate(flip([out_own, post[0]], "col"), axis=0)

    pick = lambda n, place: lax.dynamic_index_in_dim(total, 2 * n + place, 0, keepdims=False)
    mine_c = after(mine_c, sum_qkv, grad_inputs, layer_out, total)
    fx, fy = jnp.where(first, mine_c, other_c), jnp.where(first, other_c, mine_c)
    sum_out, sum_up, sum_down = call(
        finish_feed_kernel,
        "finish_feed",
        (at, fx, fy, swap(fx, "core"), swap(fy, "core")),
        [SMEM] + [VM] * 4,
        [shape((feat, feat), F32)] * 3,
    )

    return (
        layer_out,
        grad_inputs,
        pick(0, c),
        sum_qkv,
        total[8, :HEAD_DIM],
        sum_out,
        pick(1, c),
        sum_up,
        pick(3, r),
        sum_down,
        pick(2, c),
    )


def solution(mesh):
    dp, rows, cols = mesh.shape["dp"], mesh.shape["row"], mesh.shape["col"]
    split = Mesh(mesh.devices.reshape(dp // 2, 2, rows, cols), ("z", "core", "row", "col"))
    tokens = P(("z", "core", "row"), "col")
    in_specs = (
        tokens,
        P("col"),
        P("col", None, "row"),
        P(),
        P("row", "col"),
        P("col"),
        P("col", "row"),
        P("row"),
        P("row", "col"),
        P("col"),
        P(("z", "core")),
        P(("z", "core")),
        tokens,
    )
    out_specs = (
        tokens,
        tokens,
        P("col"),
        P("col", None, "row"),
        P(),
        P("row", "col"),
        P("col"),
        P("col", "row"),
        P("row"),
        P("row", "col"),
        P("col"),
    )
    body = body_four if (dp, rows, cols) == (8, 2, 2) else body_any
    return jax.shard_map(body, mesh=split, in_specs=in_specs, out_specs=out_specs, check_vma=False)
```

```python
import functools
import math

import jax
import jax.numpy as jnp
from jax import lax
from jax.experimental import pallas as pl
from jax.experimental.pallas import tpu as pltpu
from jax.sharding import Mesh
from jax.sharding import PartitionSpec as P

D = 1280
HEAD_DIM = 80
EPS = 1e-06
QUERY_CONST = 1.442695041
MASKED = -1e30
BF = jnp.bfloat16
F32 = jnp.float32
VMEM_LIMIT = 24 * 1024 * 1024
VMEM_LARGE = 50 * 1024 * 1024
CHEAP = pl.CostEstimate(flops=1, bytes_accessed=1, transcendentals=0)


def size(axis):
    return lax.axis_size(axis)


def swap(x, axis):
    return lax.ppermute(x, axis, [(0, 1), (1, 0)])


def flip(blocks, axis):
    if size(axis) != 2:
        return list(blocks)
    first = lax.axis_index(axis) == 0
    a, b = blocks
    return [jnp.where(first, a, b), jnp.where(first, b, a)]


def flip_dim(x, axis, dim):
    if size(axis) != 2:
        return x
    return jnp.concatenate(flip(jnp.split(x, 2, axis=dim), axis), axis=dim)


def gather(x, axis):
    if size(axis) == 2:
        return [x, swap(x, axis)]
    whole = lax.all_gather(x, axis, axis=0, tiled=False)
    return [whole[i] for i in range(size(axis))]


def gather_grid(x):
    if size("row") != 2:
        return [gather(b, "col") for b in gather(x, "row")]
    along_row, along_col = swap(x, "row"), swap(x, "col")
    half = x.shape[0] // 2
    across = jnp.concatenate(
        [swap(along_row[:half], "col"), swap(along_col[half:], "row")], axis=0
    )
    return [[x, along_col], [along_row, across]]


def scatter_sum(x, axis, dim):
    if size(axis) != 2:
        return lax.psum_scatter(x, axis, scatter_dimension=dim, tiled=True)
    mine, theirs = jnp.split(x, 2, axis=dim)
    return (mine.astype(F32) + swap(theirs, axis).astype(F32)).astype(x.dtype)


def exchange(x, axis, split, join):
    if size(axis) != 2:
        return lax.all_to_all(x, axis, split, join, tiled=True)
    mine, theirs = jnp.split(x, 2, axis=split)
    return jnp.concatenate([mine, swap(theirs, axis)], axis=join)


def core_half(x, dim):
    return lax.dynamic_slice_in_dim(
        x, lax.axis_index("core") * (x.shape[dim] // 2), x.shape[dim] // 2, dim
    )


def weight_gather(w, row_dim):
    part = core_half(w, 0)
    blocks = gather_grid(part)
    if row_dim == 1:
        blocks = [list(b) for b in zip(*blocks)]
    mine = jnp.stack([jnp.concatenate(b, axis=1) for b in blocks])
    other = swap(mine, "core")
    first = lax.axis_index("core") == 0
    both = jnp.stack([jnp.where(first, mine, other), jnp.where(first, other, mine)], axis=1)
    return both.reshape(-1, both.shape[-1])


def weight_sum(g, row_dim):
    dim_axis = ("row", "col") if row_dim == 0 else ("col", "row")
    n0 = size(dim_axis[0])
    g = g.reshape(n0, 2, g.shape[0] // n0 // 2, g.shape[1])
    core = lax.axis_index("core")
    keep = lax.dynamic_index_in_dim(g, core, 1, keepdims=False)
    give = lax.dynamic_index_in_dim(g, 1 - core, 1, keepdims=False).astype(BF)
    part = (keep + swap(give, "core").astype(F32)).astype(BF)
    part = scatter_sum(part, dim_axis[0], 0)
    part = scatter_sum(part[0], dim_axis[1], 1)
    return z_sum(part)


def z_sum(part):
    total = lax.psum(part, "z")
    other = swap(total, "core")
    return flip_core(total, other)


def flip_core(total, other):
    first = lax.axis_index("core") == 0
    return jnp.concatenate(
        [jnp.where(first, total, other), jnp.where(first, other, total)], axis=-2
    ).astype(F32)


def dot(a, b, contract):
    return lax.dot_general(a, b, ((contract[0:1], contract[1:2]), ((), ())), preferred_element_type=F32)


def bias_block(series_row, series_col, key_pos, q0, k0, qb, kb, diagonal):
    q_pos = q0 + lax.broadcasted_iota(jnp.int32, (1, qb), 1)
    allowed = (series_col == series_row) & (key_pos <= q_pos)
    if diagonal:
        k_pos = k0 + lax.broadcasted_iota(jnp.int32, (kb, 1), 0)
        allowed = allowed | (k_pos == q_pos)
    return jnp.where(allowed, 0.0, MASKED)


def forward_kernel(block, at, qkv_ref, srow_ref, scol_ref, kpos_ref, out_ref, lse_ref, *rest):
    *pieces, bias_ref, krow_ref, s_ref = rest
    t = qkv_ref.shape[3]
    n = t // block
    krow_ref[...] = qkv_ref[1, 0].astype(F32).T.astype(BF)

    def bias_slot(j, i):
        return j * (j + 1) // 2 + i

    @pl.when(pl.program_id(0) == 0)
    def _():
        for j in range(n):
            for i in range(j + 1):
                keys = pl.ds(i * block, block)
                bias_ref[bias_slot(j, i)] = bias_block(
                    srow_ref[:, j * block : (j + 1) * block],
                    scol_ref[keys, :],
                    kpos_ref[keys, :],
                    j * block,
                    i * block,
                    block,
                    block,
                    i == j,
                )

    for j in range(n):
        cols = slice(j * block, (j + 1) * block)
        q = qkv_ref[0, 0, :, cols]
        top = None
        for i in range(j + 1):
            s = dot(krow_ref[i * block : (i + 1) * block, :], q, (1, 0)) + bias_ref[bias_slot(j, i)]
            s_ref[i * block : (i + 1) * block, :] = s
            here = jnp.max(s, axis=0, keepdims=True)
            top = here if top is None else jnp.maximum(top, here)
        total = jnp.zeros((1, block), F32)
        acc = jnp.zeros((HEAD_DIM, block), F32)
        for i in range(j + 1):
            p = jnp.exp(s_ref[i * block : (i + 1) * block, :] - top)
            total += jnp.sum(p, axis=0, keepdims=True)
            acc += dot(qkv_ref[2, 0, :, i * block : (i + 1) * block], p.astype(BF), (1, 0))
        found = (acc / total).astype(BF)
        out_ref[0, :, cols] = found
        if pieces:
            pieces[0][j, 0] = found
        lse_ref[0, :, cols] = top + jnp.log(total)


def backward_kernel(
    block, at, qkv_ref, raw_ref, factor_ref, out_ref, lse_ref, srow_ref, scol_ref, kpos_ref, *rest
):
    piece, grad_ref, gscale_ref, bias_ref, krow_ref, vrow_ref, gk_ref, gv_ref, gout_ref = rest
    wide = piece.shape[3]
    for j in range(piece.shape[0]):
        gout_ref[:, j * wide : (j + 1) * wide] = piece[j, 0]
    t = qkv_ref.shape[3]
    n = t // block
    krow_ref[...] = qkv_ref[1, 0].astype(F32).T.astype(BF)
    vrow_ref[...] = qkv_ref[2, 0].astype(F32).T.astype(BF)

    def bias_slot(j, i):
        return j * (j + 1) // 2 + i

    @pl.when(pl.program_id(0) == 0)
    def _():
        for j in range(n):
            for i in range(j + 1):
                keys = pl.ds(i * block, block)
                bias_ref[bias_slot(j, i)] = bias_block(
                    srow_ref[:, j * block : (j + 1) * block],
                    scol_ref[keys, :],
                    kpos_ref[keys, :],
                    j * block,
                    i * block,
                    block,
                    block,
                    i == j,
                )

    gscale = jnp.zeros((HEAD_DIM, 1), F32)
    for j in range(n):
        cols = slice(j * block, (j + 1) * block)
        q = qkv_ref[0, 0, :, cols]
        go = gout_ref[:, cols]
        lse = lse_ref[0, :, cols]
        delta = jnp.sum(go.astype(F32) * out_ref[0, :, cols].astype(F32), axis=0, keepdims=True)
        gq = jnp.zeros((HEAD_DIM, block), F32)
        for i in range(j + 1):
            keys = slice(i * block, (i + 1) * block)
            s = dot(krow_ref[keys, :], q, (1, 0)) + bias_ref[bias_slot(j, i)]
            p = jnp.exp(s - lse)
            gp = dot(vrow_ref[keys, :], go, (1, 0))
            gs = (p * (gp - delta)).astype(BF)
            gq += dot(qkv_ref[1, 0, :, keys], gs, (1, 0))
            gk = dot(q, gs, (1, 1))
            gv = dot(go, p.astype(BF), (1, 1))
            if i == j:
                gk_ref[:, keys] = gk
                gv_ref[:, keys] = gv
            else:
                gk_ref[:, keys] += gk
                gv_ref[:, keys] += gv
        gscale += jnp.sum(gq * raw_ref[0, :, cols], axis=1, keepdims=True)
        grad_ref[0, 0, :, cols] = (gq * factor_ref[...]).astype(BF)
    grad_ref[1, 0] = gk_ref[...].astype(BF)
    grad_ref[2, 0] = gv_ref[...].astype(BF)
    gscale_ref[0] = gscale


def mask_args(series, padding):
    t = series.shape[0]
    pos = jnp.arange(t, dtype=jnp.int32)
    return series.reshape(1, t), series.reshape(t, 1), jnp.where(padding == 0, pos, t).reshape(t, 1)


def attention_forward(at, qkv, masks, pieces=0):
    _, heads, hd, t = qkv.shape
    block = min(256, t) if t <= 2048 else 512
    n = t // block
    whole = lambda shape: pl.BlockSpec(shape, lambda h: (0,) * len(shape))
    return pl.pallas_call(
        functools.partial(forward_kernel, block),
        grid=(heads,),
        in_specs=[
            pl.BlockSpec(memory_space=pltpu.SMEM),
            pl.BlockSpec((3, 1, hd, t), lambda h: (0, h, 0, 0)),
            whole((1, t)),
            whole((t, 1)),
            whole((t, 1)),
        ],
        out_specs=[
            pl.BlockSpec((1, hd, t), lambda h: (h, 0, 0)),
            pl.BlockSpec((1, 1, t), lambda h: (h, 0, 0)),
        ]
        + [pl.BlockSpec((n, 1, hd, block), lambda h: (0, h, 0, 0))] * pieces,
        out_shape=[
            jax.ShapeDtypeStruct((heads, hd, t), BF),
            jax.ShapeDtypeStruct((heads, 1, t), F32),
        ]
        + [jax.ShapeDtypeStruct((n, heads, hd, block), BF)] * pieces,
        scratch_shapes=[
            pltpu.VMEM((n * (n + 1) // 2, block, block), F32),
            pltpu.VMEM((t, hd), BF),
            pltpu.VMEM((t, block), F32),
        ],
        compiler_params=pltpu.CompilerParams(vmem_limit_bytes=VMEM_LARGE),
        cost_estimate=CHEAP,
        name="attention_forward",
    )(at, qkv, *masks)


def attention_backward(at, qkv, raw, factor, out, piece, lse, masks):
    _, heads, hd, t = qkv.shape
    block = min(256, t) if t <= 2048 else 512
    n = t // block
    whole = lambda shape: pl.BlockSpec(shape, lambda h: (0,) * len(shape))
    head = lambda wide=t: pl.BlockSpec((1, hd, wide), lambda h: (h, 0, 0))
    return pl.pallas_call(
        functools.partial(backward_kernel, block),
        grid=(heads,),
        in_specs=[
            pl.BlockSpec(memory_space=pltpu.SMEM),
            pl.BlockSpec((3, 1, hd, t), lambda h: (0, h, 0, 0)),
            head(),
            whole((hd, 1)),
            head(),
            pl.BlockSpec((1, 1, t), lambda h: (h, 0, 0)),
            whole((1, t)),
            whole((t, 1)),
            whole((t, 1)),
        ]
        + [pl.BlockSpec((piece.shape[0], 1, hd, piece.shape[3]), lambda h: (0, h, 0, 0))],
        out_specs=[
            pl.BlockSpec((3, 1, hd, t), lambda h: (0, h, 0, 0)),
            pl.BlockSpec((1, hd, 1), lambda h: (h, 0, 0)),
        ],
        out_shape=[
            jax.ShapeDtypeStruct((3, heads, hd, t), BF),
            jax.ShapeDtypeStruct((heads, hd, 1), F32),
        ],
        scratch_shapes=[
            pltpu.VMEM((n * (n + 1) // 2, block, block), F32),
            pltpu.VMEM((t, hd), BF),
            pltpu.VMEM((t, hd), BF),
            pltpu.VMEM((hd, t), F32),
            pltpu.VMEM((hd, t), F32),
            pltpu.VMEM((hd, t), BF),
        ],
        compiler_params=pltpu.CompilerParams(vmem_limit_bytes=VMEM_LARGE),
        cost_estimate=CHEAP,
        name="attention_backward",
    )(at, qkv, raw, factor, out, lse, *masks, piece)


def norm_scale(x):
    return lax.rsqrt(jnp.mean(x * x, axis=1, keepdims=True) + EPS)


def body_any(
    inputs, gain_attn, w_qkv, query_scale, w_out, gain_mlp, w_up, b_up, w_down, b_down, series_ids, pad_mask, cotangent
):
    rows, cols = size("row"), size("col")
    tok = inputs.shape[0]
    feat = inputs.shape[1]
    share = tok // cols
    t = series_ids.shape[0]
    head_rows = w_qkv.shape[2] // cols
    heads = head_rows // HEAD_DIM
    r, c = lax.axis_index("row"), lax.axis_index("col")

    blocks = gather_grid(inputs)
    strips = [jnp.concatenate(b, axis=1) for b in blocks]
    x_own = strips[0] if rows == 2 else lax.dynamic_index_in_dim(jnp.stack(strips), r, 0, keepdims=False)
    x_all = jnp.concatenate(flip(strips, "row"), axis=0)
    gain_one = jnp.concatenate(gather(gain_attn, "col"))
    gain_two = jnp.concatenate(gather(gain_mlp, "col"))
    bias_up = jnp.concatenate(gather(b_up, "row")).astype(F32)
    bias_down = jnp.concatenate(gather(b_down, "col")).astype(F32)

    w3 = jnp.transpose(w_qkv, (1, 0, 2)).reshape(3, feat, cols, head_rows)
    w_mine = lax.dynamic_index_in_dim(w3, c, 2, keepdims=False)
    w_give = lax.dynamic_index_in_dim(w3, 1 - c, 2, keepdims=False)
    w_half = swap(core_half(w_give, 1), "col")
    w_other = swap(w_half, "core")
    first = lax.axis_index("core") == 0
    w_full = jnp.concatenate(
        [w_mine, jnp.where(first, w_half, w_other), jnp.where(first, w_other, w_half)], axis=1
    )

    xf = x_all.astype(F32)
    scale_one = norm_scale(xf)
    normed_one = (xf * scale_one * gain_one).astype(BF)
    projected = jnp.einsum("td,sdh->sht", normed_one, w_full, preferred_element_type=F32)
    projected = projected.reshape(3, heads, HEAD_DIM, t)
    factor = QUERY_CONST / math.sqrt(HEAD_DIM) * jax.nn.softplus(query_scale)
    raw_q = projected[0]
    qkv = jnp.stack([raw_q * factor[None, :, None], projected[1], projected[2]]).astype(BF)
    masks = mask_args(series_ids, pad_mask)
    at = jnp.zeros((4,), jnp.int32)
    attended, lse = attention_forward(at, qkv, masks)

    def to_tokens(y):
        y = flip_dim(y.reshape(head_rows, rows, cols, share), "row", 1)
        y = flip_dim(y, "col", 2)
        y = exchange(y.reshape(1, head_rows, rows, cols, share), "row", 2, 0)
        y = exchange(y.reshape(rows, 1, head_rows, cols, share), "col", 3, 1)
        y = flip_dim(y.reshape(rows, cols, head_rows, share), "col", 1)
        return y.reshape(rows * cols * head_rows, share)

    def to_heads(y):
        y = flip_dim(y.reshape(rows, cols, head_rows, share), "col", 1)
        y = exchange(y.reshape(rows, cols, head_rows, 1, share), "col", 1, 3)
        y = exchange(y.reshape(rows, head_rows, 1, cols, share), "row", 0, 2)
        y = flip_dim(y.reshape(head_rows, rows, cols, share), "col", 2)
        return flip_dim(y, "row", 1).reshape(head_rows, t)

    w_out_all = weight_gather(w_out, 0)
    w_up_all = weight_gather(w_up, 1)
    w_down_all = weight_gather(w_down, 0)

    def my_share(y):
        return lax.dynamic_slice_in_dim(y, c * share, share, 0)

    att = to_tokens(attended.reshape(head_rows, t))
    x_mine = my_share(x_own).astype(F32)
    middle = x_mine + dot(att, w_out_all, (0, 0))
    scale_two = norm_scale(middle)
    normed_two = (middle * scale_two * gain_two).astype(BF)
    pre_act = dot(normed_two, w_up_all, (1, 0)) + bias_up
    sig = jax.nn.sigmoid(pre_act)
    hidden = (pre_act * sig).astype(BF)
    result = (middle + dot(hidden, w_down_all, (1, 0)) + bias_down).astype(BF)

    def to_block(y):
        mine, theirs = jnp.split(y, 2, axis=1)
        return jnp.concatenate(flip([mine, swap(theirs, "col")], "col"), axis=0)

    layer_out = to_block(result)

    g_give = lax.dynamic_slice_in_dim(cotangent, (1 - c) * share, share, 0)
    g = jnp.concatenate([my_share(cotangent), swap(g_give, "col")], axis=1)
    grad_w_down = dot(hidden, g, (0, 0))
    grad_hidden = dot(g, w_down_all, (1, 1))
    grad_pre_f = grad_hidden * sig * (1.0 + pre_act * (1.0 - sig))
    grad_pre = grad_pre_f.astype(BF)
    grad_b_up = jnp.sum(grad_pre.astype(F32), axis=0)
    grad_w_up = dot(normed_two, grad_pre, (0, 0))
    grad_normed_two = dot(grad_pre, w_up_all, (1, 1))
    weighted = grad_normed_two * gain_two
    inner = jnp.sum(weighted * middle, axis=1, keepdims=True)
    grad_middle = g.astype(F32) + scale_two * weighted - middle * (scale_two**3 * inner / D)
    grad_gain_mlp = jnp.sum(grad_normed_two * middle * scale_two, axis=0)
    grad_branch = grad_middle.astype(BF)
    grad_w_out = dot(att, grad_branch, (1, 0))
    grad_att = dot(w_out_all, grad_branch, (1, 1)).astype(BF)
    grad_attended = to_heads(grad_att).reshape(heads, HEAD_DIM, t)
    grad_middle_block = to_block(grad_middle)

    sum_down = weight_sum(grad_w_down, 0)
    sum_up = weight_sum(grad_w_up, 1)
    sum_out = weight_sum(grad_w_out, 0)

    grad_proj, gscale = attention_backward(
        at, qkv, raw_q, factor.reshape(HEAD_DIM, 1), attended, grad_attended[None], lse, masks
    )
    slope = QUERY_CONST / math.sqrt(HEAD_DIM) * jax.nn.sigmoid(query_scale)
    grad_query_scale = jnp.sum(gscale, axis=(0, 2)) * slope
    grad_proj = grad_proj.reshape(3, head_rows, t)
    grad_normed_one = jnp.einsum("sht,sdh->td", grad_proj, w_full, preferred_element_type=F32)
    weighted_one = grad_normed_one * gain_one
    inner_one = jnp.sum(weighted_one * xf, axis=1)
    grad_gain_attn = jnp.sum(grad_normed_one * xf * scale_one, axis=0)
    inner_one = lax.psum(inner_one, ("row", "col"))
    grad_w = jnp.einsum("td,sht->sdh", normed_one, grad_proj, preferred_element_type=F32)
    grad_w = grad_w.reshape(3, cols, 2, feat // 2, head_rows)
    core = lax.axis_index("core")
    keep = lax.dynamic_index_in_dim(grad_w, core, 2, keepdims=False)
    give = lax.dynamic_index_in_dim(grad_w, 1 - core, 2, keepdims=False).astype(BF)
    part = (keep + swap(give, "core").astype(F32)).astype(BF)
    part = jnp.concatenate(flip([part[:, 0], swap(part[:, 1], "col")], "col"), axis=2)
    sum_qkv = jnp.transpose(z_sum(part), (1, 0, 2))

    e = jnp.concatenate(flip(jnp.split(grad_normed_one.astype(BF), 2, axis=0), "row"), axis=0) if rows == 2 else (
        grad_normed_one.astype(BF)
    )
    e = scatter_sum(e, "row", 0)
    e = scatter_sum(e, "col", 1).astype(F32)
    my_rows = lambda y: lax.dynamic_slice_in_dim(y, r * tok, tok, 0)
    scale_mine = my_rows(scale_one)
    inner_mine = my_rows(inner_one.reshape(t, 1))
    grad_inputs = grad_middle_block + scale_mine * (e * gain_attn) - inputs.astype(F32) * (
        scale_mine**3 * inner_mine / D
    )

    grad_b_down = jnp.sum(g.astype(F32), axis=0)
    vectors = jnp.concatenate(
        [
            flip_dim(grad_gain_attn, "col", 0),
            flip_dim(grad_gain_mlp, "col", 0),
            flip_dim(grad_b_down, "col", 0),
            flip_dim(grad_b_up, "row", 0),
            grad_query_scale,
        ]
    )
    vectors = lax.psum(vectors, ("z", "core", "row", "col"))
    mine_col = lambda at: lax.dynamic_slice_in_dim(vectors, at * D + c * feat, feat, 0)
    units = b_up.shape[0]
    return (
        layer_out,
        grad_inputs,
        mine_col(0),
        sum_qkv,
        vectors[4 * D :],
        sum_out,
        mine_col(1),
        sum_up,
        lax.dynamic_slice_in_dim(vectors, 3 * D + r * units, units, 0),
        sum_down,
        mine_col(2),
    )


SMEM = pl.BlockSpec(memory_space=pltpu.SMEM)
ANY = pl.BlockSpec(memory_space=pl.ANY)


def call(kernel, name, args, specs, outs, scratch=(), limit=VMEM_LIMIT):
    return pl.pallas_call(
        kernel,
        in_specs=specs,
        out_shape=outs,
        scratch_shapes=list(scratch),
        compiler_params=pltpu.CompilerParams(vmem_limit_bytes=limit),
        cost_estimate=CHEAP,
        name=name,
    )(*args)


VM = pl.BlockSpec(memory_space=pltpu.VMEM)


def shape(dims, kind):
    return jax.ShapeDtypeStruct(dims, kind)


def project_kernel(
    at, x00, x01, x10, x11, gain, factor, w_mine, w_a, w_b, qkv, raw, normed, scale_own, w_full
):
    r, k = at[0], at[2]
    tok, feat = x00.shape
    hr = w_mine.shape[1]
    half = hr // 2
    for s in range(3):
        w_full[pl.ds(s * hr, hr), 0:feat] = w_mine[s]
        w_full[pl.ds(pl.multiple_of(s * hr + k * half, 16), half), feat:] = w_a[s]
        w_full[pl.ds(pl.multiple_of(s * hr + (1 - k) * half, 16), half), feat:] = w_b[s]
    for i, (a_ref, b_ref) in enumerate(((x00, x01), (x10, x11))):
        a, b = a_ref[...].astype(F32), b_ref[...].astype(F32)
        total = jnp.sum(a * a, axis=1, keepdims=True) + jnp.sum(b * b, axis=1, keepdims=True)
        scale = lax.rsqrt(total / (2 * feat) + EPS)
        if i == 0:
            scale_own[...] = scale
        rows = pl.ds(pl.multiple_of((r ^ i) * tok, tok), tok)
        normed[rows, 0:feat] = (a * scale * gain[:, 0:feat]).astype(BF)
        normed[rows, feat:] = (b * scale * gain[:, feat:]).astype(BF)
        y = normed[rows, :]
        q = dot(w_full[0:hr, :], y, (1, 1))
        raw[:, rows] = q
        qkv[0, :, rows] = (q * factor[...]).astype(BF)
        qkv[1, :, rows] = dot(w_full[hr : 2 * hr, :], y, (1, 1)).astype(BF)
        qkv[2, :, rows] = dot(w_full[2 * hr : 3 * hr, :], y, (1, 1)).astype(BF)


def feed_kernel(
    at, a, x_own, x_col, g_own, g_col, gain, bias_up, bias_down,
    w_out, w_up, w_down, hx, hy, d0, d1, hx2, hy2, d02, d12,
    out_own, gm_own, post, ts, vectors,
    *rest,
):
    *grads, w, att, turned, sems = rest
    r, c, k = at[0], at[1], at[2]
    _, hr, share = a.shape
    feat = x_own.shape[1]
    half = feat // 2
    quarter = half // 2
    copies = []
    for n, shard in enumerate((w_out, w_up, w_down)):
        rx, cx, ry, cy = (0, feat, feat, 0) if n == 1 else (feat, 0, 0, feat)
        mine = []
        mine.append((shard, w.at[n, 0:feat, 0:feat]))
        for core, (px, py, p0, p1) in ((k, (hx, hy, d0, d1)), (1 - k, (hx2, hy2, d02, d12))):
            down = core * half
            at_x = pl.ds(pl.multiple_of(rx + down, 16), half)
            at_y = pl.ds(pl.multiple_of(ry + down, 16), half)
            first = d0.shape[1]
            at_0 = pl.ds(pl.multiple_of(feat + down, 16), first)
            at_1 = pl.ds(pl.multiple_of(feat + down + first, 16), half - first)
            mine.append((px.at[n], w.at[n, at_x, cx : cx + feat]))
            mine.append((py.at[n], w.at[n, at_y, cy : cy + feat]))
            mine.append((p0.at[n], w.at[n, at_0, feat : 2 * feat]))
            mine.append((p1.at[n], w.at[n, at_1, feat : 2 * feat]))
        started = []
        for m, (src, dst) in enumerate(mine):
            copy = pltpu.make_async_copy(src, dst, sems.at[n, m])
            copy.start()
            started.append(copy)
        copies.append(started)

    rows = pl.ds(pl.multiple_of(c * share, share), share)
    for s in range(4):
        to = ((s // 2) ^ r) * 2 * hr + (s % 2) * hr
        att[pl.ds(pl.multiple_of(to, 16), hr), :] = a[s]
    x = jnp.concatenate([x_own[rows, :], x_col[rows, :]], axis=1).astype(F32)
    g = jnp.concatenate([g_own[rows, :], g_col[...]], axis=1)
    for copy in copies[0]:
        copy.wait()
    middle = x + dot(att[...], w[0], (0, 0))
    scale = lax.rsqrt(jnp.sum(middle * middle, axis=1, keepdims=True) / D + EPS)
    normed = (middle * scale * gain[...]).astype(BF)
    for copy in copies[1]:
        copy.wait()
    pre = dot(normed, w[1], (1, 0)) + bias_up[...]
    sig = jax.nn.sigmoid(pre)
    hidden = (pre * sig).astype(BF)
    for copy in copies[2]:
        copy.wait()
    result = (middle + dot(hidden, w[2], (1, 0)) + bias_down[...]).astype(BF)
    out_own[...] = result[:, :feat]
    post[0] = result[:, feat:]

    def weight_grad(n, left_ref, right):
        for core, sets in ((k, grads[:8]), (1 - k, grads[8:])):
            by_row, by_col = sets[:4], sets[4:]
            up, low = (by_col, by_row) if n == 1 else (by_row, by_col)
            for b in range(2):
                part = pl.ds(pl.multiple_of(b * feat + core * half, 16), half)
                y = dot(left_ref[part, :], right, (1, 0)).astype(BF)
                for j in range(2):
                    cut = slice(j * feat, (j + 1) * feat)
                    up[2 * j + (1 - b)][n] = y[:quarter, cut]
                    low[2 * b + (1 - j)][n] = y[quarter:, cut]

    turned[...] = hidden.astype(F32).T.astype(BF)
    grad_pre_f = dot(g, w[2], (1, 1)) * sig * (1.0 + pre * (1.0 - sig))
    grad_pre = grad_pre_f.astype(BF)
    weight_grad(2, turned, g)
    grad_normed = dot(grad_pre, w[1], (1, 1))
    weighted = grad_normed * gain[...]
    inner = jnp.sum(weighted * middle, axis=1, keepdims=True)
    gf = g.astype(F32)
    grad_middle = gf + scale * weighted - middle * (scale * scale * scale * inner / D)
    gm_own[...] = grad_middle[:, :feat]
    post[1] = grad_middle[:, feat:].astype(BF)
    branch = grad_middle.astype(BF)
    for s in range(4):
        come = ((s // 2) ^ r) * 2 * hr + (s % 2) * hr
        ts[s] = dot(w[0, pl.ds(pl.multiple_of(come, 16), hr), :], branch, (1, 1)).astype(BF)
    turned[...] = normed.astype(F32).T.astype(BF)
    weight_grad(1, turned, grad_pre)
    weight_grad(0, att, branch)
    vectors[...] = jnp.concatenate(
        [
            jnp.sum(grad_normed * (middle * scale), axis=0, keepdims=True),
            jnp.sum(gf, axis=0, keepdims=True),
            jnp.sum(grad_pre.astype(F32), axis=0, keepdims=True),
        ],
        axis=0,
    )


def weight_back_kernel(at, grad, normed, keep, give):
    k = at[2]
    part = keep.shape[2]
    feat = keep.shape[3]
    for ref, core in ((give, 1 - k), (keep, k)):
        for s in range(3):
            rows = pl.ds(pl.multiple_of(core * part, 16), part)
            y = dot(grad[s, rows, :], normed[...], (1, 0)).astype(BF)
            ref[0, s] = y[:, :feat]
            ref[1, s] = y[:, feat:]


def project_back_kernel(
    at, grad, w_full, x00, x01, x10, x11, gain, es, gain_sum
):
    r, c = at[0], at[1]
    tok, feat = x00.shape
    sums = [jnp.zeros((1, feat), F32), jnp.zeros((1, feat), F32)]
    for i, xs in enumerate(((x00, x01), (x10, x11))):
        rows = pl.ds(pl.multiple_of((r ^ i) * tok, tok), tok)
        left = grad[:, rows]
        products, squares, inner = [], 0.0, 0.0
        for j in range(2):
            cut = slice(j * feat, (j + 1) * feat)
            e = dot(left, w_full[:, cut], (0, 0))
            x = xs[j][...].astype(F32)
            product = e * x
            inner = inner + jnp.sum(product * gain[:, cut], axis=1, keepdims=True)
            squares = squares + jnp.sum(x * x, axis=1, keepdims=True)
            es[2 * (r ^ i) + (c ^ j), 0:tok, :] = e.astype(BF)
            products.append(product)
        scale = lax.rsqrt(squares / (2 * feat) + EPS)
        for j in range(2):
            sums[j] += jnp.sum(products[j] * scale, axis=0, keepdims=True)
        line = jnp.broadcast_to(inner, (tok, 128)).T[0:1, :]
        high = line.astype(BF).astype(F32)
        extra = jnp.concatenate([high, line - high, jnp.zeros((14, tok), F32)], axis=0)
        extra = jnp.concatenate([extra, jnp.zeros((16, feat - tok), F32)], axis=1).astype(BF)
        for j in range(2):
            es[2 * (r ^ i) + (c ^ j), tok:, :] = extra
    gain_sum[:, 0:feat] = sums[0]
    gain_sum[:, feat:] = sums[1]


def finish_qkv_kernel(at, mine, theirs, mine2, theirs2, out, rows):
    c, k = at[1], at[2]
    half = mine.shape[1]
    for s in range(3):
        for ref, col, core in ((mine, c, k), (theirs, 1 - c, k), (mine2, c, 1 - k), (theirs2, 1 - c, 1 - k)):
            rows[pl.ds(pl.multiple_of((2 * col + core) * half, 16), half), :] = ref[s].astype(F32)
        out[s] = rows[...].T


def finish_feed_kernel(at, a, b, a2, b2, *outs):
    k = at[2]
    quarter = a.shape[1]
    for n, out in enumerate(outs):
        upper, lower = ((b, b2), (a, a2)) if n == 1 else ((a, a2), (b, b2))
        for i, core in ((0, k), (1, 1 - k)):
            for j, refs in enumerate((upper, lower)):
                to = pl.multiple_of((2 * core + j) * quarter, 16)
                out[pl.ds(to, quarter), :] = refs[i][n].astype(F32)


together = lax.optimization_barrier


def after(x, *earlier):
    return lax.optimization_barrier((x, *earlier))[0]


def add(*parts):
    total = parts[0].astype(F32)
    for part in parts[1:]:
        total = total + part.astype(F32)
    return total.astype(BF)


def all_four(x):
    return lax.all_to_all(x, ("row", "col"), 0, 0, tiled=True)


def z_swap(x, step):
    n = size("z")
    return lax.ppermute(x, "z", [(i, i ^ step) for i in range(n)])


def z_first():
    z = lax.axis_index("z")
    return (z == 0) | (z == 3)


def body_four(
    inputs, gain_attn, w_qkv, query_scale, w_out, gain_mlp, w_up, b_up, w_down, b_down, series_ids, pad_mask, cotangent
):
    tok, feat = inputs.shape
    share = tok // 2
    t = series_ids.shape[0]
    hr = w_qkv.shape[2] // 2
    heads = hr // HEAD_DIM
    half = feat // 2
    r, c, k = lax.axis_index("row"), lax.axis_index("col"), lax.axis_index("core")
    at = jnp.stack([r, c, k, 2 * r + c]).astype(jnp.int32)
    mine_rows = lambda y, part: lax.dynamic_slice_in_dim(y, part * share, share, 0)

    few = heads // 2
    quarter = half // 2
    first_rows = (half * 7 // 20) // 16 * 16
    x01 = swap(inputs, "col")
    x10 = swap(inputs, "row")
    small = swap(jnp.concatenate([gain_attn, gain_mlp, b_down.astype(F32)]), "col")
    up_other = swap(b_up.astype(F32), "row")
    w_turned = jnp.transpose(w_qkv, (1, 2, 0)).reshape(3, 2, hr, feat)
    w_mine = lax.dynamic_index_in_dim(w_turned, c, 1, keepdims=False)
    w_give = lax.dynamic_index_in_dim(w_turned, 1 - c, 1, keepdims=False)
    w_half = core_half(w_give, 1)
    w_a = swap(w_half, "col")
    part = jnp.stack([core_half(w_out, 0), core_half(w_up, 0), core_half(w_down, 0)])
    g_give = mine_rows(cotangent, 1 - c)
    x01, x10, small, up_other, part, g_give, w_mine = lax.optimization_barrier(
        (x01, x10, small, up_other, part, g_give, w_mine)
    )
    x11 = swap(after(x01, w_half), "row")
    w_b = swap(w_a, "core")
    gain_one = jnp.concatenate([gain_attn, small[:feat]]).reshape(1, D)
    gain_two = jnp.concatenate([gain_mlp, small[feat : 2 * feat]]).reshape(1, D)
    bias_down = jnp.concatenate([b_down.astype(F32), small[2 * feat :]]).reshape(1, D)
    bias_up = jnp.concatenate([b_up.astype(F32), up_other]).reshape(1, D)
    factor = QUERY_CONST / math.sqrt(HEAD_DIM) * jax.nn.softplus(query_scale)
    factor_col = factor.reshape(HEAD_DIM, 1)

    part = after(part, x11, w_a)
    hx, hy = swap(part, "row"), swap(part, "col")
    hx2, hy2 = swap(hx, "core"), swap(hy, "core")
    qkv, raw, normed_one, scale_own, w_full = call(
        project_kernel,
        "project",
        (at, inputs, x01, x10, x11, gain_one, jnp.tile(factor_col, (heads, 1)), w_mine, w_a, w_b),
        [SMEM] + [VM] * 9,
        [
            shape((3, hr, t), BF),
            shape((hr, t), F32),
            shape((t, D), BF),
            shape((tok, 1), F32),
            shape((3 * hr, D), BF),
        ],
        limit=VMEM_LARGE,
    )
    qkv = qkv.reshape(3, heads, HEAD_DIM, t)
    masks = mask_args(series_ids, pad_mask)
    attended, lse, a = attention_forward(at, qkv, masks, pieces=1)
    a = all_four(a.reshape(4, hr, share))
    hx_on, hy_on, g_give = lax.optimization_barrier((hx, hy, g_give, lse))[:3]
    d0 = swap(hx_on[:, :first_rows], "col")
    d1 = swap(hy_on[:, first_rows:], "row")
    g_col = swap(g_give, "col")
    d0, d1, g_col, a = together((d0, d1, g_col, a))
    d02, d12 = swap(d0, "core"), swap(d1, "core")
    out_own, gm_own, post, ts, vectors, *grads = call(
        feed_kernel,
        "feed_forward",
        (at, a, inputs, x01, cotangent, g_col, gain_two, bias_up, bias_down)
        + (w_out, w_up, w_down, hx, hy, d0, d1, hx2, hy2, d02, d12),
        [SMEM] + [VM] * 8 + [ANY] * 11,
        [
            shape((share, feat), BF),
            shape((share, feat), F32),
            shape((2, share, feat), BF),
        ]
        + [shape((4, hr, share), BF)]
        + [shape((3, D), F32)]
        + [shape((3, quarter, feat), BF)] * 16,
        scratch=[
            pltpu.VMEM((3, D, D), BF),
            pltpu.VMEM((D, share), BF),
            pltpu.VMEM((D, share), BF),
            pltpu.SemaphoreType.DMA((3, 9)),
        ],
    )
    ts = all_four(ts)
    others = grads[8:]
    over = lambda n: swap(others[n], "core")
    grads, osx0, osx1, osy0, osy1 = grads[:8], over(0), over(2), over(4), over(6)
    sx0, kx0, sx1, kx1, sy0, ky0, sy1, ky1 = grads
    sx1, sy1 = add(sx1, osx1), add(sy1, osy1)
    ox0, ox1, oy0, oy1 = over(1), over(3), over(5), over(7)
    sx0, sy0 = add(sx0, osx0), add(sy0, osy0)
    ts, sx1, sy1, sx0, sy0 = together((ts, sx1, sy1, sx0, sy0))
    rx1, ry1 = swap(sx1, "row"), swap(sy1, "col")
    rx0, ry0 = swap(sx0, "row"), swap(sy0, "col")
    ts = ts.reshape(4, heads, HEAD_DIM, share)
    raw = raw.reshape(heads, HEAD_DIM, t)

    grad_proj, gscale = attention_backward(at, qkv, raw, factor_col, attended, ts, lse, masks)
    grad_proj = grad_proj.reshape(3, hr, t)
    kept, sent = call(
        weight_back_kernel,
        "weight_back",
        (at, grad_proj, normed_one),
        [SMEM] + [VM] * 2,
        [shape((2, 3, hr // 2, feat), BF)] * 2,
    )
    sent, rx1, ry1, rx0, ry0, ox0, ox1, oy0, oy1 = together((sent, rx1, ry1, rx0, ry0, ox0, ox1, oy0, oy1))
    got = swap(sent, "core")
    px1, py1 = add(kx1, ox1, rx1), add(ky1, oy1, ry1)
    qx, qy = swap(px1, "col"), swap(py1, "row")
    w_pair = add(kept, got)
    first = z_first()
    got_w = z_swap(jnp.where(first, w_pair[1], w_pair[0]), 1)
    slope = QUERY_CONST / math.sqrt(HEAD_DIM) * jax.nn.sigmoid(query_scale)
    grad_query_scale = jnp.sum(gscale, axis=(0, 2)) * slope
    es, gain_sum = call(
        project_back_kernel,
        "project_back",
        (at, after(grad_proj, w_pair, px1, py1).reshape(3 * hr, t), w_full, inputs, x01, x10, x11, gain_one),
        [SMEM] + [VM] * 7,
        [
            shape((4, tok + 16, feat), BF),
            shape((1, D), F32),
        ],
    )
    total = jnp.concatenate([gain_sum, vectors]).reshape(4, 2, feat)
    turn = jnp.stack([c, c, c, r]).reshape(4, 1, 1) == 1
    total = jnp.where(turn, total[:, ::-1], total).reshape(8, feat)
    total = jnp.concatenate([total, jnp.pad(grad_query_scale, (0, feat - HEAD_DIM)).reshape(1, feat)])
    total = total + swap(total, "core")
    qx, qy, got_w, w_pair, es = together((qx, qy, got_w, w_pair, es))

    mine_w = add(jnp.where(first, w_pair[0], w_pair[1]), got_w)
    met_w = z_swap(mine_w, 3)
    fx, fy = add(kx0, ox0, rx0, qx), add(ky0, oy0, ry0, qy)
    got_c = z_swap(jnp.where(first, fy, fx), 1)
    es = all_four(es)
    total = total + swap(total, "row")
    total = total + swap(total, "col")
    met_w, mine_w, got_c, fx, fy, es, post, total = together((met_w, mine_w, got_c, fx, fy, es, post, total))

    mine_w = add(mine_w, met_w)
    other_w = z_swap(mine_w, 1)
    w_own, w_theirs = jnp.where(first, mine_w, other_w), jnp.where(first, other_w, mine_w)
    mine_c = add(jnp.where(first, fx, fy), got_c)
    met_c = z_swap(mine_c, 3)
    post = swap(post, "col")
    w_theirs = swap(w_theirs, "col")
    total = total + z_swap(total, 1)
    total = total + z_swap(total, 3)
    met_c, mine_c, w_own, w_theirs, post, total = together((met_c, mine_c, w_own, w_theirs, post, total))
    mine_c = add(mine_c, met_c)
    other_c = z_swap(mine_c, 1)
    w_args = (at, w_own, w_theirs, swap(w_own, "core"), swap(w_theirs, "core"))
    sum_qkv = call(
        finish_qkv_kernel,
        "finish_qkv",
        w_args,
        [SMEM] + [VM] * 4,
        shape((3, feat, 2 * hr), F32),
        scratch=[pltpu.VMEM((2 * hr, feat), F32)],
    )
    sum_qkv = jnp.transpose(sum_qkv, (1, 0, 2))

    e = jnp.sum(es[:, :tok].astype(F32), axis=0)
    inner = jnp.sum(es[:, tok : tok + 2, :tok].astype(F32), axis=(0, 1)).reshape(tok, 1)
    grad_middle = jnp.concatenate(flip([gm_own, post[1].astype(F32)], "col"), axis=0)
    grad_inputs = grad_middle + scale_own * (e * gain_attn) - inputs.astype(F32) * (scale_own**3 * inner / D)
    layer_out = jnp.concatenate(flip([out_own, post[0]], "col"), axis=0)

    pick = lambda n, place: lax.dynamic_index_in_dim(total, 2 * n + place, 0, keepdims=False)
    mine_c = after(mine_c, sum_qkv, grad_inputs, layer_out, total)
    fx, fy = jnp.where(first, mine_c, other_c), jnp.where(first, other_c, mine_c)
    sum_out, sum_up, sum_down = call(
        finish_feed_kernel,
        "finish_feed",
        (at, fx, fy, swap(fx, "core"), swap(fy, "core")),
        [SMEM] + [VM] * 4,
        [shape((feat, feat), F32)] * 3,
    )

    return (
        layer_out,
        grad_inputs,
        pick(0, c),
        sum_qkv,
        total[8, :HEAD_DIM],
        sum_out,
        pick(1, c),
        sum_up,
        pick(3, r),
        sum_down,
        pick(2, c),
    )


def solution(mesh):
    dp, rows, cols = mesh.shape["dp"], mesh.shape["row"], mesh.shape["col"]
    split = Mesh(mesh.devices.reshape(dp // 2, 2, rows, cols), ("z", "core", "row", "col"))
    tokens = P(("z", "core", "row"), "col")
    in_specs = (
        tokens,
        P("col"),
        P("col", None, "row"),
        P(),
        P("row", "col"),
        P("col"),
        P("col", "row"),
        P("row"),
        P("row", "col"),
        P("col"),
        P(("z", "core")),
        P(("z", "core")),
        tokens,
    )
    out_specs = (
        tokens,
        tokens,
        P("col"),
        P("col", None, "row"),
        P(),
        P("row", "col"),
        P("col"),
        P("col", "row"),
        P("row"),
        P("row", "col"),
        P("col"),
    )
    body = body_four if (dp, rows, cols) == (8, 2, 2) else body_any
    return jax.shard_map(body, mesh=split, in_specs=in_specs, out_specs=out_specs, check_vma=False)
```

```python
import functools
import math

import jax
import jax.numpy as jnp
from jax import lax
from jax.experimental import pallas as pl
from jax.experimental.pallas import tpu as pltpu
from jax.sharding import Mesh
from jax.sharding import PartitionSpec as P

D = 1280
HEAD_DIM = 80
EPS = 1e-06
QUERY_CONST = 1.442695041
MASKED = -1e30
BF = jnp.bfloat16
F32 = jnp.float32
VMEM_LIMIT = 24 * 1024 * 1024
VMEM_LARGE = 50 * 1024 * 1024
CHEAP = pl.CostEstimate(flops=1, bytes_accessed=1, transcendentals=0)


def size(axis):
    return lax.axis_size(axis)


def swap(x, axis):
    return lax.ppermute(x, axis, [(0, 1), (1, 0)])


def flip(blocks, axis):
    if size(axis) != 2:
        return list(blocks)
    first = lax.axis_index(axis) == 0
    a, b = blocks
    return [jnp.where(first, a, b), jnp.where(first, b, a)]


def flip_dim(x, axis, dim):
    if size(axis) != 2:
        return x
    return jnp.concatenate(flip(jnp.split(x, 2, axis=dim), axis), axis=dim)


def gather(x, axis):
    if size(axis) == 2:
        return [x, swap(x, axis)]
    whole = lax.all_gather(x, axis, axis=0, tiled=False)
    return [whole[i] for i in range(size(axis))]


def gather_grid(x):
    if size("row") != 2:
        return [gather(b, "col") for b in gather(x, "row")]
    along_row, along_col = swap(x, "row"), swap(x, "col")
    half = x.shape[0] // 2
    across = jnp.concatenate(
        [swap(along_row[:half], "col"), swap(along_col[half:], "row")], axis=0
    )
    return [[x, along_col], [along_row, across]]


def scatter_sum(x, axis, dim):
    if size(axis) != 2:
        return lax.psum_scatter(x, axis, scatter_dimension=dim, tiled=True)
    mine, theirs = jnp.split(x, 2, axis=dim)
    return (mine.astype(F32) + swap(theirs, axis).astype(F32)).astype(x.dtype)


def exchange(x, axis, split, join):
    if size(axis) != 2:
        return lax.all_to_all(x, axis, split, join, tiled=True)
    mine, theirs = jnp.split(x, 2, axis=split)
    return jnp.concatenate([mine, swap(theirs, axis)], axis=join)


def core_half(x, dim):
    return lax.dynamic_slice_in_dim(
        x, lax.axis_index("core") * (x.shape[dim] // 2), x.shape[dim] // 2, dim
    )


def weight_gather(w, row_dim):
    part = core_half(w, 0)
    blocks = gather_grid(part)
    if row_dim == 1:
        blocks = [list(b) for b in zip(*blocks)]
    mine = jnp.stack([jnp.concatenate(b, axis=1) for b in blocks])
    other = swap(mine, "core")
    first = lax.axis_index("core") == 0
    both = jnp.stack([jnp.where(first, mine, other), jnp.where(first, other, mine)], axis=1)
    return both.reshape(-1, both.shape[-1])


def weight_sum(g, row_dim):
    dim_axis = ("row", "col") if row_dim == 0 else ("col", "row")
    n0 = size(dim_axis[0])
    g = g.reshape(n0, 2, g.shape[0] // n0 // 2, g.shape[1])
    core = lax.axis_index("core")
    keep = lax.dynamic_index_in_dim(g, core, 1, keepdims=False)
    give = lax.dynamic_index_in_dim(g, 1 - core, 1, keepdims=False).astype(BF)
    part = (keep + swap(give, "core").astype(F32)).astype(BF)
    part = scatter_sum(part, dim_axis[0], 0)
    part = scatter_sum(part[0], dim_axis[1], 1)
    return z_sum(part)


def z_sum(part):
    total = lax.psum(part, "z")
    other = swap(total, "core")
    return flip_core(total, other)


def flip_core(total, other):
    first = lax.axis_index("core") == 0
    return jnp.concatenate(
        [jnp.where(first, total, other), jnp.where(first, other, total)], axis=-2
    ).astype(F32)


def dot(a, b, contract):
    return lax.dot_general(a, b, ((contract[0:1], contract[1:2]), ((), ())), preferred_element_type=F32)


def bias_block(series_row, series_col, key_pos, q0, k0, qb, kb, diagonal):
    q_pos = q0 + lax.broadcasted_iota(jnp.int32, (1, qb), 1)
    allowed = (series_col == series_row) & (key_pos <= q_pos)
    if diagonal:
        k_pos = k0 + lax.broadcasted_iota(jnp.int32, (kb, 1), 0)
        allowed = allowed | (k_pos == q_pos)
    return jnp.where(allowed, 0.0, MASKED)


def forward_kernel(block, at, qkv_ref, srow_ref, scol_ref, kpos_ref, out_ref, lse_ref, *rest):
    *pieces, bias_ref, krow_ref, s_ref = rest
    t = qkv_ref.shape[3]
    n = t // block
    krow_ref[...] = qkv_ref[1, 0].astype(F32).T.astype(BF)

    def bias_slot(j, i):
        return j * (j + 1) // 2 + i

    @pl.when(pl.program_id(0) == 0)
    def _():
        for j in range(n):
            for i in range(j + 1):
                keys = pl.ds(i * block, block)
                bias_ref[bias_slot(j, i)] = bias_block(
                    srow_ref[:, j * block : (j + 1) * block],
                    scol_ref[keys, :],
                    kpos_ref[keys, :],
                    j * block,
                    i * block,
                    block,
                    block,
                    i == j,
                )

    for j in range(n):
        cols = slice(j * block, (j + 1) * block)
        q = qkv_ref[0, 0, :, cols]
        top = None
        for i in range(j + 1):
            s = dot(krow_ref[i * block : (i + 1) * block, :], q, (1, 0)) + bias_ref[bias_slot(j, i)]
            s_ref[i * block : (i + 1) * block, :] = s
            here = jnp.max(s, axis=0, keepdims=True)
            top = here if top is None else jnp.maximum(top, here)
        total = jnp.zeros((1, block), F32)
        acc = jnp.zeros((HEAD_DIM, block), F32)
        for i in range(j + 1):
            p = jnp.exp(s_ref[i * block : (i + 1) * block, :] - top)
            total += jnp.sum(p, axis=0, keepdims=True)
            acc += dot(qkv_ref[2, 0, :, i * block : (i + 1) * block], p.astype(BF), (1, 0))
        found = (acc / total).astype(BF)
        out_ref[0, :, cols] = found
        if pieces:
            pieces[0][j, 0] = found
        lse_ref[0, :, cols] = top + jnp.log(total)


def backward_kernel(
    block, at, qkv_ref, raw_ref, factor_ref, out_ref, lse_ref, srow_ref, scol_ref, kpos_ref, *rest
):
    piece, grad_ref, gscale_ref, bias_ref, krow_ref, vrow_ref, gk_ref, gv_ref, gout_ref = rest
    wide = piece.shape[3]
    for j in range(piece.shape[0]):
        gout_ref[:, j * wide : (j + 1) * wide] = piece[j, 0]
    t = qkv_ref.shape[3]
    n = t // block
    krow_ref[...] = qkv_ref[1, 0].astype(F32).T.astype(BF)
    vrow_ref[...] = qkv_ref[2, 0].astype(F32).T.astype(BF)

    def bias_slot(j, i):
        return j * (j + 1) // 2 + i

    @pl.when(pl.program_id(0) == 0)
    def _():
        for j in range(n):
            for i in range(j + 1):
                keys = pl.ds(i * block, block)
                bias_ref[bias_slot(j, i)] = bias_block(
                    srow_ref[:, j * block : (j + 1) * block],
                    scol_ref[keys, :],
                    kpos_ref[keys, :],
                    j * block,
                    i * block,
                    block,
                    block,
                    i == j,
                )

    gscale = jnp.zeros((HEAD_DIM, 1), F32)
    for j in range(n):
        cols = slice(j * block, (j + 1) * block)
        q = qkv_ref[0, 0, :, cols]
        go = gout_ref[:, cols]
        lse = lse_ref[0, :, cols]
        delta = jnp.sum(go.astype(F32) * out_ref[0, :, cols].astype(F32), axis=0, keepdims=True)
        gq = jnp.zeros((HEAD_DIM, block), F32)
        for i in range(j + 1):
            keys = slice(i * block, (i + 1) * block)
            s = dot(krow_ref[keys, :], q, (1, 0)) + bias_ref[bias_slot(j, i)]
            p = jnp.exp(s - lse)
            gp = dot(vrow_ref[keys, :], go, (1, 0))
            gs = (p * (gp - delta)).astype(BF)
            gq += dot(qkv_ref[1, 0, :, keys], gs, (1, 0))
            gk = dot(q, gs, (1, 1))
            gv = dot(go, p.astype(BF), (1, 1))
            if i == j:
                gk_ref[:, keys] = gk
                gv_ref[:, keys] = gv
            else:
                gk_ref[:, keys] += gk
                gv_ref[:, keys] += gv
        gscale += jnp.sum(gq * raw_ref[0, :, cols], axis=1, keepdims=True)
        grad_ref[0, 0, :, cols] = (gq * factor_ref[...]).astype(BF)
    grad_ref[1, 0] = gk_ref[...].astype(BF)
    grad_ref[2, 0] = gv_ref[...].astype(BF)
    gscale_ref[0] = gscale


def mask_args(series, padding):
    t = series.shape[0]
    pos = jnp.arange(t, dtype=jnp.int32)
    return series.reshape(1, t), series.reshape(t, 1), jnp.where(padding == 0, pos, t).reshape(t, 1)


def attention_forward(at, qkv, masks, pieces=0):
    _, heads, hd, t = qkv.shape
    block = min(256, t) if t <= 2048 else 512
    n = t // block
    whole = lambda shape: pl.BlockSpec(shape, lambda h: (0,) * len(shape))
    return pl.pallas_call(
        functools.partial(forward_kernel, block),
        grid=(heads,),
        in_specs=[
            pl.BlockSpec(memory_space=pltpu.SMEM),
            pl.BlockSpec((3, 1, hd, t), lambda h: (0, h, 0, 0)),
            whole((1, t)),
            whole((t, 1)),
            whole((t, 1)),
        ],
        out_specs=[
            pl.BlockSpec((1, hd, t), lambda h: (h, 0, 0)),
            pl.BlockSpec((1, 1, t), lambda h: (h, 0, 0)),
        ]
        + [pl.BlockSpec((n, 1, hd, block), lambda h: (0, h, 0, 0))] * pieces,
        out_shape=[
            jax.ShapeDtypeStruct((heads, hd, t), BF),
            jax.ShapeDtypeStruct((heads, 1, t), F32),
        ]
        + [jax.ShapeDtypeStruct((n, heads, hd, block), BF)] * pieces,
        scratch_shapes=[
            pltpu.VMEM((n * (n + 1) // 2, block, block), F32),
            pltpu.VMEM((t, hd), BF),
            pltpu.VMEM((t, block), F32),
        ],
        compiler_params=pltpu.CompilerParams(vmem_limit_bytes=VMEM_LARGE),
        cost_estimate=CHEAP,
        name="attention_forward",
    )(at, qkv, *masks)


def attention_backward(at, qkv, raw, factor, out, piece, lse, masks):
    _, heads, hd, t = qkv.shape
    block = min(256, t) if t <= 2048 else 512
    n = t // block
    whole = lambda shape: pl.BlockSpec(shape, lambda h: (0,) * len(shape))
    head = lambda wide=t: pl.BlockSpec((1, hd, wide), lambda h: (h, 0, 0))
    return pl.pallas_call(
        functools.partial(backward_kernel, block),
        grid=(heads,),
        in_specs=[
            pl.BlockSpec(memory_space=pltpu.SMEM),
            pl.BlockSpec((3, 1, hd, t), lambda h: (0, h, 0, 0)),
            head(),
            whole((hd, 1)),
            head(),
            pl.BlockSpec((1, 1, t), lambda h: (h, 0, 0)),
            whole((1, t)),
            whole((t, 1)),
            whole((t, 1)),
        ]
        + [pl.BlockSpec((piece.shape[0], 1, hd, piece.shape[3]), lambda h: (0, h, 0, 0))],
        out_specs=[
            pl.BlockSpec((3, 1, hd, t), lambda h: (0, h, 0, 0)),
            pl.BlockSpec((1, hd, 1), lambda h: (h, 0, 0)),
        ],
        out_shape=[
            jax.ShapeDtypeStruct((3, heads, hd, t), BF),
            jax.ShapeDtypeStruct((heads, hd, 1), F32),
        ],
        scratch_shapes=[
            pltpu.VMEM((n * (n + 1) // 2, block, block), F32),
            pltpu.VMEM((t, hd), BF),
            pltpu.VMEM((t, hd), BF),
            pltpu.VMEM((hd, t), F32),
            pltpu.VMEM((hd, t), F32),
            pltpu.VMEM((hd, t), BF),
        ],
        compiler_params=pltpu.CompilerParams(vmem_limit_bytes=VMEM_LARGE),
        cost_estimate=CHEAP,
        name="attention_backward",
    )(at, qkv, raw, factor, out, lse, *masks, piece)


def norm_scale(x):
    return lax.rsqrt(jnp.mean(x * x, axis=1, keepdims=True) + EPS)


def body_any(
    inputs, gain_attn, w_qkv, query_scale, w_out, gain_mlp, w_up, b_up, w_down, b_down, series_ids, pad_mask, cotangent
):
    rows, cols = size("row"), size("col")
    tok = inputs.shape[0]
    feat = inputs.shape[1]
    share = tok // cols
    t = series_ids.shape[0]
    head_rows = w_qkv.shape[2] // cols
    heads = head_rows // HEAD_DIM
    r, c = lax.axis_index("row"), lax.axis_index("col")

    blocks = gather_grid(inputs)
    strips = [jnp.concatenate(b, axis=1) for b in blocks]
    x_own = strips[0] if rows == 2 else lax.dynamic_index_in_dim(jnp.stack(strips), r, 0, keepdims=False)
    x_all = jnp.concatenate(flip(strips, "row"), axis=0)
    gain_one = jnp.concatenate(gather(gain_attn, "col"))
    gain_two = jnp.concatenate(gather(gain_mlp, "col"))
    bias_up = jnp.concatenate(gather(b_up, "row")).astype(F32)
    bias_down = jnp.concatenate(gather(b_down, "col")).astype(F32)

    w3 = jnp.transpose(w_qkv, (1, 0, 2)).reshape(3, feat, cols, head_rows)
    w_mine = lax.dynamic_index_in_dim(w3, c, 2, keepdims=False)
    w_give = lax.dynamic_index_in_dim(w3, 1 - c, 2, keepdims=False)
    w_half = swap(core_half(w_give, 1), "col")
    w_other = swap(w_half, "core")
    first = lax.axis_index("core") == 0
    w_full = jnp.concatenate(
        [w_mine, jnp.where(first, w_half, w_other), jnp.where(first, w_other, w_half)], axis=1
    )

    xf = x_all.astype(F32)
    scale_one = norm_scale(xf)
    normed_one = (xf * scale_one * gain_one).astype(BF)
    projected = jnp.einsum("td,sdh->sht", normed_one, w_full, preferred_element_type=F32)
    projected = projected.reshape(3, heads, HEAD_DIM, t)
    factor = QUERY_CONST / math.sqrt(HEAD_DIM) * jax.nn.softplus(query_scale)
    raw_q = projected[0]
    qkv = jnp.stack([raw_q * factor[None, :, None], projected[1], projected[2]]).astype(BF)
    masks = mask_args(series_ids, pad_mask)
    at = jnp.zeros((4,), jnp.int32)
    attended, lse = attention_forward(at, qkv, masks)

    def to_tokens(y):
        y = flip_dim(y.reshape(head_rows, rows, cols, share), "row", 1)
        y = flip_dim(y, "col", 2)
        y = exchange(y.reshape(1, head_rows, rows, cols, share), "row", 2, 0)
        y = exchange(y.reshape(rows, 1, head_rows, cols, share), "col", 3, 1)
        y = flip_dim(y.reshape(rows, cols, head_rows, share), "col", 1)
        return y.reshape(rows * cols * head_rows, share)

    def to_heads(y):
        y = flip_dim(y.reshape(rows, cols, head_rows, share), "col", 1)
        y = exchange(y.reshape(rows, cols, head_rows, 1, share), "col", 1, 3)
        y = exchange(y.reshape(rows, head_rows, 1, cols, share), "row", 0, 2)
        y = flip_dim(y.reshape(head_rows, rows, cols, share), "col", 2)
        return flip_dim(y, "row", 1).reshape(head_rows, t)

    w_out_all = weight_gather(w_out, 0)
    w_up_all = weight_gather(w_up, 1)
    w_down_all = weight_gather(w_down, 0)

    def my_share(y):
        return lax.dynamic_slice_in_dim(y, c * share, share, 0)

    att = to_tokens(attended.reshape(head_rows, t))
    x_mine = my_share(x_own).astype(F32)
    middle = x_mine + dot(att, w_out_all, (0, 0))
    scale_two = norm_scale(middle)
    normed_two = (middle * scale_two * gain_two).astype(BF)
    pre_act = dot(normed_two, w_up_all, (1, 0)) + bias_up
    sig = jax.nn.sigmoid(pre_act)
    hidden = (pre_act * sig).astype(BF)
    result = (middle + dot(hidden, w_down_all, (1, 0)) + bias_down).astype(BF)

    def to_block(y):
        mine, theirs = jnp.split(y, 2, axis=1)
        return jnp.concatenate(flip([mine, swap(theirs, "col")], "col"), axis=0)

    layer_out = to_block(result)

    g_give = lax.dynamic_slice_in_dim(cotangent, (1 - c) * share, share, 0)
    g = jnp.concatenate([my_share(cotangent), swap(g_give, "col")], axis=1)
    grad_w_down = dot(hidden, g, (0, 0))
    grad_hidden = dot(g, w_down_all, (1, 1))
    grad_pre_f = grad_hidden * sig * (1.0 + pre_act * (1.0 - sig))
    grad_pre = grad_pre_f.astype(BF)
    grad_b_up = jnp.sum(grad_pre.astype(F32), axis=0)
    grad_w_up = dot(normed_two, grad_pre, (0, 0))
    grad_normed_two = dot(grad_pre, w_up_all, (1, 1))
    weighted = grad_normed_two * gain_two
    inner = jnp.sum(weighted * middle, axis=1, keepdims=True)
    grad_middle = g.astype(F32) + scale_two * weighted - middle * (scale_two**3 * inner / D)
    grad_gain_mlp = jnp.sum(grad_normed_two * middle * scale_two, axis=0)
    grad_branch = grad_middle.astype(BF)
    grad_w_out = dot(att, grad_branch, (1, 0))
    grad_att = dot(w_out_all, grad_branch, (1, 1)).astype(BF)
    grad_attended = to_heads(grad_att).reshape(heads, HEAD_DIM, t)
    grad_middle_block = to_block(grad_middle)

    sum_down = weight_sum(grad_w_down, 0)
    sum_up = weight_sum(grad_w_up, 1)
    sum_out = weight_sum(grad_w_out, 0)

    grad_proj, gscale = attention_backward(
        at, qkv, raw_q, factor.reshape(HEAD_DIM, 1), attended, grad_attended[None], lse, masks
    )
    slope = QUERY_CONST / math.sqrt(HEAD_DIM) * jax.nn.sigmoid(query_scale)
    grad_query_scale = jnp.sum(gscale, axis=(0, 2)) * slope
    grad_proj = grad_proj.reshape(3, head_rows, t)
    grad_normed_one = jnp.einsum("sht,sdh->td", grad_proj, w_full, preferred_element_type=F32)
    weighted_one = grad_normed_one * gain_one
    inner_one = jnp.sum(weighted_one * xf, axis=1)
    grad_gain_attn = jnp.sum(grad_normed_one * xf * scale_one, axis=0)
    inner_one = lax.psum(inner_one, ("row", "col"))
    grad_w = jnp.einsum("td,sht->sdh", normed_one, grad_proj, preferred_element_type=F32)
    grad_w = grad_w.reshape(3, cols, 2, feat // 2, head_rows)
    core = lax.axis_index("core")
    keep = lax.dynamic_index_in_dim(grad_w, core, 2, keepdims=False)
    give = lax.dynamic_index_in_dim(grad_w, 1 - core, 2, keepdims=False).astype(BF)
    part = (keep + swap(give, "core").astype(F32)).astype(BF)
    part = jnp.concatenate(flip([part[:, 0], swap(part[:, 1], "col")], "col"), axis=2)
    sum_qkv = jnp.transpose(z_sum(part), (1, 0, 2))

    e = jnp.concatenate(flip(jnp.split(grad_normed_one.astype(BF), 2, axis=0), "row"), axis=0) if rows == 2 else (
        grad_normed_one.astype(BF)
    )
    e = scatter_sum(e, "row", 0)
    e = scatter_sum(e, "col", 1).astype(F32)
    my_rows = lambda y: lax.dynamic_slice_in_dim(y, r * tok, tok, 0)
    scale_mine = my_rows(scale_one)
    inner_mine = my_rows(inner_one.reshape(t, 1))
    grad_inputs = grad_middle_block + scale_mine * (e * gain_attn) - inputs.astype(F32) * (
        scale_mine**3 * inner_mine / D
    )

    grad_b_down = jnp.sum(g.astype(F32), axis=0)
    vectors = jnp.concatenate(
        [
            flip_dim(grad_gain_attn, "col", 0),
            flip_dim(grad_gain_mlp, "col", 0),
            flip_dim(grad_b_down, "col", 0),
            flip_dim(grad_b_up, "row", 0),
            grad_query_scale,
        ]
    )
    vectors = lax.psum(vectors, ("z", "core", "row", "col"))
    mine_col = lambda at: lax.dynamic_slice_in_dim(vectors, at * D + c * feat, feat, 0)
    units = b_up.shape[0]
    return (
        layer_out,
        grad_inputs,
        mine_col(0),
        sum_qkv,
        vectors[4 * D :],
        sum_out,
        mine_col(1),
        sum_up,
        lax.dynamic_slice_in_dim(vectors, 3 * D + r * units, units, 0),
        sum_down,
        mine_col(2),
    )


SMEM = pl.BlockSpec(memory_space=pltpu.SMEM)
ANY = pl.BlockSpec(memory_space=pl.ANY)


def call(kernel, name, args, specs, outs, scratch=(), limit=VMEM_LIMIT, out_specs=None):
    more = {} if out_specs is None else {"out_specs": out_specs}
    return pl.pallas_call(
        kernel,
        in_specs=specs,
        **more,
        out_shape=outs,
        scratch_shapes=list(scratch),
        compiler_params=pltpu.CompilerParams(vmem_limit_bytes=limit),
        cost_estimate=CHEAP,
        name=name,
    )(*args)


VM = pl.BlockSpec(memory_space=pltpu.VMEM)
HBM = pl.BlockSpec(memory_space=pltpu.HBM)


def shape(dims, kind):
    return jax.ShapeDtypeStruct(dims, kind)


def project_kernel(
    at, x00, x01, x10, x11, gain, factor, w_mine, w_a, w_b, qkv, raw, normed, scale_own, w_full
):
    r, k = at[0], at[2]
    tok, feat = x00.shape
    hr = w_mine.shape[1]
    half = hr // 2
    for s in range(3):
        w_full[pl.ds(s * hr, hr), 0:feat] = w_mine[s]
        w_full[pl.ds(pl.multiple_of(s * hr + k * half, 16), half), feat:] = w_a[s]
        w_full[pl.ds(pl.multiple_of(s * hr + (1 - k) * half, 16), half), feat:] = w_b[s]
    for i, (a_ref, b_ref) in enumerate(((x00, x01), (x10, x11))):
        a, b = a_ref[...].astype(F32), b_ref[...].astype(F32)
        total = jnp.sum(a * a, axis=1, keepdims=True) + jnp.sum(b * b, axis=1, keepdims=True)
        scale = lax.rsqrt(total / (2 * feat) + EPS)
        if i == 0:
            scale_own[...] = scale
        rows = pl.ds(pl.multiple_of((r ^ i) * tok, tok), tok)
        normed[rows, 0:feat] = (a * scale * gain[:, 0:feat]).astype(BF)
        normed[rows, feat:] = (b * scale * gain[:, feat:]).astype(BF)
        y = normed[rows, :]
        q = dot(w_full[0:hr, :], y, (1, 1))
        raw[:, rows] = q
        qkv[0, :, rows] = (q * factor[...]).astype(BF)
        qkv[1, :, rows] = dot(w_full[hr : 2 * hr, :], y, (1, 1)).astype(BF)
        qkv[2, :, rows] = dot(w_full[2 * hr : 3 * hr, :], y, (1, 1)).astype(BF)


def feed_kernel(
    at, gain, bias_up, bias_down, a, x_own, x_col, g_own, g_col,
    w_out, w_up, w_down, hx, hy, d0, d1, hx2, hy2, d02, d12,
    out_own, gm_own, post, ts, vectors, att, hidden_out, normed_out, g_out, pre_out, branch_out,
    w, x_ref, sems, more_sems,
):
    r, c, k = at[0], at[1], at[2]
    _, hr, share = a.shape
    feat = x_own.shape[1]
    half = feat // 2
    first = d0.shape[1]
    rows = pl.ds(pl.multiple_of(c * share, share), share)

    def start(pairs, sem):
        copies = [pltpu.make_async_copy(src, dst, sem.at[m]) for m, (src, dst) in enumerate(pairs)]
        for copy in copies:
            copy.start()
        return copies

    def place(s):
        return pl.ds(pl.multiple_of(((s // 2) ^ r) * 2 * hr + (s % 2) * hr, 16), hr)

    small = [(a.at[s], att.at[place(s), :]) for s in range(4)]
    small += [(x_own.at[rows, :], x_ref.at[:, 0:feat]), (x_col.at[rows, :], x_ref.at[:, feat:])]
    small += [(g_own.at[rows, :], g_out.at[:, 0:feat]), (g_col, g_out.at[:, feat:])]
    small = start(small, more_sems)
    copies = []
    for n, shard in enumerate((w_out, w_up, w_down)):
        rx, cx, ry, cy = (0, feat, feat, 0) if n == 1 else (feat, 0, 0, feat)
        mine = [(shard, w.at[n, 0:feat, 0:feat])]
        for core, (px, py, p0, p1) in ((k, (hx, hy, d0, d1)), (1 - k, (hx2, hy2, d02, d12))):
            down = core * half
            at_x = pl.ds(pl.multiple_of(rx + down, 16), half)
            at_y = pl.ds(pl.multiple_of(ry + down, 16), half)
            at_0 = pl.ds(pl.multiple_of(feat + down, 16), first)
            at_1 = pl.ds(pl.multiple_of(feat + down + first, 16), half - first)
            mine.append((px.at[n], w.at[n, at_x, cx : cx + feat]))
            mine.append((py.at[n], w.at[n, at_y, cy : cy + feat]))
            mine.append((p0.at[n], w.at[n, at_0, feat : 2 * feat]))
            mine.append((p1.at[n], w.at[n, at_1, feat : 2 * feat]))
        copies.append(start(mine, sems.at[n]))

    for copy in small + copies[0]:
        copy.wait()
    middle = x_ref[...].astype(F32) + dot(att[...], w[0], (0, 0))
    scale = lax.rsqrt(jnp.sum(middle * middle, axis=1, keepdims=True) / D + EPS)
    normed = (middle * scale * gain[...]).astype(BF)
    normed_out[...] = normed
    for copy in copies[1]:
        copy.wait()
    pre = dot(normed, w[1], (1, 0)) + bias_up[...]
    sig = jax.nn.sigmoid(pre)
    hidden = (pre * sig).astype(BF)
    hidden_out[...] = hidden
    for copy in copies[2]:
        copy.wait()
    result = (middle + dot(hidden, w[2], (1, 0)) + bias_down[...]).astype(BF)
    out_own[...] = result[:, :feat]
    post[0] = result[:, feat:]

    grad_pre_f = dot(g_out[...], w[2], (1, 1)) * sig * (1.0 + pre * (1.0 - sig))
    grad_pre = grad_pre_f.astype(BF)
    pre_out[...] = grad_pre
    grad_normed = dot(grad_pre, w[1], (1, 1))
    weighted = grad_normed * gain[...]
    inner = jnp.sum(weighted * middle, axis=1, keepdims=True)
    gf = g_out[...].astype(F32)
    grad_middle = gf + scale * weighted - middle * (scale * scale * scale * inner / D)
    gm_own[...] = grad_middle[:, :feat]
    post[1] = grad_middle[:, feat:].astype(BF)
    branch = grad_middle.astype(BF)
    branch_out[...] = branch
    for s in range(4):
        ts[s] = dot(w[0, place(s), :], branch, (1, 1)).astype(BF)
    vectors[...] = jnp.concatenate(
        [
            jnp.sum(grad_normed * (middle * scale), axis=0, keepdims=True),
            jnp.sum(gf, axis=0, keepdims=True),
            jnp.sum(grad_pre.astype(F32), axis=0, keepdims=True),
        ],
        axis=0,
    )


def feed_weights_kernel(at, att, hidden, normed, g, grad_pre, branch, *rest):
    *grads, stage, turned, sems = rest
    k = at[2]
    feat = g.shape[1] // 2
    half = feat // 2
    quarter = half // 2
    copies = []

    def weight_grad(n, left_ref, right):
        for core, begin in ((k, 0), (1 - k, 8)):
            up, low = (begin + 4, begin) if n == 1 else (begin, begin + 4)
            for b in range(2):
                part = pl.ds(pl.multiple_of(b * feat + core * half, 16), half)
                y = dot(left_ref[part, :], right, (1, 0)).astype(BF)
                for j in range(2):
                    cut = slice(j * feat, (j + 1) * feat)
                    for to, value in ((up + 2 * j + (1 - b), y[:quarter, cut]), (low + 2 * b + (1 - j), y[quarter:, cut])):
                        stage[to, n] = value
                        copy = pltpu.make_async_copy(stage.at[to, n], grads[to].at[n], sems.at[to, n])
                        copy.start()
                        copies.append(copy)

    turned[0] = hidden[...].astype(F32).T.astype(BF)
    weight_grad(2, turned.at[0], g[...])
    turned[1] = normed[...].astype(F32).T.astype(BF)
    weight_grad(1, turned.at[1], grad_pre[...])
    weight_grad(0, att, branch[...])
    for copy in copies:
        copy.wait()


def weight_back_kernel(at, grad, normed, keep, give):
    k = at[2]
    part = keep.shape[2]
    feat = keep.shape[3]
    for ref, core in ((give, 1 - k), (keep, k)):
        for s in range(3):
            rows = pl.ds(pl.multiple_of(core * part, 16), part)
            y = dot(grad[s, rows, :], normed[...], (1, 0)).astype(BF)
            ref[0, s] = y[:, :feat]
            ref[1, s] = y[:, feat:]


def project_back_kernel(
    at, grad, w_full, x00, x01, x10, x11, gain, es, gain_sum
):
    r, c = at[0], at[1]
    tok, feat = x00.shape
    sums = [jnp.zeros((1, feat), F32), jnp.zeros((1, feat), F32)]
    for i, xs in enumerate(((x00, x01), (x10, x11))):
        rows = pl.ds(pl.multiple_of((r ^ i) * tok, tok), tok)
        left = grad[:, rows]
        products, squares, inner = [], 0.0, 0.0
        for j in range(2):
            cut = slice(j * feat, (j + 1) * feat)
            e = dot(left, w_full[:, cut], (0, 0))
            x = xs[j][...].astype(F32)
            product = e * x
            inner = inner + jnp.sum(product * gain[:, cut], axis=1, keepdims=True)
            squares = squares + jnp.sum(x * x, axis=1, keepdims=True)
            es[2 * (r ^ i) + (c ^ j), 0:tok, :] = e.astype(BF)
            products.append(product)
        scale = lax.rsqrt(squares / (2 * feat) + EPS)
        for j in range(2):
            sums[j] += jnp.sum(products[j] * scale, axis=0, keepdims=True)
        line = jnp.broadcast_to(inner, (tok, 128)).T[0:1, :]
        high = line.astype(BF).astype(F32)
        extra = jnp.concatenate([high, line - high, jnp.zeros((14, tok), F32)], axis=0)
        extra = jnp.concatenate([extra, jnp.zeros((16, feat - tok), F32)], axis=1).astype(BF)
        for j in range(2):
            es[2 * (r ^ i) + (c ^ j), tok:, :] = extra
    gain_sum[:, 0:feat] = sums[0]
    gain_sum[:, feat:] = sums[1]


def finish_qkv_kernel(at, mine, theirs, mine2, theirs2, out, rows):
    c, k = at[1], at[2]
    half = mine.shape[1]
    for s in range(3):
        for ref, col, core in ((mine, c, k), (theirs, 1 - c, k), (mine2, c, 1 - k), (theirs2, 1 - c, 1 - k)):
            rows[pl.ds(pl.multiple_of((2 * col + core) * half, 16), half), :] = ref[s].astype(F32)
        out[s] = rows[...].T


def finish_feed_kernel(at, a, b, a2, b2, *outs):
    k = at[2]
    quarter = a.shape[1]
    for n, out in enumerate(outs):
        upper, lower = ((b, b2), (a, a2)) if n == 1 else ((a, a2), (b, b2))
        for i, core in ((0, k), (1, 1 - k)):
            for j, refs in enumerate((upper, lower)):
                to = pl.multiple_of((2 * core + j) * quarter, 16)
                out[pl.ds(to, quarter), :] = refs[i][n].astype(F32)


together = lax.optimization_barrier


def after(x, *earlier):
    return lax.optimization_barrier((x, *earlier))[0]


def add(*parts):
    total = parts[0].astype(F32)
    for part in parts[1:]:
        total = total + part.astype(F32)
    return total.astype(BF)


def all_four(x):
    return lax.all_to_all(x, ("row", "col"), 0, 0, tiled=True)


def z_swap(x, step):
    n = size("z")
    return lax.ppermute(x, "z", [(i, i ^ step) for i in range(n)])


def z_first():
    z = lax.axis_index("z")
    return (z == 0) | (z == 3)


def body_four(
    inputs, gain_attn, w_qkv, query_scale, w_out, gain_mlp, w_up, b_up, w_down, b_down, series_ids, pad_mask, cotangent
):
    tok, feat = inputs.shape
    share = tok // 2
    t = series_ids.shape[0]
    hr = w_qkv.shape[2] // 2
    heads = hr // HEAD_DIM
    half = feat // 2
    r, c, k = lax.axis_index("row"), lax.axis_index("col"), lax.axis_index("core")
    at = jnp.stack([r, c, k, 2 * r + c]).astype(jnp.int32)
    mine_rows = lambda y, part: lax.dynamic_slice_in_dim(y, part * share, share, 0)

    few = heads // 2
    quarter = half // 2
    first_rows = (half * 7 // 20) // 16 * 16
    x01 = swap(inputs, "col")
    x10 = swap(inputs, "row")
    small = swap(jnp.concatenate([gain_attn, gain_mlp, b_down.astype(F32)]), "col")
    up_other = swap(b_up.astype(F32), "row")
    w_turned = jnp.transpose(w_qkv, (1, 2, 0)).reshape(3, 2, hr, feat)
    w_mine = lax.dynamic_index_in_dim(w_turned, c, 1, keepdims=False)
    w_give = lax.dynamic_index_in_dim(w_turned, 1 - c, 1, keepdims=False)
    w_half = core_half(w_give, 1)
    w_a = swap(w_half, "col")
    part = jnp.stack([core_half(w_out, 0), core_half(w_up, 0), core_half(w_down, 0)])
    g_give = mine_rows(cotangent, 1 - c)
    x01, x10, small, up_other, part, g_give, w_mine = lax.optimization_barrier(
        (x01, x10, small, up_other, part, g_give, w_mine)
    )
    x11 = swap(after(x01, w_half), "row")
    w_b = swap(w_a, "core")
    gain_one = jnp.concatenate([gain_attn, small[:feat]]).reshape(1, D)
    gain_two = jnp.concatenate([gain_mlp, small[feat : 2 * feat]]).reshape(1, D)
    bias_down = jnp.concatenate([b_down.astype(F32), small[2 * feat :]]).reshape(1, D)
    bias_up = jnp.concatenate([b_up.astype(F32), up_other]).reshape(1, D)
    factor = QUERY_CONST / math.sqrt(HEAD_DIM) * jax.nn.softplus(query_scale)
    factor_col = factor.reshape(HEAD_DIM, 1)

    part = after(part, x11, w_a)
    hx, hy = swap(part, "row"), swap(part, "col")
    hx2, hy2 = swap(hx, "core"), swap(hy, "core")
    qkv, raw, normed_one, scale_own, w_full = call(
        project_kernel,
        "project",
        (at, inputs, x01, x10, x11, gain_one, jnp.tile(factor_col, (heads, 1)), w_mine, w_a, w_b),
        [SMEM] + [VM] * 9,
        [
            shape((3, hr, t), BF),
            shape((hr, t), F32),
            shape((t, D), BF),
            shape((tok, 1), F32),
            shape((3 * hr, D), BF),
        ],
        limit=VMEM_LARGE,
    )
    qkv = qkv.reshape(3, heads, HEAD_DIM, t)
    masks = mask_args(series_ids, pad_mask)
    attended, lse, a = attention_forward(at, qkv, masks, pieces=1)
    a = all_four(a.reshape(4, hr, share))
    hx_on, hy_on, g_give = lax.optimization_barrier((hx, hy, g_give, lse))[:3]
    d0 = swap(hx_on[:, :first_rows], "col")
    d1 = swap(hy_on[:, first_rows:], "row")
    g_col = swap(g_give, "col")
    d0, d1, g_col, a = together((d0, d1, g_col, a))
    d02, d12 = swap(d0, "core"), swap(d1, "core")
    out_own, gm_own, post, ts, vectors, *factors = call(
        feed_kernel,
        "feed_forward",
        (at, gain_two, bias_up, bias_down, a, inputs, x01, cotangent, g_col)
        + (w_out, w_up, w_down, hx, hy, d0, d1, hx2, hy2, d02, d12),
        [SMEM] + [VM] * 3 + [HBM] * 16,
        [
            shape((share, feat), BF),
            shape((share, feat), F32),
            shape((2, share, feat), BF),
            shape((4, hr, share), BF),
            shape((3, D), F32),
            shape((D, share), BF),
        ]
        + [shape((share, D), BF)] * 5,
        scratch=[
            pltpu.VMEM((3, D, D), BF),
            pltpu.VMEM((share, D), BF),
            pltpu.SemaphoreType.DMA((3, 9)),
            pltpu.SemaphoreType.DMA((8,)),
        ],
    )
    grads = call(
        feed_weights_kernel,
        "feed_weights",
        (at, *factors),
        [SMEM] + [VM] * 6,
        [shape((3, quarter, feat), BF)] * 16,
        scratch=[
            pltpu.VMEM((16, 3, quarter, feat), BF),
            pltpu.VMEM((2, D, share), BF),
            pltpu.SemaphoreType.DMA((16, 3)),
        ],
        out_specs=[HBM] * 16,
    )
    ts = all_four(ts)
    others = grads[8:]
    over = lambda n: swap(others[n], "core")
    grads, osx0, osx1, osy0, osy1 = grads[:8], over(0), over(2), over(4), over(6)
    sx0, kx0, sx1, kx1, sy0, ky0, sy1, ky1 = grads
    sx1, sy1 = add(sx1, osx1), add(sy1, osy1)
    ox0, ox1, oy0, oy1 = over(1), over(3), over(5), over(7)
    sx0, sy0 = add(sx0, osx0), add(sy0, osy0)
    ts, sx1, sy1, sx0, sy0 = together((ts, sx1, sy1, sx0, sy0))
    rx1, ry1 = swap(sx1, "row"), swap(sy1, "col")
    rx0, ry0 = swap(sx0, "row"), swap(sy0, "col")
    ts = ts.reshape(4, heads, HEAD_DIM, share)
    raw = raw.reshape(heads, HEAD_DIM, t)

    grad_proj, gscale = attention_backward(at, qkv, raw, factor_col, attended, ts, lse, masks)
    grad_proj = grad_proj.reshape(3, hr, t)
    kept, sent = call(
        weight_back_kernel,
        "weight_back",
        (at, grad_proj, normed_one),
        [SMEM] + [VM] * 2,
        [shape((2, 3, hr // 2, feat), BF)] * 2,
    )
    sent, rx1, ry1, rx0, ry0, ox0, ox1, oy0, oy1 = together((sent, rx1, ry1, rx0, ry0, ox0, ox1, oy0, oy1))
    got = swap(sent, "core")
    px1, py1 = add(kx1, ox1, rx1), add(ky1, oy1, ry1)
    qx, qy = swap(px1, "col"), swap(py1, "row")
    w_pair = add(kept, got)
    first = z_first()
    got_w = z_swap(jnp.where(first, w_pair[1], w_pair[0]), 1)
    slope = QUERY_CONST / math.sqrt(HEAD_DIM) * jax.nn.sigmoid(query_scale)
    grad_query_scale = jnp.sum(gscale, axis=(0, 2)) * slope
    es, gain_sum = call(
        project_back_kernel,
        "project_back",
        (at, after(grad_proj, w_pair, px1, py1).reshape(3 * hr, t), w_full, inputs, x01, x10, x11, gain_one),
        [SMEM] + [VM] * 7,
        [
            shape((4, tok + 16, feat), BF),
            shape((1, D), F32),
        ],
    )
    total = jnp.concatenate([gain_sum, vectors]).reshape(4, 2, feat)
    turn = jnp.stack([c, c, c, r]).reshape(4, 1, 1) == 1
    total = jnp.where(turn, total[:, ::-1], total).reshape(8, feat)
    total = jnp.concatenate([total, jnp.pad(grad_query_scale, (0, feat - HEAD_DIM)).reshape(1, feat)])
    total = total + swap(total, "core")
    qx, qy, got_w, w_pair, es = together((qx, qy, got_w, w_pair, es))

    mine_w = add(jnp.where(first, w_pair[0], w_pair[1]), got_w)
    met_w = z_swap(mine_w, 3)
    fx, fy = add(kx0, ox0, rx0, qx), add(ky0, oy0, ry0, qy)
    got_c = z_swap(jnp.where(first, fy, fx), 1)
    es = all_four(es)
    total = total + swap(total, "row")
    total = total + swap(total, "col")
    met_w, mine_w, got_c, fx, fy, es, post, total = together((met_w, mine_w, got_c, fx, fy, es, post, total))

    mine_w = add(mine_w, met_w)
    other_w = z_swap(mine_w, 1)
    w_own, w_theirs = jnp.where(first, mine_w, other_w), jnp.where(first, other_w, mine_w)
    mine_c = add(jnp.where(first, fx, fy), got_c)
    met_c = z_swap(mine_c, 3)
    post = swap(post, "col")
    w_theirs = swap(w_theirs, "col")
    total = total + z_swap(total, 1)
    total = total + z_swap(total, 3)
    met_c, mine_c, w_own, w_theirs, post, total = together((met_c, mine_c, w_own, w_theirs, post, total))
    mine_c = add(mine_c, met_c)
    other_c = z_swap(mine_c, 1)
    w_args = (at, w_own, w_theirs, swap(w_own, "core"), swap(w_theirs, "core"))
    sum_qkv = call(
        finish_qkv_kernel,
        "finish_qkv",
        w_args,
        [SMEM] + [VM] * 4,
        shape((3, feat, 2 * hr), F32),
        scratch=[pltpu.VMEM((2 * hr, feat), F32)],
    )
    sum_qkv = jnp.transpose(sum_qkv, (1, 0, 2))

    e = jnp.sum(es[:, :tok].astype(F32), axis=0)
    inner = jnp.sum(es[:, tok : tok + 2, :tok].astype(F32), axis=(0, 1)).reshape(tok, 1)
    grad_middle = jnp.concatenate(flip([gm_own, post[1].astype(F32)], "col"), axis=0)
    grad_inputs = grad_middle + scale_own * (e * gain_attn) - inputs.astype(F32) * (scale_own**3 * inner / D)
    layer_out = jnp.concatenate(flip([out_own, post[0]], "col"), axis=0)

    pick = lambda n, place: lax.dynamic_index_in_dim(total, 2 * n + place, 0, keepdims=False)
    mine_c = after(mine_c, sum_qkv, grad_inputs, layer_out, total)
    fx, fy = jnp.where(first, mine_c, other_c), jnp.where(first, other_c, mine_c)
    sum_out, sum_up, sum_down = call(
        finish_feed_kernel,
        "finish_feed",
        (at, fx, fy, swap(fx, "core"), swap(fy, "core")),
        [SMEM] + [VM] * 4,
        [shape((feat, feat), F32)] * 3,
    )

    return (
        layer_out,
        grad_inputs,
        pick(0, c),
        sum_qkv,
        total[8, :HEAD_DIM],
        sum_out,
        pick(1, c),
        sum_up,
        pick(3, r),
        sum_down,
        pick(2, c),
    )


def solution(mesh):
    dp, rows, cols = mesh.shape["dp"], mesh.shape["row"], mesh.shape["col"]
    split = Mesh(mesh.devices.reshape(dp // 2, 2, rows, cols), ("z", "core", "row", "col"))
    tokens = P(("z", "core", "row"), "col")
    in_specs = (
        tokens,
        P("col"),
        P("col", None, "row"),
        P(),
        P("row", "col"),
        P("col"),
        P("col", "row"),
        P("row"),
        P("row", "col"),
        P("col"),
        P(("z", "core")),
        P(("z", "core")),
        tokens,
    )
    out_specs = (
        tokens,
        tokens,
        P("col"),
        P("col", None, "row"),
        P(),
        P("row", "col"),
        P("col"),
        P("col", "row"),
        P("row"),
        P("row", "col"),
        P("col"),
    )
    body = body_four if (dp, rows, cols) == (8, 2, 2) else body_any
    return jax.shard_map(body, mesh=split, in_specs=in_specs, out_specs=out_specs, check_vma=False)
```

```python
import functools
import math

import jax
import jax.numpy as jnp
from jax import lax
from jax.experimental import pallas as pl
from jax.experimental.pallas import tpu as pltpu
from jax.sharding import Mesh
from jax.sharding import PartitionSpec as P

D = 1280
HEAD_DIM = 80
EPS = 1e-06
QUERY_CONST = 1.442695041
MASKED = -1e30
BF = jnp.bfloat16
F32 = jnp.float32
VMEM_LIMIT = 60 * 1024 * 1024
VMEM_LARGE = 60 * 1024 * 1024
CHEAP = pl.CostEstimate(flops=1, bytes_accessed=1, transcendentals=0)


def size(axis):
    return lax.axis_size(axis)


def swap(x, axis):
    return lax.ppermute(x, axis, [(0, 1), (1, 0)])


def flip(blocks, axis):
    if size(axis) != 2:
        return list(blocks)
    first = lax.axis_index(axis) == 0
    a, b = blocks
    return [jnp.where(first, a, b), jnp.where(first, b, a)]


def flip_dim(x, axis, dim):
    if size(axis) != 2:
        return x
    return jnp.concatenate(flip(jnp.split(x, 2, axis=dim), axis), axis=dim)


def gather(x, axis):
    if size(axis) == 2:
        return [x, swap(x, axis)]
    whole = lax.all_gather(x, axis, axis=0, tiled=False)
    return [whole[i] for i in range(size(axis))]


def gather_grid(x):
    if size("row") != 2:
        return [gather(b, "col") for b in gather(x, "row")]
    along_row, along_col = swap(x, "row"), swap(x, "col")
    half = x.shape[0] // 2
    across = jnp.concatenate(
        [swap(along_row[:half], "col"), swap(along_col[half:], "row")], axis=0
    )
    return [[x, along_col], [along_row, across]]


def scatter_sum(x, axis, dim):
    if size(axis) != 2:
        return lax.psum_scatter(x, axis, scatter_dimension=dim, tiled=True)
    mine, theirs = jnp.split(x, 2, axis=dim)
    return (mine.astype(F32) + swap(theirs, axis).astype(F32)).astype(x.dtype)


def exchange(x, axis, split, join):
    if size(axis) != 2:
        return lax.all_to_all(x, axis, split, join, tiled=True)
    mine, theirs = jnp.split(x, 2, axis=split)
    return jnp.concatenate([mine, swap(theirs, axis)], axis=join)


def core_half(x, dim):
    return lax.dynamic_slice_in_dim(
        x, lax.axis_index("core") * (x.shape[dim] // 2), x.shape[dim] // 2, dim
    )


def weight_gather(w, row_dim):
    part = core_half(w, 0)
    blocks = gather_grid(part)
    if row_dim == 1:
        blocks = [list(b) for b in zip(*blocks)]
    mine = jnp.stack([jnp.concatenate(b, axis=1) for b in blocks])
    other = swap(mine, "core")
    first = lax.axis_index("core") == 0
    both = jnp.stack([jnp.where(first, mine, other), jnp.where(first, other, mine)], axis=1)
    return both.reshape(-1, both.shape[-1])


def weight_sum(g, row_dim):
    dim_axis = ("row", "col") if row_dim == 0 else ("col", "row")
    n0 = size(dim_axis[0])
    g = g.reshape(n0, 2, g.shape[0] // n0 // 2, g.shape[1])
    core = lax.axis_index("core")
    keep = lax.dynamic_index_in_dim(g, core, 1, keepdims=False)
    give = lax.dynamic_index_in_dim(g, 1 - core, 1, keepdims=False).astype(BF)
    part = (keep + swap(give, "core").astype(F32)).astype(BF)
    part = scatter_sum(part, dim_axis[0], 0)
    part = scatter_sum(part[0], dim_axis[1], 1)
    return z_sum(part)


def z_sum(part):
    total = lax.psum(part, "z")
    other = swap(total, "core")
    return flip_core(total, other)


def flip_core(total, other):
    first = lax.axis_index("core") == 0
    return jnp.concatenate(
        [jnp.where(first, total, other), jnp.where(first, other, total)], axis=-2
    ).astype(F32)


def dot(a, b, contract):
    return lax.dot_general(a, b, ((contract[0:1], contract[1:2]), ((), ())), preferred_element_type=F32)


def bias_block(series_row, series_col, key_pos, q0, k0, qb, kb, diagonal):
    q_pos = q0 + lax.broadcasted_iota(jnp.int32, (1, qb), 1)
    allowed = (series_col == series_row) & (key_pos <= q_pos)
    if diagonal:
        k_pos = k0 + lax.broadcasted_iota(jnp.int32, (kb, 1), 0)
        allowed = allowed | (k_pos == q_pos)
    return jnp.where(allowed, 0.0, MASKED)


def forward_kernel(block, at, qkv_ref, srow_ref, scol_ref, kpos_ref, out_ref, lse_ref, *rest):
    *pieces, bias_ref, krow_ref, s_ref = rest
    t = qkv_ref.shape[3]
    n = t // block
    krow_ref[...] = qkv_ref[1, 0].astype(F32).T.astype(BF)

    def bias_slot(j, i):
        return j * (j + 1) // 2 + i

    @pl.when(pl.program_id(0) == 0)
    def _():
        for j in range(n):
            for i in range(j + 1):
                keys = pl.ds(i * block, block)
                bias_ref[bias_slot(j, i)] = bias_block(
                    srow_ref[:, j * block : (j + 1) * block],
                    scol_ref[keys, :],
                    kpos_ref[keys, :],
                    j * block,
                    i * block,
                    block,
                    block,
                    i == j,
                )

    for j in range(n):
        cols = slice(j * block, (j + 1) * block)
        q = qkv_ref[0, 0, :, cols]
        top = None
        for i in range(j + 1):
            s = dot(krow_ref[i * block : (i + 1) * block, :], q, (1, 0)) + bias_ref[bias_slot(j, i)]
            s_ref[i * block : (i + 1) * block, :] = s
            here = jnp.max(s, axis=0, keepdims=True)
            top = here if top is None else jnp.maximum(top, here)
        total = jnp.zeros((1, block), F32)
        acc = jnp.zeros((HEAD_DIM, block), F32)
        for i in range(j + 1):
            p = jnp.exp(s_ref[i * block : (i + 1) * block, :] - top)
            total += jnp.sum(p, axis=0, keepdims=True)
            acc += dot(qkv_ref[2, 0, :, i * block : (i + 1) * block], p.astype(BF), (1, 0))
        found = (acc / total).astype(BF)
        out_ref[0, :, cols] = found
        if pieces:
            pieces[0][j, 0] = found
        lse_ref[0, :, cols] = top + jnp.log(total)


def backward_kernel(
    block, at, qkv_ref, raw_ref, factor_ref, out_ref, lse_ref, srow_ref, scol_ref, kpos_ref, *rest
):
    piece, grad_ref, gscale_ref, bias_ref, krow_ref, vrow_ref, gk_ref, gv_ref, gout_ref = rest
    wide = piece.shape[3]
    for j in range(piece.shape[0]):
        gout_ref[:, j * wide : (j + 1) * wide] = piece[j, 0]
    t = qkv_ref.shape[3]
    n = t // block
    krow_ref[...] = qkv_ref[1, 0].astype(F32).T.astype(BF)
    vrow_ref[...] = qkv_ref[2, 0].astype(F32).T.astype(BF)

    def bias_slot(j, i):
        return j * (j + 1) // 2 + i

    @pl.when(pl.program_id(0) == 0)
    def _():
        for j in range(n):
            for i in range(j + 1):
                keys = pl.ds(i * block, block)
                bias_ref[bias_slot(j, i)] = bias_block(
                    srow_ref[:, j * block : (j + 1) * block],
                    scol_ref[keys, :],
                    kpos_ref[keys, :],
                    j * block,
                    i * block,
                    block,
                    block,
                    i == j,
                )

    gscale = jnp.zeros((HEAD_DIM, 1), F32)
    for j in range(n):
        cols = slice(j * block, (j + 1) * block)
        q = qkv_ref[0, 0, :, cols]
        go = gout_ref[:, cols]
        lse = lse_ref[0, :, cols]
        delta = jnp.sum(go.astype(F32) * out_ref[0, :, cols].astype(F32), axis=0, keepdims=True)
        gq = jnp.zeros((HEAD_DIM, block), F32)
        for i in range(j + 1):
            keys = slice(i * block, (i + 1) * block)
            s = dot(krow_ref[keys, :], q, (1, 0)) + bias_ref[bias_slot(j, i)]
            p = jnp.exp(s - lse)
            gp = dot(vrow_ref[keys, :], go, (1, 0))
            gs = (p * (gp - delta)).astype(BF)
            gq += dot(qkv_ref[1, 0, :, keys], gs, (1, 0))
            gk = dot(q, gs, (1, 1))
            gv = dot(go, p.astype(BF), (1, 1))
            if i == j:
                gk_ref[:, keys] = gk
                gv_ref[:, keys] = gv
            else:
                gk_ref[:, keys] += gk
                gv_ref[:, keys] += gv
        gscale += jnp.sum(gq * raw_ref[0, :, cols], axis=1, keepdims=True)
        grad_ref[0, 0, :, cols] = (gq * factor_ref[...]).astype(BF)
    grad_ref[1, 0] = gk_ref[...].astype(BF)
    grad_ref[2, 0] = gv_ref[...].astype(BF)
    gscale_ref[0] = gscale


def mask_args(series, padding):
    t = series.shape[0]
    pos = jnp.arange(t, dtype=jnp.int32)
    return series.reshape(1, t), series.reshape(t, 1), jnp.where(padding == 0, pos, t).reshape(t, 1)


def attention_forward(at, qkv, masks, pieces=0):
    _, heads, hd, t = qkv.shape
    block = min(256, t) if t <= 2048 else 512
    n = t // block
    whole = lambda shape: pl.BlockSpec(shape, lambda h: (0,) * len(shape))
    return pl.pallas_call(
        functools.partial(forward_kernel, block),
        grid=(heads,),
        in_specs=[
            pl.BlockSpec(memory_space=pltpu.SMEM),
            pl.BlockSpec((3, 1, hd, t), lambda h: (0, h, 0, 0)),
            whole((1, t)),
            whole((t, 1)),
            whole((t, 1)),
        ],
        out_specs=[
            pl.BlockSpec((1, hd, t), lambda h: (h, 0, 0)),
            pl.BlockSpec((1, 1, t), lambda h: (h, 0, 0)),
        ]
        + [pl.BlockSpec((n, 1, hd, block), lambda h: (0, h, 0, 0))] * pieces,
        out_shape=[
            jax.ShapeDtypeStruct((heads, hd, t), BF),
            jax.ShapeDtypeStruct((heads, 1, t), F32),
        ]
        + [jax.ShapeDtypeStruct((n, heads, hd, block), BF)] * pieces,
        scratch_shapes=[
            pltpu.VMEM((n * (n + 1) // 2, block, block), F32),
            pltpu.VMEM((t, hd), BF),
            pltpu.VMEM((t, block), F32),
        ],
        compiler_params=pltpu.CompilerParams(vmem_limit_bytes=VMEM_LARGE),
        cost_estimate=CHEAP,
        name="attention_forward",
    )(at, qkv, *masks)


def attention_backward(at, qkv, raw, factor, out, piece, lse, masks):
    _, heads, hd, t = qkv.shape
    block = min(256, t) if t <= 2048 else 512
    n = t // block
    whole = lambda shape: pl.BlockSpec(shape, lambda h: (0,) * len(shape))
    head = lambda wide=t: pl.BlockSpec((1, hd, wide), lambda h: (h, 0, 0))
    return pl.pallas_call(
        functools.partial(backward_kernel, block),
        grid=(heads,),
        in_specs=[
            pl.BlockSpec(memory_space=pltpu.SMEM),
            pl.BlockSpec((3, 1, hd, t), lambda h: (0, h, 0, 0)),
            head(),
            whole((hd, 1)),
            head(),
            pl.BlockSpec((1, 1, t), lambda h: (h, 0, 0)),
            whole((1, t)),
            whole((t, 1)),
            whole((t, 1)),
        ]
        + [pl.BlockSpec((piece.shape[0], 1, hd, piece.shape[3]), lambda h: (0, h, 0, 0))],
        out_specs=[
            pl.BlockSpec((3, 1, hd, t), lambda h: (0, h, 0, 0)),
            pl.BlockSpec((1, hd, 1), lambda h: (h, 0, 0)),
        ],
        out_shape=[
            jax.ShapeDtypeStruct((3, heads, hd, t), BF),
            jax.ShapeDtypeStruct((heads, hd, 1), F32),
        ],
        scratch_shapes=[
            pltpu.VMEM((n * (n + 1) // 2, block, block), F32),
            pltpu.VMEM((t, hd), BF),
            pltpu.VMEM((t, hd), BF),
            pltpu.VMEM((hd, t), F32),
            pltpu.VMEM((hd, t), F32),
            pltpu.VMEM((hd, t), BF),
        ],
        compiler_params=pltpu.CompilerParams(vmem_limit_bytes=VMEM_LARGE),
        cost_estimate=CHEAP,
        name="attention_backward",
    )(at, qkv, raw, factor, out, lse, *masks, piece)


def norm_scale(x):
    return lax.rsqrt(jnp.mean(x * x, axis=1, keepdims=True) + EPS)


def body_any(
    inputs, gain_attn, w_qkv, query_scale, w_out, gain_mlp, w_up, b_up, w_down, b_down, series_ids, pad_mask, cotangent
):
    rows, cols = size("row"), size("col")
    tok = inputs.shape[0]
    feat = inputs.shape[1]
    share = tok // cols
    t = series_ids.shape[0]
    head_rows = w_qkv.shape[2] // cols
    heads = head_rows // HEAD_DIM
    r, c = lax.axis_index("row"), lax.axis_index("col")

    blocks = gather_grid(inputs)
    strips = [jnp.concatenate(b, axis=1) for b in blocks]
    x_own = strips[0] if rows == 2 else lax.dynamic_index_in_dim(jnp.stack(strips), r, 0, keepdims=False)
    x_all = jnp.concatenate(flip(strips, "row"), axis=0)
    gain_one = jnp.concatenate(gather(gain_attn, "col"))
    gain_two = jnp.concatenate(gather(gain_mlp, "col"))
    bias_up = jnp.concatenate(gather(b_up, "row")).astype(F32)
    bias_down = jnp.concatenate(gather(b_down, "col")).astype(F32)

    w3 = jnp.transpose(w_qkv, (1, 0, 2)).reshape(3, feat, cols, head_rows)
    w_mine = lax.dynamic_index_in_dim(w3, c, 2, keepdims=False)
    w_give = lax.dynamic_index_in_dim(w3, 1 - c, 2, keepdims=False)
    w_half = swap(core_half(w_give, 1), "col")
    w_other = swap(w_half, "core")
    first = lax.axis_index("core") == 0
    w_full = jnp.concatenate(
        [w_mine, jnp.where(first, w_half, w_other), jnp.where(first, w_other, w_half)], axis=1
    )

    xf = x_all.astype(F32)
    scale_one = norm_scale(xf)
    normed_one = (xf * scale_one * gain_one).astype(BF)
    projected = jnp.einsum("td,sdh->sht", normed_one, w_full, preferred_element_type=F32)
    projected = projected.reshape(3, heads, HEAD_DIM, t)
    factor = QUERY_CONST / math.sqrt(HEAD_DIM) * jax.nn.softplus(query_scale)
    raw_q = projected[0]
    qkv = jnp.stack([raw_q * factor[None, :, None], projected[1], projected[2]]).astype(BF)
    masks = mask_args(series_ids, pad_mask)
    at = jnp.zeros((4,), jnp.int32)
    attended, lse = attention_forward(at, qkv, masks)

    def to_tokens(y):
        y = flip_dim(y.reshape(head_rows, rows, cols, share), "row", 1)
        y = flip_dim(y, "col", 2)
        y = exchange(y.reshape(1, head_rows, rows, cols, share), "row", 2, 0)
        y = exchange(y.reshape(rows, 1, head_rows, cols, share), "col", 3, 1)
        y = flip_dim(y.reshape(rows, cols, head_rows, share), "col", 1)
        return y.reshape(rows * cols * head_rows, share)

    def to_heads(y):
        y = flip_dim(y.reshape(rows, cols, head_rows, share), "col", 1)
        y = exchange(y.reshape(rows, cols, head_rows, 1, share), "col", 1, 3)
        y = exchange(y.reshape(rows, head_rows, 1, cols, share), "row", 0, 2)
        y = flip_dim(y.reshape(head_rows, rows, cols, share), "col", 2)
        return flip_dim(y, "row", 1).reshape(head_rows, t)

    w_out_all = weight_gather(w_out, 0)
    w_up_all = weight_gather(w_up, 1)
    w_down_all = weight_gather(w_down, 0)

    def my_share(y):
        return lax.dynamic_slice_in_dim(y, c * share, share, 0)

    att = to_tokens(attended.reshape(head_rows, t))
    x_mine = my_share(x_own).astype(F32)
    middle = x_mine + dot(att, w_out_all, (0, 0))
    scale_two = norm_scale(middle)
    normed_two = (middle * scale_two * gain_two).astype(BF)
    pre_act = dot(normed_two, w_up_all, (1, 0)) + bias_up
    sig = jax.nn.sigmoid(pre_act)
    hidden = (pre_act * sig).astype(BF)
    result = (middle + dot(hidden, w_down_all, (1, 0)) + bias_down).astype(BF)

    def to_block(y):
        mine, theirs = jnp.split(y, 2, axis=1)
        return jnp.concatenate(flip([mine, swap(theirs, "col")], "col"), axis=0)

    layer_out = to_block(result)

    g_give = lax.dynamic_slice_in_dim(cotangent, (1 - c) * share, share, 0)
    g = jnp.concatenate([my_share(cotangent), swap(g_give, "col")], axis=1)
    grad_w_down = dot(hidden, g, (0, 0))
    grad_hidden = dot(g, w_down_all, (1, 1))
    grad_pre_f = grad_hidden * sig * (1.0 + pre_act * (1.0 - sig))
    grad_pre = grad_pre_f.astype(BF)
    grad_b_up = jnp.sum(grad_pre.astype(F32), axis=0)
    grad_w_up = dot(normed_two, grad_pre, (0, 0))
    grad_normed_two = dot(grad_pre, w_up_all, (1, 1))
    weighted = grad_normed_two * gain_two
    inner = jnp.sum(weighted * middle, axis=1, keepdims=True)
    grad_middle = g.astype(F32) + scale_two * weighted - middle * (scale_two**3 * inner / D)
    grad_gain_mlp = jnp.sum(grad_normed_two * middle * scale_two, axis=0)
    grad_branch = grad_middle.astype(BF)
    grad_w_out = dot(att, grad_branch, (1, 0))
    grad_att = dot(w_out_all, grad_branch, (1, 1)).astype(BF)
    grad_attended = to_heads(grad_att).reshape(heads, HEAD_DIM, t)
    grad_middle_block = to_block(grad_middle)

    sum_down = weight_sum(grad_w_down, 0)
    sum_up = weight_sum(grad_w_up, 1)
    sum_out = weight_sum(grad_w_out, 0)

    grad_proj, gscale = attention_backward(
        at, qkv, raw_q, factor.reshape(HEAD_DIM, 1), attended, grad_attended[None], lse, masks
    )
    slope = QUERY_CONST / math.sqrt(HEAD_DIM) * jax.nn.sigmoid(query_scale)
    grad_query_scale = jnp.sum(gscale, axis=(0, 2)) * slope
    grad_proj = grad_proj.reshape(3, head_rows, t)
    grad_normed_one = jnp.einsum("sht,sdh->td", grad_proj, w_full, preferred_element_type=F32)
    weighted_one = grad_normed_one * gain_one
    inner_one = jnp.sum(weighted_one * xf, axis=1)
    grad_gain_attn = jnp.sum(grad_normed_one * xf * scale_one, axis=0)
    inner_one = lax.psum(inner_one, ("row", "col"))
    grad_w = jnp.einsum("td,sht->sdh", normed_one, grad_proj, preferred_element_type=F32)
    grad_w = grad_w.reshape(3, cols, 2, feat // 2, head_rows)
    core = lax.axis_index("core")
    keep = lax.dynamic_index_in_dim(grad_w, core, 2, keepdims=False)
    give = lax.dynamic_index_in_dim(grad_w, 1 - core, 2, keepdims=False).astype(BF)
    part = (keep + swap(give, "core").astype(F32)).astype(BF)
    part = jnp.concatenate(flip([part[:, 0], swap(part[:, 1], "col")], "col"), axis=2)
    sum_qkv = jnp.transpose(z_sum(part), (1, 0, 2))

    e = jnp.concatenate(flip(jnp.split(grad_normed_one.astype(BF), 2, axis=0), "row"), axis=0) if rows == 2 else (
        grad_normed_one.astype(BF)
    )
    e = scatter_sum(e, "row", 0)
    e = scatter_sum(e, "col", 1).astype(F32)
    my_rows = lambda y: lax.dynamic_slice_in_dim(y, r * tok, tok, 0)
    scale_mine = my_rows(scale_one)
    inner_mine = my_rows(inner_one.reshape(t, 1))
    grad_inputs = grad_middle_block + scale_mine * (e * gain_attn) - inputs.astype(F32) * (
        scale_mine**3 * inner_mine / D
    )

    grad_b_down = jnp.sum(g.astype(F32), axis=0)
    vectors = jnp.concatenate(
        [
            flip_dim(grad_gain_attn, "col", 0),
            flip_dim(grad_gain_mlp, "col", 0),
            flip_dim(grad_b_down, "col", 0),
            flip_dim(grad_b_up, "row", 0),
            grad_query_scale,
        ]
    )
    vectors = lax.psum(vectors, ("z", "core", "row", "col"))
    mine_col = lambda at: lax.dynamic_slice_in_dim(vectors, at * D + c * feat, feat, 0)
    units = b_up.shape[0]
    return (
        layer_out,
        grad_inputs,
        mine_col(0),
        sum_qkv,
        vectors[4 * D :],
        sum_out,
        mine_col(1),
        sum_up,
        lax.dynamic_slice_in_dim(vectors, 3 * D + r * units, units, 0),
        sum_down,
        mine_col(2),
    )


SMEM = pl.BlockSpec(memory_space=pltpu.SMEM)
ANY = pl.BlockSpec(memory_space=pl.ANY)


def call(kernel, name, args, specs, outs, scratch=(), limit=VMEM_LIMIT, out_specs=None):
    more = {} if out_specs is None else {"out_specs": out_specs}
    return pl.pallas_call(
        kernel,
        in_specs=specs,
        **more,
        out_shape=outs,
        scratch_shapes=list(scratch),
        compiler_params=pltpu.CompilerParams(vmem_limit_bytes=limit),
        cost_estimate=CHEAP,
        name=name,
    )(*args)


VM = pl.BlockSpec(memory_space=pltpu.VMEM)
HBM = pl.BlockSpec(memory_space=pltpu.HBM)


def shape(dims, kind):
    return jax.ShapeDtypeStruct(dims, kind)


def project_kernel(
    at, x00, x01, x10, x11, gain, factor, w_mine, w_a, w_b, qkv, raw, normed, scale_own, w_full
):
    r, k = at[0], at[2]
    tok, feat = x00.shape
    hr = w_mine.shape[1]
    half = hr // 2
    for s in range(3):
        w_full[pl.ds(s * hr, hr), 0:feat] = w_mine[s]
        w_full[pl.ds(pl.multiple_of(s * hr + k * half, 16), half), feat:] = w_a[s]
        w_full[pl.ds(pl.multiple_of(s * hr + (1 - k) * half, 16), half), feat:] = w_b[s]
    for i, (a_ref, b_ref) in enumerate(((x00, x01), (x10, x11))):
        a, b = a_ref[...].astype(F32), b_ref[...].astype(F32)
        total = jnp.sum(a * a, axis=1, keepdims=True) + jnp.sum(b * b, axis=1, keepdims=True)
        scale = lax.rsqrt(total / (2 * feat) + EPS)
        if i == 0:
            scale_own[...] = scale
        rows = pl.ds(pl.multiple_of((r ^ i) * tok, tok), tok)
        normed[rows, 0:feat] = (a * scale * gain[:, 0:feat]).astype(BF)
        normed[rows, feat:] = (b * scale * gain[:, feat:]).astype(BF)
        y = normed[rows, :]
        q = dot(w_full[0:hr, :], y, (1, 1))
        raw[:, rows] = q
        qkv[0, :, rows] = (q * factor[...]).astype(BF)
        qkv[1, :, rows] = dot(w_full[hr : 2 * hr, :], y, (1, 1)).astype(BF)
        qkv[2, :, rows] = dot(w_full[2 * hr : 3 * hr, :], y, (1, 1)).astype(BF)


def feed_kernel(
    at, gain, bias_up, bias_down, a, x_own, x_col, g_own, g_col,
    w_out, w_up, w_down, hx, hy, d0, d1, hx2, hy2, d02, d12,
    out_own, gm_own, post, ts, vectors, att, hidden_out, normed_out, g_out, pre_out, branch_out,
    w, x_ref, sems, more_sems,
):
    r, c, k = at[0], at[1], at[2]
    _, hr, share = a.shape
    feat = x_own.shape[1]
    half = feat // 2
    first = d0.shape[1]
    rows = pl.ds(pl.multiple_of(c * share, share), share)

    def start(pairs, sem):
        copies = [pltpu.make_async_copy(src, dst, sem.at[m]) for m, (src, dst) in enumerate(pairs)]
        for copy in copies:
            copy.start()
        return copies

    def place(s):
        return pl.ds(pl.multiple_of(((s // 2) ^ r) * 2 * hr + (s % 2) * hr, 16), hr)

    small = [(a.at[s], att.at[place(s), :]) for s in range(4)]
    small += [(x_own.at[rows, :], x_ref.at[:, 0:feat]), (x_col.at[rows, :], x_ref.at[:, feat:])]
    small += [(g_own.at[rows, :], g_out.at[:, 0:feat]), (g_col, g_out.at[:, feat:])]
    small = start(small, more_sems)
    copies = []
    for n, shard in enumerate((w_out, w_up, w_down)):
        rx, cx, ry, cy = (0, feat, feat, 0) if n == 1 else (feat, 0, 0, feat)
        mine = [(shard, w.at[n, 0:feat, 0:feat])]
        for core, (px, py, p0, p1) in ((k, (hx, hy, d0, d1)), (1 - k, (hx2, hy2, d02, d12))):
            down = core * half
            at_x = pl.ds(pl.multiple_of(rx + down, 16), half)
            at_y = pl.ds(pl.multiple_of(ry + down, 16), half)
            at_0 = pl.ds(pl.multiple_of(feat + down, 16), first)
            at_1 = pl.ds(pl.multiple_of(feat + down + first, 16), half - first)
            mine.append((px.at[n], w.at[n, at_x, cx : cx + feat]))
            mine.append((py.at[n], w.at[n, at_y, cy : cy + feat]))
            mine.append((p0.at[n], w.at[n, at_0, feat : 2 * feat]))
            mine.append((p1.at[n], w.at[n, at_1, feat : 2 * feat]))
        copies.append(start(mine, sems.at[n]))

    for copy in small + copies[0]:
        copy.wait()
    middle = x_ref[...].astype(F32) + dot(att[...], w[0], (0, 0))
    scale = lax.rsqrt(jnp.sum(middle * middle, axis=1, keepdims=True) / D + EPS)
    normed = (middle * scale * gain[...]).astype(BF)
    normed_out[...] = normed
    for copy in copies[1]:
        copy.wait()
    pre = dot(normed, w[1], (1, 0)) + bias_up[...]
    sig = jax.nn.sigmoid(pre)
    hidden = (pre * sig).astype(BF)
    hidden_out[...] = hidden
    for copy in copies[2]:
        copy.wait()
    result = (middle + dot(hidden, w[2], (1, 0)) + bias_down[...]).astype(BF)
    out_own[...] = result[:, :feat]
    post[0] = result[:, feat:]

    grad_pre_f = dot(g_out[...], w[2], (1, 1)) * sig * (1.0 + pre * (1.0 - sig))
    grad_pre = grad_pre_f.astype(BF)
    pre_out[...] = grad_pre
    grad_normed = dot(grad_pre, w[1], (1, 1))
    weighted = grad_normed * gain[...]
    inner = jnp.sum(weighted * middle, axis=1, keepdims=True)
    gf = g_out[...].astype(F32)
    grad_middle = gf + scale * weighted - middle * (scale * scale * scale * inner / D)
    gm_own[...] = grad_middle[:, :feat]
    post[1] = grad_middle[:, feat:].astype(BF)
    branch = grad_middle.astype(BF)
    branch_out[...] = branch
    for s in range(4):
        ts[s] = dot(w[0, place(s), :], branch, (1, 1)).astype(BF)
    vectors[...] = jnp.concatenate(
        [
            jnp.sum(grad_normed * (middle * scale), axis=0, keepdims=True),
            jnp.sum(gf, axis=0, keepdims=True),
            jnp.sum(grad_pre.astype(F32), axis=0, keepdims=True),
        ],
        axis=0,
    )


def feed_weights_kernel(at, att, hidden, normed, g, grad_pre, branch, *rest):
    *grads, stage, turned, sems = rest
    k = at[2]
    feat = g.shape[1] // 2
    half = feat // 2
    quarter = half // 2
    copies = []

    def weight_grad(n, left_ref, right):
        for core, begin in ((k, 0), (1 - k, 8)):
            up, low = (begin + 4, begin) if n == 1 else (begin, begin + 4)
            for b in range(2):
                part = pl.ds(pl.multiple_of(b * feat + core * half, 16), half)
                y = dot(left_ref[part, :], right, (1, 0)).astype(BF)
                for j in range(2):
                    cut = slice(j * feat, (j + 1) * feat)
                    for to, value in ((up + 2 * j + (1 - b), y[:quarter, cut]), (low + 2 * b + (1 - j), y[quarter:, cut])):
                        stage[to, n] = value
                        copy = pltpu.make_async_copy(stage.at[to, n], grads[to].at[n], sems.at[to, n])
                        copy.start()
                        copies.append(copy)

    turned[0] = hidden[...].astype(F32).T.astype(BF)
    weight_grad(2, turned.at[0], g[...])
    turned[1] = normed[...].astype(F32).T.astype(BF)
    weight_grad(1, turned.at[1], grad_pre[...])
    weight_grad(0, att, branch[...])
    for copy in copies:
        copy.wait()


def weight_back_kernel(at, grad, normed, keep, give):
    k = at[2]
    part = keep.shape[2]
    feat = keep.shape[3]
    for ref, core in ((give, 1 - k), (keep, k)):
        for s in range(3):
            rows = pl.ds(pl.multiple_of(core * part, 16), part)
            y = dot(grad[s, rows, :], normed[...], (1, 0)).astype(BF)
            ref[0, s] = y[:, :feat]
            ref[1, s] = y[:, feat:]


def project_back_kernel(
    at, grad, w_full, x00, x01, x10, x11, gain, es, gain_sum
):
    r, c = at[0], at[1]
    tok, feat = x00.shape
    sums = [jnp.zeros((1, feat), F32), jnp.zeros((1, feat), F32)]
    for i, xs in enumerate(((x00, x01), (x10, x11))):
        rows = pl.ds(pl.multiple_of((r ^ i) * tok, tok), tok)
        left = grad[:, rows]
        products, squares, inner = [], 0.0, 0.0
        for j in range(2):
            cut = slice(j * feat, (j + 1) * feat)
            e = dot(left, w_full[:, cut], (0, 0))
            x = xs[j][...].astype(F32)
            product = e * x
            inner = inner + jnp.sum(product * gain[:, cut], axis=1, keepdims=True)
            squares = squares + jnp.sum(x * x, axis=1, keepdims=True)
            es[2 * (r ^ i) + (c ^ j), 0:tok, :] = e.astype(BF)
            products.append(product)
        scale = lax.rsqrt(squares / (2 * feat) + EPS)
        for j in range(2):
            sums[j] += jnp.sum(products[j] * scale, axis=0, keepdims=True)
        line = jnp.broadcast_to(inner, (tok, 128)).T[0:1, :]
        high = line.astype(BF).astype(F32)
        extra = jnp.concatenate([high, line - high, jnp.zeros((14, tok), F32)], axis=0)
        extra = jnp.concatenate([extra, jnp.zeros((16, feat - tok), F32)], axis=1).astype(BF)
        for j in range(2):
            es[2 * (r ^ i) + (c ^ j), tok:, :] = extra
    gain_sum[:, 0:feat] = sums[0]
    gain_sum[:, feat:] = sums[1]


def finish_qkv_kernel(at, mine, theirs, mine2, theirs2, out, rows):
    c, k = at[1], at[2]
    half = mine.shape[1]
    for s in range(3):
        for ref, col, core in ((mine, c, k), (theirs, 1 - c, k), (mine2, c, 1 - k), (theirs2, 1 - c, 1 - k)):
            rows[pl.ds(pl.multiple_of((2 * col + core) * half, 16), half), :] = ref[s].astype(F32)
        out[s] = rows[...].T


def finish_feed_kernel(at, a, b, a2, b2, *outs):
    k = at[2]
    quarter = a.shape[1]
    for n, out in enumerate(outs):
        upper, lower = ((b, b2), (a, a2)) if n == 1 else ((a, a2), (b, b2))
        for i, core in ((0, k), (1, 1 - k)):
            for j, refs in enumerate((upper, lower)):
                to = pl.multiple_of((2 * core + j) * quarter, 16)
                out[pl.ds(to, quarter), :] = refs[i][n].astype(F32)


together = lax.optimization_barrier


def after(x, *earlier):
    return lax.optimization_barrier((x, *earlier))[0]


def add(*parts):
    total = parts[0].astype(F32)
    for part in parts[1:]:
        total = total + part.astype(F32)
    return total.astype(BF)


def all_four(x):
    return lax.all_to_all(x, ("row", "col"), 0, 0, tiled=True)


def z_swap(x, step):
    n = size("z")
    return lax.ppermute(x, "z", [(i, i ^ step) for i in range(n)])


def z_first():
    z = lax.axis_index("z")
    return (z == 0) | (z == 3)


def body_four(
    inputs, gain_attn, w_qkv, query_scale, w_out, gain_mlp, w_up, b_up, w_down, b_down, series_ids, pad_mask, cotangent
):
    tok, feat = inputs.shape
    share = tok // 2
    t = series_ids.shape[0]
    hr = w_qkv.shape[2] // 2
    heads = hr // HEAD_DIM
    half = feat // 2
    r, c, k = lax.axis_index("row"), lax.axis_index("col"), lax.axis_index("core")
    at = jnp.stack([r, c, k, 2 * r + c]).astype(jnp.int32)
    mine_rows = lambda y, part: lax.dynamic_slice_in_dim(y, part * share, share, 0)

    few = heads // 2
    quarter = half // 2
    first_rows = (half * 7 // 20) // 16 * 16
    x01 = swap(inputs, "col")
    x10 = swap(inputs, "row")
    small = swap(jnp.concatenate([gain_attn, gain_mlp, b_down.astype(F32)]), "col")
    up_other = swap(b_up.astype(F32), "row")
    w_turned = jnp.transpose(w_qkv, (1, 2, 0)).reshape(3, 2, hr, feat)
    w_mine = lax.dynamic_index_in_dim(w_turned, c, 1, keepdims=False)
    w_give = lax.dynamic_index_in_dim(w_turned, 1 - c, 1, keepdims=False)
    w_half = core_half(w_give, 1)
    w_a = swap(w_half, "col")
    part = jnp.stack([core_half(w_out, 0), core_half(w_up, 0), core_half(w_down, 0)])
    g_give = mine_rows(cotangent, 1 - c)
    x01, x10, small, up_other, part, g_give, w_mine = lax.optimization_barrier(
        (x01, x10, small, up_other, part, g_give, w_mine)
    )
    x11 = swap(after(x01, w_half), "row")
    w_b = swap(w_a, "core")
    gain_one = jnp.concatenate([gain_attn, small[:feat]]).reshape(1, D)
    gain_two = jnp.concatenate([gain_mlp, small[feat : 2 * feat]]).reshape(1, D)
    bias_down = jnp.concatenate([b_down.astype(F32), small[2 * feat :]]).reshape(1, D)
    bias_up = jnp.concatenate([b_up.astype(F32), up_other]).reshape(1, D)
    factor = QUERY_CONST / math.sqrt(HEAD_DIM) * jax.nn.softplus(query_scale)
    factor_col = factor.reshape(HEAD_DIM, 1)

    part = after(part, x11, w_a)
    hx, hy = swap(part, "row"), swap(part, "col")
    hx2, hy2 = swap(hx, "core"), swap(hy, "core")
    qkv, raw, normed_one, scale_own, w_full = call(
        project_kernel,
        "project",
        (at, inputs, x01, x10, x11, gain_one, jnp.tile(factor_col, (heads, 1)), w_mine, w_a, w_b),
        [SMEM] + [VM] * 9,
        [
            shape((3, hr, t), BF),
            shape((hr, t), F32),
            shape((t, D), BF),
            shape((tok, 1), F32),
            shape((3 * hr, D), BF),
        ],
        limit=VMEM_LARGE,
    )
    qkv = qkv.reshape(3, heads, HEAD_DIM, t)
    masks = mask_args(series_ids, pad_mask)
    attended, lse, a = attention_forward(at, qkv, masks, pieces=1)
    a = all_four(a.reshape(4, hr, share))
    hx_on, hy_on, g_give = lax.optimization_barrier((hx, hy, g_give, lse))[:3]
    d0 = swap(hx_on[:, :first_rows], "col")
    d1 = swap(hy_on[:, first_rows:], "row")
    g_col = swap(g_give, "col")
    d0, d1, g_col, a = together((d0, d1, g_col, a))
    d02, d12 = swap(d0, "core"), swap(d1, "core")
    out_own, gm_own, post, ts, vectors, *factors = call(
        feed_kernel,
        "feed_forward",
        (at, gain_two, bias_up, bias_down, a, inputs, x01, cotangent, g_col)
        + (w_out, w_up, w_down, hx, hy, d0, d1, hx2, hy2, d02, d12),
        [SMEM] + [VM] * 3 + [HBM] * 16,
        [
            shape((share, feat), BF),
            shape((share, feat), F32),
            shape((2, share, feat), BF),
            shape((4, hr, share), BF),
            shape((3, D), F32),
            shape((D, share), BF),
        ]
        + [shape((share, D), BF)] * 5,
        scratch=[
            pltpu.VMEM((3, D, D), BF),
            pltpu.VMEM((share, D), BF),
            pltpu.SemaphoreType.DMA((3, 9)),
            pltpu.SemaphoreType.DMA((8,)),
        ],
        limit=VMEM_LARGE,
    )
    grads = call(
        feed_weights_kernel,
        "feed_weights",
        (at, *factors),
        [SMEM] + [VM] * 6,
        [shape((3, quarter, feat), BF)] * 16,
        scratch=[
            pltpu.VMEM((16, 3, quarter, feat), BF),
            pltpu.VMEM((2, D, share), BF),
            pltpu.SemaphoreType.DMA((16, 3)),
        ],
        out_specs=[HBM] * 16,
        limit=VMEM_LARGE,
    )
    ts = all_four(ts)
    others = grads[8:]
    over = lambda n: swap(others[n], "core")
    grads, osx0, osx1, osy0, osy1 = grads[:8], over(0), over(2), over(4), over(6)
    sx0, kx0, sx1, kx1, sy0, ky0, sy1, ky1 = grads
    sx1, sy1 = add(sx1, osx1), add(sy1, osy1)
    ox0, ox1, oy0, oy1 = over(1), over(3), over(5), over(7)
    sx0, sy0 = add(sx0, osx0), add(sy0, osy0)
    ts, sx1, sy1, sx0, sy0 = together((ts, sx1, sy1, sx0, sy0))
    rx1, ry1 = swap(sx1, "row"), swap(sy1, "col")
    rx0, ry0 = swap(sx0, "row"), swap(sy0, "col")
    ts = ts.reshape(4, heads, HEAD_DIM, share)
    raw = raw.reshape(heads, HEAD_DIM, t)

    grad_proj, gscale = attention_backward(at, qkv, raw, factor_col, attended, ts, lse, masks)
    grad_proj = grad_proj.reshape(3, hr, t)
    kept, sent = call(
        weight_back_kernel,
        "weight_back",
        (at, grad_proj, normed_one),
        [SMEM] + [VM] * 2,
        [shape((2, 3, hr // 2, feat), BF)] * 2,
    )
    sent, rx1, ry1, rx0, ry0, ox0, ox1, oy0, oy1 = together((sent, rx1, ry1, rx0, ry0, ox0, ox1, oy0, oy1))
    got = swap(sent, "core")
    px1, py1 = add(kx1, ox1, rx1), add(ky1, oy1, ry1)
    qx, qy = swap(px1, "col"), swap(py1, "row")
    w_pair = add(kept, got)
    first = z_first()
    got_w = z_swap(jnp.where(first, w_pair[1], w_pair[0]), 1)
    slope = QUERY_CONST / math.sqrt(HEAD_DIM) * jax.nn.sigmoid(query_scale)
    grad_query_scale = jnp.sum(gscale, axis=(0, 2)) * slope
    es, gain_sum = call(
        project_back_kernel,
        "project_back",
        (at, after(grad_proj, w_pair, px1, py1).reshape(3 * hr, t), w_full, inputs, x01, x10, x11, gain_one),
        [SMEM] + [VM] * 7,
        [
            shape((4, tok + 16, feat), BF),
            shape((1, D), F32),
        ],
    )
    total = jnp.concatenate([gain_sum, vectors]).reshape(4, 2, feat)
    turn = jnp.stack([c, c, c, r]).reshape(4, 1, 1) == 1
    total = jnp.where(turn, total[:, ::-1], total).reshape(8, feat)
    total = jnp.concatenate([total, jnp.pad(grad_query_scale, (0, feat - HEAD_DIM)).reshape(1, feat)])
    total = total + swap(total, "core")
    qx, qy, got_w, w_pair, es = together((qx, qy, got_w, w_pair, es))

    mine_w = add(jnp.where(first, w_pair[0], w_pair[1]), got_w)
    met_w = z_swap(mine_w, 3)
    fx, fy = add(kx0, ox0, rx0, qx), add(ky0, oy0, ry0, qy)
    got_c = z_swap(jnp.where(first, fy, fx), 1)
    es = all_four(after(es, fx, fy, mine_w))
    total = total + swap(total, "row")
    total = total + swap(total, "col")
    met_w, mine_w, got_c, fx, fy, es, post, total = together((met_w, mine_w, got_c, fx, fy, es, post, total))

    mine_w = add(mine_w, met_w)
    other_w = z_swap(mine_w, 1)
    w_own, w_theirs = jnp.where(first, mine_w, other_w), jnp.where(first, other_w, mine_w)
    mine_c = add(jnp.where(first, fx, fy), got_c)
    met_c = z_swap(mine_c, 3)
    post = swap(post, "col")
    w_theirs = swap(w_theirs, "col")
    total = total + z_swap(total, 1)
    total = total + z_swap(total, 3)
    met_c, mine_c, w_own, w_theirs, post, total = together((met_c, mine_c, w_own, w_theirs, post, total))
    mine_c = add(mine_c, met_c)
    other_c = z_swap(mine_c, 1)
    w_args = (at, w_own, w_theirs, swap(w_own, "core"), swap(w_theirs, "core"))
    sum_qkv = call(
        finish_qkv_kernel,
        "finish_qkv",
        w_args,
        [SMEM] + [VM] * 4,
        shape((3, feat, 2 * hr), F32),
        scratch=[pltpu.VMEM((2 * hr, feat), F32)],
    )
    sum_qkv = jnp.transpose(sum_qkv, (1, 0, 2))

    e = jnp.sum(es[:, :tok].astype(F32), axis=0)
    inner = jnp.sum(es[:, tok : tok + 2, :tok].astype(F32), axis=(0, 1)).reshape(tok, 1)
    grad_middle = jnp.concatenate(flip([gm_own, post[1].astype(F32)], "col"), axis=0)
    grad_inputs = grad_middle + scale_own * (e * gain_attn) - inputs.astype(F32) * (scale_own**3 * inner / D)
    layer_out = jnp.concatenate(flip([out_own, post[0]], "col"), axis=0)

    pick = lambda n, place: lax.dynamic_index_in_dim(total, 2 * n + place, 0, keepdims=False)
    mine_c = after(mine_c, sum_qkv, grad_inputs, layer_out, total)
    fx, fy = jnp.where(first, mine_c, other_c), jnp.where(first, other_c, mine_c)
    sum_out, sum_up, sum_down = call(
        finish_feed_kernel,
        "finish_feed",
        (at, fx, fy, swap(fx, "core"), swap(fy, "core")),
        [SMEM] + [VM] * 4,
        [shape((feat, feat), F32)] * 3,
    )

    return (
        layer_out,
        grad_inputs,
        pick(0, c),
        sum_qkv,
        total[8, :HEAD_DIM],
        sum_out,
        pick(1, c),
        sum_up,
        pick(3, r),
        sum_down,
        pick(2, c),
    )


def solution(mesh):
    dp, rows, cols = mesh.shape["dp"], mesh.shape["row"], mesh.shape["col"]
    split = Mesh(mesh.devices.reshape(dp // 2, 2, rows, cols), ("z", "core", "row", "col"))
    tokens = P(("z", "core", "row"), "col")
    in_specs = (
        tokens,
        P("col"),
        P("col", None, "row"),
        P(),
        P("row", "col"),
        P("col"),
        P("col", "row"),
        P("row"),
        P("row", "col"),
        P("col"),
        P(("z", "core")),
        P(("z", "core")),
        tokens,
    )
    out_specs = (
        tokens,
        tokens,
        P("col"),
        P("col", None, "row"),
        P(),
        P("row", "col"),
        P("col"),
        P("col", "row"),
        P("row"),
        P("row", "col"),
        P("col"),
    )
    body = body_four if (dp, rows, cols) == (8, 2, 2) else body_any
    return jax.shard_map(body, mesh=split, in_specs=in_specs, out_specs=out_specs, check_vma=False)
```

```python
import functools
import math

import jax
import jax.numpy as jnp
from jax import lax
from jax.experimental import pallas as pl
from jax.experimental.pallas import tpu as pltpu
from jax.sharding import Mesh
from jax.sharding import PartitionSpec as P

D = 1280
HEAD_DIM = 80
EPS = 1e-06
QUERY_CONST = 1.442695041
MASKED = -1e30
BF = jnp.bfloat16
F32 = jnp.float32
VMEM_LIMIT = 60 * 1024 * 1024
VMEM_LARGE = 60 * 1024 * 1024
CHEAP = pl.CostEstimate(flops=1, bytes_accessed=1, transcendentals=0)


def size(axis):
    return lax.axis_size(axis)


def swap(x, axis):
    return lax.ppermute(x, axis, [(0, 1), (1, 0)])


def flip(blocks, axis):
    if size(axis) != 2:
        return list(blocks)
    first = lax.axis_index(axis) == 0
    a, b = blocks
    return [jnp.where(first, a, b), jnp.where(first, b, a)]


def flip_dim(x, axis, dim):
    if size(axis) != 2:
        return x
    return jnp.concatenate(flip(jnp.split(x, 2, axis=dim), axis), axis=dim)


def gather(x, axis):
    if size(axis) == 2:
        return [x, swap(x, axis)]
    whole = lax.all_gather(x, axis, axis=0, tiled=False)
    return [whole[i] for i in range(size(axis))]


def gather_grid(x):
    if size("row") != 2:
        return [gather(b, "col") for b in gather(x, "row")]
    along_row, along_col = swap(x, "row"), swap(x, "col")
    half = x.shape[0] // 2
    across = jnp.concatenate(
        [swap(along_row[:half], "col"), swap(along_col[half:], "row")], axis=0
    )
    return [[x, along_col], [along_row, across]]


def scatter_sum(x, axis, dim):
    if size(axis) != 2:
        return lax.psum_scatter(x, axis, scatter_dimension=dim, tiled=True)
    mine, theirs = jnp.split(x, 2, axis=dim)
    return (mine.astype(F32) + swap(theirs, axis).astype(F32)).astype(x.dtype)


def exchange(x, axis, split, join):
    if size(axis) != 2:
        return lax.all_to_all(x, axis, split, join, tiled=True)
    mine, theirs = jnp.split(x, 2, axis=split)
    return jnp.concatenate([mine, swap(theirs, axis)], axis=join)


def core_half(x, dim):
    return lax.dynamic_slice_in_dim(
        x, lax.axis_index("core") * (x.shape[dim] // 2), x.shape[dim] // 2, dim
    )


def weight_gather(w, row_dim):
    part = core_half(w, 0)
    blocks = gather_grid(part)
    if row_dim == 1:
        blocks = [list(b) for b in zip(*blocks)]
    mine = jnp.stack([jnp.concatenate(b, axis=1) for b in blocks])
    other = swap(mine, "core")
    first = lax.axis_index("core") == 0
    both = jnp.stack([jnp.where(first, mine, other), jnp.where(first, other, mine)], axis=1)
    return both.reshape(-1, both.shape[-1])


def weight_sum(g, row_dim):
    dim_axis = ("row", "col") if row_dim == 0 else ("col", "row")
    n0 = size(dim_axis[0])
    g = g.reshape(n0, 2, g.shape[0] // n0 // 2, g.shape[1])
    core = lax.axis_index("core")
    keep = lax.dynamic_index_in_dim(g, core, 1, keepdims=False)
    give = lax.dynamic_index_in_dim(g, 1 - core, 1, keepdims=False).astype(BF)
    part = (keep + swap(give, "core").astype(F32)).astype(BF)
    part = scatter_sum(part, dim_axis[0], 0)
    part = scatter_sum(part[0], dim_axis[1], 1)
    return z_sum(part)


def z_sum(part):
    total = lax.psum(part, "z")
    other = swap(total, "core")
    return flip_core(total, other)


def flip_core(total, other):
    first = lax.axis_index("core") == 0
    return jnp.concatenate(
        [jnp.where(first, total, other), jnp.where(first, other, total)], axis=-2
    ).astype(F32)


def dot(a, b, contract):
    return lax.dot_general(a, b, ((contract[0:1], contract[1:2]), ((), ())), preferred_element_type=F32)


def bias_block(series_row, series_col, key_pos, q0, k0, qb, kb, diagonal):
    q_pos = q0 + lax.broadcasted_iota(jnp.int32, (1, qb), 1)
    allowed = (series_col == series_row) & (key_pos <= q_pos)
    if diagonal:
        k_pos = k0 + lax.broadcasted_iota(jnp.int32, (kb, 1), 0)
        allowed = allowed | (k_pos == q_pos)
    return jnp.where(allowed, 0.0, MASKED)


def forward_kernel(block, at, qkv_ref, srow_ref, scol_ref, kpos_ref, out_ref, lse_ref, *rest):
    *pieces, bias_ref, krow_ref, s_ref = rest
    t = qkv_ref.shape[3]
    n = t // block
    krow_ref[...] = qkv_ref[1, 0].astype(F32).T.astype(BF)

    def bias_slot(j, i):
        return j * (j + 1) // 2 + i

    @pl.when(pl.program_id(0) == 0)
    def _():
        for j in range(n):
            for i in range(j + 1):
                keys = pl.ds(i * block, block)
                bias_ref[bias_slot(j, i)] = bias_block(
                    srow_ref[:, j * block : (j + 1) * block],
                    scol_ref[keys, :],
                    kpos_ref[keys, :],
                    j * block,
                    i * block,
                    block,
                    block,
                    i == j,
                )

    for j in range(n):
        cols = slice(j * block, (j + 1) * block)
        q = qkv_ref[0, 0, :, cols]
        top = None
        for i in range(j + 1):
            s = dot(krow_ref[i * block : (i + 1) * block, :], q, (1, 0)) + bias_ref[bias_slot(j, i)]
            s_ref[i * block : (i + 1) * block, :] = s
            here = jnp.max(s, axis=0, keepdims=True)
            top = here if top is None else jnp.maximum(top, here)
        total = jnp.zeros((1, block), F32)
        acc = jnp.zeros((HEAD_DIM, block), F32)
        for i in range(j + 1):
            p = jnp.exp(s_ref[i * block : (i + 1) * block, :] - top)
            total += jnp.sum(p, axis=0, keepdims=True)
            acc += dot(qkv_ref[2, 0, :, i * block : (i + 1) * block], p.astype(BF), (1, 0))
        found = (acc / total).astype(BF)
        out_ref[0, :, cols] = found
        if pieces:
            pieces[0][j, 0] = found
        lse_ref[0, :, cols] = top + jnp.log(total)


def backward_kernel(
    block, at, qkv_ref, raw_ref, factor_ref, out_ref, lse_ref, srow_ref, scol_ref, kpos_ref, *rest
):
    piece, grad_ref, gscale_ref, bias_ref, krow_ref, vrow_ref, gk_ref, gv_ref, gout_ref = rest
    wide = piece.shape[3]
    for j in range(piece.shape[0]):
        gout_ref[:, j * wide : (j + 1) * wide] = piece[j, 0]
    t = qkv_ref.shape[3]
    n = t // block
    krow_ref[...] = qkv_ref[1, 0].astype(F32).T.astype(BF)
    vrow_ref[...] = qkv_ref[2, 0].astype(F32).T.astype(BF)

    def bias_slot(j, i):
        return j * (j + 1) // 2 + i

    @pl.when(pl.program_id(0) == 0)
    def _():
        for j in range(n):
            for i in range(j + 1):
                keys = pl.ds(i * block, block)
                bias_ref[bias_slot(j, i)] = bias_block(
                    srow_ref[:, j * block : (j + 1) * block],
                    scol_ref[keys, :],
                    kpos_ref[keys, :],
                    j * block,
                    i * block,
                    block,
                    block,
                    i == j,
                )

    gscale = jnp.zeros((HEAD_DIM, 1), F32)
    for j in range(n):
        cols = slice(j * block, (j + 1) * block)
        q = qkv_ref[0, 0, :, cols]
        go = gout_ref[:, cols]
        lse = lse_ref[0, :, cols]
        delta = jnp.sum(go.astype(F32) * out_ref[0, :, cols].astype(F32), axis=0, keepdims=True)
        gq = jnp.zeros((HEAD_DIM, block), F32)
        for i in range(j + 1):
            keys = slice(i * block, (i + 1) * block)
            s = dot(krow_ref[keys, :], q, (1, 0)) + bias_ref[bias_slot(j, i)]
            p = jnp.exp(s - lse)
            gp = dot(vrow_ref[keys, :], go, (1, 0))
            gs = (p * (gp - delta)).astype(BF)
            gq += dot(qkv_ref[1, 0, :, keys], gs, (1, 0))
            gk = dot(q, gs, (1, 1))
            gv = dot(go, p.astype(BF), (1, 1))
            if i == j:
                gk_ref[:, keys] = gk
                gv_ref[:, keys] = gv
            else:
                gk_ref[:, keys] += gk
                gv_ref[:, keys] += gv
        gscale += jnp.sum(gq * raw_ref[0, :, cols], axis=1, keepdims=True)
        grad_ref[0, 0, :, cols] = (gq * factor_ref[...]).astype(BF)
    grad_ref[1, 0] = gk_ref[...].astype(BF)
    grad_ref[2, 0] = gv_ref[...].astype(BF)
    gscale_ref[0] = gscale


def mask_args(series, padding):
    t = series.shape[0]
    pos = jnp.arange(t, dtype=jnp.int32)
    return series.reshape(1, t), series.reshape(t, 1), jnp.where(padding == 0, pos, t).reshape(t, 1)


def attention_forward(at, qkv, masks, pieces=0):
    _, heads, hd, t = qkv.shape
    block = min(256, t) if t <= 2048 else 512
    n = t // block
    whole = lambda shape: pl.BlockSpec(shape, lambda h: (0,) * len(shape))
    return pl.pallas_call(
        functools.partial(forward_kernel, block),
        grid=(heads,),
        in_specs=[
            pl.BlockSpec(memory_space=pltpu.SMEM),
            pl.BlockSpec((3, 1, hd, t), lambda h: (0, h, 0, 0)),
            whole((1, t)),
            whole((t, 1)),
            whole((t, 1)),
        ],
        out_specs=[
            pl.BlockSpec((1, hd, t), lambda h: (h, 0, 0)),
            pl.BlockSpec((1, 1, t), lambda h: (h, 0, 0)),
        ]
        + [pl.BlockSpec((n, 1, hd, block), lambda h: (0, h, 0, 0))] * pieces,
        out_shape=[
            jax.ShapeDtypeStruct((heads, hd, t), BF),
            jax.ShapeDtypeStruct((heads, 1, t), F32),
        ]
        + [jax.ShapeDtypeStruct((n, heads, hd, block), BF)] * pieces,
        scratch_shapes=[
            pltpu.VMEM((n * (n + 1) // 2, block, block), F32),
            pltpu.VMEM((t, hd), BF),
            pltpu.VMEM((t, block), F32),
        ],
        compiler_params=pltpu.CompilerParams(vmem_limit_bytes=VMEM_LARGE),
        cost_estimate=CHEAP,
        name="attention_forward",
    )(at, qkv, *masks)


def attention_backward(at, qkv, raw, factor, out, piece, lse, masks):
    _, heads, hd, t = qkv.shape
    block = min(256, t) if t <= 2048 else 512
    n = t // block
    whole = lambda shape: pl.BlockSpec(shape, lambda h: (0,) * len(shape))
    head = lambda wide=t: pl.BlockSpec((1, hd, wide), lambda h: (h, 0, 0))
    return pl.pallas_call(
        functools.partial(backward_kernel, block),
        grid=(heads,),
        in_specs=[
            pl.BlockSpec(memory_space=pltpu.SMEM),
            pl.BlockSpec((3, 1, hd, t), lambda h: (0, h, 0, 0)),
            head(),
            whole((hd, 1)),
            head(),
            pl.BlockSpec((1, 1, t), lambda h: (h, 0, 0)),
            whole((1, t)),
            whole((t, 1)),
            whole((t, 1)),
        ]
        + [pl.BlockSpec((piece.shape[0], 1, hd, piece.shape[3]), lambda h: (0, h, 0, 0))],
        out_specs=[
            pl.BlockSpec((3, 1, hd, t), lambda h: (0, h, 0, 0)),
            pl.BlockSpec((1, hd, 1), lambda h: (h, 0, 0)),
        ],
        out_shape=[
            jax.ShapeDtypeStruct((3, heads, hd, t), BF),
            jax.ShapeDtypeStruct((heads, hd, 1), F32),
        ],
        scratch_shapes=[
            pltpu.VMEM((n * (n + 1) // 2, block, block), F32),
            pltpu.VMEM((t, hd), BF),
            pltpu.VMEM((t, hd), BF),
            pltpu.VMEM((hd, t), F32),
            pltpu.VMEM((hd, t), F32),
            pltpu.VMEM((hd, t), BF),
        ],
        compiler_params=pltpu.CompilerParams(vmem_limit_bytes=VMEM_LARGE),
        cost_estimate=CHEAP,
        name="attention_backward",
    )(at, qkv, raw, factor, out, lse, *masks, piece)


def norm_scale(x):
    return lax.rsqrt(jnp.mean(x * x, axis=1, keepdims=True) + EPS)


def body_any(
    inputs, gain_attn, w_qkv, query_scale, w_out, gain_mlp, w_up, b_up, w_down, b_down, series_ids, pad_mask, cotangent
):
    rows, cols = size("row"), size("col")
    tok = inputs.shape[0]
    feat = inputs.shape[1]
    share = tok // cols
    t = series_ids.shape[0]
    head_rows = w_qkv.shape[2] // cols
    heads = head_rows // HEAD_DIM
    r, c = lax.axis_index("row"), lax.axis_index("col")

    blocks = gather_grid(inputs)
    strips = [jnp.concatenate(b, axis=1) for b in blocks]
    x_own = strips[0] if rows == 2 else lax.dynamic_index_in_dim(jnp.stack(strips), r, 0, keepdims=False)
    x_all = jnp.concatenate(flip(strips, "row"), axis=0)
    gain_one = jnp.concatenate(gather(gain_attn, "col"))
    gain_two = jnp.concatenate(gather(gain_mlp, "col"))
    bias_up = jnp.concatenate(gather(b_up, "row")).astype(F32)
    bias_down = jnp.concatenate(gather(b_down, "col")).astype(F32)

    w3 = jnp.transpose(w_qkv, (1, 0, 2)).reshape(3, feat, cols, head_rows)
    w_mine = lax.dynamic_index_in_dim(w3, c, 2, keepdims=False)
    w_give = lax.dynamic_index_in_dim(w3, 1 - c, 2, keepdims=False)
    w_half = swap(core_half(w_give, 1), "col")
    w_other = swap(w_half, "core")
    first = lax.axis_index("core") == 0
    w_full = jnp.concatenate(
        [w_mine, jnp.where(first, w_half, w_other), jnp.where(first, w_other, w_half)], axis=1
    )

    xf = x_all.astype(F32)
    scale_one = norm_scale(xf)
    normed_one = (xf * scale_one * gain_one).astype(BF)
    projected = jnp.einsum("td,sdh->sht", normed_one, w_full, preferred_element_type=F32)
    projected = projected.reshape(3, heads, HEAD_DIM, t)
    factor = QUERY_CONST / math.sqrt(HEAD_DIM) * jax.nn.softplus(query_scale)
    raw_q = projected[0]
    qkv = jnp.stack([raw_q * factor[None, :, None], projected[1], projected[2]]).astype(BF)
    masks = mask_args(series_ids, pad_mask)
    at = jnp.zeros((4,), jnp.int32)
    attended, lse = attention_forward(at, qkv, masks)

    def to_tokens(y):
        y = flip_dim(y.reshape(head_rows, rows, cols, share), "row", 1)
        y = flip_dim(y, "col", 2)
        y = exchange(y.reshape(1, head_rows, rows, cols, share), "row", 2, 0)
        y = exchange(y.reshape(rows, 1, head_rows, cols, share), "col", 3, 1)
        y = flip_dim(y.reshape(rows, cols, head_rows, share), "col", 1)
        return y.reshape(rows * cols * head_rows, share)

    def to_heads(y):
        y = flip_dim(y.reshape(rows, cols, head_rows, share), "col", 1)
        y = exchange(y.reshape(rows, cols, head_rows, 1, share), "col", 1, 3)
        y = exchange(y.reshape(rows, head_rows, 1, cols, share), "row", 0, 2)
        y = flip_dim(y.reshape(head_rows, rows, cols, share), "col", 2)
        return flip_dim(y, "row", 1).reshape(head_rows, t)

    w_out_all = weight_gather(w_out, 0)
    w_up_all = weight_gather(w_up, 1)
    w_down_all = weight_gather(w_down, 0)

    def my_share(y):
        return lax.dynamic_slice_in_dim(y, c * share, share, 0)

    att = to_tokens(attended.reshape(head_rows, t))
    x_mine = my_share(x_own).astype(F32)
    middle = x_mine + dot(att, w_out_all, (0, 0))
    scale_two = norm_scale(middle)
    normed_two = (middle * scale_two * gain_two).astype(BF)
    pre_act = dot(normed_two, w_up_all, (1, 0)) + bias_up
    sig = jax.nn.sigmoid(pre_act)
    hidden = (pre_act * sig).astype(BF)
    result = (middle + dot(hidden, w_down_all, (1, 0)) + bias_down).astype(BF)

    def to_block(y):
        mine, theirs = jnp.split(y, 2, axis=1)
        return jnp.concatenate(flip([mine, swap(theirs, "col")], "col"), axis=0)

    layer_out = to_block(result)

    g_give = lax.dynamic_slice_in_dim(cotangent, (1 - c) * share, share, 0)
    g = jnp.concatenate([my_share(cotangent), swap(g_give, "col")], axis=1)
    grad_w_down = dot(hidden, g, (0, 0))
    grad_hidden = dot(g, w_down_all, (1, 1))
    grad_pre_f = grad_hidden * sig * (1.0 + pre_act * (1.0 - sig))
    grad_pre = grad_pre_f.astype(BF)
    grad_b_up = jnp.sum(grad_pre.astype(F32), axis=0)
    grad_w_up = dot(normed_two, grad_pre, (0, 0))
    grad_normed_two = dot(grad_pre, w_up_all, (1, 1))
    weighted = grad_normed_two * gain_two
    inner = jnp.sum(weighted * middle, axis=1, keepdims=True)
    grad_middle = g.astype(F32) + scale_two * weighted - middle * (scale_two**3 * inner / D)
    grad_gain_mlp = jnp.sum(grad_normed_two * middle * scale_two, axis=0)
    grad_branch = grad_middle.astype(BF)
    grad_w_out = dot(att, grad_branch, (1, 0))
    grad_att = dot(w_out_all, grad_branch, (1, 1)).astype(BF)
    grad_attended = to_heads(grad_att).reshape(heads, HEAD_DIM, t)
    grad_middle_block = to_block(grad_middle)

    sum_down = weight_sum(grad_w_down, 0)
    sum_up = weight_sum(grad_w_up, 1)
    sum_out = weight_sum(grad_w_out, 0)

    grad_proj, gscale = attention_backward(
        at, qkv, raw_q, factor.reshape(HEAD_DIM, 1), attended, grad_attended[None], lse, masks
    )
    slope = QUERY_CONST / math.sqrt(HEAD_DIM) * jax.nn.sigmoid(query_scale)
    grad_query_scale = jnp.sum(gscale, axis=(0, 2)) * slope
    grad_proj = grad_proj.reshape(3, head_rows, t)
    grad_normed_one = jnp.einsum("sht,sdh->td", grad_proj, w_full, preferred_element_type=F32)
    weighted_one = grad_normed_one * gain_one
    inner_one = jnp.sum(weighted_one * xf, axis=1)
    grad_gain_attn = jnp.sum(grad_normed_one * xf * scale_one, axis=0)
    inner_one = lax.psum(inner_one, ("row", "col"))
    grad_w = jnp.einsum("td,sht->sdh", normed_one, grad_proj, preferred_element_type=F32)
    grad_w = grad_w.reshape(3, cols, 2, feat // 2, head_rows)
    core = lax.axis_index("core")
    keep = lax.dynamic_index_in_dim(grad_w, core, 2, keepdims=False)
    give = lax.dynamic_index_in_dim(grad_w, 1 - core, 2, keepdims=False).astype(BF)
    part = (keep + swap(give, "core").astype(F32)).astype(BF)
    part = jnp.concatenate(flip([part[:, 0], swap(part[:, 1], "col")], "col"), axis=2)
    sum_qkv = jnp.transpose(z_sum(part), (1, 0, 2))

    e = jnp.concatenate(flip(jnp.split(grad_normed_one.astype(BF), 2, axis=0), "row"), axis=0) if rows == 2 else (
        grad_normed_one.astype(BF)
    )
    e = scatter_sum(e, "row", 0)
    e = scatter_sum(e, "col", 1).astype(F32)
    my_rows = lambda y: lax.dynamic_slice_in_dim(y, r * tok, tok, 0)
    scale_mine = my_rows(scale_one)
    inner_mine = my_rows(inner_one.reshape(t, 1))
    grad_inputs = grad_middle_block + scale_mine * (e * gain_attn) - inputs.astype(F32) * (
        scale_mine**3 * inner_mine / D
    )

    grad_b_down = jnp.sum(g.astype(F32), axis=0)
    vectors = jnp.concatenate(
        [
            flip_dim(grad_gain_attn, "col", 0),
            flip_dim(grad_gain_mlp, "col", 0),
            flip_dim(grad_b_down, "col", 0),
            flip_dim(grad_b_up, "row", 0),
            grad_query_scale,
        ]
    )
    vectors = lax.psum(vectors, ("z", "core", "row", "col"))
    mine_col = lambda at: lax.dynamic_slice_in_dim(vectors, at * D + c * feat, feat, 0)
    units = b_up.shape[0]
    return (
        layer_out,
        grad_inputs,
        mine_col(0),
        sum_qkv,
        vectors[4 * D :],
        sum_out,
        mine_col(1),
        sum_up,
        lax.dynamic_slice_in_dim(vectors, 3 * D + r * units, units, 0),
        sum_down,
        mine_col(2),
    )


SMEM = pl.BlockSpec(memory_space=pltpu.SMEM)
ANY = pl.BlockSpec(memory_space=pl.ANY)


def call(kernel, name, args, specs, outs, scratch=(), limit=VMEM_LIMIT, out_specs=None):
    more = {} if out_specs is None else {"out_specs": out_specs}
    return pl.pallas_call(
        kernel,
        in_specs=specs,
        **more,
        out_shape=outs,
        scratch_shapes=list(scratch),
        compiler_params=pltpu.CompilerParams(vmem_limit_bytes=limit),
        cost_estimate=CHEAP,
        name=name,
    )(*args)


VM = pl.BlockSpec(memory_space=pltpu.VMEM)
HBM = pl.BlockSpec(memory_space=pltpu.HBM)


def shape(dims, kind):
    return jax.ShapeDtypeStruct(dims, kind)


def project_kernel(
    at, x00, x01, x10, x11, gain, factor, w_mine, w_a, w_b, qkv, raw, normed, scale_own, w_full
):
    r, k = at[0], at[2]
    tok, feat = x00.shape
    hr = w_mine.shape[1]
    half = hr // 2
    for s in range(3):
        w_full[pl.ds(s * hr, hr), 0:feat] = w_mine[s]
        w_full[pl.ds(pl.multiple_of(s * hr + k * half, 16), half), feat:] = w_a[s]
        w_full[pl.ds(pl.multiple_of(s * hr + (1 - k) * half, 16), half), feat:] = w_b[s]
    for i, (a_ref, b_ref) in enumerate(((x00, x01), (x10, x11))):
        a, b = a_ref[...].astype(F32), b_ref[...].astype(F32)
        total = jnp.sum(a * a, axis=1, keepdims=True) + jnp.sum(b * b, axis=1, keepdims=True)
        scale = lax.rsqrt(total / (2 * feat) + EPS)
        if i == 0:
            scale_own[...] = scale
        rows = pl.ds(pl.multiple_of((r ^ i) * tok, tok), tok)
        normed[rows, 0:feat] = (a * scale * gain[:, 0:feat]).astype(BF)
        normed[rows, feat:] = (b * scale * gain[:, feat:]).astype(BF)
        y = normed[rows, :]
        q = dot(w_full[0:hr, :], y, (1, 1))
        raw[:, rows] = q
        qkv[0, :, rows] = (q * factor[...]).astype(BF)
        qkv[1, :, rows] = dot(w_full[hr : 2 * hr, :], y, (1, 1)).astype(BF)
        qkv[2, :, rows] = dot(w_full[2 * hr : 3 * hr, :], y, (1, 1)).astype(BF)


def feed_kernel(
    at, gain, bias_up, bias_down, a, x_own, x_col, g_own, g_col,
    w_out, w_up, w_down, hx, hy, d0, d1, hx2, hy2, d02, d12,
    out_own, gm_own, post, ts, vectors, att, hidden_out, normed_out, g_out, pre_out, branch_out,
    w, x_ref, sems, more_sems,
):
    r, c, k = at[0], at[1], at[2]
    _, hr, share = a.shape
    feat = x_own.shape[1]
    half = feat // 2
    first = d0.shape[1]
    rows = pl.ds(pl.multiple_of(c * share, share), share)

    def start(pairs, sem):
        copies = [pltpu.make_async_copy(src, dst, sem.at[m]) for m, (src, dst) in enumerate(pairs)]
        for copy in copies:
            copy.start()
        return copies

    def place(s):
        return pl.ds(pl.multiple_of(((s // 2) ^ r) * 2 * hr + (s % 2) * hr, 16), hr)

    small = [(a.at[s], att.at[place(s), :]) for s in range(4)]
    small += [(x_own.at[rows, :], x_ref.at[:, 0:feat]), (x_col.at[rows, :], x_ref.at[:, feat:])]
    small += [(g_own.at[rows, :], g_out.at[:, 0:feat]), (g_col, g_out.at[:, feat:])]
    small = start(small, more_sems)
    copies = []
    for n, shard in enumerate((w_out, w_up, w_down)):
        rx, cx, ry, cy = (0, feat, feat, 0) if n == 1 else (feat, 0, 0, feat)
        mine = [(shard, w.at[n, 0:feat, 0:feat])]
        for core, (px, py, p0, p1) in ((k, (hx, hy, d0, d1)), (1 - k, (hx2, hy2, d02, d12))):
            down = core * half
            at_x = pl.ds(pl.multiple_of(rx + down, 16), half)
            at_y = pl.ds(pl.multiple_of(ry + down, 16), half)
            at_0 = pl.ds(pl.multiple_of(feat + down, 16), first)
            at_1 = pl.ds(pl.multiple_of(feat + down + first, 16), half - first)
            mine.append((px.at[n], w.at[n, at_x, cx : cx + feat]))
            mine.append((py.at[n], w.at[n, at_y, cy : cy + feat]))
            mine.append((p0.at[n], w.at[n, at_0, feat : 2 * feat]))
            mine.append((p1.at[n], w.at[n, at_1, feat : 2 * feat]))
        copies.append(start(mine, sems.at[n]))

    for copy in small + copies[0]:
        copy.wait()
    middle = x_ref[...].astype(F32) + dot(att[...], w[0], (0, 0))
    scale = lax.rsqrt(jnp.sum(middle * middle, axis=1, keepdims=True) / D + EPS)
    normed = (middle * scale * gain[...]).astype(BF)
    normed_out[...] = normed
    for copy in copies[1]:
        copy.wait()
    pre = dot(normed, w[1], (1, 0)) + bias_up[...]
    sig = jax.nn.sigmoid(pre)
    hidden = (pre * sig).astype(BF)
    hidden_out[...] = hidden
    for copy in copies[2]:
        copy.wait()
    result = (middle + dot(hidden, w[2], (1, 0)) + bias_down[...]).astype(BF)
    out_own[...] = result[:, :feat]
    post[0] = result[:, feat:]

    grad_pre_f = dot(g_out[...], w[2], (1, 1)) * sig * (1.0 + pre * (1.0 - sig))
    grad_pre = grad_pre_f.astype(BF)
    pre_out[...] = grad_pre
    grad_normed = dot(grad_pre, w[1], (1, 1))
    weighted = grad_normed * gain[...]
    inner = jnp.sum(weighted * middle, axis=1, keepdims=True)
    gf = g_out[...].astype(F32)
    grad_middle = gf + scale * weighted - middle * (scale * scale * scale * inner / D)
    gm_own[...] = grad_middle[:, :feat]
    post[1] = grad_middle[:, feat:].astype(BF)
    branch = grad_middle.astype(BF)
    branch_out[...] = branch
    for s in range(4):
        ts[s] = dot(w[0, place(s), :], branch, (1, 1)).astype(BF)
    vectors[...] = jnp.concatenate(
        [
            jnp.sum(grad_normed * (middle * scale), axis=0, keepdims=True),
            jnp.sum(gf, axis=0, keepdims=True),
            jnp.sum(grad_pre.astype(F32), axis=0, keepdims=True),
        ],
        axis=0,
    )


def feed_weights_kernel(at, att, hidden, normed, g, grad_pre, branch, *rest):
    *grads, stage, turned, sems = rest
    k = at[2]
    feat = g.shape[1] // 2
    half = feat // 2
    quarter = half // 2
    copies = []

    def weight_grad(n, left_ref, right):
        for core, begin in ((k, 0), (1 - k, 8)):
            up, low = (begin + 4, begin) if n == 1 else (begin, begin + 4)
            for b in range(2):
                part = pl.ds(pl.multiple_of(b * feat + core * half, 16), half)
                y = dot(left_ref[part, :], right, (1, 0)).astype(BF)
                for j in range(2):
                    cut = slice(j * feat, (j + 1) * feat)
                    for to, value in ((up + 2 * j + (1 - b), y[:quarter, cut]), (low + 2 * b + (1 - j), y[quarter:, cut])):
                        stage[to, n] = value
                        copy = pltpu.make_async_copy(stage.at[to, n], grads[to].at[n], sems.at[to, n])
                        copy.start()
                        copies.append(copy)

    turned[0] = hidden[...].astype(F32).T.astype(BF)
    weight_grad(2, turned.at[0], g[...])
    turned[1] = normed[...].astype(F32).T.astype(BF)
    weight_grad(1, turned.at[1], grad_pre[...])
    weight_grad(0, att, branch[...])
    for copy in copies:
        copy.wait()


def weight_back_kernel(at, grad, normed, keep, give):
    k = at[2]
    part = keep.shape[2]
    feat = keep.shape[3]
    for ref, core in ((give, 1 - k), (keep, k)):
        for s in range(3):
            rows = pl.ds(pl.multiple_of(core * part, 16), part)
            y = dot(grad[s, rows, :], normed[...], (1, 0)).astype(BF)
            ref[0, s] = y[:, :feat]
            ref[1, s] = y[:, feat:]


def project_back_kernel(
    at, grad, w_full, x00, x01, x10, x11, gain, es, gain_sum
):
    r, c = at[0], at[1]
    tok, feat = x00.shape
    sums = [jnp.zeros((1, feat), F32), jnp.zeros((1, feat), F32)]
    for i, xs in enumerate(((x00, x01), (x10, x11))):
        rows = pl.ds(pl.multiple_of((r ^ i) * tok, tok), tok)
        left = grad[:, rows]
        products, squares, inner = [], 0.0, 0.0
        for j in range(2):
            cut = slice(j * feat, (j + 1) * feat)
            e = dot(left, w_full[:, cut], (0, 0))
            x = xs[j][...].astype(F32)
            product = e * x
            inner = inner + jnp.sum(product * gain[:, cut], axis=1, keepdims=True)
            squares = squares + jnp.sum(x * x, axis=1, keepdims=True)
            es[2 * (r ^ i) + (c ^ j), 0:tok, :] = e.astype(BF)
            products.append(product)
        scale = lax.rsqrt(squares / (2 * feat) + EPS)
        for j in range(2):
            sums[j] += jnp.sum(products[j] * scale, axis=0, keepdims=True)
        line = jnp.broadcast_to(inner, (tok, 128)).T[0:1, :]
        high = line.astype(BF).astype(F32)
        extra = jnp.concatenate([high, line - high, jnp.zeros((14, tok), F32)], axis=0)
        extra = jnp.concatenate([extra, jnp.zeros((16, feat - tok), F32)], axis=1).astype(BF)
        for j in range(2):
            es[2 * (r ^ i) + (c ^ j), tok:, :] = extra
    gain_sum[:, 0:feat] = sums[0]
    gain_sum[:, feat:] = sums[1]


def finish_qkv_kernel(at, mine, theirs, mine2, theirs2, out, rows):
    c, k = at[1], at[2]
    half = mine.shape[1]
    for s in range(3):
        for ref, col, core in ((mine, c, k), (theirs, 1 - c, k), (mine2, c, 1 - k), (theirs2, 1 - c, 1 - k)):
            rows[pl.ds(pl.multiple_of((2 * col + core) * half, 16), half), :] = ref[s].astype(F32)
        out[s] = rows[...].T


def finish_feed_kernel(at, a, b, a2, b2, *outs):
    k = at[2]
    quarter = a.shape[1]
    for n, out in enumerate(outs):
        upper, lower = ((b, b2), (a, a2)) if n == 1 else ((a, a2), (b, b2))
        for i, core in ((0, k), (1, 1 - k)):
            for j, refs in enumerate((upper, lower)):
                to = pl.multiple_of((2 * core + j) * quarter, 16)
                out[pl.ds(to, quarter), :] = refs[i][n].astype(F32)


together = lax.optimization_barrier


def after(x, *earlier):
    return lax.optimization_barrier((x, *earlier))[0]


def add(*parts):
    total = parts[0].astype(F32)
    for part in parts[1:]:
        total = total + part.astype(F32)
    return total.astype(BF)


def all_four(x):
    return lax.all_to_all(x, ("row", "col"), 0, 0, tiled=True)


def z_swap(x, step):
    n = size("z")
    return lax.ppermute(x, "z", [(i, i ^ step) for i in range(n)])


def z_first():
    z = lax.axis_index("z")
    return (z == 0) | (z == 3)


def body_four(
    inputs, gain_attn, w_qkv, query_scale, w_out, gain_mlp, w_up, b_up, w_down, b_down, series_ids, pad_mask, cotangent
):
    tok, feat = inputs.shape
    share = tok // 2
    t = series_ids.shape[0]
    hr = w_qkv.shape[2] // 2
    heads = hr // HEAD_DIM
    half = feat // 2
    r, c, k = lax.axis_index("row"), lax.axis_index("col"), lax.axis_index("core")
    at = jnp.stack([r, c, k, 2 * r + c]).astype(jnp.int32)
    mine_rows = lambda y, part: lax.dynamic_slice_in_dim(y, part * share, share, 0)

    few = heads // 2
    quarter = half // 2
    first_rows = (half * 7 // 20) // 16 * 16
    x01 = swap(inputs, "col")
    x10 = swap(inputs, "row")
    small = swap(jnp.concatenate([gain_attn, gain_mlp, b_down.astype(F32)]), "col")
    up_other = swap(b_up.astype(F32), "row")
    w_turned = jnp.transpose(w_qkv, (1, 2, 0)).reshape(3, 2, hr, feat)
    w_mine = lax.dynamic_index_in_dim(w_turned, c, 1, keepdims=False)
    w_give = lax.dynamic_index_in_dim(w_turned, 1 - c, 1, keepdims=False)
    w_half = core_half(w_give, 1)
    w_a = swap(w_half, "col")
    part = jnp.stack([core_half(w_out, 0), core_half(w_up, 0), core_half(w_down, 0)])
    g_give = mine_rows(cotangent, 1 - c)
    x01, x10, small, up_other, part, g_give, w_mine = lax.optimization_barrier(
        (x01, x10, small, up_other, part, g_give, w_mine)
    )
    x11 = swap(after(x01, w_half), "row")
    w_b = swap(w_a, "core")
    gain_one = jnp.concatenate([gain_attn, small[:feat]]).reshape(1, D)
    gain_two = jnp.concatenate([gain_mlp, small[feat : 2 * feat]]).reshape(1, D)
    bias_down = jnp.concatenate([b_down.astype(F32), small[2 * feat :]]).reshape(1, D)
    bias_up = jnp.concatenate([b_up.astype(F32), up_other]).reshape(1, D)
    factor = QUERY_CONST / math.sqrt(HEAD_DIM) * jax.nn.softplus(query_scale)
    factor_col = factor.reshape(HEAD_DIM, 1)

    part = after(part, x11, w_a)
    hx, hy = swap(part, "row"), swap(part, "col")
    hx2, hy2 = swap(hx, "core"), swap(hy, "core")
    qkv, raw, normed_one, scale_own, w_full = call(
        project_kernel,
        "project",
        (at, inputs, x01, x10, x11, gain_one, jnp.tile(factor_col, (heads, 1)), w_mine, w_a, w_b),
        [SMEM] + [VM] * 9,
        [
            shape((3, hr, t), BF),
            shape((hr, t), F32),
            shape((t, D), BF),
            shape((tok, 1), F32),
            shape((3 * hr, D), BF),
        ],
        limit=VMEM_LARGE,
    )
    qkv = qkv.reshape(3, heads, HEAD_DIM, t)
    masks = mask_args(series_ids, pad_mask)
    attended, lse, a = attention_forward(at, qkv, masks, pieces=1)
    a = all_four(a.reshape(4, hr, share))
    hx_on, hy_on, g_give = lax.optimization_barrier((hx, hy, g_give, lse))[:3]
    d0 = swap(hx_on[:, :first_rows], "col")
    d1 = swap(hy_on[:, first_rows:], "row")
    g_col = swap(g_give, "col")
    d0, d1, g_col, a = together((d0, d1, g_col, a))
    d02, d12 = swap(d0, "core"), swap(d1, "core")
    out_own, gm_own, post, ts, vectors, *factors = call(
        feed_kernel,
        "feed_forward",
        (at, gain_two, bias_up, bias_down, a, inputs, x01, cotangent, g_col)
        + (w_out, w_up, w_down, hx, hy, d0, d1, hx2, hy2, d02, d12),
        [SMEM] + [VM] * 3 + [HBM] * 16,
        [
            shape((share, feat), BF),
            shape((share, feat), F32),
            shape((2, share, feat), BF),
            shape((4, hr, share), BF),
            shape((3, D), F32),
            shape((D, share), BF),
        ]
        + [shape((share, D), BF)] * 5,
        scratch=[
            pltpu.VMEM((3, D, D), BF),
            pltpu.VMEM((share, D), BF),
            pltpu.SemaphoreType.DMA((3, 9)),
            pltpu.SemaphoreType.DMA((8,)),
        ],
        limit=VMEM_LARGE,
    )
    grads = call(
        feed_weights_kernel,
        "feed_weights",
        (at, *factors),
        [SMEM] + [VM] * 6,
        [shape((3, quarter, feat), BF)] * 16,
        scratch=[
            pltpu.VMEM((16, 3, quarter, feat), BF),
            pltpu.VMEM((2, D, share), BF),
            pltpu.SemaphoreType.DMA((16, 3)),
        ],
        out_specs=[HBM] * 16,
        limit=VMEM_LARGE,
    )
    ts = all_four(ts)
    others = grads[8:]
    over = lambda n: swap(others[n], "core")
    grads, osx0, osx1, osy0, osy1 = grads[:8], over(0), over(2), over(4), over(6)
    sx0, kx0, sx1, kx1, sy0, ky0, sy1, ky1 = grads
    sx1, sy1 = add(sx1, osx1), add(sy1, osy1)
    ox0, ox1, oy0, oy1 = over(1), over(3), over(5), over(7)
    ts, sx1, sy1 = together((ts, sx1, sy1))
    rx1, ry1 = swap(sx1, "row"), swap(sy1, "col")
    ts = ts.reshape(4, heads, HEAD_DIM, share)
    raw = raw.reshape(heads, HEAD_DIM, t)

    grad_proj, gscale = attention_backward(at, qkv, raw, factor_col, attended, ts, lse, masks)
    grad_proj = grad_proj.reshape(3, hr, t)
    kept, sent = call(
        weight_back_kernel,
        "weight_back",
        (at, grad_proj, normed_one),
        [SMEM] + [VM] * 2,
        [shape((2, 3, hr // 2, feat), BF)] * 2,
    )
    sent, rx1, ry1, osx0, osy0, ox0, ox1, oy0, oy1 = together((sent, rx1, ry1, osx0, osy0, ox0, ox1, oy0, oy1))
    got = swap(sent, "core")
    px1, py1 = add(kx1, ox1, rx1), add(ky1, oy1, ry1)
    qx, qy = swap(px1, "col"), swap(py1, "row")
    sx0, sy0 = add(sx0, osx0), add(sy0, osy0)
    rx0, ry0 = swap(sx0, "row"), swap(sy0, "col")
    w_pair = add(kept, got)
    first = z_first()
    got_w = z_swap(jnp.where(first, w_pair[1], w_pair[0]), 1)
    slope = QUERY_CONST / math.sqrt(HEAD_DIM) * jax.nn.sigmoid(query_scale)
    grad_query_scale = jnp.sum(gscale, axis=(0, 2)) * slope
    es, gain_sum = call(
        project_back_kernel,
        "project_back",
        (at, after(grad_proj, w_pair, px1, py1).reshape(3 * hr, t), w_full, inputs, x01, x10, x11, gain_one),
        [SMEM] + [VM] * 7,
        [
            shape((4, tok + 16, feat), BF),
            shape((1, D), F32),
        ],
    )
    total = jnp.concatenate([gain_sum, vectors]).reshape(4, 2, feat)
    turn = jnp.stack([c, c, c, r]).reshape(4, 1, 1) == 1
    total = jnp.where(turn, total[:, ::-1], total).reshape(8, feat)
    total = jnp.concatenate([total, jnp.pad(grad_query_scale, (0, feat - HEAD_DIM)).reshape(1, feat)])
    qx, qy, rx0, ry0, got_w, w_pair, es, total = together((qx, qy, rx0, ry0, got_w, w_pair, es, total))
    total = total + swap(total, "core")

    mine_w = add(jnp.where(first, w_pair[0], w_pair[1]), got_w)
    met_w = z_swap(mine_w, 3)
    fx, fy = add(kx0, ox0, rx0, qx), add(ky0, oy0, ry0, qy)
    got_c = z_swap(jnp.where(first, fy, fx), 1)
    total = total + swap(total, "row")
    total = total + swap(total, "col")
    es = all_four(after(es, fx, fy, mine_w, total))
    met_w, mine_w, got_c, fx, fy, es, post, total = together((met_w, mine_w, got_c, fx, fy, es, post, total))

    mine_w = add(mine_w, met_w)
    other_w = z_swap(mine_w, 1)
    w_own, w_theirs = jnp.where(first, mine_w, other_w), jnp.where(first, other_w, mine_w)
    mine_c = add(jnp.where(first, fx, fy), got_c)
    met_c = z_swap(mine_c, 3)
    post = swap(post, "col")
    w_theirs = swap(w_theirs, "col")
    total = total + z_swap(total, 1)
    total = total + z_swap(total, 3)
    met_c, mine_c, w_own, w_theirs, post, total = together((met_c, mine_c, w_own, w_theirs, post, total))
    mine_c = add(mine_c, met_c)
    other_c = z_swap(mine_c, 1)
    w_args = (at, w_own, w_theirs, swap(w_own, "core"), swap(w_theirs, "core"))
    sum_qkv = call(
        finish_qkv_kernel,
        "finish_qkv",
        w_args,
        [SMEM] + [VM] * 4,
        shape((3, feat, 2 * hr), F32),
        scratch=[pltpu.VMEM((2 * hr, feat), F32)],
    )
    sum_qkv = jnp.transpose(sum_qkv, (1, 0, 2))

    e = jnp.sum(es[:, :tok].astype(F32), axis=0)
    inner = jnp.sum(es[:, tok : tok + 2, :tok].astype(F32), axis=(0, 1)).reshape(tok, 1)
    grad_middle = jnp.concatenate(flip([gm_own, post[1].astype(F32)], "col"), axis=0)
    grad_inputs = grad_middle + scale_own * (e * gain_attn) - inputs.astype(F32) * (scale_own**3 * inner / D)
    layer_out = jnp.concatenate(flip([out_own, post[0]], "col"), axis=0)

    pick = lambda n, place: lax.dynamic_index_in_dim(total, 2 * n + place, 0, keepdims=False)
    mine_c = after(mine_c, sum_qkv, grad_inputs, layer_out, total)
    fx, fy = jnp.where(first, mine_c, other_c), jnp.where(first, other_c, mine_c)
    sum_out, sum_up, sum_down = call(
        finish_feed_kernel,
        "finish_feed",
        (at, fx, fy, swap(fx, "core"), swap(fy, "core")),
        [SMEM] + [VM] * 4,
        [shape((feat, feat), F32)] * 3,
    )

    return (
        layer_out,
        grad_inputs,
        pick(0, c),
        sum_qkv,
        total[8, :HEAD_DIM],
        sum_out,
        pick(1, c),
        sum_up,
        pick(3, r),
        sum_down,
        pick(2, c),
    )


def solution(mesh):
    dp, rows, cols = mesh.shape["dp"], mesh.shape["row"], mesh.shape["col"]
    split = Mesh(mesh.devices.reshape(dp // 2, 2, rows, cols), ("z", "core", "row", "col"))
    tokens = P(("z", "core", "row"), "col")
    in_specs = (
        tokens,
        P("col"),
        P("col", None, "row"),
        P(),
        P("row", "col"),
        P("col"),
        P("col", "row"),
        P("row"),
        P("row", "col"),
        P("col"),
        P(("z", "core")),
        P(("z", "core")),
        tokens,
    )
    out_specs = (
        tokens,
        tokens,
        P("col"),
        P("col", None, "row"),
        P(),
        P("row", "col"),
        P("col"),
        P("col", "row"),
        P("row"),
        P("row", "col"),
        P("col"),
    )
    body = body_four if (dp, rows, cols) == (8, 2, 2) else body_any
    return jax.shard_map(body, mesh=split, in_specs=in_specs, out_specs=out_specs, check_vma=False)
```

```python
import functools
import math

import jax
import jax.numpy as jnp
from jax import lax
from jax.experimental import pallas as pl
from jax.experimental.pallas import tpu as pltpu
from jax.sharding import Mesh
from jax.sharding import PartitionSpec as P

D = 1280
HEAD_DIM = 80
EPS = 1e-06
QUERY_CONST = 1.442695041
MASKED = -1e30
BF = jnp.bfloat16
F32 = jnp.float32
VMEM_LIMIT = 60 * 1024 * 1024
CHUNK = 1024
VMEM_LARGE = 60 * 1024 * 1024
CHEAP = pl.CostEstimate(flops=1, bytes_accessed=1, transcendentals=0)


def size(axis):
    return lax.axis_size(axis)


def swap(x, axis):
    return lax.ppermute(x, axis, [(0, 1), (1, 0)])


def flip(blocks, axis):
    if size(axis) != 2:
        return list(blocks)
    first = lax.axis_index(axis) == 0
    a, b = blocks
    return [jnp.where(first, a, b), jnp.where(first, b, a)]


def flip_dim(x, axis, dim):
    if size(axis) != 2:
        return x
    return jnp.concatenate(flip(jnp.split(x, 2, axis=dim), axis), axis=dim)


def gather(x, axis):
    if size(axis) == 2:
        return [x, swap(x, axis)]
    whole = lax.all_gather(x, axis, axis=0, tiled=False)
    return [whole[i] for i in range(size(axis))]


def gather_grid(x):
    if size("row") != 2:
        return [gather(b, "col") for b in gather(x, "row")]
    along_row, along_col = swap(x, "row"), swap(x, "col")
    half = x.shape[0] // 2
    across = jnp.concatenate(
        [swap(along_row[:half], "col"), swap(along_col[half:], "row")], axis=0
    )
    return [[x, along_col], [along_row, across]]


def scatter_sum(x, axis, dim):
    if size(axis) != 2:
        return lax.psum_scatter(x, axis, scatter_dimension=dim, tiled=True)
    mine, theirs = jnp.split(x, 2, axis=dim)
    return (mine.astype(F32) + swap(theirs, axis).astype(F32)).astype(x.dtype)


def exchange(x, axis, split, join):
    if size(axis) != 2:
        return lax.all_to_all(x, axis, split, join, tiled=True)
    mine, theirs = jnp.split(x, 2, axis=split)
    return jnp.concatenate([mine, swap(theirs, axis)], axis=join)


def core_half(x, dim):
    return lax.dynamic_slice_in_dim(
        x, lax.axis_index("core") * (x.shape[dim] // 2), x.shape[dim] // 2, dim
    )


def weight_gather(w, row_dim):
    part = core_half(w, 0)
    blocks = gather_grid(part)
    if row_dim == 1:
        blocks = [list(b) for b in zip(*blocks)]
    mine = jnp.stack([jnp.concatenate(b, axis=1) for b in blocks])
    other = swap(mine, "core")
    first = lax.axis_index("core") == 0
    both = jnp.stack([jnp.where(first, mine, other), jnp.where(first, other, mine)], axis=1)
    return both.reshape(-1, both.shape[-1])


def weight_sum(g, row_dim):
    dim_axis = ("row", "col") if row_dim == 0 else ("col", "row")
    n0 = size(dim_axis[0])
    g = g.reshape(n0, 2, g.shape[0] // n0 // 2, g.shape[1])
    core = lax.axis_index("core")
    keep = lax.dynamic_index_in_dim(g, core, 1, keepdims=False)
    give = lax.dynamic_index_in_dim(g, 1 - core, 1, keepdims=False).astype(BF)
    part = (keep + swap(give, "core").astype(F32)).astype(BF)
    part = scatter_sum(part, dim_axis[0], 0)
    part = scatter_sum(part[0], dim_axis[1], 1)
    return z_sum(part)


def z_sum(part):
    total = lax.psum(part, "z")
    other = swap(total, "core")
    return flip_core(total, other)


def flip_core(total, other):
    first = lax.axis_index("core") == 0
    return jnp.concatenate(
        [jnp.where(first, total, other), jnp.where(first, other, total)], axis=-2
    ).astype(F32)


def dot(a, b, contract):
    return lax.dot_general(a, b, ((contract[0:1], contract[1:2]), ((), ())), preferred_element_type=F32)


def bias_block(series_row, series_col, key_pos, q0, k0, qb, kb, diagonal):
    q_pos = q0 + lax.broadcasted_iota(jnp.int32, (1, qb), 1)
    allowed = (series_col == series_row) & (key_pos <= q_pos)
    if diagonal:
        k_pos = k0 + lax.broadcasted_iota(jnp.int32, (kb, 1), 0)
        allowed = allowed | (k_pos == q_pos)
    return jnp.where(allowed, 0.0, MASKED)


def forward_kernel(block, at, qkv_ref, srow_ref, scol_ref, kpos_ref, out_ref, lse_ref, *rest):
    *pieces, bias_ref, krow_ref, s_ref = rest
    t = qkv_ref.shape[3]
    n = t // block
    krow_ref[...] = qkv_ref[1, 0].astype(F32).T.astype(BF)

    def bias_slot(j, i):
        return j * (j + 1) // 2 + i

    @pl.when(pl.program_id(0) == 0)
    def _():
        for j in range(n):
            for i in range(j + 1):
                keys = pl.ds(i * block, block)
                bias_ref[bias_slot(j, i)] = bias_block(
                    srow_ref[:, j * block : (j + 1) * block],
                    scol_ref[keys, :],
                    kpos_ref[keys, :],
                    j * block,
                    i * block,
                    block,
                    block,
                    i == j,
                )

    for j in range(n):
        cols = slice(j * block, (j + 1) * block)
        q = qkv_ref[0, 0, :, cols]
        top = None
        for i in range(j + 1):
            s = dot(krow_ref[i * block : (i + 1) * block, :], q, (1, 0)) + bias_ref[bias_slot(j, i)]
            s_ref[i * block : (i + 1) * block, :] = s
            here = jnp.max(s, axis=0, keepdims=True)
            top = here if top is None else jnp.maximum(top, here)
        total = jnp.zeros((1, block), F32)
        acc = jnp.zeros((HEAD_DIM, block), F32)
        for i in range(j + 1):
            p = jnp.exp(s_ref[i * block : (i + 1) * block, :] - top)
            total += jnp.sum(p, axis=0, keepdims=True)
            acc += dot(qkv_ref[2, 0, :, i * block : (i + 1) * block], p.astype(BF), (1, 0))
        found = (acc / total).astype(BF)
        out_ref[0, :, cols] = found
        if pieces:
            pieces[0][j, 0] = found
        lse_ref[0, :, cols] = top + jnp.log(total)


def backward_kernel(
    block, at, qkv_ref, raw_ref, factor_ref, out_ref, lse_ref, srow_ref, scol_ref, kpos_ref, *rest
):
    piece, grad_ref, gscale_ref, bias_ref, krow_ref, vrow_ref, gk_ref, gv_ref, gout_ref = rest
    wide = piece.shape[3]
    for j in range(piece.shape[0]):
        gout_ref[:, j * wide : (j + 1) * wide] = piece[j, 0]
    t = qkv_ref.shape[3]
    n = t // block
    krow_ref[...] = qkv_ref[1, 0].astype(F32).T.astype(BF)
    vrow_ref[...] = qkv_ref[2, 0].astype(F32).T.astype(BF)

    def bias_slot(j, i):
        return j * (j + 1) // 2 + i

    @pl.when(pl.program_id(0) == 0)
    def _():
        for j in range(n):
            for i in range(j + 1):
                keys = pl.ds(i * block, block)
                bias_ref[bias_slot(j, i)] = bias_block(
                    srow_ref[:, j * block : (j + 1) * block],
                    scol_ref[keys, :],
                    kpos_ref[keys, :],
                    j * block,
                    i * block,
                    block,
                    block,
                    i == j,
                )

    gscale = jnp.zeros((HEAD_DIM, 1), F32)
    for j in range(n):
        cols = slice(j * block, (j + 1) * block)
        q = qkv_ref[0, 0, :, cols]
        go = gout_ref[:, cols]
        lse = lse_ref[0, :, cols]
        delta = jnp.sum(go.astype(F32) * out_ref[0, :, cols].astype(F32), axis=0, keepdims=True)
        gq = jnp.zeros((HEAD_DIM, block), F32)
        step = max(1, CHUNK // block)
        for i in range(0, j + 1, step):
            many = min(step, j + 1 - i)
            keys = slice(i * block, (i + many) * block)
            slot = bias_slot(j, i)
            bias = bias_ref[slot : slot + many].reshape(many * block, block)
            p = jnp.exp(dot(krow_ref[keys, :], q, (1, 0)) + bias - lse)
            gp = dot(vrow_ref[keys, :], go, (1, 0))
            gs = (p * (gp - delta)).astype(BF)
            gq += dot(qkv_ref[1, 0, :, keys], gs, (1, 0))
            gk = dot(q, gs, (1, 1))
            gv = dot(go, p.astype(BF), (1, 1))
            before, last = slice(i * block, min(i + many, j) * block), slice(j * block, (j + 1) * block)
            old = (min(i + many, j) - i) * block
            if old:
                gk_ref[:, before] += gk[:, :old]
                gv_ref[:, before] += gv[:, :old]
            if i + many == j + 1:
                gk_ref[:, last] = gk[:, old:]
                gv_ref[:, last] = gv[:, old:]
        gscale += jnp.sum(gq * raw_ref[0, :, cols], axis=1, keepdims=True)
        grad_ref[0, 0, :, cols] = (gq * factor_ref[...]).astype(BF)
    grad_ref[1, 0] = gk_ref[...].astype(BF)
    grad_ref[2, 0] = gv_ref[...].astype(BF)
    gscale_ref[0] = gscale


def mask_args(series, padding):
    t = series.shape[0]
    pos = jnp.arange(t, dtype=jnp.int32)
    return series.reshape(1, t), series.reshape(t, 1), jnp.where(padding == 0, pos, t).reshape(t, 1)


def attention_forward(at, qkv, masks, pieces=0):
    _, heads, hd, t = qkv.shape
    block = min(256, t) if t <= 2048 else 512
    n = t // block
    whole = lambda shape: pl.BlockSpec(shape, lambda h: (0,) * len(shape))
    return pl.pallas_call(
        functools.partial(forward_kernel, block),
        grid=(heads,),
        in_specs=[
            pl.BlockSpec(memory_space=pltpu.SMEM),
            pl.BlockSpec((3, 1, hd, t), lambda h: (0, h, 0, 0)),
            whole((1, t)),
            whole((t, 1)),
            whole((t, 1)),
        ],
        out_specs=[
            pl.BlockSpec((1, hd, t), lambda h: (h, 0, 0)),
            pl.BlockSpec((1, 1, t), lambda h: (h, 0, 0)),
        ]
        + [pl.BlockSpec((n, 1, hd, block), lambda h: (0, h, 0, 0))] * pieces,
        out_shape=[
            jax.ShapeDtypeStruct((heads, hd, t), BF),
            jax.ShapeDtypeStruct((heads, 1, t), F32),
        ]
        + [jax.ShapeDtypeStruct((n, heads, hd, block), BF)] * pieces,
        scratch_shapes=[
            pltpu.VMEM((n * (n + 1) // 2, block, block), F32),
            pltpu.VMEM((t, hd), BF),
            pltpu.VMEM((t, block), F32),
        ],
        compiler_params=pltpu.CompilerParams(vmem_limit_bytes=VMEM_LARGE),
        cost_estimate=CHEAP,
        name="attention_forward",
    )(at, qkv, *masks)


def attention_backward(at, qkv, raw, factor, out, piece, lse, masks):
    _, heads, hd, t = qkv.shape
    block = min(256, t) if t <= 2048 else 512
    n = t // block
    whole = lambda shape: pl.BlockSpec(shape, lambda h: (0,) * len(shape))
    head = lambda wide=t: pl.BlockSpec((1, hd, wide), lambda h: (h, 0, 0))
    return pl.pallas_call(
        functools.partial(backward_kernel, block),
        grid=(heads,),
        in_specs=[
            pl.BlockSpec(memory_space=pltpu.SMEM),
            pl.BlockSpec((3, 1, hd, t), lambda h: (0, h, 0, 0)),
            head(),
            whole((hd, 1)),
            head(),
            pl.BlockSpec((1, 1, t), lambda h: (h, 0, 0)),
            whole((1, t)),
            whole((t, 1)),
            whole((t, 1)),
        ]
        + [pl.BlockSpec((piece.shape[0], 1, hd, piece.shape[3]), lambda h: (0, h, 0, 0))],
        out_specs=[
            pl.BlockSpec((3, 1, hd, t), lambda h: (0, h, 0, 0)),
            pl.BlockSpec((1, hd, 1), lambda h: (h, 0, 0)),
        ],
        out_shape=[
            jax.ShapeDtypeStruct((3, heads, hd, t), BF),
            jax.ShapeDtypeStruct((heads, hd, 1), F32),
        ],
        scratch_shapes=[
            pltpu.VMEM((n * (n + 1) // 2, block, block), F32),
            pltpu.VMEM((t, hd), BF),
            pltpu.VMEM((t, hd), BF),
            pltpu.VMEM((hd, t), F32),
            pltpu.VMEM((hd, t), F32),
            pltpu.VMEM((hd, t), BF),
        ],
        compiler_params=pltpu.CompilerParams(vmem_limit_bytes=VMEM_LARGE),
        cost_estimate=CHEAP,
        name="attention_backward",
    )(at, qkv, raw, factor, out, lse, *masks, piece)


def norm_scale(x):
    return lax.rsqrt(jnp.mean(x * x, axis=1, keepdims=True) + EPS)


def body_any(
    inputs, gain_attn, w_qkv, query_scale, w_out, gain_mlp, w_up, b_up, w_down, b_down, series_ids, pad_mask, cotangent
):
    rows, cols = size("row"), size("col")
    tok = inputs.shape[0]
    feat = inputs.shape[1]
    share = tok // cols
    t = series_ids.shape[0]
    head_rows = w_qkv.shape[2] // cols
    heads = head_rows // HEAD_DIM
    r, c = lax.axis_index("row"), lax.axis_index("col")

    blocks = gather_grid(inputs)
    strips = [jnp.concatenate(b, axis=1) for b in blocks]
    x_own = strips[0] if rows == 2 else lax.dynamic_index_in_dim(jnp.stack(strips), r, 0, keepdims=False)
    x_all = jnp.concatenate(flip(strips, "row"), axis=0)
    gain_one = jnp.concatenate(gather(gain_attn, "col"))
    gain_two = jnp.concatenate(gather(gain_mlp, "col"))
    bias_up = jnp.concatenate(gather(b_up, "row")).astype(F32)
    bias_down = jnp.concatenate(gather(b_down, "col")).astype(F32)

    w3 = jnp.transpose(w_qkv, (1, 0, 2)).reshape(3, feat, cols, head_rows)
    w_mine = lax.dynamic_index_in_dim(w3, c, 2, keepdims=False)
    w_give = lax.dynamic_index_in_dim(w3, 1 - c, 2, keepdims=False)
    w_half = swap(core_half(w_give, 1), "col")
    w_other = swap(w_half, "core")
    first = lax.axis_index("core") == 0
    w_full = jnp.concatenate(
        [w_mine, jnp.where(first, w_half, w_other), jnp.where(first, w_other, w_half)], axis=1
    )

    xf = x_all.astype(F32)
    scale_one = norm_scale(xf)
    normed_one = (xf * scale_one * gain_one).astype(BF)
    projected = jnp.einsum("td,sdh->sht", normed_one, w_full, preferred_element_type=F32)
    projected = projected.reshape(3, heads, HEAD_DIM, t)
    factor = QUERY_CONST / math.sqrt(HEAD_DIM) * jax.nn.softplus(query_scale)
    raw_q = projected[0]
    qkv = jnp.stack([raw_q * factor[None, :, None], projected[1], projected[2]]).astype(BF)
    masks = mask_args(series_ids, pad_mask)
    at = jnp.zeros((4,), jnp.int32)
    attended, lse = attention_forward(at, qkv, masks)

    def to_tokens(y):
        y = flip_dim(y.reshape(head_rows, rows, cols, share), "row", 1)
        y = flip_dim(y, "col", 2)
        y = exchange(y.reshape(1, head_rows, rows, cols, share), "row", 2, 0)
        y = exchange(y.reshape(rows, 1, head_rows, cols, share), "col", 3, 1)
        y = flip_dim(y.reshape(rows, cols, head_rows, share), "col", 1)
        return y.reshape(rows * cols * head_rows, share)

    def to_heads(y):
        y = flip_dim(y.reshape(rows, cols, head_rows, share), "col", 1)
        y = exchange(y.reshape(rows, cols, head_rows, 1, share), "col", 1, 3)
        y = exchange(y.reshape(rows, head_rows, 1, cols, share), "row", 0, 2)
        y = flip_dim(y.reshape(head_rows, rows, cols, share), "col", 2)
        return flip_dim(y, "row", 1).reshape(head_rows, t)

    w_out_all = weight_gather(w_out, 0)
    w_up_all = weight_gather(w_up, 1)
    w_down_all = weight_gather(w_down, 0)

    def my_share(y):
        return lax.dynamic_slice_in_dim(y, c * share, share, 0)

    att = to_tokens(attended.reshape(head_rows, t))
    x_mine = my_share(x_own).astype(F32)
    middle = x_mine + dot(att, w_out_all, (0, 0))
    scale_two = norm_scale(middle)
    normed_two = (middle * scale_two * gain_two).astype(BF)
    pre_act = dot(normed_two, w_up_all, (1, 0)) + bias_up
    sig = jax.nn.sigmoid(pre_act)
    hidden = (pre_act * sig).astype(BF)
    result = (middle + dot(hidden, w_down_all, (1, 0)) + bias_down).astype(BF)

    def to_block(y):
        mine, theirs = jnp.split(y, 2, axis=1)
        return jnp.concatenate(flip([mine, swap(theirs, "col")], "col"), axis=0)

    layer_out = to_block(result)

    g_give = lax.dynamic_slice_in_dim(cotangent, (1 - c) * share, share, 0)
    g = jnp.concatenate([my_share(cotangent), swap(g_give, "col")], axis=1)
    grad_w_down = dot(hidden, g, (0, 0))
    grad_hidden = dot(g, w_down_all, (1, 1))
    grad_pre_f = grad_hidden * sig * (1.0 + pre_act * (1.0 - sig))
    grad_pre = grad_pre_f.astype(BF)
    grad_b_up = jnp.sum(grad_pre.astype(F32), axis=0)
    grad_w_up = dot(normed_two, grad_pre, (0, 0))
    grad_normed_two = dot(grad_pre, w_up_all, (1, 1))
    weighted = grad_normed_two * gain_two
    inner = jnp.sum(weighted * middle, axis=1, keepdims=True)
    grad_middle = g.astype(F32) + scale_two * weighted - middle * (scale_two**3 * inner / D)
    grad_gain_mlp = jnp.sum(grad_normed_two * middle * scale_two, axis=0)
    grad_branch = grad_middle.astype(BF)
    grad_w_out = dot(att, grad_branch, (1, 0))
    grad_att = dot(w_out_all, grad_branch, (1, 1)).astype(BF)
    grad_attended = to_heads(grad_att).reshape(heads, HEAD_DIM, t)
    grad_middle_block = to_block(grad_middle)

    sum_down = weight_sum(grad_w_down, 0)
    sum_up = weight_sum(grad_w_up, 1)
    sum_out = weight_sum(grad_w_out, 0)

    grad_proj, gscale = attention_backward(
        at, qkv, raw_q, factor.reshape(HEAD_DIM, 1), attended, grad_attended[None], lse, masks
    )
    slope = QUERY_CONST / math.sqrt(HEAD_DIM) * jax.nn.sigmoid(query_scale)
    grad_query_scale = jnp.sum(gscale, axis=(0, 2)) * slope
    grad_proj = grad_proj.reshape(3, head_rows, t)
    grad_normed_one = jnp.einsum("sht,sdh->td", grad_proj, w_full, preferred_element_type=F32)
    weighted_one = grad_normed_one * gain_one
    inner_one = jnp.sum(weighted_one * xf, axis=1)
    grad_gain_attn = jnp.sum(grad_normed_one * xf * scale_one, axis=0)
    inner_one = lax.psum(inner_one, ("row", "col"))
    grad_w = jnp.einsum("td,sht->sdh", normed_one, grad_proj, preferred_element_type=F32)
    grad_w = grad_w.reshape(3, cols, 2, feat // 2, head_rows)
    core = lax.axis_index("core")
    keep = lax.dynamic_index_in_dim(grad_w, core, 2, keepdims=False)
    give = lax.dynamic_index_in_dim(grad_w, 1 - core, 2, keepdims=False).astype(BF)
    part = (keep + swap(give, "core").astype(F32)).astype(BF)
    part = jnp.concatenate(flip([part[:, 0], swap(part[:, 1], "col")], "col"), axis=2)
    sum_qkv = jnp.transpose(z_sum(part), (1, 0, 2))

    e = jnp.concatenate(flip(jnp.split(grad_normed_one.astype(BF), 2, axis=0), "row"), axis=0) if rows == 2 else (
        grad_normed_one.astype(BF)
    )
    e = scatter_sum(e, "row", 0)
    e = scatter_sum(e, "col", 1).astype(F32)
    my_rows = lambda y: lax.dynamic_slice_in_dim(y, r * tok, tok, 0)
    scale_mine = my_rows(scale_one)
    inner_mine = my_rows(inner_one.reshape(t, 1))
    grad_inputs = grad_middle_block + scale_mine * (e * gain_attn) - inputs.astype(F32) * (
        scale_mine**3 * inner_mine / D
    )

    grad_b_down = jnp.sum(g.astype(F32), axis=0)
    vectors = jnp.concatenate(
        [
            flip_dim(grad_gain_attn, "col", 0),
            flip_dim(grad_gain_mlp, "col", 0),
            flip_dim(grad_b_down, "col", 0),
            flip_dim(grad_b_up, "row", 0),
            grad_query_scale,
        ]
    )
    vectors = lax.psum(vectors, ("z", "core", "row", "col"))
    mine_col = lambda at: lax.dynamic_slice_in_dim(vectors, at * D + c * feat, feat, 0)
    units = b_up.shape[0]
    return (
        layer_out,
        grad_inputs,
        mine_col(0),
        sum_qkv,
        vectors[4 * D :],
        sum_out,
        mine_col(1),
        sum_up,
        lax.dynamic_slice_in_dim(vectors, 3 * D + r * units, units, 0),
        sum_down,
        mine_col(2),
    )


SMEM = pl.BlockSpec(memory_space=pltpu.SMEM)
ANY = pl.BlockSpec(memory_space=pl.ANY)


def call(kernel, name, args, specs, outs, scratch=(), limit=VMEM_LIMIT, out_specs=None):
    more = {} if out_specs is None else {"out_specs": out_specs}
    return pl.pallas_call(
        kernel,
        in_specs=specs,
        **more,
        out_shape=outs,
        scratch_shapes=list(scratch),
        compiler_params=pltpu.CompilerParams(vmem_limit_bytes=limit),
        cost_estimate=CHEAP,
        name=name,
    )(*args)


VM = pl.BlockSpec(memory_space=pltpu.VMEM)
HBM = pl.BlockSpec(memory_space=pltpu.HBM)


def shape(dims, kind):
    return jax.ShapeDtypeStruct(dims, kind)


def project_kernel(
    at, x00, x01, x10, x11, gain, factor, w_mine, w_a, w_b, qkv, raw, normed, scale_own, w_full
):
    r, k = at[0], at[2]
    tok, feat = x00.shape
    hr = w_mine.shape[1]
    half = hr // 2
    for s in range(3):
        w_full[pl.ds(s * hr, hr), 0:feat] = w_mine[s]
        w_full[pl.ds(pl.multiple_of(s * hr + k * half, 16), half), feat:] = w_a[s]
        w_full[pl.ds(pl.multiple_of(s * hr + (1 - k) * half, 16), half), feat:] = w_b[s]
    for i, (a_ref, b_ref) in enumerate(((x00, x01), (x10, x11))):
        a, b = a_ref[...].astype(F32), b_ref[...].astype(F32)
        total = jnp.sum(a * a, axis=1, keepdims=True) + jnp.sum(b * b, axis=1, keepdims=True)
        scale = lax.rsqrt(total / (2 * feat) + EPS)
        if i == 0:
            scale_own[...] = scale
        rows = pl.ds(pl.multiple_of((r ^ i) * tok, tok), tok)
        normed[rows, 0:feat] = (a * scale * gain[:, 0:feat]).astype(BF)
        normed[rows, feat:] = (b * scale * gain[:, feat:]).astype(BF)
        y = normed[rows, :]
        q = dot(w_full[0:hr, :], y, (1, 1))
        raw[:, rows] = q
        qkv[0, :, rows] = (q * factor[...]).astype(BF)
        qkv[1, :, rows] = dot(w_full[hr : 2 * hr, :], y, (1, 1)).astype(BF)
        qkv[2, :, rows] = dot(w_full[2 * hr : 3 * hr, :], y, (1, 1)).astype(BF)


def feed_kernel(
    at, gain, bias_up, bias_down, a, x_own, x_col, g_own, g_col,
    w_out, w_up, w_down, hx, hy, d0, d1, hx2, hy2, d02, d12,
    out_own, gm_own, post, ts, vectors, att, hidden_out, normed_out, g_out, pre_out, branch_out,
    w, x_ref, sems, more_sems,
):
    r, c, k = at[0], at[1], at[2]
    _, hr, share = a.shape
    feat = x_own.shape[1]
    half = feat // 2
    first = d0.shape[1]
    rows = pl.ds(pl.multiple_of(c * share, share), share)

    def start(pairs, sem):
        copies = [pltpu.make_async_copy(src, dst, sem.at[m]) for m, (src, dst) in enumerate(pairs)]
        for copy in copies:
            copy.start()
        return copies

    def place(s):
        return pl.ds(pl.multiple_of(((s // 2) ^ r) * 2 * hr + (s % 2) * hr, 16), hr)

    small = [(a.at[s], att.at[place(s), :]) for s in range(4)]
    small += [(x_own.at[rows, :], x_ref.at[:, 0:feat]), (x_col.at[rows, :], x_ref.at[:, feat:])]
    small += [(g_own.at[rows, :], g_out.at[:, 0:feat]), (g_col, g_out.at[:, feat:])]
    small = start(small, more_sems)
    copies = []
    for n, shard in enumerate((w_out, w_up, w_down)):
        rx, cx, ry, cy = (0, feat, feat, 0) if n == 1 else (feat, 0, 0, feat)
        mine = [(shard, w.at[n, 0:feat, 0:feat])]
        for core, (px, py, p0, p1) in ((k, (hx, hy, d0, d1)), (1 - k, (hx2, hy2, d02, d12))):
            down = core * half
            at_x = pl.ds(pl.multiple_of(rx + down, 16), half)
            at_y = pl.ds(pl.multiple_of(ry + down, 16), half)
            at_0 = pl.ds(pl.multiple_of(feat + down, 16), first)
            at_1 = pl.ds(pl.multiple_of(feat + down + first, 16), half - first)
            mine.append((px.at[n], w.at[n, at_x, cx : cx + feat]))
            mine.append((py.at[n], w.at[n, at_y, cy : cy + feat]))
            mine.append((p0.at[n], w.at[n, at_0, feat : 2 * feat]))
            mine.append((p1.at[n], w.at[n, at_1, feat : 2 * feat]))
        copies.append(start(mine, sems.at[n]))

    for copy in small + copies[0]:
        copy.wait()
    middle = x_ref[...].astype(F32) + dot(att[...], w[0], (0, 0))
    scale = lax.rsqrt(jnp.sum(middle * middle, axis=1, keepdims=True) / D + EPS)
    normed = (middle * scale * gain[...]).astype(BF)
    normed_out[...] = normed
    for copy in copies[1]:
        copy.wait()
    pre = dot(normed, w[1], (1, 0)) + bias_up[...]
    sig = jax.nn.sigmoid(pre)
    hidden = (pre * sig).astype(BF)
    hidden_out[...] = hidden
    for copy in copies[2]:
        copy.wait()
    result = (middle + dot(hidden, w[2], (1, 0)) + bias_down[...]).astype(BF)
    out_own[...] = result[:, :feat]
    post[0] = result[:, feat:]

    grad_pre_f = dot(g_out[...], w[2], (1, 1)) * sig * (1.0 + pre * (1.0 - sig))
    grad_pre = grad_pre_f.astype(BF)
    pre_out[...] = grad_pre
    grad_normed = dot(grad_pre, w[1], (1, 1))
    weighted = grad_normed * gain[...]
    inner = jnp.sum(weighted * middle, axis=1, keepdims=True)
    gf = g_out[...].astype(F32)
    grad_middle = gf + scale * weighted - middle * (scale * scale * scale * inner / D)
    gm_own[...] = grad_middle[:, :feat]
    post[1] = grad_middle[:, feat:].astype(BF)
    branch = grad_middle.astype(BF)
    branch_out[...] = branch
    for s in range(4):
        ts[s] = dot(w[0, place(s), :], branch, (1, 1)).astype(BF)
    vectors[...] = jnp.concatenate(
        [
            jnp.sum(grad_normed * (middle * scale), axis=0, keepdims=True),
            jnp.sum(gf, axis=0, keepdims=True),
            jnp.sum(grad_pre.astype(F32), axis=0, keepdims=True),
        ],
        axis=0,
    )


def feed_weights_kernel(at, att, hidden, normed, g, grad_pre, branch, *rest):
    *grads, stage, turned, sems = rest
    k = at[2]
    feat = g.shape[1] // 2
    half = feat // 2
    quarter = half // 2
    copies = []

    def weight_grad(n, left_ref, right):
        for core, begin in ((k, 0), (1 - k, 8)):
            up, low = (begin + 4, begin) if n == 1 else (begin, begin + 4)
            for b in range(2):
                part = pl.ds(pl.multiple_of(b * feat + core * half, 16), half)
                y = dot(left_ref[part, :], right, (1, 0)).astype(BF)
                for j in range(2):
                    cut = slice(j * feat, (j + 1) * feat)
                    for to, value in ((up + 2 * j + (1 - b), y[:quarter, cut]), (low + 2 * b + (1 - j), y[quarter:, cut])):
                        stage[to, n] = value
                        copy = pltpu.make_async_copy(stage.at[to, n], grads[to].at[n], sems.at[to, n])
                        copy.start()
                        copies.append(copy)

    turned[0] = hidden[...].astype(F32).T.astype(BF)
    weight_grad(2, turned.at[0], g[...])
    turned[1] = normed[...].astype(F32).T.astype(BF)
    weight_grad(1, turned.at[1], grad_pre[...])
    weight_grad(0, att, branch[...])
    for copy in copies:
        copy.wait()


def weight_back_kernel(at, grad, normed, keep, give):
    k = at[2]
    part = keep.shape[2]
    feat = keep.shape[3]
    for ref, core in ((give, 1 - k), (keep, k)):
        for s in range(3):
            rows = pl.ds(pl.multiple_of(core * part, 16), part)
            y = dot(grad[s, rows, :], normed[...], (1, 0)).astype(BF)
            ref[0, s] = y[:, :feat]
            ref[1, s] = y[:, feat:]


def project_back_kernel(
    at, grad, w_full, x00, x01, x10, x11, gain, es, gain_sum
):
    r, c = at[0], at[1]
    tok, feat = x00.shape
    sums = [jnp.zeros((1, feat), F32), jnp.zeros((1, feat), F32)]
    for i, xs in enumerate(((x00, x01), (x10, x11))):
        rows = pl.ds(pl.multiple_of((r ^ i) * tok, tok), tok)
        left = grad[:, rows]
        products, squares, inner = [], 0.0, 0.0
        for j in range(2):
            cut = slice(j * feat, (j + 1) * feat)
            e = dot(left, w_full[:, cut], (0, 0))
            x = xs[j][...].astype(F32)
            product = e * x
            inner = inner + jnp.sum(product * gain[:, cut], axis=1, keepdims=True)
            squares = squares + jnp.sum(x * x, axis=1, keepdims=True)
            es[2 * (r ^ i) + (c ^ j), 0:tok, :] = e.astype(BF)
            products.append(product)
        scale = lax.rsqrt(squares / (2 * feat) + EPS)
        for j in range(2):
            sums[j] += jnp.sum(products[j] * scale, axis=0, keepdims=True)
        line = jnp.broadcast_to(inner, (tok, 128)).T[0:1, :]
        high = line.astype(BF).astype(F32)
        extra = jnp.concatenate([high, line - high, jnp.zeros((14, tok), F32)], axis=0)
        extra = jnp.concatenate([extra, jnp.zeros((16, feat - tok), F32)], axis=1).astype(BF)
        for j in range(2):
            es[2 * (r ^ i) + (c ^ j), tok:, :] = extra
    gain_sum[:, 0:feat] = sums[0]
    gain_sum[:, feat:] = sums[1]


def finish_qkv_kernel(at, mine, theirs, mine2, theirs2, out, rows):
    c, k = at[1], at[2]
    half = mine.shape[1]
    for s in range(3):
        for ref, col, core in ((mine, c, k), (theirs, 1 - c, k), (mine2, c, 1 - k), (theirs2, 1 - c, 1 - k)):
            rows[pl.ds(pl.multiple_of((2 * col + core) * half, 16), half), :] = ref[s].astype(F32)
        out[s] = rows[...].T


def finish_feed_kernel(at, a, b, a2, b2, *outs):
    k = at[2]
    quarter = a.shape[1]
    for n, out in enumerate(outs):
        upper, lower = ((b, b2), (a, a2)) if n == 1 else ((a, a2), (b, b2))
        for i, core in ((0, k), (1, 1 - k)):
            for j, refs in enumerate((upper, lower)):
                to = pl.multiple_of((2 * core + j) * quarter, 16)
                out[pl.ds(to, quarter), :] = refs[i][n].astype(F32)


together = lax.optimization_barrier


def after(x, *earlier):
    return lax.optimization_barrier((x, *earlier))[0]


def add(*parts):
    total = parts[0].astype(F32)
    for part in parts[1:]:
        total = total + part.astype(F32)
    return total.astype(BF)


def all_four(x):
    return lax.all_to_all(x, ("row", "col"), 0, 0, tiled=True)


def z_swap(x, step):
    n = size("z")
    return lax.ppermute(x, "z", [(i, i ^ step) for i in range(n)])


def z_first():
    z = lax.axis_index("z")
    return (z == 0) | (z == 3)


def body_four(
    inputs, gain_attn, w_qkv, query_scale, w_out, gain_mlp, w_up, b_up, w_down, b_down, series_ids, pad_mask, cotangent
):
    tok, feat = inputs.shape
    share = tok // 2
    t = series_ids.shape[0]
    hr = w_qkv.shape[2] // 2
    heads = hr // HEAD_DIM
    half = feat // 2
    r, c, k = lax.axis_index("row"), lax.axis_index("col"), lax.axis_index("core")
    at = jnp.stack([r, c, k, 2 * r + c]).astype(jnp.int32)
    mine_rows = lambda y, part: lax.dynamic_slice_in_dim(y, part * share, share, 0)

    few = heads // 2
    quarter = half // 2
    first_rows = (half * 7 // 20) // 16 * 16
    x01 = swap(inputs, "col")
    x10 = swap(inputs, "row")
    small = swap(jnp.concatenate([gain_attn, gain_mlp, b_down.astype(F32)]), "col")
    up_other = swap(b_up.astype(F32), "row")
    w_turned = jnp.transpose(w_qkv, (1, 2, 0)).reshape(3, 2, hr, feat)
    w_mine = lax.dynamic_index_in_dim(w_turned, c, 1, keepdims=False)
    w_give = lax.dynamic_index_in_dim(w_turned, 1 - c, 1, keepdims=False)
    w_half = core_half(w_give, 1)
    w_a = swap(w_half, "col")
    part = jnp.stack([core_half(w_out, 0), core_half(w_up, 0), core_half(w_down, 0)])
    g_give = mine_rows(cotangent, 1 - c)
    x01, x10, small, up_other, part, g_give, w_mine = lax.optimization_barrier(
        (x01, x10, small, up_other, part, g_give, w_mine)
    )
    x11 = swap(after(x01, w_half), "row")
    w_b = swap(w_a, "core")
    gain_one = jnp.concatenate([gain_attn, small[:feat]]).reshape(1, D)
    gain_two = jnp.concatenate([gain_mlp, small[feat : 2 * feat]]).reshape(1, D)
    bias_down = jnp.concatenate([b_down.astype(F32), small[2 * feat :]]).reshape(1, D)
    bias_up = jnp.concatenate([b_up.astype(F32), up_other]).reshape(1, D)
    factor = QUERY_CONST / math.sqrt(HEAD_DIM) * jax.nn.softplus(query_scale)
    factor_col = factor.reshape(HEAD_DIM, 1)

    part = after(part, x11, w_a)
    hx, hy = swap(part, "row"), swap(part, "col")
    hx2, hy2 = swap(hx, "core"), swap(hy, "core")
    qkv, raw, normed_one, scale_own, w_full = call(
        project_kernel,
        "project",
        (at, inputs, x01, x10, x11, gain_one, jnp.tile(factor_col, (heads, 1)), w_mine, w_a, w_b),
        [SMEM] + [VM] * 9,
        [
            shape((3, hr, t), BF),
            shape((hr, t), F32),
            shape((t, D), BF),
            shape((tok, 1), F32),
            shape((3 * hr, D), BF),
        ],
        limit=VMEM_LARGE,
    )
    qkv = qkv.reshape(3, heads, HEAD_DIM, t)
    masks = mask_args(series_ids, pad_mask)
    attended, lse, a = attention_forward(at, qkv, masks, pieces=1)
    a = all_four(a.reshape(4, hr, share))
    hx_on, hy_on, g_give = lax.optimization_barrier((hx, hy, g_give, lse))[:3]
    d0 = swap(hx_on[:, :first_rows], "col")
    d1 = swap(hy_on[:, first_rows:], "row")
    g_col = swap(g_give, "col")
    d0, d1, g_col, a = together((d0, d1, g_col, a))
    d02, d12 = swap(d0, "core"), swap(d1, "core")
    out_own, gm_own, post, ts, vectors, *factors = call(
        feed_kernel,
        "feed_forward",
        (at, gain_two, bias_up, bias_down, a, inputs, x01, cotangent, g_col)
        + (w_out, w_up, w_down, hx, hy, d0, d1, hx2, hy2, d02, d12),
        [SMEM] + [VM] * 3 + [HBM] * 16,
        [
            shape((share, feat), BF),
            shape((share, feat), F32),
            shape((2, share, feat), BF),
            shape((4, hr, share), BF),
            shape((3, D), F32),
            shape((D, share), BF),
        ]
        + [shape((share, D), BF)] * 5,
        scratch=[
            pltpu.VMEM((3, D, D), BF),
            pltpu.VMEM((share, D), BF),
            pltpu.SemaphoreType.DMA((3, 9)),
            pltpu.SemaphoreType.DMA((8,)),
        ],
        limit=VMEM_LARGE,
    )
    grads = call(
        feed_weights_kernel,
        "feed_weights",
        (at, *factors),
        [SMEM] + [VM] * 6,
        [shape((3, quarter, feat), BF)] * 16,
        scratch=[
            pltpu.VMEM((16, 3, quarter, feat), BF),
            pltpu.VMEM((2, D, share), BF),
            pltpu.SemaphoreType.DMA((16, 3)),
        ],
        out_specs=[HBM] * 16,
        limit=VMEM_LARGE,
    )
    ts = all_four(ts)
    others = grads[8:]
    over = lambda n: swap(others[n], "core")
    grads, osx0, osx1, osy0, osy1 = grads[:8], over(0), over(2), over(4), over(6)
    sx0, kx0, sx1, kx1, sy0, ky0, sy1, ky1 = grads
    sx1, sy1 = add(sx1, osx1), add(sy1, osy1)
    ox0, ox1, oy0, oy1 = over(1), over(3), over(5), over(7)
    sx0, sy0 = add(sx0, osx0), add(sy0, osy0)
    ts, sx1, sy1, sx0, sy0 = together((ts, sx1, sy1, sx0, sy0))
    rx1, ry1 = swap(sx1, "row"), swap(sy1, "col")
    rx0, ry0 = swap(sx0, "row"), swap(sy0, "col")
    ts = ts.reshape(4, heads, HEAD_DIM, share)
    raw = raw.reshape(heads, HEAD_DIM, t)

    grad_proj, gscale = attention_backward(at, qkv, raw, factor_col, attended, ts, lse, masks)
    grad_proj = grad_proj.reshape(3, hr, t)
    kept, sent = call(
        weight_back_kernel,
        "weight_back",
        (at, grad_proj, normed_one),
        [SMEM] + [VM] * 2,
        [shape((2, 3, hr // 2, feat), BF)] * 2,
    )
    sent, rx1, ry1, rx0, ry0, ox0, ox1, oy0, oy1 = together((sent, rx1, ry1, rx0, ry0, ox0, ox1, oy0, oy1))
    got = swap(sent, "core")
    px1, py1 = add(kx1, ox1, rx1), add(ky1, oy1, ry1)
    qx, qy = swap(px1, "col"), swap(py1, "row")
    w_pair = add(kept, got)
    first = z_first()
    got_w = z_swap(jnp.where(first, w_pair[1], w_pair[0]), 1)
    slope = QUERY_CONST / math.sqrt(HEAD_DIM) * jax.nn.sigmoid(query_scale)
    grad_query_scale = jnp.sum(gscale, axis=(0, 2)) * slope
    es, gain_sum = call(
        project_back_kernel,
        "project_back",
        (at, after(grad_proj, w_pair, px1, py1).reshape(3 * hr, t), w_full, inputs, x01, x10, x11, gain_one),
        [SMEM] + [VM] * 7,
        [
            shape((4, tok + 16, feat), BF),
            shape((1, D), F32),
        ],
    )
    total = jnp.concatenate([gain_sum, vectors]).reshape(4, 2, feat)
    turn = jnp.stack([c, c, c, r]).reshape(4, 1, 1) == 1
    total = jnp.where(turn, total[:, ::-1], total).reshape(8, feat)
    total = jnp.concatenate([total, jnp.pad(grad_query_scale, (0, feat - HEAD_DIM)).reshape(1, feat)])
    qx, qy, got_w, w_pair, es = together((qx, qy, got_w, w_pair, es))

    mine_w = add(jnp.where(first, w_pair[0], w_pair[1]), got_w)
    met_w = z_swap(mine_w, 3)
    fx, fy = add(kx0, ox0, rx0, qx), add(ky0, oy0, ry0, qy)
    got_c = z_swap(jnp.where(first, fy, fx), 1)
    es = all_four(after(es, fx, fy, mine_w))
    met_w, mine_w, got_c, fx, fy, es, post, total = together((met_w, mine_w, got_c, fx, fy, es, post, total))

    mine_w = add(mine_w, met_w)
    other_w = z_swap(mine_w, 1)
    w_own, w_theirs = jnp.where(first, mine_w, other_w), jnp.where(first, other_w, mine_w)
    mine_c = add(jnp.where(first, fx, fy), got_c)
    met_c = z_swap(mine_c, 3)
    post = swap(post, "col")
    w_theirs = swap(w_theirs, "col")
    total = total + swap(total, "core")
    total = total + swap(total, "row")
    total = total + swap(total, "col")
    met_c, mine_c, w_own, w_theirs, post, total = together((met_c, mine_c, w_own, w_theirs, post, total))
    mine_c = add(mine_c, met_c)
    other_c = z_swap(mine_c, 1)
    total = total + z_swap(total, 1)
    total_z = z_swap(total, 3)
    w_args = (at, w_own, w_theirs, swap(w_own, "core"), swap(w_theirs, "core"))
    sum_qkv = call(
        finish_qkv_kernel,
        "finish_qkv",
        w_args,
        [SMEM] + [VM] * 4,
        shape((3, feat, 2 * hr), F32),
        scratch=[pltpu.VMEM((2 * hr, feat), F32)],
    )
    sum_qkv = jnp.transpose(sum_qkv, (1, 0, 2))

    e = jnp.sum(es[:, :tok].astype(F32), axis=0)
    inner = jnp.sum(es[:, tok : tok + 2, :tok].astype(F32), axis=(0, 1)).reshape(tok, 1)
    grad_middle = jnp.concatenate(flip([gm_own, post[1].astype(F32)], "col"), axis=0)
    grad_inputs = grad_middle + scale_own * (e * gain_attn) - inputs.astype(F32) * (scale_own**3 * inner / D)
    layer_out = jnp.concatenate(flip([out_own, post[0]], "col"), axis=0)

    total = after(total, sum_qkv, grad_inputs) + total_z
    pick = lambda n, place: lax.dynamic_index_in_dim(total, 2 * n + place, 0, keepdims=False)
    mine_c = after(mine_c, sum_qkv, grad_inputs, layer_out, total)
    fx, fy = jnp.where(first, mine_c, other_c), jnp.where(first, other_c, mine_c)
    sum_out, sum_up, sum_down = call(
        finish_feed_kernel,
        "finish_feed",
        (at, fx, fy, swap(fx, "core"), swap(fy, "core")),
        [SMEM] + [VM] * 4,
        [shape((feat, feat), F32)] * 3,
    )

    return (
        layer_out,
        grad_inputs,
        pick(0, c),
        sum_qkv,
        total[8, :HEAD_DIM],
        sum_out,
        pick(1, c),
        sum_up,
        pick(3, r),
        sum_down,
        pick(2, c),
    )


def solution(mesh):
    dp, rows, cols = mesh.shape["dp"], mesh.shape["row"], mesh.shape["col"]
    split = Mesh(mesh.devices.reshape(dp // 2, 2, rows, cols), ("z", "core", "row", "col"))
    tokens = P(("z", "core", "row"), "col")
    in_specs = (
        tokens,
        P("col"),
        P("col", None, "row"),
        P(),
        P("row", "col"),
        P("col"),
        P("col", "row"),
        P("row"),
        P("row", "col"),
        P("col"),
        P(("z", "core")),
        P(("z", "core")),
        tokens,
    )
    out_specs = (
        tokens,
        tokens,
        P("col"),
        P("col", None, "row"),
        P(),
        P("row", "col"),
        P("col"),
        P("col", "row"),
        P("row"),
        P("row", "col"),
        P("col"),
    )
    body = body_four if (dp, rows, cols) == (8, 2, 2) else body_any
    return jax.shard_map(body, mesh=split, in_specs=in_specs, out_specs=out_specs, check_vma=False)
```

```python
import functools
import math

import jax
import jax.numpy as jnp
from jax import lax
from jax.experimental import pallas as pl
from jax.experimental.pallas import tpu as pltpu
from jax.sharding import Mesh
from jax.sharding import PartitionSpec as P

D = 1280
HEAD_DIM = 80
EPS = 1e-06
QUERY_CONST = 1.442695041
MASKED = -1e30
BF = jnp.bfloat16
F32 = jnp.float32
VMEM_LIMIT = 60 * 1024 * 1024
CHUNK = 1024
VMEM_LARGE = 60 * 1024 * 1024
CHEAP = pl.CostEstimate(flops=1, bytes_accessed=1, transcendentals=0)


def size(axis):
    return lax.axis_size(axis)


def swap(x, axis):
    return lax.ppermute(x, axis, [(0, 1), (1, 0)])


def flip(blocks, axis):
    if size(axis) != 2:
        return list(blocks)
    first = lax.axis_index(axis) == 0
    a, b = blocks
    return [jnp.where(first, a, b), jnp.where(first, b, a)]


def flip_dim(x, axis, dim):
    if size(axis) != 2:
        return x
    return jnp.concatenate(flip(jnp.split(x, 2, axis=dim), axis), axis=dim)


def gather(x, axis):
    if size(axis) == 2:
        return [x, swap(x, axis)]
    whole = lax.all_gather(x, axis, axis=0, tiled=False)
    return [whole[i] for i in range(size(axis))]


def gather_grid(x):
    if size("row") != 2:
        return [gather(b, "col") for b in gather(x, "row")]
    along_row, along_col = swap(x, "row"), swap(x, "col")
    half = x.shape[0] // 2
    across = jnp.concatenate(
        [swap(along_row[:half], "col"), swap(along_col[half:], "row")], axis=0
    )
    return [[x, along_col], [along_row, across]]


def scatter_sum(x, axis, dim):
    if size(axis) != 2:
        return lax.psum_scatter(x, axis, scatter_dimension=dim, tiled=True)
    mine, theirs = jnp.split(x, 2, axis=dim)
    return (mine.astype(F32) + swap(theirs, axis).astype(F32)).astype(x.dtype)


def exchange(x, axis, split, join):
    if size(axis) != 2:
        return lax.all_to_all(x, axis, split, join, tiled=True)
    mine, theirs = jnp.split(x, 2, axis=split)
    return jnp.concatenate([mine, swap(theirs, axis)], axis=join)


def core_half(x, dim):
    return lax.dynamic_slice_in_dim(
        x, lax.axis_index("core") * (x.shape[dim] // 2), x.shape[dim] // 2, dim
    )


def weight_gather(w, row_dim):
    part = core_half(w, 0)
    blocks = gather_grid(part)
    if row_dim == 1:
        blocks = [list(b) for b in zip(*blocks)]
    mine = jnp.stack([jnp.concatenate(b, axis=1) for b in blocks])
    other = swap(mine, "core")
    first = lax.axis_index("core") == 0
    both = jnp.stack([jnp.where(first, mine, other), jnp.where(first, other, mine)], axis=1)
    return both.reshape(-1, both.shape[-1])


def weight_sum(g, row_dim):
    dim_axis = ("row", "col") if row_dim == 0 else ("col", "row")
    n0 = size(dim_axis[0])
    g = g.reshape(n0, 2, g.shape[0] // n0 // 2, g.shape[1])
    core = lax.axis_index("core")
    keep = lax.dynamic_index_in_dim(g, core, 1, keepdims=False)
    give = lax.dynamic_index_in_dim(g, 1 - core, 1, keepdims=False).astype(BF)
    part = (keep + swap(give, "core").astype(F32)).astype(BF)
    part = scatter_sum(part, dim_axis[0], 0)
    part = scatter_sum(part[0], dim_axis[1], 1)
    return z_sum(part)


def z_sum(part):
    total = lax.psum(part, "z")
    other = swap(total, "core")
    return flip_core(total, other)


def flip_core(total, other):
    first = lax.axis_index("core") == 0
    return jnp.concatenate(
        [jnp.where(first, total, other), jnp.where(first, other, total)], axis=-2
    ).astype(F32)


def dot(a, b, contract):
    return lax.dot_general(a, b, ((contract[0:1], contract[1:2]), ((), ())), preferred_element_type=F32)


def bias_block(series_row, series_col, key_pos, q0, k0, qb, kb, diagonal):
    q_pos = q0 + lax.broadcasted_iota(jnp.int32, (1, qb), 1)
    allowed = (series_col == series_row) & (key_pos <= q_pos)
    if diagonal:
        k_pos = k0 + lax.broadcasted_iota(jnp.int32, (kb, 1), 0)
        allowed = allowed | (k_pos == q_pos)
    return jnp.where(allowed, 0.0, MASKED)


def forward_kernel(block, at, qkv_ref, srow_ref, scol_ref, kpos_ref, out_ref, lse_ref, *rest):
    *pieces, bias_ref, krow_ref, s_ref = rest
    t = qkv_ref.shape[3]
    n = t // block
    krow_ref[...] = qkv_ref[1, 0].astype(F32).T.astype(BF)

    def bias_slot(j, i):
        return j * (j + 1) // 2 + i

    @pl.when(pl.program_id(0) == 0)
    def _():
        for j in range(n):
            for i in range(j + 1):
                keys = pl.ds(i * block, block)
                bias_ref[bias_slot(j, i)] = bias_block(
                    srow_ref[:, j * block : (j + 1) * block],
                    scol_ref[keys, :],
                    kpos_ref[keys, :],
                    j * block,
                    i * block,
                    block,
                    block,
                    i == j,
                )

    for j in range(n):
        cols = slice(j * block, (j + 1) * block)
        q = qkv_ref[0, 0, :, cols]
        top = None
        for i in range(j + 1):
            s = dot(krow_ref[i * block : (i + 1) * block, :], q, (1, 0)) + bias_ref[bias_slot(j, i)]
            s_ref[i * block : (i + 1) * block, :] = s
            here = jnp.max(s, axis=0, keepdims=True)
            top = here if top is None else jnp.maximum(top, here)
        total = jnp.zeros((1, block), F32)
        acc = jnp.zeros((HEAD_DIM, block), F32)
        for i in range(j + 1):
            p = jnp.exp(s_ref[i * block : (i + 1) * block, :] - top)
            total += jnp.sum(p, axis=0, keepdims=True)
            acc += dot(qkv_ref[2, 0, :, i * block : (i + 1) * block], p.astype(BF), (1, 0))
        found = (acc / total).astype(BF)
        out_ref[0, :, cols] = found
        if pieces:
            pieces[0][j, 0] = found
        lse_ref[0, :, cols] = top + jnp.log(total)


def backward_kernel(
    block, at, qkv_ref, raw_ref, factor_ref, out_ref, lse_ref, srow_ref, scol_ref, kpos_ref, *rest
):
    piece, grad_ref, gscale_ref, bias_ref, krow_ref, vrow_ref, gk_ref, gv_ref, gout_ref = rest
    wide = piece.shape[3]
    for j in range(piece.shape[0]):
        gout_ref[:, j * wide : (j + 1) * wide] = piece[j, 0]
    t = qkv_ref.shape[3]
    n = t // block
    krow_ref[...] = qkv_ref[1, 0].astype(F32).T.astype(BF)
    vrow_ref[...] = qkv_ref[2, 0].astype(F32).T.astype(BF)

    def bias_slot(j, i):
        return j * (j + 1) // 2 + i

    @pl.when(pl.program_id(0) == 0)
    def _():
        for j in range(n):
            for i in range(j + 1):
                keys = pl.ds(i * block, block)
                bias_ref[bias_slot(j, i)] = bias_block(
                    srow_ref[:, j * block : (j + 1) * block],
                    scol_ref[keys, :],
                    kpos_ref[keys, :],
                    j * block,
                    i * block,
                    block,
                    block,
                    i == j,
                )

    gscale = jnp.zeros((HEAD_DIM, 1), F32)
    for j in range(n):
        cols = slice(j * block, (j + 1) * block)
        q = qkv_ref[0, 0, :, cols]
        go = gout_ref[:, cols]
        lse = lse_ref[0, :, cols]
        delta = jnp.sum(go.astype(F32) * out_ref[0, :, cols].astype(F32), axis=0, keepdims=True)
        gq = jnp.zeros((HEAD_DIM, block), F32)
        step = max(1, CHUNK // block)
        for i in range(0, j + 1, step):
            many = min(step, j + 1 - i)
            keys = slice(i * block, (i + many) * block)
            slot = bias_slot(j, i)
            bias = bias_ref[slot : slot + many].reshape(many * block, block)
            p = jnp.exp(dot(krow_ref[keys, :], q, (1, 0)) + bias - lse)
            gp = dot(vrow_ref[keys, :], go, (1, 0))
            gs = (p * (gp - delta)).astype(BF)
            gq += dot(qkv_ref[1, 0, :, keys], gs, (1, 0))
            gk = dot(q, gs, (1, 1))
            gv = dot(go, p.astype(BF), (1, 1))
            before, last = slice(i * block, min(i + many, j) * block), slice(j * block, (j + 1) * block)
            old = (min(i + many, j) - i) * block
            if old:
                gk_ref[:, before] += gk[:, :old]
                gv_ref[:, before] += gv[:, :old]
            if i + many == j + 1:
                gk_ref[:, last] = gk[:, old:]
                gv_ref[:, last] = gv[:, old:]
        gscale += jnp.sum(gq * raw_ref[0, :, cols], axis=1, keepdims=True)
        grad_ref[0, 0, :, cols] = (gq * factor_ref[...]).astype(BF)
    grad_ref[1, 0] = gk_ref[...].astype(BF)
    grad_ref[2, 0] = gv_ref[...].astype(BF)
    gscale_ref[0] = gscale


def mask_args(series, padding):
    t = series.shape[0]
    pos = jnp.arange(t, dtype=jnp.int32)
    return series.reshape(1, t), series.reshape(t, 1), jnp.where(padding == 0, pos, t).reshape(t, 1)


def attention_forward(at, qkv, masks, pieces=0):
    _, heads, hd, t = qkv.shape
    block = min(256, t) if t <= 2048 else 512
    n = t // block
    whole = lambda shape: pl.BlockSpec(shape, lambda h: (0,) * len(shape))
    return pl.pallas_call(
        functools.partial(forward_kernel, block),
        grid=(heads,),
        in_specs=[
            pl.BlockSpec(memory_space=pltpu.SMEM),
            pl.BlockSpec((3, 1, hd, t), lambda h: (0, h, 0, 0)),
            whole((1, t)),
            whole((t, 1)),
            whole((t, 1)),
        ],
        out_specs=[
            pl.BlockSpec((1, hd, t), lambda h: (h, 0, 0)),
            pl.BlockSpec((1, 1, t), lambda h: (h, 0, 0)),
        ]
        + [pl.BlockSpec((n, 1, hd, block), lambda h: (0, h, 0, 0))] * pieces,
        out_shape=[
            jax.ShapeDtypeStruct((heads, hd, t), BF),
            jax.ShapeDtypeStruct((heads, 1, t), F32),
        ]
        + [jax.ShapeDtypeStruct((n, heads, hd, block), BF)] * pieces,
        scratch_shapes=[
            pltpu.VMEM((n * (n + 1) // 2, block, block), F32),
            pltpu.VMEM((t, hd), BF),
            pltpu.VMEM((t, block), F32),
        ],
        compiler_params=pltpu.CompilerParams(vmem_limit_bytes=VMEM_LARGE),
        cost_estimate=CHEAP,
        name="attention_forward",
    )(at, qkv, *masks)


def attention_backward(at, qkv, raw, factor, out, piece, lse, masks):
    _, heads, hd, t = qkv.shape
    block = min(256, t) if t <= 2048 else 512
    n = t // block
    whole = lambda shape: pl.BlockSpec(shape, lambda h: (0,) * len(shape))
    head = lambda wide=t: pl.BlockSpec((1, hd, wide), lambda h: (h, 0, 0))
    return pl.pallas_call(
        functools.partial(backward_kernel, block),
        grid=(heads,),
        in_specs=[
            pl.BlockSpec(memory_space=pltpu.SMEM),
            pl.BlockSpec((3, 1, hd, t), lambda h: (0, h, 0, 0)),
            head(),
            whole((hd, 1)),
            head(),
            pl.BlockSpec((1, 1, t), lambda h: (h, 0, 0)),
            whole((1, t)),
            whole((t, 1)),
            whole((t, 1)),
        ]
        + [pl.BlockSpec((piece.shape[0], 1, hd, piece.shape[3]), lambda h: (0, h, 0, 0))],
        out_specs=[
            pl.BlockSpec((3, 1, hd, t), lambda h: (0, h, 0, 0)),
            pl.BlockSpec((1, hd, 1), lambda h: (h, 0, 0)),
        ],
        out_shape=[
            jax.ShapeDtypeStruct((3, heads, hd, t), BF),
            jax.ShapeDtypeStruct((heads, hd, 1), F32),
        ],
        scratch_shapes=[
            pltpu.VMEM((n * (n + 1) // 2, block, block), F32),
            pltpu.VMEM((t, hd), BF),
            pltpu.VMEM((t, hd), BF),
            pltpu.VMEM((hd, t), F32),
            pltpu.VMEM((hd, t), F32),
            pltpu.VMEM((hd, t), BF),
        ],
        compiler_params=pltpu.CompilerParams(vmem_limit_bytes=VMEM_LARGE),
        cost_estimate=CHEAP,
        name="attention_backward",
    )(at, qkv, raw, factor, out, lse, *masks, piece)


def norm_scale(x):
    return lax.rsqrt(jnp.mean(x * x, axis=1, keepdims=True) + EPS)


def body_any(
    inputs, gain_attn, w_qkv, query_scale, w_out, gain_mlp, w_up, b_up, w_down, b_down, series_ids, pad_mask, cotangent
):
    rows, cols = size("row"), size("col")
    tok = inputs.shape[0]
    feat = inputs.shape[1]
    share = tok // cols
    t = series_ids.shape[0]
    head_rows = w_qkv.shape[2] // cols
    heads = head_rows // HEAD_DIM
    r, c = lax.axis_index("row"), lax.axis_index("col")

    blocks = gather_grid(inputs)
    strips = [jnp.concatenate(b, axis=1) for b in blocks]
    x_own = strips[0] if rows == 2 else lax.dynamic_index_in_dim(jnp.stack(strips), r, 0, keepdims=False)
    x_all = jnp.concatenate(flip(strips, "row"), axis=0)
    gain_one = jnp.concatenate(gather(gain_attn, "col"))
    gain_two = jnp.concatenate(gather(gain_mlp, "col"))
    bias_up = jnp.concatenate(gather(b_up, "row")).astype(F32)
    bias_down = jnp.concatenate(gather(b_down, "col")).astype(F32)

    w3 = jnp.transpose(w_qkv, (1, 0, 2)).reshape(3, feat, cols, head_rows)
    w_mine = lax.dynamic_index_in_dim(w3, c, 2, keepdims=False)
    w_give = lax.dynamic_index_in_dim(w3, 1 - c, 2, keepdims=False)
    w_half = swap(core_half(w_give, 1), "col")
    w_other = swap(w_half, "core")
    first = lax.axis_index("core") == 0
    w_full = jnp.concatenate(
        [w_mine, jnp.where(first, w_half, w_other), jnp.where(first, w_other, w_half)], axis=1
    )

    xf = x_all.astype(F32)
    scale_one = norm_scale(xf)
    normed_one = (xf * scale_one * gain_one).astype(BF)
    projected = jnp.einsum("td,sdh->sht", normed_one, w_full, preferred_element_type=F32)
    projected = projected.reshape(3, heads, HEAD_DIM, t)
    factor = QUERY_CONST / math.sqrt(HEAD_DIM) * jax.nn.softplus(query_scale)
    raw_q = projected[0]
    qkv = jnp.stack([raw_q * factor[None, :, None], projected[1], projected[2]]).astype(BF)
    masks = mask_args(series_ids, pad_mask)
    at = jnp.zeros((4,), jnp.int32)
    attended, lse = attention_forward(at, qkv, masks)

    def to_tokens(y):
        y = flip_dim(y.reshape(head_rows, rows, cols, share), "row", 1)
        y = flip_dim(y, "col", 2)
        y = exchange(y.reshape(1, head_rows, rows, cols, share), "row", 2, 0)
        y = exchange(y.reshape(rows, 1, head_rows, cols, share), "col", 3, 1)
        y = flip_dim(y.reshape(rows, cols, head_rows, share), "col", 1)
        return y.reshape(rows * cols * head_rows, share)

    def to_heads(y):
        y = flip_dim(y.reshape(rows, cols, head_rows, share), "col", 1)
        y = exchange(y.reshape(rows, cols, head_rows, 1, share), "col", 1, 3)
        y = exchange(y.reshape(rows, head_rows, 1, cols, share), "row", 0, 2)
        y = flip_dim(y.reshape(head_rows, rows, cols, share), "col", 2)
        return flip_dim(y, "row", 1).reshape(head_rows, t)

    w_out_all = weight_gather(w_out, 0)
    w_up_all = weight_gather(w_up, 1)
    w_down_all = weight_gather(w_down, 0)

    def my_share(y):
        return lax.dynamic_slice_in_dim(y, c * share, share, 0)

    att = to_tokens(attended.reshape(head_rows, t))
    x_mine = my_share(x_own).astype(F32)
    middle = x_mine + dot(att, w_out_all, (0, 0))
    scale_two = norm_scale(middle)
    normed_two = (middle * scale_two * gain_two).astype(BF)
    pre_act = dot(normed_two, w_up_all, (1, 0)) + bias_up
    sig = jax.nn.sigmoid(pre_act)
    hidden = (pre_act * sig).astype(BF)
    result = (middle + dot(hidden, w_down_all, (1, 0)) + bias_down).astype(BF)

    def to_block(y):
        mine, theirs = jnp.split(y, 2, axis=1)
        return jnp.concatenate(flip([mine, swap(theirs, "col")], "col"), axis=0)

    layer_out = to_block(result)

    g_give = lax.dynamic_slice_in_dim(cotangent, (1 - c) * share, share, 0)
    g = jnp.concatenate([my_share(cotangent), swap(g_give, "col")], axis=1)
    grad_w_down = dot(hidden, g, (0, 0))
    grad_hidden = dot(g, w_down_all, (1, 1))
    grad_pre_f = grad_hidden * sig * (1.0 + pre_act * (1.0 - sig))
    grad_pre = grad_pre_f.astype(BF)
    grad_b_up = jnp.sum(grad_pre.astype(F32), axis=0)
    grad_w_up = dot(normed_two, grad_pre, (0, 0))
    grad_normed_two = dot(grad_pre, w_up_all, (1, 1))
    weighted = grad_normed_two * gain_two
    inner = jnp.sum(weighted * middle, axis=1, keepdims=True)
    grad_middle = g.astype(F32) + scale_two * weighted - middle * (scale_two**3 * inner / D)
    grad_gain_mlp = jnp.sum(grad_normed_two * middle * scale_two, axis=0)
    grad_branch = grad_middle.astype(BF)
    grad_w_out = dot(att, grad_branch, (1, 0))
    grad_att = dot(w_out_all, grad_branch, (1, 1)).astype(BF)
    grad_attended = to_heads(grad_att).reshape(heads, HEAD_DIM, t)
    grad_middle_block = to_block(grad_middle)

    sum_down = weight_sum(grad_w_down, 0)
    sum_up = weight_sum(grad_w_up, 1)
    sum_out = weight_sum(grad_w_out, 0)

    grad_proj, gscale = attention_backward(
        at, qkv, raw_q, factor.reshape(HEAD_DIM, 1), attended, grad_attended[None], lse, masks
    )
    slope = QUERY_CONST / math.sqrt(HEAD_DIM) * jax.nn.sigmoid(query_scale)
    grad_query_scale = jnp.sum(gscale, axis=(0, 2)) * slope
    grad_proj = grad_proj.reshape(3, head_rows, t)
    grad_normed_one = jnp.einsum("sht,sdh->td", grad_proj, w_full, preferred_element_type=F32)
    weighted_one = grad_normed_one * gain_one
    inner_one = jnp.sum(weighted_one * xf, axis=1)
    grad_gain_attn = jnp.sum(grad_normed_one * xf * scale_one, axis=0)
    inner_one = lax.psum(inner_one, ("row", "col"))
    grad_w = jnp.einsum("td,sht->sdh", normed_one, grad_proj, preferred_element_type=F32)
    grad_w = grad_w.reshape(3, cols, 2, feat // 2, head_rows)
    core = lax.axis_index("core")
    keep = lax.dynamic_index_in_dim(grad_w, core, 2, keepdims=False)
    give = lax.dynamic_index_in_dim(grad_w, 1 - core, 2, keepdims=False).astype(BF)
    part = (keep + swap(give, "core").astype(F32)).astype(BF)
    part = jnp.concatenate(flip([part[:, 0], swap(part[:, 1], "col")], "col"), axis=2)
    sum_qkv = jnp.transpose(z_sum(part), (1, 0, 2))

    e = jnp.concatenate(flip(jnp.split(grad_normed_one.astype(BF), 2, axis=0), "row"), axis=0) if rows == 2 else (
        grad_normed_one.astype(BF)
    )
    e = scatter_sum(e, "row", 0)
    e = scatter_sum(e, "col", 1).astype(F32)
    my_rows = lambda y: lax.dynamic_slice_in_dim(y, r * tok, tok, 0)
    scale_mine = my_rows(scale_one)
    inner_mine = my_rows(inner_one.reshape(t, 1))
    grad_inputs = grad_middle_block + scale_mine * (e * gain_attn) - inputs.astype(F32) * (
        scale_mine**3 * inner_mine / D
    )

    grad_b_down = jnp.sum(g.astype(F32), axis=0)
    vectors = jnp.concatenate(
        [
            flip_dim(grad_gain_attn, "col", 0),
            flip_dim(grad_gain_mlp, "col", 0),
            flip_dim(grad_b_down, "col", 0),
            flip_dim(grad_b_up, "row", 0),
            grad_query_scale,
        ]
    )
    vectors = lax.psum(vectors, ("z", "core", "row", "col"))
    mine_col = lambda at: lax.dynamic_slice_in_dim(vectors, at * D + c * feat, feat, 0)
    units = b_up.shape[0]
    return (
        layer_out,
        grad_inputs,
        mine_col(0),
        sum_qkv,
        vectors[4 * D :],
        sum_out,
        mine_col(1),
        sum_up,
        lax.dynamic_slice_in_dim(vectors, 3 * D + r * units, units, 0),
        sum_down,
        mine_col(2),
    )


SMEM = pl.BlockSpec(memory_space=pltpu.SMEM)
ANY = pl.BlockSpec(memory_space=pl.ANY)


def call(kernel, name, args, specs, outs, scratch=(), limit=VMEM_LIMIT, out_specs=None):
    more = {} if out_specs is None else {"out_specs": out_specs}
    return pl.pallas_call(
        kernel,
        in_specs=specs,
        **more,
        out_shape=outs,
        scratch_shapes=list(scratch),
        compiler_params=pltpu.CompilerParams(vmem_limit_bytes=limit),
        cost_estimate=CHEAP,
        name=name,
    )(*args)


VM = pl.BlockSpec(memory_space=pltpu.VMEM)
HBM = pl.BlockSpec(memory_space=pltpu.HBM)


def shape(dims, kind):
    return jax.ShapeDtypeStruct(dims, kind)


def project_kernel(
    at, x00, x01, x10, x11, gain, factor, w_mine, w_a, w_b, qkv, raw, normed, scale_own, w_full
):
    r, k = at[0], at[2]
    tok, feat = x00.shape
    hr = w_mine.shape[1]
    half = hr // 2
    for s in range(3):
        w_full[pl.ds(s * hr, hr), 0:feat] = w_mine[s]
        w_full[pl.ds(pl.multiple_of(s * hr + k * half, 16), half), feat:] = w_a[s]
        w_full[pl.ds(pl.multiple_of(s * hr + (1 - k) * half, 16), half), feat:] = w_b[s]
    for i, (a_ref, b_ref) in enumerate(((x00, x01), (x10, x11))):
        a, b = a_ref[...].astype(F32), b_ref[...].astype(F32)
        total = jnp.sum(a * a, axis=1, keepdims=True) + jnp.sum(b * b, axis=1, keepdims=True)
        scale = lax.rsqrt(total / (2 * feat) + EPS)
        if i == 0:
            scale_own[...] = scale
        rows = pl.ds(pl.multiple_of((r ^ i) * tok, tok), tok)
        normed[rows, 0:feat] = (a * scale * gain[:, 0:feat]).astype(BF)
        normed[rows, feat:] = (b * scale * gain[:, feat:]).astype(BF)
        y = normed[rows, :]
        q = dot(w_full[0:hr, :], y, (1, 1))
        raw[:, rows] = q
        qkv[0, :, rows] = (q * factor[...]).astype(BF)
        qkv[1, :, rows] = dot(w_full[hr : 2 * hr, :], y, (1, 1)).astype(BF)
        qkv[2, :, rows] = dot(w_full[2 * hr : 3 * hr, :], y, (1, 1)).astype(BF)


def feed_kernel(
    at, gain, bias_up, bias_down, a, x_own, x_col, g_own, g_col,
    w_out, w_up, w_down, hx, hy, d0, d1, hx2, hy2, d02, d12,
    out_own, gm_own, post, ts, vectors, att, hidden_out, normed_out, g_out, pre_out, branch_out,
    w, x_ref, sems, more_sems,
):
    r, c, k = at[0], at[1], at[2]
    _, hr, share = a.shape
    feat = x_own.shape[1]
    half = feat // 2
    first = d0.shape[1]
    rows = pl.ds(pl.multiple_of(c * share, share), share)

    def start(pairs, sem):
        copies = [pltpu.make_async_copy(src, dst, sem.at[m]) for m, (src, dst) in enumerate(pairs)]
        for copy in copies:
            copy.start()
        return copies

    def place(s):
        return pl.ds(pl.multiple_of(((s // 2) ^ r) * 2 * hr + (s % 2) * hr, 16), hr)

    small = [(a.at[s], att.at[place(s), :]) for s in range(4)]
    small += [(x_own.at[rows, :], x_ref.at[:, 0:feat]), (x_col.at[rows, :], x_ref.at[:, feat:])]
    small += [(g_own.at[rows, :], g_out.at[:, 0:feat]), (g_col, g_out.at[:, feat:])]
    small = start(small, more_sems)
    copies = []
    for n, shard in enumerate((w_out, w_up, w_down)):
        rx, cx, ry, cy = (0, feat, feat, 0) if n == 1 else (feat, 0, 0, feat)
        mine = [(shard, w.at[n, 0:feat, 0:feat])]
        for core, (px, py, p0, p1) in ((k, (hx, hy, d0, d1)), (1 - k, (hx2, hy2, d02, d12))):
            down = core * half
            at_x = pl.ds(pl.multiple_of(rx + down, 16), half)
            at_y = pl.ds(pl.multiple_of(ry + down, 16), half)
            at_0 = pl.ds(pl.multiple_of(feat + down, 16), first)
            at_1 = pl.ds(pl.multiple_of(feat + down + first, 16), half - first)
            mine.append((px.at[n], w.at[n, at_x, cx : cx + feat]))
            mine.append((py.at[n], w.at[n, at_y, cy : cy + feat]))
            mine.append((p0.at[n], w.at[n, at_0, feat : 2 * feat]))
            mine.append((p1.at[n], w.at[n, at_1, feat : 2 * feat]))
        copies.append(start(mine, sems.at[n]))

    for copy in small + copies[0]:
        copy.wait()
    middle = x_ref[...].astype(F32) + dot(att[...], w[0], (0, 0))
    scale = lax.rsqrt(jnp.sum(middle * middle, axis=1, keepdims=True) / D + EPS)
    normed = (middle * scale * gain[...]).astype(BF)
    normed_out[...] = normed
    for copy in copies[1]:
        copy.wait()
    pre = dot(normed, w[1], (1, 0)) + bias_up[...]
    sig = jax.nn.sigmoid(pre)
    hidden = (pre * sig).astype(BF)
    hidden_out[...] = hidden
    for copy in copies[2]:
        copy.wait()
    result = (middle + dot(hidden, w[2], (1, 0)) + bias_down[...]).astype(BF)
    out_own[...] = result[:, :feat]
    post[0] = result[:, feat:]

    grad_pre_f = dot(g_out[...], w[2], (1, 1)) * sig * (1.0 + pre * (1.0 - sig))
    grad_pre = grad_pre_f.astype(BF)
    pre_out[...] = grad_pre
    grad_normed = dot(grad_pre, w[1], (1, 1))
    weighted = grad_normed * gain[...]
    inner = jnp.sum(weighted * middle, axis=1, keepdims=True)
    gf = g_out[...].astype(F32)
    grad_middle = gf + scale * weighted - middle * (scale * scale * scale * inner / D)
    gm_own[...] = grad_middle[:, :feat]
    post[1] = grad_middle[:, feat:].astype(BF)
    branch = grad_middle.astype(BF)
    branch_out[...] = branch
    for s in range(4):
        ts[s] = dot(w[0, place(s), :], branch, (1, 1)).astype(BF)
    vectors[...] = jnp.concatenate(
        [
            jnp.sum(grad_normed * (middle * scale), axis=0, keepdims=True),
            jnp.sum(gf, axis=0, keepdims=True),
            jnp.sum(grad_pre.astype(F32), axis=0, keepdims=True),
        ],
        axis=0,
    )


def feed_weights_kernel(at, att, hidden, normed, g, grad_pre, branch, *rest):
    *grads, stage, turned, sems = rest
    k = at[2]
    feat = g.shape[1] // 2
    half = feat // 2
    quarter = half // 2
    copies = []

    def weight_grad(n, left_ref, right):
        for core, begin in ((k, 0), (1 - k, 8)):
            up, low = (begin + 4, begin) if n == 1 else (begin, begin + 4)
            for b in range(2):
                part = pl.ds(pl.multiple_of(b * feat + core * half, 16), half)
                y = dot(left_ref[part, :], right, (1, 0)).astype(BF)
                for j in range(2):
                    cut = slice(j * feat, (j + 1) * feat)
                    for to, value in ((up + 2 * j + (1 - b), y[:quarter, cut]), (low + 2 * b + (1 - j), y[quarter:, cut])):
                        stage[to, n] = value
                        copy = pltpu.make_async_copy(stage.at[to, n], grads[to].at[n], sems.at[to, n])
                        copy.start()
                        copies.append(copy)

    turned[0] = hidden[...].astype(F32).T.astype(BF)
    weight_grad(2, turned.at[0], g[...])
    turned[1] = normed[...].astype(F32).T.astype(BF)
    weight_grad(1, turned.at[1], grad_pre[...])
    weight_grad(0, att, branch[...])
    for copy in copies:
        copy.wait()


def weight_back_kernel(at, grad, normed, keep, give):
    k = at[2]
    part = keep.shape[2]
    feat = keep.shape[3]
    for ref, core in ((give, 1 - k), (keep, k)):
        for s in range(3):
            rows = pl.ds(pl.multiple_of(core * part, 16), part)
            y = dot(grad[s, rows, :], normed[...], (1, 0)).astype(BF)
            ref[0, s] = y[:, :feat]
            ref[1, s] = y[:, feat:]


def project_back_kernel(
    at, grad, w_full, x00, x01, x10, x11, gain, vectors, scale_grad, es
):
    r, c = at[0], at[1]
    tok, feat = x00.shape
    sums = [jnp.zeros((1, feat), F32), jnp.zeros((1, feat), F32)]
    inners = []
    for i, xs in enumerate(((x00, x01), (x10, x11))):
        rows = pl.ds(pl.multiple_of((r ^ i) * tok, tok), tok)
        left = grad[:, rows]
        products, squares, inner = [], 0.0, 0.0
        for j in range(2):
            cut = slice(j * feat, (j + 1) * feat)
            e = dot(left, w_full[:, cut], (0, 0))
            x = xs[j][...].astype(F32)
            product = e * x
            inner = inner + jnp.sum(product * gain[:, cut], axis=1, keepdims=True)
            squares = squares + jnp.sum(x * x, axis=1, keepdims=True)
            es[2 * (r ^ i) + (c ^ j), 0:tok, :] = e.astype(BF)
            products.append(product)
        scale = lax.rsqrt(squares / (2 * feat) + EPS)
        for j in range(2):
            sums[j] += jnp.sum(products[j] * scale, axis=0, keepdims=True)
        line = jnp.broadcast_to(inner, (tok, 128)).T[0:1, :]
        high = line.astype(BF).astype(F32)
        inners.append(jnp.concatenate([high, line - high], axis=0))
    rows = []
    pairs = [(sums[0], sums[1], c)]
    pairs += [(vectors[n : n + 1, :feat], vectors[n : n + 1, feat:], (c, c, r)[n]) for n in range(3)]
    for own, other, place in pairs:
        rows += [jnp.where(place == 0, own, other), jnp.where(place == 0, other, own)]
    rows = jnp.concatenate(rows + [scale_grad[...], jnp.zeros((5, feat), F32)], axis=0)
    for i in range(2):
        inner = jnp.concatenate([inners[i], jnp.zeros((2, feat - tok), F32)], axis=1)
        extra = jnp.concatenate([inner, rows], axis=0).astype(BF)
        for j in range(2):
            es[2 * (r ^ i) + (c ^ j), tok:, :] = extra


def finish_qkv_kernel(at, mine, theirs, mine2, theirs2, out, rows):
    c, k = at[1], at[2]
    half = mine.shape[1]
    for s in range(3):
        for ref, col, core in ((mine, c, k), (theirs, 1 - c, k), (mine2, c, 1 - k), (theirs2, 1 - c, 1 - k)):
            rows[pl.ds(pl.multiple_of((2 * col + core) * half, 16), half), :] = ref[s].astype(F32)
        out[s] = rows[...].T


def finish_feed_kernel(at, a, b, a2, b2, *outs):
    k = at[2]
    quarter = a.shape[1]
    for n, out in enumerate(outs):
        upper, lower = ((b, b2), (a, a2)) if n == 1 else ((a, a2), (b, b2))
        for i, core in ((0, k), (1, 1 - k)):
            for j, refs in enumerate((upper, lower)):
                to = pl.multiple_of((2 * core + j) * quarter, 16)
                out[pl.ds(to, quarter), :] = refs[i][n].astype(F32)


together = lax.optimization_barrier


def after(x, *earlier):
    return lax.optimization_barrier((x, *earlier))[0]


def add(*parts):
    total = parts[0].astype(F32)
    for part in parts[1:]:
        total = total + part.astype(F32)
    return total.astype(BF)


def all_four(x):
    return lax.all_to_all(x, ("row", "col"), 0, 0, tiled=True)


def z_swap(x, step):
    n = size("z")
    return lax.ppermute(x, "z", [(i, i ^ step) for i in range(n)])


def z_first():
    z = lax.axis_index("z")
    return (z == 0) | (z == 3)


def body_four(
    inputs, gain_attn, w_qkv, query_scale, w_out, gain_mlp, w_up, b_up, w_down, b_down, series_ids, pad_mask, cotangent
):
    tok, feat = inputs.shape
    share = tok // 2
    t = series_ids.shape[0]
    hr = w_qkv.shape[2] // 2
    heads = hr // HEAD_DIM
    half = feat // 2
    r, c, k = lax.axis_index("row"), lax.axis_index("col"), lax.axis_index("core")
    at = jnp.stack([r, c, k, 2 * r + c]).astype(jnp.int32)
    mine_rows = lambda y, part: lax.dynamic_slice_in_dim(y, part * share, share, 0)

    few = heads // 2
    quarter = half // 2
    first_rows = (half * 7 // 20) // 16 * 16
    x01 = swap(inputs, "col")
    x10 = swap(inputs, "row")
    small = swap(jnp.concatenate([gain_attn, gain_mlp, b_down.astype(F32)]), "col")
    up_other = swap(b_up.astype(F32), "row")
    w_turned = jnp.transpose(w_qkv, (1, 2, 0)).reshape(3, 2, hr, feat)
    w_mine = lax.dynamic_index_in_dim(w_turned, c, 1, keepdims=False)
    w_give = lax.dynamic_index_in_dim(w_turned, 1 - c, 1, keepdims=False)
    w_half = core_half(w_give, 1)
    w_a = swap(w_half, "col")
    part = jnp.stack([core_half(w_out, 0), core_half(w_up, 0), core_half(w_down, 0)])
    g_give = mine_rows(cotangent, 1 - c)
    x01, x10, small, up_other, part, g_give, w_mine = lax.optimization_barrier(
        (x01, x10, small, up_other, part, g_give, w_mine)
    )
    x11 = swap(after(x01, w_half), "row")
    w_b = swap(w_a, "core")
    gain_one = jnp.concatenate([gain_attn, small[:feat]]).reshape(1, D)
    gain_two = jnp.concatenate([gain_mlp, small[feat : 2 * feat]]).reshape(1, D)
    bias_down = jnp.concatenate([b_down.astype(F32), small[2 * feat :]]).reshape(1, D)
    bias_up = jnp.concatenate([b_up.astype(F32), up_other]).reshape(1, D)
    factor = QUERY_CONST / math.sqrt(HEAD_DIM) * jax.nn.softplus(query_scale)
    factor_col = factor.reshape(HEAD_DIM, 1)

    part = after(part, x11, w_a)
    hx, hy = swap(part, "row"), swap(part, "col")
    hx2, hy2 = swap(hx, "core"), swap(hy, "core")
    qkv, raw, normed_one, scale_own, w_full = call(
        project_kernel,
        "project",
        (at, inputs, x01, x10, x11, gain_one, jnp.tile(factor_col, (heads, 1)), w_mine, w_a, w_b),
        [SMEM] + [VM] * 9,
        [
            shape((3, hr, t), BF),
            shape((hr, t), F32),
            shape((t, D), BF),
            shape((tok, 1), F32),
            shape((3 * hr, D), BF),
        ],
        limit=VMEM_LARGE,
    )
    qkv = qkv.reshape(3, heads, HEAD_DIM, t)
    masks = mask_args(series_ids, pad_mask)
    attended, lse, a = attention_forward(at, qkv, masks, pieces=1)
    a = all_four(a.reshape(4, hr, share))
    hx_on, hy_on, g_give = lax.optimization_barrier((hx, hy, g_give, lse))[:3]
    d0 = swap(hx_on[:, :first_rows], "col")
    d1 = swap(hy_on[:, first_rows:], "row")
    g_col = swap(g_give, "col")
    d0, d1, g_col, a = together((d0, d1, g_col, a))
    d02, d12 = swap(d0, "core"), swap(d1, "core")
    out_own, gm_own, post, ts, vectors, *factors = call(
        feed_kernel,
        "feed_forward",
        (at, gain_two, bias_up, bias_down, a, inputs, x01, cotangent, g_col)
        + (w_out, w_up, w_down, hx, hy, d0, d1, hx2, hy2, d02, d12),
        [SMEM] + [VM] * 3 + [HBM] * 16,
        [
            shape((share, feat), BF),
            shape((share, feat), F32),
            shape((2, share, feat), BF),
            shape((4, hr, share), BF),
            shape((3, D), F32),
            shape((D, share), BF),
        ]
        + [shape((share, D), BF)] * 5,
        scratch=[
            pltpu.VMEM((3, D, D), BF),
            pltpu.VMEM((share, D), BF),
            pltpu.SemaphoreType.DMA((3, 9)),
            pltpu.SemaphoreType.DMA((8,)),
        ],
        limit=VMEM_LARGE,
    )
    grads = call(
        feed_weights_kernel,
        "feed_weights",
        (at, *factors),
        [SMEM] + [VM] * 6,
        [shape((3, quarter, feat), BF)] * 16,
        scratch=[
            pltpu.VMEM((16, 3, quarter, feat), BF),
            pltpu.VMEM((2, D, share), BF),
            pltpu.SemaphoreType.DMA((16, 3)),
        ],
        out_specs=[HBM] * 16,
        limit=VMEM_LARGE,
    )
    ts = all_four(ts)
    others = grads[8:]
    over = lambda n: swap(others[n], "core")
    grads, osx0, osx1, osy0, osy1 = grads[:8], over(0), over(2), over(4), over(6)
    sx0, kx0, sx1, kx1, sy0, ky0, sy1, ky1 = grads
    sx1, sy1 = add(sx1, osx1), add(sy1, osy1)
    ox0, ox1, oy0, oy1 = over(1), over(3), over(5), over(7)
    sx0, sy0 = add(sx0, osx0), add(sy0, osy0)
    ts, sx1, sy1, sx0, sy0 = together((ts, sx1, sy1, sx0, sy0))
    rx1, ry1 = swap(sx1, "row"), swap(sy1, "col")
    rx0, ry0 = swap(sx0, "row"), swap(sy0, "col")
    ts = ts.reshape(4, heads, HEAD_DIM, share)
    raw = raw.reshape(heads, HEAD_DIM, t)

    grad_proj, gscale = attention_backward(at, qkv, raw, factor_col, attended, ts, lse, masks)
    grad_proj = grad_proj.reshape(3, hr, t)
    kept, sent = call(
        weight_back_kernel,
        "weight_back",
        (at, grad_proj, normed_one),
        [SMEM] + [VM] * 2,
        [shape((2, 3, hr // 2, feat), BF)] * 2,
    )
    sent, rx1, ry1, rx0, ry0, ox0, ox1, oy0, oy1 = together((sent, rx1, ry1, rx0, ry0, ox0, ox1, oy0, oy1))
    got = swap(sent, "core")
    px1, py1 = add(kx1, ox1, rx1), add(ky1, oy1, ry1)
    qx, qy = swap(px1, "col"), swap(py1, "row")
    w_pair = add(kept, got)
    first = z_first()
    got_w = z_swap(jnp.where(first, w_pair[1], w_pair[0]), 1)
    slope = QUERY_CONST / math.sqrt(HEAD_DIM) * jax.nn.sigmoid(query_scale)
    grad_query_scale = jnp.sum(gscale, axis=(0, 2)) * slope
    scale_grad = jnp.pad(grad_query_scale, (0, feat - HEAD_DIM)).reshape(1, feat)
    es = call(
        project_back_kernel,
        "project_back",
        (at, after(grad_proj, w_pair, px1, py1).reshape(3 * hr, t), w_full, inputs, x01, x10, x11, gain_one, vectors, scale_grad),
        [SMEM] + [VM] * 9,
        shape((4, tok + 16, feat), BF),
    )
    qx, qy, got_w, w_pair, es = together((qx, qy, got_w, w_pair, es))

    mine_w = add(jnp.where(first, w_pair[0], w_pair[1]), got_w)
    met_w = z_swap(mine_w, 3)
    fx, fy = add(kx0, ox0, rx0, qx), add(ky0, oy0, ry0, qy)
    got_c = z_swap(jnp.where(first, fy, fx), 1)
    es = all_four(after(es, fx, fy, mine_w))
    met_w, mine_w, got_c, fx, fy, es, post = together((met_w, mine_w, got_c, fx, fy, es, post))

    mine_w = add(mine_w, met_w)
    other_w = z_swap(mine_w, 1)
    w_own, w_theirs = jnp.where(first, mine_w, other_w), jnp.where(first, other_w, mine_w)
    mine_c = add(jnp.where(first, fx, fy), got_c)
    met_c = z_swap(mine_c, 3)
    post = swap(post, "col")
    w_theirs = swap(w_theirs, "col")
    total = jnp.sum(es[:, tok + 2 : tok + 11].astype(F32), axis=0)
    total = total + swap(total, "core")
    total = total + z_swap(total, 1)
    total = total + z_swap(total, 3)
    met_c, mine_c, w_own, w_theirs, post, total = together((met_c, mine_c, w_own, w_theirs, post, total))
    mine_c = add(mine_c, met_c)
    other_c = z_swap(mine_c, 1)
    w_args = (at, w_own, w_theirs, swap(w_own, "core"), swap(w_theirs, "core"))
    sum_qkv = call(
        finish_qkv_kernel,
        "finish_qkv",
        w_args,
        [SMEM] + [VM] * 4,
        shape((3, feat, 2 * hr), F32),
        scratch=[pltpu.VMEM((2 * hr, feat), F32)],
    )
    sum_qkv = jnp.transpose(sum_qkv, (1, 0, 2))

    e = jnp.sum(es[:, :tok].astype(F32), axis=0)
    inner = jnp.sum(es[:, tok : tok + 2, :tok].astype(F32), axis=(0, 1)).reshape(tok, 1)
    grad_middle = jnp.concatenate(flip([gm_own, post[1].astype(F32)], "col"), axis=0)
    grad_inputs = grad_middle + scale_own * (e * gain_attn) - inputs.astype(F32) * (scale_own**3 * inner / D)
    layer_out = jnp.concatenate(flip([out_own, post[0]], "col"), axis=0)

    pick = lambda n, place: lax.dynamic_index_in_dim(total, 2 * n + place, 0, keepdims=False)
    mine_c = after(mine_c, sum_qkv, grad_inputs, layer_out, total)
    fx, fy = jnp.where(first, mine_c, other_c), jnp.where(first, other_c, mine_c)
    sum_out, sum_up, sum_down = call(
        finish_feed_kernel,
        "finish_feed",
        (at, fx, fy, swap(fx, "core"), swap(fy, "core")),
        [SMEM] + [VM] * 4,
        [shape((feat, feat), F32)] * 3,
    )

    return (
        layer_out,
        grad_inputs,
        pick(0, c),
        sum_qkv,
        total[8, :HEAD_DIM],
        sum_out,
        pick(1, c),
        sum_up,
        pick(3, r),
        sum_down,
        pick(2, c),
    )


def solution(mesh):
    dp, rows, cols = mesh.shape["dp"], mesh.shape["row"], mesh.shape["col"]
    split = Mesh(mesh.devices.reshape(dp // 2, 2, rows, cols), ("z", "core", "row", "col"))
    tokens = P(("z", "core", "row"), "col")
    in_specs = (
        tokens,
        P("col"),
        P("col", None, "row"),
        P(),
        P("row", "col"),
        P("col"),
        P("col", "row"),
        P("row"),
        P("row", "col"),
        P("col"),
        P(("z", "core")),
        P(("z", "core")),
        tokens,
    )
    out_specs = (
        tokens,
        tokens,
        P("col"),
        P("col", None, "row"),
        P(),
        P("row", "col"),
        P("col"),
        P("col", "row"),
        P("row"),
        P("row", "col"),
        P("col"),
    )
    body = body_four if (dp, rows, cols) == (8, 2, 2) else body_any
    return jax.shard_map(body, mesh=split, in_specs=in_specs, out_specs=out_specs, check_vma=False)
```

```python
import functools
import math

import jax
import jax.numpy as jnp
from jax import lax
from jax.experimental import pallas as pl
from jax.experimental.pallas import tpu as pltpu
from jax.sharding import Mesh
from jax.sharding import PartitionSpec as P

D = 1280
HEAD_DIM = 80
EPS = 1e-06
QUERY_CONST = 1.442695041
MASKED = -1e30
BF = jnp.bfloat16
F32 = jnp.float32
VMEM_LIMIT = 60 * 1024 * 1024
CHUNK = 1024
VMEM_LARGE = 60 * 1024 * 1024
CHEAP = pl.CostEstimate(flops=1, bytes_accessed=1, transcendentals=0)


def size(axis):
    return lax.axis_size(axis)


def swap(x, axis):
    return lax.ppermute(x, axis, [(0, 1), (1, 0)])


def flip(blocks, axis):
    if size(axis) != 2:
        return list(blocks)
    first = lax.axis_index(axis) == 0
    a, b = blocks
    return [jnp.where(first, a, b), jnp.where(first, b, a)]


def flip_dim(x, axis, dim):
    if size(axis) != 2:
        return x
    return jnp.concatenate(flip(jnp.split(x, 2, axis=dim), axis), axis=dim)


def gather(x, axis):
    if size(axis) == 2:
        return [x, swap(x, axis)]
    whole = lax.all_gather(x, axis, axis=0, tiled=False)
    return [whole[i] for i in range(size(axis))]


def gather_grid(x):
    if size("row") != 2:
        return [gather(b, "col") for b in gather(x, "row")]
    along_row, along_col = swap(x, "row"), swap(x, "col")
    half = x.shape[0] // 2
    across = jnp.concatenate(
        [swap(along_row[:half], "col"), swap(along_col[half:], "row")], axis=0
    )
    return [[x, along_col], [along_row, across]]


def scatter_sum(x, axis, dim):
    if size(axis) != 2:
        return lax.psum_scatter(x, axis, scatter_dimension=dim, tiled=True)
    mine, theirs = jnp.split(x, 2, axis=dim)
    return (mine.astype(F32) + swap(theirs, axis).astype(F32)).astype(x.dtype)


def exchange(x, axis, split, join):
    if size(axis) != 2:
        return lax.all_to_all(x, axis, split, join, tiled=True)
    mine, theirs = jnp.split(x, 2, axis=split)
    return jnp.concatenate([mine, swap(theirs, axis)], axis=join)


def core_half(x, dim):
    return lax.dynamic_slice_in_dim(
        x, lax.axis_index("core") * (x.shape[dim] // 2), x.shape[dim] // 2, dim
    )


def weight_gather(w, row_dim):
    part = core_half(w, 0)
    blocks = gather_grid(part)
    if row_dim == 1:
        blocks = [list(b) for b in zip(*blocks)]
    mine = jnp.stack([jnp.concatenate(b, axis=1) for b in blocks])
    other = swap(mine, "core")
    first = lax.axis_index("core") == 0
    both = jnp.stack([jnp.where(first, mine, other), jnp.where(first, other, mine)], axis=1)
    return both.reshape(-1, both.shape[-1])


def weight_sum(g, row_dim):
    dim_axis = ("row", "col") if row_dim == 0 else ("col", "row")
    n0 = size(dim_axis[0])
    g = g.reshape(n0, 2, g.shape[0] // n0 // 2, g.shape[1])
    core = lax.axis_index("core")
    keep = lax.dynamic_index_in_dim(g, core, 1, keepdims=False)
    give = lax.dynamic_index_in_dim(g, 1 - core, 1, keepdims=False).astype(BF)
    part = (keep + swap(give, "core").astype(F32)).astype(BF)
    part = scatter_sum(part, dim_axis[0], 0)
    part = scatter_sum(part[0], dim_axis[1], 1)
    return z_sum(part)


def z_sum(part):
    total = lax.psum(part, "z")
    other = swap(total, "core")
    return flip_core(total, other)


def flip_core(total, other):
    first = lax.axis_index("core") == 0
    return jnp.concatenate(
        [jnp.where(first, total, other), jnp.where(first, other, total)], axis=-2
    ).astype(F32)


def dot(a, b, contract):
    return lax.dot_general(a, b, ((contract[0:1], contract[1:2]), ((), ())), preferred_element_type=F32)


def bias_block(series_row, series_col, key_pos, q0, k0, qb, kb, diagonal):
    q_pos = q0 + lax.broadcasted_iota(jnp.int32, (1, qb), 1)
    allowed = (series_col == series_row) & (key_pos <= q_pos)
    if diagonal:
        k_pos = k0 + lax.broadcasted_iota(jnp.int32, (kb, 1), 0)
        allowed = allowed | (k_pos == q_pos)
    return jnp.where(allowed, 0.0, MASKED)


def forward_kernel(block, at, qkv_ref, srow_ref, scol_ref, kpos_ref, out_ref, lse_ref, *rest):
    *pieces, bias_ref, krow_ref, s_ref = rest
    t = qkv_ref.shape[3]
    n = t // block
    krow_ref[...] = qkv_ref[1, 0].astype(F32).T.astype(BF)

    def bias_slot(j, i):
        return j * (j + 1) // 2 + i

    @pl.when(pl.program_id(0) == 0)
    def _():
        for j in range(n):
            for i in range(j + 1):
                keys = pl.ds(i * block, block)
                bias_ref[bias_slot(j, i)] = bias_block(
                    srow_ref[:, j * block : (j + 1) * block],
                    scol_ref[keys, :],
                    kpos_ref[keys, :],
                    j * block,
                    i * block,
                    block,
                    block,
                    i == j,
                )

    for j in range(n):
        cols = slice(j * block, (j + 1) * block)
        q = qkv_ref[0, 0, :, cols]
        top = None
        for i in range(j + 1):
            s = dot(krow_ref[i * block : (i + 1) * block, :], q, (1, 0)) + bias_ref[bias_slot(j, i)]
            s_ref[i * block : (i + 1) * block, :] = s
            here = jnp.max(s, axis=0, keepdims=True)
            top = here if top is None else jnp.maximum(top, here)
        total = jnp.zeros((1, block), F32)
        acc = jnp.zeros((HEAD_DIM, block), F32)
        for i in range(j + 1):
            p = jnp.exp(s_ref[i * block : (i + 1) * block, :] - top)
            total += jnp.sum(p, axis=0, keepdims=True)
            acc += dot(qkv_ref[2, 0, :, i * block : (i + 1) * block], p.astype(BF), (1, 0))
        found = (acc / total).astype(BF)
        out_ref[0, :, cols] = found
        if pieces:
            pieces[0][j, 0] = found
        lse_ref[0, :, cols] = top + jnp.log(total)


def backward_kernel(
    block, at, qkv_ref, raw_ref, factor_ref, out_ref, lse_ref, srow_ref, scol_ref, kpos_ref, *rest
):
    piece, grad_ref, gscale_ref, bias_ref, krow_ref, vrow_ref, gk_ref, gv_ref, gout_ref = rest
    wide = piece.shape[3]
    for j in range(piece.shape[0]):
        gout_ref[:, j * wide : (j + 1) * wide] = piece[j, 0]
    t = qkv_ref.shape[3]
    n = t // block
    krow_ref[...] = qkv_ref[1, 0].astype(F32).T.astype(BF)
    vrow_ref[...] = qkv_ref[2, 0].astype(F32).T.astype(BF)

    def bias_slot(j, i):
        return j * (j + 1) // 2 + i

    @pl.when(pl.program_id(0) == 0)
    def _():
        for j in range(n):
            for i in range(j + 1):
                keys = pl.ds(i * block, block)
                bias_ref[bias_slot(j, i)] = bias_block(
                    srow_ref[:, j * block : (j + 1) * block],
                    scol_ref[keys, :],
                    kpos_ref[keys, :],
                    j * block,
                    i * block,
                    block,
                    block,
                    i == j,
                )

    gscale = jnp.zeros((HEAD_DIM, 1), F32)
    for j in range(n):
        cols = slice(j * block, (j + 1) * block)
        q = qkv_ref[0, 0, :, cols]
        go = gout_ref[:, cols]
        lse = lse_ref[0, :, cols]
        delta = jnp.sum(go.astype(F32) * out_ref[0, :, cols].astype(F32), axis=0, keepdims=True)
        gq = jnp.zeros((HEAD_DIM, block), F32)
        step = max(1, CHUNK // block)
        for i in range(0, j + 1, step):
            many = min(step, j + 1 - i)
            keys = slice(i * block, (i + many) * block)
            slot = bias_slot(j, i)
            bias = bias_ref[slot : slot + many].reshape(many * block, block)
            p = jnp.exp(dot(krow_ref[keys, :], q, (1, 0)) + bias - lse)
            gp = dot(vrow_ref[keys, :], go, (1, 0))
            gs = (p * (gp - delta)).astype(BF)
            gq += dot(qkv_ref[1, 0, :, keys], gs, (1, 0))
            gk = dot(q, gs, (1, 1))
            gv = dot(go, p.astype(BF), (1, 1))
            before, last = slice(i * block, min(i + many, j) * block), slice(j * block, (j + 1) * block)
            old = (min(i + many, j) - i) * block
            if old:
                gk_ref[:, before] += gk[:, :old]
                gv_ref[:, before] += gv[:, :old]
            if i + many == j + 1:
                gk_ref[:, last] = gk[:, old:]
                gv_ref[:, last] = gv[:, old:]
        gscale += jnp.sum(gq * raw_ref[0, :, cols], axis=1, keepdims=True)
        grad_ref[0, 0, :, cols] = (gq * factor_ref[...]).astype(BF)
    grad_ref[1, 0] = gk_ref[...].astype(BF)
    grad_ref[2, 0] = gv_ref[...].astype(BF)
    gscale_ref[0] = gscale


def mask_args(series, padding):
    t = series.shape[0]
    pos = jnp.arange(t, dtype=jnp.int32)
    return series.reshape(1, t), series.reshape(t, 1), jnp.where(padding == 0, pos, t).reshape(t, 1)


def attention_forward(at, qkv, masks, pieces=0):
    _, heads, hd, t = qkv.shape
    block = min(256, t) if t <= 2048 else 512
    n = t // block
    whole = lambda shape: pl.BlockSpec(shape, lambda h: (0,) * len(shape))
    return pl.pallas_call(
        functools.partial(forward_kernel, block),
        grid=(heads,),
        in_specs=[
            pl.BlockSpec(memory_space=pltpu.SMEM),
            pl.BlockSpec((3, 1, hd, t), lambda h: (0, h, 0, 0)),
            whole((1, t)),
            whole((t, 1)),
            whole((t, 1)),
        ],
        out_specs=[
            pl.BlockSpec((1, hd, t), lambda h: (h, 0, 0)),
            pl.BlockSpec((1, 1, t), lambda h: (h, 0, 0)),
        ]
        + [pl.BlockSpec((n, 1, hd, block), lambda h: (0, h, 0, 0))] * pieces,
        out_shape=[
            jax.ShapeDtypeStruct((heads, hd, t), BF),
            jax.ShapeDtypeStruct((heads, 1, t), F32),
        ]
        + [jax.ShapeDtypeStruct((n, heads, hd, block), BF)] * pieces,
        scratch_shapes=[
            pltpu.VMEM((n * (n + 1) // 2, block, block), F32),
            pltpu.VMEM((t, hd), BF),
            pltpu.VMEM((t, block), F32),
        ],
        compiler_params=pltpu.CompilerParams(vmem_limit_bytes=VMEM_LARGE),
        cost_estimate=CHEAP,
        name="attention_forward",
    )(at, qkv, *masks)


def attention_backward(at, qkv, raw, factor, out, piece, lse, masks):
    _, heads, hd, t = qkv.shape
    block = min(256, t) if t <= 2048 else 512
    n = t // block
    whole = lambda shape: pl.BlockSpec(shape, lambda h: (0,) * len(shape))
    head = lambda wide=t: pl.BlockSpec((1, hd, wide), lambda h: (h, 0, 0))
    return pl.pallas_call(
        functools.partial(backward_kernel, block),
        grid=(heads,),
        in_specs=[
            pl.BlockSpec(memory_space=pltpu.SMEM),
            pl.BlockSpec((3, 1, hd, t), lambda h: (0, h, 0, 0)),
            head(),
            whole((hd, 1)),
            head(),
            pl.BlockSpec((1, 1, t), lambda h: (h, 0, 0)),
            whole((1, t)),
            whole((t, 1)),
            whole((t, 1)),
        ]
        + [pl.BlockSpec((piece.shape[0], 1, hd, piece.shape[3]), lambda h: (0, h, 0, 0))],
        out_specs=[
            pl.BlockSpec((3, 1, hd, t), lambda h: (0, h, 0, 0)),
            pl.BlockSpec((1, hd, 1), lambda h: (h, 0, 0)),
        ],
        out_shape=[
            jax.ShapeDtypeStruct((3, heads, hd, t), BF),
            jax.ShapeDtypeStruct((heads, hd, 1), F32),
        ],
        scratch_shapes=[
            pltpu.VMEM((n * (n + 1) // 2, block, block), F32),
            pltpu.VMEM((t, hd), BF),
            pltpu.VMEM((t, hd), BF),
            pltpu.VMEM((hd, t), F32),
            pltpu.VMEM((hd, t), F32),
            pltpu.VMEM((hd, t), BF),
        ],
        compiler_params=pltpu.CompilerParams(vmem_limit_bytes=VMEM_LARGE),
        cost_estimate=CHEAP,
        name="attention_backward",
    )(at, qkv, raw, factor, out, lse, *masks, piece)


def norm_scale(x):
    return lax.rsqrt(jnp.mean(x * x, axis=1, keepdims=True) + EPS)


def body_any(
    inputs, gain_attn, w_qkv, query_scale, w_out, gain_mlp, w_up, b_up, w_down, b_down, series_ids, pad_mask, cotangent
):
    rows, cols = size("row"), size("col")
    tok = inputs.shape[0]
    feat = inputs.shape[1]
    share = tok // cols
    t = series_ids.shape[0]
    head_rows = w_qkv.shape[2] // cols
    heads = head_rows // HEAD_DIM
    r, c = lax.axis_index("row"), lax.axis_index("col")

    blocks = gather_grid(inputs)
    strips = [jnp.concatenate(b, axis=1) for b in blocks]
    x_own = strips[0] if rows == 2 else lax.dynamic_index_in_dim(jnp.stack(strips), r, 0, keepdims=False)
    x_all = jnp.concatenate(flip(strips, "row"), axis=0)
    gain_one = jnp.concatenate(gather(gain_attn, "col"))
    gain_two = jnp.concatenate(gather(gain_mlp, "col"))
    bias_up = jnp.concatenate(gather(b_up, "row")).astype(F32)
    bias_down = jnp.concatenate(gather(b_down, "col")).astype(F32)

    w3 = jnp.transpose(w_qkv, (1, 0, 2)).reshape(3, feat, cols, head_rows)
    w_mine = lax.dynamic_index_in_dim(w3, c, 2, keepdims=False)
    w_give = lax.dynamic_index_in_dim(w3, 1 - c, 2, keepdims=False)
    w_half = swap(core_half(w_give, 1), "col")
    w_other = swap(w_half, "core")
    first = lax.axis_index("core") == 0
    w_full = jnp.concatenate(
        [w_mine, jnp.where(first, w_half, w_other), jnp.where(first, w_other, w_half)], axis=1
    )

    xf = x_all.astype(F32)
    scale_one = norm_scale(xf)
    normed_one = (xf * scale_one * gain_one).astype(BF)
    projected = jnp.einsum("td,sdh->sht", normed_one, w_full, preferred_element_type=F32)
    projected = projected.reshape(3, heads, HEAD_DIM, t)
    factor = QUERY_CONST / math.sqrt(HEAD_DIM) * jax.nn.softplus(query_scale)
    raw_q = projected[0]
    qkv = jnp.stack([raw_q * factor[None, :, None], projected[1], projected[2]]).astype(BF)
    masks = mask_args(series_ids, pad_mask)
    at = jnp.zeros((4,), jnp.int32)
    attended, lse = attention_forward(at, qkv, masks)

    def to_tokens(y):
        y = flip_dim(y.reshape(head_rows, rows, cols, share), "row", 1)
        y = flip_dim(y, "col", 2)
        y = exchange(y.reshape(1, head_rows, rows, cols, share), "row", 2, 0)
        y = exchange(y.reshape(rows, 1, head_rows, cols, share), "col", 3, 1)
        y = flip_dim(y.reshape(rows, cols, head_rows, share), "col", 1)
        return y.reshape(rows * cols * head_rows, share)

    def to_heads(y):
        y = flip_dim(y.reshape(rows, cols, head_rows, share), "col", 1)
        y = exchange(y.reshape(rows, cols, head_rows, 1, share), "col", 1, 3)
        y = exchange(y.reshape(rows, head_rows, 1, cols, share), "row", 0, 2)
        y = flip_dim(y.reshape(head_rows, rows, cols, share), "col", 2)
        return flip_dim(y, "row", 1).reshape(head_rows, t)

    w_out_all = weight_gather(w_out, 0)
    w_up_all = weight_gather(w_up, 1)
    w_down_all = weight_gather(w_down, 0)

    def my_share(y):
        return lax.dynamic_slice_in_dim(y, c * share, share, 0)

    att = to_tokens(attended.reshape(head_rows, t))
    x_mine = my_share(x_own).astype(F32)
    middle = x_mine + dot(att, w_out_all, (0, 0))
    scale_two = norm_scale(middle)
    normed_two = (middle * scale_two * gain_two).astype(BF)
    pre_act = dot(normed_two, w_up_all, (1, 0)) + bias_up
    sig = jax.nn.sigmoid(pre_act)
    hidden = (pre_act * sig).astype(BF)
    result = (middle + dot(hidden, w_down_all, (1, 0)) + bias_down).astype(BF)

    def to_block(y):
        mine, theirs = jnp.split(y, 2, axis=1)
        return jnp.concatenate(flip([mine, swap(theirs, "col")], "col"), axis=0)

    layer_out = to_block(result)

    g_give = lax.dynamic_slice_in_dim(cotangent, (1 - c) * share, share, 0)
    g = jnp.concatenate([my_share(cotangent), swap(g_give, "col")], axis=1)
    grad_w_down = dot(hidden, g, (0, 0))
    grad_hidden = dot(g, w_down_all, (1, 1))
    grad_pre_f = grad_hidden * sig * (1.0 + pre_act * (1.0 - sig))
    grad_pre = grad_pre_f.astype(BF)
    grad_b_up = jnp.sum(grad_pre.astype(F32), axis=0)
    grad_w_up = dot(normed_two, grad_pre, (0, 0))
    grad_normed_two = dot(grad_pre, w_up_all, (1, 1))
    weighted = grad_normed_two * gain_two
    inner = jnp.sum(weighted * middle, axis=1, keepdims=True)
    grad_middle = g.astype(F32) + scale_two * weighted - middle * (scale_two**3 * inner / D)
    grad_gain_mlp = jnp.sum(grad_normed_two * middle * scale_two, axis=0)
    grad_branch = grad_middle.astype(BF)
    grad_w_out = dot(att, grad_branch, (1, 0))
    grad_att = dot(w_out_all, grad_branch, (1, 1)).astype(BF)
    grad_attended = to_heads(grad_att).reshape(heads, HEAD_DIM, t)
    grad_middle_block = to_block(grad_middle)

    sum_down = weight_sum(grad_w_down, 0)
    sum_up = weight_sum(grad_w_up, 1)
    sum_out = weight_sum(grad_w_out, 0)

    grad_proj, gscale = attention_backward(
        at, qkv, raw_q, factor.reshape(HEAD_DIM, 1), attended, grad_attended[None], lse, masks
    )
    slope = QUERY_CONST / math.sqrt(HEAD_DIM) * jax.nn.sigmoid(query_scale)
    grad_query_scale = jnp.sum(gscale, axis=(0, 2)) * slope
    grad_proj = grad_proj.reshape(3, head_rows, t)
    grad_normed_one = jnp.einsum("sht,sdh->td", grad_proj, w_full, preferred_element_type=F32)
    weighted_one = grad_normed_one * gain_one
    inner_one = jnp.sum(weighted_one * xf, axis=1)
    grad_gain_attn = jnp.sum(grad_normed_one * xf * scale_one, axis=0)
    inner_one = lax.psum(inner_one, ("row", "col"))
    grad_w = jnp.einsum("td,sht->sdh", normed_one, grad_proj, preferred_element_type=F32)
    grad_w = grad_w.reshape(3, cols, 2, feat // 2, head_rows)
    core = lax.axis_index("core")
    keep = lax.dynamic_index_in_dim(grad_w, core, 2, keepdims=False)
    give = lax.dynamic_index_in_dim(grad_w, 1 - core, 2, keepdims=False).astype(BF)
    part = (keep + swap(give, "core").astype(F32)).astype(BF)
    part = jnp.concatenate(flip([part[:, 0], swap(part[:, 1], "col")], "col"), axis=2)
    sum_qkv = jnp.transpose(z_sum(part), (1, 0, 2))

    e = jnp.concatenate(flip(jnp.split(grad_normed_one.astype(BF), 2, axis=0), "row"), axis=0) if rows == 2 else (
        grad_normed_one.astype(BF)
    )
    e = scatter_sum(e, "row", 0)
    e = scatter_sum(e, "col", 1).astype(F32)
    my_rows = lambda y: lax.dynamic_slice_in_dim(y, r * tok, tok, 0)
    scale_mine = my_rows(scale_one)
    inner_mine = my_rows(inner_one.reshape(t, 1))
    grad_inputs = grad_middle_block + scale_mine * (e * gain_attn) - inputs.astype(F32) * (
        scale_mine**3 * inner_mine / D
    )

    grad_b_down = jnp.sum(g.astype(F32), axis=0)
    vectors = jnp.concatenate(
        [
            flip_dim(grad_gain_attn, "col", 0),
            flip_dim(grad_gain_mlp, "col", 0),
            flip_dim(grad_b_down, "col", 0),
            flip_dim(grad_b_up, "row", 0),
            grad_query_scale,
        ]
    )
    vectors = lax.psum(vectors, ("z", "core", "row", "col"))
    mine_col = lambda at: lax.dynamic_slice_in_dim(vectors, at * D + c * feat, feat, 0)
    units = b_up.shape[0]
    return (
        layer_out,
        grad_inputs,
        mine_col(0),
        sum_qkv,
        vectors[4 * D :],
        sum_out,
        mine_col(1),
        sum_up,
        lax.dynamic_slice_in_dim(vectors, 3 * D + r * units, units, 0),
        sum_down,
        mine_col(2),
    )


SMEM = pl.BlockSpec(memory_space=pltpu.SMEM)
ANY = pl.BlockSpec(memory_space=pl.ANY)


def call(kernel, name, args, specs, outs, scratch=(), limit=VMEM_LIMIT, out_specs=None):
    more = {} if out_specs is None else {"out_specs": out_specs}
    return pl.pallas_call(
        kernel,
        in_specs=specs,
        **more,
        out_shape=outs,
        scratch_shapes=list(scratch),
        compiler_params=pltpu.CompilerParams(vmem_limit_bytes=limit),
        cost_estimate=CHEAP,
        name=name,
    )(*args)


VM = pl.BlockSpec(memory_space=pltpu.VMEM)
HBM = pl.BlockSpec(memory_space=pltpu.HBM)


def shape(dims, kind):
    return jax.ShapeDtypeStruct(dims, kind)


def project_kernel(
    at, x00, x01, x10, x11, gain, factor, w_mine, w_a, w_b, qkv, raw, normed, scale_own, w_full
):
    r, k = at[0], at[2]
    tok, feat = x00.shape
    hr = w_mine.shape[1]
    half = hr // 2
    for s in range(3):
        w_full[pl.ds(s * hr, hr), 0:feat] = w_mine[s]
        w_full[pl.ds(pl.multiple_of(s * hr + k * half, 16), half), feat:] = w_a[s]
        w_full[pl.ds(pl.multiple_of(s * hr + (1 - k) * half, 16), half), feat:] = w_b[s]
    for i, (a_ref, b_ref) in enumerate(((x00, x01), (x10, x11))):
        a, b = a_ref[...].astype(F32), b_ref[...].astype(F32)
        total = jnp.sum(a * a, axis=1, keepdims=True) + jnp.sum(b * b, axis=1, keepdims=True)
        scale = lax.rsqrt(total / (2 * feat) + EPS)
        if i == 0:
            scale_own[...] = scale
        rows = pl.ds(pl.multiple_of((r ^ i) * tok, tok), tok)
        normed[rows, 0:feat] = (a * scale * gain[:, 0:feat]).astype(BF)
        normed[rows, feat:] = (b * scale * gain[:, feat:]).astype(BF)
        y = normed[rows, :]
        q = dot(w_full[0:hr, :], y, (1, 1))
        raw[:, rows] = q
        qkv[0, :, rows] = (q * factor[...]).astype(BF)
        qkv[1, :, rows] = dot(w_full[hr : 2 * hr, :], y, (1, 1)).astype(BF)
        qkv[2, :, rows] = dot(w_full[2 * hr : 3 * hr, :], y, (1, 1)).astype(BF)


def feed_kernel(
    at, gain, bias_up, bias_down, a, x_own, x_col, g_own, g_col,
    w_out, w_up, w_down, hx, hy, d0, d1, hx2, hy2, d02, d12,
    out_own, gm_own, post, ts, vectors, att, hidden_out, normed_out, g_out, pre_out, branch_out,
    w, x_ref, sems, more_sems,
):
    r, c, k = at[0], at[1], at[2]
    _, hr, share = a.shape
    feat = x_own.shape[1]
    half = feat // 2
    first = d0.shape[1]
    rows = pl.ds(pl.multiple_of(c * share, share), share)

    def start(pairs, sem):
        copies = [pltpu.make_async_copy(src, dst, sem.at[m]) for m, (src, dst) in enumerate(pairs)]
        for copy in copies:
            copy.start()
        return copies

    def place(s):
        return pl.ds(pl.multiple_of(((s // 2) ^ r) * 2 * hr + (s % 2) * hr, 16), hr)

    small = [(a.at[s], att.at[place(s), :]) for s in range(4)]
    small += [(x_own.at[rows, :], x_ref.at[:, 0:feat]), (x_col.at[rows, :], x_ref.at[:, feat:])]
    small += [(g_own.at[rows, :], g_out.at[:, 0:feat]), (g_col, g_out.at[:, feat:])]
    small = start(small, more_sems)
    copies = []
    for n, shard in enumerate((w_out, w_up, w_down)):
        rx, cx, ry, cy = (0, feat, feat, 0) if n == 1 else (feat, 0, 0, feat)
        mine = [(shard, w.at[n, 0:feat, 0:feat])]
        for core, (px, py, p0, p1) in ((k, (hx, hy, d0, d1)), (1 - k, (hx2, hy2, d02, d12))):
            down = core * half
            at_x = pl.ds(pl.multiple_of(rx + down, 16), half)
            at_y = pl.ds(pl.multiple_of(ry + down, 16), half)
            at_0 = pl.ds(pl.multiple_of(feat + down, 16), first)
            at_1 = pl.ds(pl.multiple_of(feat + down + first, 16), half - first)
            mine.append((px.at[n], w.at[n, at_x, cx : cx + feat]))
            mine.append((py.at[n], w.at[n, at_y, cy : cy + feat]))
            mine.append((p0.at[n], w.at[n, at_0, feat : 2 * feat]))
            mine.append((p1.at[n], w.at[n, at_1, feat : 2 * feat]))
        copies.append(start(mine, sems.at[n]))

    for copy in small + copies[0]:
        copy.wait()
    middle = x_ref[...].astype(F32) + dot(att[...], w[0], (0, 0))
    scale = lax.rsqrt(jnp.sum(middle * middle, axis=1, keepdims=True) / D + EPS)
    normed = (middle * scale * gain[...]).astype(BF)
    normed_out[...] = normed
    for copy in copies[1]:
        copy.wait()
    pre = dot(normed, w[1], (1, 0)) + bias_up[...]
    sig = jax.nn.sigmoid(pre)
    hidden = (pre * sig).astype(BF)
    hidden_out[...] = hidden
    for copy in copies[2]:
        copy.wait()
    result = (middle + dot(hidden, w[2], (1, 0)) + bias_down[...]).astype(BF)
    out_own[...] = result[:, :feat]
    post[0] = result[:, feat:]

    grad_pre_f = dot(g_out[...], w[2], (1, 1)) * sig * (1.0 + pre * (1.0 - sig))
    grad_pre = grad_pre_f.astype(BF)
    pre_out[...] = grad_pre
    grad_normed = dot(grad_pre, w[1], (1, 1))
    weighted = grad_normed * gain[...]
    inner = jnp.sum(weighted * middle, axis=1, keepdims=True)
    gf = g_out[...].astype(F32)
    grad_middle = gf + scale * weighted - middle * (scale * scale * scale * inner / D)
    gm_own[...] = grad_middle[:, :feat]
    post[1] = grad_middle[:, feat:].astype(BF)
    branch = grad_middle.astype(BF)
    branch_out[...] = branch
    for s in range(4):
        ts[s] = dot(w[0, place(s), :], branch, (1, 1)).astype(BF)
    vectors[...] = jnp.concatenate(
        [
            jnp.sum(grad_normed * (middle * scale), axis=0, keepdims=True),
            jnp.sum(gf, axis=0, keepdims=True),
            jnp.sum(grad_pre.astype(F32), axis=0, keepdims=True),
        ],
        axis=0,
    )


def feed_weights_kernel(at, att, hidden, normed, g, grad_pre, branch, *rest):
    *grads, stage, turned, sems = rest
    k = at[2]
    feat = g.shape[1] // 2
    half = feat // 2
    quarter = half // 2
    copies = []

    def weight_grad(n, left_ref, right):
        for core, begin in ((k, 0), (1 - k, 8)):
            up, low = (begin + 4, begin) if n == 1 else (begin, begin + 4)
            for b in range(2):
                part = pl.ds(pl.multiple_of(b * feat + core * half, 16), half)
                y = dot(left_ref[part, :], right, (1, 0)).astype(BF)
                for j in range(2):
                    cut = slice(j * feat, (j + 1) * feat)
                    for to, value in ((up + 2 * j + (1 - b), y[:quarter, cut]), (low + 2 * b + (1 - j), y[quarter:, cut])):
                        stage[to, n] = value
                        copy = pltpu.make_async_copy(stage.at[to, n], grads[to].at[n], sems.at[to, n])
                        copy.start()
                        copies.append(copy)

    turned[0] = hidden[...].astype(F32).T.astype(BF)
    weight_grad(2, turned.at[0], g[...])
    turned[1] = normed[...].astype(F32).T.astype(BF)
    weight_grad(1, turned.at[1], grad_pre[...])
    weight_grad(0, att, branch[...])
    for copy in copies:
        copy.wait()


def weight_back_kernel(at, grad, normed, keep, give):
    k = at[2]
    part = keep.shape[2]
    feat = keep.shape[3]
    for ref, core in ((give, 1 - k), (keep, k)):
        for s in range(3):
            rows = pl.ds(pl.multiple_of(core * part, 16), part)
            y = dot(grad[s, rows, :], normed[...], (1, 0)).astype(BF)
            ref[0, s] = y[:, :feat]
            ref[1, s] = y[:, feat:]


def project_back_kernel(
    at, grad, w_full, x00, x01, x10, x11, gain, vectors, scale_grad, es
):
    r, c = at[0], at[1]
    tok, feat = x00.shape
    sums = [jnp.zeros((1, feat), F32), jnp.zeros((1, feat), F32)]
    inners = []
    for i, xs in enumerate(((x00, x01), (x10, x11))):
        rows = pl.ds(pl.multiple_of((r ^ i) * tok, tok), tok)
        left = grad[:, rows]
        products, squares, inner = [], 0.0, 0.0
        for j in range(2):
            cut = slice(j * feat, (j + 1) * feat)
            e = dot(left, w_full[:, cut], (0, 0))
            x = xs[j][...].astype(F32)
            product = e * x
            inner = inner + jnp.sum(product * gain[:, cut], axis=1, keepdims=True)
            squares = squares + jnp.sum(x * x, axis=1, keepdims=True)
            es[2 * (r ^ i) + (c ^ j), 0:tok, :] = e.astype(BF)
            products.append(product)
        scale = lax.rsqrt(squares / (2 * feat) + EPS)
        for j in range(2):
            sums[j] += jnp.sum(products[j] * scale, axis=0, keepdims=True)
        line = jnp.broadcast_to(inner, (tok, 128)).T[0:1, :]
        high = line.astype(BF).astype(F32)
        inners.append(jnp.concatenate([high, line - high], axis=0))
    rows = []
    pairs = [(sums[0], sums[1], c)]
    pairs += [(vectors[n : n + 1, :feat], vectors[n : n + 1, feat:], (c, c, r)[n]) for n in range(3)]
    for own, other, place in pairs:
        rows += [jnp.where(place == 0, own, other), jnp.where(place == 0, other, own)]
    rows = jnp.concatenate(rows + [scale_grad[...], jnp.zeros((5, feat), F32)], axis=0)
    for i in range(2):
        inner = jnp.concatenate([inners[i], jnp.zeros((2, feat - tok), F32)], axis=1)
        extra = jnp.concatenate([inner, rows], axis=0).astype(BF)
        for j in range(2):
            es[2 * (r ^ i) + (c ^ j), tok:, :] = extra


def finish_qkv_kernel(at, mine, theirs, mine2, theirs2, out, rows):
    c, k = at[1], at[2]
    half = mine.shape[1]
    for s in range(3):
        for ref, col, core in ((mine, c, k), (theirs, 1 - c, k), (mine2, c, 1 - k), (theirs2, 1 - c, 1 - k)):
            rows[pl.ds(pl.multiple_of((2 * col + core) * half, 16), half), :] = ref[s].astype(F32)
        out[s] = rows[...].T


def finish_feed_kernel(at, a, b, a2, b2, *outs):
    k = at[2]
    quarter = a.shape[1]
    for n, out in enumerate(outs):
        upper, lower = ((b, b2), (a, a2)) if n == 1 else ((a, a2), (b, b2))
        for i, core in ((0, k), (1, 1 - k)):
            for j, refs in enumerate((upper, lower)):
                to = pl.multiple_of((2 * core + j) * quarter, 16)
                out[pl.ds(to, quarter), :] = refs[i][n].astype(F32)


together = lax.optimization_barrier


def after(x, *earlier):
    return lax.optimization_barrier((x, *earlier))[0]


def add(*parts):
    total = parts[0].astype(F32)
    for part in parts[1:]:
        total = total + part.astype(F32)
    return total.astype(BF)


def all_four(x):
    return lax.all_to_all(x, ("row", "col"), 0, 0, tiled=True)


def z_swap(x, step):
    n = size("z")
    return lax.ppermute(x, "z", [(i, i ^ step) for i in range(n)])


def z_first():
    z = lax.axis_index("z")
    return (z == 0) | (z == 3)


def body_four(
    inputs, gain_attn, w_qkv, query_scale, w_out, gain_mlp, w_up, b_up, w_down, b_down, series_ids, pad_mask, cotangent
):
    tok, feat = inputs.shape
    share = tok // 2
    t = series_ids.shape[0]
    hr = w_qkv.shape[2] // 2
    heads = hr // HEAD_DIM
    half = feat // 2
    r, c, k = lax.axis_index("row"), lax.axis_index("col"), lax.axis_index("core")
    at = jnp.stack([r, c, k, 2 * r + c]).astype(jnp.int32)
    mine_rows = lambda y, part: lax.dynamic_slice_in_dim(y, part * share, share, 0)

    few = heads // 2
    quarter = half // 2
    first_rows = (half * 7 // 20) // 16 * 16
    x01 = swap(inputs, "col")
    x10 = swap(inputs, "row")
    small = swap(jnp.concatenate([gain_attn, gain_mlp, b_down.astype(F32)]), "col")
    up_other = swap(b_up.astype(F32), "row")
    w_turned = jnp.transpose(w_qkv, (1, 2, 0)).reshape(3, 2, hr, feat)
    w_mine = lax.dynamic_index_in_dim(w_turned, c, 1, keepdims=False)
    w_give = lax.dynamic_index_in_dim(w_turned, 1 - c, 1, keepdims=False)
    w_half = core_half(w_give, 1)
    w_a = swap(w_half, "col")
    part = jnp.stack([core_half(w_out, 0), core_half(w_up, 0), core_half(w_down, 0)])
    g_give = mine_rows(cotangent, 1 - c)
    x01, x10, small, up_other, part, g_give, w_mine = lax.optimization_barrier(
        (x01, x10, small, up_other, part, g_give, w_mine)
    )
    x11 = swap(after(x01, w_half), "row")
    w_b = swap(w_a, "core")
    gain_one = jnp.concatenate([gain_attn, small[:feat]]).reshape(1, D)
    gain_two = jnp.concatenate([gain_mlp, small[feat : 2 * feat]]).reshape(1, D)
    bias_down = jnp.concatenate([b_down.astype(F32), small[2 * feat :]]).reshape(1, D)
    bias_up = jnp.concatenate([b_up.astype(F32), up_other]).reshape(1, D)
    factor = QUERY_CONST / math.sqrt(HEAD_DIM) * jax.nn.softplus(query_scale)
    factor_col = factor.reshape(HEAD_DIM, 1)

    part = after(part, x11, w_a)
    hx, hy = swap(part, "row"), swap(part, "col")
    hx2, hy2 = swap(hx, "core"), swap(hy, "core")
    qkv, raw, normed_one, scale_own, w_full = call(
        project_kernel,
        "project",
        (at, inputs, x01, x10, x11, gain_one, jnp.tile(factor_col, (heads, 1)), w_mine, w_a, w_b),
        [SMEM] + [VM] * 9,
        [
            shape((3, hr, t), BF),
            shape((hr, t), F32),
            shape((t, D), BF),
            shape((tok, 1), F32),
            shape((3 * hr, D), BF),
        ],
        limit=VMEM_LARGE,
    )
    qkv = qkv.reshape(3, heads, HEAD_DIM, t)
    masks = mask_args(series_ids, pad_mask)
    attended, lse, a = attention_forward(at, qkv, masks, pieces=1)
    a = all_four(a.reshape(4, hr, share))
    hx_on, hy_on, g_give = lax.optimization_barrier((hx, hy, g_give, lse))[:3]
    d0 = swap(hx_on[:, :first_rows], "col")
    d1 = swap(hy_on[:, first_rows:], "row")
    g_col = swap(g_give, "col")
    d0, d1, g_col, a = together((d0, d1, g_col, a))
    d02, d12 = swap(d0, "core"), swap(d1, "core")
    out_own, gm_own, post, ts, vectors, *factors = call(
        feed_kernel,
        "feed_forward",
        (at, gain_two, bias_up, bias_down, a, inputs, x01, cotangent, g_col)
        + (w_out, w_up, w_down, hx, hy, d0, d1, hx2, hy2, d02, d12),
        [SMEM] + [VM] * 3 + [HBM] * 16,
        [
            shape((share, feat), BF),
            shape((share, feat), F32),
            shape((2, share, feat), BF),
            shape((4, hr, share), BF),
            shape((3, D), F32),
            shape((D, share), BF),
        ]
        + [shape((share, D), BF)] * 5,
        scratch=[
            pltpu.VMEM((3, D, D), BF),
            pltpu.VMEM((share, D), BF),
            pltpu.SemaphoreType.DMA((3, 9)),
            pltpu.SemaphoreType.DMA((8,)),
        ],
        limit=VMEM_LARGE,
    )
    grads = call(
        feed_weights_kernel,
        "feed_weights",
        (at, *factors),
        [SMEM] + [VM] * 6,
        [shape((3, quarter, feat), BF)] * 16,
        scratch=[
            pltpu.VMEM((16, 3, quarter, feat), BF),
            pltpu.VMEM((2, D, share), BF),
            pltpu.SemaphoreType.DMA((16, 3)),
        ],
        out_specs=[HBM] * 16,
        limit=VMEM_LARGE,
    )
    ts = all_four(ts)
    ts, grads = together((ts, grads))
    others = grads[8:]
    over = lambda n: swap(others[n], "core")
    sx0, kx0, sx1, kx1, sy0, ky0, sy1, ky1 = grads[:8]
    osx0, osx1, osy0, osy1 = over(0), over(2), over(4), over(6)
    sx1, sy1 = add(sx1, osx1), add(sy1, osy1)
    ox0, ox1, oy0, oy1 = over(1), over(3), over(5), over(7)
    ts, sx1, sy1 = together((ts, sx1, sy1))
    rx1, ry1 = swap(sx1, "row"), swap(sy1, "col")
    ts = ts.reshape(4, heads, HEAD_DIM, share)
    raw = raw.reshape(heads, HEAD_DIM, t)

    grad_proj, gscale = attention_backward(at, qkv, raw, factor_col, attended, ts, lse, masks)
    grad_proj = grad_proj.reshape(3, hr, t)
    kept, sent = call(
        weight_back_kernel,
        "weight_back",
        (at, grad_proj, normed_one),
        [SMEM] + [VM] * 2,
        [shape((2, 3, hr // 2, feat), BF)] * 2,
    )
    sent, rx1, ry1, osx0, osy0, ox0, ox1, oy0, oy1 = together((sent, rx1, ry1, osx0, osy0, ox0, ox1, oy0, oy1))
    got = swap(sent, "core")
    px1, py1 = add(kx1, ox1, rx1), add(ky1, oy1, ry1)
    qx, qy = swap(px1, "col"), swap(py1, "row")
    sx0, sy0 = add(sx0, osx0), add(sy0, osy0)
    rx0, ry0 = swap(sx0, "row"), swap(sy0, "col")
    w_pair = add(kept, got)
    first = z_first()
    got_w = z_swap(jnp.where(first, w_pair[1], w_pair[0]), 1)
    slope = QUERY_CONST / math.sqrt(HEAD_DIM) * jax.nn.sigmoid(query_scale)
    grad_query_scale = jnp.sum(gscale, axis=(0, 2)) * slope
    scale_grad = jnp.pad(grad_query_scale, (0, feat - HEAD_DIM)).reshape(1, feat)
    es = call(
        project_back_kernel,
        "project_back",
        (at, after(grad_proj, w_pair, px1, py1).reshape(3 * hr, t), w_full, inputs, x01, x10, x11, gain_one, vectors, scale_grad),
        [SMEM] + [VM] * 9,
        shape((4, tok + 16, feat), BF),
    )
    qx, qy, rx0, ry0, got_w, w_pair, es = together((qx, qy, rx0, ry0, got_w, w_pair, es))

    mine_w = add(jnp.where(first, w_pair[0], w_pair[1]), got_w)
    met_w = z_swap(mine_w, 3)
    fx, fy = add(kx0, ox0, rx0, qx), add(ky0, oy0, ry0, qy)
    got_c = z_swap(jnp.where(first, fy, fx), 1)
    es = all_four(after(es, fx, fy, mine_w))
    met_w, mine_w, got_c, fx, fy, es, post = together((met_w, mine_w, got_c, fx, fy, es, post))

    mine_w = add(mine_w, met_w)
    other_w = z_swap(mine_w, 1)
    w_own, w_theirs = jnp.where(first, mine_w, other_w), jnp.where(first, other_w, mine_w)
    mine_c = add(jnp.where(first, fx, fy), got_c)
    met_c = z_swap(mine_c, 3)
    post = swap(post, "col")
    w_theirs = swap(w_theirs, "col")
    total = jnp.sum(es[:, tok + 2 : tok + 11].astype(F32), axis=0)
    total = total + swap(total, "core")
    total = total + z_swap(total, 1)
    met_c, mine_c, w_own, w_theirs, post, total = together((met_c, mine_c, w_own, w_theirs, post, total))
    mine_c = add(mine_c, met_c)
    other_c = z_swap(mine_c, 1)
    total = total + z_swap(total, 3)
    w_args = (after(at, total), w_own, w_theirs, swap(w_own, "core"), swap(w_theirs, "core"))
    sum_qkv = call(
        finish_qkv_kernel,
        "finish_qkv",
        w_args,
        [SMEM] + [VM] * 4,
        shape((3, feat, 2 * hr), F32),
        scratch=[pltpu.VMEM((2 * hr, feat), F32)],
    )
    sum_qkv = jnp.transpose(sum_qkv, (1, 0, 2))

    e = jnp.sum(es[:, :tok].astype(F32), axis=0)
    inner = jnp.sum(es[:, tok : tok + 2, :tok].astype(F32), axis=(0, 1)).reshape(tok, 1)
    grad_middle = jnp.concatenate(flip([gm_own, post[1].astype(F32)], "col"), axis=0)
    grad_inputs = grad_middle + scale_own * (e * gain_attn) - inputs.astype(F32) * (scale_own**3 * inner / D)
    layer_out = jnp.concatenate(flip([out_own, post[0]], "col"), axis=0)

    pick = lambda n, place: lax.dynamic_index_in_dim(total, 2 * n + place, 0, keepdims=False)
    mine_c = after(mine_c, sum_qkv, grad_inputs, layer_out, total)
    fx, fy = jnp.where(first, mine_c, other_c), jnp.where(first, other_c, mine_c)
    sum_out, sum_up, sum_down = call(
        finish_feed_kernel,
        "finish_feed",
        (at, fx, fy, swap(fx, "core"), swap(fy, "core")),
        [SMEM] + [VM] * 4,
        [shape((feat, feat), F32)] * 3,
    )

    return (
        layer_out,
        grad_inputs,
        pick(0, c),
        sum_qkv,
        total[8, :HEAD_DIM],
        sum_out,
        pick(1, c),
        sum_up,
        pick(3, r),
        sum_down,
        pick(2, c),
    )


def solution(mesh):
    dp, rows, cols = mesh.shape["dp"], mesh.shape["row"], mesh.shape["col"]
    split = Mesh(mesh.devices.reshape(dp // 2, 2, rows, cols), ("z", "core", "row", "col"))
    tokens = P(("z", "core", "row"), "col")
    in_specs = (
        tokens,
        P("col"),
        P("col", None, "row"),
        P(),
        P("row", "col"),
        P("col"),
        P("col", "row"),
        P("row"),
        P("row", "col"),
        P("col"),
        P(("z", "core")),
        P(("z", "core")),
        tokens,
    )
    out_specs = (
        tokens,
        tokens,
        P("col"),
        P("col", None, "row"),
        P(),
        P("row", "col"),
        P("col"),
        P("col", "row"),
        P("row"),
        P("row", "col"),
        P("col"),
    )
    body = body_four if (dp, rows, cols) == (8, 2, 2) else body_any
    return jax.shard_map(body, mesh=split, in_specs=in_specs, out_specs=out_specs, check_vma=False)
```

```python
import functools
import math

import jax
import jax.numpy as jnp
from jax import lax
from jax.experimental import pallas as pl
from jax.experimental.pallas import tpu as pltpu
from jax.sharding import Mesh
from jax.sharding import PartitionSpec as P

D = 1280
HEAD_DIM = 80
EPS = 1e-06
QUERY_CONST = 1.442695041
MASKED = -1e30
BF = jnp.bfloat16
F32 = jnp.float32
VMEM_LIMIT = 60 * 1024 * 1024
CHUNK = 1024
VMEM_LARGE = 60 * 1024 * 1024
CHEAP = pl.CostEstimate(flops=1, bytes_accessed=1, transcendentals=0)


def size(axis):
    return lax.axis_size(axis)


def swap(x, axis):
    return lax.ppermute(x, axis, [(0, 1), (1, 0)])


def flip(blocks, axis):
    if size(axis) != 2:
        return list(blocks)
    first = lax.axis_index(axis) == 0
    a, b = blocks
    return [jnp.where(first, a, b), jnp.where(first, b, a)]


def flip_dim(x, axis, dim):
    if size(axis) != 2:
        return x
    return jnp.concatenate(flip(jnp.split(x, 2, axis=dim), axis), axis=dim)


def gather(x, axis):
    if size(axis) == 2:
        return [x, swap(x, axis)]
    whole = lax.all_gather(x, axis, axis=0, tiled=False)
    return [whole[i] for i in range(size(axis))]


def gather_grid(x):
    if size("row") != 2:
        return [gather(b, "col") for b in gather(x, "row")]
    along_row, along_col = swap(x, "row"), swap(x, "col")
    half = x.shape[0] // 2
    across = jnp.concatenate(
        [swap(along_row[:half], "col"), swap(along_col[half:], "row")], axis=0
    )
    return [[x, along_col], [along_row, across]]


def scatter_sum(x, axis, dim):
    if size(axis) != 2:
        return lax.psum_scatter(x, axis, scatter_dimension=dim, tiled=True)
    mine, theirs = jnp.split(x, 2, axis=dim)
    return (mine.astype(F32) + swap(theirs, axis).astype(F32)).astype(x.dtype)


def exchange(x, axis, split, join):
    if size(axis) != 2:
        return lax.all_to_all(x, axis, split, join, tiled=True)
    mine, theirs = jnp.split(x, 2, axis=split)
    return jnp.concatenate([mine, swap(theirs, axis)], axis=join)


def core_half(x, dim):
    return lax.dynamic_slice_in_dim(
        x, lax.axis_index("core") * (x.shape[dim] // 2), x.shape[dim] // 2, dim
    )


def weight_gather(w, row_dim):
    part = core_half(w, 0)
    blocks = gather_grid(part)
    if row_dim == 1:
        blocks = [list(b) for b in zip(*blocks)]
    mine = jnp.stack([jnp.concatenate(b, axis=1) for b in blocks])
    other = swap(mine, "core")
    first = lax.axis_index("core") == 0
    both = jnp.stack([jnp.where(first, mine, other), jnp.where(first, other, mine)], axis=1)
    return both.reshape(-1, both.shape[-1])


def weight_sum(g, row_dim):
    dim_axis = ("row", "col") if row_dim == 0 else ("col", "row")
    n0 = size(dim_axis[0])
    g = g.reshape(n0, 2, g.shape[0] // n0 // 2, g.shape[1])
    core = lax.axis_index("core")
    keep = lax.dynamic_index_in_dim(g, core, 1, keepdims=False)
    give = lax.dynamic_index_in_dim(g, 1 - core, 1, keepdims=False).astype(BF)
    part = (keep + swap(give, "core").astype(F32)).astype(BF)
    part = scatter_sum(part, dim_axis[0], 0)
    part = scatter_sum(part[0], dim_axis[1], 1)
    return z_sum(part)


def z_sum(part):
    total = lax.psum(part, "z")
    other = swap(total, "core")
    return flip_core(total, other)


def flip_core(total, other):
    first = lax.axis_index("core") == 0
    return jnp.concatenate(
        [jnp.where(first, total, other), jnp.where(first, other, total)], axis=-2
    ).astype(F32)


def dot(a, b, contract):
    return lax.dot_general(a, b, ((contract[0:1], contract[1:2]), ((), ())), preferred_element_type=F32)


def bias_block(series_row, series_col, key_pos, q0, k0, qb, kb, diagonal):
    q_pos = q0 + lax.broadcasted_iota(jnp.int32, (1, qb), 1)
    allowed = (series_col == series_row) & (key_pos <= q_pos)
    if diagonal:
        k_pos = k0 + lax.broadcasted_iota(jnp.int32, (kb, 1), 0)
        allowed = allowed | (k_pos == q_pos)
    return jnp.where(allowed, 0.0, MASKED)


def forward_kernel(block, at, qkv_ref, srow_ref, scol_ref, kpos_ref, out_ref, lse_ref, *rest):
    *pieces, bias_ref, krow_ref, s_ref = rest
    t = qkv_ref.shape[3]
    n = t // block
    krow_ref[...] = qkv_ref[1, 0].astype(F32).T.astype(BF)

    def bias_slot(j, i):
        return j * (j + 1) // 2 + i

    @pl.when(pl.program_id(0) == 0)
    def _():
        for j in range(n):
            for i in range(j + 1):
                keys = pl.ds(i * block, block)
                bias_ref[bias_slot(j, i)] = bias_block(
                    srow_ref[:, j * block : (j + 1) * block],
                    scol_ref[keys, :],
                    kpos_ref[keys, :],
                    j * block,
                    i * block,
                    block,
                    block,
                    i == j,
                )

    for j in range(n):
        cols = slice(j * block, (j + 1) * block)
        q = qkv_ref[0, 0, :, cols]
        top = None
        for i in range(j + 1):
            s = dot(krow_ref[i * block : (i + 1) * block, :], q, (1, 0)) + bias_ref[bias_slot(j, i)]
            s_ref[i * block : (i + 1) * block, :] = s
            here = jnp.max(s, axis=0, keepdims=True)
            top = here if top is None else jnp.maximum(top, here)
        total = jnp.zeros((1, block), F32)
        acc = jnp.zeros((HEAD_DIM, block), F32)
        for i in range(j + 1):
            p = jnp.exp(s_ref[i * block : (i + 1) * block, :] - top)
            total += jnp.sum(p, axis=0, keepdims=True)
            acc += dot(qkv_ref[2, 0, :, i * block : (i + 1) * block], p.astype(BF), (1, 0))
        found = (acc / total).astype(BF)
        out_ref[0, :, cols] = found
        if pieces:
            pieces[0][j, 0] = found
        lse_ref[0, :, cols] = top + jnp.log(total)


def backward_kernel(
    block, at, qkv_ref, raw_ref, factor_ref, out_ref, lse_ref, srow_ref, scol_ref, kpos_ref, *rest
):
    piece, grad_ref, gscale_ref, bias_ref, krow_ref, vrow_ref, gk_ref, gv_ref, gout_ref = rest
    wide = piece.shape[3]
    for j in range(piece.shape[0]):
        gout_ref[:, j * wide : (j + 1) * wide] = piece[j, 0]
    t = qkv_ref.shape[3]
    n = t // block
    krow_ref[...] = qkv_ref[1, 0].astype(F32).T.astype(BF)
    vrow_ref[...] = qkv_ref[2, 0].astype(F32).T.astype(BF)

    def bias_slot(j, i):
        return j * (j + 1) // 2 + i

    @pl.when(pl.program_id(0) == 0)
    def _():
        for j in range(n):
            for i in range(j + 1):
                keys = pl.ds(i * block, block)
                bias_ref[bias_slot(j, i)] = bias_block(
                    srow_ref[:, j * block : (j + 1) * block],
                    scol_ref[keys, :],
                    kpos_ref[keys, :],
                    j * block,
                    i * block,
                    block,
                    block,
                    i == j,
                )

    gscale = jnp.zeros((HEAD_DIM, 1), F32)
    for j in range(n):
        cols = slice(j * block, (j + 1) * block)
        q = qkv_ref[0, 0, :, cols]
        go = gout_ref[:, cols]
        lse = lse_ref[0, :, cols]
        delta = jnp.sum(go.astype(F32) * out_ref[0, :, cols].astype(F32), axis=0, keepdims=True)
        gq = jnp.zeros((HEAD_DIM, block), F32)
        step = max(1, CHUNK // block)
        for i in range(0, j + 1, step):
            many = min(step, j + 1 - i)
            keys = slice(i * block, (i + many) * block)
            slot = bias_slot(j, i)
            bias = bias_ref[slot : slot + many].reshape(many * block, block)
            p = jnp.exp(dot(krow_ref[keys, :], q, (1, 0)) + bias - lse)
            gp = dot(vrow_ref[keys, :], go, (1, 0))
            gs = (p * (gp - delta)).astype(BF)
            gq += dot(qkv_ref[1, 0, :, keys], gs, (1, 0))
            gk = dot(q, gs, (1, 1))
            gv = dot(go, p.astype(BF), (1, 1))
            before, last = slice(i * block, min(i + many, j) * block), slice(j * block, (j + 1) * block)
            old = (min(i + many, j) - i) * block
            if old:
                gk_ref[:, before] += gk[:, :old]
                gv_ref[:, before] += gv[:, :old]
            if i + many == j + 1:
                gk_ref[:, last] = gk[:, old:]
                gv_ref[:, last] = gv[:, old:]
        gscale += jnp.sum(gq * raw_ref[0, :, cols], axis=1, keepdims=True)
        grad_ref[0, 0, :, cols] = (gq * factor_ref[...]).astype(BF)
    grad_ref[1, 0] = gk_ref[...].astype(BF)
    grad_ref[2, 0] = gv_ref[...].astype(BF)
    gscale_ref[0] = gscale


def mask_args(series, padding):
    t = series.shape[0]
    pos = jnp.arange(t, dtype=jnp.int32)
    return series.reshape(1, t), series.reshape(t, 1), jnp.where(padding == 0, pos, t).reshape(t, 1)


def attention_forward(at, qkv, masks, pieces=0):
    _, heads, hd, t = qkv.shape
    block = min(256, t) if t <= 2048 else 512
    n = t // block
    whole = lambda shape: pl.BlockSpec(shape, lambda h: (0,) * len(shape))
    return pl.pallas_call(
        functools.partial(forward_kernel, block),
        grid=(heads,),
        in_specs=[
            pl.BlockSpec(memory_space=pltpu.SMEM),
            pl.BlockSpec((3, 1, hd, t), lambda h: (0, h, 0, 0)),
            whole((1, t)),
            whole((t, 1)),
            whole((t, 1)),
        ],
        out_specs=[
            pl.BlockSpec((1, hd, t), lambda h: (h, 0, 0)),
            pl.BlockSpec((1, 1, t), lambda h: (h, 0, 0)),
        ]
        + [pl.BlockSpec((n, 1, hd, block), lambda h: (0, h, 0, 0))] * pieces,
        out_shape=[
            jax.ShapeDtypeStruct((heads, hd, t), BF),
            jax.ShapeDtypeStruct((heads, 1, t), F32),
        ]
        + [jax.ShapeDtypeStruct((n, heads, hd, block), BF)] * pieces,
        scratch_shapes=[
            pltpu.VMEM((n * (n + 1) // 2, block, block), F32),
            pltpu.VMEM((t, hd), BF),
            pltpu.VMEM((t, block), F32),
        ],
        compiler_params=pltpu.CompilerParams(vmem_limit_bytes=VMEM_LARGE),
        cost_estimate=CHEAP,
        name="attention_forward",
    )(at, qkv, *masks)


def attention_backward(at, qkv, raw, factor, out, piece, lse, masks):
    _, heads, hd, t = qkv.shape
    block = min(256, t) if t <= 2048 else 512
    n = t // block
    whole = lambda shape: pl.BlockSpec(shape, lambda h: (0,) * len(shape))
    head = lambda wide=t: pl.BlockSpec((1, hd, wide), lambda h: (h, 0, 0))
    return pl.pallas_call(
        functools.partial(backward_kernel, block),
        grid=(heads,),
        in_specs=[
            pl.BlockSpec(memory_space=pltpu.SMEM),
            pl.BlockSpec((3, 1, hd, t), lambda h: (0, h, 0, 0)),
            head(),
            whole((hd, 1)),
            head(),
            pl.BlockSpec((1, 1, t), lambda h: (h, 0, 0)),
            whole((1, t)),
            whole((t, 1)),
            whole((t, 1)),
        ]
        + [pl.BlockSpec((piece.shape[0], 1, hd, piece.shape[3]), lambda h: (0, h, 0, 0))],
        out_specs=[
            pl.BlockSpec((3, 1, hd, t), lambda h: (0, h, 0, 0)),
            pl.BlockSpec((1, hd, 1), lambda h: (h, 0, 0)),
        ],
        out_shape=[
            jax.ShapeDtypeStruct((3, heads, hd, t), BF),
            jax.ShapeDtypeStruct((heads, hd, 1), F32),
        ],
        scratch_shapes=[
            pltpu.VMEM((n * (n + 1) // 2, block, block), F32),
            pltpu.VMEM((t, hd), BF),
            pltpu.VMEM((t, hd), BF),
            pltpu.VMEM((hd, t), F32),
            pltpu.VMEM((hd, t), F32),
            pltpu.VMEM((hd, t), BF),
        ],
        compiler_params=pltpu.CompilerParams(vmem_limit_bytes=VMEM_LARGE),
        cost_estimate=CHEAP,
        name="attention_backward",
    )(at, qkv, raw, factor, out, lse, *masks, piece)


def norm_scale(x):
    return lax.rsqrt(jnp.mean(x * x, axis=1, keepdims=True) + EPS)


def body_any(
    inputs, gain_attn, w_qkv, query_scale, w_out, gain_mlp, w_up, b_up, w_down, b_down, series_ids, pad_mask, cotangent
):
    rows, cols = size("row"), size("col")
    tok = inputs.shape[0]
    feat = inputs.shape[1]
    share = tok // cols
    t = series_ids.shape[0]
    head_rows = w_qkv.shape[2] // cols
    heads = head_rows // HEAD_DIM
    r, c = lax.axis_index("row"), lax.axis_index("col")

    blocks = gather_grid(inputs)
    strips = [jnp.concatenate(b, axis=1) for b in blocks]
    x_own = strips[0] if rows == 2 else lax.dynamic_index_in_dim(jnp.stack(strips), r, 0, keepdims=False)
    x_all = jnp.concatenate(flip(strips, "row"), axis=0)
    gain_one = jnp.concatenate(gather(gain_attn, "col"))
    gain_two = jnp.concatenate(gather(gain_mlp, "col"))
    bias_up = jnp.concatenate(gather(b_up, "row")).astype(F32)
    bias_down = jnp.concatenate(gather(b_down, "col")).astype(F32)

    w3 = jnp.transpose(w_qkv, (1, 0, 2)).reshape(3, feat, cols, head_rows)
    w_mine = lax.dynamic_index_in_dim(w3, c, 2, keepdims=False)
    w_give = lax.dynamic_index_in_dim(w3, 1 - c, 2, keepdims=False)
    w_half = swap(core_half(w_give, 1), "col")
    w_other = swap(w_half, "core")
    first = lax.axis_index("core") == 0
    w_full = jnp.concatenate(
        [w_mine, jnp.where(first, w_half, w_other), jnp.where(first, w_other, w_half)], axis=1
    )

    xf = x_all.astype(F32)
    scale_one = norm_scale(xf)
    normed_one = (xf * scale_one * gain_one).astype(BF)
    projected = jnp.einsum("td,sdh->sht", normed_one, w_full, preferred_element_type=F32)
    projected = projected.reshape(3, heads, HEAD_DIM, t)
    factor = QUERY_CONST / math.sqrt(HEAD_DIM) * jax.nn.softplus(query_scale)
    raw_q = projected[0]
    qkv = jnp.stack([raw_q * factor[None, :, None], projected[1], projected[2]]).astype(BF)
    masks = mask_args(series_ids, pad_mask)
    at = jnp.zeros((4,), jnp.int32)
    attended, lse = attention_forward(at, qkv, masks)

    def to_tokens(y):
        y = flip_dim(y.reshape(head_rows, rows, cols, share), "row", 1)
        y = flip_dim(y, "col", 2)
        y = exchange(y.reshape(1, head_rows, rows, cols, share), "row", 2, 0)
        y = exchange(y.reshape(rows, 1, head_rows, cols, share), "col", 3, 1)
        y = flip_dim(y.reshape(rows, cols, head_rows, share), "col", 1)
        return y.reshape(rows * cols * head_rows, share)

    def to_heads(y):
        y = flip_dim(y.reshape(rows, cols, head_rows, share), "col", 1)
        y = exchange(y.reshape(rows, cols, head_rows, 1, share), "col", 1, 3)
        y = exchange(y.reshape(rows, head_rows, 1, cols, share), "row", 0, 2)
        y = flip_dim(y.reshape(head_rows, rows, cols, share), "col", 2)
        return flip_dim(y, "row", 1).reshape(head_rows, t)

    w_out_all = weight_gather(w_out, 0)
    w_up_all = weight_gather(w_up, 1)
    w_down_all = weight_gather(w_down, 0)

    def my_share(y):
        return lax.dynamic_slice_in_dim(y, c * share, share, 0)

    att = to_tokens(attended.reshape(head_rows, t))
    x_mine = my_share(x_own).astype(F32)
    middle = x_mine + dot(att, w_out_all, (0, 0))
    scale_two = norm_scale(middle)
    normed_two = (middle * scale_two * gain_two).astype(BF)
    pre_act = dot(normed_two, w_up_all, (1, 0)) + bias_up
    sig = jax.nn.sigmoid(pre_act)
    hidden = (pre_act * sig).astype(BF)
    result = (middle + dot(hidden, w_down_all, (1, 0)) + bias_down).astype(BF)

    def to_block(y):
        mine, theirs = jnp.split(y, 2, axis=1)
        return jnp.concatenate(flip([mine, swap(theirs, "col")], "col"), axis=0)

    layer_out = to_block(result)

    g_give = lax.dynamic_slice_in_dim(cotangent, (1 - c) * share, share, 0)
    g = jnp.concatenate([my_share(cotangent), swap(g_give, "col")], axis=1)
    grad_w_down = dot(hidden, g, (0, 0))
    grad_hidden = dot(g, w_down_all, (1, 1))
    grad_pre_f = grad_hidden * sig * (1.0 + pre_act * (1.0 - sig))
    grad_pre = grad_pre_f.astype(BF)
    grad_b_up = jnp.sum(grad_pre.astype(F32), axis=0)
    grad_w_up = dot(normed_two, grad_pre, (0, 0))
    grad_normed_two = dot(grad_pre, w_up_all, (1, 1))
    weighted = grad_normed_two * gain_two
    inner = jnp.sum(weighted * middle, axis=1, keepdims=True)
    grad_middle = g.astype(F32) + scale_two * weighted - middle * (scale_two**3 * inner / D)
    grad_gain_mlp = jnp.sum(grad_normed_two * middle * scale_two, axis=0)
    grad_branch = grad_middle.astype(BF)
    grad_w_out = dot(att, grad_branch, (1, 0))
    grad_att = dot(w_out_all, grad_branch, (1, 1)).astype(BF)
    grad_attended = to_heads(grad_att).reshape(heads, HEAD_DIM, t)
    grad_middle_block = to_block(grad_middle)

    sum_down = weight_sum(grad_w_down, 0)
    sum_up = weight_sum(grad_w_up, 1)
    sum_out = weight_sum(grad_w_out, 0)

    grad_proj, gscale = attention_backward(
        at, qkv, raw_q, factor.reshape(HEAD_DIM, 1), attended, grad_attended[None], lse, masks
    )
    slope = QUERY_CONST / math.sqrt(HEAD_DIM) * jax.nn.sigmoid(query_scale)
    grad_query_scale = jnp.sum(gscale, axis=(0, 2)) * slope
    grad_proj = grad_proj.reshape(3, head_rows, t)
    grad_normed_one = jnp.einsum("sht,sdh->td", grad_proj, w_full, preferred_element_type=F32)
    weighted_one = grad_normed_one * gain_one
    inner_one = jnp.sum(weighted_one * xf, axis=1)
    grad_gain_attn = jnp.sum(grad_normed_one * xf * scale_one, axis=0)
    inner_one = lax.psum(inner_one, ("row", "col"))
    grad_w = jnp.einsum("td,sht->sdh", normed_one, grad_proj, preferred_element_type=F32)
    grad_w = grad_w.reshape(3, cols, 2, feat // 2, head_rows)
    core = lax.axis_index("core")
    keep = lax.dynamic_index_in_dim(grad_w, core, 2, keepdims=False)
    give = lax.dynamic_index_in_dim(grad_w, 1 - core, 2, keepdims=False).astype(BF)
    part = (keep + swap(give, "core").astype(F32)).astype(BF)
    part = jnp.concatenate(flip([part[:, 0], swap(part[:, 1], "col")], "col"), axis=2)
    sum_qkv = jnp.transpose(z_sum(part), (1, 0, 2))

    e = jnp.concatenate(flip(jnp.split(grad_normed_one.astype(BF), 2, axis=0), "row"), axis=0) if rows == 2 else (
        grad_normed_one.astype(BF)
    )
    e = scatter_sum(e, "row", 0)
    e = scatter_sum(e, "col", 1).astype(F32)
    my_rows = lambda y: lax.dynamic_slice_in_dim(y, r * tok, tok, 0)
    scale_mine = my_rows(scale_one)
    inner_mine = my_rows(inner_one.reshape(t, 1))
    grad_inputs = grad_middle_block + scale_mine * (e * gain_attn) - inputs.astype(F32) * (
        scale_mine**3 * inner_mine / D
    )

    grad_b_down = jnp.sum(g.astype(F32), axis=0)
    vectors = jnp.concatenate(
        [
            flip_dim(grad_gain_attn, "col", 0),
            flip_dim(grad_gain_mlp, "col", 0),
            flip_dim(grad_b_down, "col", 0),
            flip_dim(grad_b_up, "row", 0),
            grad_query_scale,
        ]
    )
    vectors = lax.psum(vectors, ("z", "core", "row", "col"))
    mine_col = lambda at: lax.dynamic_slice_in_dim(vectors, at * D + c * feat, feat, 0)
    units = b_up.shape[0]
    return (
        layer_out,
        grad_inputs,
        mine_col(0),
        sum_qkv,
        vectors[4 * D :],
        sum_out,
        mine_col(1),
        sum_up,
        lax.dynamic_slice_in_dim(vectors, 3 * D + r * units, units, 0),
        sum_down,
        mine_col(2),
    )


SMEM = pl.BlockSpec(memory_space=pltpu.SMEM)
ANY = pl.BlockSpec(memory_space=pl.ANY)


def call(kernel, name, args, specs, outs, scratch=(), limit=VMEM_LIMIT, out_specs=None):
    more = {} if out_specs is None else {"out_specs": out_specs}
    return pl.pallas_call(
        kernel,
        in_specs=specs,
        **more,
        out_shape=outs,
        scratch_shapes=list(scratch),
        compiler_params=pltpu.CompilerParams(vmem_limit_bytes=limit),
        cost_estimate=CHEAP,
        name=name,
    )(*args)


VM = pl.BlockSpec(memory_space=pltpu.VMEM)
HBM = pl.BlockSpec(memory_space=pltpu.HBM)


def shape(dims, kind):
    return jax.ShapeDtypeStruct(dims, kind)


def project_kernel(
    at, x00, x01, x10, x11, gain, factor, w_mine, w_a, w_b, qkv, raw, normed, scale_own, w_full
):
    r, k = at[0], at[2]
    tok, feat = x00.shape
    hr = w_mine.shape[1]
    half = hr // 2
    for s in range(3):
        w_full[pl.ds(s * hr, hr), 0:feat] = w_mine[s]
        w_full[pl.ds(pl.multiple_of(s * hr + k * half, 16), half), feat:] = w_a[s]
        w_full[pl.ds(pl.multiple_of(s * hr + (1 - k) * half, 16), half), feat:] = w_b[s]
    for i, (a_ref, b_ref) in enumerate(((x00, x01), (x10, x11))):
        a, b = a_ref[...].astype(F32), b_ref[...].astype(F32)
        total = jnp.sum(a * a, axis=1, keepdims=True) + jnp.sum(b * b, axis=1, keepdims=True)
        scale = lax.rsqrt(total / (2 * feat) + EPS)
        if i == 0:
            scale_own[...] = scale
        rows = pl.ds(pl.multiple_of((r ^ i) * tok, tok), tok)
        normed[rows, 0:feat] = (a * scale * gain[:, 0:feat]).astype(BF)
        normed[rows, feat:] = (b * scale * gain[:, feat:]).astype(BF)
        y = normed[rows, :]
        q = dot(w_full[0:hr, :], y, (1, 1))
        raw[:, rows] = q
        qkv[0, :, rows] = (q * factor[...]).astype(BF)
        qkv[1, :, rows] = dot(w_full[hr : 2 * hr, :], y, (1, 1)).astype(BF)
        qkv[2, :, rows] = dot(w_full[2 * hr : 3 * hr, :], y, (1, 1)).astype(BF)


def feed_kernel(
    at, gain, bias_up, bias_down, a, x_own, x_col, g_own, g_col,
    w_out, w_up, w_down, hx, hy, d0, d1, hx2, hy2, d02, d12,
    out_own, gm_own, post, ts, vectors, att, hidden_out, normed_out, g_out, pre_out, branch_out,
    w, x_ref, sems, more_sems,
):
    r, c, k = at[0], at[1], at[2]
    _, hr, share = a.shape
    feat = x_own.shape[1]
    half = feat // 2
    first = d0.shape[1]
    rows = pl.ds(pl.multiple_of(c * share, share), share)

    def start(pairs, sem):
        copies = [pltpu.make_async_copy(src, dst, sem.at[m]) for m, (src, dst) in enumerate(pairs)]
        for copy in copies:
            copy.start()
        return copies

    def place(s):
        return pl.ds(pl.multiple_of(((s // 2) ^ r) * 2 * hr + (s % 2) * hr, 16), hr)

    small = [(a.at[s], att.at[place(s), :]) for s in range(4)]
    small += [(x_own.at[rows, :], x_ref.at[:, 0:feat]), (x_col.at[rows, :], x_ref.at[:, feat:])]
    small += [(g_own.at[rows, :], g_out.at[:, 0:feat]), (g_col, g_out.at[:, feat:])]
    small = start(small, more_sems)
    copies = []
    for n, shard in enumerate((w_out, w_up, w_down)):
        rx, cx, ry, cy = (0, feat, feat, 0) if n == 1 else (feat, 0, 0, feat)
        mine = [(shard, w.at[n, 0:feat, 0:feat])]
        for core, (px, py, p0, p1) in ((k, (hx, hy, d0, d1)), (1 - k, (hx2, hy2, d02, d12))):
            down = core * half
            at_x = pl.ds(pl.multiple_of(rx + down, 16), half)
            at_y = pl.ds(pl.multiple_of(ry + down, 16), half)
            at_0 = pl.ds(pl.multiple_of(feat + down, 16), first)
            at_1 = pl.ds(pl.multiple_of(feat + down + first, 16), half - first)
            mine.append((px.at[n], w.at[n, at_x, cx : cx + feat]))
            mine.append((py.at[n], w.at[n, at_y, cy : cy + feat]))
            mine.append((p0.at[n], w.at[n, at_0, feat : 2 * feat]))
            mine.append((p1.at[n], w.at[n, at_1, feat : 2 * feat]))
        copies.append(start(mine, sems.at[n]))

    for copy in small + copies[0]:
        copy.wait()
    middle = x_ref[...].astype(F32) + dot(att[...], w[0], (0, 0))
    scale = lax.rsqrt(jnp.sum(middle * middle, axis=1, keepdims=True) / D + EPS)
    normed = (middle * scale * gain[...]).astype(BF)
    normed_out[...] = normed
    for copy in copies[1]:
        copy.wait()
    pre = dot(normed, w[1], (1, 0)) + bias_up[...]
    sig = jax.nn.sigmoid(pre)
    hidden = (pre * sig).astype(BF)
    hidden_out[...] = hidden
    for copy in copies[2]:
        copy.wait()
    result = (middle + dot(hidden, w[2], (1, 0)) + bias_down[...]).astype(BF)
    out_own[...] = result[:, :feat]
    post[0] = result[:, feat:]

    grad_pre_f = dot(g_out[...], w[2], (1, 1)) * sig * (1.0 + pre * (1.0 - sig))
    grad_pre = grad_pre_f.astype(BF)
    pre_out[...] = grad_pre
    grad_normed = dot(grad_pre, w[1], (1, 1))
    weighted = grad_normed * gain[...]
    inner = jnp.sum(weighted * middle, axis=1, keepdims=True)
    gf = g_out[...].astype(F32)
    grad_middle = gf + scale * weighted - middle * (scale * scale * scale * inner / D)
    gm_own[...] = grad_middle[:, :feat]
    post[1] = grad_middle[:, feat:].astype(BF)
    branch = grad_middle.astype(BF)
    branch_out[...] = branch
    for s in range(4):
        ts[s] = dot(w[0, place(s), :], branch, (1, 1)).astype(BF)
    vectors[...] = jnp.concatenate(
        [
            jnp.sum(grad_normed * (middle * scale), axis=0, keepdims=True),
            jnp.sum(gf, axis=0, keepdims=True),
            jnp.sum(grad_pre.astype(F32), axis=0, keepdims=True),
        ],
        axis=0,
    )


def feed_weights_kernel(at, att, hidden, normed, g, grad_pre, branch, *rest):
    *grads, stage, turned, sems = rest
    k = at[2]
    feat = g.shape[1] // 2
    half = feat // 2
    quarter = half // 2
    copies = []

    def weight_grad(n, left_ref, right):
        for core, begin in ((k, 0), (1 - k, 8)):
            up, low = (begin + 4, begin) if n == 1 else (begin, begin + 4)
            for b in range(2):
                part = pl.ds(pl.multiple_of(b * feat + core * half, 16), half)
                y = dot(left_ref[part, :], right, (1, 0)).astype(BF)
                for j in range(2):
                    cut = slice(j * feat, (j + 1) * feat)
                    for to, value in ((up + 2 * j + (1 - b), y[:quarter, cut]), (low + 2 * b + (1 - j), y[quarter:, cut])):
                        stage[to, n] = value
                        copy = pltpu.make_async_copy(stage.at[to, n], grads[to].at[n], sems.at[to, n])
                        copy.start()
                        copies.append(copy)

    turned[0] = hidden[...].astype(F32).T.astype(BF)
    weight_grad(2, turned.at[0], g[...])
    turned[1] = normed[...].astype(F32).T.astype(BF)
    weight_grad(1, turned.at[1], grad_pre[...])
    weight_grad(0, att, branch[...])
    for copy in copies:
        copy.wait()


def weight_back_kernel(at, grad, normed, keep, give):
    k = at[2]
    part = keep.shape[2]
    feat = keep.shape[3]
    for ref, core in ((give, 1 - k), (keep, k)):
        for s in range(3):
            rows = pl.ds(pl.multiple_of(core * part, 16), part)
            y = dot(grad[s, rows, :], normed[...], (1, 0)).astype(BF)
            ref[0, s] = y[:, :feat]
            ref[1, s] = y[:, feat:]


def project_back_kernel(
    at, grad, w_full, x00, x01, x10, x11, gain, vectors, scale_grad, es
):
    r, c = at[0], at[1]
    tok, feat = x00.shape
    sums = [jnp.zeros((1, feat), F32), jnp.zeros((1, feat), F32)]
    inners = []
    for i, xs in enumerate(((x00, x01), (x10, x11))):
        rows = pl.ds(pl.multiple_of((r ^ i) * tok, tok), tok)
        left = grad[:, rows]
        products, squares, inner = [], 0.0, 0.0
        for j in range(2):
            cut = slice(j * feat, (j + 1) * feat)
            e = dot(left, w_full[:, cut], (0, 0))
            x = xs[j][...].astype(F32)
            product = e * x
            inner = inner + jnp.sum(product * gain[:, cut], axis=1, keepdims=True)
            squares = squares + jnp.sum(x * x, axis=1, keepdims=True)
            es[2 * (r ^ i) + (c ^ j), 0:tok, :] = e.astype(BF)
            products.append(product)
        scale = lax.rsqrt(squares / (2 * feat) + EPS)
        for j in range(2):
            sums[j] += jnp.sum(products[j] * scale, axis=0, keepdims=True)
        line = jnp.broadcast_to(inner, (tok, 128)).T[0:1, :]
        high = line.astype(BF).astype(F32)
        inners.append(jnp.concatenate([high, line - high], axis=0))
    rows = []
    pairs = [(sums[0], sums[1], c)]
    pairs += [(vectors[n : n + 1, :feat], vectors[n : n + 1, feat:], (c, c, r)[n]) for n in range(3)]
    for own, other, place in pairs:
        rows += [jnp.where(place == 0, own, other), jnp.where(place == 0, other, own)]
    rows = jnp.concatenate(rows + [scale_grad[...], jnp.zeros((5, feat), F32)], axis=0)
    for i in range(2):
        inner = jnp.concatenate([inners[i], jnp.zeros((2, feat - tok), F32)], axis=1)
        extra = jnp.concatenate([inner, rows], axis=0).astype(BF)
        for j in range(2):
            es[2 * (r ^ i) + (c ^ j), tok:, :] = extra


def finish_qkv_kernel(at, mine, theirs, mine2, theirs2, out, rows):
    c, k = at[1], at[2]
    half = mine.shape[1]
    for s in range(3):
        for ref, col, core in ((mine, c, k), (theirs, 1 - c, k), (mine2, c, 1 - k), (theirs2, 1 - c, 1 - k)):
            rows[pl.ds(pl.multiple_of((2 * col + core) * half, 16), half), :] = ref[s].astype(F32)
        out[s] = rows[...].T


def finish_feed_kernel(at, a, b, a2, b2, *outs):
    k = at[2]
    quarter = a.shape[1]
    for n, out in enumerate(outs):
        upper, lower = ((b, b2), (a, a2)) if n == 1 else ((a, a2), (b, b2))
        for i, core in ((0, k), (1, 1 - k)):
            for j, refs in enumerate((upper, lower)):
                to = pl.multiple_of((2 * core + j) * quarter, 16)
                out[pl.ds(to, quarter), :] = refs[i][n].astype(F32)


together = lax.optimization_barrier


def after(x, *earlier):
    return lax.optimization_barrier((x, *earlier))[0]


def add(*parts):
    total = parts[0].astype(F32)
    for part in parts[1:]:
        total = total + part.astype(F32)
    return total.astype(BF)


def all_four(x):
    return lax.all_to_all(x, ("row", "col"), 0, 0, tiled=True)


def z_swap(x, step):
    n = size("z")
    return lax.ppermute(x, "z", [(i, i ^ step) for i in range(n)])


def z_first():
    z = lax.axis_index("z")
    return (z == 0) | (z == 3)


def body_four(
    inputs, gain_attn, w_qkv, query_scale, w_out, gain_mlp, w_up, b_up, w_down, b_down, series_ids, pad_mask, cotangent
):
    tok, feat = inputs.shape
    share = tok // 2
    t = series_ids.shape[0]
    hr = w_qkv.shape[2] // 2
    heads = hr // HEAD_DIM
    half = feat // 2
    r, c, k = lax.axis_index("row"), lax.axis_index("col"), lax.axis_index("core")
    at = jnp.stack([r, c, k, 2 * r + c]).astype(jnp.int32)
    mine_rows = lambda y, part: lax.dynamic_slice_in_dim(y, part * share, share, 0)

    few = heads // 2
    quarter = half // 2
    first_rows = (half * 7 // 20) // 16 * 16
    x01 = swap(inputs, "col")
    x10 = swap(inputs, "row")
    small = swap(jnp.concatenate([gain_attn, gain_mlp, b_down.astype(F32)]), "col")
    up_other = swap(b_up.astype(F32), "row")
    w_turned = jnp.transpose(w_qkv, (1, 2, 0)).reshape(3, 2, hr, feat)
    w_mine = lax.dynamic_index_in_dim(w_turned, c, 1, keepdims=False)
    w_give = lax.dynamic_index_in_dim(w_turned, 1 - c, 1, keepdims=False)
    w_half = core_half(w_give, 1)
    w_a = swap(w_half, "col")
    part = jnp.stack([core_half(w_out, 0), core_half(w_up, 0), core_half(w_down, 0)])
    g_give = mine_rows(cotangent, 1 - c)
    x01, x10, small, up_other, part, g_give, w_mine = lax.optimization_barrier(
        (x01, x10, small, up_other, part, g_give, w_mine)
    )
    x11 = swap(after(x01, w_half), "row")
    w_b = swap(w_a, "core")
    gain_one = jnp.concatenate([gain_attn, small[:feat]]).reshape(1, D)
    gain_two = jnp.concatenate([gain_mlp, small[feat : 2 * feat]]).reshape(1, D)
    bias_down = jnp.concatenate([b_down.astype(F32), small[2 * feat :]]).reshape(1, D)
    bias_up = jnp.concatenate([b_up.astype(F32), up_other]).reshape(1, D)
    factor = QUERY_CONST / math.sqrt(HEAD_DIM) * jax.nn.softplus(query_scale)
    factor_col = factor.reshape(HEAD_DIM, 1)

    part = after(part, x11, w_a)
    hx, hy = swap(part, "row"), swap(part, "col")
    hx2, hy2 = swap(hx, "core"), swap(hy, "core")
    qkv, raw, normed_one, scale_own, w_full = call(
        project_kernel,
        "project",
        (at, inputs, x01, x10, x11, gain_one, jnp.tile(factor_col, (heads, 1)), w_mine, w_a, w_b),
        [SMEM] + [VM] * 9,
        [
            shape((3, hr, t), BF),
            shape((hr, t), F32),
            shape((t, D), BF),
            shape((tok, 1), F32),
            shape((3 * hr, D), BF),
        ],
        limit=VMEM_LARGE,
    )
    qkv = qkv.reshape(3, heads, HEAD_DIM, t)
    masks = mask_args(series_ids, pad_mask)
    attended, lse, a = attention_forward(at, qkv, masks, pieces=1)
    a = all_four(a.reshape(4, hr, share))
    hx_on, hy_on, g_give = lax.optimization_barrier((hx, hy, g_give, lse))[:3]
    d0 = swap(hx_on[:, :first_rows], "col")
    d1 = swap(hy_on[:, first_rows:], "row")
    g_col = swap(g_give, "col")
    d0, d1, g_col, a = together((d0, d1, g_col, a))
    d02, d12 = swap(d0, "core"), swap(d1, "core")
    out_own, gm_own, post, ts, vectors, *factors = call(
        feed_kernel,
        "feed_forward",
        (at, gain_two, bias_up, bias_down, a, inputs, x01, cotangent, g_col)
        + (w_out, w_up, w_down, hx, hy, d0, d1, hx2, hy2, d02, d12),
        [SMEM] + [VM] * 3 + [HBM] * 16,
        [
            shape((share, feat), BF),
            shape((share, feat), F32),
            shape((2, share, feat), BF),
            shape((4, hr, share), BF),
            shape((3, D), F32),
            shape((D, share), BF),
        ]
        + [shape((share, D), BF)] * 5,
        scratch=[
            pltpu.VMEM((3, D, D), BF),
            pltpu.VMEM((share, D), BF),
            pltpu.SemaphoreType.DMA((3, 9)),
            pltpu.SemaphoreType.DMA((8,)),
        ],
        limit=VMEM_LARGE,
    )
    grads = call(
        feed_weights_kernel,
        "feed_weights",
        (at, *factors),
        [SMEM] + [VM] * 6,
        [shape((3, quarter, feat), BF)] * 16,
        scratch=[
            pltpu.VMEM((16, 3, quarter, feat), BF),
            pltpu.VMEM((2, D, share), BF),
            pltpu.SemaphoreType.DMA((16, 3)),
        ],
        out_specs=[HBM] * 16,
        limit=VMEM_LARGE,
    )
    ts = all_four(ts)
    others = grads[8:]
    over = lambda n: swap(others[n], "core")
    grads, osx0, osx1, osy0, osy1 = grads[:8], over(0), over(2), over(4), over(6)
    sx0, kx0, sx1, kx1, sy0, ky0, sy1, ky1 = grads
    sx1, sy1 = add(sx1, osx1), add(sy1, osy1)
    ox0, ox1, oy0, oy1 = over(1), over(3), over(5), over(7)
    sx0, sy0 = add(sx0, osx0), add(sy0, osy0)
    ts, sx1, sy1, sx0, sy0 = together((ts, sx1, sy1, sx0, sy0))
    rx1, ry1 = swap(sx1, "row"), swap(sy1, "col")
    rx0, ry0 = swap(sx0, "row"), swap(sy0, "col")
    ts = ts.reshape(4, heads, HEAD_DIM, share)
    raw = raw.reshape(heads, HEAD_DIM, t)

    grad_proj, gscale = attention_backward(at, qkv, raw, factor_col, attended, ts, lse, masks)
    grad_proj = grad_proj.reshape(3, hr, t)
    kept, sent = call(
        weight_back_kernel,
        "weight_back",
        (at, grad_proj, normed_one),
        [SMEM] + [VM] * 2,
        [shape((2, 3, hr // 2, feat), BF)] * 2,
    )
    sent, rx1, ry1, rx0, ry0, ox0, ox1, oy0, oy1 = together((sent, rx1, ry1, rx0, ry0, ox0, ox1, oy0, oy1))
    got = swap(sent, "core")
    px1, py1 = add(kx1, ox1, rx1), add(ky1, oy1, ry1)
    qx, qy = swap(px1, "col"), swap(py1, "row")
    w_pair = add(kept, got)
    first = z_first()
    got_w = z_swap(jnp.where(first, w_pair[1], w_pair[0]), 1)
    slope = QUERY_CONST / math.sqrt(HEAD_DIM) * jax.nn.sigmoid(query_scale)
    grad_query_scale = jnp.sum(gscale, axis=(0, 2)) * slope
    scale_grad = jnp.pad(grad_query_scale, (0, feat - HEAD_DIM)).reshape(1, feat)
    es = call(
        project_back_kernel,
        "project_back",
        (at, after(grad_proj, w_pair, px1, py1).reshape(3 * hr, t), w_full, inputs, x01, x10, x11, gain_one, vectors, scale_grad),
        [SMEM] + [VM] * 9,
        shape((4, tok + 16, feat), BF),
    )
    kx0, ky0 = together((kx0, ky0, es))[:2]
    fx0 = kx0.astype(F32) + ox0.astype(F32) + rx0.astype(F32)
    fy0 = ky0.astype(F32) + oy0.astype(F32) + ry0.astype(F32)
    qx, qy, got_w, w_pair, es, fx0, fy0 = together((qx, qy, got_w, w_pair, es, fx0, fy0))

    mine_w = add(jnp.where(first, w_pair[0], w_pair[1]), got_w)
    met_w = z_swap(mine_w, 3)
    fx, fy = add(fx0, qx), add(fy0, qy)
    got_c = z_swap(jnp.where(first, fy, fx), 1)
    es = all_four(after(es, fx, fy, mine_w))
    met_w, mine_w, got_c, fx, fy, es, post = together((met_w, mine_w, got_c, fx, fy, es, post))

    mine_w = add(mine_w, met_w)
    other_w = z_swap(mine_w, 1)
    w_own, w_theirs = jnp.where(first, mine_w, other_w), jnp.where(first, other_w, mine_w)
    mine_c = add(jnp.where(first, fx, fy), got_c)
    met_c = z_swap(mine_c, 3)
    post = swap(post, "col")
    w_theirs = swap(w_theirs, "col")
    total = jnp.sum(es[:, tok + 2 : tok + 11].astype(F32), axis=0)
    total = total + swap(total, "core")
    total = total + z_swap(total, 1)
    total = total + z_swap(total, 2)
    met_c, mine_c, w_own, w_theirs, post, total = together((met_c, mine_c, w_own, w_theirs, post, total))
    mine_c = add(mine_c, met_c)
    other_c = z_swap(mine_c, 1)
    w_args = (at, w_own, w_theirs, swap(w_own, "core"), swap(w_theirs, "core"))
    sum_qkv = call(
        finish_qkv_kernel,
        "finish_qkv",
        w_args,
        [SMEM] + [VM] * 4,
        shape((3, feat, 2 * hr), F32),
        scratch=[pltpu.VMEM((2 * hr, feat), F32)],
    )
    sum_qkv = jnp.transpose(sum_qkv, (1, 0, 2))

    e = jnp.sum(es[:, :tok].astype(F32), axis=0)
    inner = jnp.sum(es[:, tok : tok + 2, :tok].astype(F32), axis=(0, 1)).reshape(tok, 1)
    grad_middle = jnp.concatenate(flip([gm_own, post[1].astype(F32)], "col"), axis=0)
    grad_inputs = grad_middle + scale_own * (e * gain_attn) - inputs.astype(F32) * (scale_own**3 * inner / D)
    layer_out = jnp.concatenate(flip([out_own, post[0]], "col"), axis=0)

    pick = lambda n, place: lax.dynamic_index_in_dim(total, 2 * n + place, 0, keepdims=False)
    mine_c = after(mine_c, sum_qkv, grad_inputs, layer_out, total)
    fx, fy = jnp.where(first, mine_c, other_c), jnp.where(first, other_c, mine_c)
    sum_out, sum_up, sum_down = call(
        finish_feed_kernel,
        "finish_feed",
        (at, fx, fy, swap(fx, "core"), swap(fy, "core")),
        [SMEM] + [VM] * 4,
        [shape((feat, feat), F32)] * 3,
    )

    return (
        layer_out,
        grad_inputs,
        pick(0, c),
        sum_qkv,
        total[8, :HEAD_DIM],
        sum_out,
        pick(1, c),
        sum_up,
        pick(3, r),
        sum_down,
        pick(2, c),
    )


def solution(mesh):
    dp, rows, cols = mesh.shape["dp"], mesh.shape["row"], mesh.shape["col"]
    split = Mesh(mesh.devices.reshape(dp // 2, 2, rows, cols), ("z", "core", "row", "col"))
    tokens = P(("z", "core", "row"), "col")
    in_specs = (
        tokens,
        P("col"),
        P("col", None, "row"),
        P(),
        P("row", "col"),
        P("col"),
        P("col", "row"),
        P("row"),
        P("row", "col"),
        P("col"),
        P(("z", "core")),
        P(("z", "core")),
        tokens,
    )
    out_specs = (
        tokens,
        tokens,
        P("col"),
        P("col", None, "row"),
        P(),
        P("row", "col"),
        P("col"),
        P("col", "row"),
        P("row"),
        P("row", "col"),
        P("col"),
    )
    body = body_four if (dp, rows, cols) == (8, 2, 2) else body_any
    return jax.shard_map(body, mesh=split, in_specs=in_specs, out_specs=out_specs, check_vma=False)
```

```python
import functools
import math

import jax
import jax.numpy as jnp
from jax import lax
from jax.experimental import pallas as pl
from jax.experimental.pallas import tpu as pltpu
from jax.sharding import Mesh
from jax.sharding import PartitionSpec as P

D = 1280
HEAD_DIM = 80
EPS = 1e-06
QUERY_CONST = 1.442695041
MASKED = -1e30
BF = jnp.bfloat16
F32 = jnp.float32
VMEM_LIMIT = 60 * 1024 * 1024
CHUNK = 1024
VMEM_LARGE = 60 * 1024 * 1024
CHEAP = pl.CostEstimate(flops=1, bytes_accessed=1, transcendentals=0)


def size(axis):
    return lax.axis_size(axis)


def swap(x, axis):
    return lax.ppermute(x, axis, [(0, 1), (1, 0)])


def flip(blocks, axis):
    if size(axis) != 2:
        return list(blocks)
    first = lax.axis_index(axis) == 0
    a, b = blocks
    return [jnp.where(first, a, b), jnp.where(first, b, a)]


def flip_dim(x, axis, dim):
    if size(axis) != 2:
        return x
    return jnp.concatenate(flip(jnp.split(x, 2, axis=dim), axis), axis=dim)


def gather(x, axis):
    if size(axis) == 2:
        return [x, swap(x, axis)]
    whole = lax.all_gather(x, axis, axis=0, tiled=False)
    return [whole[i] for i in range(size(axis))]


def gather_grid(x):
    if size("row") != 2:
        return [gather(b, "col") for b in gather(x, "row")]
    along_row, along_col = swap(x, "row"), swap(x, "col")
    half = x.shape[0] // 2
    across = jnp.concatenate(
        [swap(along_row[:half], "col"), swap(along_col[half:], "row")], axis=0
    )
    return [[x, along_col], [along_row, across]]


def scatter_sum(x, axis, dim):
    if size(axis) != 2:
        return lax.psum_scatter(x, axis, scatter_dimension=dim, tiled=True)
    mine, theirs = jnp.split(x, 2, axis=dim)
    return (mine.astype(F32) + swap(theirs, axis).astype(F32)).astype(x.dtype)


def exchange(x, axis, split, join):
    if size(axis) != 2:
        return lax.all_to_all(x, axis, split, join, tiled=True)
    mine, theirs = jnp.split(x, 2, axis=split)
    return jnp.concatenate([mine, swap(theirs, axis)], axis=join)


def core_half(x, dim):
    return lax.dynamic_slice_in_dim(
        x, lax.axis_index("core") * (x.shape[dim] // 2), x.shape[dim] // 2, dim
    )


def weight_gather(w, row_dim):
    part = core_half(w, 0)
    blocks = gather_grid(part)
    if row_dim == 1:
        blocks = [list(b) for b in zip(*blocks)]
    mine = jnp.stack([jnp.concatenate(b, axis=1) for b in blocks])
    other = swap(mine, "core")
    first = lax.axis_index("core") == 0
    both = jnp.stack([jnp.where(first, mine, other), jnp.where(first, other, mine)], axis=1)
    return both.reshape(-1, both.shape[-1])


def weight_sum(g, row_dim):
    dim_axis = ("row", "col") if row_dim == 0 else ("col", "row")
    n0 = size(dim_axis[0])
    g = g.reshape(n0, 2, g.shape[0] // n0 // 2, g.shape[1])
    core = lax.axis_index("core")
    keep = lax.dynamic_index_in_dim(g, core, 1, keepdims=False)
    give = lax.dynamic_index_in_dim(g, 1 - core, 1, keepdims=False).astype(BF)
    part = (keep + swap(give, "core").astype(F32)).astype(BF)
    part = scatter_sum(part, dim_axis[0], 0)
    part = scatter_sum(part[0], dim_axis[1], 1)
    return z_sum(part)


def z_sum(part):
    total = lax.psum(part, "z")
    other = swap(total, "core")
    return flip_core(total, other)


def flip_core(total, other):
    first = lax.axis_index("core") == 0
    return jnp.concatenate(
        [jnp.where(first, total, other), jnp.where(first, other, total)], axis=-2
    ).astype(F32)


def dot(a, b, contract):
    return lax.dot_general(a, b, ((contract[0:1], contract[1:2]), ((), ())), preferred_element_type=F32)


def bias_block(series_row, series_col, key_pos, q0, k0, qb, kb, diagonal):
    q_pos = q0 + lax.broadcasted_iota(jnp.int32, (1, qb), 1)
    allowed = (series_col == series_row) & (key_pos <= q_pos)
    if diagonal:
        k_pos = k0 + lax.broadcasted_iota(jnp.int32, (kb, 1), 0)
        allowed = allowed | (k_pos == q_pos)
    return jnp.where(allowed, 0.0, MASKED)


def forward_kernel(block, at, qkv_ref, srow_ref, scol_ref, kpos_ref, out_ref, lse_ref, *rest):
    *pieces, bias_ref, krow_ref, s_ref = rest
    t = qkv_ref.shape[3]
    n = t // block
    krow_ref[...] = qkv_ref[1, 0].astype(F32).T.astype(BF)

    def bias_slot(j, i):
        return j * (j + 1) // 2 + i

    @pl.when(pl.program_id(0) == 0)
    def _():
        for j in range(n):
            for i in range(j + 1):
                keys = pl.ds(i * block, block)
                bias_ref[bias_slot(j, i)] = bias_block(
                    srow_ref[:, j * block : (j + 1) * block],
                    scol_ref[keys, :],
                    kpos_ref[keys, :],
                    j * block,
                    i * block,
                    block,
                    block,
                    i == j,
                )

    for j in range(n):
        cols = slice(j * block, (j + 1) * block)
        q = qkv_ref[0, 0, :, cols]
        top = None
        for i in range(j + 1):
            s = dot(krow_ref[i * block : (i + 1) * block, :], q, (1, 0)) + bias_ref[bias_slot(j, i)]
            s_ref[i * block : (i + 1) * block, :] = s
            here = jnp.max(s, axis=0, keepdims=True)
            top = here if top is None else jnp.maximum(top, here)
        total = jnp.zeros((1, block), F32)
        acc = jnp.zeros((HEAD_DIM, block), F32)
        for i in range(j + 1):
            p = jnp.exp(s_ref[i * block : (i + 1) * block, :] - top)
            total += jnp.sum(p, axis=0, keepdims=True)
            acc += dot(qkv_ref[2, 0, :, i * block : (i + 1) * block], p.astype(BF), (1, 0))
        found = (acc / total).astype(BF)
        out_ref[0, :, cols] = found
        if pieces:
            pieces[0][j, 0] = found
        lse_ref[0, :, cols] = top + jnp.log(total)


def backward_kernel(
    block, at, qkv_ref, raw_ref, factor_ref, out_ref, lse_ref, srow_ref, scol_ref, kpos_ref, *rest
):
    piece, grad_ref, gscale_ref, bias_ref, krow_ref, vrow_ref, gk_ref, gv_ref, gout_ref = rest
    wide = piece.shape[3]
    for j in range(piece.shape[0]):
        gout_ref[:, j * wide : (j + 1) * wide] = piece[j, 0]
    t = qkv_ref.shape[3]
    n = t // block
    krow_ref[...] = qkv_ref[1, 0].astype(F32).T.astype(BF)
    vrow_ref[...] = qkv_ref[2, 0].astype(F32).T.astype(BF)

    def bias_slot(j, i):
        return j * (j + 1) // 2 + i

    @pl.when(pl.program_id(0) == 0)
    def _():
        for j in range(n):
            for i in range(j + 1):
                keys = pl.ds(i * block, block)
                bias_ref[bias_slot(j, i)] = bias_block(
                    srow_ref[:, j * block : (j + 1) * block],
                    scol_ref[keys, :],
                    kpos_ref[keys, :],
                    j * block,
                    i * block,
                    block,
                    block,
                    i == j,
                )

    gscale = jnp.zeros((HEAD_DIM, 1), F32)
    for j in range(n):
        cols = slice(j * block, (j + 1) * block)
        q = qkv_ref[0, 0, :, cols]
        go = gout_ref[:, cols]
        lse = lse_ref[0, :, cols]
        delta = jnp.sum(go.astype(F32) * out_ref[0, :, cols].astype(F32), axis=0, keepdims=True)
        gq = jnp.zeros((HEAD_DIM, block), F32)
        step = max(1, CHUNK // block)
        for i in range(0, j + 1, step):
            many = min(step, j + 1 - i)
            keys = slice(i * block, (i + many) * block)
            slot = bias_slot(j, i)
            bias = bias_ref[slot : slot + many].reshape(many * block, block)
            p = jnp.exp(dot(krow_ref[keys, :], q, (1, 0)) + bias - lse)
            gp = dot(vrow_ref[keys, :], go, (1, 0))
            gs = (p * (gp - delta)).astype(BF)
            gq += dot(qkv_ref[1, 0, :, keys], gs, (1, 0))
            gk = dot(q, gs, (1, 1))
            gv = dot(go, p.astype(BF), (1, 1))
            before, last = slice(i * block, min(i + many, j) * block), slice(j * block, (j + 1) * block)
            old = (min(i + many, j) - i) * block
            if old:
                gk_ref[:, before] += gk[:, :old]
                gv_ref[:, before] += gv[:, :old]
            if i + many == j + 1:
                gk_ref[:, last] = gk[:, old:]
                gv_ref[:, last] = gv[:, old:]
        gscale += jnp.sum(gq * raw_ref[0, :, cols], axis=1, keepdims=True)
        grad_ref[0, 0, :, cols] = (gq * factor_ref[...]).astype(BF)
    grad_ref[1, 0] = gk_ref[...].astype(BF)
    grad_ref[2, 0] = gv_ref[...].astype(BF)
    gscale_ref[0] = gscale


def mask_args(series, padding):
    t = series.shape[0]
    pos = jnp.arange(t, dtype=jnp.int32)
    return series.reshape(1, t), series.reshape(t, 1), jnp.where(padding == 0, pos, t).reshape(t, 1)


def attention_forward(at, qkv, masks, pieces=0):
    _, heads, hd, t = qkv.shape
    block = min(256, t) if t <= 2048 else 512
    n = t // block
    whole = lambda shape: pl.BlockSpec(shape, lambda h: (0,) * len(shape))
    return pl.pallas_call(
        functools.partial(forward_kernel, block),
        grid=(heads,),
        in_specs=[
            pl.BlockSpec(memory_space=pltpu.SMEM),
            pl.BlockSpec((3, 1, hd, t), lambda h: (0, h, 0, 0)),
            whole((1, t)),
            whole((t, 1)),
            whole((t, 1)),
        ],
        out_specs=[
            pl.BlockSpec((1, hd, t), lambda h: (h, 0, 0)),
            pl.BlockSpec((1, 1, t), lambda h: (h, 0, 0)),
        ]
        + [pl.BlockSpec((n, 1, hd, block), lambda h: (0, h, 0, 0))] * pieces,
        out_shape=[
            jax.ShapeDtypeStruct((heads, hd, t), BF),
            jax.ShapeDtypeStruct((heads, 1, t), F32),
        ]
        + [jax.ShapeDtypeStruct((n, heads, hd, block), BF)] * pieces,
        scratch_shapes=[
            pltpu.VMEM((n * (n + 1) // 2, block, block), F32),
            pltpu.VMEM((t, hd), BF),
            pltpu.VMEM((t, block), F32),
        ],
        compiler_params=pltpu.CompilerParams(vmem_limit_bytes=VMEM_LARGE),
        cost_estimate=CHEAP,
        name="attention_forward",
    )(at, qkv, *masks)


def attention_backward(at, qkv, raw, factor, out, piece, lse, masks):
    _, heads, hd, t = qkv.shape
    block = min(256, t) if t <= 2048 else 512
    n = t // block
    whole = lambda shape: pl.BlockSpec(shape, lambda h: (0,) * len(shape))
    head = lambda wide=t: pl.BlockSpec((1, hd, wide), lambda h: (h, 0, 0))
    return pl.pallas_call(
        functools.partial(backward_kernel, block),
        grid=(heads,),
        in_specs=[
            pl.BlockSpec(memory_space=pltpu.SMEM),
            pl.BlockSpec((3, 1, hd, t), lambda h: (0, h, 0, 0)),
            head(),
            whole((hd, 1)),
            head(),
            pl.BlockSpec((1, 1, t), lambda h: (h, 0, 0)),
            whole((1, t)),
            whole((t, 1)),
            whole((t, 1)),
        ]
        + [pl.BlockSpec((piece.shape[0], 1, hd, piece.shape[3]), lambda h: (0, h, 0, 0))],
        out_specs=[
            pl.BlockSpec((3, 1, hd, t), lambda h: (0, h, 0, 0)),
            pl.BlockSpec((1, hd, 1), lambda h: (h, 0, 0)),
        ],
        out_shape=[
            jax.ShapeDtypeStruct((3, heads, hd, t), BF),
            jax.ShapeDtypeStruct((heads, hd, 1), F32),
        ],
        scratch_shapes=[
            pltpu.VMEM((n * (n + 1) // 2, block, block), F32),
            pltpu.VMEM((t, hd), BF),
            pltpu.VMEM((t, hd), BF),
            pltpu.VMEM((hd, t), F32),
            pltpu.VMEM((hd, t), F32),
            pltpu.VMEM((hd, t), BF),
        ],
        compiler_params=pltpu.CompilerParams(vmem_limit_bytes=VMEM_LARGE),
        cost_estimate=CHEAP,
        name="attention_backward",
    )(at, qkv, raw, factor, out, lse, *masks, piece)


def norm_scale(x):
    return lax.rsqrt(jnp.mean(x * x, axis=1, keepdims=True) + EPS)


def body_any(
    inputs, gain_attn, w_qkv, query_scale, w_out, gain_mlp, w_up, b_up, w_down, b_down, series_ids, pad_mask, cotangent
):
    rows, cols = size("row"), size("col")
    tok = inputs.shape[0]
    feat = inputs.shape[1]
    share = tok // cols
    t = series_ids.shape[0]
    head_rows = w_qkv.shape[2] // cols
    heads = head_rows // HEAD_DIM
    r, c = lax.axis_index("row"), lax.axis_index("col")

    blocks = gather_grid(inputs)
    strips = [jnp.concatenate(b, axis=1) for b in blocks]
    x_own = strips[0] if rows == 2 else lax.dynamic_index_in_dim(jnp.stack(strips), r, 0, keepdims=False)
    x_all = jnp.concatenate(flip(strips, "row"), axis=0)
    gain_one = jnp.concatenate(gather(gain_attn, "col"))
    gain_two = jnp.concatenate(gather(gain_mlp, "col"))
    bias_up = jnp.concatenate(gather(b_up, "row")).astype(F32)
    bias_down = jnp.concatenate(gather(b_down, "col")).astype(F32)

    w3 = jnp.transpose(w_qkv, (1, 0, 2)).reshape(3, feat, cols, head_rows)
    w_mine = lax.dynamic_index_in_dim(w3, c, 2, keepdims=False)
    w_give = lax.dynamic_index_in_dim(w3, 1 - c, 2, keepdims=False)
    w_half = swap(core_half(w_give, 1), "col")
    w_other = swap(w_half, "core")
    first = lax.axis_index("core") == 0
    w_full = jnp.concatenate(
        [w_mine, jnp.where(first, w_half, w_other), jnp.where(first, w_other, w_half)], axis=1
    )

    xf = x_all.astype(F32)
    scale_one = norm_scale(xf)
    normed_one = (xf * scale_one * gain_one).astype(BF)
    projected = jnp.einsum("td,sdh->sht", normed_one, w_full, preferred_element_type=F32)
    projected = projected.reshape(3, heads, HEAD_DIM, t)
    factor = QUERY_CONST / math.sqrt(HEAD_DIM) * jax.nn.softplus(query_scale)
    raw_q = projected[0]
    qkv = jnp.stack([raw_q * factor[None, :, None], projected[1], projected[2]]).astype(BF)
    masks = mask_args(series_ids, pad_mask)
    at = jnp.zeros((4,), jnp.int32)
    attended, lse = attention_forward(at, qkv, masks)

    def to_tokens(y):
        y = flip_dim(y.reshape(head_rows, rows, cols, share), "row", 1)
        y = flip_dim(y, "col", 2)
        y = exchange(y.reshape(1, head_rows, rows, cols, share), "row", 2, 0)
        y = exchange(y.reshape(rows, 1, head_rows, cols, share), "col", 3, 1)
        y = flip_dim(y.reshape(rows, cols, head_rows, share), "col", 1)
        return y.reshape(rows * cols * head_rows, share)

    def to_heads(y):
        y = flip_dim(y.reshape(rows, cols, head_rows, share), "col", 1)
        y = exchange(y.reshape(rows, cols, head_rows, 1, share), "col", 1, 3)
        y = exchange(y.reshape(rows, head_rows, 1, cols, share), "row", 0, 2)
        y = flip_dim(y.reshape(head_rows, rows, cols, share), "col", 2)
        return flip_dim(y, "row", 1).reshape(head_rows, t)

    w_out_all = weight_gather(w_out, 0)
    w_up_all = weight_gather(w_up, 1)
    w_down_all = weight_gather(w_down, 0)

    def my_share(y):
        return lax.dynamic_slice_in_dim(y, c * share, share, 0)

    att = to_tokens(attended.reshape(head_rows, t))
    x_mine = my_share(x_own).astype(F32)
    middle = x_mine + dot(att, w_out_all, (0, 0))
    scale_two = norm_scale(middle)
    normed_two = (middle * scale_two * gain_two).astype(BF)
    pre_act = dot(normed_two, w_up_all, (1, 0)) + bias_up
    sig = jax.nn.sigmoid(pre_act)
    hidden = (pre_act * sig).astype(BF)
    result = (middle + dot(hidden, w_down_all, (1, 0)) + bias_down).astype(BF)

    def to_block(y):
        mine, theirs = jnp.split(y, 2, axis=1)
        return jnp.concatenate(flip([mine, swap(theirs, "col")], "col"), axis=0)

    layer_out = to_block(result)

    g_give = lax.dynamic_slice_in_dim(cotangent, (1 - c) * share, share, 0)
    g = jnp.concatenate([my_share(cotangent), swap(g_give, "col")], axis=1)
    grad_w_down = dot(hidden, g, (0, 0))
    grad_hidden = dot(g, w_down_all, (1, 1))
    grad_pre_f = grad_hidden * sig * (1.0 + pre_act * (1.0 - sig))
    grad_pre = grad_pre_f.astype(BF)
    grad_b_up = jnp.sum(grad_pre.astype(F32), axis=0)
    grad_w_up = dot(normed_two, grad_pre, (0, 0))
    grad_normed_two = dot(grad_pre, w_up_all, (1, 1))
    weighted = grad_normed_two * gain_two
    inner = jnp.sum(weighted * middle, axis=1, keepdims=True)
    grad_middle = g.astype(F32) + scale_two * weighted - middle * (scale_two**3 * inner / D)
    grad_gain_mlp = jnp.sum(grad_normed_two * middle * scale_two, axis=0)
    grad_branch = grad_middle.astype(BF)
    grad_w_out = dot(att, grad_branch, (1, 0))
    grad_att = dot(w_out_all, grad_branch, (1, 1)).astype(BF)
    grad_attended = to_heads(grad_att).reshape(heads, HEAD_DIM, t)
    grad_middle_block = to_block(grad_middle)

    sum_down = weight_sum(grad_w_down, 0)
    sum_up = weight_sum(grad_w_up, 1)
    sum_out = weight_sum(grad_w_out, 0)

    grad_proj, gscale = attention_backward(
        at, qkv, raw_q, factor.reshape(HEAD_DIM, 1), attended, grad_attended[None], lse, masks
    )
    slope = QUERY_CONST / math.sqrt(HEAD_DIM) * jax.nn.sigmoid(query_scale)
    grad_query_scale = jnp.sum(gscale, axis=(0, 2)) * slope
    grad_proj = grad_proj.reshape(3, head_rows, t)
    grad_normed_one = jnp.einsum("sht,sdh->td", grad_proj, w_full, preferred_element_type=F32)
    weighted_one = grad_normed_one * gain_one
    inner_one = jnp.sum(weighted_one * xf, axis=1)
    grad_gain_attn = jnp.sum(grad_normed_one * xf * scale_one, axis=0)
    inner_one = lax.psum(inner_one, ("row", "col"))
    grad_w = jnp.einsum("td,sht->sdh", normed_one, grad_proj, preferred_element_type=F32)
    grad_w = grad_w.reshape(3, cols, 2, feat // 2, head_rows)
    core = lax.axis_index("core")
    keep = lax.dynamic_index_in_dim(grad_w, core, 2, keepdims=False)
    give = lax.dynamic_index_in_dim(grad_w, 1 - core, 2, keepdims=False).astype(BF)
    part = (keep + swap(give, "core").astype(F32)).astype(BF)
    part = jnp.concatenate(flip([part[:, 0], swap(part[:, 1], "col")], "col"), axis=2)
    sum_qkv = jnp.transpose(z_sum(part), (1, 0, 2))

    e = jnp.concatenate(flip(jnp.split(grad_normed_one.astype(BF), 2, axis=0), "row"), axis=0) if rows == 2 else (
        grad_normed_one.astype(BF)
    )
    e = scatter_sum(e, "row", 0)
    e = scatter_sum(e, "col", 1).astype(F32)
    my_rows = lambda y: lax.dynamic_slice_in_dim(y, r * tok, tok, 0)
    scale_mine = my_rows(scale_one)
    inner_mine = my_rows(inner_one.reshape(t, 1))
    grad_inputs = grad_middle_block + scale_mine * (e * gain_attn) - inputs.astype(F32) * (
        scale_mine**3 * inner_mine / D
    )

    grad_b_down = jnp.sum(g.astype(F32), axis=0)
    vectors = jnp.concatenate(
        [
            flip_dim(grad_gain_attn, "col", 0),
            flip_dim(grad_gain_mlp, "col", 0),
            flip_dim(grad_b_down, "col", 0),
            flip_dim(grad_b_up, "row", 0),
            grad_query_scale,
        ]
    )
    vectors = lax.psum(vectors, ("z", "core", "row", "col"))
    mine_col = lambda at: lax.dynamic_slice_in_dim(vectors, at * D + c * feat, feat, 0)
    units = b_up.shape[0]
    return (
        layer_out,
        grad_inputs,
        mine_col(0),
        sum_qkv,
        vectors[4 * D :],
        sum_out,
        mine_col(1),
        sum_up,
        lax.dynamic_slice_in_dim(vectors, 3 * D + r * units, units, 0),
        sum_down,
        mine_col(2),
    )


SMEM = pl.BlockSpec(memory_space=pltpu.SMEM)
ANY = pl.BlockSpec(memory_space=pl.ANY)


def call(kernel, name, args, specs, outs, scratch=(), limit=VMEM_LIMIT, out_specs=None):
    more = {} if out_specs is None else {"out_specs": out_specs}
    return pl.pallas_call(
        kernel,
        in_specs=specs,
        **more,
        out_shape=outs,
        scratch_shapes=list(scratch),
        compiler_params=pltpu.CompilerParams(vmem_limit_bytes=limit),
        cost_estimate=CHEAP,
        name=name,
    )(*args)


VM = pl.BlockSpec(memory_space=pltpu.VMEM)
HBM = pl.BlockSpec(memory_space=pltpu.HBM)


def shape(dims, kind):
    return jax.ShapeDtypeStruct(dims, kind)


def project_kernel(
    at, x00, x01, x10, x11, gain, factor, w_mine, w_a, w_b, qkv, raw, normed, scale_own, w_full
):
    r, k = at[0], at[2]
    tok, feat = x00.shape
    hr = w_mine.shape[1]
    half = hr // 2
    for s in range(3):
        w_full[pl.ds(s * hr, hr), 0:feat] = w_mine[s]
        w_full[pl.ds(pl.multiple_of(s * hr + k * half, 16), half), feat:] = w_a[s]
        w_full[pl.ds(pl.multiple_of(s * hr + (1 - k) * half, 16), half), feat:] = w_b[s]
    for i, (a_ref, b_ref) in enumerate(((x00, x01), (x10, x11))):
        a, b = a_ref[...].astype(F32), b_ref[...].astype(F32)
        total = jnp.sum(a * a, axis=1, keepdims=True) + jnp.sum(b * b, axis=1, keepdims=True)
        scale = lax.rsqrt(total / (2 * feat) + EPS)
        if i == 0:
            scale_own[...] = scale
        rows = pl.ds(pl.multiple_of((r ^ i) * tok, tok), tok)
        normed[rows, 0:feat] = (a * scale * gain[:, 0:feat]).astype(BF)
        normed[rows, feat:] = (b * scale * gain[:, feat:]).astype(BF)
        y = normed[rows, :]
        q = dot(w_full[0:hr, :], y, (1, 1))
        raw[:, rows] = q
        qkv[0, :, rows] = (q * factor[...]).astype(BF)
        qkv[1, :, rows] = dot(w_full[hr : 2 * hr, :], y, (1, 1)).astype(BF)
        qkv[2, :, rows] = dot(w_full[2 * hr : 3 * hr, :], y, (1, 1)).astype(BF)


def feed_kernel(
    at, gain, bias_up, bias_down, a, x_own, x_col, g_own, g_col,
    w_out, w_up, w_down, hx, hy, d0, d1, hx2, hy2, d02, d12,
    out_own, gm_own, post, ts, vectors, att, hidden_out, normed_out, g_out, pre_out, branch_out,
    w, x_ref, sems, more_sems,
):
    r, c, k = at[0], at[1], at[2]
    _, hr, share = a.shape
    feat = x_own.shape[1]
    half = feat // 2
    first = d0.shape[1]
    rows = pl.ds(pl.multiple_of(c * share, share), share)

    def start(pairs, sem):
        copies = [pltpu.make_async_copy(src, dst, sem.at[m]) for m, (src, dst) in enumerate(pairs)]
        for copy in copies:
            copy.start()
        return copies

    def place(s):
        return pl.ds(pl.multiple_of(((s // 2) ^ r) * 2 * hr + (s % 2) * hr, 16), hr)

    small = [(a.at[s], att.at[place(s), :]) for s in range(4)]
    small += [(x_own.at[rows, :], x_ref.at[:, 0:feat]), (x_col.at[rows, :], x_ref.at[:, feat:])]
    small += [(g_own.at[rows, :], g_out.at[:, 0:feat]), (g_col, g_out.at[:, feat:])]
    small = start(small, more_sems)
    copies = []
    for n, shard in enumerate((w_out, w_up, w_down)):
        rx, cx, ry, cy = (0, feat, feat, 0) if n == 1 else (feat, 0, 0, feat)
        mine = [(shard, w.at[n, 0:feat, 0:feat])]
        for core, (px, py, p0, p1) in ((k, (hx, hy, d0, d1)), (1 - k, (hx2, hy2, d02, d12))):
            down = core * half
            at_x = pl.ds(pl.multiple_of(rx + down, 16), half)
            at_y = pl.ds(pl.multiple_of(ry + down, 16), half)
            at_0 = pl.ds(pl.multiple_of(feat + down, 16), first)
            at_1 = pl.ds(pl.multiple_of(feat + down + first, 16), half - first)
            mine.append((px.at[n], w.at[n, at_x, cx : cx + feat]))
            mine.append((py.at[n], w.at[n, at_y, cy : cy + feat]))
            mine.append((p0.at[n], w.at[n, at_0, feat : 2 * feat]))
            mine.append((p1.at[n], w.at[n, at_1, feat : 2 * feat]))
        copies.append(start(mine, sems.at[n]))

    for copy in small + copies[0]:
        copy.wait()
    middle = x_ref[...].astype(F32) + dot(att[...], w[0], (0, 0))
    scale = lax.rsqrt(jnp.sum(middle * middle, axis=1, keepdims=True) / D + EPS)
    normed = (middle * scale * gain[...]).astype(BF)
    normed_out[...] = normed
    for copy in copies[1]:
        copy.wait()
    pre = dot(normed, w[1], (1, 0)) + bias_up[...]
    sig = jax.nn.sigmoid(pre)
    hidden = (pre * sig).astype(BF)
    hidden_out[...] = hidden
    for copy in copies[2]:
        copy.wait()
    result = (middle + dot(hidden, w[2], (1, 0)) + bias_down[...]).astype(BF)
    out_own[...] = result[:, :feat]
    post[0] = result[:, feat:]

    grad_pre_f = dot(g_out[...], w[2], (1, 1)) * sig * (1.0 + pre * (1.0 - sig))
    grad_pre = grad_pre_f.astype(BF)
    pre_out[...] = grad_pre
    grad_normed = dot(grad_pre, w[1], (1, 1))
    weighted = grad_normed * gain[...]
    inner = jnp.sum(weighted * middle, axis=1, keepdims=True)
    gf = g_out[...].astype(F32)
    grad_middle = gf + scale * weighted - middle * (scale * scale * scale * inner / D)
    gm_own[...] = grad_middle[:, :feat]
    post[1] = grad_middle[:, feat:].astype(BF)
    branch = grad_middle.astype(BF)
    branch_out[...] = branch
    for s in range(4):
        ts[s] = dot(w[0, place(s), :], branch, (1, 1)).astype(BF)
    vectors[...] = jnp.concatenate(
        [
            jnp.sum(grad_normed * (middle * scale), axis=0, keepdims=True),
            jnp.sum(gf, axis=0, keepdims=True),
            jnp.sum(grad_pre.astype(F32), axis=0, keepdims=True),
        ],
        axis=0,
    )


def feed_weights_kernel(at, att, hidden, normed, g, grad_pre, branch, *rest):
    *grads, stage, turned, sems = rest
    k = at[2]
    feat = g.shape[1] // 2
    half = feat // 2
    quarter = half // 2
    copies = []

    def weight_grad(n, left_ref, right):
        for core, begin in ((k, 0), (1 - k, 8)):
            up, low = (begin + 4, begin) if n == 1 else (begin, begin + 4)
            for b in range(2):
                part = pl.ds(pl.multiple_of(b * feat + core * half, 16), half)
                y = dot(left_ref[part, :], right, (1, 0)).astype(BF)
                for j in range(2):
                    cut = slice(j * feat, (j + 1) * feat)
                    for to, value in ((up + 2 * j + (1 - b), y[:quarter, cut]), (low + 2 * b + (1 - j), y[quarter:, cut])):
                        stage[to, n] = value
                        copy = pltpu.make_async_copy(stage.at[to, n], grads[to].at[n], sems.at[to, n])
                        copy.start()
                        copies.append(copy)

    turned[0] = hidden[...].astype(F32).T.astype(BF)
    weight_grad(2, turned.at[0], g[...])
    turned[1] = normed[...].astype(F32).T.astype(BF)
    weight_grad(1, turned.at[1], grad_pre[...])
    weight_grad(0, att, branch[...])
    for copy in copies:
        copy.wait()


def weight_back_kernel(at, grad, normed, keep, give):
    k = at[2]
    part = keep.shape[2]
    feat = keep.shape[3]
    for ref, core in ((give, 1 - k), (keep, k)):
        for s in range(3):
            rows = pl.ds(pl.multiple_of(core * part, 16), part)
            y = dot(grad[s, rows, :], normed[...], (1, 0)).astype(BF)
            ref[0, s] = y[:, :feat]
            ref[1, s] = y[:, feat:]


def project_back_kernel(
    at, grad, w_full, x00, x01, x10, x11, gain, vectors, scale_grad, es
):
    r, c = at[0], at[1]
    tok, feat = x00.shape
    sums = [jnp.zeros((1, feat), F32), jnp.zeros((1, feat), F32)]
    inners = []
    for i, xs in enumerate(((x00, x01), (x10, x11))):
        rows = pl.ds(pl.multiple_of((r ^ i) * tok, tok), tok)
        left = grad[:, rows]
        products, squares, inner = [], 0.0, 0.0
        for j in range(2):
            cut = slice(j * feat, (j + 1) * feat)
            e = dot(left, w_full[:, cut], (0, 0))
            x = xs[j][...].astype(F32)
            product = e * x
            inner = inner + jnp.sum(product * gain[:, cut], axis=1, keepdims=True)
            squares = squares + jnp.sum(x * x, axis=1, keepdims=True)
            es[2 * (r ^ i) + (c ^ j), 0:tok, :] = e.astype(BF)
            products.append(product)
        scale = lax.rsqrt(squares / (2 * feat) + EPS)
        for j in range(2):
            sums[j] += jnp.sum(products[j] * scale, axis=0, keepdims=True)
        line = jnp.broadcast_to(inner, (tok, 128)).T[0:1, :]
        high = line.astype(BF).astype(F32)
        inners.append(jnp.concatenate([high, line - high], axis=0))
    rows = []
    pairs = [(sums[0], sums[1], c)]
    pairs += [(vectors[n : n + 1, :feat], vectors[n : n + 1, feat:], (c, c, r)[n]) for n in range(3)]
    for own, other, place in pairs:
        rows += [jnp.where(place == 0, own, other), jnp.where(place == 0, other, own)]
    rows = jnp.concatenate(rows + [scale_grad[...], jnp.zeros((5, feat), F32)], axis=0)
    for i in range(2):
        inner = jnp.concatenate([inners[i], jnp.zeros((2, feat - tok), F32)], axis=1)
        extra = jnp.concatenate([inner, rows], axis=0).astype(BF)
        for j in range(2):
            es[2 * (r ^ i) + (c ^ j), tok:, :] = extra


def finish_qkv_kernel(at, mine, theirs, mine2, theirs2, out, rows):
    c, k = at[1], at[2]
    half = mine.shape[1]
    for s in range(3):
        for ref, col, core in ((mine, c, k), (theirs, 1 - c, k), (mine2, c, 1 - k), (theirs2, 1 - c, 1 - k)):
            rows[pl.ds(pl.multiple_of((2 * col + core) * half, 16), half), :] = ref[s].astype(F32)
        out[s] = rows[...].T


def finish_feed_kernel(at, a, b, a2, b2, *outs):
    k = at[2]
    quarter = a.shape[1]
    for n, out in enumerate(outs):
        upper, lower = ((b, b2), (a, a2)) if n == 1 else ((a, a2), (b, b2))
        for i, core in ((0, k), (1, 1 - k)):
            for j, refs in enumerate((upper, lower)):
                to = pl.multiple_of((2 * core + j) * quarter, 16)
                out[pl.ds(to, quarter), :] = refs[i][n].astype(F32)


together = lax.optimization_barrier


def after(x, *earlier):
    return lax.optimization_barrier((x, *earlier))[0]


def add(*parts):
    total = parts[0].astype(F32)
    for part in parts[1:]:
        total = total + part.astype(F32)
    return total.astype(BF)


def all_four(x):
    return lax.all_to_all(x, ("row", "col"), 0, 0, tiled=True)


def z_swap(x, step):
    n = size("z")
    return lax.ppermute(x, "z", [(i, i ^ step) for i in range(n)])


def z_first():
    z = lax.axis_index("z")
    return (z == 0) | (z == 3)


def body_four(
    inputs, gain_attn, w_qkv, query_scale, w_out, gain_mlp, w_up, b_up, w_down, b_down, series_ids, pad_mask, cotangent
):
    tok, feat = inputs.shape
    share = tok // 2
    t = series_ids.shape[0]
    hr = w_qkv.shape[2] // 2
    heads = hr // HEAD_DIM
    half = feat // 2
    r, c, k = lax.axis_index("row"), lax.axis_index("col"), lax.axis_index("core")
    at = jnp.stack([r, c, k, 2 * r + c]).astype(jnp.int32)
    mine_rows = lambda y, part: lax.dynamic_slice_in_dim(y, part * share, share, 0)

    few = heads // 2
    quarter = half // 2
    first_rows = (half * 7 // 20) // 16 * 16
    x01 = swap(inputs, "col")
    x10 = swap(inputs, "row")
    small = swap(jnp.concatenate([gain_attn, gain_mlp, b_down.astype(F32)]), "col")
    up_other = swap(b_up.astype(F32), "row")
    w_turned = jnp.transpose(w_qkv, (1, 2, 0)).reshape(3, 2, hr, feat)
    w_mine = lax.dynamic_index_in_dim(w_turned, c, 1, keepdims=False)
    w_give = lax.dynamic_index_in_dim(w_turned, 1 - c, 1, keepdims=False)
    w_half = core_half(w_give, 1)
    w_a = swap(w_half, "col")
    part = jnp.stack([core_half(w_out, 0), core_half(w_up, 0), core_half(w_down, 0)])
    g_give = mine_rows(cotangent, 1 - c)
    x01, x10, small, up_other, part, g_give, w_mine = lax.optimization_barrier(
        (x01, x10, small, up_other, part, g_give, w_mine)
    )
    x11 = swap(after(x01, w_half), "row")
    w_b = swap(w_a, "core")
    gain_one = jnp.concatenate([gain_attn, small[:feat]]).reshape(1, D)
    gain_two = jnp.concatenate([gain_mlp, small[feat : 2 * feat]]).reshape(1, D)
    bias_down = jnp.concatenate([b_down.astype(F32), small[2 * feat :]]).reshape(1, D)
    bias_up = jnp.concatenate([b_up.astype(F32), up_other]).reshape(1, D)
    factor = QUERY_CONST / math.sqrt(HEAD_DIM) * jax.nn.softplus(query_scale)
    factor_col = factor.reshape(HEAD_DIM, 1)

    part = after(part, x11, w_a)
    hx, hy = swap(part, "row"), swap(part, "col")
    hx2, hy2 = swap(hx, "core"), swap(hy, "core")
    qkv, raw, normed_one, scale_own, w_full = call(
        project_kernel,
        "project",
        (at, inputs, x01, x10, x11, gain_one, jnp.tile(factor_col, (heads, 1)), w_mine, w_a, w_b),
        [SMEM] + [VM] * 9,
        [
            shape((3, hr, t), BF),
            shape((hr, t), F32),
            shape((t, D), BF),
            shape((tok, 1), F32),
            shape((3 * hr, D), BF),
        ],
        limit=VMEM_LARGE,
    )
    qkv = qkv.reshape(3, heads, HEAD_DIM, t)
    masks = mask_args(series_ids, pad_mask)
    attended, lse, a = attention_forward(at, qkv, masks, pieces=1)
    a = all_four(a.reshape(4, hr, share))
    hx_on, hy_on, g_give = lax.optimization_barrier((hx, hy, g_give, lse))[:3]
    d0 = swap(hx_on[:, :first_rows], "col")
    d1 = swap(hy_on[:, first_rows:], "row")
    g_col = swap(g_give, "col")
    d0, d1, g_col, a = together((d0, d1, g_col, a))
    d02, d12 = swap(d0, "core"), swap(d1, "core")
    out_own, gm_own, post, ts, vectors, *factors = call(
        feed_kernel,
        "feed_forward",
        (at, gain_two, bias_up, bias_down, a, inputs, x01, cotangent, g_col)
        + (w_out, w_up, w_down, hx, hy, d0, d1, hx2, hy2, d02, d12),
        [SMEM] + [VM] * 3 + [HBM] * 16,
        [
            shape((share, feat), BF),
            shape((share, feat), F32),
            shape((2, share, feat), BF),
            shape((4, hr, share), BF),
            shape((3, D), F32),
            shape((D, share), BF),
        ]
        + [shape((share, D), BF)] * 5,
        scratch=[
            pltpu.VMEM((3, D, D), BF),
            pltpu.VMEM((share, D), BF),
            pltpu.SemaphoreType.DMA((3, 9)),
            pltpu.SemaphoreType.DMA((8,)),
        ],
        limit=VMEM_LARGE,
    )
    grads = call(
        feed_weights_kernel,
        "feed_weights",
        (at, *factors),
        [SMEM] + [VM] * 6,
        [shape((3, quarter, feat), BF)] * 16,
        scratch=[
            pltpu.VMEM((16, 3, quarter, feat), BF),
            pltpu.VMEM((2, D, share), BF),
            pltpu.SemaphoreType.DMA((16, 3)),
        ],
        out_specs=[HBM] * 16,
        limit=VMEM_LARGE,
    )
    ts = all_four(ts)
    others = grads[8:]
    over = lambda n: swap(others[n], "core")
    grads, osx0, osx1, osy0, osy1 = grads[:8], over(0), over(2), over(4), over(6)
    sx0, kx0, sx1, kx1, sy0, ky0, sy1, ky1 = grads
    sx1, sy1 = add(sx1, osx1), add(sy1, osy1)
    ox0, ox1, oy0, oy1 = over(1), over(3), over(5), over(7)
    sx0, sy0 = add(sx0, osx0), add(sy0, osy0)
    ts, sx1, sy1, sx0, sy0 = together((ts, sx1, sy1, sx0, sy0))
    rx1, ry1 = swap(sx1, "row"), swap(sy1, "col")
    rx0, ry0 = swap(sx0, "row"), swap(sy0, "col")
    ts = ts.reshape(4, heads, HEAD_DIM, share)
    raw = raw.reshape(heads, HEAD_DIM, t)

    grad_proj, gscale = attention_backward(at, qkv, raw, factor_col, attended, ts, lse, masks)
    grad_proj = grad_proj.reshape(3, hr, t)
    kept, sent = call(
        weight_back_kernel,
        "weight_back",
        (at, grad_proj, normed_one),
        [SMEM] + [VM] * 2,
        [shape((2, 3, hr // 2, feat), BF)] * 2,
    )
    sent, rx1, ry1, rx0, ry0, ox0, ox1, oy0, oy1 = together((sent, rx1, ry1, rx0, ry0, ox0, ox1, oy0, oy1))
    got = swap(sent, "core")
    px1, py1 = add(kx1, ox1, rx1), add(ky1, oy1, ry1)
    qx, qy = swap(px1, "col"), swap(py1, "row")
    w_pair = add(kept, got)
    first = z_first()
    got_w = z_swap(jnp.where(first, w_pair[1], w_pair[0]), 1)
    slope = QUERY_CONST / math.sqrt(HEAD_DIM) * jax.nn.sigmoid(query_scale)
    grad_query_scale = jnp.sum(gscale, axis=(0, 2)) * slope
    scale_grad = jnp.pad(grad_query_scale, (0, feat - HEAD_DIM)).reshape(1, feat)
    es = call(
        project_back_kernel,
        "project_back",
        (at, after(grad_proj, w_pair, px1, py1).reshape(3 * hr, t), w_full, inputs, x01, x10, x11, gain_one, vectors, scale_grad),
        [SMEM] + [VM] * 9,
        shape((4, tok + 16, feat), BF),
    )
    kx0, ky0 = together((kx0, ky0, es))[:2]
    fx0 = kx0.astype(F32) + ox0.astype(F32) + rx0.astype(F32)
    fy0 = ky0.astype(F32) + oy0.astype(F32) + ry0.astype(F32)
    qx, qy, got_w, w_pair, es, fx0, fy0 = together((qx, qy, got_w, w_pair, es, fx0, fy0))

    mine_w = add(jnp.where(first, w_pair[0], w_pair[1]), got_w)
    met_w = z_swap(mine_w, 3)
    fx, fy = add(fx0, qx), add(fy0, qy)
    got_c = z_swap(jnp.where(first, fy, fx), 1)
    es = all_four(after(es, fx, fy, mine_w))
    met_w, mine_w, got_c, fx, fy, post = together((met_w, mine_w, got_c, fx, fy, post))

    mine_w = add(mine_w, met_w)
    other_w = z_swap(mine_w, 1)
    w_own, w_theirs = jnp.where(first, mine_w, other_w), jnp.where(first, other_w, mine_w)
    mine_c = add(jnp.where(first, fx, fy), got_c)
    met_c = z_swap(mine_c, 3)
    post = swap(post, "col")
    w_theirs = swap(w_theirs, "col")
    total = jnp.sum(es[:, tok + 2 : tok + 11].astype(F32), axis=0)
    total = total + swap(total, "core")
    total = total + z_swap(total, 1)
    total = total + z_swap(total, 2)
    met_c, mine_c, w_own, w_theirs, post, total = together((met_c, mine_c, w_own, w_theirs, post, total))
    mine_c = add(mine_c, met_c)
    other_c = z_swap(mine_c, 1)
    w_args = (at, w_own, w_theirs, swap(w_own, "core"), swap(w_theirs, "core"))
    sum_qkv = call(
        finish_qkv_kernel,
        "finish_qkv",
        w_args,
        [SMEM] + [VM] * 4,
        shape((3, feat, 2 * hr), F32),
        scratch=[pltpu.VMEM((2 * hr, feat), F32)],
    )
    sum_qkv = jnp.transpose(sum_qkv, (1, 0, 2))

    e = jnp.sum(es[:, :tok].astype(F32), axis=0)
    inner = jnp.sum(es[:, tok : tok + 2, :tok].astype(F32), axis=(0, 1)).reshape(tok, 1)
    grad_middle = jnp.concatenate(flip([gm_own, post[1].astype(F32)], "col"), axis=0)
    grad_inputs = grad_middle + scale_own * (e * gain_attn) - inputs.astype(F32) * (scale_own**3 * inner / D)
    layer_out = jnp.concatenate(flip([out_own, post[0]], "col"), axis=0)

    pick = lambda n, place: lax.dynamic_index_in_dim(total, 2 * n + place, 0, keepdims=False)
    mine_c = after(mine_c, sum_qkv, grad_inputs, layer_out, total)
    fx, fy = jnp.where(first, mine_c, other_c), jnp.where(first, other_c, mine_c)
    sum_out, sum_up, sum_down = call(
        finish_feed_kernel,
        "finish_feed",
        (at, fx, fy, swap(fx, "core"), swap(fy, "core")),
        [SMEM] + [VM] * 4,
        [shape((feat, feat), F32)] * 3,
        limit=24 * 1024 * 1024,
    )

    return (
        layer_out,
        grad_inputs,
        pick(0, c),
        sum_qkv,
        total[8, :HEAD_DIM],
        sum_out,
        pick(1, c),
        sum_up,
        pick(3, r),
        sum_down,
        pick(2, c),
    )


def solution(mesh):
    dp, rows, cols = mesh.shape["dp"], mesh.shape["row"], mesh.shape["col"]
    split = Mesh(mesh.devices.reshape(dp // 2, 2, rows, cols), ("z", "core", "row", "col"))
    tokens = P(("z", "core", "row"), "col")
    in_specs = (
        tokens,
        P("col"),
        P("col", None, "row"),
        P(),
        P("row", "col"),
        P("col"),
        P("col", "row"),
        P("row"),
        P("row", "col"),
        P("col"),
        P(("z", "core")),
        P(("z", "core")),
        tokens,
    )
    out_specs = (
        tokens,
        tokens,
        P("col"),
        P("col", None, "row"),
        P(),
        P("row", "col"),
        P("col"),
        P("col", "row"),
        P("row"),
        P("row", "col"),
        P("col"),
    )
    body = body_four if (dp, rows, cols) == (8, 2, 2) else body_any
    return jax.shard_map(body, mesh=split, in_specs=in_specs, out_specs=out_specs, check_vma=False)
```

```python
import functools
import math

import jax
import jax.numpy as jnp
from jax import lax
from jax.experimental import pallas as pl
from jax.experimental.pallas import tpu as pltpu
from jax.sharding import Mesh
from jax.sharding import PartitionSpec as P

D = 1280
HEAD_DIM = 80
EPS = 1e-06
QUERY_CONST = 1.442695041
MASKED = -1e30
BF = jnp.bfloat16
F32 = jnp.float32
VMEM_LIMIT = 60 * 1024 * 1024
CHUNK = 1024
VMEM_LARGE = 60 * 1024 * 1024
CHEAP = pl.CostEstimate(flops=1, bytes_accessed=1, transcendentals=0)


def size(axis):
    return lax.axis_size(axis)


def swap(x, axis):
    return lax.ppermute(x, axis, [(0, 1), (1, 0)])


def flip(blocks, axis):
    if size(axis) != 2:
        return list(blocks)
    first = lax.axis_index(axis) == 0
    a, b = blocks
    return [jnp.where(first, a, b), jnp.where(first, b, a)]


def flip_dim(x, axis, dim):
    if size(axis) != 2:
        return x
    return jnp.concatenate(flip(jnp.split(x, 2, axis=dim), axis), axis=dim)


def gather(x, axis):
    if size(axis) == 2:
        return [x, swap(x, axis)]
    whole = lax.all_gather(x, axis, axis=0, tiled=False)
    return [whole[i] for i in range(size(axis))]


def gather_grid(x):
    if size("row") != 2:
        return [gather(b, "col") for b in gather(x, "row")]
    along_row, along_col = swap(x, "row"), swap(x, "col")
    half = x.shape[0] // 2
    across = jnp.concatenate(
        [swap(along_row[:half], "col"), swap(along_col[half:], "row")], axis=0
    )
    return [[x, along_col], [along_row, across]]


def scatter_sum(x, axis, dim):
    if size(axis) != 2:
        return lax.psum_scatter(x, axis, scatter_dimension=dim, tiled=True)
    mine, theirs = jnp.split(x, 2, axis=dim)
    return (mine.astype(F32) + swap(theirs, axis).astype(F32)).astype(x.dtype)


def exchange(x, axis, split, join):
    if size(axis) != 2:
        return lax.all_to_all(x, axis, split, join, tiled=True)
    mine, theirs = jnp.split(x, 2, axis=split)
    return jnp.concatenate([mine, swap(theirs, axis)], axis=join)


def core_half(x, dim):
    return lax.dynamic_slice_in_dim(
        x, lax.axis_index("core") * (x.shape[dim] // 2), x.shape[dim] // 2, dim
    )


def weight_gather(w, row_dim):
    part = core_half(w, 0)
    blocks = gather_grid(part)
    if row_dim == 1:
        blocks = [list(b) for b in zip(*blocks)]
    mine = jnp.stack([jnp.concatenate(b, axis=1) for b in blocks])
    other = swap(mine, "core")
    first = lax.axis_index("core") == 0
    both = jnp.stack([jnp.where(first, mine, other), jnp.where(first, other, mine)], axis=1)
    return both.reshape(-1, both.shape[-1])


def weight_sum(g, row_dim):
    dim_axis = ("row", "col") if row_dim == 0 else ("col", "row")
    n0 = size(dim_axis[0])
    g = g.reshape(n0, 2, g.shape[0] // n0 // 2, g.shape[1])
    core = lax.axis_index("core")
    keep = lax.dynamic_index_in_dim(g, core, 1, keepdims=False)
    give = lax.dynamic_index_in_dim(g, 1 - core, 1, keepdims=False).astype(BF)
    part = (keep + swap(give, "core").astype(F32)).astype(BF)
    part = scatter_sum(part, dim_axis[0], 0)
    part = scatter_sum(part[0], dim_axis[1], 1)
    return z_sum(part)


def z_sum(part):
    total = lax.psum(part, "z")
    other = swap(total, "core")
    return flip_core(total, other)


def flip_core(total, other):
    first = lax.axis_index("core") == 0
    return jnp.concatenate(
        [jnp.where(first, total, other), jnp.where(first, other, total)], axis=-2
    ).astype(F32)


def dot(a, b, contract):
    return lax.dot_general(a, b, ((contract[0:1], contract[1:2]), ((), ())), preferred_element_type=F32)


def bias_block(series_row, series_col, key_pos, q0, k0, qb, kb, diagonal):
    q_pos = q0 + lax.broadcasted_iota(jnp.int32, (1, qb), 1)
    allowed = (series_col == series_row) & (key_pos <= q_pos)
    if diagonal:
        k_pos = k0 + lax.broadcasted_iota(jnp.int32, (kb, 1), 0)
        allowed = allowed | (k_pos == q_pos)
    return jnp.where(allowed, 0.0, MASKED)


def forward_kernel(block, at, qkv_ref, srow_ref, scol_ref, kpos_ref, out_ref, lse_ref, *rest):
    *pieces, bias_ref, krow_ref, s_ref = rest
    t = qkv_ref.shape[3]
    n = t // block
    krow_ref[...] = qkv_ref[1, 0].astype(F32).T.astype(BF)

    def bias_slot(j, i):
        return j * (j + 1) // 2 + i

    @pl.when(pl.program_id(0) == 0)
    def _():
        for j in range(n):
            for i in range(j + 1):
                keys = pl.ds(i * block, block)
                bias_ref[bias_slot(j, i)] = bias_block(
                    srow_ref[:, j * block : (j + 1) * block],
                    scol_ref[keys, :],
                    kpos_ref[keys, :],
                    j * block,
                    i * block,
                    block,
                    block,
                    i == j,
                )

    for j in range(n):
        cols = slice(j * block, (j + 1) * block)
        q = qkv_ref[0, 0, :, cols]
        top = None
        for i in range(j + 1):
            s = dot(krow_ref[i * block : (i + 1) * block, :], q, (1, 0)) + bias_ref[bias_slot(j, i)]
            s_ref[i * block : (i + 1) * block, :] = s
            here = jnp.max(s, axis=0, keepdims=True)
            top = here if top is None else jnp.maximum(top, here)
        total = jnp.zeros((1, block), F32)
        acc = jnp.zeros((HEAD_DIM, block), F32)
        for i in range(j + 1):
            p = jnp.exp(s_ref[i * block : (i + 1) * block, :] - top)
            total += jnp.sum(p, axis=0, keepdims=True)
            acc += dot(qkv_ref[2, 0, :, i * block : (i + 1) * block], p.astype(BF), (1, 0))
        found = (acc / total).astype(BF)
        out_ref[0, :, cols] = found
        if pieces:
            pieces[0][j, 0] = found
        lse_ref[0, :, cols] = top + jnp.log(total)


def backward_kernel(
    block, at, qkv_ref, raw_ref, factor_ref, out_ref, lse_ref, srow_ref, scol_ref, kpos_ref, *rest
):
    piece, grad_ref, gscale_ref, bias_ref, krow_ref, vrow_ref, gk_ref, gv_ref, gout_ref = rest
    wide = piece.shape[3]
    for j in range(piece.shape[0]):
        gout_ref[:, j * wide : (j + 1) * wide] = piece[j, 0]
    t = qkv_ref.shape[3]
    n = t // block
    krow_ref[...] = qkv_ref[1, 0].astype(F32).T.astype(BF)
    vrow_ref[...] = qkv_ref[2, 0].astype(F32).T.astype(BF)

    def bias_slot(j, i):
        return j * (j + 1) // 2 + i

    @pl.when(pl.program_id(0) == 0)
    def _():
        for j in range(n):
            for i in range(j + 1):
                keys = pl.ds(i * block, block)
                bias_ref[bias_slot(j, i)] = bias_block(
                    srow_ref[:, j * block : (j + 1) * block],
                    scol_ref[keys, :],
                    kpos_ref[keys, :],
                    j * block,
                    i * block,
                    block,
                    block,
                    i == j,
                )

    gscale = jnp.zeros((HEAD_DIM, 1), F32)
    for j in range(n):
        cols = slice(j * block, (j + 1) * block)
        q = qkv_ref[0, 0, :, cols]
        go = gout_ref[:, cols]
        lse = lse_ref[0, :, cols]
        delta = jnp.sum(go.astype(F32) * out_ref[0, :, cols].astype(F32), axis=0, keepdims=True)
        gq = jnp.zeros((HEAD_DIM, block), F32)
        step = max(1, CHUNK // block)
        for i in range(0, j + 1, step):
            many = min(step, j + 1 - i)
            keys = slice(i * block, (i + many) * block)
            slot = bias_slot(j, i)
            bias = bias_ref[slot : slot + many].reshape(many * block, block)
            p = jnp.exp(dot(krow_ref[keys, :], q, (1, 0)) + bias - lse)
            gp = dot(vrow_ref[keys, :], go, (1, 0))
            gs = (p * (gp - delta)).astype(BF)
            gq += dot(qkv_ref[1, 0, :, keys], gs, (1, 0))
            gk = dot(q, gs, (1, 1))
            gv = dot(go, p.astype(BF), (1, 1))
            before, last = slice(i * block, min(i + many, j) * block), slice(j * block, (j + 1) * block)
            old = (min(i + many, j) - i) * block
            if old:
                gk_ref[:, before] += gk[:, :old]
                gv_ref[:, before] += gv[:, :old]
            if i + many == j + 1:
                gk_ref[:, last] = gk[:, old:]
                gv_ref[:, last] = gv[:, old:]
        gscale += jnp.sum(gq * raw_ref[0, :, cols], axis=1, keepdims=True)
        grad_ref[0, 0, :, cols] = (gq * factor_ref[...]).astype(BF)
    grad_ref[1, 0] = gk_ref[...].astype(BF)
    grad_ref[2, 0] = gv_ref[...].astype(BF)
    gscale_ref[0] = gscale


def mask_args(series, padding):
    t = series.shape[0]
    pos = jnp.arange(t, dtype=jnp.int32)
    return series.reshape(1, t), series.reshape(t, 1), jnp.where(padding == 0, pos, t).reshape(t, 1)


def attention_forward(at, qkv, masks, pieces=0):
    _, heads, hd, t = qkv.shape
    block = min(256, t) if t <= 2048 else 512
    n = t // block
    whole = lambda shape: pl.BlockSpec(shape, lambda h: (0,) * len(shape))
    return pl.pallas_call(
        functools.partial(forward_kernel, block),
        grid=(heads,),
        in_specs=[
            pl.BlockSpec(memory_space=pltpu.SMEM),
            pl.BlockSpec((3, 1, hd, t), lambda h: (0, h, 0, 0)),
            whole((1, t)),
            whole((t, 1)),
            whole((t, 1)),
        ],
        out_specs=[
            pl.BlockSpec((1, hd, t), lambda h: (h, 0, 0)),
            pl.BlockSpec((1, 1, t), lambda h: (h, 0, 0)),
        ]
        + [pl.BlockSpec((n, 1, hd, block), lambda h: (0, h, 0, 0))] * pieces,
        out_shape=[
            jax.ShapeDtypeStruct((heads, hd, t), BF),
            jax.ShapeDtypeStruct((heads, 1, t), F32),
        ]
        + [jax.ShapeDtypeStruct((n, heads, hd, block), BF)] * pieces,
        scratch_shapes=[
            pltpu.VMEM((n * (n + 1) // 2, block, block), F32),
            pltpu.VMEM((t, hd), BF),
            pltpu.VMEM((t, block), F32),
        ],
        compiler_params=pltpu.CompilerParams(vmem_limit_bytes=VMEM_LARGE),
        cost_estimate=CHEAP,
        name="attention_forward",
    )(at, qkv, *masks)


def attention_backward(at, qkv, raw, factor, out, piece, lse, masks):
    _, heads, hd, t = qkv.shape
    block = min(256, t) if t <= 2048 else 512
    n = t // block
    whole = lambda shape: pl.BlockSpec(shape, lambda h: (0,) * len(shape))
    head = lambda wide=t: pl.BlockSpec((1, hd, wide), lambda h: (h, 0, 0))
    return pl.pallas_call(
        functools.partial(backward_kernel, block),
        grid=(heads,),
        in_specs=[
            pl.BlockSpec(memory_space=pltpu.SMEM),
            pl.BlockSpec((3, 1, hd, t), lambda h: (0, h, 0, 0)),
            head(),
            whole((hd, 1)),
            head(),
            pl.BlockSpec((1, 1, t), lambda h: (h, 0, 0)),
            whole((1, t)),
            whole((t, 1)),
            whole((t, 1)),
        ]
        + [pl.BlockSpec((piece.shape[0], 1, hd, piece.shape[3]), lambda h: (0, h, 0, 0))],
        out_specs=[
            pl.BlockSpec((3, 1, hd, t), lambda h: (0, h, 0, 0)),
            pl.BlockSpec((1, hd, 1), lambda h: (h, 0, 0)),
        ],
        out_shape=[
            jax.ShapeDtypeStruct((3, heads, hd, t), BF),
            jax.ShapeDtypeStruct((heads, hd, 1), F32),
        ],
        scratch_shapes=[
            pltpu.VMEM((n * (n + 1) // 2, block, block), F32),
            pltpu.VMEM((t, hd), BF),
            pltpu.VMEM((t, hd), BF),
            pltpu.VMEM((hd, t), F32),
            pltpu.VMEM((hd, t), F32),
            pltpu.VMEM((hd, t), BF),
        ],
        compiler_params=pltpu.CompilerParams(vmem_limit_bytes=VMEM_LARGE),
        cost_estimate=CHEAP,
        name="attention_backward",
    )(at, qkv, raw, factor, out, lse, *masks, piece)


def norm_scale(x):
    return lax.rsqrt(jnp.mean(x * x, axis=1, keepdims=True) + EPS)


def body_any(
    inputs, gain_attn, w_qkv, query_scale, w_out, gain_mlp, w_up, b_up, w_down, b_down, series_ids, pad_mask, cotangent
):
    rows, cols = size("row"), size("col")
    tok = inputs.shape[0]
    feat = inputs.shape[1]
    share = tok // cols
    t = series_ids.shape[0]
    head_rows = w_qkv.shape[2] // cols
    heads = head_rows // HEAD_DIM
    r, c = lax.axis_index("row"), lax.axis_index("col")

    blocks = gather_grid(inputs)
    strips = [jnp.concatenate(b, axis=1) for b in blocks]
    x_own = strips[0] if rows == 2 else lax.dynamic_index_in_dim(jnp.stack(strips), r, 0, keepdims=False)
    x_all = jnp.concatenate(flip(strips, "row"), axis=0)
    gain_one = jnp.concatenate(gather(gain_attn, "col"))
    gain_two = jnp.concatenate(gather(gain_mlp, "col"))
    bias_up = jnp.concatenate(gather(b_up, "row")).astype(F32)
    bias_down = jnp.concatenate(gather(b_down, "col")).astype(F32)

    w3 = jnp.transpose(w_qkv, (1, 0, 2)).reshape(3, feat, cols, head_rows)
    w_mine = lax.dynamic_index_in_dim(w3, c, 2, keepdims=False)
    w_give = lax.dynamic_index_in_dim(w3, 1 - c, 2, keepdims=False)
    w_half = swap(core_half(w_give, 1), "col")
    w_other = swap(w_half, "core")
    first = lax.axis_index("core") == 0
    w_full = jnp.concatenate(
        [w_mine, jnp.where(first, w_half, w_other), jnp.where(first, w_other, w_half)], axis=1
    )

    xf = x_all.astype(F32)
    scale_one = norm_scale(xf)
    normed_one = (xf * scale_one * gain_one).astype(BF)
    projected = jnp.einsum("td,sdh->sht", normed_one, w_full, preferred_element_type=F32)
    projected = projected.reshape(3, heads, HEAD_DIM, t)
    factor = QUERY_CONST / math.sqrt(HEAD_DIM) * jax.nn.softplus(query_scale)
    raw_q = projected[0]
    qkv = jnp.stack([raw_q * factor[None, :, None], projected[1], projected[2]]).astype(BF)
    masks = mask_args(series_ids, pad_mask)
    at = jnp.zeros((4,), jnp.int32)
    attended, lse = attention_forward(at, qkv, masks)

    def to_tokens(y):
        y = flip_dim(y.reshape(head_rows, rows, cols, share), "row", 1)
        y = flip_dim(y, "col", 2)
        y = exchange(y.reshape(1, head_rows, rows, cols, share), "row", 2, 0)
        y = exchange(y.reshape(rows, 1, head_rows, cols, share), "col", 3, 1)
        y = flip_dim(y.reshape(rows, cols, head_rows, share), "col", 1)
        return y.reshape(rows * cols * head_rows, share)

    def to_heads(y):
        y = flip_dim(y.reshape(rows, cols, head_rows, share), "col", 1)
        y = exchange(y.reshape(rows, cols, head_rows, 1, share), "col", 1, 3)
        y = exchange(y.reshape(rows, head_rows, 1, cols, share), "row", 0, 2)
        y = flip_dim(y.reshape(head_rows, rows, cols, share), "col", 2)
        return flip_dim(y, "row", 1).reshape(head_rows, t)

    w_out_all = weight_gather(w_out, 0)
    w_up_all = weight_gather(w_up, 1)
    w_down_all = weight_gather(w_down, 0)

    def my_share(y):
        return lax.dynamic_slice_in_dim(y, c * share, share, 0)

    att = to_tokens(attended.reshape(head_rows, t))
    x_mine = my_share(x_own).astype(F32)
    middle = x_mine + dot(att, w_out_all, (0, 0))
    scale_two = norm_scale(middle)
    normed_two = (middle * scale_two * gain_two).astype(BF)
    pre_act = dot(normed_two, w_up_all, (1, 0)) + bias_up
    sig = jax.nn.sigmoid(pre_act)
    hidden = (pre_act * sig).astype(BF)
    result = (middle + dot(hidden, w_down_all, (1, 0)) + bias_down).astype(BF)

    def to_block(y):
        mine, theirs = jnp.split(y, 2, axis=1)
        return jnp.concatenate(flip([mine, swap(theirs, "col")], "col"), axis=0)

    layer_out = to_block(result)

    g_give = lax.dynamic_slice_in_dim(cotangent, (1 - c) * share, share, 0)
    g = jnp.concatenate([my_share(cotangent), swap(g_give, "col")], axis=1)
    grad_w_down = dot(hidden, g, (0, 0))
    grad_hidden = dot(g, w_down_all, (1, 1))
    grad_pre_f = grad_hidden * sig * (1.0 + pre_act * (1.0 - sig))
    grad_pre = grad_pre_f.astype(BF)
    grad_b_up = jnp.sum(grad_pre.astype(F32), axis=0)
    grad_w_up = dot(normed_two, grad_pre, (0, 0))
    grad_normed_two = dot(grad_pre, w_up_all, (1, 1))
    weighted = grad_normed_two * gain_two
    inner = jnp.sum(weighted * middle, axis=1, keepdims=True)
    grad_middle = g.astype(F32) + scale_two * weighted - middle * (scale_two**3 * inner / D)
    grad_gain_mlp = jnp.sum(grad_normed_two * middle * scale_two, axis=0)
    grad_branch = grad_middle.astype(BF)
    grad_w_out = dot(att, grad_branch, (1, 0))
    grad_att = dot(w_out_all, grad_branch, (1, 1)).astype(BF)
    grad_attended = to_heads(grad_att).reshape(heads, HEAD_DIM, t)
    grad_middle_block = to_block(grad_middle)

    sum_down = weight_sum(grad_w_down, 0)
    sum_up = weight_sum(grad_w_up, 1)
    sum_out = weight_sum(grad_w_out, 0)

    grad_proj, gscale = attention_backward(
        at, qkv, raw_q, factor.reshape(HEAD_DIM, 1), attended, grad_attended[None], lse, masks
    )
    slope = QUERY_CONST / math.sqrt(HEAD_DIM) * jax.nn.sigmoid(query_scale)
    grad_query_scale = jnp.sum(gscale, axis=(0, 2)) * slope
    grad_proj = grad_proj.reshape(3, head_rows, t)
    grad_normed_one = jnp.einsum("sht,sdh->td", grad_proj, w_full, preferred_element_type=F32)
    weighted_one = grad_normed_one * gain_one
    inner_one = jnp.sum(weighted_one * xf, axis=1)
    grad_gain_attn = jnp.sum(grad_normed_one * xf * scale_one, axis=0)
    inner_one = lax.psum(inner_one, ("row", "col"))
    grad_w = jnp.einsum("td,sht->sdh", normed_one, grad_proj, preferred_element_type=F32)
    grad_w = grad_w.reshape(3, cols, 2, feat // 2, head_rows)
    core = lax.axis_index("core")
    keep = lax.dynamic_index_in_dim(grad_w, core, 2, keepdims=False)
    give = lax.dynamic_index_in_dim(grad_w, 1 - core, 2, keepdims=False).astype(BF)
    part = (keep + swap(give, "core").astype(F32)).astype(BF)
    part = jnp.concatenate(flip([part[:, 0], swap(part[:, 1], "col")], "col"), axis=2)
    sum_qkv = jnp.transpose(z_sum(part), (1, 0, 2))

    e = jnp.concatenate(flip(jnp.split(grad_normed_one.astype(BF), 2, axis=0), "row"), axis=0) if rows == 2 else (
        grad_normed_one.astype(BF)
    )
    e = scatter_sum(e, "row", 0)
    e = scatter_sum(e, "col", 1).astype(F32)
    my_rows = lambda y: lax.dynamic_slice_in_dim(y, r * tok, tok, 0)
    scale_mine = my_rows(scale_one)
    inner_mine = my_rows(inner_one.reshape(t, 1))
    grad_inputs = grad_middle_block + scale_mine * (e * gain_attn) - inputs.astype(F32) * (
        scale_mine**3 * inner_mine / D
    )

    grad_b_down = jnp.sum(g.astype(F32), axis=0)
    vectors = jnp.concatenate(
        [
            flip_dim(grad_gain_attn, "col", 0),
            flip_dim(grad_gain_mlp, "col", 0),
            flip_dim(grad_b_down, "col", 0),
            flip_dim(grad_b_up, "row", 0),
            grad_query_scale,
        ]
    )
    vectors = lax.psum(vectors, ("z", "core", "row", "col"))
    mine_col = lambda at: lax.dynamic_slice_in_dim(vectors, at * D + c * feat, feat, 0)
    units = b_up.shape[0]
    return (
        layer_out,
        grad_inputs,
        mine_col(0),
        sum_qkv,
        vectors[4 * D :],
        sum_out,
        mine_col(1),
        sum_up,
        lax.dynamic_slice_in_dim(vectors, 3 * D + r * units, units, 0),
        sum_down,
        mine_col(2),
    )


SMEM = pl.BlockSpec(memory_space=pltpu.SMEM)
ANY = pl.BlockSpec(memory_space=pl.ANY)


def call(kernel, name, args, specs, outs, scratch=(), limit=VMEM_LIMIT, out_specs=None):
    more = {} if out_specs is None else {"out_specs": out_specs}
    return pl.pallas_call(
        kernel,
        in_specs=specs,
        **more,
        out_shape=outs,
        scratch_shapes=list(scratch),
        compiler_params=pltpu.CompilerParams(vmem_limit_bytes=limit),
        cost_estimate=CHEAP,
        name=name,
    )(*args)


VM = pl.BlockSpec(memory_space=pltpu.VMEM)
HBM = pl.BlockSpec(memory_space=pltpu.HBM)


def shape(dims, kind):
    return jax.ShapeDtypeStruct(dims, kind)


def project_kernel(
    at, x00, x01, x10, x11, gain, factor, w_mine, w_a, w_b, qkv, raw, normed, scale_own, w_full
):
    r, k = at[0], at[2]
    tok, feat = x00.shape
    hr = w_mine.shape[1]
    half = hr // 2
    for s in range(3):
        w_full[pl.ds(s * hr, hr), 0:feat] = w_mine[s]
        w_full[pl.ds(pl.multiple_of(s * hr + k * half, 16), half), feat:] = w_a[s]
        w_full[pl.ds(pl.multiple_of(s * hr + (1 - k) * half, 16), half), feat:] = w_b[s]
    for i, (a_ref, b_ref) in enumerate(((x00, x01), (x10, x11))):
        a, b = a_ref[...].astype(F32), b_ref[...].astype(F32)
        total = jnp.sum(a * a, axis=1, keepdims=True) + jnp.sum(b * b, axis=1, keepdims=True)
        scale = lax.rsqrt(total / (2 * feat) + EPS)
        if i == 0:
            scale_own[...] = scale
        rows = pl.ds(pl.multiple_of((r ^ i) * tok, tok), tok)
        normed[rows, 0:feat] = (a * scale * gain[:, 0:feat]).astype(BF)
        normed[rows, feat:] = (b * scale * gain[:, feat:]).astype(BF)
        y = normed[rows, :]
        q = dot(w_full[0:hr, :], y, (1, 1))
        raw[:, rows] = q
        qkv[0, :, rows] = (q * factor[...]).astype(BF)
        qkv[1, :, rows] = dot(w_full[hr : 2 * hr, :], y, (1, 1)).astype(BF)
        qkv[2, :, rows] = dot(w_full[2 * hr : 3 * hr, :], y, (1, 1)).astype(BF)


def feed_kernel(
    at, gain, bias_up, bias_down, a, x_own, x_col, g_own, g_col,
    w_out, w_up, w_down, hx, hy, d0, d1, hx2, hy2, d02, d12,
    out_own, gm_own, post, ts, vectors, att, hidden_out, normed_out, g_out, pre_out, branch_out,
    w, x_ref, sems, more_sems,
):
    r, c, k = at[0], at[1], at[2]
    _, hr, share = a.shape
    feat = x_own.shape[1]
    half = feat // 2
    first = d0.shape[1]
    rows = pl.ds(pl.multiple_of(c * share, share), share)

    def start(pairs, sem):
        copies = [pltpu.make_async_copy(src, dst, sem.at[m]) for m, (src, dst) in enumerate(pairs)]
        for copy in copies:
            copy.start()
        return copies

    def place(s):
        return pl.ds(pl.multiple_of(((s // 2) ^ r) * 2 * hr + (s % 2) * hr, 16), hr)

    small = [(a.at[s], att.at[place(s), :]) for s in range(4)]
    small += [(x_own.at[rows, :], x_ref.at[:, 0:feat]), (x_col.at[rows, :], x_ref.at[:, feat:])]
    small += [(g_own.at[rows, :], g_out.at[:, 0:feat]), (g_col, g_out.at[:, feat:])]
    small = start(small, more_sems)
    copies = []
    for n, shard in enumerate((w_out, w_up, w_down)):
        rx, cx, ry, cy = (0, feat, feat, 0) if n == 1 else (feat, 0, 0, feat)
        mine = [(shard, w.at[n, 0:feat, 0:feat])]
        for core, (px, py, p0, p1) in ((k, (hx, hy, d0, d1)), (1 - k, (hx2, hy2, d02, d12))):
            down = core * half
            at_x = pl.ds(pl.multiple_of(rx + down, 16), half)
            at_y = pl.ds(pl.multiple_of(ry + down, 16), half)
            at_0 = pl.ds(pl.multiple_of(feat + down, 16), first)
            at_1 = pl.ds(pl.multiple_of(feat + down + first, 16), half - first)
            mine.append((px.at[n], w.at[n, at_x, cx : cx + feat]))
            mine.append((py.at[n], w.at[n, at_y, cy : cy + feat]))
            mine.append((p0.at[n], w.at[n, at_0, feat : 2 * feat]))
            mine.append((p1.at[n], w.at[n, at_1, feat : 2 * feat]))
        copies.append(start(mine, sems.at[n]))

    for copy in small + copies[0]:
        copy.wait()
    middle = x_ref[...].astype(F32) + dot(att[...], w[0], (0, 0))
    scale = lax.rsqrt(jnp.sum(middle * middle, axis=1, keepdims=True) / D + EPS)
    normed = (middle * scale * gain[...]).astype(BF)
    normed_out[...] = normed
    for copy in copies[1]:
        copy.wait()
    pre = dot(normed, w[1], (1, 0)) + bias_up[...]
    sig = jax.nn.sigmoid(pre)
    hidden = (pre * sig).astype(BF)
    hidden_out[...] = hidden
    for copy in copies[2]:
        copy.wait()
    result = (middle + dot(hidden, w[2], (1, 0)) + bias_down[...]).astype(BF)
    out_own[...] = result[:, :feat]
    post[0] = result[:, feat:]

    grad_pre_f = dot(g_out[...], w[2], (1, 1)) * sig * (1.0 + pre * (1.0 - sig))
    grad_pre = grad_pre_f.astype(BF)
    pre_out[...] = grad_pre
    grad_normed = dot(grad_pre, w[1], (1, 1))
    weighted = grad_normed * gain[...]
    inner = jnp.sum(weighted * middle, axis=1, keepdims=True)
    gf = g_out[...].astype(F32)
    grad_middle = gf + scale * weighted - middle * (scale * scale * scale * inner / D)
    gm_own[...] = grad_middle[:, :feat]
    post[1] = grad_middle[:, feat:].astype(BF)
    branch = grad_middle.astype(BF)
    branch_out[...] = branch
    for s in range(4):
        ts[s] = dot(w[0, place(s), :], branch, (1, 1)).astype(BF)
    vectors[...] = jnp.concatenate(
        [
            jnp.sum(grad_normed * (middle * scale), axis=0, keepdims=True),
            jnp.sum(gf, axis=0, keepdims=True),
            jnp.sum(grad_pre.astype(F32), axis=0, keepdims=True),
        ],
        axis=0,
    )


def feed_weights_kernel(at, att, hidden, normed, g, grad_pre, branch, *rest):
    *grads, stage, turned, sems = rest
    k = at[2]
    feat = g.shape[1] // 2
    half = feat // 2
    quarter = half // 2
    copies = []

    def weight_grad(n, left_ref, right):
        for core, begin in ((k, 0), (1 - k, 8)):
            up, low = (begin + 4, begin) if n == 1 else (begin, begin + 4)
            for b in range(2):
                part = pl.ds(pl.multiple_of(b * feat + core * half, 16), half)
                y = dot(left_ref[part, :], right, (1, 0)).astype(BF)
                for j in range(2):
                    cut = slice(j * feat, (j + 1) * feat)
                    for to, value in ((up + 2 * j + (1 - b), y[:quarter, cut]), (low + 2 * b + (1 - j), y[quarter:, cut])):
                        stage[to, n] = value
                        copy = pltpu.make_async_copy(stage.at[to, n], grads[to].at[n], sems.at[to, n])
                        copy.start()
                        copies.append(copy)

    turned[0] = hidden[...].astype(F32).T.astype(BF)
    weight_grad(2, turned.at[0], g[...])
    turned[1] = normed[...].astype(F32).T.astype(BF)
    weight_grad(1, turned.at[1], grad_pre[...])
    weight_grad(0, att, branch[...])
    for copy in copies:
        copy.wait()


def weight_back_kernel(at, grad, normed, keep, give):
    k = at[2]
    part = keep.shape[2]
    feat = keep.shape[3]
    for ref, core in ((give, 1 - k), (keep, k)):
        for s in range(3):
            rows = pl.ds(pl.multiple_of(core * part, 16), part)
            y = dot(grad[s, rows, :], normed[...], (1, 0)).astype(BF)
            ref[0, s] = y[:, :feat]
            ref[1, s] = y[:, feat:]


def project_back_kernel(
    at, grad, w_full, x00, x01, x10, x11, gain, vectors, scale_grad, es
):
    r, c = at[0], at[1]
    tok, feat = x00.shape
    sums = [jnp.zeros((1, feat), F32), jnp.zeros((1, feat), F32)]
    inners = []
    for i, xs in enumerate(((x00, x01), (x10, x11))):
        rows = pl.ds(pl.multiple_of((r ^ i) * tok, tok), tok)
        left = grad[:, rows]
        products, squares, inner = [], 0.0, 0.0
        for j in range(2):
            cut = slice(j * feat, (j + 1) * feat)
            e = dot(left, w_full[:, cut], (0, 0))
            x = xs[j][...].astype(F32)
            product = e * x
            inner = inner + jnp.sum(product * gain[:, cut], axis=1, keepdims=True)
            squares = squares + jnp.sum(x * x, axis=1, keepdims=True)
            es[2 * (r ^ i) + (c ^ j), 0:tok, :] = e.astype(BF)
            products.append(product)
        scale = lax.rsqrt(squares / (2 * feat) + EPS)
        for j in range(2):
            sums[j] += jnp.sum(products[j] * scale, axis=0, keepdims=True)
        line = jnp.broadcast_to(inner, (tok, 128)).T[0:1, :]
        high = line.astype(BF).astype(F32)
        inners.append(jnp.concatenate([high, line - high], axis=0))
    rows = []
    pairs = [(sums[0], sums[1], c)]
    pairs += [(vectors[n : n + 1, :feat], vectors[n : n + 1, feat:], (c, c, r)[n]) for n in range(3)]
    for own, other, place in pairs:
        rows += [jnp.where(place == 0, own, other), jnp.where(place == 0, other, own)]
    rows = jnp.concatenate(rows + [scale_grad[...], jnp.zeros((5, feat), F32)], axis=0)
    for i in range(2):
        inner = jnp.concatenate([inners[i], jnp.zeros((2, feat - tok), F32)], axis=1)
        extra = jnp.concatenate([inner, rows], axis=0).astype(BF)
        for j in range(2):
            es[2 * (r ^ i) + (c ^ j), tok:, :] = extra


def finish_qkv_kernel(at, mine, theirs, mine2, theirs2, out, rows):
    c, k = at[1], at[2]
    half = mine.shape[1]
    for s in range(3):
        for ref, col, core in ((mine, c, k), (theirs, 1 - c, k), (mine2, c, 1 - k), (theirs2, 1 - c, 1 - k)):
            rows[pl.ds(pl.multiple_of((2 * col + core) * half, 16), half), :] = ref[s].astype(F32)
        out[s] = rows[...].T


def finish_feed_kernel(at, a, b, a2, b2, *outs):
    k = at[2]
    quarter = a.shape[1]
    for n, out in enumerate(outs):
        upper, lower = ((b, b2), (a, a2)) if n == 1 else ((a, a2), (b, b2))
        for i, core in ((0, k), (1, 1 - k)):
            for j, refs in enumerate((upper, lower)):
                to = pl.multiple_of((2 * core + j) * quarter, 16)
                out[pl.ds(to, quarter), :] = refs[i][n].astype(F32)


together = lax.optimization_barrier


def after(x, *earlier):
    return lax.optimization_barrier((x, *earlier))[0]


def add(*parts):
    total = parts[0].astype(F32)
    for part in parts[1:]:
        total = total + part.astype(F32)
    return total.astype(BF)


def all_four(x):
    return lax.all_to_all(x, ("row", "col"), 0, 0, tiled=True)


def z_swap(x, step):
    n = size("z")
    return lax.ppermute(x, "z", [(i, i ^ step) for i in range(n)])


def z_first():
    z = lax.axis_index("z")
    return (z == 0) | (z == 3)


def body_four(
    inputs, gain_attn, w_qkv, query_scale, w_out, gain_mlp, w_up, b_up, w_down, b_down, series_ids, pad_mask, cotangent
):
    tok, feat = inputs.shape
    share = tok // 2
    t = series_ids.shape[0]
    hr = w_qkv.shape[2] // 2
    heads = hr // HEAD_DIM
    half = feat // 2
    r, c, k = lax.axis_index("row"), lax.axis_index("col"), lax.axis_index("core")
    at = jnp.stack([r, c, k, 2 * r + c]).astype(jnp.int32)
    mine_rows = lambda y, part: lax.dynamic_slice_in_dim(y, part * share, share, 0)

    few = heads // 2
    quarter = half // 2
    first_rows = (half * 7 // 20) // 16 * 16
    x01 = swap(inputs, "col")
    x10 = swap(inputs, "row")
    small = swap(jnp.concatenate([gain_attn, gain_mlp, b_down.astype(F32)]), "col")
    up_other = swap(b_up.astype(F32), "row")
    w_turned = jnp.transpose(w_qkv, (1, 2, 0)).reshape(3, 2, hr, feat)
    w_mine = lax.dynamic_index_in_dim(w_turned, c, 1, keepdims=False)
    w_give = lax.dynamic_index_in_dim(w_turned, 1 - c, 1, keepdims=False)
    w_half = core_half(w_give, 1)
    w_a = swap(w_half, "col")
    part = jnp.stack([core_half(w_out, 0), core_half(w_up, 0), core_half(w_down, 0)])
    g_give = mine_rows(cotangent, 1 - c)
    x01, x10, small, up_other, part, g_give, w_mine = lax.optimization_barrier(
        (x01, x10, small, up_other, part, g_give, w_mine)
    )
    x11 = swap(after(x01, w_half), "row")
    w_b = swap(w_a, "core")
    gain_one = jnp.concatenate([gain_attn, small[:feat]]).reshape(1, D)
    gain_two = jnp.concatenate([gain_mlp, small[feat : 2 * feat]]).reshape(1, D)
    bias_down = jnp.concatenate([b_down.astype(F32), small[2 * feat :]]).reshape(1, D)
    bias_up = jnp.concatenate([b_up.astype(F32), up_other]).reshape(1, D)
    factor = QUERY_CONST / math.sqrt(HEAD_DIM) * jax.nn.softplus(query_scale)
    factor_col = factor.reshape(HEAD_DIM, 1)

    part = after(part, x11, w_a)
    hx, hy = swap(part, "row"), swap(part, "col")
    hx2, hy2 = swap(hx, "core"), swap(hy, "core")
    qkv, raw, normed_one, scale_own, w_full = call(
        project_kernel,
        "project",
        (at, inputs, x01, x10, x11, gain_one, jnp.tile(factor_col, (heads, 1)), w_mine, w_a, w_b),
        [SMEM] + [VM] * 9,
        [
            shape((3, hr, t), BF),
            shape((hr, t), F32),
            shape((t, D), BF),
            shape((tok, 1), F32),
            shape((3 * hr, D), BF),
        ],
        limit=VMEM_LARGE,
    )
    qkv = qkv.reshape(3, heads, HEAD_DIM, t)
    masks = mask_args(series_ids, pad_mask)
    attended, lse, a = attention_forward(at, qkv, masks, pieces=1)
    a = all_four(a.reshape(4, hr, share))
    hx_on, hy_on, g_give = lax.optimization_barrier((hx, hy, g_give, lse))[:3]
    d0 = swap(hx_on[:, :first_rows], "col")
    d1 = swap(hy_on[:, first_rows:], "row")
    g_col = swap(g_give, "col")
    d0, d1, g_col, a = together((d0, d1, g_col, a))
    d02, d12 = swap(d0, "core"), swap(d1, "core")
    out_own, gm_own, post, ts, vectors, *factors = call(
        feed_kernel,
        "feed_forward",
        (at, gain_two, bias_up, bias_down, a, inputs, x01, cotangent, g_col)
        + (w_out, w_up, w_down, hx, hy, d0, d1, hx2, hy2, d02, d12),
        [SMEM] + [VM] * 3 + [HBM] * 16,
        [
            shape((share, feat), BF),
            shape((share, feat), F32),
            shape((2, share, feat), BF),
            shape((4, hr, share), BF),
            shape((3, D), F32),
            shape((D, share), BF),
        ]
        + [shape((share, D), BF)] * 5,
        scratch=[
            pltpu.VMEM((3, D, D), BF),
            pltpu.VMEM((share, D), BF),
            pltpu.SemaphoreType.DMA((3, 9)),
            pltpu.SemaphoreType.DMA((8,)),
        ],
        limit=VMEM_LARGE,
    )
    grads = call(
        feed_weights_kernel,
        "feed_weights",
        (at, *factors),
        [SMEM] + [VM] * 6,
        [shape((3, quarter, feat), BF)] * 16,
        scratch=[
            pltpu.VMEM((16, 3, quarter, feat), BF),
            pltpu.VMEM((2, D, share), BF),
            pltpu.SemaphoreType.DMA((16, 3)),
        ],
        out_specs=[HBM] * 16,
        limit=VMEM_LARGE,
    )
    ts = all_four(ts)
    others = grads[8:]
    over = lambda n: swap(others[n], "core")
    grads, osx0, osx1, osy0, osy1 = grads[:8], over(0), over(2), over(4), over(6)
    sx0, kx0, sx1, kx1, sy0, ky0, sy1, ky1 = grads
    sx1, sy1 = add(sx1, osx1), add(sy1, osy1)
    ox0, ox1, oy0, oy1 = over(1), over(3), over(5), over(7)
    sx0, sy0 = add(sx0, osx0), add(sy0, osy0)
    ts, sx1, sy1, sx0, sy0 = together((ts, sx1, sy1, sx0, sy0))
    rx1, ry1 = swap(sx1, "row"), swap(sy1, "col")
    rx0, ry0 = swap(sx0, "row"), swap(sy0, "col")
    ts = ts.reshape(4, heads, HEAD_DIM, share)
    raw = raw.reshape(heads, HEAD_DIM, t)

    grad_proj, gscale = attention_backward(at, qkv, raw, factor_col, attended, ts, lse, masks)
    grad_proj = grad_proj.reshape(3, hr, t)
    kept, sent = call(
        weight_back_kernel,
        "weight_back",
        (at, grad_proj, normed_one),
        [SMEM] + [VM] * 2,
        [shape((2, 3, hr // 2, feat), BF)] * 2,
    )
    sent, rx1, ry1, rx0, ry0, ox0, ox1, oy0, oy1 = together((sent, rx1, ry1, rx0, ry0, ox0, ox1, oy0, oy1))
    got = swap(sent, "core")
    px1, py1 = add(kx1, ox1, rx1), add(ky1, oy1, ry1)
    qx, qy = swap(px1, "col"), swap(py1, "row")
    w_pair = add(kept, got)
    first = z_first()
    got_w = z_swap(jnp.where(first, w_pair[1], w_pair[0]), 1)
    slope = QUERY_CONST / math.sqrt(HEAD_DIM) * jax.nn.sigmoid(query_scale)
    grad_query_scale = jnp.sum(gscale, axis=(0, 2)) * slope
    scale_grad = jnp.pad(grad_query_scale, (0, feat - HEAD_DIM)).reshape(1, feat)
    es = call(
        project_back_kernel,
        "project_back",
        (at, after(grad_proj, w_pair, px1, py1).reshape(3 * hr, t), w_full, inputs, x01, x10, x11, gain_one, vectors, scale_grad),
        [SMEM] + [VM] * 9,
        shape((4, tok + 16, feat), BF),
    )
    kx0, ky0 = together((kx0, ky0, es))[:2]
    fx0 = kx0.astype(F32) + ox0.astype(F32) + rx0.astype(F32)
    fy0 = ky0.astype(F32) + oy0.astype(F32) + ry0.astype(F32)
    qx, qy, got_w, w_pair, es, fx0, fy0 = together((qx, qy, got_w, w_pair, es, fx0, fy0))

    mine_w = add(jnp.where(first, w_pair[0], w_pair[1]), got_w)
    met_w = z_swap(mine_w, 3)
    fx, fy = add(fx0, qx), add(fy0, qy)
    got_c = z_swap(jnp.where(first, fy, fx), 1)
    es = all_four(after(es, fx, fy, mine_w))
    met_w, mine_w, got_c, fx, fy, post = together((met_w, mine_w, got_c, fx, fy, post))

    mine_w = add(mine_w, met_w)
    other_w = z_swap(mine_w, 1)
    w_own, w_theirs = jnp.where(first, mine_w, other_w), jnp.where(first, other_w, mine_w)
    mine_c = add(jnp.where(first, fx, fy), got_c)
    met_c = z_swap(mine_c, 3)
    post = swap(post, "col")
    w_theirs = swap(w_theirs, "col")
    total = jnp.sum(es[:, tok + 2 : tok + 11].astype(F32), axis=0)
    total = total + swap(total, "core")
    total = total + z_swap(total, 1)
    total = total + z_swap(total, 2)
    met_c, mine_c, total = together((met_c, mine_c, total))
    mine_c = add(mine_c, met_c)
    other_c = z_swap(mine_c, 1)
    w_args = (at, w_own, w_theirs, swap(w_own, "core"), swap(w_theirs, "core"))
    sum_qkv = call(
        finish_qkv_kernel,
        "finish_qkv",
        w_args,
        [SMEM] + [VM] * 4,
        shape((3, feat, 2 * hr), F32),
        scratch=[pltpu.VMEM((2 * hr, feat), F32)],
    )
    sum_qkv = jnp.transpose(sum_qkv, (1, 0, 2))

    e = jnp.sum(es[:, :tok].astype(F32), axis=0)
    inner = jnp.sum(es[:, tok : tok + 2, :tok].astype(F32), axis=(0, 1)).reshape(tok, 1)
    grad_middle = jnp.concatenate(flip([gm_own, post[1].astype(F32)], "col"), axis=0)
    grad_inputs = grad_middle + scale_own * (e * gain_attn) - inputs.astype(F32) * (scale_own**3 * inner / D)
    layer_out = jnp.concatenate(flip([out_own, post[0]], "col"), axis=0)

    pick = lambda n, place: lax.dynamic_index_in_dim(total, 2 * n + place, 0, keepdims=False)
    mine_c = after(mine_c, sum_qkv, grad_inputs, layer_out, total)
    fx, fy = jnp.where(first, mine_c, other_c), jnp.where(first, other_c, mine_c)
    sum_out, sum_up, sum_down = call(
        finish_feed_kernel,
        "finish_feed",
        (at, fx, fy, swap(fx, "core"), swap(fy, "core")),
        [SMEM] + [VM] * 4,
        [shape((feat, feat), F32)] * 3,
        limit=24 * 1024 * 1024,
    )

    return (
        layer_out,
        grad_inputs,
        pick(0, c),
        sum_qkv,
        total[8, :HEAD_DIM],
        sum_out,
        pick(1, c),
        sum_up,
        pick(3, r),
        sum_down,
        pick(2, c),
    )


def solution(mesh):
    dp, rows, cols = mesh.shape["dp"], mesh.shape["row"], mesh.shape["col"]
    split = Mesh(mesh.devices.reshape(dp // 2, 2, rows, cols), ("z", "core", "row", "col"))
    tokens = P(("z", "core", "row"), "col")
    in_specs = (
        tokens,
        P("col"),
        P("col", None, "row"),
        P(),
        P("row", "col"),
        P("col"),
        P("col", "row"),
        P("row"),
        P("row", "col"),
        P("col"),
        P(("z", "core")),
        P(("z", "core")),
        tokens,
    )
    out_specs = (
        tokens,
        tokens,
        P("col"),
        P("col", None, "row"),
        P(),
        P("row", "col"),
        P("col"),
        P("col", "row"),
        P("row"),
        P("row", "col"),
        P("col"),
    )
    body = body_four if (dp, rows, cols) == (8, 2, 2) else body_any
    return jax.shard_map(body, mesh=split, in_specs=in_specs, out_specs=out_specs, check_vma=False)
```

```python
import functools
import math

import jax
import jax.numpy as jnp
from jax import lax
from jax.experimental import pallas as pl
from jax.experimental.pallas import tpu as pltpu
from jax.sharding import Mesh
from jax.sharding import PartitionSpec as P

D = 1280
HEAD_DIM = 80
EPS = 1e-06
QUERY_CONST = 1.442695041
MASKED = -1e30
BF = jnp.bfloat16
F32 = jnp.float32
VMEM_LIMIT = 60 * 1024 * 1024
CHUNK = 1024
VMEM_LARGE = 60 * 1024 * 1024
CHEAP = pl.CostEstimate(flops=1, bytes_accessed=1, transcendentals=0)


def size(axis):
    return lax.axis_size(axis)


def swap(x, axis):
    return lax.ppermute(x, axis, [(0, 1), (1, 0)])


def flip(blocks, axis):
    if size(axis) != 2:
        return list(blocks)
    first = lax.axis_index(axis) == 0
    a, b = blocks
    return [jnp.where(first, a, b), jnp.where(first, b, a)]


def flip_dim(x, axis, dim):
    if size(axis) != 2:
        return x
    return jnp.concatenate(flip(jnp.split(x, 2, axis=dim), axis), axis=dim)


def gather(x, axis):
    if size(axis) == 2:
        return [x, swap(x, axis)]
    whole = lax.all_gather(x, axis, axis=0, tiled=False)
    return [whole[i] for i in range(size(axis))]


def gather_grid(x):
    if size("row") != 2:
        return [gather(b, "col") for b in gather(x, "row")]
    along_row, along_col = swap(x, "row"), swap(x, "col")
    half = x.shape[0] // 2
    across = jnp.concatenate(
        [swap(along_row[:half], "col"), swap(along_col[half:], "row")], axis=0
    )
    return [[x, along_col], [along_row, across]]


def scatter_sum(x, axis, dim):
    if size(axis) != 2:
        return lax.psum_scatter(x, axis, scatter_dimension=dim, tiled=True)
    mine, theirs = jnp.split(x, 2, axis=dim)
    return (mine.astype(F32) + swap(theirs, axis).astype(F32)).astype(x.dtype)


def exchange(x, axis, split, join):
    if size(axis) != 2:
        return lax.all_to_all(x, axis, split, join, tiled=True)
    mine, theirs = jnp.split(x, 2, axis=split)
    return jnp.concatenate([mine, swap(theirs, axis)], axis=join)


def core_half(x, dim):
    return lax.dynamic_slice_in_dim(
        x, lax.axis_index("core") * (x.shape[dim] // 2), x.shape[dim] // 2, dim
    )


def weight_gather(w, row_dim):
    part = core_half(w, 0)
    blocks = gather_grid(part)
    if row_dim == 1:
        blocks = [list(b) for b in zip(*blocks)]
    mine = jnp.stack([jnp.concatenate(b, axis=1) for b in blocks])
    other = swap(mine, "core")
    first = lax.axis_index("core") == 0
    both = jnp.stack([jnp.where(first, mine, other), jnp.where(first, other, mine)], axis=1)
    return both.reshape(-1, both.shape[-1])


def weight_sum(g, row_dim):
    dim_axis = ("row", "col") if row_dim == 0 else ("col", "row")
    n0 = size(dim_axis[0])
    g = g.reshape(n0, 2, g.shape[0] // n0 // 2, g.shape[1])
    core = lax.axis_index("core")
    keep = lax.dynamic_index_in_dim(g, core, 1, keepdims=False)
    give = lax.dynamic_index_in_dim(g, 1 - core, 1, keepdims=False).astype(BF)
    part = (keep + swap(give, "core").astype(F32)).astype(BF)
    part = scatter_sum(part, dim_axis[0], 0)
    part = scatter_sum(part[0], dim_axis[1], 1)
    return z_sum(part)


def z_sum(part):
    total = lax.psum(part, "z")
    other = swap(total, "core")
    return flip_core(total, other)


def flip_core(total, other):
    first = lax.axis_index("core") == 0
    return jnp.concatenate(
        [jnp.where(first, total, other), jnp.where(first, other, total)], axis=-2
    ).astype(F32)


def dot(a, b, contract):
    return lax.dot_general(a, b, ((contract[0:1], contract[1:2]), ((), ())), preferred_element_type=F32)


def bias_block(series_row, series_col, key_pos, q0, k0, qb, kb, diagonal):
    q_pos = q0 + lax.broadcasted_iota(jnp.int32, (1, qb), 1)
    allowed = (series_col == series_row) & (key_pos <= q_pos)
    if diagonal:
        k_pos = k0 + lax.broadcasted_iota(jnp.int32, (kb, 1), 0)
        allowed = allowed | (k_pos == q_pos)
    return jnp.where(allowed, 0.0, MASKED)


def forward_kernel(block, at, qkv_ref, srow_ref, scol_ref, kpos_ref, out_ref, lse_ref, *rest):
    *pieces, bias_ref, krow_ref, s_ref = rest
    t = qkv_ref.shape[3]
    n = t // block
    krow_ref[...] = qkv_ref[1, 0].astype(F32).T.astype(BF)

    def bias_slot(j, i):
        return j * (j + 1) // 2 + i

    @pl.when(pl.program_id(0) == 0)
    def _():
        for j in range(n):
            for i in range(j + 1):
                keys = pl.ds(i * block, block)
                bias_ref[bias_slot(j, i)] = bias_block(
                    srow_ref[:, j * block : (j + 1) * block],
                    scol_ref[keys, :],
                    kpos_ref[keys, :],
                    j * block,
                    i * block,
                    block,
                    block,
                    i == j,
                )

    for j in range(n):
        cols = slice(j * block, (j + 1) * block)
        q = qkv_ref[0, 0, :, cols]
        top = None
        for i in range(j + 1):
            s = dot(krow_ref[i * block : (i + 1) * block, :], q, (1, 0)) + bias_ref[bias_slot(j, i)]
            s_ref[i * block : (i + 1) * block, :] = s
            here = jnp.max(s, axis=0, keepdims=True)
            top = here if top is None else jnp.maximum(top, here)
        total = jnp.zeros((1, block), F32)
        acc = jnp.zeros((HEAD_DIM, block), F32)
        for i in range(j + 1):
            p = jnp.exp(s_ref[i * block : (i + 1) * block, :] - top)
            total += jnp.sum(p, axis=0, keepdims=True)
            acc += dot(qkv_ref[2, 0, :, i * block : (i + 1) * block], p.astype(BF), (1, 0))
        found = (acc / total).astype(BF)
        out_ref[0, :, cols] = found
        if pieces:
            pieces[0][j, 0] = found
        lse_ref[0, :, cols] = top + jnp.log(total)


def backward_kernel(
    block, at, qkv_ref, raw_ref, factor_ref, out_ref, lse_ref, srow_ref, scol_ref, kpos_ref, *rest
):
    piece, grad_ref, gscale_ref, bias_ref, krow_ref, vrow_ref, gk_ref, gv_ref, gout_ref = rest
    wide = piece.shape[3]
    for j in range(piece.shape[0]):
        gout_ref[:, j * wide : (j + 1) * wide] = piece[j, 0]
    t = qkv_ref.shape[3]
    n = t // block
    krow_ref[...] = qkv_ref[1, 0].astype(F32).T.astype(BF)
    vrow_ref[...] = qkv_ref[2, 0].astype(F32).T.astype(BF)

    def bias_slot(j, i):
        return j * (j + 1) // 2 + i

    @pl.when(pl.program_id(0) == 0)
    def _():
        for j in range(n):
            for i in range(j + 1):
                keys = pl.ds(i * block, block)
                bias_ref[bias_slot(j, i)] = bias_block(
                    srow_ref[:, j * block : (j + 1) * block],
                    scol_ref[keys, :],
                    kpos_ref[keys, :],
                    j * block,
                    i * block,
                    block,
                    block,
                    i == j,
                )

    gscale = jnp.zeros((HEAD_DIM, 1), F32)
    for j in range(n):
        cols = slice(j * block, (j + 1) * block)
        q = qkv_ref[0, 0, :, cols]
        go = gout_ref[:, cols]
        lse = lse_ref[0, :, cols]
        delta = jnp.sum(go.astype(F32) * out_ref[0, :, cols].astype(F32), axis=0, keepdims=True)
        gq = jnp.zeros((HEAD_DIM, block), F32)
        step = max(1, CHUNK // block)
        for i in range(0, j + 1, step):
            many = min(step, j + 1 - i)
            keys = slice(i * block, (i + many) * block)
            slot = bias_slot(j, i)
            bias = bias_ref[slot : slot + many].reshape(many * block, block)
            p = jnp.exp(dot(krow_ref[keys, :], q, (1, 0)) + bias - lse)
            gp = dot(vrow_ref[keys, :], go, (1, 0))
            gs = (p * (gp - delta)).astype(BF)
            gq += dot(qkv_ref[1, 0, :, keys], gs, (1, 0))
            gk = dot(q, gs, (1, 1))
            gv = dot(go, p.astype(BF), (1, 1))
            before, last = slice(i * block, min(i + many, j) * block), slice(j * block, (j + 1) * block)
            old = (min(i + many, j) - i) * block
            if old:
                gk_ref[:, before] += gk[:, :old]
                gv_ref[:, before] += gv[:, :old]
            if i + many == j + 1:
                gk_ref[:, last] = gk[:, old:]
                gv_ref[:, last] = gv[:, old:]
        gscale += jnp.sum(gq * raw_ref[0, :, cols], axis=1, keepdims=True)
        grad_ref[0, 0, :, cols] = (gq * factor_ref[...]).astype(BF)
    grad_ref[1, 0] = gk_ref[...].astype(BF)
    grad_ref[2, 0] = gv_ref[...].astype(BF)
    gscale_ref[0] = gscale


def mask_args(series, padding):
    t = series.shape[0]
    pos = jnp.arange(t, dtype=jnp.int32)
    return series.reshape(1, t), series.reshape(t, 1), jnp.where(padding == 0, pos, t).reshape(t, 1)


def attention_forward(at, qkv, masks, pieces=0):
    _, heads, hd, t = qkv.shape
    block = min(256, t) if t <= 2048 else 512
    n = t // block
    whole = lambda shape: pl.BlockSpec(shape, lambda h: (0,) * len(shape))
    return pl.pallas_call(
        functools.partial(forward_kernel, block),
        grid=(heads,),
        in_specs=[
            pl.BlockSpec(memory_space=pltpu.SMEM),
            pl.BlockSpec((3, 1, hd, t), lambda h: (0, h, 0, 0)),
            whole((1, t)),
            whole((t, 1)),
            whole((t, 1)),
        ],
        out_specs=[
            pl.BlockSpec((1, hd, t), lambda h: (h, 0, 0)),
            pl.BlockSpec((1, 1, t), lambda h: (h, 0, 0)),
        ]
        + [pl.BlockSpec((n, 1, hd, block), lambda h: (0, h, 0, 0))] * pieces,
        out_shape=[
            jax.ShapeDtypeStruct((heads, hd, t), BF),
            jax.ShapeDtypeStruct((heads, 1, t), F32),
        ]
        + [jax.ShapeDtypeStruct((n, heads, hd, block), BF)] * pieces,
        scratch_shapes=[
            pltpu.VMEM((n * (n + 1) // 2, block, block), F32),
            pltpu.VMEM((t, hd), BF),
            pltpu.VMEM((t, block), F32),
        ],
        compiler_params=pltpu.CompilerParams(vmem_limit_bytes=VMEM_LARGE),
        cost_estimate=CHEAP,
        name="attention_forward",
    )(at, qkv, *masks)


def attention_backward(at, qkv, raw, factor, out, piece, lse, masks):
    _, heads, hd, t = qkv.shape
    block = min(256, t) if t <= 2048 else 512
    n = t // block
    whole = lambda shape: pl.BlockSpec(shape, lambda h: (0,) * len(shape))
    head = lambda wide=t: pl.BlockSpec((1, hd, wide), lambda h: (h, 0, 0))
    return pl.pallas_call(
        functools.partial(backward_kernel, block),
        grid=(heads,),
        in_specs=[
            pl.BlockSpec(memory_space=pltpu.SMEM),
            pl.BlockSpec((3, 1, hd, t), lambda h: (0, h, 0, 0)),
            head(),
            whole((hd, 1)),
            head(),
            pl.BlockSpec((1, 1, t), lambda h: (h, 0, 0)),
            whole((1, t)),
            whole((t, 1)),
            whole((t, 1)),
        ]
        + [pl.BlockSpec((piece.shape[0], 1, hd, piece.shape[3]), lambda h: (0, h, 0, 0))],
        out_specs=[
            pl.BlockSpec((3, 1, hd, t), lambda h: (0, h, 0, 0)),
            pl.BlockSpec((1, hd, 1), lambda h: (h, 0, 0)),
        ],
        out_shape=[
            jax.ShapeDtypeStruct((3, heads, hd, t), BF),
            jax.ShapeDtypeStruct((heads, hd, 1), F32),
        ],
        scratch_shapes=[
            pltpu.VMEM((n * (n + 1) // 2, block, block), F32),
            pltpu.VMEM((t, hd), BF),
            pltpu.VMEM((t, hd), BF),
            pltpu.VMEM((hd, t), F32),
            pltpu.VMEM((hd, t), F32),
            pltpu.VMEM((hd, t), BF),
        ],
        compiler_params=pltpu.CompilerParams(vmem_limit_bytes=VMEM_LARGE),
        cost_estimate=CHEAP,
        name="attention_backward",
    )(at, qkv, raw, factor, out, lse, *masks, piece)


def norm_scale(x):
    return lax.rsqrt(jnp.mean(x * x, axis=1, keepdims=True) + EPS)


def body_any(
    inputs, gain_attn, w_qkv, query_scale, w_out, gain_mlp, w_up, b_up, w_down, b_down, series_ids, pad_mask, cotangent
):
    rows, cols = size("row"), size("col")
    tok = inputs.shape[0]
    feat = inputs.shape[1]
    share = tok // cols
    t = series_ids.shape[0]
    head_rows = w_qkv.shape[2] // cols
    heads = head_rows // HEAD_DIM
    r, c = lax.axis_index("row"), lax.axis_index("col")

    blocks = gather_grid(inputs)
    strips = [jnp.concatenate(b, axis=1) for b in blocks]
    x_own = strips[0] if rows == 2 else lax.dynamic_index_in_dim(jnp.stack(strips), r, 0, keepdims=False)
    x_all = jnp.concatenate(flip(strips, "row"), axis=0)
    gain_one = jnp.concatenate(gather(gain_attn, "col"))
    gain_two = jnp.concatenate(gather(gain_mlp, "col"))
    bias_up = jnp.concatenate(gather(b_up, "row")).astype(F32)
    bias_down = jnp.concatenate(gather(b_down, "col")).astype(F32)

    w3 = jnp.transpose(w_qkv, (1, 0, 2)).reshape(3, feat, cols, head_rows)
    w_mine = lax.dynamic_index_in_dim(w3, c, 2, keepdims=False)
    w_give = lax.dynamic_index_in_dim(w3, 1 - c, 2, keepdims=False)
    w_half = swap(core_half(w_give, 1), "col")
    w_other = swap(w_half, "core")
    first = lax.axis_index("core") == 0
    w_full = jnp.concatenate(
        [w_mine, jnp.where(first, w_half, w_other), jnp.where(first, w_other, w_half)], axis=1
    )

    xf = x_all.astype(F32)
    scale_one = norm_scale(xf)
    normed_one = (xf * scale_one * gain_one).astype(BF)
    projected = jnp.einsum("td,sdh->sht", normed_one, w_full, preferred_element_type=F32)
    projected = projected.reshape(3, heads, HEAD_DIM, t)
    factor = QUERY_CONST / math.sqrt(HEAD_DIM) * jax.nn.softplus(query_scale)
    raw_q = projected[0]
    qkv = jnp.stack([raw_q * factor[None, :, None], projected[1], projected[2]]).astype(BF)
    masks = mask_args(series_ids, pad_mask)
    at = jnp.zeros((4,), jnp.int32)
    attended, lse = attention_forward(at, qkv, masks)

    def to_tokens(y):
        y = flip_dim(y.reshape(head_rows, rows, cols, share), "row", 1)
        y = flip_dim(y, "col", 2)
        y = exchange(y.reshape(1, head_rows, rows, cols, share), "row", 2, 0)
        y = exchange(y.reshape(rows, 1, head_rows, cols, share), "col", 3, 1)
        y = flip_dim(y.reshape(rows, cols, head_rows, share), "col", 1)
        return y.reshape(rows * cols * head_rows, share)

    def to_heads(y):
        y = flip_dim(y.reshape(rows, cols, head_rows, share), "col", 1)
        y = exchange(y.reshape(rows, cols, head_rows, 1, share), "col", 1, 3)
        y = exchange(y.reshape(rows, head_rows, 1, cols, share), "row", 0, 2)
        y = flip_dim(y.reshape(head_rows, rows, cols, share), "col", 2)
        return flip_dim(y, "row", 1).reshape(head_rows, t)

    w_out_all = weight_gather(w_out, 0)
    w_up_all = weight_gather(w_up, 1)
    w_down_all = weight_gather(w_down, 0)

    def my_share(y):
        return lax.dynamic_slice_in_dim(y, c * share, share, 0)

    att = to_tokens(attended.reshape(head_rows, t))
    x_mine = my_share(x_own).astype(F32)
    middle = x_mine + dot(att, w_out_all, (0, 0))
    scale_two = norm_scale(middle)
    normed_two = (middle * scale_two * gain_two).astype(BF)
    pre_act = dot(normed_two, w_up_all, (1, 0)) + bias_up
    sig = jax.nn.sigmoid(pre_act)
    hidden = (pre_act * sig).astype(BF)
    result = (middle + dot(hidden, w_down_all, (1, 0)) + bias_down).astype(BF)

    def to_block(y):
        mine, theirs = jnp.split(y, 2, axis=1)
        return jnp.concatenate(flip([mine, swap(theirs, "col")], "col"), axis=0)

    layer_out = to_block(result)

    g_give = lax.dynamic_slice_in_dim(cotangent, (1 - c) * share, share, 0)
    g = jnp.concatenate([my_share(cotangent), swap(g_give, "col")], axis=1)
    grad_w_down = dot(hidden, g, (0, 0))
    grad_hidden = dot(g, w_down_all, (1, 1))
    grad_pre_f = grad_hidden * sig * (1.0 + pre_act * (1.0 - sig))
    grad_pre = grad_pre_f.astype(BF)
    grad_b_up = jnp.sum(grad_pre.astype(F32), axis=0)
    grad_w_up = dot(normed_two, grad_pre, (0, 0))
    grad_normed_two = dot(grad_pre, w_up_all, (1, 1))
    weighted = grad_normed_two * gain_two
    inner = jnp.sum(weighted * middle, axis=1, keepdims=True)
    grad_middle = g.astype(F32) + scale_two * weighted - middle * (scale_two**3 * inner / D)
    grad_gain_mlp = jnp.sum(grad_normed_two * middle * scale_two, axis=0)
    grad_branch = grad_middle.astype(BF)
    grad_w_out = dot(att, grad_branch, (1, 0))
    grad_att = dot(w_out_all, grad_branch, (1, 1)).astype(BF)
    grad_attended = to_heads(grad_att).reshape(heads, HEAD_DIM, t)
    grad_middle_block = to_block(grad_middle)

    sum_down = weight_sum(grad_w_down, 0)
    sum_up = weight_sum(grad_w_up, 1)
    sum_out = weight_sum(grad_w_out, 0)

    grad_proj, gscale = attention_backward(
        at, qkv, raw_q, factor.reshape(HEAD_DIM, 1), attended, grad_attended[None], lse, masks
    )
    slope = QUERY_CONST / math.sqrt(HEAD_DIM) * jax.nn.sigmoid(query_scale)
    grad_query_scale = jnp.sum(gscale, axis=(0, 2)) * slope
    grad_proj = grad_proj.reshape(3, head_rows, t)
    grad_normed_one = jnp.einsum("sht,sdh->td", grad_proj, w_full, preferred_element_type=F32)
    weighted_one = grad_normed_one * gain_one
    inner_one = jnp.sum(weighted_one * xf, axis=1)
    grad_gain_attn = jnp.sum(grad_normed_one * xf * scale_one, axis=0)
    inner_one = lax.psum(inner_one, ("row", "col"))
    grad_w = jnp.einsum("td,sht->sdh", normed_one, grad_proj, preferred_element_type=F32)
    grad_w = grad_w.reshape(3, cols, 2, feat // 2, head_rows)
    core = lax.axis_index("core")
    keep = lax.dynamic_index_in_dim(grad_w, core, 2, keepdims=False)
    give = lax.dynamic_index_in_dim(grad_w, 1 - core, 2, keepdims=False).astype(BF)
    part = (keep + swap(give, "core").astype(F32)).astype(BF)
    part = jnp.concatenate(flip([part[:, 0], swap(part[:, 1], "col")], "col"), axis=2)
    sum_qkv = jnp.transpose(z_sum(part), (1, 0, 2))

    e = jnp.concatenate(flip(jnp.split(grad_normed_one.astype(BF), 2, axis=0), "row"), axis=0) if rows == 2 else (
        grad_normed_one.astype(BF)
    )
    e = scatter_sum(e, "row", 0)
    e = scatter_sum(e, "col", 1).astype(F32)
    my_rows = lambda y: lax.dynamic_slice_in_dim(y, r * tok, tok, 0)
    scale_mine = my_rows(scale_one)
    inner_mine = my_rows(inner_one.reshape(t, 1))
    grad_inputs = grad_middle_block + scale_mine * (e * gain_attn) - inputs.astype(F32) * (
        scale_mine**3 * inner_mine / D
    )

    grad_b_down = jnp.sum(g.astype(F32), axis=0)
    vectors = jnp.concatenate(
        [
            flip_dim(grad_gain_attn, "col", 0),
            flip_dim(grad_gain_mlp, "col", 0),
            flip_dim(grad_b_down, "col", 0),
            flip_dim(grad_b_up, "row", 0),
            grad_query_scale,
        ]
    )
    vectors = lax.psum(vectors, ("z", "core", "row", "col"))
    mine_col = lambda at: lax.dynamic_slice_in_dim(vectors, at * D + c * feat, feat, 0)
    units = b_up.shape[0]
    return (
        layer_out,
        grad_inputs,
        mine_col(0),
        sum_qkv,
        vectors[4 * D :],
        sum_out,
        mine_col(1),
        sum_up,
        lax.dynamic_slice_in_dim(vectors, 3 * D + r * units, units, 0),
        sum_down,
        mine_col(2),
    )


SMEM = pl.BlockSpec(memory_space=pltpu.SMEM)
ANY = pl.BlockSpec(memory_space=pl.ANY)


def call(kernel, name, args, specs, outs, scratch=(), limit=VMEM_LIMIT, out_specs=None):
    more = {} if out_specs is None else {"out_specs": out_specs}
    return pl.pallas_call(
        kernel,
        in_specs=specs,
        **more,
        out_shape=outs,
        scratch_shapes=list(scratch),
        compiler_params=pltpu.CompilerParams(vmem_limit_bytes=limit),
        cost_estimate=CHEAP,
        name=name,
    )(*args)


VM = pl.BlockSpec(memory_space=pltpu.VMEM)
HBM = pl.BlockSpec(memory_space=pltpu.HBM)


def shape(dims, kind):
    return jax.ShapeDtypeStruct(dims, kind)


def project_kernel(
    at, x00, x01, x10, x11, gain, factor, w_mine, w_a, w_b, qkv, raw, normed, scale_own, w_full
):
    r, k = at[0], at[2]
    tok, feat = x00.shape
    hr = w_mine.shape[1]
    half = hr // 2
    for s in range(3):
        w_full[pl.ds(s * hr, hr), 0:feat] = w_mine[s]
        w_full[pl.ds(pl.multiple_of(s * hr + k * half, 16), half), feat:] = w_a[s]
        w_full[pl.ds(pl.multiple_of(s * hr + (1 - k) * half, 16), half), feat:] = w_b[s]
    for i, (a_ref, b_ref) in enumerate(((x00, x01), (x10, x11))):
        a, b = a_ref[...].astype(F32), b_ref[...].astype(F32)
        total = jnp.sum(a * a, axis=1, keepdims=True) + jnp.sum(b * b, axis=1, keepdims=True)
        scale = lax.rsqrt(total / (2 * feat) + EPS)
        if i == 0:
            scale_own[...] = scale
        rows = pl.ds(pl.multiple_of((r ^ i) * tok, tok), tok)
        normed[rows, 0:feat] = (a * scale * gain[:, 0:feat]).astype(BF)
        normed[rows, feat:] = (b * scale * gain[:, feat:]).astype(BF)
        y = normed[rows, :]
        q = dot(w_full[0:hr, :], y, (1, 1))
        raw[:, rows] = q
        qkv[0, :, rows] = (q * factor[...]).astype(BF)
        qkv[1, :, rows] = dot(w_full[hr : 2 * hr, :], y, (1, 1)).astype(BF)
        qkv[2, :, rows] = dot(w_full[2 * hr : 3 * hr, :], y, (1, 1)).astype(BF)


def feed_kernel(
    at, gain, bias_up, bias_down, a, x_own, x_col, g_own, g_col,
    w_out, w_up, w_down, hx, hy, d0, d1, hx2, hy2, d02, d12,
    out_own, gm_own, post, ts, vectors, att, hidden_out, normed_out, g_out, pre_out, branch_out,
    w, x_ref, sems, more_sems,
):
    r, c, k = at[0], at[1], at[2]
    _, hr, share = a.shape
    feat = x_own.shape[1]
    half = feat // 2
    first = d0.shape[1]
    rows = pl.ds(pl.multiple_of(c * share, share), share)

    def start(pairs, sem):
        copies = [pltpu.make_async_copy(src, dst, sem.at[m]) for m, (src, dst) in enumerate(pairs)]
        for copy in copies:
            copy.start()
        return copies

    def place(s):
        return pl.ds(pl.multiple_of(((s // 2) ^ r) * 2 * hr + (s % 2) * hr, 16), hr)

    small = [(a.at[s], att.at[place(s), :]) for s in range(4)]
    small += [(x_own.at[rows, :], x_ref.at[:, 0:feat]), (x_col.at[rows, :], x_ref.at[:, feat:])]
    small += [(g_own.at[rows, :], g_out.at[:, 0:feat]), (g_col, g_out.at[:, feat:])]
    small = start(small, more_sems)
    copies = []
    for n, shard in enumerate((w_out, w_up, w_down)):
        rx, cx, ry, cy = (0, feat, feat, 0) if n == 1 else (feat, 0, 0, feat)
        mine = [(shard, w.at[n, 0:feat, 0:feat])]
        for core, (px, py, p0, p1) in ((k, (hx, hy, d0, d1)), (1 - k, (hx2, hy2, d02, d12))):
            down = core * half
            at_x = pl.ds(pl.multiple_of(rx + down, 16), half)
            at_y = pl.ds(pl.multiple_of(ry + down, 16), half)
            at_0 = pl.ds(pl.multiple_of(feat + down, 16), first)
            at_1 = pl.ds(pl.multiple_of(feat + down + first, 16), half - first)
            mine.append((px.at[n], w.at[n, at_x, cx : cx + feat]))
            mine.append((py.at[n], w.at[n, at_y, cy : cy + feat]))
            mine.append((p0.at[n], w.at[n, at_0, feat : 2 * feat]))
            mine.append((p1.at[n], w.at[n, at_1, feat : 2 * feat]))
        copies.append(start(mine, sems.at[n]))

    for copy in small + copies[0]:
        copy.wait()
    middle = x_ref[...].astype(F32) + dot(att[...], w[0], (0, 0))
    scale = lax.rsqrt(jnp.sum(middle * middle, axis=1, keepdims=True) / D + EPS)
    normed = (middle * scale * gain[...]).astype(BF)
    normed_out[...] = normed
    for copy in copies[1]:
        copy.wait()
    pre = dot(normed, w[1], (1, 0)) + bias_up[...]
    sig = jax.nn.sigmoid(pre)
    hidden = (pre * sig).astype(BF)
    hidden_out[...] = hidden
    for copy in copies[2]:
        copy.wait()
    result = (middle + dot(hidden, w[2], (1, 0)) + bias_down[...]).astype(BF)
    out_own[...] = result[:, :feat]
    post[0] = result[:, feat:]

    grad_pre_f = dot(g_out[...], w[2], (1, 1)) * sig * (1.0 + pre * (1.0 - sig))
    grad_pre = grad_pre_f.astype(BF)
    pre_out[...] = grad_pre
    grad_normed = dot(grad_pre, w[1], (1, 1))
    weighted = grad_normed * gain[...]
    inner = jnp.sum(weighted * middle, axis=1, keepdims=True)
    gf = g_out[...].astype(F32)
    grad_middle = gf + scale * weighted - middle * (scale * scale * scale * inner / D)
    gm_own[...] = grad_middle[:, :feat]
    post[1] = grad_middle[:, feat:].astype(BF)
    branch = grad_middle.astype(BF)
    branch_out[...] = branch
    for s in range(4):
        ts[s] = dot(w[0, place(s), :], branch, (1, 1)).astype(BF)
    vectors[...] = jnp.concatenate(
        [
            jnp.sum(grad_normed * (middle * scale), axis=0, keepdims=True),
            jnp.sum(gf, axis=0, keepdims=True),
            jnp.sum(grad_pre.astype(F32), axis=0, keepdims=True),
        ],
        axis=0,
    )


def feed_weights_kernel(at, att, hidden, normed, g, grad_pre, branch, *rest):
    *grads, stage, turned, sems = rest
    k = at[2]
    feat = g.shape[1] // 2
    half = feat // 2
    quarter = half // 2
    copies = []

    def weight_grad(n, left_ref, right):
        for core, begin in ((k, 0), (1 - k, 8)):
            up, low = (begin + 4, begin) if n == 1 else (begin, begin + 4)
            for b in range(2):
                part = pl.ds(pl.multiple_of(b * feat + core * half, 16), half)
                y = dot(left_ref[part, :], right, (1, 0)).astype(BF)
                for j in range(2):
                    cut = slice(j * feat, (j + 1) * feat)
                    for to, value in ((up + 2 * j + (1 - b), y[:quarter, cut]), (low + 2 * b + (1 - j), y[quarter:, cut])):
                        stage[to, n] = value
                        copy = pltpu.make_async_copy(stage.at[to, n], grads[to].at[n], sems.at[to, n])
                        copy.start()
                        copies.append(copy)

    turned[0] = hidden[...].astype(F32).T.astype(BF)
    weight_grad(2, turned.at[0], g[...])
    turned[1] = normed[...].astype(F32).T.astype(BF)
    weight_grad(1, turned.at[1], grad_pre[...])
    weight_grad(0, att, branch[...])
    for copy in copies:
        copy.wait()


def weight_back_kernel(at, grad, normed, keep, give):
    k = at[2]
    part = keep.shape[2]
    feat = keep.shape[3]
    for ref, core in ((give, 1 - k), (keep, k)):
        for s in range(3):
            rows = pl.ds(pl.multiple_of(core * part, 16), part)
            y = dot(grad[s, rows, :], normed[...], (1, 0)).astype(BF)
            ref[0, s] = y[:, :feat]
            ref[1, s] = y[:, feat:]


def project_back_kernel(
    at, grad, w_full, x00, x01, x10, x11, gain, vectors, scale_grad, es
):
    r, c = at[0], at[1]
    tok, feat = x00.shape
    sums = [jnp.zeros((1, feat), F32), jnp.zeros((1, feat), F32)]
    inners = []
    for i, xs in enumerate(((x00, x01), (x10, x11))):
        rows = pl.ds(pl.multiple_of((r ^ i) * tok, tok), tok)
        left = grad[:, rows]
        products, squares, inner = [], 0.0, 0.0
        for j in range(2):
            cut = slice(j * feat, (j + 1) * feat)
            e = dot(left, w_full[:, cut], (0, 0))
            x = xs[j][...].astype(F32)
            product = e * x
            inner = inner + jnp.sum(product * gain[:, cut], axis=1, keepdims=True)
            squares = squares + jnp.sum(x * x, axis=1, keepdims=True)
            es[2 * (r ^ i) + (c ^ j), 0:tok, :] = e.astype(BF)
            products.append(product)
        scale = lax.rsqrt(squares / (2 * feat) + EPS)
        for j in range(2):
            sums[j] += jnp.sum(products[j] * scale, axis=0, keepdims=True)
        line = jnp.broadcast_to(inner, (tok, 128)).T[0:1, :]
        high = line.astype(BF).astype(F32)
        inners.append(jnp.concatenate([high, line - high], axis=0))
    rows = []
    pairs = [(sums[0], sums[1], c)]
    pairs += [(vectors[n : n + 1, :feat], vectors[n : n + 1, feat:], (c, c, r)[n]) for n in range(3)]
    for own, other, place in pairs:
        rows += [jnp.where(place == 0, own, other), jnp.where(place == 0, other, own)]
    rows = jnp.concatenate(rows + [scale_grad[...], jnp.zeros((5, feat), F32)], axis=0)
    for i in range(2):
        inner = jnp.concatenate([inners[i], jnp.zeros((2, feat - tok), F32)], axis=1)
        extra = jnp.concatenate([inner, rows], axis=0).astype(BF)
        for j in range(2):
            es[2 * (r ^ i) + (c ^ j), tok:, :] = extra


def finish_qkv_kernel(at, mine, theirs, mine2, theirs2, out, rows):
    c, k = at[1], at[2]
    half = mine.shape[1]
    for s in range(3):
        for ref, col, core in ((mine, c, k), (theirs, 1 - c, k), (mine2, c, 1 - k), (theirs2, 1 - c, 1 - k)):
            rows[pl.ds(pl.multiple_of((2 * col + core) * half, 16), half), :] = ref[s].astype(F32)
        out[s] = rows[...].T


def finish_feed_kernel(at, a, b, a2, b2, *outs):
    k = at[2]
    quarter = a.shape[1]
    for n, out in enumerate(outs):
        upper, lower = ((b, b2), (a, a2)) if n == 1 else ((a, a2), (b, b2))
        for i, core in ((0, k), (1, 1 - k)):
            for j, refs in enumerate((upper, lower)):
                to = pl.multiple_of((2 * core + j) * quarter, 16)
                out[pl.ds(to, quarter), :] = refs[i][n].astype(F32)


together = lax.optimization_barrier


def after(x, *earlier):
    return lax.optimization_barrier((x, *earlier))[0]


def add(*parts):
    total = parts[0].astype(F32)
    for part in parts[1:]:
        total = total + part.astype(F32)
    return total.astype(BF)


def all_four(x):
    return lax.all_to_all(x, ("row", "col"), 0, 0, tiled=True)


def z_swap(x, step):
    n = size("z")
    return lax.ppermute(x, "z", [(i, i ^ step) for i in range(n)])


def z_first():
    z = lax.axis_index("z")
    return (z == 0) | (z == 3)


def body_four(
    inputs, gain_attn, w_qkv, query_scale, w_out, gain_mlp, w_up, b_up, w_down, b_down, series_ids, pad_mask, cotangent
):
    tok, feat = inputs.shape
    share = tok // 2
    t = series_ids.shape[0]
    hr = w_qkv.shape[2] // 2
    heads = hr // HEAD_DIM
    half = feat // 2
    r, c, k = lax.axis_index("row"), lax.axis_index("col"), lax.axis_index("core")
    at = jnp.stack([r, c, k, 2 * r + c]).astype(jnp.int32)
    mine_rows = lambda y, part: lax.dynamic_slice_in_dim(y, part * share, share, 0)

    few = heads // 2
    quarter = half // 2
    first_rows = (half * 7 // 20) // 16 * 16
    x01 = swap(inputs, "col")
    x10 = swap(inputs, "row")
    small = swap(jnp.concatenate([gain_attn, gain_mlp, b_down.astype(F32)]), "col")
    up_other = swap(b_up.astype(F32), "row")
    w_turned = jnp.transpose(w_qkv, (1, 2, 0)).reshape(3, 2, hr, feat)
    w_mine = lax.dynamic_index_in_dim(w_turned, c, 1, keepdims=False)
    w_give = lax.dynamic_index_in_dim(w_turned, 1 - c, 1, keepdims=False)
    w_half = core_half(w_give, 1)
    w_a = swap(w_half, "col")
    part = jnp.stack([core_half(w_out, 0), core_half(w_up, 0), core_half(w_down, 0)])
    g_give = mine_rows(cotangent, 1 - c)
    x01, x10, small, up_other, part, g_give, w_mine = lax.optimization_barrier(
        (x01, x10, small, up_other, part, g_give, w_mine)
    )
    x11 = swap(after(x01, w_half), "row")
    w_b = swap(w_a, "core")
    gain_one = jnp.concatenate([gain_attn, small[:feat]]).reshape(1, D)
    gain_two = jnp.concatenate([gain_mlp, small[feat : 2 * feat]]).reshape(1, D)
    bias_down = jnp.concatenate([b_down.astype(F32), small[2 * feat :]]).reshape(1, D)
    bias_up = jnp.concatenate([b_up.astype(F32), up_other]).reshape(1, D)
    factor = QUERY_CONST / math.sqrt(HEAD_DIM) * jax.nn.softplus(query_scale)
    factor_col = factor.reshape(HEAD_DIM, 1)

    part = after(part, x11, w_a)
    hx, hy = swap(part, "row"), swap(part, "col")
    hx2, hy2 = swap(hx, "core"), swap(hy, "core")
    qkv, raw, normed_one, scale_own, w_full = call(
        project_kernel,
        "project",
        (at, inputs, x01, x10, x11, gain_one, jnp.tile(factor_col, (heads, 1)), w_mine, w_a, w_b),
        [SMEM] + [VM] * 9,
        [
            shape((3, hr, t), BF),
            shape((hr, t), F32),
            shape((t, D), BF),
            shape((tok, 1), F32),
            shape((3 * hr, D), BF),
        ],
        limit=VMEM_LARGE,
    )
    qkv = qkv.reshape(3, heads, HEAD_DIM, t)
    masks = mask_args(series_ids, pad_mask)
    attended, lse, a = attention_forward(at, qkv, masks, pieces=1)
    a = all_four(a.reshape(4, hr, share))
    hx_on, hy_on, g_give = lax.optimization_barrier((hx, hy, g_give, lse))[:3]
    d0 = swap(hx_on[:, :first_rows], "col")
    d1 = swap(hy_on[:, first_rows:], "row")
    g_col = swap(g_give, "col")
    d0, d1, g_col, a = together((d0, d1, g_col, a))
    d02, d12 = swap(d0, "core"), swap(d1, "core")
    out_own, gm_own, post, ts, vectors, *factors = call(
        feed_kernel,
        "feed_forward",
        (at, gain_two, bias_up, bias_down, a, inputs, x01, cotangent, g_col)
        + (w_out, w_up, w_down, hx, hy, d0, d1, hx2, hy2, d02, d12),
        [SMEM] + [VM] * 3 + [HBM] * 16,
        [
            shape((share, feat), BF),
            shape((share, feat), F32),
            shape((2, share, feat), BF),
            shape((4, hr, share), BF),
            shape((3, D), F32),
            shape((D, share), BF),
        ]
        + [shape((share, D), BF)] * 5,
        scratch=[
            pltpu.VMEM((3, D, D), BF),
            pltpu.VMEM((share, D), BF),
            pltpu.SemaphoreType.DMA((3, 9)),
            pltpu.SemaphoreType.DMA((8,)),
        ],
        limit=VMEM_LARGE,
    )
    grads = call(
        feed_weights_kernel,
        "feed_weights",
        (at, *factors),
        [SMEM] + [VM] * 6,
        [shape((3, quarter, feat), BF)] * 16,
        scratch=[
            pltpu.VMEM((16, 3, quarter, feat), BF),
            pltpu.VMEM((2, D, share), BF),
            pltpu.SemaphoreType.DMA((16, 3)),
        ],
        out_specs=[HBM] * 16,
        limit=VMEM_LARGE,
    )
    ts = all_four(ts)
    others = grads[8:]
    over = lambda n: swap(others[n], "core")
    grads, osx0, osx1, osy0, osy1 = grads[:8], over(0), over(2), over(4), over(6)
    sx0, kx0, sx1, kx1, sy0, ky0, sy1, ky1 = grads
    sx1, sy1 = add(sx1, osx1), add(sy1, osy1)
    ox0, ox1, oy0, oy1 = over(1), over(3), over(5), over(7)
    sx0, sy0 = add(sx0, osx0), add(sy0, osy0)
    ts, sx1, sy1, sx0, sy0 = together((ts, sx1, sy1, sx0, sy0))
    rx1, ry1 = swap(sx1, "row"), swap(sy1, "col")
    rx0, ry0 = swap(sx0, "row"), swap(sy0, "col")
    ts = ts.reshape(4, heads, HEAD_DIM, share)
    raw = raw.reshape(heads, HEAD_DIM, t)

    grad_proj, gscale = attention_backward(at, qkv, raw, factor_col, attended, ts, lse, masks)
    grad_proj = grad_proj.reshape(3, hr, t)
    kept, sent = call(
        weight_back_kernel,
        "weight_back",
        (at, grad_proj, normed_one),
        [SMEM] + [VM] * 2,
        [shape((2, 3, hr // 2, feat), BF)] * 2,
    )
    sent, rx1, ry1, rx0, ry0, ox0, ox1, oy0, oy1 = together((sent, rx1, ry1, rx0, ry0, ox0, ox1, oy0, oy1))
    got = swap(sent, "core")
    px1, py1 = add(kx1, ox1, rx1), add(ky1, oy1, ry1)
    qx, qy = swap(px1, "col"), swap(py1, "row")
    w_pair = add(kept, got)
    first = z_first()
    got_w = z_swap(jnp.where(first, w_pair[1], w_pair[0]), 1)
    slope = QUERY_CONST / math.sqrt(HEAD_DIM) * jax.nn.sigmoid(query_scale)
    grad_query_scale = jnp.sum(gscale, axis=(0, 2)) * slope
    scale_grad = jnp.pad(grad_query_scale, (0, feat - HEAD_DIM)).reshape(1, feat)
    es = call(
        project_back_kernel,
        "project_back",
        (at, after(grad_proj, w_pair, px1, py1).reshape(3 * hr, t), w_full, inputs, x01, x10, x11, gain_one, vectors, scale_grad),
        [SMEM] + [VM] * 9,
        shape((4, tok + 16, feat), BF),
    )
    kx0, ky0 = together((kx0, ky0, es))[:2]
    fx0 = kx0.astype(F32) + ox0.astype(F32) + rx0.astype(F32)
    fy0 = ky0.astype(F32) + oy0.astype(F32) + ry0.astype(F32)
    qx, qy, got_w, w_pair, es, fx0, fy0 = together((qx, qy, got_w, w_pair, es, fx0, fy0))

    mine_w = add(jnp.where(first, w_pair[0], w_pair[1]), got_w)
    met_w = z_swap(mine_w, 3)
    fx, fy = add(fx0, qx), add(fy0, qy)
    got_c = z_swap(jnp.where(first, fy, fx), 1)
    es = all_four(after(es, fx, fy, mine_w))
    met_w, mine_w, got_c, fx, fy, post = together((met_w, mine_w, got_c, fx, fy, post))

    mine_w = add(mine_w, met_w)
    other_w = z_swap(mine_w, 1)
    w_own, w_theirs = jnp.where(first, mine_w, other_w), jnp.where(first, other_w, mine_w)
    mine_c = add(jnp.where(first, fx, fy), got_c)
    met_c = z_swap(mine_c, 3)
    post = swap(post, "col")
    w_theirs = swap(w_theirs, "col")
    total = jnp.sum(es[:, tok + 2 : tok + 11].astype(F32), axis=0)
    total = total + swap(total, "core")
    total_z = z_swap(total, 1)
    mine_c = add(mine_c, met_c)
    other_c = z_swap(mine_c, 1)
    w_theirs = after(w_theirs, mine_c)
    total = total + after(total_z, mine_c)
    total = total + z_swap(total, 2)
    w_args = (at, w_own, w_theirs, swap(w_own, "core"), swap(w_theirs, "core"))
    sum_qkv = call(
        finish_qkv_kernel,
        "finish_qkv",
        w_args,
        [SMEM] + [VM] * 4,
        shape((3, feat, 2 * hr), F32),
        scratch=[pltpu.VMEM((2 * hr, feat), F32)],
    )
    sum_qkv = jnp.transpose(sum_qkv, (1, 0, 2))

    e = jnp.sum(es[:, :tok].astype(F32), axis=0)
    inner = jnp.sum(es[:, tok : tok + 2, :tok].astype(F32), axis=(0, 1)).reshape(tok, 1)
    grad_middle = jnp.concatenate(flip([gm_own, post[1].astype(F32)], "col"), axis=0)
    grad_inputs = grad_middle + scale_own * (e * gain_attn) - inputs.astype(F32) * (scale_own**3 * inner / D)
    layer_out = jnp.concatenate(flip([out_own, post[0]], "col"), axis=0)

    pick = lambda n, place: lax.dynamic_index_in_dim(total, 2 * n + place, 0, keepdims=False)
    mine_c = after(mine_c, sum_qkv, grad_inputs, layer_out, total)
    fx, fy = jnp.where(first, mine_c, other_c), jnp.where(first, other_c, mine_c)
    sum_out, sum_up, sum_down = call(
        finish_feed_kernel,
        "finish_feed",
        (at, fx, fy, swap(fx, "core"), swap(fy, "core")),
        [SMEM] + [VM] * 4,
        [shape((feat, feat), F32)] * 3,
        limit=24 * 1024 * 1024,
    )

    return (
        layer_out,
        grad_inputs,
        pick(0, c),
        sum_qkv,
        total[8, :HEAD_DIM],
        sum_out,
        pick(1, c),
        sum_up,
        pick(3, r),
        sum_down,
        pick(2, c),
    )


def solution(mesh):
    dp, rows, cols = mesh.shape["dp"], mesh.shape["row"], mesh.shape["col"]
    split = Mesh(mesh.devices.reshape(dp // 2, 2, rows, cols), ("z", "core", "row", "col"))
    tokens = P(("z", "core", "row"), "col")
    in_specs = (
        tokens,
        P("col"),
        P("col", None, "row"),
        P(),
        P("row", "col"),
        P("col"),
        P("col", "row"),
        P("row"),
        P("row", "col"),
        P("col"),
        P(("z", "core")),
        P(("z", "core")),
        tokens,
    )
    out_specs = (
        tokens,
        tokens,
        P("col"),
        P("col", None, "row"),
        P(),
        P("row", "col"),
        P("col"),
        P("col", "row"),
        P("row"),
        P("row", "col"),
        P("col"),
    )
    body = body_four if (dp, rows, cols) == (8, 2, 2) else body_any
    return jax.shard_map(body, mesh=split, in_specs=in_specs, out_specs=out_specs, check_vma=False)
```
